32 devices in a mesh: dp: 2 (over core), frames: 4 (over y, x), rows: 4 (over z).
Axes of the slice: x: 2, y: 2, z: 4, core: 2. Of those that a mesh axis runs over, the one named last changes fastest.
Arguments:
- acts_fine: bfloat16 [2, 8, 16, 16, 512], P('dp', 'frames', 'rows'), may hold values from -120 to 120
- acts_coarse: bfloat16 [2, 8, 8, 8, 512], P('dp', 'frames', 'rows'), may hold values from -120 to 120
- grad_coarse: bfloat16 [2, 8, 8, 8, 512], P('dp', 'frames', 'rows'), may hold values from -20 to 20
- gain_fine: float32 [512], replicated, may hold values from 0.5 to 1.5
- bias_fine: float32 [512], replicated, may hold values from -1 to 1
- kernel_fine: bfloat16 [27, 512, 512], P(None, 'rows'), may hold values from -0.0546875 to 0.0546875
- gain_coarse: float32 [512], replicated, may hold values from 0.5 to 1.5
- bias_coarse: float32 [512], replicated, may hold values from -1 to 1
- kernel_coarse: bfloat16 [27, 512, 512], P(None, 'rows'), may hold values from -0.0546875 to 0.0546875
Outputs:
- grad_fine: bfloat16 [2, 8, 16, 16, 512], P('dp', 'frames', 'rows')
- gain_grad_fine: float32 [512], replicated
- bias_grad_fine: float32 [512], replicated
- gain_grad_coarse: float32 [512], replicated
- bias_grad_coarse: float32 [512], replicated
The draws below stay inside these ranges and needn't reach their ends.
All inputs are finite; a program needn't handle non-finite values.
Results may differ from the reference program's by a relative error of at most 0.0048.
Values may be sent and summed in bfloat16 or wider, within the bound.
No kernel may reach another device: no remote copies, remote signals or barrier semaphores. Data moves between devices by JAX's collectives and lax.ppermute only.
A program may use at most 64 MiB of HBM per device.

```python
import jax
import jax.numpy as jnp
from jax import lax

C = 512
GROUPS = 32
WIDTH = 16
CLIPS = 2
FRAMES = 8
HEIGHT = 16


def ramped(key, dims_shape, chan_low, chan_high, offset_size):
    key_list = jax.random.split(key, 3)
    clip_count, frame_num, height, col_width, channels = dims_shape
    time_pos = jnp.arange(frame_num, dtype=jnp.float32) / max(frame_num - 1, 1)
    row_pos = jnp.arange(height, dtype=jnp.float32) / max(height - 1, 1)
    ramp_scale = (1.0 + 2.0 * time_pos)[None, :, None, None, None] * (1.0 + 2.0 * row_pos)[None, None, :, None, None]
    scales = jnp.exp(jax.random.uniform(key_list[0], (channels,), jnp.float32, jnp.log(chan_low), jnp.log(chan_high)))
    offsets = offset_size * jax.random.uniform(key_list[1], (channels,), jnp.float32, -1.0, 1.0)
    noise_field = jnp.clip(jax.random.normal(key_list[2], dims_shape, jnp.float32), -4.0, 4.0)
    return offsets * scales + scales * ramp_scale * noise_field


def draw_acts_fine(key, part):
    return ramped(jax.random.fold_in(key, 11), (CLIPS, FRAMES, HEIGHT, WIDTH, C), 0.3, 3.0, 1.0).astype(jnp.bfloat16)


def draw_acts_coarse(key, part):
    return ramped(jax.random.fold_in(key, 12), (CLIPS, FRAMES, HEIGHT // 2, WIDTH // 2, C), 0.3, 3.0, 1.0).astype(jnp.bfloat16)


def draw_grad_coarse(key, part):
    return ramped(jax.random.fold_in(key, 13), (CLIPS, FRAMES, HEIGHT // 2, WIDTH // 2, C), 0.17, 0.5, 0.3).astype(jnp.bfloat16)


def shard_levels(stream_key, dims, shards, least, largest):
    level = 1.0
    for axis_at, blocks in shards:
        draws = jax.random.uniform(jax.random.fold_in(jax.random.fold_in(stream_key, 6), axis_at), (blocks,), jnp.float32, least / len(shards), largest / len(shards))
        level = level * jnp.repeat(jnp.exp(draws), dims[axis_at] // blocks).reshape((-1,) + (1,) * (len(dims) - 1 - axis_at))
    return level


def gaussian(rng, extent, scale, limit, shards=(), kind=jnp.bfloat16):
    values = scale * jax.random.normal(rng, extent, jnp.float32)
    if shards:
        values = values * shard_levels(rng, extent, shards, -0.22, 0.18)
    return jnp.clip(values, -limit, limit).astype(kind)


def setup_inputs(seed: int = 0) -> dict:
    arg_keys = jax.random.split(jax.random.key(seed), 10)
    acts_fine = draw_acts_fine(jax.random.fold_in(arg_keys[9], 71), 0)
    acts_coarse = draw_acts_coarse(jax.random.fold_in(arg_keys[9], 71), 0)
    grad_coarse = draw_grad_coarse(jax.random.fold_in(arg_keys[9], 71), 0)
    gain_fine = jnp.clip(jax.random.uniform(arg_keys[3], (C,), jnp.float32, 0.5, 1.5), 0.5, 1.5)
    bias_fine = jnp.clip(jax.random.uniform(arg_keys[4], (C,), jnp.float32, -1.0, 1.0), -1.0, 1.0)
    kernel_fine = gaussian(arg_keys[5], (27, C, C), (27 * C) ** -0.5, 0.0546875, ((1, 4),))
    gain_coarse = jnp.clip(jax.random.uniform(arg_keys[6], (C,), jnp.float32, 0.5, 1.5), 0.5, 1.5)
    bias_coarse = jnp.clip(jax.random.uniform(arg_keys[7], (C,), jnp.float32, -1.0, 1.0), -1.0, 1.0)
    kernel_coarse = gaussian(arg_keys[8], (27, C, C), (27 * C) ** -0.5, 0.0546875, ((1, 4),))
    return {"acts_fine": acts_fine, "acts_coarse": acts_coarse, "grad_coarse": grad_coarse, "gain_fine": gain_fine, "bias_fine": bias_fine, "kernel_fine": kernel_fine, "gain_coarse": gain_coarse, "bias_coarse": bias_coarse, "kernel_coarse": kernel_coarse}


EPSILON = 1e-06

def transposed_conv(cotangent, kernel):
    frame_num, height, col_width, channels = cotangent.shape
    padded = jnp.pad(cotangent.astype(jnp.float32), ((0, 2), (1, 1), (1, 1), (0, 0)))
    weights = kernel.astype(jnp.float32)
    accumulated = jnp.zeros((frame_num, height, col_width, channels), jnp.float32)
    for tap_index in range(27):
        time_tap = tap_index // 9
        row_tap = tap_index // 3 % 3
        col_tap = tap_index % 3
        window = padded[2 - time_tap:2 - time_tap + frame_num, 2 - row_tap:2 - row_tap + height, 2 - col_tap:2 - col_tap + col_width]
        accumulated = accumulated + jnp.einsum('thwo,io->thwi', window, weights[tap_index])
    return accumulated

def group_back(acts, cotangent, gain, bias, kernel):
    conv_grad = transposed_conv(cotangent, kernel)
    values = acts.astype(jnp.float32)
    frame_num, height, col_width, channels = values.shape
    group_width = channels // GROUPS
    entries = frame_num * height * col_width * group_width
    grouped = values.reshape(-1, GROUPS, group_width)
    group_mean = lax.optimization_barrier(jnp.sum(grouped, axis=(0, 2))) / entries
    square = lax.optimization_barrier(jnp.sum(grouped * grouped, axis=(0, 2))) / entries
    inv_std = lax.rsqrt(square - group_mean * group_mean + EPSILON)
    mean_chan = jnp.repeat(group_mean, group_width)
    inv_chan = jnp.repeat(inv_std, group_width)
    normed = (values - mean_chan) * inv_chan
    preact = gain * normed + bias
    squash = jax.nn.sigmoid(preact)
    pre_grad = conv_grad * squash * (1.0 + preact * (1.0 - squash))
    sum_one = lax.optimization_barrier(jnp.sum(pre_grad, axis=(0, 1, 2)))
    sum_two = lax.optimization_barrier(jnp.sum(pre_grad * normed, axis=(0, 1, 2)))
    group_one = lax.optimization_barrier(jnp.sum((gain * sum_one).reshape(GROUPS, group_width), axis=1)) / entries
    group_two = lax.optimization_barrier(jnp.sum((gain * sum_two).reshape(GROUPS, group_width), axis=1)) / entries
    level_grad = cotangent.astype(jnp.float32) + inv_chan * (gain * pre_grad - jnp.repeat(group_one, group_width) - normed * jnp.repeat(group_two, group_width))
    return (level_grad, sum_one, sum_two)

def reference(acts_fine, acts_coarse, grad_coarse, gain_fine, bias_fine, kernel_fine, gain_coarse, bias_coarse, kernel_coarse):

    def per_clip(clip_items):
        fine_acts, coarse_acts, cotangent = clip_items
        coarse_input_grad, coarse_one, coarse_two = group_back(coarse_acts, cotangent, gain_coarse, bias_coarse, kernel_coarse)
        upsampled = (jnp.repeat(jnp.repeat(coarse_input_grad, 2, axis=1), 2, axis=2) * 0.25).astype(jnp.bfloat16)
        fine_grad, fine_one, fine_two = group_back(fine_acts, upsampled, gain_fine, bias_fine, kernel_fine)
        return (fine_grad.astype(jnp.bfloat16), fine_one, fine_two, coarse_one, coarse_two)
    results = lax.map(per_clip, (acts_fine, acts_coarse, grad_coarse))
    scale_fine = 1.0 / jnp.sqrt(jnp.float32(CLIPS * FRAMES * HEIGHT * WIDTH))
    scale_coarse = 1.0 / jnp.sqrt(jnp.float32(CLIPS * FRAMES * HEIGHT * WIDTH // 4))
    gain_grad_fine = lax.optimization_barrier(jnp.sum(results[2], axis=0)) * scale_fine
    bias_grad_fine = lax.optimization_barrier(jnp.sum(results[1], axis=0)) * scale_fine
    gain_grad_coarse = lax.optimization_barrier(jnp.sum(results[4], axis=0)) * scale_coarse
    bias_grad_coarse = lax.optimization_barrier(jnp.sum(results[3], axis=0)) * scale_coarse
    return (results[0], gain_grad_fine, bias_grad_fine, gain_grad_coarse, bias_grad_coarse)
```

```python
import jax
import jax.numpy as jnp
from jax import lax
from jax.sharding import PartitionSpec as P

GROUPS = 32
EPSILON = 1e-06
BLOCK = ("frames", "rows")


def to_everyone(block, count):
    copies = jnp.broadcast_to(block[None], (count,) + block.shape)
    return lax.all_to_all(copies, BLOCK, 0, 0)


def ahead(field, axis, distance):
    size = field.shape[axis]
    if distance == 0:
        return field
    widths = [(0, 0)] * field.ndim
    if distance > 0:
        widths[axis] = (0, distance)
        kept = lax.slice_in_dim(field, distance, size, axis=axis)
    else:
        widths[axis] = (-distance, 0)
        kept = lax.slice_in_dim(field, 0, size + distance, axis=axis)
    return jnp.pad(kept, widths)


def tap_products(source, kernel):
    sub = kernel.shape[1]
    frames, rows, cols, channels = source.shape
    products = lax.dot_general(
        kernel.reshape(27 * sub, channels),
        source.reshape(frames * rows * cols, channels),
        (((1,), (1,)), ((), ())),
        preferred_element_type=jnp.float32,
    ).reshape(3, 3, 3, sub, frames, rows, cols)
    return sum(ahead(products[depth], 3, 2 - depth) for depth in range(3))


def coarse_conv(source, kernel):
    spatial = tap_products(source, kernel)
    total = 0.0
    for row in range(3):
        part = sum(ahead(spatial[row, col], 3, 1 - col) for col in range(3))
        total = total + ahead(part, 2, 1 - row)
    return total


def fine_conv(source, kernel):
    spatial = tap_products(source, kernel)
    result = []
    for p in range(2):
        rows_of = []
        for q in range(2):
            total = 0.0
            for row in range(3):
                part = sum(ahead(spatial[row, col], 3, (q + 1 - col) // 2) for col in range(3))
                total = total + ahead(part, 2, (p + 1 - row) // 2)
            rows_of.append(total)
        result.append(jnp.stack(rows_of, 1))
    return jnp.stack(result, 1)


def group_total(sums, group_width):
    sub = sums.shape[-1]
    if sub % group_width == 0:
        grouped = jnp.sum(sums.reshape(-1, sub // group_width, group_width), axis=-1)
        return jnp.repeat(grouped, group_width, axis=-1)
    spread = jnp.moveaxis(lax.all_gather(sums, "frames"), 0, 1).reshape(sums.shape[0], -1, group_width)
    mine = lax.axis_index("frames") * sub // group_width
    grouped = lax.dynamic_index_in_dim(jnp.sum(spread, -1), mine, 1)
    return jnp.broadcast_to(grouped, sums.shape)


def level(acts, conv_grad, cotangent, gain, bias, group_width):
    sub = acts.shape[0]
    places = acts.size // sub
    values = acts.astype(jnp.float32).reshape(sub, places)
    conv_grad = conv_grad.reshape(sub, places)
    entries = places * group_width
    moments = group_total(
        jnp.stack([jnp.sum(values, 1), jnp.sum(values * values, 1)]), group_width
    ) / entries
    mean = moments[0]
    inv_std = lax.rsqrt(moments[1] - mean * mean + EPSILON)
    normed = (values - mean[:, None]) * inv_std[:, None]
    preact = gain[:, None] * normed + bias[:, None]
    squash = jax.nn.sigmoid(preact)
    pre_grad = conv_grad * squash * (1.0 + preact * (1.0 - squash))
    sums = jnp.stack([jnp.sum(pre_grad, 1), jnp.sum(pre_grad * normed, 1)])
    terms = group_total(sums * gain, group_width) / entries
    grad = cotangent.reshape(sub, places) + inv_std[:, None] * (
        gain[:, None] * pre_grad - terms[0][:, None] - normed * terms[1][:, None]
    )
    return grad, sums


def shards(
    acts_fine,
    acts_coarse,
    grad_coarse,
    gain_fine,
    bias_fine,
    kernel_fine,
    gain_coarse,
    bias_coarse,
    kernel_coarse,
):
    nf, nr, nd = lax.axis_size("frames"), lax.axis_size("rows"), lax.axis_size("dp")
    count = nf * nr
    channels = acts_fine.shape[-1]
    slice_width = kernel_fine.shape[1]
    sub = slice_width // nf
    group_width = channels // GROUPS
    tl, hl, w = acts_coarse.shape[1:4]
    frames, rows = tl * nf, hl * nr
    f, r = lax.axis_index("frames"), lax.axis_index("rows")

    gathered = to_everyone(grad_coarse[0], count)
    source = (
        gathered.reshape(nf, nr, tl, hl, w, channels)
        .transpose(0, 2, 1, 3, 4, 5)
        .reshape(frames, rows, w, channels)
    )
    coarse_in = acts_coarse[0].reshape(tl, hl, w, nr, nf, sub).transpose(4, 3, 5, 0, 1, 2)
    coarse_in = lax.all_to_all(coarse_in.reshape(count, sub, tl * hl * w), BLOCK, 0, 0)
    fine_in = acts_fine[0].reshape(tl, hl, 2, w, 2, nr, nf, sub).transpose(6, 5, 7, 2, 4, 0, 1, 3)
    fine_in = lax.all_to_all(fine_in.reshape(count, sub, 4 * tl * hl * w), BLOCK, 0, 0)

    def mine(vector):
        return lax.dynamic_slice_in_dim(vector, r * slice_width + f * sub, sub)

    def own(kernel):
        return lax.dynamic_slice_in_dim(kernel, f * sub, sub, axis=1)

    coarse_vals = (
        coarse_in.reshape(nf, nr, sub, tl, hl, w).transpose(2, 0, 3, 1, 4, 5).reshape(sub, frames, rows, w)
    )
    cot = lax.dynamic_slice_in_dim(source, r * slice_width + f * sub, sub, axis=3)
    cot = cot.astype(jnp.float32).transpose(3, 0, 1, 2)
    conv = coarse_conv(source, own(kernel_coarse))
    coarse_grad, coarse_sums = level(
        coarse_vals, conv, cot, mine(gain_coarse), mine(bias_coarse), group_width
    )
    quartered = (coarse_grad * 0.25).astype(jnp.bfloat16)
    spread = to_everyone(quartered, count)
    source_fine = (
        spread.reshape(nf, nr, sub, frames, rows, w)
        .transpose(3, 4, 5, 1, 0, 2)
        .reshape(frames, rows, w, channels)
    )
    conv = fine_conv(source_fine, own(kernel_fine))
    fine_vals = (
        fine_in.reshape(nf, nr, sub, 2, 2, tl, hl, w)
        .transpose(2, 3, 4, 0, 5, 1, 6, 7)
        .reshape(sub, 2, 2, frames, rows, w)
    )
    cot = jnp.broadcast_to(
        quartered.astype(jnp.float32).reshape(sub, 1, 1, frames, rows, w), conv.shape
    )
    fine_grad, fine_sums = level(
        fine_vals, conv, cot, mine(gain_fine), mine(bias_fine), group_width
    )
    back = (
        fine_grad.astype(jnp.bfloat16)
        .reshape(sub, 2, 2, nf, tl, nr, hl, w)
        .transpose(3, 5, 0, 1, 2, 4, 6, 7)
        .reshape(count, sub, 4 * tl * hl * w)
    )
    sums = to_everyone(jnp.concatenate([fine_sums, coarse_sums]), count)
    back = lax.all_to_all(back, BLOCK, 0, 0)
    out = (
        back.reshape(nf, nr, sub, 2, 2, tl, hl, w)
        .transpose(5, 6, 3, 7, 4, 1, 0, 2)
        .reshape(1, tl, 2 * hl, 2 * w, channels)
    )
    sums = sums.reshape(nf, nr, 4, sub).transpose(2, 1, 0, 3).reshape(4, channels)
    totals = lax.psum(sums, "dp")
    cells = nd * frames * rows * w
    scale_fine = 1.0 / jnp.sqrt(jnp.float32(4 * cells))
    scale_coarse = 1.0 / jnp.sqrt(jnp.float32(cells))
    return (
        out,
        totals[1] * scale_fine,
        totals[0] * scale_fine,
        totals[3] * scale_coarse,
        totals[2] * scale_coarse,
    )


def solution(mesh):
    in_specs = (
        P("dp", "frames", "rows", None, None),
        P("dp", "frames", "rows", None, None),
        P("dp", "frames", "rows", None, None),
        P(),
        P(),
        P(None, "rows", None),
        P(),
        P(),
        P(None, "rows", None),
    )
    out_specs = (P("dp", "frames", "rows", None, None), P(), P(), P(), P())
    return jax.shard_map(shards, mesh=mesh, in_specs=in_specs, out_specs=out_specs, check_vma=False)
```

```python
import functools
import math

import jax
import jax.numpy as jnp
from jax import lax
from jax.experimental import pallas as pl
from jax.experimental.pallas import tpu as pltpu
from jax.sharding import PartitionSpec as P

GROUPS = 32
EPSILON = 1e-06
BLOCK = ("frames", "rows")


def to_everyone(block, count):
    copies = jnp.broadcast_to(block[None], (count,) + block.shape)
    return lax.all_to_all(copies, BLOCK, 0, 0)


def ahead(field, axis, distance):
    size = field.shape[axis]
    if distance == 0:
        return field
    widths = [(0, 0)] * field.ndim
    if distance > 0:
        widths[axis] = (0, distance)
        kept = lax.slice_in_dim(field, distance, size, axis=axis)
    else:
        widths[axis] = (-distance, 0)
        kept = lax.slice_in_dim(field, 0, size + distance, axis=axis)
    return jnp.pad(kept, widths)


def tap_products(source, kernel):
    sub = kernel.shape[1]
    frames, rows, cols, channels = source.shape
    products = lax.dot_general(
        kernel.reshape(27 * sub, channels),
        source.reshape(frames * rows * cols, channels),
        (((1,), (1,)), ((), ())),
        preferred_element_type=jnp.float32,
    ).reshape(3, 3, 3, sub, frames, rows, cols)
    return sum(ahead(products[depth], 3, 2 - depth) for depth in range(3))


def coarse_conv(source, kernel):
    spatial = tap_products(source, kernel)
    total = 0.0
    for row in range(3):
        part = sum(ahead(spatial[row, col], 3, 1 - col) for col in range(3))
        total = total + ahead(part, 2, 1 - row)
    return total


def fine_conv(source, kernel):
    spatial = tap_products(source, kernel)
    result = []
    for p in range(2):
        rows_of = []
        for q in range(2):
            total = 0.0
            for row in range(3):
                part = sum(ahead(spatial[row, col], 3, (q + 1 - col) // 2) for col in range(3))
                total = total + ahead(part, 2, (p + 1 - row) // 2)
            rows_of.append(total)
        result.append(jnp.stack(rows_of, 1))
    return jnp.stack(result, 1)


def group_total(sums, group_width):
    sub = sums.shape[-1]
    if sub % group_width == 0:
        grouped = jnp.sum(sums.reshape(-1, sub // group_width, group_width), axis=-1)
        return jnp.repeat(grouped, group_width, axis=-1)
    spread = jnp.moveaxis(lax.all_gather(sums, "frames"), 0, 1).reshape(sums.shape[0], -1, group_width)
    mine = lax.axis_index("frames") * sub // group_width
    grouped = lax.dynamic_index_in_dim(jnp.sum(spread, -1), mine, 1)
    return jnp.broadcast_to(grouped, sums.shape)


def level(acts, conv_grad, cotangent, gain, bias, group_width):
    sub = acts.shape[0]
    places = acts.size // sub
    values = acts.astype(jnp.float32).reshape(sub, places)
    conv_grad = conv_grad.reshape(sub, places)
    entries = places * group_width
    moments = group_total(
        jnp.stack([jnp.sum(values, 1), jnp.sum(values * values, 1)]), group_width
    ) / entries
    mean = moments[0]
    inv_std = lax.rsqrt(moments[1] - mean * mean + EPSILON)
    normed = (values - mean[:, None]) * inv_std[:, None]
    preact = gain[:, None] * normed + bias[:, None]
    squash = jax.nn.sigmoid(preact)
    pre_grad = conv_grad * squash * (1.0 + preact * (1.0 - squash))
    sums = jnp.stack([jnp.sum(pre_grad, 1), jnp.sum(pre_grad * normed, 1)])
    terms = group_total(sums * gain, group_width) / entries
    grad = cotangent.reshape(sub, places) + inv_std[:, None] * (
        gain[:, None] * pre_grad - terms[0][:, None] - normed * terms[1][:, None]
    )
    return grad, sums


def plain_shards(
    acts_fine,
    acts_coarse,
    grad_coarse,
    gain_fine,
    bias_fine,
    kernel_fine,
    gain_coarse,
    bias_coarse,
    kernel_coarse,
):
    nf, nr, nd = lax.axis_size("frames"), lax.axis_size("rows"), lax.axis_size("dp")
    count = nf * nr
    channels = acts_fine.shape[-1]
    slice_width = kernel_fine.shape[1]
    sub = slice_width // nf
    group_width = channels // GROUPS
    tl, hl, w = acts_coarse.shape[1:4]
    frames, rows = tl * nf, hl * nr
    f, r = lax.axis_index("frames"), lax.axis_index("rows")

    gathered = to_everyone(grad_coarse[0], count)
    source = (
        gathered.reshape(nf, nr, tl, hl, w, channels)
        .transpose(0, 2, 1, 3, 4, 5)
        .reshape(frames, rows, w, channels)
    )
    coarse_in = acts_coarse[0].reshape(tl, hl, w, nr, nf, sub).transpose(4, 3, 5, 0, 1, 2)
    coarse_in = lax.all_to_all(coarse_in.reshape(count, sub, tl * hl * w), BLOCK, 0, 0)
    fine_in = acts_fine[0].reshape(tl, hl, 2, w, 2, nr, nf, sub).transpose(6, 5, 7, 2, 4, 0, 1, 3)
    fine_in = lax.all_to_all(fine_in.reshape(count, sub, 4 * tl * hl * w), BLOCK, 0, 0)

    def mine(vector):
        return lax.dynamic_slice_in_dim(vector, r * slice_width + f * sub, sub)

    def own(kernel):
        return lax.dynamic_slice_in_dim(kernel, f * sub, sub, axis=1)

    coarse_vals = (
        coarse_in.reshape(nf, nr, sub, tl, hl, w).transpose(2, 0, 3, 1, 4, 5).reshape(sub, frames, rows, w)
    )
    cot = lax.dynamic_slice_in_dim(source, r * slice_width + f * sub, sub, axis=3)
    cot = cot.astype(jnp.float32).transpose(3, 0, 1, 2)
    conv = coarse_conv(source, own(kernel_coarse))
    coarse_grad, coarse_sums = level(
        coarse_vals, conv, cot, mine(gain_coarse), mine(bias_coarse), group_width
    )
    quartered = (coarse_grad * 0.25).astype(jnp.bfloat16)
    spread = to_everyone(quartered, count)
    source_fine = (
        spread.reshape(nf, nr, sub, frames, rows, w)
        .transpose(3, 4, 5, 1, 0, 2)
        .reshape(frames, rows, w, channels)
    )
    conv = fine_conv(source_fine, own(kernel_fine))
    fine_vals = (
        fine_in.reshape(nf, nr, sub, 2, 2, tl, hl, w)
        .transpose(2, 3, 4, 0, 5, 1, 6, 7)
        .reshape(sub, 2, 2, frames, rows, w)
    )
    cot = jnp.broadcast_to(
        quartered.astype(jnp.float32).reshape(sub, 1, 1, frames, rows, w), conv.shape
    )
    fine_grad, fine_sums = level(
        fine_vals, conv, cot, mine(gain_fine), mine(bias_fine), group_width
    )
    back = (
        fine_grad.astype(jnp.bfloat16)
        .reshape(sub, 2, 2, nf, tl, nr, hl, w)
        .transpose(3, 5, 0, 1, 2, 4, 6, 7)
        .reshape(count, sub, 4 * tl * hl * w)
    )
    sums = to_everyone(jnp.concatenate([fine_sums, coarse_sums]), count)
    back = lax.all_to_all(back, BLOCK, 0, 0)
    out = (
        back.reshape(nf, nr, sub, 2, 2, tl, hl, w)
        .transpose(5, 6, 3, 7, 4, 1, 0, 2)
        .reshape(1, tl, 2 * hl, 2 * w, channels)
    )
    sums = sums.reshape(nf, nr, 4, sub).transpose(2, 1, 0, 3).reshape(4, channels)
    totals = lax.psum(sums, "dp")
    cells = nd * frames * rows * w
    scale_fine = 1.0 / jnp.sqrt(jnp.float32(4 * cells))
    scale_coarse = 1.0 / jnp.sqrt(jnp.float32(cells))
    return (
        out,
        totals[1] * scale_fine,
        totals[0] * scale_fine,
        totals[3] * scale_coarse,
        totals[2] * scale_coarse,
    )


def lanes_at(shape, axis):
    return lax.broadcasted_iota(jnp.int32, shape, axis)


def pixel_order(tl, hl, w):
    size = 4 * tl * hl * w
    lane = lanes_at((size, size), 1)
    j, i, t = lane % w, lane // w % hl, lane // (w * hl) % tl
    q, p = lane // (w * hl * tl) % 2, lane // (2 * w * hl * tl)
    pixel = (t * 2 * hl + 2 * i + p) * 2 * w + 2 * j + q
    return (lanes_at((size, size), 0) == pixel).astype(jnp.float32).astype(jnp.bfloat16)


def merged_order(nr, outer, tl, cells):
    size = nr * outer * tl * cells
    a = lanes_at((size, size), 0)
    cell, t = a % cells, a // cells % tl
    o, dev = a // (cells * tl) % outer, a // (cells * tl * outer)
    target = ((o * tl + t) * nr + dev) * cells + cell
    return (lanes_at((size, size), 1) == target).astype(jnp.float32).astype(jnp.bfloat16)


def packed_order(nr, tl, cells, half):
    shape = (nr * 128, nr * tl * cells)
    a = lanes_at(shape, 0)
    lane, dev = a % 128 - half * tl * cells, a // 128
    target = (lane // cells * nr + dev) * cells + lane % cells
    held = (lane >= 0) & (lane < tl * cells)
    return (held & (lanes_at(shape, 1) == target)).astype(jnp.float32).astype(jnp.bfloat16)


def one_hot_dot(a, b, dims):
    return lax.dot_general(a, b, (dims, ((), ())), preferred_element_type=jnp.float32)


def moved(field, distance, kept):
    size = field.shape[1]
    return jnp.where(kept, pltpu.roll(field, (-distance) % size, 1), 0.0)


def own_column(row, base, sub):
    shape = (sub, row.shape[1])
    mine = lanes_at(shape, 1) == lanes_at(shape, 0) + base
    return jnp.sum(jnp.where(mine, row, 0.0), axis=1, keepdims=True)


def as_row(column):
    shape = (column.shape[0], 128)
    here = lanes_at(shape, 1) == lanes_at(shape, 0)
    return jnp.sum(jnp.where(here, column, 0.0), axis=0, keepdims=True)


def in_groups(column, group_width):
    sub = column.shape[0]
    grouped = jnp.sum(column.reshape(sub // group_width, group_width, 1), axis=1, keepdims=True)
    return jnp.broadcast_to(grouped, (sub // group_width, group_width, 1)).reshape(sub, 1)


def total(parts):
    return sum(jnp.sum(part, axis=1, keepdims=True) for part in parts)


def normalised(parts, gain, bias, entries, group_width):
    mean = in_groups(total(parts), group_width) / entries
    square = in_groups(total([part * part for part in parts]), group_width) / entries
    inv_std = lax.rsqrt(square - mean * mean + EPSILON)
    normed, slope = [], []
    for part in parts:
        unit = (part - mean) * inv_std
        preact = gain * unit + bias
        squash = jax.nn.sigmoid(preact)
        normed.append(unit)
        slope.append(squash * (1.0 + preact * (1.0 - squash)))
    return normed, slope, inv_std


def finished(convs, normed, slope, cots, gain, inv_std, entries, group_width):
    pre = [conv * part for conv, part in zip(convs, slope)]
    one = total(pre)
    two = total([a * b for a, b in zip(pre, normed)])
    group_one = in_groups(gain * one, group_width) / entries
    group_two = in_groups(gain * two, group_width) / entries
    grads = [
        cot + inv_std * (gain * part - group_one - unit * group_two)
        for cot, part, unit in zip(cots, pre, normed)
    ]
    return grads, one, two


class Plan:
    def __init__(self, mesh_sizes, acts_coarse, slice_width):
        self.nf, self.nr = mesh_sizes
        self.count = self.nf * self.nr
        self.tl, self.hl, self.w, self.channels = acts_coarse
        self.slice_width = slice_width
        self.sub = slice_width // self.nf
        self.cells = self.hl * self.w
        self.local = self.tl * self.cells
        self.image = self.cells * self.nr
        self.frames = self.tl * self.nf
        self.places = self.frames * self.image
        self.group_width = self.channels // GROUPS
        self.fits = (
            self.sub == 32
            and self.group_width == 16
            and self.cells == 16
            and self.tl == 2
            and self.nr == 4
            and self.channels % 128 == 0
            and self.slice_width * self.nr == self.channels
        )

    def place_masks(self):
        lane = lanes_at((1, self.places), 1)
        col, row = lane % self.w, lane // self.w % (self.hl * self.nr)
        last_row = self.hl * self.nr - 1
        return (lane, col > 0, col < self.w - 1, row > 0, row < last_row)


def pack_kernel(plan, g_ref, coarse_ref, fine_ref, out_ref):
    sub, chunks = plan.sub, plan.channels // 128
    order = pixel_order(plan.tl, plan.hl, plan.w)
    fine = one_hot_dot(fine_ref[...], order, ((0,), (0,))).astype(jnp.bfloat16)
    shape = (plan.local, 128)
    low = (lanes_at(shape, 0) == lanes_at(shape, 1)).astype(jnp.float32).astype(jnp.bfloat16)
    high = (lanes_at(shape, 0) + plan.local == lanes_at(shape, 1)).astype(jnp.float32).astype(jnp.bfloat16)
    first = one_hot_dot(coarse_ref[...], low, ((0,), (0,)))
    second = one_hot_dot(coarse_ref[...], high, ((0,), (0,)))
    for f in range(plan.nf):
        for r in range(plan.nr):
            dest, c = f * plan.nr + r, r * plan.slice_width + f * sub
            for k in range(chunks):
                out_ref[dest, k * plan.local : (k + 1) * plan.local, :] = g_ref[:, k * 128 : (k + 1) * 128]
            at = chunks * plan.local
            out_ref[dest, at : at + sub, :] = fine[c : c + sub]
            at += sub
            half = sub // 2
            out_ref[dest, at : at + half, :] = (first[c : c + half] + second[c + half : c + sub]).astype(jnp.bfloat16)


def frame_sum(products_ref, tap, sub, lane, places, image):
    near = products_ref[pl.ds((18 + tap) * sub, sub), :]
    middle = products_ref[pl.ds((9 + tap) * sub, sub), :]
    far = products_ref[pl.ds(tap * sub, sub), :]
    return near + moved(middle, image, lane < places - image) + moved(far, 2 * image, lane < places - 2 * image)


def coarse_kernel(plan, got_ref, gain_ref, bias_ref, kernel_ref, out_ref, sums_ref, weights, source, products, sem):
    sub, nr, nf, cells, tl = plan.sub, plan.nr, plan.nf, plan.cells, plan.tl
    f, r = lax.axis_index("frames"), lax.axis_index("rows")
    base = r * plan.slice_width + f * sub
    copy = pltpu.make_async_copy(
        kernel_ref.at[:, pl.ds(pl.multiple_of(f * sub, sub), sub), :], weights.at[pl.ds(0, 27)], sem
    )
    copy.start()
    chunks = plan.channels // 128
    shape = (sub, plan.channels)
    weights[27] = (lanes_at(shape, 1) == lanes_at(shape, 0) + base).astype(jnp.float32).astype(jnp.bfloat16)
    for s_f in range(nf):
        for s_r in range(nr):
            for t in range(tl):
                at = (s_f * tl + t) * plan.image + s_r * cells
                for k in range(chunks):
                    source[at : at + cells, k * 128 : (k + 1) * 128] = got_ref[
                        s_f * nr + s_r, k * plan.local + t * cells : k * plan.local + (t + 1) * cells, :
                    ]
    at, half = chunks * plan.local + sub, sub // 2
    stacked = jnp.concatenate(
        [
            jnp.concatenate([got_ref[s_f * nr + s_r, at : at + half, :] for s_r in range(nr)], axis=1)
            for s_f in range(nf)
        ],
        axis=0,
    )
    halves = [one_hot_dot(stacked, packed_order(nr, tl, cells, h), ((1,), (0,))) for h in range(2)]
    values = jnp.concatenate(
        [
            jnp.concatenate([part[s_f * half : (s_f + 1) * half] for s_f in range(nf)], axis=1)
            for part in halves
        ],
        axis=0,
    )
    gain = own_column(gain_ref[...], base, sub)
    bias = own_column(bias_ref[...], base, sub)
    entries = plan.places * plan.group_width
    normed, slope, inv_std = normalised([values], gain, bias, entries, plan.group_width)
    copy.wait()
    products[...] = lax.dot_general(
        weights[...].reshape(28 * sub, plan.channels),
        source[...],
        (((1,), (1,)), ((), ())),
        preferred_element_type=jnp.float32,
    )
    lane, has_left, has_right, has_up, has_down = plan.place_masks()
    by_col = []
    for col in range(3):
        parts = [frame_sum(products, 3 * row + col, sub, lane, plan.places, plan.image) for row in range(3)]
        by_col.append(parts[1] + moved(parts[0], plan.w, has_down) + moved(parts[2], -plan.w, has_up))
    conv = by_col[1] + moved(by_col[0], 1, has_right) + moved(by_col[2], -1, has_left)
    cot = products[pl.ds(27 * sub, sub), :]
    grads, one, two = finished([conv], normed, slope, [cot], gain, inv_std, entries, plan.group_width)
    quartered = (grads[0] * 0.25).astype(jnp.bfloat16)
    for dest in range(plan.count):
        out_ref[dest] = quartered
    sums_ref[...] = jnp.concatenate([as_row(one), as_row(two)], axis=0)


def unpack_kernel(plan, got_ref, gain_ref, bias_ref, normed_ref, slope_ref, inv_ref):
    sub, nr, nf = plan.sub, plan.nr, plan.nf
    base = lax.axis_index("rows") * plan.slice_width + lax.axis_index("frames") * sub
    at = plan.channels // 128 * plan.local
    stacked = jnp.concatenate(
        [
            jnp.concatenate([got_ref[s_f * nr + s_r, at : at + sub, :] for s_r in range(nr)], axis=1)
            for s_f in range(nf)
        ],
        axis=0,
    )
    merged = one_hot_dot(stacked, merged_order(nr, 4, plan.tl, plan.cells), ((1,), (0,)))
    width = plan.tl * plan.image
    parts = [
        jnp.concatenate(
            [merged[s_f * sub : (s_f + 1) * sub, pq * width : (pq + 1) * width] for s_f in range(nf)], axis=1
        )
        for pq in range(4)
    ]
    gain = own_column(gain_ref[...], base, sub)
    bias = own_column(bias_ref[...], base, sub)
    entries = 4 * plan.places * plan.group_width
    normed, slope, inv_std = normalised(parts, gain, bias, entries, plan.group_width)
    for pq in range(4):
        normed_ref[pq] = normed[pq]
        slope_ref[pq] = slope[pq]
    inv_ref[...] = jnp.broadcast_to(inv_std, (sub, 128))


def fine_kernel(
    plan, got_ref, normed_ref, slope_ref, inv_ref, gain_ref, sums_ref, kernel_ref, out_ref, weights, source, products, sem
):
    sub, nr, nf = plan.sub, plan.nr, plan.nf
    f, r = lax.axis_index("frames"), lax.axis_index("rows")
    base = r * plan.slice_width + f * sub
    copy = pltpu.make_async_copy(
        kernel_ref.at[:, pl.ds(pl.multiple_of(f * sub, sub), sub), :], weights, sem
    )
    copy.start()
    for s_f in range(nf):
        for s_r in range(nr):
            c = s_r * plan.slice_width + s_f * sub
            source[c : c + sub, :] = got_ref[s_f * nr + s_r]
    gain = own_column(gain_ref[...], base, sub)
    copy.wait()
    products[...] = lax.dot_general(
        weights[...].reshape(27 * sub, plan.channels),
        source[...],
        (((1,), (0,)), ((), ())),
        preferred_element_type=jnp.float32,
    )
    lane, has_left, has_right, has_up, has_down = plan.place_masks()
    by_row = []
    for row in range(3):
        a, b, c = [frame_sum(products, 3 * row + col, sub, lane, plan.places, plan.image) for col in range(3)]
        by_row.append((a + b + moved(c, -1, has_left), moved(a, 1, has_right) + b + c))
    convs = [by_row[0][q] + by_row[1][q] + moved(by_row[2][q], -plan.w, has_up) for q in range(2)]
    convs += [moved(by_row[0][q], plan.w, has_down) + by_row[1][q] + by_row[2][q] for q in range(2)]
    cot = got_ref[f * nr + r].astype(jnp.float32)
    entries = 4 * plan.places * plan.group_width
    grads, one, two = finished(
        convs,
        [normed_ref[pq] for pq in range(4)],
        [slope_ref[pq] for pq in range(4)],
        [cot] * 4,
        gain,
        inv_ref[:, 0:1],
        entries,
        plan.group_width,
    )
    width = plan.tl * plan.image
    stacked = jnp.concatenate(
        [
            jnp.concatenate(
                [grads[pq][:, s_f * width : (s_f + 1) * width].astype(jnp.bfloat16) for pq in range(4)], axis=1
            )
            for s_f in range(nf)
        ],
        axis=0,
    )
    sent = one_hot_dot(stacked, merged_order(nr, 4, plan.tl, plan.cells), ((1,), (1,))).astype(jnp.bfloat16)
    sums = jnp.concatenate([as_row(one), as_row(two), sums_ref[...]], axis=0)
    top = sums.astype(jnp.bfloat16).astype(jnp.float32)
    middle = (sums - top).astype(jnp.bfloat16).astype(jnp.float32)
    low = sums - top - middle
    coded = jnp.concatenate([top, middle, low, jnp.zeros_like(top)], axis=0).astype(jnp.bfloat16)
    for s_f in range(nf):
        for s_r in range(nr):
            out_ref[s_f * nr + s_r, 0:sub, :] = sent[s_f * sub : (s_f + 1) * sub, s_r * 128 : (s_r + 1) * 128]
            out_ref[s_f * nr + s_r, sub : sub + 16, :] = coded


def spread_kernel(plan, scales, got_ref, out_ref, *rest):
    sum_refs, source = rest[:4], rest[4]
    sub, nr, nf = plan.sub, plan.nr, plan.nf
    for s_f in range(nf):
        for s_r in range(nr):
            c = s_r * plan.slice_width + s_f * sub
            source[c : c + sub, :] = got_ref[s_f * nr + s_r, 0:sub, :]
    order = pixel_order(plan.tl, plan.hl, plan.w)
    out_ref[...] = one_hot_dot(order, source[...], ((1,), (1,))).astype(jnp.bfloat16)
    columns = []
    for s_r in range(nr):
        held = 0.0
        for s_f in range(nf):
            coded = got_ref[s_f * nr + s_r, sub : sub + 16, :].astype(jnp.float32)
            sums = coded[0:4] + coded[4:8] + coded[8:12]
            held = held + (pltpu.roll(sums, s_f * sub, 1) if s_f else sums)
        columns.append(held)
    rows = jnp.concatenate(columns, axis=1)
    for k in range(4):
        sum_refs[k][...] = rows[k : k + 1] * scales[k]


def in_vmem(count):
    return [pl.BlockSpec(memory_space=pltpu.VMEM)] * count


def shape_of(shape, kind):
    return jax.ShapeDtypeStruct(shape, kind)


LIMIT = pltpu.CompilerParams(vmem_limit_bytes=40 * 1024 * 1024)


def fast_shards(
    plan,
    acts_fine,
    acts_coarse,
    grad_coarse,
    gain_fine,
    bias_fine,
    kernel_fine,
    gain_coarse,
    bias_coarse,
    kernel_coarse,
):
    nd = lax.axis_size("dp")
    count, sub, channels, places, local = plan.count, plan.sub, plan.channels, plan.places, plan.local
    chunks = channels // 128
    packed_rows = chunks * local + sub + sub // 2
    f32, bf16 = jnp.float32, jnp.bfloat16
    packed = pl.pallas_call(
        functools.partial(pack_kernel, plan),
        out_shape=shape_of((count, packed_rows, 128), bf16),
        in_specs=in_vmem(3),
        out_specs=in_vmem(1)[0],
        compiler_params=LIMIT,
    )(
        grad_coarse.reshape(local, channels),
        acts_coarse.reshape(local, channels),
        acts_fine.reshape(4 * local, channels),
    )
    got = lax.all_to_all(packed, BLOCK, 0, 0)
    quartered, coarse_sums = pl.pallas_call(
        functools.partial(coarse_kernel, plan),
        out_shape=(shape_of((count, sub, places), bf16), shape_of((2, 128), f32)),
        in_specs=in_vmem(3) + [pl.BlockSpec(memory_space=pl.ANY)],
        out_specs=tuple(in_vmem(2)),
        scratch_shapes=[
            pltpu.VMEM((28, sub, channels), bf16),
            pltpu.VMEM((places, channels), bf16),
            pltpu.VMEM((28 * sub, places), f32),
            pltpu.SemaphoreType.DMA,
        ],
        compiler_params=LIMIT,
    )(got, gain_coarse.reshape(1, channels), bias_coarse.reshape(1, channels), kernel_coarse)
    spread = lax.all_to_all(quartered, BLOCK, 0, 0)
    normed, slope, inv_std = pl.pallas_call(
        functools.partial(unpack_kernel, plan),
        out_shape=(
            shape_of((4, sub, places), f32),
            shape_of((4, sub, places), f32),
            shape_of((sub, 128), f32),
        ),
        in_specs=in_vmem(3),
        out_specs=tuple(in_vmem(3)),
        compiler_params=LIMIT,
    )(got, gain_fine.reshape(1, channels), bias_fine.reshape(1, channels))
    sent = pl.pallas_call(
        functools.partial(fine_kernel, plan),
        out_shape=shape_of((count, sub + 16, 128), bf16),
        in_specs=in_vmem(6) + [pl.BlockSpec(memory_space=pl.ANY)],
        out_specs=in_vmem(1)[0],
        scratch_shapes=[
            pltpu.VMEM((27, sub, channels), bf16),
            pltpu.VMEM((channels, places), bf16),
            pltpu.VMEM((27 * sub, places), f32),
            pltpu.SemaphoreType.DMA,
        ],
        compiler_params=LIMIT,
    )(spread, normed, slope, inv_std, gain_fine.reshape(1, channels), coarse_sums, kernel_fine)
    back = lax.all_to_all(sent, BLOCK, 0, 0)
    cells = nd * places
    fine_scale, coarse_scale = 1.0 / math.sqrt(4 * cells), 1.0 / math.sqrt(cells)
    out, *sums = pl.pallas_call(
        functools.partial(spread_kernel, plan, (fine_scale, fine_scale, coarse_scale, coarse_scale)),
        out_shape=(shape_of((4 * local, channels), bf16),) + (shape_of((1, channels), f32),) * 4,
        in_specs=in_vmem(1),
        out_specs=tuple(in_vmem(5)),
        scratch_shapes=[pltpu.VMEM((channels, 4 * local), bf16)],
        compiler_params=LIMIT,
    )(back)
    bias_f, gain_f, bias_c, gain_c = lax.psum(tuple(part.reshape(channels) for part in sums), "dp")
    return out.reshape(acts_fine.shape), gain_f, bias_f, gain_c, bias_c


def solution(mesh):
    def shards(*arrays):
        sizes = (lax.axis_size("frames"), lax.axis_size("rows"))
        plan = Plan(sizes, arrays[1].shape[1:], arrays[5].shape[1])
        if plan.fits:
            return fast_shards(plan, *arrays)
        return plain_shards(*arrays)

    in_specs = (
        P("dp", "frames", "rows", None, None),
        P("dp", "frames", "rows", None, None),
        P("dp", "frames", "rows", None, None),
        P(),
        P(),
        P(None, "rows", None),
        P(),
        P(),
        P(None, "rows", None),
    )
    out_specs = (P("dp", "frames", "rows", None, None), P(), P(), P(), P())
    return jax.shard_map(shards, mesh=mesh, in_specs=in_specs, out_specs=out_specs, check_vma=False)
```

```python
import functools
import math

import jax
import jax.numpy as jnp
from jax import lax
from jax.experimental import pallas as pl
from jax.experimental.pallas import tpu as pltpu
from jax.sharding import PartitionSpec as P

GROUPS = 32
EPSILON = 1e-06
BLOCK = ("frames", "rows")


def to_everyone(block, count):
    copies = jnp.broadcast_to(block[None], (count,) + block.shape)
    return lax.all_to_all(copies, BLOCK, 0, 0)


def ahead(field, axis, distance):
    size = field.shape[axis]
    if distance == 0:
        return field
    widths = [(0, 0)] * field.ndim
    if distance > 0:
        widths[axis] = (0, distance)
        kept = lax.slice_in_dim(field, distance, size, axis=axis)
    else:
        widths[axis] = (-distance, 0)
        kept = lax.slice_in_dim(field, 0, size + distance, axis=axis)
    return jnp.pad(kept, widths)


def tap_products(source, kernel):
    sub = kernel.shape[1]
    frames, rows, cols, channels = source.shape
    products = lax.dot_general(
        kernel.reshape(27 * sub, channels),
        source.reshape(frames * rows * cols, channels),
        (((1,), (1,)), ((), ())),
        preferred_element_type=jnp.float32,
    ).reshape(3, 3, 3, sub, frames, rows, cols)
    return sum(ahead(products[depth], 3, 2 - depth) for depth in range(3))


def coarse_conv(source, kernel):
    spatial = tap_products(source, kernel)
    total = 0.0
    for row in range(3):
        part = sum(ahead(spatial[row, col], 3, 1 - col) for col in range(3))
        total = total + ahead(part, 2, 1 - row)
    return total


def fine_conv(source, kernel):
    spatial = tap_products(source, kernel)
    result = []
    for p in range(2):
        rows_of = []
        for q in range(2):
            total = 0.0
            for row in range(3):
                part = sum(ahead(spatial[row, col], 3, (q + 1 - col) // 2) for col in range(3))
                total = total + ahead(part, 2, (p + 1 - row) // 2)
            rows_of.append(total)
        result.append(jnp.stack(rows_of, 1))
    return jnp.stack(result, 1)


def group_total(sums, group_width):
    sub = sums.shape[-1]
    if sub % group_width == 0:
        grouped = jnp.sum(sums.reshape(-1, sub // group_width, group_width), axis=-1)
        return jnp.repeat(grouped, group_width, axis=-1)
    spread = jnp.moveaxis(lax.all_gather(sums, "frames"), 0, 1).reshape(sums.shape[0], -1, group_width)
    mine = lax.axis_index("frames") * sub // group_width
    grouped = lax.dynamic_index_in_dim(jnp.sum(spread, -1), mine, 1)
    return jnp.broadcast_to(grouped, sums.shape)


def level(acts, conv_grad, cotangent, gain, bias, group_width):
    sub = acts.shape[0]
    places = acts.size // sub
    values = acts.astype(jnp.float32).reshape(sub, places)
    conv_grad = conv_grad.reshape(sub, places)
    entries = places * group_width
    moments = group_total(
        jnp.stack([jnp.sum(values, 1), jnp.sum(values * values, 1)]), group_width
    ) / entries
    mean = moments[0]
    inv_std = lax.rsqrt(moments[1] - mean * mean + EPSILON)
    normed = (values - mean[:, None]) * inv_std[:, None]
    preact = gain[:, None] * normed + bias[:, None]
    squash = jax.nn.sigmoid(preact)
    pre_grad = conv_grad * squash * (1.0 + preact * (1.0 - squash))
    sums = jnp.stack([jnp.sum(pre_grad, 1), jnp.sum(pre_grad * normed, 1)])
    terms = group_total(sums * gain, group_width) / entries
    grad = cotangent.reshape(sub, places) + inv_std[:, None] * (
        gain[:, None] * pre_grad - terms[0][:, None] - normed * terms[1][:, None]
    )
    return grad, sums


def plain_shards(
    acts_fine,
    acts_coarse,
    grad_coarse,
    gain_fine,
    bias_fine,
    kernel_fine,
    gain_coarse,
    bias_coarse,
    kernel_coarse,
):
    nf, nr, nd = lax.axis_size("frames"), lax.axis_size("rows"), lax.axis_size("dp")
    count = nf * nr
    channels = acts_fine.shape[-1]
    slice_width = kernel_fine.shape[1]
    sub = slice_width // nf
    group_width = channels // GROUPS
    tl, hl, w = acts_coarse.shape[1:4]
    frames, rows = tl * nf, hl * nr
    f, r = lax.axis_index("frames"), lax.axis_index("rows")

    gathered = to_everyone(grad_coarse[0], count)
    source = (
        gathered.reshape(nf, nr, tl, hl, w, channels)
        .transpose(0, 2, 1, 3, 4, 5)
        .reshape(frames, rows, w, channels)
    )
    coarse_in = acts_coarse[0].reshape(tl, hl, w, nr, nf, sub).transpose(4, 3, 5, 0, 1, 2)
    coarse_in = lax.all_to_all(coarse_in.reshape(count, sub, tl * hl * w), BLOCK, 0, 0)
    fine_in = acts_fine[0].reshape(tl, hl, 2, w, 2, nr, nf, sub).transpose(6, 5, 7, 2, 4, 0, 1, 3)
    fine_in = lax.all_to_all(fine_in.reshape(count, sub, 4 * tl * hl * w), BLOCK, 0, 0)

    def mine(vector):
        return lax.dynamic_slice_in_dim(vector, r * slice_width + f * sub, sub)

    def own(kernel):
        return lax.dynamic_slice_in_dim(kernel, f * sub, sub, axis=1)

    coarse_vals = (
        coarse_in.reshape(nf, nr, sub, tl, hl, w).transpose(2, 0, 3, 1, 4, 5).reshape(sub, frames, rows, w)
    )
    cot = lax.dynamic_slice_in_dim(source, r * slice_width + f * sub, sub, axis=3)
    cot = cot.astype(jnp.float32).transpose(3, 0, 1, 2)
    conv = coarse_conv(source, own(kernel_coarse))
    coarse_grad, coarse_sums = level(
        coarse_vals, conv, cot, mine(gain_coarse), mine(bias_coarse), group_width
    )
    quartered = (coarse_grad * 0.25).astype(jnp.bfloat16)
    spread = to_everyone(quartered, count)
    source_fine = (
        spread.reshape(nf, nr, sub, frames, rows, w)
        .transpose(3, 4, 5, 1, 0, 2)
        .reshape(frames, rows, w, channels)
    )
    conv = fine_conv(source_fine, own(kernel_fine))
    fine_vals = (
        fine_in.reshape(nf, nr, sub, 2, 2, tl, hl, w)
        .transpose(2, 3, 4, 0, 5, 1, 6, 7)
        .reshape(sub, 2, 2, frames, rows, w)
    )
    cot = jnp.broadcast_to(
        quartered.astype(jnp.float32).reshape(sub, 1, 1, frames, rows, w), conv.shape
    )
    fine_grad, fine_sums = level(
        fine_vals, conv, cot, mine(gain_fine), mine(bias_fine), group_width
    )
    back = (
        fine_grad.astype(jnp.bfloat16)
        .reshape(sub, 2, 2, nf, tl, nr, hl, w)
        .transpose(3, 5, 0, 1, 2, 4, 6, 7)
        .reshape(count, sub, 4 * tl * hl * w)
    )
    sums = to_everyone(jnp.concatenate([fine_sums, coarse_sums]), count)
    back = lax.all_to_all(back, BLOCK, 0, 0)
    out = (
        back.reshape(nf, nr, sub, 2, 2, tl, hl, w)
        .transpose(5, 6, 3, 7, 4, 1, 0, 2)
        .reshape(1, tl, 2 * hl, 2 * w, channels)
    )
    sums = sums.reshape(nf, nr, 4, sub).transpose(2, 1, 0, 3).reshape(4, channels)
    totals = lax.psum(sums, "dp")
    cells = nd * frames * rows * w
    scale_fine = 1.0 / jnp.sqrt(jnp.float32(4 * cells))
    scale_coarse = 1.0 / jnp.sqrt(jnp.float32(cells))
    return (
        out,
        totals[1] * scale_fine,
        totals[0] * scale_fine,
        totals[3] * scale_coarse,
        totals[2] * scale_coarse,
    )


def lanes_at(shape, axis):
    return lax.broadcasted_iota(jnp.int32, shape, axis)


def pixel_order(tl, hl, w):
    size = 4 * tl * hl * w
    lane = lanes_at((size, size), 1)
    j, i, t = lane % w, lane // w % hl, lane // (w * hl) % tl
    q, p = lane // (w * hl * tl) % 2, lane // (2 * w * hl * tl)
    pixel = (t * 2 * hl + 2 * i + p) * 2 * w + 2 * j + q
    return (lanes_at((size, size), 0) == pixel).astype(jnp.float32).astype(jnp.bfloat16)


def merged_order(nr, outer, tl, cells):
    size = nr * outer * tl * cells
    a = lanes_at((size, size), 0)
    cell, t = a % cells, a // cells % tl
    o, dev = a // (cells * tl) % outer, a // (cells * tl * outer)
    target = ((o * tl + t) * nr + dev) * cells + cell
    return (lanes_at((size, size), 1) == target).astype(jnp.float32).astype(jnp.bfloat16)


def one_hot_dot(a, b, dims):
    return lax.dot_general(a, b, (dims, ((), ())), preferred_element_type=jnp.float32)


def moved(field, distance, kept):
    size = field.shape[1]
    return jnp.where(kept, pltpu.roll(field, (-distance) % size, 1), 0.0)


def own_column(row, base, sub):
    shape = (sub, row.shape[1])
    mine = lanes_at(shape, 1) == lanes_at(shape, 0) + base
    return jnp.sum(jnp.where(mine, row, 0.0), axis=1, keepdims=True)


def as_row(column):
    shape = (column.shape[0], 128)
    here = lanes_at(shape, 1) == lanes_at(shape, 0)
    return jnp.sum(jnp.where(here, column, 0.0), axis=0, keepdims=True)


def in_groups(column, group_width):
    sub = column.shape[0]
    grouped = jnp.sum(column.reshape(sub // group_width, group_width, 1), axis=1, keepdims=True)
    return jnp.broadcast_to(grouped, (sub // group_width, group_width, 1)).reshape(sub, 1)


def total(parts):
    return sum(jnp.sum(part, axis=1, keepdims=True) for part in parts)


def normalised(parts, gain, bias, entries, group_width):
    mean = in_groups(total(parts), group_width) / entries
    square = in_groups(total([part * part for part in parts]), group_width) / entries
    inv_std = lax.rsqrt(square - mean * mean + EPSILON)
    normed, slope = [], []
    for part in parts:
        unit = (part - mean) * inv_std
        preact = gain * unit + bias
        squash = jax.nn.sigmoid(preact)
        normed.append(unit)
        slope.append(squash * (1.0 + preact * (1.0 - squash)))
    return normed, slope, inv_std


def finished(convs, normed, slope, cots, gain, inv_std, entries, group_width):
    pre = [conv * part for conv, part in zip(convs, slope)]
    one = total(pre)
    two = total([a * b for a, b in zip(pre, normed)])
    group_one = in_groups(gain * one, group_width) / entries
    group_two = in_groups(gain * two, group_width) / entries
    grads = [
        cot + inv_std * (gain * part - group_one - unit * group_two)
        for cot, part, unit in zip(cots, pre, normed)
    ]
    return grads, one, two


class Plan:
    def __init__(self, mesh_sizes, acts_coarse, slice_width):
        self.nf, self.nr = mesh_sizes
        self.count = self.nf * self.nr
        self.tl, self.hl, self.w, self.channels = acts_coarse
        self.slice_width = slice_width
        self.sub = slice_width // self.nf
        self.cells = self.hl * self.w
        self.local = self.tl * self.cells
        self.image = self.cells * self.nr
        self.frames = self.tl * self.nf
        self.places = self.frames * self.image
        self.group_width = self.channels // GROUPS
        self.fits = (
            self.sub == 32
            and self.group_width == 16
            and self.cells == 16
            and self.tl == 2
            and self.nr == 4
            and self.channels % 128 == 0
            and self.slice_width * self.nr == self.channels
        )

    def place_masks(self):
        lane = lanes_at((1, self.places), 1)
        col, row = lane % self.w, lane // self.w % (self.hl * self.nr)
        last_row = self.hl * self.nr - 1
        return (lane, col > 0, col < self.w - 1, row > 0, row < last_row)


def fetched(pairs, sems):
    copies = [pltpu.make_async_copy(src, dst, sems.at[k]) for k, (src, dst) in enumerate(pairs)]
    for copy in copies:
        copy.start()
    return copies


def pack_kernel(plan, g_hbm, coarse_hbm, fine_hbm, out_ref, g_ref, coarse_ref, fine_ref, sems):
    sub, chunks, local = plan.sub, plan.channels // 128, plan.local
    copies = fetched(((fine_hbm, fine_ref), (coarse_hbm, coarse_ref), (g_hbm, g_ref)), sems)
    order = pixel_order(plan.tl, plan.hl, plan.w)
    shape = (local, 128)
    places = [
        (lanes_at(shape, 0) + k * local == lanes_at(shape, 1)).astype(jnp.float32).astype(jnp.bfloat16)
        for k in range(4)
    ]
    copies[0].wait()
    fine = one_hot_dot(fine_ref[...], order, ((0,), (0,))).astype(jnp.bfloat16)
    copies[1].wait()
    quarters = [one_hot_dot(coarse_ref[...], place, ((0,), (0,))) for place in places]
    copies[2].wait()
    for f in range(plan.nf):
        for r in range(plan.nr):
            dest, c = f * plan.nr + r, r * plan.slice_width + f * sub
            for k in range(chunks):
                out_ref[dest, k * local : (k + 1) * local, :] = g_ref[:, k * 128 : (k + 1) * 128]
            at = chunks * local
            out_ref[dest, at : at + sub, :] = fine[c : c + sub]
            coarse = sum(quarters[k][c + 8 * k : c + 8 * k + 8] for k in range(4))
            out_ref[dest, at + sub : at + sub + 8, :] = coarse.astype(jnp.bfloat16)


def stage_kernel(
    plan,
    kernel_c,
    kernel_f,
    gain_c,
    bias_c,
    gain_f,
    bias_f,
    weights_c,
    weights_f,
    columns,
    order,
    rows,
    sems,
):
    sub = plan.sub
    f, r = lax.axis_index("frames"), lax.axis_index("rows")
    base = r * plan.slice_width + f * sub
    own = pl.ds(pl.multiple_of(f * sub, sub), sub)
    copies = fetched(
        [(row, rows.at[k]) for k, row in enumerate((gain_c, bias_c, gain_f, bias_f))]
        + [(kernel_c.at[:, own, :], weights_c.at[pl.ds(0, 27)]), (kernel_f.at[:, own, :], weights_f)],
        sems,
    )
    shape = (sub, plan.channels)
    weights_c[27] = (lanes_at(shape, 1) == lanes_at(shape, 0) + base).astype(jnp.float32).astype(jnp.bfloat16)
    order[...] = merged_order(plan.nr, 4, plan.tl, plan.cells)
    for copy in copies:
        copy.wait()
    for k in range(4):
        columns[k] = jnp.broadcast_to(own_column(rows[k], base, sub), (sub, 128))


def by_frame_device(plan, got_ref, at, height):
    return jnp.concatenate(
        [
            jnp.concatenate(
                [got_ref[f * plan.nr + r, at : at + height, :] for r in range(plan.nr)], axis=1
            )
            for f in range(plan.nf)
        ],
        axis=0,
    )


def in_places(plan, merged, height):
    width = plan.tl * plan.image
    return [
        jnp.concatenate(
            [merged[f * height : (f + 1) * height, k * width : (k + 1) * width] for f in range(plan.nf)],
            axis=1,
        )
        for k in range(4)
    ]


def frame_sum(products_ref, tap, sub, lane, places, image):
    near = products_ref[pl.ds((18 + tap) * sub, sub), :]
    middle = products_ref[pl.ds((9 + tap) * sub, sub), :]
    far = products_ref[pl.ds(tap * sub, sub), :]
    return near + moved(middle, image, lane < places - image) + moved(far, 2 * image, lane < places - 2 * image)


def coarse_kernel(plan, got_ref, weights, columns, order, out_ref, sums_ref, source, products):
    sub, nr, nf, cells, tl, local = plan.sub, plan.nr, plan.nf, plan.cells, plan.tl, plan.local
    chunks = plan.channels // 128
    for s_f in range(nf):
        for s_r in range(nr):
            for t in range(tl):
                at = (s_f * tl + t) * plan.image + s_r * cells
                for k in range(chunks):
                    source[at : at + cells, k * 128 : (k + 1) * 128] = got_ref[
                        s_f * nr + s_r, k * local + t * cells : k * local + (t + 1) * cells, :
                    ]
    products[...] = lax.dot_general(
        weights[...].reshape(28 * sub, plan.channels),
        source[...],
        (((1,), (1,)), ((), ())),
        preferred_element_type=jnp.float32,
    )
    packed = by_frame_device(plan, got_ref, chunks * local + sub, 8)
    merged = one_hot_dot(packed, order[...], ((1,), (0,)))
    values = jnp.concatenate(in_places(plan, merged, 8), axis=0)
    gain, bias = columns[0][:, 0:1], columns[1][:, 0:1]
    entries = plan.places * plan.group_width
    normed, slope, inv_std = normalised([values], gain, bias, entries, plan.group_width)
    lane, has_left, has_right, has_up, has_down = plan.place_masks()
    by_col = []
    for col in range(3):
        parts = [frame_sum(products, 3 * row + col, sub, lane, plan.places, plan.image) for row in range(3)]
        by_col.append(parts[1] + moved(parts[0], plan.w, has_down) + moved(parts[2], -plan.w, has_up))
    conv = by_col[1] + moved(by_col[0], 1, has_right) + moved(by_col[2], -1, has_left)
    cot = products[pl.ds(27 * sub, sub), :]
    grads, one, two = finished([conv], normed, slope, [cot], gain, inv_std, entries, plan.group_width)
    quartered = (grads[0] * 0.25).astype(jnp.bfloat16)
    for dest in range(plan.count):
        out_ref[dest] = quartered
    sums_ref[...] = jnp.concatenate([as_row(one), as_row(two)], axis=0)


def unpack_kernel(plan, got_ref, columns, order, normed_ref, slope_ref, inv_ref):
    sub = plan.sub
    packed = by_frame_device(plan, got_ref, plan.channels // 128 * plan.local, sub)
    parts = in_places(plan, one_hot_dot(packed, order[...], ((1,), (0,))), sub)
    gain, bias = columns[2][:, 0:1], columns[3][:, 0:1]
    entries = 4 * plan.places * plan.group_width
    normed, slope, inv_std = normalised(parts, gain, bias, entries, plan.group_width)
    for pq in range(4):
        normed_ref[pq] = normed[pq]
        slope_ref[pq] = slope[pq]
    inv_ref[...] = jnp.broadcast_to(inv_std, (sub, 128))


def fine_kernel(
    plan, got_ref, normed_ref, slope_ref, inv_ref, columns, order, sums_ref, weights, out_ref, source, products
):
    sub, nr, nf = plan.sub, plan.nr, plan.nf
    f, r = lax.axis_index("frames"), lax.axis_index("rows")
    for s_f in range(nf):
        for s_r in range(nr):
            c = s_r * plan.slice_width + s_f * sub
            source[c : c + sub, :] = got_ref[s_f * nr + s_r]
    gain = columns[2][:, 0:1]
    products[...] = lax.dot_general(
        weights[...].reshape(27 * sub, plan.channels),
        source[...],
        (((1,), (0,)), ((), ())),
        preferred_element_type=jnp.float32,
    )
    lane, has_left, has_right, has_up, has_down = plan.place_masks()
    by_row = []
    for row in range(3):
        a, b, c = [frame_sum(products, 3 * row + col, sub, lane, plan.places, plan.image) for col in range(3)]
        by_row.append((a + b + moved(c, -1, has_left), moved(a, 1, has_right) + b + c))
    convs = [by_row[0][q] + by_row[1][q] + moved(by_row[2][q], -plan.w, has_up) for q in range(2)]
    convs += [moved(by_row[0][q], plan.w, has_down) + by_row[1][q] + by_row[2][q] for q in range(2)]
    cot = got_ref[f * nr + r].astype(jnp.float32)
    entries = 4 * plan.places * plan.group_width
    grads, one, two = finished(
        convs,
        [normed_ref[pq] for pq in range(4)],
        [slope_ref[pq] for pq in range(4)],
        [cot] * 4,
        gain,
        inv_ref[:, 0:1],
        entries,
        plan.group_width,
    )
    width = plan.tl * plan.image
    stacked = jnp.concatenate(
        [
            jnp.concatenate(
                [grads[pq][:, s_f * width : (s_f + 1) * width].astype(jnp.bfloat16) for pq in range(4)], axis=1
            )
            for s_f in range(nf)
        ],
        axis=0,
    )
    sent = one_hot_dot(stacked, order[...], ((1,), (1,))).astype(jnp.bfloat16)
    sums = jnp.concatenate([as_row(one), as_row(two), sums_ref[...]], axis=0)
    top = sums.astype(jnp.bfloat16).astype(jnp.float32)
    coded = jnp.concatenate([top, sums - top], axis=0).astype(jnp.bfloat16)
    for s_f in range(nf):
        for s_r in range(nr):
            out_ref[s_f * nr + s_r, 0:sub, :] = sent[s_f * sub : (s_f + 1) * sub, s_r * 128 : (s_r + 1) * 128]
            out_ref[s_f * nr + s_r, sub : sub + 8, :] = coded


def spread_kernel(plan, scales, got_ref, out_ref, *rest):
    sum_refs, source = rest[:4], rest[4]
    sub, nr, nf = plan.sub, plan.nr, plan.nf
    for s_f in range(nf):
        for s_r in range(nr):
            c = s_r * plan.slice_width + s_f * sub
            source[c : c + sub, :] = got_ref[s_f * nr + s_r, 0:sub, :]
    order = pixel_order(plan.tl, plan.hl, plan.w)
    out_ref[...] = one_hot_dot(order, source[...], ((1,), (1,))).astype(jnp.bfloat16)
    columns = []
    for s_r in range(nr):
        held = 0.0
        for s_f in range(nf):
            coded = got_ref[s_f * nr + s_r, sub : sub + 8, :].astype(jnp.float32)
            sums = coded[0:4] + coded[4:8]
            held = held + (pltpu.roll(sums, s_f * sub, 1) if s_f else sums)
        columns.append(held)
    rows = jnp.concatenate(columns, axis=1)
    for k in range(4):
        sum_refs[k][...] = rows[k : k + 1] * scales[k]


def in_vmem(count):
    return [pl.BlockSpec(memory_space=pltpu.VMEM)] * count


def in_hbm(count):
    return [pl.BlockSpec(memory_space=pltpu.HBM)] * count


def shape_of(shape, kind):
    return jax.ShapeDtypeStruct(shape, kind)


LIMIT = pltpu.CompilerParams(vmem_limit_bytes=40 * 1024 * 1024)


def fast_shards(
    plan,
    acts_fine,
    acts_coarse,
    grad_coarse,
    gain_fine,
    bias_fine,
    kernel_fine,
    gain_coarse,
    bias_coarse,
    kernel_coarse,
):
    nd = lax.axis_size("dp")
    count, sub, channels, places, local = plan.count, plan.sub, plan.channels, plan.places, plan.local
    chunks = channels // 128
    f32, bf16 = jnp.float32, jnp.bfloat16
    packed = pl.pallas_call(
        functools.partial(pack_kernel, plan),
        out_shape=shape_of((count, chunks * local + sub + 8, 128), bf16),
        in_specs=in_hbm(3),
        out_specs=in_vmem(1)[0],
        scratch_shapes=[
            pltpu.VMEM((local, channels), bf16),
            pltpu.VMEM((local, channels), bf16),
            pltpu.VMEM((4 * local, channels), bf16),
            pltpu.SemaphoreType.DMA((3,)),
        ],
        compiler_params=LIMIT,
    )(
        grad_coarse.reshape(local, channels),
        acts_coarse.reshape(local, channels),
        acts_fine.reshape(4 * local, channels),
    )
    got = lax.all_to_all(packed, BLOCK, 0, 0)
    rows = [part.reshape(1, channels) for part in (gain_coarse, bias_coarse, gain_fine, bias_fine)]
    weights_c, weights_f, columns, order = pl.pallas_call(
        functools.partial(stage_kernel, plan),
        out_shape=(
            shape_of((28, sub, channels), bf16),
            shape_of((27, sub, channels), bf16),
            shape_of((4, sub, 128), f32),
            shape_of((4 * plan.nr * local, 4 * plan.nr * local), bf16),
        ),
        in_specs=in_hbm(6),
        out_specs=tuple(in_vmem(4)),
        scratch_shapes=[pltpu.VMEM((4, 1, channels), f32), pltpu.SemaphoreType.DMA((6,))],
        compiler_params=LIMIT,
    )(kernel_coarse, kernel_fine, *rows)
    quartered, coarse_sums = pl.pallas_call(
        functools.partial(coarse_kernel, plan),
        out_shape=(shape_of((count, sub, places), bf16), shape_of((2, 128), f32)),
        in_specs=in_vmem(4),
        out_specs=tuple(in_vmem(2)),
        scratch_shapes=[pltpu.VMEM((places, channels), bf16), pltpu.VMEM((28 * sub, places), f32)],
        compiler_params=LIMIT,
    )(got, weights_c, columns, order)
    spread = lax.all_to_all(quartered, BLOCK, 0, 0)
    normed, slope, inv_std = pl.pallas_call(
        functools.partial(unpack_kernel, plan),
        out_shape=(
            shape_of((4, sub, places), f32),
            shape_of((4, sub, places), f32),
            shape_of((sub, 128), f32),
        ),
        in_specs=in_vmem(3),
        out_specs=tuple(in_vmem(3)),
        compiler_params=LIMIT,
    )(got, columns, order)
    sent = pl.pallas_call(
        functools.partial(fine_kernel, plan),
        out_shape=shape_of((count, sub + 8, 128), bf16),
        in_specs=in_vmem(8),
        out_specs=in_vmem(1)[0],
        scratch_shapes=[pltpu.VMEM((channels, places), bf16), pltpu.VMEM((27 * sub, places), f32)],
        compiler_params=LIMIT,
    )(spread, normed, slope, inv_std, columns, order, coarse_sums, weights_f)
    back = lax.all_to_all(sent, BLOCK, 0, 0)
    cells = nd * places
    fine_scale, coarse_scale = 1.0 / math.sqrt(4 * cells), 1.0 / math.sqrt(cells)
    out, *sums = pl.pallas_call(
        functools.partial(spread_kernel, plan, (fine_scale, fine_scale, coarse_scale, coarse_scale)),
        out_shape=(shape_of((4 * local, channels), bf16),) + (shape_of((1, channels), f32),) * 4,
        in_specs=in_vmem(1),
        out_specs=tuple(in_vmem(5)),
        scratch_shapes=[pltpu.VMEM((channels, 4 * local), bf16)],
        compiler_params=LIMIT,
    )(back)
    bias_f, gain_f, bias_c, gain_c = lax.psum(tuple(part.reshape(channels) for part in sums), "dp")
    return out.reshape(acts_fine.shape), gain_f, bias_f, gain_c, bias_c


def solution(mesh):
    def shards(*arrays):
        sizes = (lax.axis_size("frames"), lax.axis_size("rows"))
        plan = Plan(sizes, arrays[1].shape[1:], arrays[5].shape[1])
        if plan.fits:
            return fast_shards(plan, *arrays)
        return plain_shards(*arrays)

    in_specs = (
        P("dp", "frames", "rows", None, None),
        P("dp", "frames", "rows", None, None),
        P("dp", "frames", "rows", None, None),
        P(),
        P(),
        P(None, "rows", None),
        P(),
        P(),
        P(None, "rows", None),
    )
    out_specs = (P("dp", "frames", "rows", None, None), P(), P(), P(), P())
    return jax.shard_map(shards, mesh=mesh, in_specs=in_specs, out_specs=out_specs, check_vma=False)
```

```python
import functools
import math

import jax
import jax.numpy as jnp
from jax import lax
from jax.experimental import pallas as pl
from jax.experimental.pallas import tpu as pltpu
from jax.sharding import PartitionSpec as P

GROUPS = 32
EPSILON = 1e-06
BLOCK = ("frames", "rows")


def to_everyone(block, count):
    copies = jnp.broadcast_to(block[None], (count,) + block.shape)
    return lax.all_to_all(copies, BLOCK, 0, 0)


def ahead(field, axis, distance):
    size = field.shape[axis]
    if distance == 0:
        return field
    widths = [(0, 0)] * field.ndim
    if distance > 0:
        widths[axis] = (0, distance)
        kept = lax.slice_in_dim(field, distance, size, axis=axis)
    else:
        widths[axis] = (-distance, 0)
        kept = lax.slice_in_dim(field, 0, size + distance, axis=axis)
    return jnp.pad(kept, widths)


def tap_products(source, kernel):
    sub = kernel.shape[1]
    frames, rows, cols, channels = source.shape
    products = lax.dot_general(
        kernel.reshape(27 * sub, channels),
        source.reshape(frames * rows * cols, channels),
        (((1,), (1,)), ((), ())),
        preferred_element_type=jnp.float32,
    ).reshape(3, 3, 3, sub, frames, rows, cols)
    return sum(ahead(products[depth], 3, 2 - depth) for depth in range(3))


def coarse_conv(source, kernel):
    spatial = tap_products(source, kernel)
    total = 0.0
    for row in range(3):
        part = sum(ahead(spatial[row, col], 3, 1 - col) for col in range(3))
        total = total + ahead(part, 2, 1 - row)
    return total


def fine_conv(source, kernel):
    spatial = tap_products(source, kernel)
    result = []
    for p in range(2):
        rows_of = []
        for q in range(2):
            total = 0.0
            for row in range(3):
                part = sum(ahead(spatial[row, col], 3, (q + 1 - col) // 2) for col in range(3))
                total = total + ahead(part, 2, (p + 1 - row) // 2)
            rows_of.append(total)
        result.append(jnp.stack(rows_of, 1))
    return jnp.stack(result, 1)


def group_total(sums, group_width):
    sub = sums.shape[-1]
    if sub % group_width == 0:
        grouped = jnp.sum(sums.reshape(-1, sub // group_width, group_width), axis=-1)
        return jnp.repeat(grouped, group_width, axis=-1)
    spread = jnp.moveaxis(lax.all_gather(sums, "frames"), 0, 1).reshape(sums.shape[0], -1, group_width)
    mine = lax.axis_index("frames") * sub // group_width
    grouped = lax.dynamic_index_in_dim(jnp.sum(spread, -1), mine, 1)
    return jnp.broadcast_to(grouped, sums.shape)


def level(acts, conv_grad, cotangent, gain, bias, group_width):
    sub = acts.shape[0]
    places = acts.size // sub
    values = acts.astype(jnp.float32).reshape(sub, places)
    conv_grad = conv_grad.reshape(sub, places)
    entries = places * group_width
    moments = group_total(
        jnp.stack([jnp.sum(values, 1), jnp.sum(values * values, 1)]), group_width
    ) / entries
    mean = moments[0]
    inv_std = lax.rsqrt(moments[1] - mean * mean + EPSILON)
    normed = (values - mean[:, None]) * inv_std[:, None]
    preact = gain[:, None] * normed + bias[:, None]
    squash = jax.nn.sigmoid(preact)
    pre_grad = conv_grad * squash * (1.0 + preact * (1.0 - squash))
    sums = jnp.stack([jnp.sum(pre_grad, 1), jnp.sum(pre_grad * normed, 1)])
    terms = group_total(sums * gain, group_width) / entries
    grad = cotangent.reshape(sub, places) + inv_std[:, None] * (
        gain[:, None] * pre_grad - terms[0][:, None] - normed * terms[1][:, None]
    )
    return grad, sums


def plain_shards(
    acts_fine,
    acts_coarse,
    grad_coarse,
    gain_fine,
    bias_fine,
    kernel_fine,
    gain_coarse,
    bias_coarse,
    kernel_coarse,
):
    nf, nr, nd = lax.axis_size("frames"), lax.axis_size("rows"), lax.axis_size("dp")
    count = nf * nr
    channels = acts_fine.shape[-1]
    slice_width = kernel_fine.shape[1]
    sub = slice_width // nf
    group_width = channels // GROUPS
    tl, hl, w = acts_coarse.shape[1:4]
    frames, rows = tl * nf, hl * nr
    f, r = lax.axis_index("frames"), lax.axis_index("rows")

    gathered = to_everyone(grad_coarse[0], count)
    source = (
        gathered.reshape(nf, nr, tl, hl, w, channels)
        .transpose(0, 2, 1, 3, 4, 5)
        .reshape(frames, rows, w, channels)
    )
    coarse_in = acts_coarse[0].reshape(tl, hl, w, nr, nf, sub).transpose(4, 3, 5, 0, 1, 2)
    coarse_in = lax.all_to_all(coarse_in.reshape(count, sub, tl * hl * w), BLOCK, 0, 0)
    fine_in = acts_fine[0].reshape(tl, hl, 2, w, 2, nr, nf, sub).transpose(6, 5, 7, 2, 4, 0, 1, 3)
    fine_in = lax.all_to_all(fine_in.reshape(count, sub, 4 * tl * hl * w), BLOCK, 0, 0)

    def mine(vector):
        return lax.dynamic_slice_in_dim(vector, r * slice_width + f * sub, sub)

    def own(kernel):
        return lax.dynamic_slice_in_dim(kernel, f * sub, sub, axis=1)

    coarse_vals = (
        coarse_in.reshape(nf, nr, sub, tl, hl, w).transpose(2, 0, 3, 1, 4, 5).reshape(sub, frames, rows, w)
    )
    cot = lax.dynamic_slice_in_dim(source, r * slice_width + f * sub, sub, axis=3)
    cot = cot.astype(jnp.float32).transpose(3, 0, 1, 2)
    conv = coarse_conv(source, own(kernel_coarse))
    coarse_grad, coarse_sums = level(
        coarse_vals, conv, cot, mine(gain_coarse), mine(bias_coarse), group_width
    )
    quartered = (coarse_grad * 0.25).astype(jnp.bfloat16)
    spread = to_everyone(quartered, count)
    source_fine = (
        spread.reshape(nf, nr, sub, frames, rows, w)
        .transpose(3, 4, 5, 1, 0, 2)
        .reshape(frames, rows, w, channels)
    )
    conv = fine_conv(source_fine, own(kernel_fine))
    fine_vals = (
        fine_in.reshape(nf, nr, sub, 2, 2, tl, hl, w)
        .transpose(2, 3, 4, 0, 5, 1, 6, 7)
        .reshape(sub, 2, 2, frames, rows, w)
    )
    cot = jnp.broadcast_to(
        quartered.astype(jnp.float32).reshape(sub, 1, 1, frames, rows, w), conv.shape
    )
    fine_grad, fine_sums = level(
        fine_vals, conv, cot, mine(gain_fine), mine(bias_fine), group_width
    )
    back = (
        fine_grad.astype(jnp.bfloat16)
        .reshape(sub, 2, 2, nf, tl, nr, hl, w)
        .transpose(3, 5, 0, 1, 2, 4, 6, 7)
        .reshape(count, sub, 4 * tl * hl * w)
    )
    sums = to_everyone(jnp.concatenate([fine_sums, coarse_sums]), count)
    back = lax.all_to_all(back, BLOCK, 0, 0)
    out = (
        back.reshape(nf, nr, sub, 2, 2, tl, hl, w)
        .transpose(5, 6, 3, 7, 4, 1, 0, 2)
        .reshape(1, tl, 2 * hl, 2 * w, channels)
    )
    sums = sums.reshape(nf, nr, 4, sub).transpose(2, 1, 0, 3).reshape(4, channels)
    totals = lax.psum(sums, "dp")
    cells = nd * frames * rows * w
    scale_fine = 1.0 / jnp.sqrt(jnp.float32(4 * cells))
    scale_coarse = 1.0 / jnp.sqrt(jnp.float32(cells))
    return (
        out,
        totals[1] * scale_fine,
        totals[0] * scale_fine,
        totals[3] * scale_coarse,
        totals[2] * scale_coarse,
    )


def lanes_at(shape, axis):
    return lax.broadcasted_iota(jnp.int32, shape, axis)


def pixel_order(tl, hl, w):
    size = 4 * tl * hl * w
    lane = lanes_at((size, size), 1)
    j, i, t = lane % w, lane // w % hl, lane // (w * hl) % tl
    q, p = lane // (w * hl * tl) % 2, lane // (2 * w * hl * tl)
    pixel = (t * 2 * hl + 2 * i + p) * 2 * w + 2 * j + q
    return (lanes_at((size, size), 0) == pixel).astype(jnp.float32).astype(jnp.bfloat16)


def merged_order(nr, outer, tl, cells):
    size = nr * outer * tl * cells
    a = lanes_at((size, size), 0)
    cell, t = a % cells, a // cells % tl
    o, dev = a // (cells * tl) % outer, a // (cells * tl * outer)
    target = ((o * tl + t) * nr + dev) * cells + cell
    return (lanes_at((size, size), 1) == target).astype(jnp.float32).astype(jnp.bfloat16)


def one_hot_dot(a, b, dims):
    return lax.dot_general(a, b, (dims, ((), ())), preferred_element_type=jnp.float32)


def moved(field, distance, kept):
    size = field.shape[1]
    return jnp.where(kept, pltpu.roll(field, (-distance) % size, 1), 0.0)


def own_column(row, base, sub):
    shape = (sub, row.shape[1])
    mine = lanes_at(shape, 1) == lanes_at(shape, 0) + base
    return jnp.sum(jnp.where(mine, row, 0.0), axis=1, keepdims=True)


def as_row(column):
    shape = (column.shape[0], 128)
    here = lanes_at(shape, 1) == lanes_at(shape, 0)
    return jnp.sum(jnp.where(here, column, 0.0), axis=0, keepdims=True)


def in_groups(column, group_width):
    sub = column.shape[0]
    grouped = jnp.sum(column.reshape(sub // group_width, group_width, 1), axis=1, keepdims=True)
    return jnp.broadcast_to(grouped, (sub // group_width, group_width, 1)).reshape(sub, 1)


def total(parts):
    return sum(jnp.sum(part, axis=1, keepdims=True) for part in parts)


def normalised(parts, gain, bias, entries, group_width):
    mean = in_groups(total(parts), group_width) / entries
    square = in_groups(total([part * part for part in parts]), group_width) / entries
    inv_std = lax.rsqrt(square - mean * mean + EPSILON)
    normed, slope = [], []
    for part in parts:
        unit = (part - mean) * inv_std
        preact = gain * unit + bias
        squash = jax.nn.sigmoid(preact)
        normed.append(unit)
        slope.append(squash * (1.0 + preact * (1.0 - squash)))
    return normed, slope, inv_std


def finished(convs, normed, slope, cots, gain, inv_std, entries, group_width):
    pre = [conv * part for conv, part in zip(convs, slope)]
    one = total(pre)
    two = total([a * b for a, b in zip(pre, normed)])
    group_one = in_groups(gain * one, group_width) / entries
    group_two = in_groups(gain * two, group_width) / entries
    grads = [
        cot + inv_std * (gain * part - group_one - unit * group_two)
        for cot, part, unit in zip(cots, pre, normed)
    ]
    return grads, one, two


class Plan:
    def __init__(self, mesh_sizes, acts_coarse, slice_width):
        self.nf, self.nr = mesh_sizes
        self.count = self.nf * self.nr
        self.tl, self.hl, self.w, self.channels = acts_coarse
        self.slice_width = slice_width
        self.sub = slice_width // self.nf
        self.cells = self.hl * self.w
        self.local = self.tl * self.cells
        self.image = self.cells * self.nr
        self.frames = self.tl * self.nf
        self.places = self.frames * self.image
        self.group_width = self.channels // GROUPS
        self.fits = (
            self.sub == 32
            and self.group_width == 16
            and self.cells == 16
            and self.tl == 2
            and self.nr == 4
            and self.channels % 128 == 0
            and self.slice_width * self.nr == self.channels
        )

    def place_masks(self):
        lane = lanes_at((1, self.places), 1)
        col, row = lane % self.w, lane // self.w % (self.hl * self.nr)
        last_row = self.hl * self.nr - 1
        return (lane, col > 0, col < self.w - 1, row > 0, row < last_row)


def fetched(pairs, sems):
    copies = [pltpu.make_async_copy(src, dst, sems.at[k]) for k, (src, dst) in enumerate(pairs)]
    for copy in copies:
        copy.start()
    return copies


def pack_kernel(plan, g_hbm, coarse_hbm, fine_hbm, out_hbm, out_ref, g_ref, coarse_ref, fine_ref, sems, out_sems):
    sub, chunks, local = plan.sub, plan.channels // 128, plan.local
    sent = []
    copies = fetched(((fine_hbm, fine_ref), (coarse_hbm, coarse_ref), (g_hbm, g_ref)), sems)
    order = pixel_order(plan.tl, plan.hl, plan.w)
    shape = (local, 128)
    places = [
        (lanes_at(shape, 0) + k * local == lanes_at(shape, 1)).astype(jnp.float32).astype(jnp.bfloat16)
        for k in range(4)
    ]
    copies[0].wait()
    fine = one_hot_dot(fine_ref[...], order, ((0,), (0,))).astype(jnp.bfloat16)
    copies[1].wait()
    quarters = [one_hot_dot(coarse_ref[...], place, ((0,), (0,))) for place in places]
    copies[2].wait()
    for f in range(plan.nf):
        for r in range(plan.nr):
            dest, c = f * plan.nr + r, r * plan.slice_width + f * sub
            for k in range(chunks):
                out_ref[dest, k * local : (k + 1) * local, :] = g_ref[:, k * 128 : (k + 1) * 128]
            at = chunks * local
            out_ref[dest, at : at + sub, :] = fine[c : c + sub]
            coarse = sum(quarters[k][c + 8 * k : c + 8 * k + 8] for k in range(4))
            out_ref[dest, at + sub : at + sub + 8, :] = coarse.astype(jnp.bfloat16)
            sent.append(pltpu.make_async_copy(out_ref.at[dest], out_hbm.at[dest], out_sems.at[dest]))
            sent[-1].start()
    for copy in sent:
        copy.wait()


def stage_kernel(
    plan,
    kernel_c,
    kernel_f,
    gain_c,
    bias_c,
    gain_f,
    bias_f,
    weights_c,
    weights_f,
    columns,
    order,
    rows,
    sems,
):
    sub = plan.sub
    f, r = lax.axis_index("frames"), lax.axis_index("rows")
    base = r * plan.slice_width + f * sub
    own = pl.ds(pl.multiple_of(f * sub, sub), sub)
    copies = fetched(
        [(row, rows.at[k]) for k, row in enumerate((gain_c, bias_c, gain_f, bias_f))]
        + [(kernel_c.at[:, own, :], weights_c.at[pl.ds(0, 27)]), (kernel_f.at[:, own, :], weights_f)],
        sems,
    )
    shape = (sub, plan.channels)
    weights_c[27] = (lanes_at(shape, 1) == lanes_at(shape, 0) + base).astype(jnp.float32).astype(jnp.bfloat16)
    order[...] = merged_order(plan.nr, 4, plan.tl, plan.cells)
    for copy in copies:
        copy.wait()
    for k in range(4):
        columns[k] = jnp.broadcast_to(own_column(rows[k], base, sub), (sub, 128))


def by_frame_device(plan, got_ref, at, height):
    return jnp.concatenate(
        [
            jnp.concatenate(
                [got_ref[f * plan.nr + r, at : at + height, :] for r in range(plan.nr)], axis=1
            )
            for f in range(plan.nf)
        ],
        axis=0,
    )


def in_places(plan, merged, height):
    width = plan.tl * plan.image
    return [
        jnp.concatenate(
            [merged[f * height : (f + 1) * height, k * width : (k + 1) * width] for f in range(plan.nf)],
            axis=1,
        )
        for k in range(4)
    ]


def frame_sum(products_ref, tap, sub, lane, places, image):
    near = products_ref[pl.ds((18 + tap) * sub, sub), :]
    middle = products_ref[pl.ds((9 + tap) * sub, sub), :]
    far = products_ref[pl.ds(tap * sub, sub), :]
    return near + moved(middle, image, lane < places - image) + moved(far, 2 * image, lane < places - 2 * image)


def coarse_kernel(plan, got_ref, weights, columns, order, out_hbm, sums_ref, source, products, out_ref, sems):
    sub, nr, nf, cells, tl, local = plan.sub, plan.nr, plan.nf, plan.cells, plan.tl, plan.local
    chunks = plan.channels // 128
    for s_f in range(nf):
        for s_r in range(nr):
            for t in range(tl):
                at = (s_f * tl + t) * plan.image + s_r * cells
                for k in range(chunks):
                    source[at : at + cells, k * 128 : (k + 1) * 128] = got_ref[
                        s_f * nr + s_r, k * local + t * cells : k * local + (t + 1) * cells, :
                    ]
    products[...] = lax.dot_general(
        weights[...].reshape(28 * sub, plan.channels),
        source[...],
        (((1,), (1,)), ((), ())),
        preferred_element_type=jnp.float32,
    )
    packed = by_frame_device(plan, got_ref, chunks * local + sub, 8)
    merged = one_hot_dot(packed, order[...], ((1,), (0,)))
    values = jnp.concatenate(in_places(plan, merged, 8), axis=0)
    gain, bias = columns[0][:, 0:1], columns[1][:, 0:1]
    entries = plan.places * plan.group_width
    normed, slope, inv_std = normalised([values], gain, bias, entries, plan.group_width)
    lane, has_left, has_right, has_up, has_down = plan.place_masks()
    by_col = []
    for col in range(3):
        parts = [frame_sum(products, 3 * row + col, sub, lane, plan.places, plan.image) for row in range(3)]
        by_col.append(parts[1] + moved(parts[0], plan.w, has_down) + moved(parts[2], -plan.w, has_up))
    conv = by_col[1] + moved(by_col[0], 1, has_right) + moved(by_col[2], -1, has_left)
    cot = products[pl.ds(27 * sub, sub), :]
    grads, one, two = finished([conv], normed, slope, [cot], gain, inv_std, entries, plan.group_width)
    out_ref[...] = (grads[0] * 0.25).astype(jnp.bfloat16)
    copies = fetched([(out_ref, out_hbm.at[dest]) for dest in range(plan.count)], sems)
    sums_ref[...] = jnp.concatenate([as_row(one), as_row(two)], axis=0)
    for copy in copies:
        copy.wait()


def unpack_kernel(plan, got_ref, columns, order, normed_ref, slope_ref, inv_ref):
    sub = plan.sub
    packed = by_frame_device(plan, got_ref, plan.channels // 128 * plan.local, sub)
    parts = in_places(plan, one_hot_dot(packed, order[...], ((1,), (0,))), sub)
    gain, bias = columns[2][:, 0:1], columns[3][:, 0:1]
    entries = 4 * plan.places * plan.group_width
    normed, slope, inv_std = normalised(parts, gain, bias, entries, plan.group_width)
    for pq in range(4):
        normed_ref[pq] = normed[pq]
        slope_ref[pq] = slope[pq]
    inv_ref[...] = jnp.broadcast_to(inv_std, (sub, 128))


def fine_kernel(
    plan, got_ref, normed_ref, slope_ref, inv_ref, columns, order, sums_ref, weights, out_ref, source, products
):
    sub, nr, nf = plan.sub, plan.nr, plan.nf
    f, r = lax.axis_index("frames"), lax.axis_index("rows")
    for s_f in range(nf):
        for s_r in range(nr):
            c = s_r * plan.slice_width + s_f * sub
            source[c : c + sub, :] = got_ref[s_f * nr + s_r]
    gain = columns[2][:, 0:1]
    products[...] = lax.dot_general(
        weights[...].reshape(27 * sub, plan.channels),
        source[...],
        (((1,), (0,)), ((), ())),
        preferred_element_type=jnp.float32,
    )
    lane, has_left, has_right, has_up, has_down = plan.place_masks()
    by_row = []
    for row in range(3):
        a, b, c = [frame_sum(products, 3 * row + col, sub, lane, plan.places, plan.image) for col in range(3)]
        by_row.append((a + b + moved(c, -1, has_left), moved(a, 1, has_right) + b + c))
    convs = [by_row[0][q] + by_row[1][q] + moved(by_row[2][q], -plan.w, has_up) for q in range(2)]
    convs += [moved(by_row[0][q], plan.w, has_down) + by_row[1][q] + by_row[2][q] for q in range(2)]
    cot = got_ref[f * nr + r].astype(jnp.float32)
    entries = 4 * plan.places * plan.group_width
    grads, one, two = finished(
        convs,
        [normed_ref[pq] for pq in range(4)],
        [slope_ref[pq] for pq in range(4)],
        [cot] * 4,
        gain,
        inv_ref[:, 0:1],
        entries,
        plan.group_width,
    )
    width = plan.tl * plan.image
    stacked = jnp.concatenate(
        [
            jnp.concatenate(
                [grads[pq][:, s_f * width : (s_f + 1) * width].astype(jnp.bfloat16) for pq in range(4)], axis=1
            )
            for s_f in range(nf)
        ],
        axis=0,
    )
    sent = one_hot_dot(stacked, order[...], ((1,), (1,))).astype(jnp.bfloat16)
    sums = jnp.concatenate([as_row(one), as_row(two), sums_ref[...]], axis=0)
    top = sums.astype(jnp.bfloat16).astype(jnp.float32)
    coded = jnp.concatenate([top, sums - top], axis=0).astype(jnp.bfloat16)
    for s_f in range(nf):
        for s_r in range(nr):
            out_ref[s_f * nr + s_r, 0:sub, :] = sent[s_f * sub : (s_f + 1) * sub, s_r * 128 : (s_r + 1) * 128]
            out_ref[s_f * nr + s_r, sub : sub + 8, :] = coded


def spread_kernel(plan, scales, got_ref, out_ref, *rest):
    sum_refs, source = rest[:4], rest[4]
    sub, nr, nf = plan.sub, plan.nr, plan.nf
    for s_f in range(nf):
        for s_r in range(nr):
            c = s_r * plan.slice_width + s_f * sub
            source[c : c + sub, :] = got_ref[s_f * nr + s_r, 0:sub, :]
    order = pixel_order(plan.tl, plan.hl, plan.w)
    out_ref[...] = one_hot_dot(order, source[...], ((1,), (1,))).astype(jnp.bfloat16)
    columns = []
    for s_r in range(nr):
        held = 0.0
        for s_f in range(nf):
            coded = got_ref[s_f * nr + s_r, sub : sub + 8, :].astype(jnp.float32)
            sums = coded[0:4] + coded[4:8]
            held = held + (pltpu.roll(sums, s_f * sub, 1) if s_f else sums)
        columns.append(held)
    rows = jnp.concatenate(columns, axis=1)
    for k in range(4):
        sum_refs[k][...] = rows[k : k + 1] * scales[k]


def in_vmem(count):
    return [pl.BlockSpec(memory_space=pltpu.VMEM)] * count


def in_hbm(count):
    return [pl.BlockSpec(memory_space=pltpu.HBM)] * count


def kept(array):
    return pltpu.with_memory_space_constraint(array, pltpu.HBM)


def shape_of(shape, kind):
    return jax.ShapeDtypeStruct(shape, kind)


LIMIT = pltpu.CompilerParams(vmem_limit_bytes=40 * 1024 * 1024)


def fast_shards(
    plan,
    acts_fine,
    acts_coarse,
    grad_coarse,
    gain_fine,
    bias_fine,
    kernel_fine,
    gain_coarse,
    bias_coarse,
    kernel_coarse,
):
    nd = lax.axis_size("dp")
    count, sub, channels, places, local = plan.count, plan.sub, plan.channels, plan.places, plan.local
    chunks = channels // 128
    f32, bf16 = jnp.float32, jnp.bfloat16
    packed = pl.pallas_call(
        functools.partial(pack_kernel, plan),
        out_shape=pltpu.HBM((count, chunks * local + sub + 8, 128), bf16),
        in_specs=in_hbm(3),
        out_specs=in_hbm(1)[0],
        scratch_shapes=[
            pltpu.VMEM((count, chunks * local + sub + 8, 128), bf16),
            pltpu.VMEM((local, channels), bf16),
            pltpu.VMEM((local, channels), bf16),
            pltpu.VMEM((4 * local, channels), bf16),
            pltpu.SemaphoreType.DMA((3,)),
            pltpu.SemaphoreType.DMA((count,)),
        ],
        compiler_params=LIMIT,
    )(
        kept(grad_coarse.reshape(local, channels)),
        kept(acts_coarse.reshape(local, channels)),
        kept(acts_fine.reshape(4 * local, channels)),
    )
    got = lax.all_to_all(packed, BLOCK, 0, 0)
    rows = [kept(part.reshape(1, channels)) for part in (gain_coarse, bias_coarse, gain_fine, bias_fine)]
    weights_c, weights_f, columns, order = pl.pallas_call(
        functools.partial(stage_kernel, plan),
        out_shape=(
            shape_of((28, sub, channels), bf16),
            shape_of((27, sub, channels), bf16),
            shape_of((4, sub, 128), f32),
            shape_of((4 * plan.nr * local, 4 * plan.nr * local), bf16),
        ),
        in_specs=in_hbm(6),
        out_specs=tuple(in_vmem(4)),
        scratch_shapes=[pltpu.VMEM((4, 1, channels), f32), pltpu.SemaphoreType.DMA((6,))],
        compiler_params=LIMIT,
    )(kept(kernel_coarse), kept(kernel_fine), *rows)
    quartered, coarse_sums = pl.pallas_call(
        functools.partial(coarse_kernel, plan),
        out_shape=(pltpu.HBM((count, sub, places), bf16), shape_of((2, 128), f32)),
        in_specs=in_vmem(4),
        out_specs=tuple(in_hbm(1) + in_vmem(1)),
        scratch_shapes=[
            pltpu.VMEM((places, channels), bf16),
            pltpu.VMEM((28 * sub, places), f32),
            pltpu.VMEM((sub, places), bf16),
            pltpu.SemaphoreType.DMA((count,)),
        ],
        compiler_params=LIMIT,
    )(got, weights_c, columns, order)
    spread = lax.all_to_all(quartered, BLOCK, 0, 0)
    normed, slope, inv_std = pl.pallas_call(
        functools.partial(unpack_kernel, plan),
        out_shape=(
            shape_of((4, sub, places), f32),
            shape_of((4, sub, places), f32),
            shape_of((sub, 128), f32),
        ),
        in_specs=in_vmem(3),
        out_specs=tuple(in_vmem(3)),
        compiler_params=LIMIT,
    )(got, columns, order)
    sent = pl.pallas_call(
        functools.partial(fine_kernel, plan),
        out_shape=shape_of((count, sub + 8, 128), bf16),
        in_specs=in_vmem(8),
        out_specs=in_vmem(1)[0],
        scratch_shapes=[pltpu.VMEM((channels, places), bf16), pltpu.VMEM((27 * sub, places), f32)],
        compiler_params=LIMIT,
    )(spread, normed, slope, inv_std, columns, order, coarse_sums, weights_f)
    back = lax.all_to_all(sent, BLOCK, 0, 0)
    cells = nd * places
    fine_scale, coarse_scale = 1.0 / math.sqrt(4 * cells), 1.0 / math.sqrt(cells)
    out, *sums = pl.pallas_call(
        functools.partial(spread_kernel, plan, (fine_scale, fine_scale, coarse_scale, coarse_scale)),
        out_shape=(shape_of((4 * local, channels), bf16),) + (shape_of((1, channels), f32),) * 4,
        in_specs=in_vmem(1),
        out_specs=tuple(in_vmem(5)),
        scratch_shapes=[pltpu.VMEM((channels, 4 * local), bf16)],
        compiler_params=LIMIT,
    )(back)
    bias_f, gain_f, bias_c, gain_c = lax.psum(tuple(part.reshape(channels) for part in sums), "dp")
    return out.reshape(acts_fine.shape), gain_f, bias_f, gain_c, bias_c


def solution(mesh):
    def shards(*arrays):
        sizes = (lax.axis_size("frames"), lax.axis_size("rows"))
        plan = Plan(sizes, arrays[1].shape[1:], arrays[5].shape[1])
        if plan.fits:
            return fast_shards(plan, *arrays)
        return plain_shards(*arrays)

    in_specs = (
        P("dp", "frames", "rows", None, None),
        P("dp", "frames", "rows", None, None),
        P("dp", "frames", "rows", None, None),
        P(),
        P(),
        P(None, "rows", None),
        P(),
        P(),
        P(None, "rows", None),
    )
    out_specs = (P("dp", "frames", "rows", None, None), P(), P(), P(), P())
    return jax.shard_map(shards, mesh=mesh, in_specs=in_specs, out_specs=out_specs, check_vma=False)
```

```python
import functools
import math

import jax
import jax.numpy as jnp
from jax import lax
from jax.experimental import pallas as pl
from jax.experimental.pallas import tpu as pltpu
from jax.sharding import PartitionSpec as P

GROUPS = 32
EPSILON = 1e-06
BLOCK = ("frames", "rows")


def to_everyone(block, count):
    copies = jnp.broadcast_to(block[None], (count,) + block.shape)
    return lax.all_to_all(copies, BLOCK, 0, 0)


def ahead(field, axis, distance):
    size = field.shape[axis]
    if distance == 0:
        return field
    widths = [(0, 0)] * field.ndim
    if distance > 0:
        widths[axis] = (0, distance)
        kept = lax.slice_in_dim(field, distance, size, axis=axis)
    else:
        widths[axis] = (-distance, 0)
        kept = lax.slice_in_dim(field, 0, size + distance, axis=axis)
    return jnp.pad(kept, widths)


def tap_products(source, kernel):
    sub = kernel.shape[1]
    frames, rows, cols, channels = source.shape
    products = lax.dot_general(
        kernel.reshape(27 * sub, channels),
        source.reshape(frames * rows * cols, channels),
        (((1,), (1,)), ((), ())),
        preferred_element_type=jnp.float32,
    ).reshape(3, 3, 3, sub, frames, rows, cols)
    return sum(ahead(products[depth], 3, 2 - depth) for depth in range(3))


def coarse_conv(source, kernel):
    spatial = tap_products(source, kernel)
    total = 0.0
    for row in range(3):
        part = sum(ahead(spatial[row, col], 3, 1 - col) for col in range(3))
        total = total + ahead(part, 2, 1 - row)
    return total


def fine_conv(source, kernel):
    spatial = tap_products(source, kernel)
    result = []
    for p in range(2):
        rows_of = []
        for q in range(2):
            total = 0.0
            for row in range(3):
                part = sum(ahead(spatial[row, col], 3, (q + 1 - col) // 2) for col in range(3))
                total = total + ahead(part, 2, (p + 1 - row) // 2)
            rows_of.append(total)
        result.append(jnp.stack(rows_of, 1))
    return jnp.stack(result, 1)


def group_total(sums, group_width):
    sub = sums.shape[-1]
    if sub % group_width == 0:
        grouped = jnp.sum(sums.reshape(-1, sub // group_width, group_width), axis=-1)
        return jnp.repeat(grouped, group_width, axis=-1)
    spread = jnp.moveaxis(lax.all_gather(sums, "frames"), 0, 1).reshape(sums.shape[0], -1, group_width)
    mine = lax.axis_index("frames") * sub // group_width
    grouped = lax.dynamic_index_in_dim(jnp.sum(spread, -1), mine, 1)
    return jnp.broadcast_to(grouped, sums.shape)


def level(acts, conv_grad, cotangent, gain, bias, group_width):
    sub = acts.shape[0]
    places = acts.size // sub
    values = acts.astype(jnp.float32).reshape(sub, places)
    conv_grad = conv_grad.reshape(sub, places)
    entries = places * group_width
    moments = group_total(
        jnp.stack([jnp.sum(values, 1), jnp.sum(values * values, 1)]), group_width
    ) / entries
    mean = moments[0]
    inv_std = lax.rsqrt(moments[1] - mean * mean + EPSILON)
    normed = (values - mean[:, None]) * inv_std[:, None]
    preact = gain[:, None] * normed + bias[:, None]
    squash = jax.nn.sigmoid(preact)
    pre_grad = conv_grad * squash * (1.0 + preact * (1.0 - squash))
    sums = jnp.stack([jnp.sum(pre_grad, 1), jnp.sum(pre_grad * normed, 1)])
    terms = group_total(sums * gain, group_width) / entries
    grad = cotangent.reshape(sub, places) + inv_std[:, None] * (
        gain[:, None] * pre_grad - terms[0][:, None] - normed * terms[1][:, None]
    )
    return grad, sums


def plain_shards(
    acts_fine,
    acts_coarse,
    grad_coarse,
    gain_fine,
    bias_fine,
    kernel_fine,
    gain_coarse,
    bias_coarse,
    kernel_coarse,
):
    nf, nr, nd = lax.axis_size("frames"), lax.axis_size("rows"), lax.axis_size("dp")
    count = nf * nr
    channels = acts_fine.shape[-1]
    slice_width = kernel_fine.shape[1]
    sub = slice_width // nf
    group_width = channels // GROUPS
    tl, hl, w = acts_coarse.shape[1:4]
    frames, rows = tl * nf, hl * nr
    f, r = lax.axis_index("frames"), lax.axis_index("rows")

    gathered = to_everyone(grad_coarse[0], count)
    source = (
        gathered.reshape(nf, nr, tl, hl, w, channels)
        .transpose(0, 2, 1, 3, 4, 5)
        .reshape(frames, rows, w, channels)
    )
    coarse_in = acts_coarse[0].reshape(tl, hl, w, nr, nf, sub).transpose(4, 3, 5, 0, 1, 2)
    coarse_in = lax.all_to_all(coarse_in.reshape(count, sub, tl * hl * w), BLOCK, 0, 0)
    fine_in = acts_fine[0].reshape(tl, hl, 2, w, 2, nr, nf, sub).transpose(6, 5, 7, 2, 4, 0, 1, 3)
    fine_in = lax.all_to_all(fine_in.reshape(count, sub, 4 * tl * hl * w), BLOCK, 0, 0)

    def mine(vector):
        return lax.dynamic_slice_in_dim(vector, r * slice_width + f * sub, sub)

    def own(kernel):
        return lax.dynamic_slice_in_dim(kernel, f * sub, sub, axis=1)

    coarse_vals = (
        coarse_in.reshape(nf, nr, sub, tl, hl, w).transpose(2, 0, 3, 1, 4, 5).reshape(sub, frames, rows, w)
    )
    cot = lax.dynamic_slice_in_dim(source, r * slice_width + f * sub, sub, axis=3)
    cot = cot.astype(jnp.float32).transpose(3, 0, 1, 2)
    conv = coarse_conv(source, own(kernel_coarse))
    coarse_grad, coarse_sums = level(
        coarse_vals, conv, cot, mine(gain_coarse), mine(bias_coarse), group_width
    )
    quartered = (coarse_grad * 0.25).astype(jnp.bfloat16)
    spread = to_everyone(quartered, count)
    source_fine = (
        spread.reshape(nf, nr, sub, frames, rows, w)
        .transpose(3, 4, 5, 1, 0, 2)
        .reshape(frames, rows, w, channels)
    )
    conv = fine_conv(source_fine, own(kernel_fine))
    fine_vals = (
        fine_in.reshape(nf, nr, sub, 2, 2, tl, hl, w)
        .transpose(2, 3, 4, 0, 5, 1, 6, 7)
        .reshape(sub, 2, 2, frames, rows, w)
    )
    cot = jnp.broadcast_to(
        quartered.astype(jnp.float32).reshape(sub, 1, 1, frames, rows, w), conv.shape
    )
    fine_grad, fine_sums = level(
        fine_vals, conv, cot, mine(gain_fine), mine(bias_fine), group_width
    )
    back = (
        fine_grad.astype(jnp.bfloat16)
        .reshape(sub, 2, 2, nf, tl, nr, hl, w)
        .transpose(3, 5, 0, 1, 2, 4, 6, 7)
        .reshape(count, sub, 4 * tl * hl * w)
    )
    sums = to_everyone(jnp.concatenate([fine_sums, coarse_sums]), count)
    back = lax.all_to_all(back, BLOCK, 0, 0)
    out = (
        back.reshape(nf, nr, sub, 2, 2, tl, hl, w)
        .transpose(5, 6, 3, 7, 4, 1, 0, 2)
        .reshape(1, tl, 2 * hl, 2 * w, channels)
    )
    sums = sums.reshape(nf, nr, 4, sub).transpose(2, 1, 0, 3).reshape(4, channels)
    totals = lax.psum(sums, "dp")
    cells = nd * frames * rows * w
    scale_fine = 1.0 / jnp.sqrt(jnp.float32(4 * cells))
    scale_coarse = 1.0 / jnp.sqrt(jnp.float32(cells))
    return (
        out,
        totals[1] * scale_fine,
        totals[0] * scale_fine,
        totals[3] * scale_coarse,
        totals[2] * scale_coarse,
    )


def lanes_at(shape, axis):
    return lax.broadcasted_iota(jnp.int32, shape, axis)


def pixel_order(tl, hl, w):
    size = 4 * tl * hl * w
    lane = lanes_at((size, size), 1)
    j, i, t = lane % w, lane // w % hl, lane // (w * hl) % tl
    q, p = lane // (w * hl * tl) % 2, lane // (2 * w * hl * tl)
    pixel = (t * 2 * hl + 2 * i + p) * 2 * w + 2 * j + q
    return (lanes_at((size, size), 0) == pixel).astype(jnp.float32).astype(jnp.bfloat16)


def merged_order(nr, outer, tl, cells):
    size = nr * outer * tl * cells
    a = lanes_at((size, size), 0)
    cell, t = a % cells, a // cells % tl
    o, dev = a // (cells * tl) % outer, a // (cells * tl * outer)
    target = ((o * tl + t) * nr + dev) * cells + cell
    return (lanes_at((size, size), 1) == target).astype(jnp.float32).astype(jnp.bfloat16)


def one_hot_dot(a, b, dims):
    return lax.dot_general(a, b, (dims, ((), ())), preferred_element_type=jnp.float32)


def moved(field, distance, kept):
    size = field.shape[1]
    return jnp.where(kept, pltpu.roll(field, (-distance) % size, 1), 0.0)


def own_column(row, base, sub):
    shape = (sub, row.shape[1])
    mine = lanes_at(shape, 1) == lanes_at(shape, 0) + base
    return jnp.sum(jnp.where(mine, row, 0.0), axis=1, keepdims=True)


def as_row(column):
    shape = (column.shape[0], 128)
    here = lanes_at(shape, 1) == lanes_at(shape, 0)
    return jnp.sum(jnp.where(here, column, 0.0), axis=0, keepdims=True)


def in_groups(column, group_width):
    sub = column.shape[0]
    grouped = jnp.sum(column.reshape(sub // group_width, group_width, 1), axis=1, keepdims=True)
    return jnp.broadcast_to(grouped, (sub // group_width, group_width, 1)).reshape(sub, 1)


def total(parts):
    return sum(jnp.sum(part, axis=1, keepdims=True) for part in parts)


def normalised(parts, gain, bias, entries, group_width):
    mean = in_groups(total(parts), group_width) / entries
    square = in_groups(total([part * part for part in parts]), group_width) / entries
    inv_std = lax.rsqrt(square - mean * mean + EPSILON)
    normed, slope = [], []
    for part in parts:
        unit = (part - mean) * inv_std
        preact = gain * unit + bias
        squash = jax.nn.sigmoid(preact)
        normed.append(unit)
        slope.append(squash * (1.0 + preact * (1.0 - squash)))
    return normed, slope, inv_std


def finished(convs, normed, slope, cots, gain, inv_std, entries, group_width):
    pre = [conv * part for conv, part in zip(convs, slope)]
    one = total(pre)
    two = total([a * b for a, b in zip(pre, normed)])
    group_one = in_groups(gain * one, group_width) / entries
    group_two = in_groups(gain * two, group_width) / entries
    grads = [
        cot + inv_std * (gain * part - group_one - unit * group_two)
        for cot, part, unit in zip(cots, pre, normed)
    ]
    return grads, one, two


class Plan:
    def __init__(self, mesh_sizes, acts_coarse, slice_width):
        self.nf, self.nr = mesh_sizes
        self.count = self.nf * self.nr
        self.tl, self.hl, self.w, self.channels = acts_coarse
        self.slice_width = slice_width
        self.sub = slice_width // self.nf
        self.cells = self.hl * self.w
        self.local = self.tl * self.cells
        self.image = self.cells * self.nr
        self.frames = self.tl * self.nf
        self.places = self.frames * self.image
        self.group_width = self.channels // GROUPS
        self.fits = (
            self.sub == 32
            and self.group_width == 16
            and self.cells == 16
            and self.tl == 2
            and self.nr == 4
            and self.channels % 128 == 0
            and self.slice_width * self.nr == self.channels
        )

    def place_masks(self):
        lane = lanes_at((1, self.places), 1)
        col, row = lane % self.w, lane // self.w % (self.hl * self.nr)
        last_row = self.hl * self.nr - 1
        return (lane, col > 0, col < self.w - 1, row > 0, row < last_row)


def fetched(pairs, sems):
    copies = [pltpu.make_async_copy(src, dst, sems.at[k]) for k, (src, dst) in enumerate(pairs)]
    for copy in copies:
        copy.start()
    return copies


def pack_kernel(plan, g_hbm, coarse_hbm, fine_hbm, out_hbm, out_ref, g_ref, coarse_ref, fine_ref, sems, out_sems):
    sub, chunks, local = plan.sub, plan.channels // 128, plan.local
    sent = []
    copies = fetched(((fine_hbm, fine_ref), (coarse_hbm, coarse_ref), (g_hbm, g_ref)), sems)
    order = pixel_order(plan.tl, plan.hl, plan.w)
    shape = (local, 128)
    places = [
        (lanes_at(shape, 0) + k * local == lanes_at(shape, 1)).astype(jnp.float32).astype(jnp.bfloat16)
        for k in range(4)
    ]
    copies[0].wait()
    fine = one_hot_dot(fine_ref[...], order, ((0,), (0,))).astype(jnp.bfloat16)
    copies[1].wait()
    quarters = [one_hot_dot(coarse_ref[...], place, ((0,), (0,))) for place in places]
    copies[2].wait()
    for f in range(plan.nf):
        for r in range(plan.nr):
            dest, c = f * plan.nr + r, r * plan.slice_width + f * sub
            for k in range(chunks):
                out_ref[dest, k * local : (k + 1) * local, :] = g_ref[:, k * 128 : (k + 1) * 128]
            at = chunks * local
            out_ref[dest, at : at + sub, :] = fine[c : c + sub]
            coarse = sum(quarters[k][c + 8 * k : c + 8 * k + 8] for k in range(4))
            out_ref[dest, at + sub : at + sub + 8, :] = coarse.astype(jnp.bfloat16)
            sent.append(pltpu.make_async_copy(out_ref.at[dest], out_hbm.at[dest], out_sems.at[dest]))
            sent[-1].start()
    for copy in sent:
        copy.wait()


def stage_kernel(
    plan,
    kernel_c,
    kernel_f,
    gain_c,
    bias_c,
    gain_f,
    bias_f,
    weights_c,
    weights_f,
    columns,
    order,
    rows,
    sems,
):
    sub = plan.sub
    f, r = lax.axis_index("frames"), lax.axis_index("rows")
    base = r * plan.slice_width + f * sub
    own = pl.ds(pl.multiple_of(f * sub, sub), sub)
    copies = fetched(
        [(row, rows.at[k]) for k, row in enumerate((gain_c, bias_c, gain_f, bias_f))]
        + [(kernel_c.at[:, own, :], weights_c.at[pl.ds(0, 27)]), (kernel_f.at[:, own, :], weights_f)],
        sems,
    )
    shape = (sub, plan.channels)
    weights_c[27] = (lanes_at(shape, 1) == lanes_at(shape, 0) + base).astype(jnp.float32).astype(jnp.bfloat16)
    order[...] = merged_order(plan.nr, 4, plan.tl, plan.cells)
    for copy in copies:
        copy.wait()
    for k in range(4):
        columns[k] = jnp.broadcast_to(own_column(rows[k], base, sub), (sub, 128))


def by_frame_device(plan, got_ref, at, height):
    return jnp.concatenate(
        [
            jnp.concatenate(
                [got_ref[f * plan.nr + r, at : at + height, :] for r in range(plan.nr)], axis=1
            )
            for f in range(plan.nf)
        ],
        axis=0,
    )


def in_places(plan, merged, height):
    width = plan.tl * plan.image
    return [
        jnp.concatenate(
            [merged[f * height : (f + 1) * height, k * width : (k + 1) * width] for f in range(plan.nf)],
            axis=1,
        )
        for k in range(4)
    ]


def frame_sum(products_ref, tap, sub, lane, places, image):
    near = products_ref[pl.ds((18 + tap) * sub, sub), :]
    middle = products_ref[pl.ds((9 + tap) * sub, sub), :]
    far = products_ref[pl.ds(tap * sub, sub), :]
    return near + moved(middle, image, lane < places - image) + moved(far, 2 * image, lane < places - 2 * image)


def coarse_kernel(plan, got_ref, weights, columns, order, out_ref, sums_ref, source, products):
    sub, nr, nf, cells, tl, local = plan.sub, plan.nr, plan.nf, plan.cells, plan.tl, plan.local
    chunks = plan.channels // 128
    for s_f in range(nf):
        for s_r in range(nr):
            for t in range(tl):
                at = (s_f * tl + t) * plan.image + s_r * cells
                for k in range(chunks):
                    source[at : at + cells, k * 128 : (k + 1) * 128] = got_ref[
                        s_f * nr + s_r, k * local + t * cells : k * local + (t + 1) * cells, :
                    ]
    products[...] = lax.dot_general(
        weights[...].reshape(28 * sub, plan.channels),
        source[...],
        (((1,), (1,)), ((), ())),
        preferred_element_type=jnp.float32,
    )
    packed = by_frame_device(plan, got_ref, chunks * local + sub, 8)
    merged = one_hot_dot(packed, order[...], ((1,), (0,)))
    values = jnp.concatenate(in_places(plan, merged, 8), axis=0)
    gain, bias = columns[0][:, 0:1], columns[1][:, 0:1]
    entries = plan.places * plan.group_width
    normed, slope, inv_std = normalised([values], gain, bias, entries, plan.group_width)
    lane, has_left, has_right, has_up, has_down = plan.place_masks()
    by_col = []
    for col in range(3):
        parts = [frame_sum(products, 3 * row + col, sub, lane, plan.places, plan.image) for row in range(3)]
        by_col.append(parts[1] + moved(parts[0], plan.w, has_down) + moved(parts[2], -plan.w, has_up))
    conv = by_col[1] + moved(by_col[0], 1, has_right) + moved(by_col[2], -1, has_left)
    cot = products[pl.ds(27 * sub, sub), :]
    grads, one, two = finished([conv], normed, slope, [cot], gain, inv_std, entries, plan.group_width)
    out_ref[...] = (grads[0] * 0.25).astype(jnp.bfloat16)
    sums_ref[...] = jnp.concatenate([as_row(one), as_row(two)], axis=0)


def unpack_kernel(plan, got_ref, columns, order, normed_ref, slope_ref, inv_ref):
    sub = plan.sub
    packed = by_frame_device(plan, got_ref, plan.channels // 128 * plan.local, sub)
    parts = in_places(plan, one_hot_dot(packed, order[...], ((1,), (0,))), sub)
    gain, bias = columns[2][:, 0:1], columns[3][:, 0:1]
    entries = 4 * plan.places * plan.group_width
    normed, slope, inv_std = normalised(parts, gain, bias, entries, plan.group_width)
    for pq in range(4):
        normed_ref[pq] = normed[pq]
        slope_ref[pq] = slope[pq]
    inv_ref[...] = jnp.broadcast_to(inv_std, (sub, 128))


def fine_kernel(
    plan, got_ref, normed_ref, slope_ref, inv_ref, columns, order, sums_ref, weights, out_ref, source, products
):
    sub, nr, nf = plan.sub, plan.nr, plan.nf
    f, r = lax.axis_index("frames"), lax.axis_index("rows")
    for s_f in range(nf):
        for s_r in range(nr):
            c = s_r * plan.slice_width + s_f * sub
            source[c : c + sub, :] = got_ref[s_f * nr + s_r]
    gain = columns[2][:, 0:1]
    products[...] = lax.dot_general(
        weights[...].reshape(27 * sub, plan.channels),
        source[...],
        (((1,), (0,)), ((), ())),
        preferred_element_type=jnp.float32,
    )
    lane, has_left, has_right, has_up, has_down = plan.place_masks()
    by_row = []
    for row in range(3):
        a, b, c = [frame_sum(products, 3 * row + col, sub, lane, plan.places, plan.image) for col in range(3)]
        by_row.append((a + b + moved(c, -1, has_left), moved(a, 1, has_right) + b + c))
    convs = [by_row[0][q] + by_row[1][q] + moved(by_row[2][q], -plan.w, has_up) for q in range(2)]
    convs += [moved(by_row[0][q], plan.w, has_down) + by_row[1][q] + by_row[2][q] for q in range(2)]
    cot = got_ref[f * nr + r].astype(jnp.float32)
    entries = 4 * plan.places * plan.group_width
    grads, one, two = finished(
        convs,
        [normed_ref[pq] for pq in range(4)],
        [slope_ref[pq] for pq in range(4)],
        [cot] * 4,
        gain,
        inv_ref[:, 0:1],
        entries,
        plan.group_width,
    )
    width = plan.tl * plan.image
    stacked = jnp.concatenate(
        [
            jnp.concatenate(
                [grads[pq][:, s_f * width : (s_f + 1) * width].astype(jnp.bfloat16) for pq in range(4)], axis=1
            )
            for s_f in range(nf)
        ],
        axis=0,
    )
    sent = one_hot_dot(stacked, order[...], ((1,), (1,))).astype(jnp.bfloat16)
    sums = jnp.concatenate([as_row(one), as_row(two), sums_ref[...]], axis=0)
    top = sums.astype(jnp.bfloat16).astype(jnp.float32)
    coded = jnp.concatenate([top, sums - top], axis=0).astype(jnp.bfloat16)
    for s_f in range(nf):
        for s_r in range(nr):
            out_ref[s_f * nr + s_r, 0:sub, :] = sent[s_f * sub : (s_f + 1) * sub, s_r * 128 : (s_r + 1) * 128]
            out_ref[s_f * nr + s_r, sub : sub + 8, :] = coded


def spread_kernel(plan, scales, got_ref, out_ref, *rest):
    sum_refs, source = rest[:4], rest[4]
    sub, nr, nf = plan.sub, plan.nr, plan.nf
    for s_f in range(nf):
        for s_r in range(nr):
            c = s_r * plan.slice_width + s_f * sub
            source[c : c + sub, :] = got_ref[s_f * nr + s_r, 0:sub, :]
    order = pixel_order(plan.tl, plan.hl, plan.w)
    out_ref[...] = one_hot_dot(order, source[...], ((1,), (1,))).astype(jnp.bfloat16)
    columns = []
    for s_r in range(nr):
        held = 0.0
        for s_f in range(nf):
            coded = got_ref[s_f * nr + s_r, sub : sub + 8, :].astype(jnp.float32)
            sums = coded[0:4] + coded[4:8]
            held = held + (pltpu.roll(sums, s_f * sub, 1) if s_f else sums)
        columns.append(held)
    rows = jnp.concatenate(columns, axis=1)
    for k in range(4):
        sum_refs[k][...] = rows[k : k + 1] * scales[k]


def in_vmem(count):
    return [pl.BlockSpec(memory_space=pltpu.VMEM)] * count


def in_hbm(count):
    return [pl.BlockSpec(memory_space=pltpu.HBM)] * count


def kept(array):
    return pltpu.with_memory_space_constraint(array, pltpu.HBM)


def shape_of(shape, kind):
    return jax.ShapeDtypeStruct(shape, kind)


LIMIT = pltpu.CompilerParams(vmem_limit_bytes=40 * 1024 * 1024)


def fast_shards(
    plan,
    acts_fine,
    acts_coarse,
    grad_coarse,
    gain_fine,
    bias_fine,
    kernel_fine,
    gain_coarse,
    bias_coarse,
    kernel_coarse,
):
    nd = lax.axis_size("dp")
    count, sub, channels, places, local = plan.count, plan.sub, plan.channels, plan.places, plan.local
    chunks = channels // 128
    f32, bf16 = jnp.float32, jnp.bfloat16
    packed = pl.pallas_call(
        functools.partial(pack_kernel, plan),
        out_shape=pltpu.HBM((count, chunks * local + sub + 8, 128), bf16),
        in_specs=in_hbm(3),
        out_specs=in_hbm(1)[0],
        scratch_shapes=[
            pltpu.VMEM((count, chunks * local + sub + 8, 128), bf16),
            pltpu.VMEM((local, channels), bf16),
            pltpu.VMEM((local, channels), bf16),
            pltpu.VMEM((4 * local, channels), bf16),
            pltpu.SemaphoreType.DMA((3,)),
            pltpu.SemaphoreType.DMA((count,)),
        ],
        compiler_params=LIMIT,
    )(
        kept(grad_coarse.reshape(local, channels)),
        kept(acts_coarse.reshape(local, channels)),
        kept(acts_fine.reshape(4 * local, channels)),
    )
    got = lax.all_to_all(packed, BLOCK, 0, 0)
    rows = [kept(part.reshape(1, channels)) for part in (gain_coarse, bias_coarse, gain_fine, bias_fine)]
    weights_c, weights_f, columns, order = pl.pallas_call(
        functools.partial(stage_kernel, plan),
        out_shape=(
            shape_of((28, sub, channels), bf16),
            shape_of((27, sub, channels), bf16),
            shape_of((4, sub, 128), f32),
            shape_of((4 * plan.nr * local, 4 * plan.nr * local), bf16),
        ),
        in_specs=in_hbm(6),
        out_specs=tuple(in_vmem(4)),
        scratch_shapes=[pltpu.VMEM((4, 1, channels), f32), pltpu.SemaphoreType.DMA((6,))],
        compiler_params=LIMIT,
    )(kept(kernel_coarse), kept(kernel_fine), *rows)
    quartered, coarse_sums = pl.pallas_call(
        functools.partial(coarse_kernel, plan),
        out_shape=(shape_of((sub, places), bf16), shape_of((2, 128), f32)),
        in_specs=in_vmem(4),
        out_specs=tuple(in_vmem(2)),
        scratch_shapes=[pltpu.VMEM((places, channels), bf16), pltpu.VMEM((28 * sub, places), f32)],
        compiler_params=LIMIT,
    )(got, weights_c, columns, order)
    spread = lax.all_gather(quartered, BLOCK)
    normed, slope, inv_std = pl.pallas_call(
        functools.partial(unpack_kernel, plan),
        out_shape=(
            shape_of((4, sub, places), f32),
            shape_of((4, sub, places), f32),
            shape_of((sub, 128), f32),
        ),
        in_specs=in_vmem(3),
        out_specs=tuple(in_vmem(3)),
        compiler_params=LIMIT,
    )(got, columns, order)
    sent = pl.pallas_call(
        functools.partial(fine_kernel, plan),
        out_shape=shape_of((count, sub + 8, 128), bf16),
        in_specs=in_vmem(8),
        out_specs=in_vmem(1)[0],
        scratch_shapes=[pltpu.VMEM((channels, places), bf16), pltpu.VMEM((27 * sub, places), f32)],
        compiler_params=LIMIT,
    )(spread, normed, slope, inv_std, columns, order, coarse_sums, weights_f)
    back = lax.all_to_all(sent, BLOCK, 0, 0)
    cells = nd * places
    fine_scale, coarse_scale = 1.0 / math.sqrt(4 * cells), 1.0 / math.sqrt(cells)
    out, *sums = pl.pallas_call(
        functools.partial(spread_kernel, plan, (fine_scale, fine_scale, coarse_scale, coarse_scale)),
        out_shape=(shape_of((4 * local, channels), bf16),) + (shape_of((1, channels), f32),) * 4,
        in_specs=in_vmem(1),
        out_specs=tuple(in_vmem(5)),
        scratch_shapes=[pltpu.VMEM((channels, 4 * local), bf16)],
        compiler_params=LIMIT,
    )(back)
    bias_f, gain_f, bias_c, gain_c = lax.psum(tuple(part.reshape(channels) for part in sums), "dp")
    return out.reshape(acts_fine.shape), gain_f, bias_f, gain_c, bias_c


def solution(mesh):
    def shards(*arrays):
        sizes = (lax.axis_size("frames"), lax.axis_size("rows"))
        plan = Plan(sizes, arrays[1].shape[1:], arrays[5].shape[1])
        if plan.fits:
            return fast_shards(plan, *arrays)
        return plain_shards(*arrays)

    in_specs = (
        P("dp", "frames", "rows", None, None),
        P("dp", "frames", "rows", None, None),
        P("dp", "frames", "rows", None, None),
        P(),
        P(),
        P(None, "rows", None),
        P(),
        P(),
        P(None, "rows", None),
    )
    out_specs = (P("dp", "frames", "rows", None, None), P(), P(), P(), P())
    return jax.shard_map(shards, mesh=mesh, in_specs=in_specs, out_specs=out_specs, check_vma=False)
```

```python
import functools
import math

import jax
import jax.numpy as jnp
from jax import lax
from jax.experimental import pallas as pl
from jax.experimental.pallas import tpu as pltpu
from jax.sharding import PartitionSpec as P

GROUPS = 32
EPSILON = 1e-06
BLOCK = ("frames", "rows")


def to_everyone(block, count):
    copies = jnp.broadcast_to(block[None], (count,) + block.shape)
    return lax.all_to_all(copies, BLOCK, 0, 0)


def ahead(field, axis, distance):
    size = field.shape[axis]
    if distance == 0:
        return field
    widths = [(0, 0)] * field.ndim
    if distance > 0:
        widths[axis] = (0, distance)
        kept = lax.slice_in_dim(field, distance, size, axis=axis)
    else:
        widths[axis] = (-distance, 0)
        kept = lax.slice_in_dim(field, 0, size + distance, axis=axis)
    return jnp.pad(kept, widths)


def tap_products(source, kernel):
    sub = kernel.shape[1]
    frames, rows, cols, channels = source.shape
    products = lax.dot_general(
        kernel.reshape(27 * sub, channels),
        source.reshape(frames * rows * cols, channels),
        (((1,), (1,)), ((), ())),
        preferred_element_type=jnp.float32,
    ).reshape(3, 3, 3, sub, frames, rows, cols)
    return sum(ahead(products[depth], 3, 2 - depth) for depth in range(3))


def coarse_conv(source, kernel):
    spatial = tap_products(source, kernel)
    total = 0.0
    for row in range(3):
        part = sum(ahead(spatial[row, col], 3, 1 - col) for col in range(3))
        total = total + ahead(part, 2, 1 - row)
    return total


def fine_conv(source, kernel):
    spatial = tap_products(source, kernel)
    result = []
    for p in range(2):
        rows_of = []
        for q in range(2):
            total = 0.0
            for row in range(3):
                part = sum(ahead(spatial[row, col], 3, (q + 1 - col) // 2) for col in range(3))
                total = total + ahead(part, 2, (p + 1 - row) // 2)
            rows_of.append(total)
        result.append(jnp.stack(rows_of, 1))
    return jnp.stack(result, 1)


def group_total(sums, group_width):
    sub = sums.shape[-1]
    if sub % group_width == 0:
        grouped = jnp.sum(sums.reshape(-1, sub // group_width, group_width), axis=-1)
        return jnp.repeat(grouped, group_width, axis=-1)
    spread = jnp.moveaxis(lax.all_gather(sums, "frames"), 0, 1).reshape(sums.shape[0], -1, group_width)
    mine = lax.axis_index("frames") * sub // group_width
    grouped = lax.dynamic_index_in_dim(jnp.sum(spread, -1), mine, 1)
    return jnp.broadcast_to(grouped, sums.shape)


def level(acts, conv_grad, cotangent, gain, bias, group_width):
    sub = acts.shape[0]
    places = acts.size // sub
    values = acts.astype(jnp.float32).reshape(sub, places)
    conv_grad = conv_grad.reshape(sub, places)
    entries = places * group_width
    moments = group_total(
        jnp.stack([jnp.sum(values, 1), jnp.sum(values * values, 1)]), group_width
    ) / entries
    mean = moments[0]
    inv_std = lax.rsqrt(moments[1] - mean * mean + EPSILON)
    normed = (values - mean[:, None]) * inv_std[:, None]
    preact = gain[:, None] * normed + bias[:, None]
    squash = jax.nn.sigmoid(preact)
    pre_grad = conv_grad * squash * (1.0 + preact * (1.0 - squash))
    sums = jnp.stack([jnp.sum(pre_grad, 1), jnp.sum(pre_grad * normed, 1)])
    terms = group_total(sums * gain, group_width) / entries
    grad = cotangent.reshape(sub, places) + inv_std[:, None] * (
        gain[:, None] * pre_grad - terms[0][:, None] - normed * terms[1][:, None]
    )
    return grad, sums


def plain_shards(
    acts_fine,
    acts_coarse,
    grad_coarse,
    gain_fine,
    bias_fine,
    kernel_fine,
    gain_coarse,
    bias_coarse,
    kernel_coarse,
):
    nf, nr, nd = lax.axis_size("frames"), lax.axis_size("rows"), lax.axis_size("dp")
    count = nf * nr
    channels = acts_fine.shape[-1]
    slice_width = kernel_fine.shape[1]
    sub = slice_width // nf
    group_width = channels // GROUPS
    tl, hl, w = acts_coarse.shape[1:4]
    frames, rows = tl * nf, hl * nr
    f, r = lax.axis_index("frames"), lax.axis_index("rows")

    gathered = to_everyone(grad_coarse[0], count)
    source = (
        gathered.reshape(nf, nr, tl, hl, w, channels)
        .transpose(0, 2, 1, 3, 4, 5)
        .reshape(frames, rows, w, channels)
    )
    coarse_in = acts_coarse[0].reshape(tl, hl, w, nr, nf, sub).transpose(4, 3, 5, 0, 1, 2)
    coarse_in = lax.all_to_all(coarse_in.reshape(count, sub, tl * hl * w), BLOCK, 0, 0)
    fine_in = acts_fine[0].reshape(tl, hl, 2, w, 2, nr, nf, sub).transpose(6, 5, 7, 2, 4, 0, 1, 3)
    fine_in = lax.all_to_all(fine_in.reshape(count, sub, 4 * tl * hl * w), BLOCK, 0, 0)

    def mine(vector):
        return lax.dynamic_slice_in_dim(vector, r * slice_width + f * sub, sub)

    def own(kernel):
        return lax.dynamic_slice_in_dim(kernel, f * sub, sub, axis=1)

    coarse_vals = (
        coarse_in.reshape(nf, nr, sub, tl, hl, w).transpose(2, 0, 3, 1, 4, 5).reshape(sub, frames, rows, w)
    )
    cot = lax.dynamic_slice_in_dim(source, r * slice_width + f * sub, sub, axis=3)
    cot = cot.astype(jnp.float32).transpose(3, 0, 1, 2)
    conv = coarse_conv(source, own(kernel_coarse))
    coarse_grad, coarse_sums = level(
        coarse_vals, conv, cot, mine(gain_coarse), mine(bias_coarse), group_width
    )
    quartered = (coarse_grad * 0.25).astype(jnp.bfloat16)
    spread = to_everyone(quartered, count)
    source_fine = (
        spread.reshape(nf, nr, sub, frames, rows, w)
        .transpose(3, 4, 5, 1, 0, 2)
        .reshape(frames, rows, w, channels)
    )
    conv = fine_conv(source_fine, own(kernel_fine))
    fine_vals = (
        fine_in.reshape(nf, nr, sub, 2, 2, tl, hl, w)
        .transpose(2, 3, 4, 0, 5, 1, 6, 7)
        .reshape(sub, 2, 2, frames, rows, w)
    )
    cot = jnp.broadcast_to(
        quartered.astype(jnp.float32).reshape(sub, 1, 1, frames, rows, w), conv.shape
    )
    fine_grad, fine_sums = level(
        fine_vals, conv, cot, mine(gain_fine), mine(bias_fine), group_width
    )
    back = (
        fine_grad.astype(jnp.bfloat16)
        .reshape(sub, 2, 2, nf, tl, nr, hl, w)
        .transpose(3, 5, 0, 1, 2, 4, 6, 7)
        .reshape(count, sub, 4 * tl * hl * w)
    )
    sums = to_everyone(jnp.concatenate([fine_sums, coarse_sums]), count)
    back = lax.all_to_all(back, BLOCK, 0, 0)
    out = (
        back.reshape(nf, nr, sub, 2, 2, tl, hl, w)
        .transpose(5, 6, 3, 7, 4, 1, 0, 2)
        .reshape(1, tl, 2 * hl, 2 * w, channels)
    )
    sums = sums.reshape(nf, nr, 4, sub).transpose(2, 1, 0, 3).reshape(4, channels)
    totals = lax.psum(sums, "dp")
    cells = nd * frames * rows * w
    scale_fine = 1.0 / jnp.sqrt(jnp.float32(4 * cells))
    scale_coarse = 1.0 / jnp.sqrt(jnp.float32(cells))
    return (
        out,
        totals[1] * scale_fine,
        totals[0] * scale_fine,
        totals[3] * scale_coarse,
        totals[2] * scale_coarse,
    )


def lanes_at(shape, axis):
    return lax.broadcasted_iota(jnp.int32, shape, axis)


def pixel_order(tl, hl, w):
    size = 4 * tl * hl * w
    lane = lanes_at((size, size), 1)
    j, i, t = lane % w, lane // w % hl, lane // (w * hl) % tl
    q, p = lane // (w * hl * tl) % 2, lane // (2 * w * hl * tl)
    pixel = (t * 2 * hl + 2 * i + p) * 2 * w + 2 * j + q
    return (lanes_at((size, size), 0) == pixel).astype(jnp.float32).astype(jnp.bfloat16)


def merged_order(nr, outer, tl, cells):
    size = nr * outer * tl * cells
    a = lanes_at((size, size), 0)
    cell, t = a % cells, a // cells % tl
    o, dev = a // (cells * tl) % outer, a // (cells * tl * outer)
    target = ((o * tl + t) * nr + dev) * cells + cell
    return (lanes_at((size, size), 1) == target).astype(jnp.float32).astype(jnp.bfloat16)


def one_hot_dot(a, b, dims):
    return lax.dot_general(a, b, (dims, ((), ())), preferred_element_type=jnp.float32)


def moved(field, distance, kept):
    size = field.shape[1]
    return jnp.where(kept, pltpu.roll(field, (-distance) % size, 1), 0.0)


def own_column(row, base, sub):
    shape = (sub, row.shape[1])
    mine = lanes_at(shape, 1) == lanes_at(shape, 0) + base
    return jnp.sum(jnp.where(mine, row, 0.0), axis=1, keepdims=True)


def as_row(column):
    shape = (column.shape[0], 128)
    here = lanes_at(shape, 1) == lanes_at(shape, 0)
    return jnp.sum(jnp.where(here, column, 0.0), axis=0, keepdims=True)


def in_groups(column, group_width):
    sub = column.shape[0]
    grouped = jnp.sum(column.reshape(sub // group_width, group_width, 1), axis=1, keepdims=True)
    return jnp.broadcast_to(grouped, (sub // group_width, group_width, 1)).reshape(sub, 1)


def total(parts):
    return sum(jnp.sum(part, axis=1, keepdims=True) for part in parts)


def normalised(parts, gain, bias, entries, group_width):
    mean = in_groups(total(parts), group_width) / entries
    square = in_groups(total([part * part for part in parts]), group_width) / entries
    inv_std = lax.rsqrt(square - mean * mean + EPSILON)
    normed, slope = [], []
    for part in parts:
        unit = (part - mean) * inv_std
        preact = gain * unit + bias
        squash = jax.nn.sigmoid(preact)
        normed.append(unit)
        slope.append(squash * (1.0 + preact * (1.0 - squash)))
    return normed, slope, inv_std


def finished(convs, normed, slope, cots, gain, inv_std, entries, group_width):
    pre = [conv * part for conv, part in zip(convs, slope)]
    one = total(pre)
    two = total([a * b for a, b in zip(pre, normed)])
    group_one = in_groups(gain * one, group_width) / entries
    group_two = in_groups(gain * two, group_width) / entries
    grads = [
        cot + inv_std * (gain * part - group_one - unit * group_two)
        for cot, part, unit in zip(cots, pre, normed)
    ]
    return grads, one, two


class Plan:
    def __init__(self, mesh_sizes, acts_coarse, slice_width):
        self.nf, self.nr = mesh_sizes
        self.count = self.nf * self.nr
        self.tl, self.hl, self.w, self.channels = acts_coarse
        self.slice_width = slice_width
        self.sub = slice_width // self.nf
        self.cells = self.hl * self.w
        self.local = self.tl * self.cells
        self.image = self.cells * self.nr
        self.frames = self.tl * self.nf
        self.places = self.frames * self.image
        self.group_width = self.channels // GROUPS
        self.fits = (
            self.sub == 32
            and self.group_width == 16
            and self.cells == 16
            and self.tl == 2
            and self.nr == 4
            and self.channels % 128 == 0
            and self.slice_width * self.nr == self.channels
        )

    def place_masks(self):
        lane = lanes_at((1, self.places), 1)
        col, row = lane % self.w, lane // self.w % (self.hl * self.nr)
        last_row = self.hl * self.nr - 1
        return (lane, col > 0, col < self.w - 1, row > 0, row < last_row)


def fetched(pairs, sems):
    copies = [pltpu.make_async_copy(src, dst, sems.at[k]) for k, (src, dst) in enumerate(pairs)]
    for copy in copies:
        copy.start()
    return copies


def pack_kernel(
    plan,
    g_hbm,
    coarse_hbm,
    fine_hbm,
    kernel_c,
    kernel_f,
    gain_c,
    bias_c,
    gain_f,
    bias_f,
    out_ref,
    weights_c,
    weights_f,
    columns,
    order,
    g_ref,
    coarse_ref,
    fine_ref,
    rows,
    sems,
):
    sub, chunks, local = plan.sub, plan.channels // 128, plan.local
    f, r = lax.axis_index("frames"), lax.axis_index("rows")
    base = r * plan.slice_width + f * sub
    own = pl.ds(pl.multiple_of(f * sub, sub), sub)
    copies = fetched(
        [(fine_hbm, fine_ref), (coarse_hbm, coarse_ref), (g_hbm, g_ref)]
        + [(row, rows.at[k]) for k, row in enumerate((gain_c, bias_c, gain_f, bias_f))]
        + [(kernel_c.at[:, own, :], weights_c.at[pl.ds(0, 27)]), (kernel_f.at[:, own, :], weights_f)],
        sems,
    )
    shape = (sub, plan.channels)
    weights_c[27] = (lanes_at(shape, 1) == lanes_at(shape, 0) + base).astype(jnp.float32).astype(jnp.bfloat16)
    order[...] = merged_order(plan.nr, 4, plan.tl, plan.cells)
    pixels = pixel_order(plan.tl, plan.hl, plan.w)
    shape = (local, 128)
    places = [
        (lanes_at(shape, 0) + k * local == lanes_at(shape, 1)).astype(jnp.float32).astype(jnp.bfloat16)
        for k in range(4)
    ]
    copies[0].wait()
    fine = one_hot_dot(fine_ref[...], pixels, ((0,), (0,))).astype(jnp.bfloat16)
    copies[1].wait()
    quarters = [one_hot_dot(coarse_ref[...], place, ((0,), (0,))) for place in places]
    copies[2].wait()
    for s_f in range(plan.nf):
        for s_r in range(plan.nr):
            dest, c = s_f * plan.nr + s_r, s_r * plan.slice_width + s_f * sub
            for k in range(chunks):
                out_ref[dest, k * local : (k + 1) * local, :] = g_ref[:, k * 128 : (k + 1) * 128]
            at = chunks * local
            out_ref[dest, at : at + sub, :] = fine[c : c + sub]
            coarse = sum(quarters[k][c + 8 * k : c + 8 * k + 8] for k in range(4))
            out_ref[dest, at + sub : at + sub + 8, :] = coarse.astype(jnp.bfloat16)
    for copy in copies[3:7]:
        copy.wait()
    for k in range(4):
        columns[k] = jnp.broadcast_to(own_column(rows[k], base, sub), (sub, 128))
    for copy in copies[7:]:
        copy.wait()


def by_frame_device(plan, got_ref, at, height):
    return jnp.concatenate(
        [
            jnp.concatenate(
                [got_ref[f * plan.nr + r, at : at + height, :] for r in range(plan.nr)], axis=1
            )
            for f in range(plan.nf)
        ],
        axis=0,
    )


def in_places(plan, merged, height):
    width = plan.tl * plan.image
    return [
        jnp.concatenate(
            [merged[f * height : (f + 1) * height, k * width : (k + 1) * width] for f in range(plan.nf)],
            axis=1,
        )
        for k in range(4)
    ]


def frame_sum(products_ref, tap, sub, lane, places, image):
    near = products_ref[pl.ds((18 + tap) * sub, sub), :]
    middle = products_ref[pl.ds((9 + tap) * sub, sub), :]
    far = products_ref[pl.ds(tap * sub, sub), :]
    return near + moved(middle, image, lane < places - image) + moved(far, 2 * image, lane < places - 2 * image)


def coarse_kernel(plan, got_ref, weights, columns, order, out_ref, sums_ref, source, products):
    sub, nr, nf, cells, tl, local = plan.sub, plan.nr, plan.nf, plan.cells, plan.tl, plan.local
    chunks = plan.channels // 128
    for s_f in range(nf):
        for s_r in range(nr):
            for t in range(tl):
                at = (s_f * tl + t) * plan.image + s_r * cells
                for k in range(chunks):
                    source[at : at + cells, k * 128 : (k + 1) * 128] = got_ref[
                        s_f * nr + s_r, k * local + t * cells : k * local + (t + 1) * cells, :
                    ]
    products[...] = lax.dot_general(
        weights[...].reshape(28 * sub, plan.channels),
        source[...],
        (((1,), (1,)), ((), ())),
        preferred_element_type=jnp.float32,
    )
    packed = by_frame_device(plan, got_ref, chunks * local + sub, 8)
    merged = one_hot_dot(packed, order[...], ((1,), (0,)))
    values = jnp.concatenate(in_places(plan, merged, 8), axis=0)
    gain, bias = columns[0][:, 0:1], columns[1][:, 0:1]
    entries = plan.places * plan.group_width
    normed, slope, inv_std = normalised([values], gain, bias, entries, plan.group_width)
    lane, has_left, has_right, has_up, has_down = plan.place_masks()
    by_col = []
    for col in range(3):
        parts = [frame_sum(products, 3 * row + col, sub, lane, plan.places, plan.image) for row in range(3)]
        by_col.append(parts[1] + moved(parts[0], plan.w, has_down) + moved(parts[2], -plan.w, has_up))
    conv = by_col[1] + moved(by_col[0], 1, has_right) + moved(by_col[2], -1, has_left)
    cot = products[pl.ds(27 * sub, sub), :]
    grads, one, two = finished([conv], normed, slope, [cot], gain, inv_std, entries, plan.group_width)
    quartered = (grads[0] * 0.25).astype(jnp.bfloat16)
    for dest in range(plan.count):
        out_ref[dest] = quartered
    sums_ref[...] = jnp.concatenate([as_row(one), as_row(two)], axis=0)


def fine_kernel(plan, got_ref, acts_ref, columns, order, sums_ref, weights, out_ref, source, products):
    sub, nr, nf = plan.sub, plan.nr, plan.nf
    f, r = lax.axis_index("frames"), lax.axis_index("rows")
    for s_f in range(nf):
        for s_r in range(nr):
            c = s_r * plan.slice_width + s_f * sub
            source[c : c + sub, :] = got_ref[s_f * nr + s_r]
    products[...] = lax.dot_general(
        weights[...].reshape(27 * sub, plan.channels),
        source[...],
        (((1,), (0,)), ((), ())),
        preferred_element_type=jnp.float32,
    )
    packed = by_frame_device(plan, acts_ref, plan.channels // 128 * plan.local, sub)
    parts = in_places(plan, one_hot_dot(packed, order[...], ((1,), (0,))), sub)
    gain, bias = columns[2][:, 0:1], columns[3][:, 0:1]
    entries = 4 * plan.places * plan.group_width
    normed, slope, inv_std = normalised(parts, gain, bias, entries, plan.group_width)
    lane, has_left, has_right, has_up, has_down = plan.place_masks()
    by_row = []
    for row in range(3):
        a, b, c = [frame_sum(products, 3 * row + col, sub, lane, plan.places, plan.image) for col in range(3)]
        by_row.append((a + b + moved(c, -1, has_left), moved(a, 1, has_right) + b + c))
    convs = [by_row[0][q] + by_row[1][q] + moved(by_row[2][q], -plan.w, has_up) for q in range(2)]
    convs += [moved(by_row[0][q], plan.w, has_down) + by_row[1][q] + by_row[2][q] for q in range(2)]
    cot = got_ref[f * nr + r].astype(jnp.float32)
    grads, one, two = finished(convs, normed, slope, [cot] * 4, gain, inv_std, entries, plan.group_width)
    width = plan.tl * plan.image
    stacked = jnp.concatenate(
        [
            jnp.concatenate(
                [grads[pq][:, s_f * width : (s_f + 1) * width].astype(jnp.bfloat16) for pq in range(4)], axis=1
            )
            for s_f in range(nf)
        ],
        axis=0,
    )
    sent = one_hot_dot(stacked, order[...], ((1,), (1,))).astype(jnp.bfloat16)
    sums = jnp.concatenate([as_row(one), as_row(two), sums_ref[...]], axis=0)
    top = sums.astype(jnp.bfloat16).astype(jnp.float32)
    coded = jnp.concatenate([top, sums - top], axis=0).astype(jnp.bfloat16)
    for s_f in range(nf):
        for s_r in range(nr):
            out_ref[s_f * nr + s_r, 0:sub, :] = sent[s_f * sub : (s_f + 1) * sub, s_r * 128 : (s_r + 1) * 128]
            out_ref[s_f * nr + s_r, sub : sub + 8, :] = coded


def spread_kernel(plan, scales, got_ref, out_ref, *rest):
    sum_refs, source = rest[:4], rest[4]
    sub, nr, nf = plan.sub, plan.nr, plan.nf
    for s_f in range(nf):
        for s_r in range(nr):
            c = s_r * plan.slice_width + s_f * sub
            source[c : c + sub, :] = got_ref[s_f * nr + s_r, 0:sub, :]
    order = pixel_order(plan.tl, plan.hl, plan.w)
    out_ref[...] = one_hot_dot(order, source[...], ((1,), (1,))).astype(jnp.bfloat16)
    columns = []
    for s_r in range(nr):
        held = 0.0
        for s_f in range(nf):
            coded = got_ref[s_f * nr + s_r, sub : sub + 8, :].astype(jnp.float32)
            sums = coded[0:4] + coded[4:8]
            held = held + (pltpu.roll(sums, s_f * sub, 1) if s_f else sums)
        columns.append(held)
    rows = jnp.concatenate(columns, axis=1)
    for k in range(4):
        sum_refs[k][...] = rows[k : k + 1] * scales[k]


def in_vmem(count):
    return [pl.BlockSpec(memory_space=pltpu.VMEM)] * count


def in_hbm(count):
    return [pl.BlockSpec(memory_space=pltpu.HBM)] * count


def kept(array):
    return pltpu.with_memory_space_constraint(array, pltpu.HBM)


def shape_of(shape, kind):
    return jax.ShapeDtypeStruct(shape, kind)


LIMIT = pltpu.CompilerParams(vmem_limit_bytes=40 * 1024 * 1024)


def fast_shards(
    plan,
    acts_fine,
    acts_coarse,
    grad_coarse,
    gain_fine,
    bias_fine,
    kernel_fine,
    gain_coarse,
    bias_coarse,
    kernel_coarse,
):
    nd = lax.axis_size("dp")
    count, sub, channels, places, local = plan.count, plan.sub, plan.channels, plan.places, plan.local
    chunks = channels // 128
    f32, bf16 = jnp.float32, jnp.bfloat16
    rows = [part.reshape(1, channels) for part in (gain_coarse, bias_coarse, gain_fine, bias_fine)]
    packed, weights_c, weights_f, columns, order = pl.pallas_call(
        functools.partial(pack_kernel, plan),
        out_shape=(
            shape_of((count, chunks * local + sub + 8, 128), bf16),
            shape_of((28, sub, channels), bf16),
            shape_of((27, sub, channels), bf16),
            shape_of((4, sub, 128), f32),
            shape_of((4 * plan.nr * local, 4 * plan.nr * local), bf16),
        ),
        in_specs=in_hbm(9),
        out_specs=tuple(in_vmem(5)),
        scratch_shapes=[
            pltpu.VMEM((local, channels), bf16),
            pltpu.VMEM((local, channels), bf16),
            pltpu.VMEM((4 * local, channels), bf16),
            pltpu.VMEM((4, 1, channels), f32),
            pltpu.SemaphoreType.DMA((9,)),
        ],
        compiler_params=LIMIT,
    )(
        kept(grad_coarse.reshape(local, channels)),
        kept(acts_coarse.reshape(local, channels)),
        kept(acts_fine.reshape(4 * local, channels)),
        kept(kernel_coarse),
        kept(kernel_fine),
        *[kept(row) for row in rows],
    )
    got = lax.all_to_all(packed, BLOCK, 0, 0)
    quartered, coarse_sums = pl.pallas_call(
        functools.partial(coarse_kernel, plan),
        out_shape=(shape_of((count, sub, places), bf16), shape_of((2, 128), f32)),
        in_specs=in_vmem(4),
        out_specs=tuple(in_vmem(2)),
        scratch_shapes=[pltpu.VMEM((places, channels), bf16), pltpu.VMEM((28 * sub, places), f32)],
        compiler_params=LIMIT,
    )(got, weights_c, columns, order)
    spread = lax.all_to_all(quartered, BLOCK, 0, 0)
    sent = pl.pallas_call(
        functools.partial(fine_kernel, plan),
        out_shape=shape_of((count, sub + 8, 128), bf16),
        in_specs=in_vmem(6),
        out_specs=in_vmem(1)[0],
        scratch_shapes=[pltpu.VMEM((channels, places), bf16), pltpu.VMEM((27 * sub, places), f32)],
        compiler_params=LIMIT,
    )(spread, got, columns, order, coarse_sums, weights_f)
    back = lax.all_to_all(sent, BLOCK, 0, 0)
    cells = nd * places
    fine_scale, coarse_scale = 1.0 / math.sqrt(4 * cells), 1.0 / math.sqrt(cells)
    out, *sums = pl.pallas_call(
        functools.partial(spread_kernel, plan, (fine_scale, fine_scale, coarse_scale, coarse_scale)),
        out_shape=(shape_of((4 * local, channels), bf16),) + (shape_of((1, channels), f32),) * 4,
        in_specs=in_vmem(1),
        out_specs=tuple(in_vmem(5)),
        scratch_shapes=[pltpu.VMEM((channels, 4 * local), bf16)],
        compiler_params=LIMIT,
    )(back)
    bias_f, gain_f, bias_c, gain_c = lax.psum(tuple(part.reshape(channels) for part in sums), "dp")
    return out.reshape(acts_fine.shape), gain_f, bias_f, gain_c, bias_c


def solution(mesh):
    def shards(*arrays):
        sizes = (lax.axis_size("frames"), lax.axis_size("rows"))
        plan = Plan(sizes, arrays[1].shape[1:], arrays[5].shape[1])
        if plan.fits:
            return fast_shards(plan, *arrays)
        return plain_shards(*arrays)

    in_specs = (
        P("dp", "frames", "rows", None, None),
        P("dp", "frames", "rows", None, None),
        P("dp", "frames", "rows", None, None),
        P(),
        P(),
        P(None, "rows", None),
        P(),
        P(),
        P(None, "rows", None),
    )
    out_specs = (P("dp", "frames", "rows", None, None), P(), P(), P(), P())
    return jax.shard_map(shards, mesh=mesh, in_specs=in_specs, out_specs=out_specs, check_vma=False)
```

```python
import functools
import math

import jax
import jax.numpy as jnp
from jax import lax
from jax.experimental import pallas as pl
from jax.experimental.pallas import tpu as pltpu
from jax.sharding import PartitionSpec as P

GROUPS = 32
EPSILON = 1e-06
BLOCK = ("rows", "frames")
PLAIN_BLOCK = ("frames", "rows")


def plain_everyone(block, count):
    copies = jnp.broadcast_to(block[None], (count,) + block.shape)
    return lax.all_to_all(copies, PLAIN_BLOCK, 0, 0)


def ahead(field, axis, distance):
    size = field.shape[axis]
    if distance == 0:
        return field
    widths = [(0, 0)] * field.ndim
    if distance > 0:
        widths[axis] = (0, distance)
        kept = lax.slice_in_dim(field, distance, size, axis=axis)
    else:
        widths[axis] = (-distance, 0)
        kept = lax.slice_in_dim(field, 0, size + distance, axis=axis)
    return jnp.pad(kept, widths)


def tap_products(source, kernel):
    sub = kernel.shape[1]
    frames, rows, cols, channels = source.shape
    products = lax.dot_general(
        kernel.reshape(27 * sub, channels),
        source.reshape(frames * rows * cols, channels),
        (((1,), (1,)), ((), ())),
        preferred_element_type=jnp.float32,
    ).reshape(3, 3, 3, sub, frames, rows, cols)
    return sum(ahead(products[depth], 3, 2 - depth) for depth in range(3))


def coarse_conv(source, kernel):
    spatial = tap_products(source, kernel)
    total = 0.0
    for row in range(3):
        part = sum(ahead(spatial[row, col], 3, 1 - col) for col in range(3))
        total = total + ahead(part, 2, 1 - row)
    return total


def fine_conv(source, kernel):
    spatial = tap_products(source, kernel)
    result = []
    for p in range(2):
        rows_of = []
        for q in range(2):
            total = 0.0
            for row in range(3):
                part = sum(ahead(spatial[row, col], 3, (q + 1 - col) // 2) for col in range(3))
                total = total + ahead(part, 2, (p + 1 - row) // 2)
            rows_of.append(total)
        result.append(jnp.stack(rows_of, 1))
    return jnp.stack(result, 1)


def group_total(sums, group_width):
    sub = sums.shape[-1]
    if sub % group_width == 0:
        grouped = jnp.sum(sums.reshape(-1, sub // group_width, group_width), axis=-1)
        return jnp.repeat(grouped, group_width, axis=-1)
    spread = jnp.moveaxis(lax.all_gather(sums, "frames"), 0, 1).reshape(sums.shape[0], -1, group_width)
    mine = lax.axis_index("frames") * sub // group_width
    grouped = lax.dynamic_index_in_dim(jnp.sum(spread, -1), mine, 1)
    return jnp.broadcast_to(grouped, sums.shape)


def level(acts, conv_grad, cotangent, gain, bias, group_width):
    sub = acts.shape[0]
    places = acts.size // sub
    values = acts.astype(jnp.float32).reshape(sub, places)
    conv_grad = conv_grad.reshape(sub, places)
    entries = places * group_width
    moments = group_total(
        jnp.stack([jnp.sum(values, 1), jnp.sum(values * values, 1)]), group_width
    ) / entries
    mean = moments[0]
    inv_std = lax.rsqrt(moments[1] - mean * mean + EPSILON)
    normed = (values - mean[:, None]) * inv_std[:, None]
    preact = gain[:, None] * normed + bias[:, None]
    squash = jax.nn.sigmoid(preact)
    pre_grad = conv_grad * squash * (1.0 + preact * (1.0 - squash))
    sums = jnp.stack([jnp.sum(pre_grad, 1), jnp.sum(pre_grad * normed, 1)])
    terms = group_total(sums * gain, group_width) / entries
    grad = cotangent.reshape(sub, places) + inv_std[:, None] * (
        gain[:, None] * pre_grad - terms[0][:, None] - normed * terms[1][:, None]
    )
    return grad, sums


def plain_shards(
    acts_fine,
    acts_coarse,
    grad_coarse,
    gain_fine,
    bias_fine,
    kernel_fine,
    gain_coarse,
    bias_coarse,
    kernel_coarse,
):
    nf, nr, nd = lax.axis_size("frames"), lax.axis_size("rows"), lax.axis_size("dp")
    count = nf * nr
    channels = acts_fine.shape[-1]
    slice_width = kernel_fine.shape[1]
    sub = slice_width // nf
    group_width = channels // GROUPS
    tl, hl, w = acts_coarse.shape[1:4]
    frames, rows = tl * nf, hl * nr
    f, r = lax.axis_index("frames"), lax.axis_index("rows")

    gathered = plain_everyone(grad_coarse[0], count)
    source = (
        gathered.reshape(nf, nr, tl, hl, w, channels)
        .transpose(0, 2, 1, 3, 4, 5)
        .reshape(frames, rows, w, channels)
    )
    coarse_in = acts_coarse[0].reshape(tl, hl, w, nr, nf, sub).transpose(4, 3, 5, 0, 1, 2)
    coarse_in = lax.all_to_all(coarse_in.reshape(count, sub, tl * hl * w), PLAIN_BLOCK, 0, 0)
    fine_in = acts_fine[0].reshape(tl, hl, 2, w, 2, nr, nf, sub).transpose(6, 5, 7, 2, 4, 0, 1, 3)
    fine_in = lax.all_to_all(fine_in.reshape(count, sub, 4 * tl * hl * w), PLAIN_BLOCK, 0, 0)

    def mine(vector):
        return lax.dynamic_slice_in_dim(vector, r * slice_width + f * sub, sub)

    def own(kernel):
        return lax.dynamic_slice_in_dim(kernel, f * sub, sub, axis=1)

    coarse_vals = (
        coarse_in.reshape(nf, nr, sub, tl, hl, w).transpose(2, 0, 3, 1, 4, 5).reshape(sub, frames, rows, w)
    )
    cot = lax.dynamic_slice_in_dim(source, r * slice_width + f * sub, sub, axis=3)
    cot = cot.astype(jnp.float32).transpose(3, 0, 1, 2)
    conv = coarse_conv(source, own(kernel_coarse))
    coarse_grad, coarse_sums = level(
        coarse_vals, conv, cot, mine(gain_coarse), mine(bias_coarse), group_width
    )
    quartered = (coarse_grad * 0.25).astype(jnp.bfloat16)
    spread = plain_everyone(quartered, count)
    source_fine = (
        spread.reshape(nf, nr, sub, frames, rows, w)
        .transpose(3, 4, 5, 1, 0, 2)
        .reshape(frames, rows, w, channels)
    )
    conv = fine_conv(source_fine, own(kernel_fine))
    fine_vals = (
        fine_in.reshape(nf, nr, sub, 2, 2, tl, hl, w)
        .transpose(2, 3, 4, 0, 5, 1, 6, 7)
        .reshape(sub, 2, 2, frames, rows, w)
    )
    cot = jnp.broadcast_to(
        quartered.astype(jnp.float32).reshape(sub, 1, 1, frames, rows, w), conv.shape
    )
    fine_grad, fine_sums = level(
        fine_vals, conv, cot, mine(gain_fine), mine(bias_fine), group_width
    )
    back = (
        fine_grad.astype(jnp.bfloat16)
        .reshape(sub, 2, 2, nf, tl, nr, hl, w)
        .transpose(3, 5, 0, 1, 2, 4, 6, 7)
        .reshape(count, sub, 4 * tl * hl * w)
    )
    sums = plain_everyone(jnp.concatenate([fine_sums, coarse_sums]), count)
    back = lax.all_to_all(back, PLAIN_BLOCK, 0, 0)
    out = (
        back.reshape(nf, nr, sub, 2, 2, tl, hl, w)
        .transpose(5, 6, 3, 7, 4, 1, 0, 2)
        .reshape(1, tl, 2 * hl, 2 * w, channels)
    )
    sums = sums.reshape(nf, nr, 4, sub).transpose(2, 1, 0, 3).reshape(4, channels)
    totals = lax.psum(sums, "dp")
    cells = nd * frames * rows * w
    scale_fine = 1.0 / jnp.sqrt(jnp.float32(4 * cells))
    scale_coarse = 1.0 / jnp.sqrt(jnp.float32(cells))
    return (
        out,
        totals[1] * scale_fine,
        totals[0] * scale_fine,
        totals[3] * scale_coarse,
        totals[2] * scale_coarse,
    )


def lanes_at(shape, axis):
    return lax.broadcasted_iota(jnp.int32, shape, axis)


def pixel_order(tl, hl, w):
    size = 4 * tl * hl * w
    lane = lanes_at((size, size), 1)
    j, i, t = lane % w, lane // w % hl, lane // (w * hl) % tl
    q, p = lane // (w * hl * tl) % 2, lane // (2 * w * hl * tl)
    pixel = (t * 2 * hl + 2 * i + p) * 2 * w + 2 * j + q
    return (lanes_at((size, size), 0) == pixel).astype(jnp.float32).astype(jnp.bfloat16)


def merged_order(nr, outer, tl, cells):
    size = nr * outer * tl * cells
    a = lanes_at((size, size), 0)
    cell, t = a % cells, a // cells % tl
    o, dev = a // (cells * tl) % outer, a // (cells * tl * outer)
    target = ((o * tl + t) * nr + dev) * cells + cell
    return (lanes_at((size, size), 1) == target).astype(jnp.float32).astype(jnp.bfloat16)


def one_hot_dot(a, b, dims):
    return lax.dot_general(a, b, (dims, ((), ())), preferred_element_type=jnp.float32)


def moved(field, distance, kept):
    size = field.shape[1]
    return jnp.where(kept, pltpu.roll(field, (-distance) % size, 1), 0.0)


def own_column(row, base, sub):
    shape = (sub, row.shape[1])
    mine = lanes_at(shape, 1) == lanes_at(shape, 0) + base
    return jnp.sum(jnp.where(mine, row, 0.0), axis=1, keepdims=True)


def as_row(column):
    shape = (column.shape[0], 128)
    here = lanes_at(shape, 1) == lanes_at(shape, 0)
    return jnp.sum(jnp.where(here, column, 0.0), axis=0, keepdims=True)


def in_groups(column, group_width):
    sub = column.shape[0]
    grouped = jnp.sum(column.reshape(sub // group_width, group_width, 1), axis=1, keepdims=True)
    return jnp.broadcast_to(grouped, (sub // group_width, group_width, 1)).reshape(sub, 1)


def total(parts):
    return sum(jnp.sum(part, axis=1, keepdims=True) for part in parts)


def normalised(parts, gain, bias, entries, group_width):
    mean = in_groups(total(parts), group_width) / entries
    square = in_groups(total([part * part for part in parts]), group_width) / entries
    inv_std = lax.rsqrt(square - mean * mean + EPSILON)
    normed, slope = [], []
    for part in parts:
        unit = (part - mean) * inv_std
        preact = gain * unit + bias
        squash = jax.nn.sigmoid(preact)
        normed.append(unit)
        slope.append(squash * (1.0 + preact * (1.0 - squash)))
    return normed, slope, inv_std


def finished(convs, normed, slope, cots, gain, inv_std, entries, group_width):
    pre = [conv * part for conv, part in zip(convs, slope)]
    one = total(pre)
    two = total([a * b for a, b in zip(pre, normed)])
    group_one = in_groups(gain * one, group_width) / entries
    group_two = in_groups(gain * two, group_width) / entries
    grads = [
        cot + inv_std * (gain * part - group_one - unit * group_two)
        for cot, part, unit in zip(cots, pre, normed)
    ]
    return grads, one, two


class Plan:
    def __init__(self, mesh_sizes, acts_coarse, slice_width):
        self.nf, self.nr = mesh_sizes
        self.count = self.nf * self.nr
        self.tl, self.hl, self.w, self.channels = acts_coarse
        self.slice_width = slice_width
        self.sub = slice_width // self.nf
        self.cells = self.hl * self.w
        self.local = self.tl * self.cells
        self.image = self.cells * self.nr
        self.frames = self.tl * self.nf
        self.places = self.frames * self.image
        self.group_width = self.channels // GROUPS
        self.fits = (
            self.sub == 32
            and self.group_width == 16
            and self.cells == 16
            and self.tl == 2
            and self.nr == 4
            and self.channels % 128 == 0
            and self.slice_width * self.nr == self.channels
        )

    def place_masks(self):
        lane = lanes_at((1, self.places), 1)
        col, row = lane % self.w, lane // self.w % (self.hl * self.nr)
        last_row = self.hl * self.nr - 1
        return (lane, col > 0, col < self.w - 1, row > 0, row < last_row)


def fetched(pairs, sems):
    copies = [pltpu.make_async_copy(src, dst, sems.at[k]) for k, (src, dst) in enumerate(pairs)]
    for copy in copies:
        copy.start()
    return copies


def pack_kernel(
    plan,
    g_hbm,
    coarse_hbm,
    fine_hbm,
    kernel_c,
    gain_c,
    bias_c,
    gain_f,
    bias_f,
    out_ref,
    weights_c,
    columns,
    order,
    g_ref,
    coarse_ref,
    fine_ref,
    rows,
    sems,
):
    sub, chunks, local = plan.sub, plan.channels // 128, plan.local
    f, r = lax.axis_index("frames"), lax.axis_index("rows")
    base = r * plan.slice_width + f * sub
    own = pl.ds(pl.multiple_of(f * sub, sub), sub)
    copies = fetched(
        [(fine_hbm, fine_ref), (coarse_hbm, coarse_ref), (g_hbm, g_ref)]
        + [(row, rows.at[k]) for k, row in enumerate((gain_c, bias_c, gain_f, bias_f))]
        + [(kernel_c.at[:, own, :], weights_c.at[pl.ds(0, 27)])],
        sems,
    )
    shape = (sub, plan.channels)
    weights_c[27] = (lanes_at(shape, 1) == lanes_at(shape, 0) + base).astype(jnp.float32).astype(jnp.bfloat16)
    order[...] = merged_order(plan.nr, 4, plan.tl, plan.cells)
    pixels = pixel_order(plan.tl, plan.hl, plan.w)
    shape = (local, 128)
    places = [
        (lanes_at(shape, 0) + k * local == lanes_at(shape, 1)).astype(jnp.float32).astype(jnp.bfloat16)
        for k in range(4)
    ]
    copies[0].wait()
    fine = one_hot_dot(fine_ref[...], pixels, ((0,), (0,))).astype(jnp.bfloat16)
    copies[1].wait()
    quarters = [one_hot_dot(coarse_ref[...], place, ((0,), (0,))) for place in places]
    copies[2].wait()
    for s_f in range(plan.nf):
        for s_r in range(plan.nr):
            dest, c = s_r * plan.nf + s_f, s_r * plan.slice_width + s_f * sub
            for k in range(chunks):
                out_ref[dest, k * local : (k + 1) * local, :] = g_ref[:, k * 128 : (k + 1) * 128]
            at = chunks * local
            out_ref[dest, at : at + sub, :] = fine[c : c + sub]
            coarse = sum(quarters[k][c + 8 * k : c + 8 * k + 8] for k in range(4))
            out_ref[dest, at + sub : at + sub + 8, :] = coarse.astype(jnp.bfloat16)
    for copy in copies[3:7]:
        copy.wait()
    for k in range(4):
        columns[k] = jnp.broadcast_to(own_column(rows[k], base, sub), (sub, 128))
    for copy in copies[7:]:
        copy.wait()


def by_frame_device(plan, got_ref, at, height):
    return jnp.concatenate(
        [
            jnp.concatenate(
                [got_ref[r * plan.nf + f, at : at + height, :] for r in range(plan.nr)], axis=1
            )
            for f in range(plan.nf)
        ],
        axis=0,
    )


def in_places(plan, merged, height):
    width = plan.tl * plan.image
    return [
        jnp.concatenate(
            [merged[f * height : (f + 1) * height, k * width : (k + 1) * width] for f in range(plan.nf)],
            axis=1,
        )
        for k in range(4)
    ]


def frame_sum(products_ref, tap, sub, lane, places, image):
    near = products_ref[pl.ds((18 + tap) * sub, sub), :]
    middle = products_ref[pl.ds((9 + tap) * sub, sub), :]
    far = products_ref[pl.ds(tap * sub, sub), :]
    return near + moved(middle, image, lane < places - image) + moved(far, 2 * image, lane < places - 2 * image)


def coarse_kernel(
    plan, got_ref, weights, columns, order, kernel_f, out_ref, sums_ref, weights_f, source, products, sem
):
    own = pl.ds(pl.multiple_of(lax.axis_index("frames") * plan.sub, plan.sub), plan.sub)
    copy = pltpu.make_async_copy(kernel_f.at[:, own, :], weights_f, sem)
    copy.start()
    sub, nr, nf, cells, tl, local = plan.sub, plan.nr, plan.nf, plan.cells, plan.tl, plan.local
    chunks = plan.channels // 128
    for s_f in range(nf):
        for s_r in range(nr):
            for t in range(tl):
                at = (s_f * tl + t) * plan.image + s_r * cells
                for k in range(chunks):
                    source[at : at + cells, k * 128 : (k + 1) * 128] = got_ref[
                        s_r * nf + s_f, k * local + t * cells : k * local + (t + 1) * cells, :
                    ]
    products[...] = lax.dot_general(
        weights[...].reshape(28 * sub, plan.channels),
        source[...],
        (((1,), (1,)), ((), ())),
        preferred_element_type=jnp.float32,
    )
    packed = by_frame_device(plan, got_ref, chunks * local + sub, 8)
    merged = one_hot_dot(packed, order[...], ((1,), (0,)))
    values = jnp.concatenate(in_places(plan, merged, 8), axis=0)
    gain, bias = columns[0][:, 0:1], columns[1][:, 0:1]
    entries = plan.places * plan.group_width
    normed, slope, inv_std = normalised([values], gain, bias, entries, plan.group_width)
    lane, has_left, has_right, has_up, has_down = plan.place_masks()
    by_col = []
    for col in range(3):
        parts = [frame_sum(products, 3 * row + col, sub, lane, plan.places, plan.image) for row in range(3)]
        by_col.append(parts[1] + moved(parts[0], plan.w, has_down) + moved(parts[2], -plan.w, has_up))
    conv = by_col[1] + moved(by_col[0], 1, has_right) + moved(by_col[2], -1, has_left)
    cot = products[pl.ds(27 * sub, sub), :]
    grads, one, two = finished([conv], normed, slope, [cot], gain, inv_std, entries, plan.group_width)
    quartered = (grads[0] * 0.25).astype(jnp.bfloat16)
    for dest in range(plan.count):
        out_ref[dest] = quartered
    sums_ref[...] = jnp.concatenate([as_row(one), as_row(two)], axis=0)
    copy.wait()


def fine_kernel(plan, got_ref, acts_ref, columns, order, sums_ref, weights, out_ref, products):
    sub, nr, nf = plan.sub, plan.nr, plan.nf
    f, r = lax.axis_index("frames"), lax.axis_index("rows")
    products[...] = lax.dot_general(
        weights[...].reshape(27 * sub, plan.channels),
        got_ref[...].reshape(plan.channels, plan.places),
        (((1,), (0,)), ((), ())),
        preferred_element_type=jnp.float32,
    )
    packed = by_frame_device(plan, acts_ref, plan.channels // 128 * plan.local, sub)
    parts = in_places(plan, one_hot_dot(packed, order[...], ((1,), (0,))), sub)
    gain, bias = columns[2][:, 0:1], columns[3][:, 0:1]
    entries = 4 * plan.places * plan.group_width
    normed, slope, inv_std = normalised(parts, gain, bias, entries, plan.group_width)
    lane, has_left, has_right, has_up, has_down = plan.place_masks()
    by_row = []
    for row in range(3):
        a, b, c = [frame_sum(products, 3 * row + col, sub, lane, plan.places, plan.image) for col in range(3)]
        by_row.append((a + b + moved(c, -1, has_left), moved(a, 1, has_right) + b + c))
    convs = [by_row[0][q] + by_row[1][q] + moved(by_row[2][q], -plan.w, has_up) for q in range(2)]
    convs += [moved(by_row[0][q], plan.w, has_down) + by_row[1][q] + by_row[2][q] for q in range(2)]
    cot = got_ref[r * nf + f].astype(jnp.float32)
    grads, one, two = finished(convs, normed, slope, [cot] * 4, gain, inv_std, entries, plan.group_width)
    width = plan.tl * plan.image
    stacked = jnp.concatenate(
        [
            jnp.concatenate(
                [grads[pq][:, s_f * width : (s_f + 1) * width].astype(jnp.bfloat16) for pq in range(4)], axis=1
            )
            for s_f in range(nf)
        ],
        axis=0,
    )
    sent = one_hot_dot(stacked, order[...], ((1,), (1,))).astype(jnp.bfloat16)
    sums = jnp.concatenate([as_row(one), as_row(two), sums_ref[...]], axis=0)
    top = sums.astype(jnp.bfloat16).astype(jnp.float32)
    coded = jnp.concatenate([top, sums - top], axis=0).astype(jnp.bfloat16)
    for s_f in range(nf):
        for s_r in range(nr):
            out_ref[s_r * nf + s_f, 0:sub, :] = sent[s_f * sub : (s_f + 1) * sub, s_r * 128 : (s_r + 1) * 128]
            out_ref[s_r * nf + s_f, sub : sub + 8, :] = coded


def spread_kernel(plan, got_ref, out_ref, sums_ref):
    sub, nr, nf = plan.sub, plan.nr, plan.nf
    order = pixel_order(plan.tl, plan.hl, plan.w)
    source = got_ref[:, 0:sub, :].reshape(plan.channels, 4 * plan.local)
    out_ref[...] = one_hot_dot(order, source, ((1,), (1,))).astype(jnp.bfloat16)
    columns = []
    for s_r in range(nr):
        held = 0.0
        for s_f in range(nf):
            coded = got_ref[s_r * nf + s_f, sub : sub + 8, :].astype(jnp.float32)
            sums = coded[0:4] + coded[4:8]
            held = held + (pltpu.roll(sums, s_f * sub, 1) if s_f else sums)
        columns.append(held)
    rows = jnp.concatenate(columns, axis=1)
    sums_ref[...] = jnp.concatenate([rows, jnp.zeros_like(rows)], axis=0)


def total_kernel(scales, both_ref, *out_refs):
    rows = sum(both_ref[k] for k in range(both_ref.shape[0]))
    for k in range(4):
        out_refs[k][...] = rows[k : k + 1] * scales[k]


def in_vmem(count):
    return [pl.BlockSpec(memory_space=pltpu.VMEM)] * count


def in_hbm(count):
    return [pl.BlockSpec(memory_space=pltpu.HBM)] * count


def kept(array):
    return pltpu.with_memory_space_constraint(array, pltpu.HBM)


def shape_of(shape, kind):
    return jax.ShapeDtypeStruct(shape, kind)


LIMIT = pltpu.CompilerParams(vmem_limit_bytes=40 * 1024 * 1024)


def fast_shards(
    plan,
    acts_fine,
    acts_coarse,
    grad_coarse,
    gain_fine,
    bias_fine,
    kernel_fine,
    gain_coarse,
    bias_coarse,
    kernel_coarse,
):
    nd = lax.axis_size("dp")
    count, sub, channels, places, local = plan.count, plan.sub, plan.channels, plan.places, plan.local
    chunks = channels // 128
    f32, bf16 = jnp.float32, jnp.bfloat16
    rows = [part.reshape(1, channels) for part in (gain_coarse, bias_coarse, gain_fine, bias_fine)]
    packed, weights_c, columns, order = pl.pallas_call(
        functools.partial(pack_kernel, plan),
        out_shape=(
            shape_of((count, chunks * local + sub + 8, 128), bf16),
            shape_of((28, sub, channels), bf16),
            shape_of((4, sub, 128), f32),
            shape_of((4 * plan.nr * local, 4 * plan.nr * local), bf16),
        ),
        in_specs=in_hbm(8),
        out_specs=tuple(in_vmem(4)),
        scratch_shapes=[
            pltpu.VMEM((local, channels), bf16),
            pltpu.VMEM((local, channels), bf16),
            pltpu.VMEM((4 * local, channels), bf16),
            pltpu.VMEM((4, 1, channels), f32),
            pltpu.SemaphoreType.DMA((8,)),
        ],
        compiler_params=LIMIT,
    )(
        kept(grad_coarse.reshape(local, channels)),
        kept(acts_coarse.reshape(local, channels)),
        kept(acts_fine.reshape(4 * local, channels)),
        kept(kernel_coarse),
        *[kept(row) for row in rows],
    )
    got = lax.all_to_all(packed, BLOCK, 0, 0)
    quartered, coarse_sums, weights_f = pl.pallas_call(
        functools.partial(coarse_kernel, plan),
        out_shape=(
            shape_of((count, sub, places), bf16),
            shape_of((2, 128), f32),
            shape_of((27, sub, channels), bf16),
        ),
        in_specs=in_vmem(4) + in_hbm(1),
        out_specs=tuple(in_vmem(3)),
        scratch_shapes=[
            pltpu.VMEM((places, channels), bf16),
            pltpu.VMEM((28 * sub, places), f32),
            pltpu.SemaphoreType.DMA,
        ],
        compiler_params=LIMIT,
    )(got, weights_c, columns, order, kept(kernel_fine))
    spread = lax.all_to_all(quartered, BLOCK, 0, 0)
    sent = pl.pallas_call(
        functools.partial(fine_kernel, plan),
        out_shape=shape_of((count, sub + 8, 128), bf16),
        in_specs=in_vmem(6),
        out_specs=in_vmem(1)[0],
        scratch_shapes=[pltpu.VMEM((27 * sub, places), f32)],
        compiler_params=LIMIT,
    )(spread, got, columns, order, coarse_sums, weights_f)
    back = lax.all_to_all(sent, BLOCK, 0, 0)
    cells = nd * places
    fine_scale, coarse_scale = 1.0 / math.sqrt(4 * cells), 1.0 / math.sqrt(cells)
    out, sums = pl.pallas_call(
        functools.partial(spread_kernel, plan),
        out_shape=(pltpu.VMEM((4 * local, channels), bf16), shape_of((8, channels), f32)),
        in_specs=in_vmem(1),
        out_specs=tuple(in_vmem(2)),
        compiler_params=LIMIT,
    )(back)
    both = lax.all_gather(sums, "dp")
    sums = pl.pallas_call(
        functools.partial(total_kernel, (fine_scale, fine_scale, coarse_scale, coarse_scale)),
        out_shape=(shape_of((1, channels), f32),) * 4,
        in_specs=in_vmem(1),
        out_specs=tuple(in_vmem(4)),
        compiler_params=LIMIT,
    )(both)
    bias_f, gain_f, bias_c, gain_c = [part.reshape(channels) for part in sums]
    return out.reshape(acts_fine.shape), gain_f, bias_f, gain_c, bias_c


def solution(mesh):
    def shards(*arrays):
        sizes = (lax.axis_size("frames"), lax.axis_size("rows"))
        plan = Plan(sizes, arrays[1].shape[1:], arrays[5].shape[1])
        if plan.fits:
            return fast_shards(plan, *arrays)
        return plain_shards(*arrays)

    in_specs = (
        P("dp", "frames", "rows", None, None),
        P("dp", "frames", "rows", None, None),
        P("dp", "frames", "rows", None, None),
        P(),
        P(),
        P(None, "rows", None),
        P(),
        P(),
        P(None, "rows", None),
    )
    out_specs = (P("dp", "frames", "rows", None, None), P(), P(), P(), P())
    return jax.shard_map(shards, mesh=mesh, in_specs=in_specs, out_specs=out_specs, check_vma=False)
```

```python
import functools
import math

import jax
import jax.numpy as jnp
from jax import lax
from jax.experimental import pallas as pl
from jax.experimental.pallas import tpu as pltpu
from jax.sharding import PartitionSpec as P

GROUPS = 32
EPSILON = 1e-06
BLOCK = ("rows", "frames")
PLAIN_BLOCK = ("frames", "rows")


def plain_everyone(block, count):
    copies = jnp.broadcast_to(block[None], (count,) + block.shape)
    return lax.all_to_all(copies, PLAIN_BLOCK, 0, 0)


def ahead(field, axis, distance):
    size = field.shape[axis]
    if distance == 0:
        return field
    widths = [(0, 0)] * field.ndim
    if distance > 0:
        widths[axis] = (0, distance)
        kept = lax.slice_in_dim(field, distance, size, axis=axis)
    else:
        widths[axis] = (-distance, 0)
        kept = lax.slice_in_dim(field, 0, size + distance, axis=axis)
    return jnp.pad(kept, widths)


def tap_products(source, kernel):
    sub = kernel.shape[1]
    frames, rows, cols, channels = source.shape
    products = lax.dot_general(
        kernel.reshape(27 * sub, channels),
        source.reshape(frames * rows * cols, channels),
        (((1,), (1,)), ((), ())),
        preferred_element_type=jnp.float32,
    ).reshape(3, 3, 3, sub, frames, rows, cols)
    return sum(ahead(products[depth], 3, 2 - depth) for depth in range(3))


def coarse_conv(source, kernel):
    spatial = tap_products(source, kernel)
    total = 0.0
    for row in range(3):
        part = sum(ahead(spatial[row, col], 3, 1 - col) for col in range(3))
        total = total + ahead(part, 2, 1 - row)
    return total


def fine_conv(source, kernel):
    spatial = tap_products(source, kernel)
    result = []
    for p in range(2):
        rows_of = []
        for q in range(2):
            total = 0.0
            for row in range(3):
                part = sum(ahead(spatial[row, col], 3, (q + 1 - col) // 2) for col in range(3))
                total = total + ahead(part, 2, (p + 1 - row) // 2)
            rows_of.append(total)
        result.append(jnp.stack(rows_of, 1))
    return jnp.stack(result, 1)


def group_total(sums, group_width):
    sub = sums.shape[-1]
    if sub % group_width == 0:
        grouped = jnp.sum(sums.reshape(-1, sub // group_width, group_width), axis=-1)
        return jnp.repeat(grouped, group_width, axis=-1)
    spread = jnp.moveaxis(lax.all_gather(sums, "frames"), 0, 1).reshape(sums.shape[0], -1, group_width)
    mine = lax.axis_index("frames") * sub // group_width
    grouped = lax.dynamic_index_in_dim(jnp.sum(spread, -1), mine, 1)
    return jnp.broadcast_to(grouped, sums.shape)


def level(acts, conv_grad, cotangent, gain, bias, group_width):
    sub = acts.shape[0]
    places = acts.size // sub
    values = acts.astype(jnp.float32).reshape(sub, places)
    conv_grad = conv_grad.reshape(sub, places)
    entries = places * group_width
    moments = group_total(
        jnp.stack([jnp.sum(values, 1), jnp.sum(values * values, 1)]), group_width
    ) / entries
    mean = moments[0]
    inv_std = lax.rsqrt(moments[1] - mean * mean + EPSILON)
    normed = (values - mean[:, None]) * inv_std[:, None]
    preact = gain[:, None] * normed + bias[:, None]
    squash = jax.nn.sigmoid(preact)
    pre_grad = conv_grad * squash * (1.0 + preact * (1.0 - squash))
    sums = jnp.stack([jnp.sum(pre_grad, 1), jnp.sum(pre_grad * normed, 1)])
    terms = group_total(sums * gain, group_width) / entries
    grad = cotangent.reshape(sub, places) + inv_std[:, None] * (
        gain[:, None] * pre_grad - terms[0][:, None] - normed * terms[1][:, None]
    )
    return grad, sums


def plain_shards(
    acts_fine,
    acts_coarse,
    grad_coarse,
    gain_fine,
    bias_fine,
    kernel_fine,
    gain_coarse,
    bias_coarse,
    kernel_coarse,
):
    nf, nr, nd = lax.axis_size("frames"), lax.axis_size("rows"), lax.axis_size("dp")
    count = nf * nr
    channels = acts_fine.shape[-1]
    slice_width = kernel_fine.shape[1]
    sub = slice_width // nf
    group_width = channels // GROUPS
    tl, hl, w = acts_coarse.shape[1:4]
    frames, rows = tl * nf, hl * nr
    f, r = lax.axis_index("frames"), lax.axis_index("rows")

    gathered = plain_everyone(grad_coarse[0], count)
    source = (
        gathered.reshape(nf, nr, tl, hl, w, channels)
        .transpose(0, 2, 1, 3, 4, 5)
        .reshape(frames, rows, w, channels)
    )
    coarse_in = acts_coarse[0].reshape(tl, hl, w, nr, nf, sub).transpose(4, 3, 5, 0, 1, 2)
    coarse_in = lax.all_to_all(coarse_in.reshape(count, sub, tl * hl * w), PLAIN_BLOCK, 0, 0)
    fine_in = acts_fine[0].reshape(tl, hl, 2, w, 2, nr, nf, sub).transpose(6, 5, 7, 2, 4, 0, 1, 3)
    fine_in = lax.all_to_all(fine_in.reshape(count, sub, 4 * tl * hl * w), PLAIN_BLOCK, 0, 0)

    def mine(vector):
        return lax.dynamic_slice_in_dim(vector, r * slice_width + f * sub, sub)

    def own(kernel):
        return lax.dynamic_slice_in_dim(kernel, f * sub, sub, axis=1)

    coarse_vals = (
        coarse_in.reshape(nf, nr, sub, tl, hl, w).transpose(2, 0, 3, 1, 4, 5).reshape(sub, frames, rows, w)
    )
    cot = lax.dynamic_slice_in_dim(source, r * slice_width + f * sub, sub, axis=3)
    cot = cot.astype(jnp.float32).transpose(3, 0, 1, 2)
    conv = coarse_conv(source, own(kernel_coarse))
    coarse_grad, coarse_sums = level(
        coarse_vals, conv, cot, mine(gain_coarse), mine(bias_coarse), group_width
    )
    quartered = (coarse_grad * 0.25).astype(jnp.bfloat16)
    spread = plain_everyone(quartered, count)
    source_fine = (
        spread.reshape(nf, nr, sub, frames, rows, w)
        .transpose(3, 4, 5, 1, 0, 2)
        .reshape(frames, rows, w, channels)
    )
    conv = fine_conv(source_fine, own(kernel_fine))
    fine_vals = (
        fine_in.reshape(nf, nr, sub, 2, 2, tl, hl, w)
        .transpose(2, 3, 4, 0, 5, 1, 6, 7)
        .reshape(sub, 2, 2, frames, rows, w)
    )
    cot = jnp.broadcast_to(
        quartered.astype(jnp.float32).reshape(sub, 1, 1, frames, rows, w), conv.shape
    )
    fine_grad, fine_sums = level(
        fine_vals, conv, cot, mine(gain_fine), mine(bias_fine), group_width
    )
    back = (
        fine_grad.astype(jnp.bfloat16)
        .reshape(sub, 2, 2, nf, tl, nr, hl, w)
        .transpose(3, 5, 0, 1, 2, 4, 6, 7)
        .reshape(count, sub, 4 * tl * hl * w)
    )
    sums = plain_everyone(jnp.concatenate([fine_sums, coarse_sums]), count)
    back = lax.all_to_all(back, PLAIN_BLOCK, 0, 0)
    out = (
        back.reshape(nf, nr, sub, 2, 2, tl, hl, w)
        .transpose(5, 6, 3, 7, 4, 1, 0, 2)
        .reshape(1, tl, 2 * hl, 2 * w, channels)
    )
    sums = sums.reshape(nf, nr, 4, sub).transpose(2, 1, 0, 3).reshape(4, channels)
    totals = lax.psum(sums, "dp")
    cells = nd * frames * rows * w
    scale_fine = 1.0 / jnp.sqrt(jnp.float32(4 * cells))
    scale_coarse = 1.0 / jnp.sqrt(jnp.float32(cells))
    return (
        out,
        totals[1] * scale_fine,
        totals[0] * scale_fine,
        totals[3] * scale_coarse,
        totals[2] * scale_coarse,
    )


def lanes_at(shape, axis):
    return lax.broadcasted_iota(jnp.int32, shape, axis)


def pixel_order(tl, hl, w):
    size = 4 * tl * hl * w
    lane = lanes_at((size, size), 1)
    j, i, t = lane % w, lane // w % hl, lane // (w * hl) % tl
    q, p = lane // (w * hl * tl) % 2, lane // (2 * w * hl * tl)
    pixel = (t * 2 * hl + 2 * i + p) * 2 * w + 2 * j + q
    return (lanes_at((size, size), 0) == pixel).astype(jnp.float32).astype(jnp.bfloat16)


def merged_order(nr, outer, tl, cells):
    size = nr * outer * tl * cells
    a = lanes_at((size, size), 0)
    cell, t = a % cells, a // cells % tl
    o, dev = a // (cells * tl) % outer, a // (cells * tl * outer)
    target = ((o * tl + t) * nr + dev) * cells + cell
    return (lanes_at((size, size), 1) == target).astype(jnp.float32).astype(jnp.bfloat16)


def one_hot_dot(a, b, dims):
    return lax.dot_general(a, b, (dims, ((), ())), preferred_element_type=jnp.float32)


def moved(field, distance, kept):
    size = field.shape[1]
    return jnp.where(kept, pltpu.roll(field, (-distance) % size, 1), 0.0)


def own_column(row, base, sub):
    shape = (sub, row.shape[1])
    mine = lanes_at(shape, 1) == lanes_at(shape, 0) + base
    return jnp.sum(jnp.where(mine, row, 0.0), axis=1, keepdims=True)


def as_row(column):
    shape = (column.shape[0], 128)
    here = lanes_at(shape, 1) == lanes_at(shape, 0)
    return jnp.sum(jnp.where(here, column, 0.0), axis=0, keepdims=True)


def in_groups(column, group_width):
    sub = column.shape[0]
    grouped = jnp.sum(column.reshape(sub // group_width, group_width, 1), axis=1, keepdims=True)
    return jnp.broadcast_to(grouped, (sub // group_width, group_width, 1)).reshape(sub, 1)


def total(parts):
    return sum(jnp.sum(part, axis=1, keepdims=True) for part in parts)


def normalised(parts, gain, bias, entries, group_width):
    mean = in_groups(total(parts), group_width) / entries
    square = in_groups(total([part * part for part in parts]), group_width) / entries
    inv_std = lax.rsqrt(square - mean * mean + EPSILON)
    normed, slope = [], []
    for part in parts:
        unit = (part - mean) * inv_std
        preact = gain * unit + bias
        squash = jax.nn.sigmoid(preact)
        normed.append(unit)
        slope.append(squash * (1.0 + preact * (1.0 - squash)))
    return normed, slope, inv_std


def finished(convs, normed, slope, cots, gain, inv_std, entries, group_width):
    pre = [conv * part for conv, part in zip(convs, slope)]
    one = total(pre)
    two = total([a * b for a, b in zip(pre, normed)])
    group_one = in_groups(gain * one, group_width) / entries
    group_two = in_groups(gain * two, group_width) / entries
    grads = [
        cot + inv_std * (gain * part - group_one - unit * group_two)
        for cot, part, unit in zip(cots, pre, normed)
    ]
    return grads, one, two


class Plan:
    def __init__(self, mesh_sizes, acts_coarse, slice_width):
        self.nf, self.nr = mesh_sizes
        self.count = self.nf * self.nr
        self.tl, self.hl, self.w, self.channels = acts_coarse
        self.slice_width = slice_width
        self.sub = slice_width // self.nf
        self.cells = self.hl * self.w
        self.local = self.tl * self.cells
        self.image = self.cells * self.nr
        self.frames = self.tl * self.nf
        self.places = self.frames * self.image
        self.group_width = self.channels // GROUPS
        self.fits = (
            self.sub == 32
            and self.group_width == 16
            and self.cells == 16
            and self.tl == 2
            and self.nr == 4
            and self.channels % 128 == 0
            and self.slice_width * self.nr == self.channels
        )

    def place_masks(self):
        lane = lanes_at((1, self.places), 1)
        col, row = lane % self.w, lane // self.w % (self.hl * self.nr)
        last_row = self.hl * self.nr - 1
        return (lane, col > 0, col < self.w - 1, row > 0, row < last_row)


def fetched(pairs, sems):
    copies = [pltpu.make_async_copy(src, dst, sems.at[k]) for k, (src, dst) in enumerate(pairs)]
    for copy in copies:
        copy.start()
    return copies


def pack_kernel(
    plan,
    g_hbm,
    coarse_hbm,
    fine_hbm,
    kernel_c,
    kernel_f,
    gain_c,
    bias_c,
    gain_f,
    bias_f,
    out_ref,
    weights_c,
    weights_f,
    columns,
    order,
    g_ref,
    coarse_ref,
    fine_ref,
    rows,
    sems,
):
    sub, chunks, local = plan.sub, plan.channels // 128, plan.local
    f, r = lax.axis_index("frames"), lax.axis_index("rows")
    base = r * plan.slice_width + f * sub
    own = pl.ds(pl.multiple_of(f * sub, sub), sub)
    copies = fetched(
        [(fine_hbm, fine_ref), (coarse_hbm, coarse_ref), (g_hbm, g_ref)]
        + [(row, rows.at[k]) for k, row in enumerate((gain_c, bias_c, gain_f, bias_f))]
        + [(kernel_c.at[:, own, :], weights_c.at[pl.ds(0, 27)]), (kernel_f.at[:, own, :], weights_f)],
        sems,
    )
    shape = (sub, plan.channels)
    weights_c[27] = (lanes_at(shape, 1) == lanes_at(shape, 0) + base).astype(jnp.float32).astype(jnp.bfloat16)
    order[...] = merged_order(plan.nr, 4, plan.tl, plan.cells)
    pixels = pixel_order(plan.tl, plan.hl, plan.w)
    shape = (local, 128)
    places = [
        (lanes_at(shape, 0) + k * local == lanes_at(shape, 1)).astype(jnp.float32).astype(jnp.bfloat16)
        for k in range(4)
    ]
    copies[0].wait()
    fine = one_hot_dot(fine_ref[...], pixels, ((0,), (0,))).astype(jnp.bfloat16)
    copies[1].wait()
    quarters = [one_hot_dot(coarse_ref[...], place, ((0,), (0,))) for place in places]
    copies[2].wait()
    for s_f in range(plan.nf):
        for s_r in range(plan.nr):
            dest, c = s_r * plan.nf + s_f, s_r * plan.slice_width + s_f * sub
            for k in range(chunks):
                out_ref[dest, k * local : (k + 1) * local, :] = g_ref[:, k * 128 : (k + 1) * 128]
            at = chunks * local
            out_ref[dest, at : at + sub, :] = fine[c : c + sub]
            coarse = sum(quarters[k][c + 8 * k : c + 8 * k + 8] for k in range(4))
            out_ref[dest, at + sub : at + sub + 8, :] = coarse.astype(jnp.bfloat16)
    for copy in copies[3:7]:
        copy.wait()
    for k in range(4):
        columns[k] = jnp.broadcast_to(own_column(rows[k], base, sub), (sub, 128))
    for copy in copies[7:]:
        copy.wait()


def by_frame_device(plan, got_ref, at, height):
    return jnp.concatenate(
        [
            jnp.concatenate(
                [got_ref[r * plan.nf + f, at : at + height, :] for r in range(plan.nr)], axis=1
            )
            for f in range(plan.nf)
        ],
        axis=0,
    )


def in_places(plan, merged, height):
    width = plan.tl * plan.image
    return [
        jnp.concatenate(
            [merged[f * height : (f + 1) * height, k * width : (k + 1) * width] for f in range(plan.nf)],
            axis=1,
        )
        for k in range(4)
    ]


def frame_sum(products_ref, tap, sub, lane, places, image):
    near = products_ref[pl.ds((18 + tap) * sub, sub), :]
    middle = products_ref[pl.ds((9 + tap) * sub, sub), :]
    far = products_ref[pl.ds(tap * sub, sub), :]
    return near + moved(middle, image, lane < places - image) + moved(far, 2 * image, lane < places - 2 * image)


def coarse_kernel(plan, got_ref, weights, columns, order, out_ref, sums_ref, source, products):
    sub, nr, nf, cells, tl, local = plan.sub, plan.nr, plan.nf, plan.cells, plan.tl, plan.local
    chunks = plan.channels // 128
    for s_f in range(nf):
        for s_r in range(nr):
            for t in range(tl):
                at = (s_f * tl + t) * plan.image + s_r * cells
                for k in range(chunks):
                    source[at : at + cells, k * 128 : (k + 1) * 128] = got_ref[
                        s_r * nf + s_f, k * local + t * cells : k * local + (t + 1) * cells, :
                    ]
    products[...] = lax.dot_general(
        weights[...].reshape(28 * sub, plan.channels),
        source[...],
        (((1,), (1,)), ((), ())),
        preferred_element_type=jnp.float32,
    )
    packed = by_frame_device(plan, got_ref, chunks * local + sub, 8)
    merged = one_hot_dot(packed, order[...], ((1,), (0,)))
    values = jnp.concatenate(in_places(plan, merged, 8), axis=0)
    gain, bias = columns[0][:, 0:1], columns[1][:, 0:1]
    entries = plan.places * plan.group_width
    normed, slope, inv_std = normalised([values], gain, bias, entries, plan.group_width)
    lane, has_left, has_right, has_up, has_down = plan.place_masks()
    by_col = []
    for col in range(3):
        parts = [frame_sum(products, 3 * row + col, sub, lane, plan.places, plan.image) for row in range(3)]
        by_col.append(parts[1] + moved(parts[0], plan.w, has_down) + moved(parts[2], -plan.w, has_up))
    conv = by_col[1] + moved(by_col[0], 1, has_right) + moved(by_col[2], -1, has_left)
    cot = products[pl.ds(27 * sub, sub), :]
    grads, one, two = finished([conv], normed, slope, [cot], gain, inv_std, entries, plan.group_width)
    quartered = (grads[0] * 0.25).astype(jnp.bfloat16)
    for dest in range(plan.count):
        out_ref[dest] = quartered
    sums_ref[...] = jnp.concatenate([as_row(one), as_row(two)], axis=0)


def fine_kernel(plan, got_ref, acts_ref, columns, order, sums_ref, weights, out_ref, products):
    sub, nr, nf = plan.sub, plan.nr, plan.nf
    f, r = lax.axis_index("frames"), lax.axis_index("rows")
    products[...] = lax.dot_general(
        weights[...].reshape(27 * sub, plan.channels),
        got_ref[...].reshape(plan.channels, plan.places),
        (((1,), (0,)), ((), ())),
        preferred_element_type=jnp.float32,
    )
    packed = by_frame_device(plan, acts_ref, plan.channels // 128 * plan.local, sub)
    parts = in_places(plan, one_hot_dot(packed, order[...], ((1,), (0,))), sub)
    gain, bias = columns[2][:, 0:1], columns[3][:, 0:1]
    entries = 4 * plan.places * plan.group_width
    normed, slope, inv_std = normalised(parts, gain, bias, entries, plan.group_width)
    lane, has_left, has_right, has_up, has_down = plan.place_masks()
    by_row = []
    for row in range(3):
        a, b, c = [frame_sum(products, 3 * row + col, sub, lane, plan.places, plan.image) for col in range(3)]
        by_row.append((a + b + moved(c, -1, has_left), moved(a, 1, has_right) + b + c))
    convs = [by_row[0][q] + by_row[1][q] + moved(by_row[2][q], -plan.w, has_up) for q in range(2)]
    convs += [moved(by_row[0][q], plan.w, has_down) + by_row[1][q] + by_row[2][q] for q in range(2)]
    cot = got_ref[r * nf + f].astype(jnp.float32)
    grads, one, two = finished(convs, normed, slope, [cot] * 4, gain, inv_std, entries, plan.group_width)
    width = plan.tl * plan.image
    stacked = jnp.concatenate(
        [
            jnp.concatenate(
                [grads[pq][:, s_f * width : (s_f + 1) * width].astype(jnp.bfloat16) for pq in range(4)], axis=1
            )
            for s_f in range(nf)
        ],
        axis=0,
    )
    sent = one_hot_dot(stacked, order[...], ((1,), (1,))).astype(jnp.bfloat16)
    sums = jnp.concatenate([as_row(one), as_row(two), sums_ref[...]], axis=0)
    top = sums.astype(jnp.bfloat16).astype(jnp.float32)
    coded = jnp.concatenate([top, sums - top], axis=0).astype(jnp.bfloat16)
    for s_f in range(nf):
        for s_r in range(nr):
            out_ref[s_r * nf + s_f, 0:sub, :] = sent[s_f * sub : (s_f + 1) * sub, s_r * 128 : (s_r + 1) * 128]
            out_ref[s_r * nf + s_f, sub : sub + 8, :] = coded


def spread_kernel(plan, got_ref, out_ref, sums_ref):
    sub, nr, nf = plan.sub, plan.nr, plan.nf
    order = pixel_order(plan.tl, plan.hl, plan.w)
    source = got_ref[:, 0:sub, :].reshape(plan.channels, 4 * plan.local)
    out_ref[...] = one_hot_dot(order, source, ((1,), (1,))).astype(jnp.bfloat16)
    columns = []
    for s_r in range(nr):
        held = 0.0
        for s_f in range(nf):
            coded = got_ref[s_r * nf + s_f, sub : sub + 8, :].astype(jnp.float32)
            sums = coded[0:4] + coded[4:8]
            held = held + (pltpu.roll(sums, s_f * sub, 1) if s_f else sums)
        columns.append(held)
    rows = jnp.concatenate(columns, axis=1)
    sums_ref[...] = jnp.concatenate([rows, jnp.zeros_like(rows)], axis=0)


def total_kernel(scales, both_ref, result_ref, result_hbm, out_hbms, rows_ref, sems):
    copies = fetched([(result_ref, result_hbm)], sems)
    rows = sum(both_ref[k] for k in range(both_ref.shape[0]))
    for k in range(4):
        rows_ref[k] = rows[k : k + 1] * scales[k]
    for k in range(4):
        copies.append(pltpu.make_async_copy(rows_ref.at[k], out_hbms[k], sems.at[k + 1]))
        copies[-1].start()
    for copy in copies:
        copy.wait()


def in_vmem(count):
    return [pl.BlockSpec(memory_space=pltpu.VMEM)] * count


def in_hbm(count):
    return [pl.BlockSpec(memory_space=pltpu.HBM)] * count


def kept(array):
    return pltpu.with_memory_space_constraint(array, pltpu.HBM)


def shape_of(shape, kind):
    return jax.ShapeDtypeStruct(shape, kind)


LIMIT = pltpu.CompilerParams(vmem_limit_bytes=40 * 1024 * 1024)


def fast_shards(
    plan,
    acts_fine,
    acts_coarse,
    grad_coarse,
    gain_fine,
    bias_fine,
    kernel_fine,
    gain_coarse,
    bias_coarse,
    kernel_coarse,
):
    nd = lax.axis_size("dp")
    count, sub, channels, places, local = plan.count, plan.sub, plan.channels, plan.places, plan.local
    chunks = channels // 128
    f32, bf16 = jnp.float32, jnp.bfloat16
    rows = [part.reshape(1, channels) for part in (gain_coarse, bias_coarse, gain_fine, bias_fine)]
    packed, weights_c, weights_f, columns, order = pl.pallas_call(
        functools.partial(pack_kernel, plan),
        out_shape=(
            shape_of((count, chunks * local + sub + 8, 128), bf16),
            shape_of((28, sub, channels), bf16),
            shape_of((27, sub, channels), bf16),
            shape_of((4, sub, 128), f32),
            shape_of((4 * plan.nr * local, 4 * plan.nr * local), bf16),
        ),
        in_specs=in_hbm(9),
        out_specs=tuple(in_vmem(5)),
        scratch_shapes=[
            pltpu.VMEM((local, channels), bf16),
            pltpu.VMEM((local, channels), bf16),
            pltpu.VMEM((4 * local, channels), bf16),
            pltpu.VMEM((4, 1, channels), f32),
            pltpu.SemaphoreType.DMA((9,)),
        ],
        compiler_params=LIMIT,
    )(
        kept(grad_coarse.reshape(local, channels)),
        kept(acts_coarse.reshape(local, channels)),
        kept(acts_fine.reshape(4 * local, channels)),
        kept(kernel_coarse),
        kept(kernel_fine),
        *[kept(row) for row in rows],
    )
    got = lax.all_to_all(packed, BLOCK, 0, 0)
    quartered, coarse_sums = pl.pallas_call(
        functools.partial(coarse_kernel, plan),
        out_shape=(shape_of((count, sub, places), bf16), shape_of((2, 128), f32)),
        in_specs=in_vmem(4),
        out_specs=tuple(in_vmem(2)),
        scratch_shapes=[pltpu.VMEM((places, channels), bf16), pltpu.VMEM((28 * sub, places), f32)],
        compiler_params=LIMIT,
    )(got, weights_c, columns, order)
    spread = lax.all_to_all(quartered, BLOCK, 0, 0)
    sent = pl.pallas_call(
        functools.partial(fine_kernel, plan),
        out_shape=shape_of((count, sub + 8, 128), bf16),
        in_specs=in_vmem(6),
        out_specs=in_vmem(1)[0],
        scratch_shapes=[pltpu.VMEM((27 * sub, places), f32)],
        compiler_params=LIMIT,
    )(spread, got, columns, order, coarse_sums, weights_f)
    back = lax.all_to_all(sent, BLOCK, 0, 0)
    cells = nd * places
    fine_scale, coarse_scale = 1.0 / math.sqrt(4 * cells), 1.0 / math.sqrt(cells)
    out, sums = pl.pallas_call(
        functools.partial(spread_kernel, plan),
        out_shape=(pltpu.VMEM((4 * local, channels), bf16), shape_of((8, channels), f32)),
        in_specs=in_vmem(1),
        out_specs=tuple(in_vmem(2)),
        compiler_params=LIMIT,
    )(back)
    both = lax.all_gather(sums, "dp")
    out, sums = pl.pallas_call(
        functools.partial(total_kernel, (fine_scale, fine_scale, coarse_scale, coarse_scale)),
        out_shape=(pltpu.HBM((4 * local, channels), bf16), (pltpu.HBM((1, channels), f32),) * 4),
        in_specs=in_vmem(2),
        out_specs=(in_hbm(1)[0], tuple(in_hbm(4))),
        scratch_shapes=[pltpu.VMEM((4, 1, channels), f32), pltpu.SemaphoreType.DMA((5,))],
        compiler_params=LIMIT,
    )(both, out)
    bias_f, gain_f, bias_c, gain_c = [part.reshape(channels) for part in sums]
    return out.reshape(acts_fine.shape), gain_f, bias_f, gain_c, bias_c


def solution(mesh):
    def shards(*arrays):
        sizes = (lax.axis_size("frames"), lax.axis_size("rows"))
        plan = Plan(sizes, arrays[1].shape[1:], arrays[5].shape[1])
        if plan.fits:
            return fast_shards(plan, *arrays)
        return plain_shards(*arrays)

    in_specs = (
        P("dp", "frames", "rows", None, None),
        P("dp", "frames", "rows", None, None),
        P("dp", "frames", "rows", None, None),
        P(),
        P(),
        P(None, "rows", None),
        P(),
        P(),
        P(None, "rows", None),
    )
    out_specs = (P("dp", "frames", "rows", None, None), P(), P(), P(), P())
    return jax.shard_map(shards, mesh=mesh, in_specs=in_specs, out_specs=out_specs, check_vma=False)
```

```python
import functools
import math

import jax
import jax.numpy as jnp
from jax import lax
from jax.experimental import pallas as pl
from jax.experimental.pallas import tpu as pltpu
from jax.sharding import PartitionSpec as P

GROUPS = 32
EPSILON = 1e-06
BLOCK = ("rows", "pairs", "member")
PLAIN_BLOCK = ("frames", "rows")


def plain_everyone(block, count):
    copies = jnp.broadcast_to(block[None], (count,) + block.shape)
    return lax.all_to_all(copies, PLAIN_BLOCK, 0, 0)


def ahead(field, axis, distance):
    size = field.shape[axis]
    if distance == 0:
        return field
    widths = [(0, 0)] * field.ndim
    if distance > 0:
        widths[axis] = (0, distance)
        kept = lax.slice_in_dim(field, distance, size, axis=axis)
    else:
        widths[axis] = (-distance, 0)
        kept = lax.slice_in_dim(field, 0, size + distance, axis=axis)
    return jnp.pad(kept, widths)


def tap_products(source, kernel):
    sub = kernel.shape[1]
    frames, rows, cols, channels = source.shape
    products = lax.dot_general(
        kernel.reshape(27 * sub, channels),
        source.reshape(frames * rows * cols, channels),
        (((1,), (1,)), ((), ())),
        preferred_element_type=jnp.float32,
    ).reshape(3, 3, 3, sub, frames, rows, cols)
    return sum(ahead(products[depth], 3, 2 - depth) for depth in range(3))


def coarse_conv(source, kernel):
    spatial = tap_products(source, kernel)
    total = 0.0
    for row in range(3):
        part = sum(ahead(spatial[row, col], 3, 1 - col) for col in range(3))
        total = total + ahead(part, 2, 1 - row)
    return total


def fine_conv(source, kernel):
    spatial = tap_products(source, kernel)
    result = []
    for p in range(2):
        rows_of = []
        for q in range(2):
            total = 0.0
            for row in range(3):
                part = sum(ahead(spatial[row, col], 3, (q + 1 - col) // 2) for col in range(3))
                total = total + ahead(part, 2, (p + 1 - row) // 2)
            rows_of.append(total)
        result.append(jnp.stack(rows_of, 1))
    return jnp.stack(result, 1)


def group_total(sums, group_width):
    sub = sums.shape[-1]
    if sub % group_width == 0:
        grouped = jnp.sum(sums.reshape(-1, sub // group_width, group_width), axis=-1)
        return jnp.repeat(grouped, group_width, axis=-1)
    spread = jnp.moveaxis(lax.all_gather(sums, "frames"), 0, 1).reshape(sums.shape[0], -1, group_width)
    mine = lax.axis_index("frames") * sub // group_width
    grouped = lax.dynamic_index_in_dim(jnp.sum(spread, -1), mine, 1)
    return jnp.broadcast_to(grouped, sums.shape)


def level(acts, conv_grad, cotangent, gain, bias, group_width):
    sub = acts.shape[0]
    places = acts.size // sub
    values = acts.astype(jnp.float32).reshape(sub, places)
    conv_grad = conv_grad.reshape(sub, places)
    entries = places * group_width
    moments = group_total(
        jnp.stack([jnp.sum(values, 1), jnp.sum(values * values, 1)]), group_width
    ) / entries
    mean = moments[0]
    inv_std = lax.rsqrt(moments[1] - mean * mean + EPSILON)
    normed = (values - mean[:, None]) * inv_std[:, None]
    preact = gain[:, None] * normed + bias[:, None]
    squash = jax.nn.sigmoid(preact)
    pre_grad = conv_grad * squash * (1.0 + preact * (1.0 - squash))
    sums = jnp.stack([jnp.sum(pre_grad, 1), jnp.sum(pre_grad * normed, 1)])
    terms = group_total(sums * gain, group_width) / entries
    grad = cotangent.reshape(sub, places) + inv_std[:, None] * (
        gain[:, None] * pre_grad - terms[0][:, None] - normed * terms[1][:, None]
    )
    return grad, sums


def plain_shards(
    acts_fine,
    acts_coarse,
    grad_coarse,
    gain_fine,
    bias_fine,
    kernel_fine,
    gain_coarse,
    bias_coarse,
    kernel_coarse,
):
    nf, nr, nd = lax.axis_size("frames"), lax.axis_size("rows"), lax.axis_size("dp")
    count = nf * nr
    channels = acts_fine.shape[-1]
    slice_width = kernel_fine.shape[1]
    sub = slice_width // nf
    group_width = channels // GROUPS
    tl, hl, w = acts_coarse.shape[1:4]
    frames, rows = tl * nf, hl * nr
    f, r = lax.axis_index("frames"), lax.axis_index("rows")

    gathered = plain_everyone(grad_coarse[0], count)
    source = (
        gathered.reshape(nf, nr, tl, hl, w, channels)
        .transpose(0, 2, 1, 3, 4, 5)
        .reshape(frames, rows, w, channels)
    )
    coarse_in = acts_coarse[0].reshape(tl, hl, w, nr, nf, sub).transpose(4, 3, 5, 0, 1, 2)
    coarse_in = lax.all_to_all(coarse_in.reshape(count, sub, tl * hl * w), PLAIN_BLOCK, 0, 0)
    fine_in = acts_fine[0].reshape(tl, hl, 2, w, 2, nr, nf, sub).transpose(6, 5, 7, 2, 4, 0, 1, 3)
    fine_in = lax.all_to_all(fine_in.reshape(count, sub, 4 * tl * hl * w), PLAIN_BLOCK, 0, 0)

    def mine(vector):
        return lax.dynamic_slice_in_dim(vector, r * slice_width + f * sub, sub)

    def own(kernel):
        return lax.dynamic_slice_in_dim(kernel, f * sub, sub, axis=1)

    coarse_vals = (
        coarse_in.reshape(nf, nr, sub, tl, hl, w).transpose(2, 0, 3, 1, 4, 5).reshape(sub, frames, rows, w)
    )
    cot = lax.dynamic_slice_in_dim(source, r * slice_width + f * sub, sub, axis=3)
    cot = cot.astype(jnp.float32).transpose(3, 0, 1, 2)
    conv = coarse_conv(source, own(kernel_coarse))
    coarse_grad, coarse_sums = level(
        coarse_vals, conv, cot, mine(gain_coarse), mine(bias_coarse), group_width
    )
    quartered = (coarse_grad * 0.25).astype(jnp.bfloat16)
    spread = plain_everyone(quartered, count)
    source_fine = (
        spread.reshape(nf, nr, sub, frames, rows, w)
        .transpose(3, 4, 5, 1, 0, 2)
        .reshape(frames, rows, w, channels)
    )
    conv = fine_conv(source_fine, own(kernel_fine))
    fine_vals = (
        fine_in.reshape(nf, nr, sub, 2, 2, tl, hl, w)
        .transpose(2, 3, 4, 0, 5, 1, 6, 7)
        .reshape(sub, 2, 2, frames, rows, w)
    )
    cot = jnp.broadcast_to(
        quartered.astype(jnp.float32).reshape(sub, 1, 1, frames, rows, w), conv.shape
    )
    fine_grad, fine_sums = level(
        fine_vals, conv, cot, mine(gain_fine), mine(bias_fine), group_width
    )
    back = (
        fine_grad.astype(jnp.bfloat16)
        .reshape(sub, 2, 2, nf, tl, nr, hl, w)
        .transpose(3, 5, 0, 1, 2, 4, 6, 7)
        .reshape(count, sub, 4 * tl * hl * w)
    )
    sums = plain_everyone(jnp.concatenate([fine_sums, coarse_sums]), count)
    back = lax.all_to_all(back, PLAIN_BLOCK, 0, 0)
    out = (
        back.reshape(nf, nr, sub, 2, 2, tl, hl, w)
        .transpose(5, 6, 3, 7, 4, 1, 0, 2)
        .reshape(1, tl, 2 * hl, 2 * w, channels)
    )
    sums = sums.reshape(nf, nr, 4, sub).transpose(2, 1, 0, 3).reshape(4, channels)
    totals = lax.psum(sums, "dp")
    cells = nd * frames * rows * w
    scale_fine = 1.0 / jnp.sqrt(jnp.float32(4 * cells))
    scale_coarse = 1.0 / jnp.sqrt(jnp.float32(cells))
    return (
        out,
        totals[1] * scale_fine,
        totals[0] * scale_fine,
        totals[3] * scale_coarse,
        totals[2] * scale_coarse,
    )


def lanes_at(shape, axis):
    return lax.broadcasted_iota(jnp.int32, shape, axis)


def one_hot(found):
    return found.astype(jnp.float32).astype(jnp.bfloat16)


def pixel_order(plan, swapped):
    tl, hl, w = plan.tl, plan.hl, plan.w // 2
    size = 4 * plan.local
    lane = lanes_at((size, size), 1)
    j, i, t = lane % w, lane // w % hl, lane // (w * hl) % tl
    q, p = lane // (w * hl * tl) % 2, lane // (2 * w * hl * tl) % 2
    half = lane // (4 * w * hl * tl)
    if swapped:
        half = 1 - half
    pixel = (t * 2 * hl + 2 * i + p) * 4 * w + 2 * (half * w + j) + q
    return one_hot(lanes_at((size, size), 0) == pixel)


def merged_order(nr, outer, tl, cells):
    size = nr * outer * tl * cells
    a = lanes_at((size, size), 0)
    cell, t = a % cells, a // cells % tl
    o, dev = a // (cells * tl) % outer, a // (cells * tl * outer)
    target = ((o * tl + t) * nr + dev) * cells + cell
    return one_hot(lanes_at((size, size), 1) == target)


def column_order(plan):
    w = plan.w // 2
    lines = plan.places // plan.w
    lane = lanes_at((1, 4 * lines * w + 4 * lines), 1)
    inner = lane % (lines * w)
    place = inner // w * plan.w + lane // (lines * w) * w + inner % w
    past = lane - 2 * lines * w
    border = past % lines * plan.w + jnp.where(past < 2 * lines, w, w - 1)
    wanted = jnp.where(past >= 0, border, place)
    shape = (plan.places, 2 * lines * w + 4 * lines)
    return one_hot(lanes_at(shape, 0) == wanted[:, : shape[1]])


def one_hot_dot(a, b, dims):
    return lax.dot_general(a, b, (dims, ((), ())), preferred_element_type=jnp.float32)


def moved(field, distance, kept):
    size = field.shape[1]
    return jnp.where(kept, pltpu.roll(field, (-distance) % size, 1), 0.0)


def own_column(row, base, sub):
    shape = (sub, row.shape[1])
    mine = lanes_at(shape, 1) == lanes_at(shape, 0) + base
    return jnp.sum(jnp.where(mine, row, 0.0), axis=1, keepdims=True)


def as_row(column):
    shape = (column.shape[0], 128)
    here = lanes_at(shape, 1) == lanes_at(shape, 0)
    return jnp.sum(jnp.where(here, column, 0.0), axis=0, keepdims=True)


def terms(value, count):
    found = []
    for _ in range(count):
        found.append(value.astype(jnp.bfloat16).astype(jnp.float32))
        value = value - found[-1]
    return found


def in_groups(column, group_width):
    sub = column.shape[0]
    grouped = jnp.sum(column.reshape(sub // group_width, group_width, 1), axis=1, keepdims=True)
    return jnp.broadcast_to(grouped, (sub // group_width, group_width, 1)).reshape(sub, 1)


def in_lane_groups(row, group_width):
    lane = lanes_at(row.shape, 1)
    size = row.shape[1]
    step = 1
    while step < group_width:
        up, down = pltpu.roll(row, size - step, 1), pltpu.roll(row, step, 1)
        row = row + jnp.where(lane // step % 2 == 0, up, down)
        step *= 2
    return row


def total(parts):
    return sum(jnp.sum(part, axis=1, keepdims=True) for part in parts)


def statistics(one, two, entries, group_width):
    mean = in_groups(one, group_width) / entries
    square = in_groups(two, group_width) / entries
    return mean, lax.rsqrt(square - mean * mean + EPSILON)


def normalised(parts, gain, bias, mean, inv_std):
    normed, slope = [], []
    for part in parts:
        unit = (part - mean) * inv_std
        preact = gain * unit + bias
        squash = jax.nn.sigmoid(preact)
        normed.append(unit)
        slope.append(squash * (1.0 + preact * (1.0 - squash)))
    return normed, slope


class Plan:
    def __init__(self, mesh_sizes, acts_coarse, slice_width):
        self.nf, self.nr = mesh_sizes
        self.count = self.nf * self.nr
        self.tl, self.hl, self.w, self.channels = acts_coarse
        self.slice_width = slice_width
        self.sub = slice_width // self.nf
        self.cells = self.hl * self.w
        self.local = self.tl * self.cells
        self.image = self.cells * self.nr
        self.frames = self.tl * self.nf
        self.places = self.frames * self.image
        self.group_width = self.channels // GROUPS
        self.chunks = self.channels // 128
        self.acts_at = self.chunks * self.local
        self.packed_at = self.acts_at + self.sub
        self.stats_at = self.packed_at + 8
        self.block_rows = self.stats_at + 8
        self.fits = (
            self.sub == 32
            and self.slice_width == 128
            and self.group_width == 16
            and self.cells == 16
            and self.w == 8
            and self.tl == 2
            and self.nr == 4
            and self.nf == 4
            and self.slice_width * self.nr == self.channels
        )

    def place_masks(self, w):
        lane = lanes_at((1, self.places // self.w * w), 1)
        col, row = lane % w, lane // w % (self.hl * self.nr)
        last_row = self.hl * self.nr - 1
        return (lane, col > 0, col < w - 1, row > 0, row < last_row)


def fetched(pairs, sems):
    copies = [pltpu.make_async_copy(src, dst, sems.at[k]) for k, (src, dst) in enumerate(pairs)]
    for copy in copies:
        copy.start()
    return copies


def own_place(plan):
    pair, member, r = lax.axis_index("pairs"), lax.axis_index("member"), lax.axis_index("rows")
    return pair, member, r, r * plan.slice_width + (2 * pair + member) * plan.sub


def pack_kernel(
    plan,
    g_hbm,
    coarse_hbm,
    fine_hbm,
    kernel_c,
    kernel_f,
    gain_c,
    bias_c,
    gain_f,
    bias_f,
    out_ref,
    fine_ref,
    weights_c,
    weights_f,
    columns,
    order,
    fine_order,
    by_column,
    rows,
    g_ref,
    coarse_ref,
    sems,
):
    sub, chunks, local = plan.sub, plan.chunks, plan.local
    pair, member, r, base = own_place(plan)
    own = pl.ds(pl.multiple_of((2 * pair + member) * sub, sub), sub)
    both = pl.ds(pl.multiple_of(2 * pair * sub, 2 * sub), 2 * sub)
    copies = fetched(
        [(fine_hbm, fine_ref), (coarse_hbm, coarse_ref), (g_hbm, g_ref)]
        + [(row, rows.at[k]) for k, row in enumerate((gain_c, bias_c, gain_f, bias_f))]
        + [(kernel_c.at[:, own, :], weights_c.at[pl.ds(0, 27)]), (kernel_f.at[:, both, :], weights_f)],
        sems,
    )
    shape = (sub, plan.channels)
    weights_c[27] = one_hot(lanes_at(shape, 1) == lanes_at(shape, 0) + base)
    order[...] = merged_order(plan.nr, 4, plan.tl, plan.cells)
    fine_order[...] = merged_order(plan.nr, 8, plan.tl, plan.cells // 2)
    by_column[...] = column_order(plan)
    shape = (local, 128)
    places = [one_hot(lanes_at(shape, 0) + k * local == lanes_at(shape, 1)) for k in range(4)]
    orders = [pixel_order(plan, swapped) for swapped in (False, True)]
    copies[0].wait()
    acts = fine_ref[...]
    halves = [one_hot_dot(acts, order_of, ((0,), (0,))).astype(jnp.bfloat16) for order_of in orders]
    values = acts.astype(jnp.float32)
    one = jnp.sum(values, axis=0, keepdims=True)
    two = jnp.sum(values * values, axis=0, keepdims=True)
    stats = terms(one, 3) + terms(two, 3)
    stats = jnp.concatenate(stats + [jnp.zeros_like(one)] * 2, axis=0).astype(jnp.bfloat16)
    copies[1].wait()
    quarters = [one_hot_dot(coarse_ref[...], place, ((0,), (0,))) for place in places]
    copies[2].wait()
    low = lanes_at((sub, 128), 1) < 64
    for s_r in range(plan.nr):
        for s_f in range(plan.nf):
            dest, c = s_r * plan.nf + s_f, s_r * plan.slice_width + s_f * sub
            for k in range(chunks):
                out_ref[dest, k * local : (k + 1) * local, :] = g_ref[:, k * 128 : (k + 1) * 128]
            first, half = s_r * plan.slice_width + s_f // 2 * 2 * sub, s_f % 2
            upper, lower = halves[half][first : first + sub], halves[1 - half][first + sub : first + 2 * sub]
            out_ref[dest, plan.acts_at : plan.packed_at, :] = jnp.where(low, upper, lower)
            coarse = sum(quarters[k][c + 8 * k : c + 8 * k + 8] for k in range(4))
            out_ref[dest, plan.packed_at : plan.stats_at, :] = coarse.astype(jnp.bfloat16)
            out_ref[dest, plan.stats_at : plan.block_rows, :] = stats[:, s_r * 128 : (s_r + 1) * 128]
    for copy in copies[3:7]:
        copy.wait()
    first = r * plan.slice_width + 2 * pair * sub
    for k in range(2):
        columns[k, 0:sub, :] = jnp.broadcast_to(own_column(rows[k], base, sub), (sub, 128))
        columns[2 + k] = jnp.broadcast_to(own_column(rows[2 + k], first, 2 * sub), (2 * sub, 128))
    for copy in copies[7:]:
        copy.wait()


def by_frame_device(plan, got_ref, at, height):
    return jnp.concatenate(
        [
            jnp.concatenate(
                [got_ref[r * plan.nf + f, at : at + height, :] for r in range(plan.nr)], axis=1
            )
            for f in range(plan.nf)
        ],
        axis=0,
    )


def in_places(plan, merged, height):
    width = plan.tl * plan.image
    return [
        jnp.concatenate(
            [merged[f * height : (f + 1) * height, k * width : (k + 1) * width] for f in range(plan.nf)],
            axis=1,
        )
        for k in range(4)
    ]


def frame_sum(products_ref, taps, sub, lane, places, image):
    near, middle, far = [products_ref[pl.ds(tap * sub, sub), :] for tap in reversed(taps)]
    return near + moved(middle, image, lane < places - image) + moved(far, 2 * image, lane < places - 2 * image)


def coarse_kernel(plan, got_ref, weights, columns, order, by_column, out_ref, sums_ref, source, products):
    sub, nr, nf, cells, tl, local = plan.sub, plan.nr, plan.nf, plan.cells, plan.tl, plan.local
    for s_f in range(nf):
        for s_r in range(nr):
            for t in range(tl):
                at = (s_f * tl + t) * plan.image + s_r * cells
                for k in range(plan.chunks):
                    source[at : at + cells, k * 128 : (k + 1) * 128] = got_ref[
                        s_r * nf + s_f, k * local + t * cells : k * local + (t + 1) * cells, :
                    ]
    products[...] = lax.dot_general(
        weights[...].reshape(28 * sub, plan.channels),
        source[...],
        (((1,), (1,)), ((), ())),
        preferred_element_type=jnp.float32,
    )
    packed = by_frame_device(plan, got_ref, plan.packed_at, 8)
    merged = one_hot_dot(packed, order[...], ((1,), (0,)))
    values = jnp.concatenate(in_places(plan, merged, 8), axis=0)
    gain, bias = columns[0][0:sub, 0:1], columns[1][0:sub, 0:1]
    entries = plan.places * plan.group_width
    mean, inv_std = statistics(total([values]), total([values * values]), entries, plan.group_width)
    (normed,), (slope,) = normalised([values], gain, bias, mean, inv_std)
    lane, has_left, has_right, has_up, has_down = plan.place_masks(plan.w)
    by_col = []
    for col in range(3):
        parts = [
            frame_sum(products, [9 * depth + 3 * row + col for depth in range(3)], sub, lane, plan.places, plan.image)
            for row in range(3)
        ]
        by_col.append(parts[1] + moved(parts[0], plan.w, has_down) + moved(parts[2], -plan.w, has_up))
    conv = by_col[1] + moved(by_col[0], 1, has_right) + moved(by_col[2], -1, has_left)
    cot = products[pl.ds(27 * sub, sub), :]
    pre = conv * slope
    one, two = total([pre]), total([pre * normed])
    group_one = in_groups(gain * one, plan.group_width) / entries
    group_two = in_groups(gain * two, plan.group_width) / entries
    grad = cot + inv_std * (gain * pre - group_one - normed * group_two)
    quartered = (grad * 0.25).astype(jnp.bfloat16)
    sent = one_hot_dot(quartered, by_column[...], ((1,), (0,))).astype(jnp.bfloat16)
    low = lanes_at((sub // 2, 128), 1) < 64
    for half in range(2):
        at = half * 256
        border = sent[:, 512 + half * 128 : 640 + half * 128]
        border = jnp.where(low, border[: sub // 2], border[sub // 2 :])
        for dest in range(half, plan.count, 2):
            out_ref[dest, 0:sub, :] = sent[:, at : at + 128]
            out_ref[dest, sub : 2 * sub, :] = sent[:, at + 128 : at + 256]
            out_ref[dest, 2 * sub : 2 * sub + sub // 2, :] = border
    sums_ref[...] = jnp.concatenate([as_row(one), as_row(two)], axis=0)


def halves_at(plan, merged):
    sub = plan.sub
    turned = jnp.concatenate([pltpu.roll(merged[:, k * 128 : (k + 1) * 128], 64, 1) for k in range(4)], axis=1)
    low = lanes_at((sub, 128), 1) < 64
    parts = []
    for pq in range(4):
        groups = []
        for group in range(2):
            e = 4 * group + pq
            at = e // 2 * 128
            strips = []
            for m in range(plan.nf // 2):
                first, second = slice(2 * m * sub, (2 * m + 1) * sub), slice((2 * m + 1) * sub, (2 * m + 2) * sub)
                if e % 2 == 0:
                    strips.append(jnp.where(low, merged[first, at : at + 128], turned[second, at : at + 128]))
                else:
                    strips.append(jnp.where(low, turned[first, at : at + 128], merged[second, at : at + 128]))
            groups.append(jnp.concatenate(strips, axis=1))
        parts.append(jnp.concatenate(groups, axis=0))
    return parts


def halves_from(plan, parts):
    sub = plan.sub
    low = lanes_at((sub, 128), 1) < 64
    down = []
    for f in range(plan.nf):
        across = []
        for v in range(4):
            pair = []
            for e in (2 * v, 2 * v + 1):
                group, pq = e // 4, e % 4
                strip = parts[pq][group * sub : (group + 1) * sub, f // 2 * 128 : (f // 2 + 1) * 128]
                pair.append(strip if e % 2 == f % 2 else pltpu.roll(strip, 64, 1))
            across.append(jnp.where(low, pair[0], pair[1]))
        down.append(jnp.concatenate(across, axis=1))
    return jnp.concatenate(down, axis=0)


def fine_kernel(
    plan, got_ref, acts_ref, columns, order, sums_ref, weights, out_ref, source, border, products, beyond
):
    sub, nr, nf, wide = plan.sub, plan.nr, plan.nf, 2 * plan.sub
    pair, member, r, _ = own_place(plan)
    w = plan.w // 2
    lines = plan.places // plan.w
    places = lines * w
    for k in range(2):
        source[:, k * 128 : (k + 1) * 128] = got_ref[:, k * sub : (k + 1) * sub, :].reshape(plan.channels, 128)
    products[...] = one_hot_dot(weights[...].reshape(27 * wide, plan.channels), source[...], ((1,), (0,)))
    packed = got_ref[:, wide : wide + sub // 2, :].reshape(plan.count * sub // 2, 128)
    shape = (128, places)
    beside = lanes_at(shape, 1) == lanes_at(shape, 0) % lines * w + (1 - member) * (w - 1)
    for k in range(2):
        here = one_hot(beside & (lanes_at(shape, 0) // lines == k))
        found = one_hot_dot(packed, here, ((1,), (0,))).astype(jnp.bfloat16)
        for s in range(plan.count):
            border[s * sub + k * (sub // 2) : s * sub + (k + 1) * (sub // 2), :] = found[
                s * (sub // 2) : (s + 1) * (sub // 2)
            ]
    facing = jnp.concatenate([weights[3 * k + 2 * member] for k in range(9)], axis=0)
    beyond[...] = one_hot_dot(facing, border[...], ((1,), (0,)))
    merged = one_hot_dot(by_frame_device(plan, acts_ref, plan.acts_at, sub), order[...], ((1,), (0,)))
    parts = halves_at(plan, merged)
    stats = sum(
        acts_ref[s, plan.stats_at : plan.block_rows, :].astype(jnp.float32) for s in range(plan.count)
    )
    entries = 4 * plan.places * plan.group_width
    one = own_column(stats[0:1] + stats[1:2] + stats[2:3], pair * wide, wide)
    two = own_column(stats[3:4] + stats[4:5] + stats[5:6], pair * wide, wide)
    mean, inv_std = statistics(one, two, entries, plan.group_width)
    gain, bias = columns[2][:, 0:1], columns[3][:, 0:1]
    normed, slope = normalised(parts, gain, bias, mean, inv_std)
    lane, has_left, has_right, has_up, has_down = plan.place_masks(w)
    image = plan.image // 2
    right, left = (1 - member).astype(jnp.float32), member.astype(jnp.float32)
    by_row = []
    for row in range(3):
        a, b, c = [
            frame_sum(products, [9 * depth + 3 * row + col for depth in range(3)], wide, lane, places, image)
            for col in range(3)
        ]
        extra = frame_sum(beyond, [3 * depth + row for depth in range(3)], wide, lane, places, image)
        by_row.append(
            (a + b + moved(c, -1, has_left) + left * extra, moved(a, 1, has_right) + b + c + right * extra)
        )
    convs = [by_row[0][q] + by_row[1][q] + moved(by_row[2][q], -w, has_up) for q in range(2)]
    convs += [moved(by_row[0][q], w, has_down) + by_row[1][q] + by_row[2][q] for q in range(2)]
    pre = [conv * part for conv, part in zip(convs, slope)]
    one = total(pre)
    two = total([a * b for a, b in zip(pre, normed)])
    cot = source[pl.ds(pl.multiple_of(r * plan.slice_width + pair * wide, wide), wide), :].astype(jnp.float32)
    scale = inv_std * gain
    stacked = halves_from(plan, [cot + scale * part for part in pre]).astype(jnp.bfloat16)
    sent = one_hot_dot(stacked, order[...], ((1,), (1,))).astype(jnp.bfloat16)
    coarse = sums_ref[0:1] + pltpu.roll(sums_ref[1:2], sub, 1)
    coded = (
        terms(as_row(one) + pltpu.roll(as_row(two), 64, 1), 2)
        + terms(coarse, 2)
        + terms(as_row(inv_std) + pltpu.roll(as_row(mean), 64, 1), 3)
    )
    coded = jnp.concatenate(coded + [jnp.zeros_like(coarse)], axis=0).astype(jnp.bfloat16)
    for s_r in range(nr):
        for s_f in range(nf):
            out_ref[s_r * nf + s_f, 0:sub, :] = sent[s_f * sub : (s_f + 1) * sub, s_r * 128 : (s_r + 1) * 128]
            out_ref[s_r * nf + s_f, sub : sub + 8, :] = coded


def spread_kernel(plan, got_ref, acts_ref, rows_ref, out_ref, sums_ref):
    sub, nr, nf = plan.sub, plan.nr, plan.nf
    low = lanes_at((sub, 128), 1) < 64
    low_row = lanes_at((1, 128), 1) < 64
    first_row = lanes_at((1, 128), 1) < sub
    source = []
    fine, coarse, moments = [[], []], [[], []], [[], []]
    for s_r in range(nr):
        ones, twos, c_ones, c_twos, invs, means = [], [], 0.0, 0.0, [], []
        for pair in range(nf // 2):
            at = s_r * nf + 2 * pair
            left, right = [got_ref[at + k, 0:sub, :].astype(jnp.float32) for k in range(2)]
            source.append(jnp.where(low, left, pltpu.roll(right, 64, 1)))
            source.append(jnp.where(low, pltpu.roll(left, 64, 1), right))
            coded = [got_ref[at + k, sub : sub + 8, :].astype(jnp.float32) for k in range(2)]
            sums = coded[0][0:1] + coded[0][1:2] + coded[1][0:1] + coded[1][1:2]
            ones.append(sums if pair == 0 else pltpu.roll(sums, 64, 1))
            twos.append(pltpu.roll(sums, 64, 1) if pair == 0 else sums)
            both = coded[0][4:5] + coded[0][5:6] + coded[0][6:7]
            invs.append(both if pair == 0 else pltpu.roll(both, 64, 1))
            means.append(pltpu.roll(both, 64, 1) if pair == 0 else both)
            for k in range(2):
                sums = coded[k][2:3] + coded[k][3:4]
                to = (2 * pair + k) * sub
                c_one = jnp.where(first_row, sums, 0.0)
                c_two = jnp.where(first_row, pltpu.roll(sums, 128 - sub, 1), 0.0)
                c_ones = c_ones + (pltpu.roll(c_one, to, 1) if to else c_one)
                c_twos = c_twos + (pltpu.roll(c_two, to, 1) if to else c_two)
        fine[0].append(jnp.where(low_row, ones[0], ones[1]))
        fine[1].append(jnp.where(low_row, twos[0], twos[1]))
        moments[0].append(jnp.where(low_row, invs[0], invs[1]))
        moments[1].append(jnp.where(low_row, means[0], means[1]))
        coarse[0].append(c_ones)
        coarse[1].append(c_twos)
    one, two, inv_std, mean, c_one, c_two = [jnp.concatenate(part, axis=1) for part in fine + moments + coarse]
    source = jnp.concatenate(source, axis=0).astype(jnp.bfloat16)
    result = one_hot_dot(pixel_order(plan, False), source, ((1,), (1,)))
    gain = rows_ref[2]
    entries = 4 * plan.places * plan.group_width
    group_one = in_lane_groups(gain * one, plan.group_width) / entries
    group_two = in_lane_groups(gain * two, plan.group_width) / entries
    normed = (acts_ref[...].astype(jnp.float32) - mean) * inv_std
    out_ref[...] = (result - inv_std * (group_one + normed * group_two)).astype(jnp.bfloat16)
    sums_ref[...] = jnp.concatenate([one, two, c_one, c_two] + [jnp.zeros_like(one)] * 4, axis=0)


def total_kernel(scales, both_ref, result_ref, result_hbm, out_hbms, rows_ref, sems):
    copies = fetched([(result_ref, result_hbm)], sems)
    rows = sum(both_ref[k] for k in range(both_ref.shape[0]))
    for k in range(4):
        rows_ref[k] = rows[k : k + 1] * scales[k]
    for k in range(4):
        copies.append(pltpu.make_async_copy(rows_ref.at[k], out_hbms[k], sems.at[k + 1]))
        copies[-1].start()
    for copy in copies:
        copy.wait()


def in_vmem(count):
    return [pl.BlockSpec(memory_space=pltpu.VMEM)] * count


def in_hbm(count):
    return [pl.BlockSpec(memory_space=pltpu.HBM)] * count


def kept(array):
    return pltpu.with_memory_space_constraint(array, pltpu.HBM)


def shape_of(shape, kind):
    return jax.ShapeDtypeStruct(shape, kind)


LIMIT = pltpu.CompilerParams(vmem_limit_bytes=40 * 1024 * 1024)


def fast_shards(
    plan,
    acts_fine,
    acts_coarse,
    grad_coarse,
    gain_fine,
    bias_fine,
    kernel_fine,
    gain_coarse,
    bias_coarse,
    kernel_coarse,
):
    nd = lax.axis_size("dp")
    count, sub, channels, places, local = plan.count, plan.sub, plan.channels, plan.places, plan.local
    f32, bf16 = jnp.float32, jnp.bfloat16
    rows = [part.reshape(1, channels) for part in (gain_coarse, bias_coarse, gain_fine, bias_fine)]
    packed, acts, weights_c, weights_f, columns, order, fine_order, by_column, rows = pl.pallas_call(
        functools.partial(pack_kernel, plan),
        out_shape=(
            shape_of((count, plan.block_rows, 128), bf16),
            shape_of((4 * local, channels), bf16),
            shape_of((28, sub, channels), bf16),
            shape_of((27, 2 * sub, channels), bf16),
            shape_of((4, 2 * sub, 128), f32),
            shape_of((4 * plan.nr * local, 4 * plan.nr * local), bf16),
            shape_of((4 * plan.nr * local, 4 * plan.nr * local), bf16),
            shape_of((places, places + places // 2), bf16),
            shape_of((4, 1, channels), f32),
        ),
        in_specs=in_hbm(9),
        out_specs=tuple(in_vmem(9)),
        scratch_shapes=[
            pltpu.VMEM((local, channels), bf16),
            pltpu.VMEM((local, channels), bf16),
            pltpu.SemaphoreType.DMA((9,)),
        ],
        compiler_params=LIMIT,
    )(
        kept(grad_coarse.reshape(local, channels)),
        kept(acts_coarse.reshape(local, channels)),
        kept(acts_fine.reshape(4 * local, channels)),
        kept(kernel_coarse),
        kept(kernel_fine),
        *[kept(row) for row in rows],
    )
    got = lax.all_to_all(packed, BLOCK, 0, 0)
    quartered, coarse_sums = pl.pallas_call(
        functools.partial(coarse_kernel, plan),
        out_shape=(shape_of((count, 2 * sub + sub // 2, 128), bf16), shape_of((2, 128), f32)),
        in_specs=in_vmem(5),
        out_specs=tuple(in_vmem(2)),
        scratch_shapes=[pltpu.VMEM((places, channels), bf16), pltpu.VMEM((28 * sub, places), f32)],
        compiler_params=LIMIT,
    )(got, weights_c, columns, order, by_column)
    spread = lax.all_to_all(quartered, BLOCK, 0, 0)
    sent = pl.pallas_call(
        functools.partial(fine_kernel, plan),
        out_shape=shape_of((count, sub + 8, 128), bf16),
        in_specs=in_vmem(6),
        out_specs=in_vmem(1)[0],
        scratch_shapes=[
            pltpu.VMEM((channels, places // 2), bf16),
            pltpu.VMEM((channels, places // 2), bf16),
            pltpu.VMEM((54 * sub, places // 2), f32),
            pltpu.VMEM((18 * sub, places // 2), f32),
        ],
        compiler_params=LIMIT,
    )(spread, got, columns, fine_order, coarse_sums, weights_f)
    back = lax.all_to_all(sent, BLOCK, 0, 0)
    cells = nd * places
    fine_scale, coarse_scale = 1.0 / math.sqrt(4 * cells), 1.0 / math.sqrt(cells)
    out, sums = pl.pallas_call(
        functools.partial(spread_kernel, plan),
        out_shape=(pltpu.VMEM((4 * local, channels), bf16), shape_of((8, channels), f32)),
        in_specs=in_vmem(3),
        out_specs=tuple(in_vmem(2)),
        compiler_params=LIMIT,
    )(back, acts, rows)
    both = lax.all_gather(sums, "dp")
    out, sums = pl.pallas_call(
        functools.partial(total_kernel, (fine_scale, fine_scale, coarse_scale, coarse_scale)),
        out_shape=(pltpu.HBM((4 * local, channels), bf16), (pltpu.HBM((1, channels), f32),) * 4),
        in_specs=in_vmem(2),
        out_specs=(in_hbm(1)[0], tuple(in_hbm(4))),
        scratch_shapes=[pltpu.VMEM((4, 1, channels), f32), pltpu.SemaphoreType.DMA((5,))],
        compiler_params=LIMIT,
    )(both, out)
    bias_f, gain_f, bias_c, gain_c = [part.reshape(channels) for part in sums]
    return out.reshape(acts_fine.shape), gain_f, bias_f, gain_c, bias_c


def solution(mesh):
    def function(*arrays):
        local = [size // mesh.shape[axis] for size, axis in zip(arrays[1].shape, ("dp", "frames", "rows"))]
        sizes = (mesh.shape["frames"], mesh.shape["rows"])
        plan = Plan(sizes, (*local[1:], *arrays[1].shape[3:]), arrays[5].shape[1] // mesh.shape["rows"])
        if plan.fits:
            split = (mesh.shape["dp"], plan.nf // 2, 2, plan.nr)
            used = jax.sharding.Mesh(mesh.devices.reshape(split), ("dp", "pairs", "member", "rows"))
            shards, frames = functools.partial(fast_shards, plan), ("pairs", "member")
        else:
            used, shards, frames = mesh, plain_shards, "frames"
        blocks, kernel = P("dp", frames, "rows", None, None), P(None, "rows", None)
        in_specs = (blocks, blocks, blocks, P(), P(), kernel, P(), P(), kernel)
        out_specs = (blocks, P(), P(), P(), P())
        mapped = jax.shard_map(shards, mesh=used, in_specs=in_specs, out_specs=out_specs, check_vma=False)
        return mapped(*arrays)

    return function
```

```python
import functools
import math

import jax
import jax.numpy as jnp
from jax import lax
from jax.experimental import pallas as pl
from jax.experimental.pallas import tpu as pltpu
from jax.sharding import PartitionSpec as P

GROUPS = 32
EPSILON = 1e-06
BLOCK = ("rows", "pairs", "member")
PLAIN_BLOCK = ("frames", "rows")


def plain_everyone(block, count):
    copies = jnp.broadcast_to(block[None], (count,) + block.shape)
    return lax.all_to_all(copies, PLAIN_BLOCK, 0, 0)


def ahead(field, axis, distance):
    size = field.shape[axis]
    if distance == 0:
        return field
    widths = [(0, 0)] * field.ndim
    if distance > 0:
        widths[axis] = (0, distance)
        kept = lax.slice_in_dim(field, distance, size, axis=axis)
    else:
        widths[axis] = (-distance, 0)
        kept = lax.slice_in_dim(field, 0, size + distance, axis=axis)
    return jnp.pad(kept, widths)


def tap_products(source, kernel):
    sub = kernel.shape[1]
    frames, rows, cols, channels = source.shape
    products = lax.dot_general(
        kernel.reshape(27 * sub, channels),
        source.reshape(frames * rows * cols, channels),
        (((1,), (1,)), ((), ())),
        preferred_element_type=jnp.float32,
    ).reshape(3, 3, 3, sub, frames, rows, cols)
    return sum(ahead(products[depth], 3, 2 - depth) for depth in range(3))


def coarse_conv(source, kernel):
    spatial = tap_products(source, kernel)
    total = 0.0
    for row in range(3):
        part = sum(ahead(spatial[row, col], 3, 1 - col) for col in range(3))
        total = total + ahead(part, 2, 1 - row)
    return total


def fine_conv(source, kernel):
    spatial = tap_products(source, kernel)
    result = []
    for p in range(2):
        rows_of = []
        for q in range(2):
            total = 0.0
            for row in range(3):
                part = sum(ahead(spatial[row, col], 3, (q + 1 - col) // 2) for col in range(3))
                total = total + ahead(part, 2, (p + 1 - row) // 2)
            rows_of.append(total)
        result.append(jnp.stack(rows_of, 1))
    return jnp.stack(result, 1)


def group_total(sums, group_width):
    sub = sums.shape[-1]
    if sub % group_width == 0:
        grouped = jnp.sum(sums.reshape(-1, sub // group_width, group_width), axis=-1)
        return jnp.repeat(grouped, group_width, axis=-1)
    spread = jnp.moveaxis(lax.all_gather(sums, "frames"), 0, 1).reshape(sums.shape[0], -1, group_width)
    mine = lax.axis_index("frames") * sub // group_width
    grouped = lax.dynamic_index_in_dim(jnp.sum(spread, -1), mine, 1)
    return jnp.broadcast_to(grouped, sums.shape)


def level(acts, conv_grad, cotangent, gain, bias, group_width):
    sub = acts.shape[0]
    places = acts.size // sub
    values = acts.astype(jnp.float32).reshape(sub, places)
    conv_grad = conv_grad.reshape(sub, places)
    entries = places * group_width
    moments = group_total(
        jnp.stack([jnp.sum(values, 1), jnp.sum(values * values, 1)]), group_width
    ) / entries
    mean = moments[0]
    inv_std = lax.rsqrt(moments[1] - mean * mean + EPSILON)
    normed = (values - mean[:, None]) * inv_std[:, None]
    preact = gain[:, None] * normed + bias[:, None]
    squash = jax.nn.sigmoid(preact)
    pre_grad = conv_grad * squash * (1.0 + preact * (1.0 - squash))
    sums = jnp.stack([jnp.sum(pre_grad, 1), jnp.sum(pre_grad * normed, 1)])
    terms = group_total(sums * gain, group_width) / entries
    grad = cotangent.reshape(sub, places) + inv_std[:, None] * (
        gain[:, None] * pre_grad - terms[0][:, None] - normed * terms[1][:, None]
    )
    return grad, sums


def plain_shards(
    acts_fine,
    acts_coarse,
    grad_coarse,
    gain_fine,
    bias_fine,
    kernel_fine,
    gain_coarse,
    bias_coarse,
    kernel_coarse,
):
    nf, nr, nd = lax.axis_size("frames"), lax.axis_size("rows"), lax.axis_size("dp")
    count = nf * nr
    channels = acts_fine.shape[-1]
    slice_width = kernel_fine.shape[1]
    sub = slice_width // nf
    group_width = channels // GROUPS
    tl, hl, w = acts_coarse.shape[1:4]
    frames, rows = tl * nf, hl * nr
    f, r = lax.axis_index("frames"), lax.axis_index("rows")

    gathered = plain_everyone(grad_coarse[0], count)
    source = (
        gathered.reshape(nf, nr, tl, hl, w, channels)
        .transpose(0, 2, 1, 3, 4, 5)
        .reshape(frames, rows, w, channels)
    )
    coarse_in = acts_coarse[0].reshape(tl, hl, w, nr, nf, sub).transpose(4, 3, 5, 0, 1, 2)
    coarse_in = lax.all_to_all(coarse_in.reshape(count, sub, tl * hl * w), PLAIN_BLOCK, 0, 0)
    fine_in = acts_fine[0].reshape(tl, hl, 2, w, 2, nr, nf, sub).transpose(6, 5, 7, 2, 4, 0, 1, 3)
    fine_in = lax.all_to_all(fine_in.reshape(count, sub, 4 * tl * hl * w), PLAIN_BLOCK, 0, 0)

    def mine(vector):
        return lax.dynamic_slice_in_dim(vector, r * slice_width + f * sub, sub)

    def own(kernel):
        return lax.dynamic_slice_in_dim(kernel, f * sub, sub, axis=1)

    coarse_vals = (
        coarse_in.reshape(nf, nr, sub, tl, hl, w).transpose(2, 0, 3, 1, 4, 5).reshape(sub, frames, rows, w)
    )
    cot = lax.dynamic_slice_in_dim(source, r * slice_width + f * sub, sub, axis=3)
    cot = cot.astype(jnp.float32).transpose(3, 0, 1, 2)
    conv = coarse_conv(source, own(kernel_coarse))
    coarse_grad, coarse_sums = level(
        coarse_vals, conv, cot, mine(gain_coarse), mine(bias_coarse), group_width
    )
    quartered = (coarse_grad * 0.25).astype(jnp.bfloat16)
    spread = plain_everyone(quartered, count)
    source_fine = (
        spread.reshape(nf, nr, sub, frames, rows, w)
        .transpose(3, 4, 5, 1, 0, 2)
        .reshape(frames, rows, w, channels)
    )
    conv = fine_conv(source_fine, own(kernel_fine))
    fine_vals = (
        fine_in.reshape(nf, nr, sub, 2, 2, tl, hl, w)
        .transpose(2, 3, 4, 0, 5, 1, 6, 7)
        .reshape(sub, 2, 2, frames, rows, w)
    )
    cot = jnp.broadcast_to(
        quartered.astype(jnp.float32).reshape(sub, 1, 1, frames, rows, w), conv.shape
    )
    fine_grad, fine_sums = level(
        fine_vals, conv, cot, mine(gain_fine), mine(bias_fine), group_width
    )
    back = (
        fine_grad.astype(jnp.bfloat16)
        .reshape(sub, 2, 2, nf, tl, nr, hl, w)
        .transpose(3, 5, 0, 1, 2, 4, 6, 7)
        .reshape(count, sub, 4 * tl * hl * w)
    )
    sums = plain_everyone(jnp.concatenate([fine_sums, coarse_sums]), count)
    back = lax.all_to_all(back, PLAIN_BLOCK, 0, 0)
    out = (
        back.reshape(nf, nr, sub, 2, 2, tl, hl, w)
        .transpose(5, 6, 3, 7, 4, 1, 0, 2)
        .reshape(1, tl, 2 * hl, 2 * w, channels)
    )
    sums = sums.reshape(nf, nr, 4, sub).transpose(2, 1, 0, 3).reshape(4, channels)
    totals = lax.psum(sums, "dp")
    cells = nd * frames * rows * w
    scale_fine = 1.0 / jnp.sqrt(jnp.float32(4 * cells))
    scale_coarse = 1.0 / jnp.sqrt(jnp.float32(cells))
    return (
        out,
        totals[1] * scale_fine,
        totals[0] * scale_fine,
        totals[3] * scale_coarse,
        totals[2] * scale_coarse,
    )


def lanes_at(shape, axis):
    return lax.broadcasted_iota(jnp.int32, shape, axis)


def one_hot(found):
    return found.astype(jnp.float32).astype(jnp.bfloat16)


def pixel_order(plan, swapped):
    tl, hl, w = plan.tl, plan.hl, plan.w // 2
    size = 4 * plan.local
    lane = lanes_at((1, size), 1)
    j, i, t = lane % w, lane // w % hl, lane // (w * hl) % tl
    q, p = lane // (w * hl * tl) % 2, lane // (2 * w * hl * tl) % 2
    half = lane // (4 * w * hl * tl)
    if swapped:
        half = 1 - half
    pixel = (t * 2 * hl + 2 * i + p) * 4 * w + 2 * (half * w + j) + q
    return one_hot(lanes_at((size, size), 0) == pixel)


def merged_order(nr, outer, tl, cells):
    size = nr * outer * tl * cells
    lane = lanes_at((1, size), 1)
    cell, dev = lane % cells, lane // cells % nr
    t, o = lane // (cells * nr) % tl, lane // (cells * nr * tl)
    return one_hot(lanes_at((size, size), 0) == ((dev * outer + o) * tl + t) * cells + cell)


def column_order(plan):
    w = plan.w // 2
    lines = plan.places // plan.w
    lane = lanes_at((1, 4 * lines * w + 4 * lines), 1)
    inner = lane % (lines * w)
    place = inner // w * plan.w + lane // (lines * w) * w + inner % w
    past = lane - 2 * lines * w
    border = past % lines * plan.w + jnp.where(past < 2 * lines, w, w - 1)
    wanted = jnp.where(past >= 0, border, place)
    shape = (plan.places, 2 * lines * w + 4 * lines)
    return one_hot(lanes_at(shape, 0) == wanted[:, : shape[1]])


def one_hot_dot(a, b, dims):
    return lax.dot_general(a, b, (dims, ((), ())), preferred_element_type=jnp.float32)


def moved(field, distance, kept):
    size = field.shape[1]
    return jnp.where(kept, pltpu.roll(field, (-distance) % size, 1), 0.0)


def own_column(row, base, sub):
    shape = (sub, row.shape[1])
    mine = lanes_at(shape, 1) == lanes_at(shape, 0) + base
    return jnp.sum(jnp.where(mine, row, 0.0), axis=1, keepdims=True)


def as_row(column):
    shape = (column.shape[0], 128)
    here = lanes_at(shape, 1) == lanes_at(shape, 0)
    return jnp.sum(jnp.where(here, column, 0.0), axis=0, keepdims=True)


def terms(value, count):
    found = []
    for _ in range(count):
        found.append(value.astype(jnp.bfloat16).astype(jnp.float32))
        value = value - found[-1]
    return found


def in_groups(column, group_width):
    sub = column.shape[0]
    grouped = jnp.sum(column.reshape(sub // group_width, group_width, 1), axis=1, keepdims=True)
    return jnp.broadcast_to(grouped, (sub // group_width, group_width, 1)).reshape(sub, 1)


def in_lane_groups(row, group_width):
    lane = lanes_at(row.shape, 1)
    size = row.shape[1]
    step = 1
    while step < group_width:
        up, down = pltpu.roll(row, size - step, 1), pltpu.roll(row, step, 1)
        row = row + jnp.where(lane // step % 2 == 0, up, down)
        step *= 2
    return row


def total(parts):
    return sum(jnp.sum(part, axis=1, keepdims=True) for part in parts)


def statistics(one, two, entries, group_width):
    mean = in_groups(one, group_width) / entries
    square = in_groups(two, group_width) / entries
    return mean, lax.rsqrt(square - mean * mean + EPSILON)


def normalised(parts, gain, bias, mean, inv_std):
    normed, slope = [], []
    for part in parts:
        unit = (part - mean) * inv_std
        preact = gain * unit + bias
        squash = jax.nn.sigmoid(preact)
        normed.append(unit)
        slope.append(squash * (1.0 + preact * (1.0 - squash)))
    return normed, slope


class Plan:
    def __init__(self, mesh_sizes, acts_coarse, slice_width):
        self.nf, self.nr = mesh_sizes
        self.count = self.nf * self.nr
        self.tl, self.hl, self.w, self.channels = acts_coarse
        self.slice_width = slice_width
        self.sub = slice_width // self.nf
        self.cells = self.hl * self.w
        self.local = self.tl * self.cells
        self.image = self.cells * self.nr
        self.frames = self.tl * self.nf
        self.places = self.frames * self.image
        self.group_width = self.channels // GROUPS
        self.chunks = self.channels // 128
        self.acts_at = self.chunks // 2 * self.local
        self.packed_at = self.acts_at + self.sub
        self.cot_at = self.packed_at + 8
        self.stats_at = self.cot_at + 8
        self.block_rows = self.stats_at + 8
        self.fits = (
            self.sub == 32
            and self.slice_width == 128
            and self.group_width == 16
            and self.cells == 16
            and self.w == 8
            and self.tl == 2
            and self.nr == 4
            and self.nf == 4
            and self.slice_width * self.nr == self.channels
        )

    def place_masks(self, w):
        lane = lanes_at((1, self.places // self.w * w), 1)
        col, row = lane % w, lane // w % (self.hl * self.nr)
        last_row = self.hl * self.nr - 1
        return (lane, col > 0, col < w - 1, row > 0, row < last_row)


def fetched(pairs, sems):
    copies = [pltpu.make_async_copy(src, dst, sems.at[k]) for k, (src, dst) in enumerate(pairs)]
    for copy in copies:
        copy.start()
    return copies


def own_place(plan):
    pair, member, r = lax.axis_index("pairs"), lax.axis_index("member"), lax.axis_index("rows")
    return pair, member, r, r * plan.slice_width + (2 * pair + member) * plan.sub


def pack_kernel(
    plan,
    g_hbm,
    coarse_hbm,
    fine_hbm,
    kernel_c,
    kernel_f,
    gain_c,
    bias_c,
    gain_f,
    bias_f,
    out_ref,
    fine_ref,
    weights_c,
    weights_f,
    columns,
    order,
    fine_order,
    by_column,
    rows,
    g_ref,
    coarse_ref,
    sems,
):
    sub, chunks, local = plan.sub, plan.chunks, plan.local
    pair, member, r, base = own_place(plan)
    depth = plan.channels // 2
    half = pl.ds(pl.multiple_of(member * depth, depth), depth)
    both = pl.ds(pl.multiple_of(2 * pair * sub, 2 * sub), 2 * sub)
    copies = fetched(
        [(fine_hbm, fine_ref), (coarse_hbm, coarse_ref), (g_hbm, g_ref)]
        + [(row, rows.at[k]) for k, row in enumerate((gain_c, bias_c, gain_f, bias_f))]
        + [(kernel_c.at[:, both, half], weights_c), (kernel_f.at[:, both, :], weights_f)],
        sems,
    )
    order[...] = merged_order(plan.nr, 4, plan.tl, plan.cells)
    fine_order[...] = merged_order(plan.nr, 8, plan.tl, plan.cells // 2)
    by_column[...] = column_order(plan)
    shape = (local, 128)
    places = [one_hot(lanes_at(shape, 0) + k * local == lanes_at(shape, 1)) for k in range(4)]
    orders = [pixel_order(plan, swapped) for swapped in (False, True)]
    copies[0].wait()
    acts = fine_ref[...]
    halves = [one_hot_dot(acts, order_of, ((0,), (0,))).astype(jnp.bfloat16) for order_of in orders]
    values = acts.astype(jnp.float32)
    one = jnp.sum(values, axis=0, keepdims=True)
    two = jnp.sum(values * values, axis=0, keepdims=True)
    stats = terms(one, 3) + terms(two, 3)
    stats = jnp.concatenate(stats + [jnp.zeros_like(one)] * 2, axis=0).astype(jnp.bfloat16)
    copies[1].wait()
    quarters = [one_hot_dot(coarse_ref[...], place, ((0,), (0,))) for place in places]
    copies[2].wait()
    cots = [one_hot_dot(g_ref[...], place, ((0,), (0,))) for place in places]
    low = lanes_at((sub, 128), 1) < 64
    for s_r in range(plan.nr):
        for s_f in range(plan.nf):
            dest, c = s_r * plan.nf + s_f, s_r * plan.slice_width + s_f * sub
            first, half = s_r * plan.slice_width + s_f // 2 * 2 * sub, s_f % 2
            for k in range(chunks // 2):
                at = (half * chunks // 2 + k) * 128
                out_ref[dest, k * local : (k + 1) * local, :] = g_ref[:, at : at + 128]
            upper, lower = halves[half][first : first + sub], halves[1 - half][first + sub : first + 2 * sub]
            out_ref[dest, plan.acts_at : plan.packed_at, :] = jnp.where(low, upper, lower)
            for at, found in ((plan.packed_at, quarters), (plan.cot_at, cots)):
                rows_of = sum(found[k][c + 8 * k : c + 8 * k + 8] for k in range(4))
                out_ref[dest, at : at + 8, :] = rows_of.astype(jnp.bfloat16)
            out_ref[dest, plan.stats_at : plan.block_rows, :] = stats[:, s_r * 128 : (s_r + 1) * 128]
    for copy in copies[3:7]:
        copy.wait()
    first = r * plan.slice_width + 2 * pair * sub
    for k in range(2):
        columns[k, 0:sub, :] = jnp.broadcast_to(own_column(rows[k], base, sub), (sub, 128))
        columns[2 + k] = jnp.broadcast_to(own_column(rows[2 + k], first, 2 * sub), (2 * sub, 128))
    for copy in copies[7:]:
        copy.wait()


def by_frame_device(plan, got_ref, at, height):
    return jnp.concatenate(
        [
            jnp.concatenate(
                [got_ref[r * plan.nf + f, at : at + height, :] for r in range(plan.nr)], axis=1
            )
            for f in range(plan.nf)
        ],
        axis=0,
    )


def in_places(plan, merged, height):
    width = plan.tl * plan.image
    return [
        jnp.concatenate(
            [merged[f * height : (f + 1) * height, k * width : (k + 1) * width] for f in range(plan.nf)],
            axis=1,
        )
        for k in range(4)
    ]


def frame_sum(products_ref, taps, sub, lane, places, image):
    near, middle, far = [products_ref[pl.ds(tap * sub, sub), :] for tap in reversed(taps)]
    return near + moved(middle, image, lane < places - image) + moved(far, 2 * image, lane < places - 2 * image)


def coarse_kernel(
    plan, got_ref, weights, columns, order, mine_ref, sent_ref, held_ref, inv_ref, source, products, conv_ref
):
    sub, nr, nf, cells, tl, local = plan.sub, plan.nr, plan.nf, plan.cells, plan.tl, plan.local
    wide, depth = 2 * sub, plan.channels // 2
    _, member, _, _ = own_place(plan)
    for s_f in range(nf):
        for s_r in range(nr):
            for t in range(tl):
                at = (s_f * tl + t) * plan.image + s_r * cells
                for k in range(plan.chunks // 2):
                    source[at : at + cells, k * 128 : (k + 1) * 128] = got_ref[
                        s_r * nf + s_f, k * local + t * cells : k * local + (t + 1) * cells, :
                    ]
    products[...] = one_hot_dot(weights[...].reshape(27 * wide, depth), source[...], ((1,), (1,)))
    found = []
    for at in (plan.packed_at, plan.cot_at):
        merged = one_hot_dot(by_frame_device(plan, got_ref, at, 8), order[...], ((1,), (0,)))
        found.append(jnp.concatenate(in_places(plan, merged, 8), axis=0))
    values, cot = found
    gain, bias = columns[0][0:sub, 0:1], columns[1][0:sub, 0:1]
    entries = plan.places * plan.group_width
    mean, inv_std = statistics(total([values]), total([values * values]), entries, plan.group_width)
    (normed,), (slope,) = normalised([values], gain, bias, mean, inv_std)
    held_ref[0], held_ref[1], held_ref[2] = normed, slope, cot
    inv_ref[...] = jnp.broadcast_to(inv_std, (sub, 128))
    lane, has_left, has_right, has_up, has_down = plan.place_masks(plan.w)
    by_col = []
    for col in range(3):
        parts = [
            frame_sum(products, [9 * k + 3 * row + col for k in range(3)], wide, lane, plan.places, plan.image)
            for row in range(3)
        ]
        by_col.append(parts[1] + moved(parts[0], plan.w, has_down) + moved(parts[2], -plan.w, has_up))
    conv_ref[...] = by_col[1] + moved(by_col[0], 1, has_right) + moved(by_col[2], -1, has_left)
    mine_ref[...] = conv_ref[pl.ds(pl.multiple_of(member * sub, sub), sub), :]
    sent_ref[...] = conv_ref[pl.ds(pl.multiple_of((1 - member) * sub, sub), sub), :].astype(jnp.bfloat16)


def quarter_kernel(plan, mine_ref, both_ref, held_ref, inv_ref, columns, by_column, out_ref, sums_ref):
    sub = plan.sub
    _, member, _, _ = own_place(plan)
    conv = mine_ref[...] + both_ref[1 - member].astype(jnp.float32)
    normed, slope, cot = held_ref[0], held_ref[1], held_ref[2]
    gain, inv_std = columns[0][0:sub, 0:1], inv_ref[:, 0:1]
    entries = plan.places * plan.group_width
    pre = conv * slope
    one, two = total([pre]), total([pre * normed])
    group_one = in_groups(gain * one, plan.group_width) / entries
    group_two = in_groups(gain * two, plan.group_width) / entries
    grad = cot + inv_std * (gain * pre - group_one - normed * group_two)
    quartered = (grad * 0.25).astype(jnp.bfloat16)
    sent = one_hot_dot(quartered, by_column[...], ((1,), (0,))).astype(jnp.bfloat16)
    low = lanes_at((sub // 2, 128), 1) < 64
    for half in range(2):
        at = half * 256
        border = sent[:, 512 + half * 128 : 640 + half * 128]
        border = jnp.where(low, border[: sub // 2], border[sub // 2 :])
        for dest in range(half, plan.count, 2):
            out_ref[dest, 0:sub, :] = sent[:, at : at + 128]
            out_ref[dest, sub : 2 * sub, :] = sent[:, at + 128 : at + 256]
            out_ref[dest, 2 * sub : 2 * sub + sub // 2, :] = border
    sums_ref[...] = jnp.concatenate([as_row(one), as_row(two)], axis=0)


def halves_at(plan, merged):
    sub = plan.sub
    turned = jnp.concatenate([pltpu.roll(merged[:, k * 128 : (k + 1) * 128], 64, 1) for k in range(4)], axis=1)
    low = lanes_at((sub, 128), 1) < 64
    parts = []
    for pq in range(4):
        groups = []
        for group in range(2):
            e = 4 * group + pq
            at = e // 2 * 128
            strips = []
            for m in range(plan.nf // 2):
                first, second = slice(2 * m * sub, (2 * m + 1) * sub), slice((2 * m + 1) * sub, (2 * m + 2) * sub)
                if e % 2 == 0:
                    strips.append(jnp.where(low, merged[first, at : at + 128], turned[second, at : at + 128]))
                else:
                    strips.append(jnp.where(low, turned[first, at : at + 128], merged[second, at : at + 128]))
            groups.append(jnp.concatenate(strips, axis=1))
        parts.append(jnp.concatenate(groups, axis=0))
    return parts


def halves_from(plan, parts):
    sub = plan.sub
    low = lanes_at((sub, 128), 1) < 64
    down = []
    for f in range(plan.nf):
        across = []
        for v in range(4):
            pair = []
            for e in (2 * v, 2 * v + 1):
                group, pq = e // 4, e % 4
                strip = parts[pq][group * sub : (group + 1) * sub, f // 2 * 128 : (f // 2 + 1) * 128]
                pair.append(strip if e % 2 == f % 2 else pltpu.roll(strip, 64, 1))
            across.append(jnp.where(low, pair[0], pair[1]))
        down.append(jnp.concatenate(across, axis=1))
    return jnp.concatenate(down, axis=0)


def fine_kernel(
    plan, got_ref, acts_ref, columns, order, sums_ref, weights, out_ref, source, border, products, beyond
):
    sub, nr, nf, wide = plan.sub, plan.nr, plan.nf, 2 * plan.sub
    pair, member, r, _ = own_place(plan)
    w = plan.w // 2
    lines = plan.places // plan.w
    places = lines * w
    for k in range(2):
        source[:, k * 128 : (k + 1) * 128] = got_ref[:, k * sub : (k + 1) * sub, :].reshape(plan.channels, 128)
    products[...] = one_hot_dot(weights[...].reshape(27 * wide, plan.channels), source[...], ((1,), (0,)))
    packed = got_ref[:, wide : wide + sub // 2, :].reshape(plan.count * sub // 2, 128)
    shape = (128, places)
    beside = lanes_at(shape, 1) == lanes_at(shape, 0) % lines * w + (1 - member) * (w - 1)
    for k in range(2):
        here = one_hot(beside & (lanes_at(shape, 0) // lines == k))
        found = one_hot_dot(packed, here, ((1,), (0,))).astype(jnp.bfloat16)
        for s in range(plan.count):
            border[s * sub + k * (sub // 2) : s * sub + (k + 1) * (sub // 2), :] = found[
                s * (sub // 2) : (s + 1) * (sub // 2)
            ]
    facing = jnp.concatenate([weights[3 * k + 2 * member] for k in range(9)], axis=0)
    beyond[...] = one_hot_dot(facing, border[...], ((1,), (0,)))
    merged = one_hot_dot(by_frame_device(plan, acts_ref, plan.acts_at, sub), order[...], ((1,), (0,)))
    parts = halves_at(plan, merged)
    stats = sum(
        acts_ref[s, plan.stats_at : plan.block_rows, :].astype(jnp.float32) for s in range(plan.count)
    )
    entries = 4 * plan.places * plan.group_width
    one = own_column(stats[0:1] + stats[1:2] + stats[2:3], pair * wide, wide)
    two = own_column(stats[3:4] + stats[4:5] + stats[5:6], pair * wide, wide)
    mean, inv_std = statistics(one, two, entries, plan.group_width)
    gain, bias = columns[2][:, 0:1], columns[3][:, 0:1]
    normed, slope = normalised(parts, gain, bias, mean, inv_std)
    lane, has_left, has_right, has_up, has_down = plan.place_masks(w)
    image = plan.image // 2
    right, left = (1 - member).astype(jnp.float32), member.astype(jnp.float32)
    by_row = []
    for row in range(3):
        a, b, c = [
            frame_sum(products, [9 * depth + 3 * row + col for depth in range(3)], wide, lane, places, image)
            for col in range(3)
        ]
        extra = frame_sum(beyond, [3 * depth + row for depth in range(3)], wide, lane, places, image)
        by_row.append(
            (a + b + moved(c, -1, has_left) + left * extra, moved(a, 1, has_right) + b + c + right * extra)
        )
    convs = [by_row[0][q] + by_row[1][q] + moved(by_row[2][q], -w, has_up) for q in range(2)]
    convs += [moved(by_row[0][q], w, has_down) + by_row[1][q] + by_row[2][q] for q in range(2)]
    pre = [conv * part for conv, part in zip(convs, slope)]
    one = total(pre)
    two = total([a * b for a, b in zip(pre, normed)])
    cot = source[pl.ds(pl.multiple_of(r * plan.slice_width + pair * wide, wide), wide), :].astype(jnp.float32)
    scale = inv_std * gain
    stacked = halves_from(plan, [cot + scale * part for part in pre]).astype(jnp.bfloat16)
    sent = one_hot_dot(stacked, order[...], ((1,), (1,))).astype(jnp.bfloat16)
    coarse = sums_ref[0:1] + pltpu.roll(sums_ref[1:2], sub, 1)
    coded = (
        terms(as_row(one) + pltpu.roll(as_row(two), 64, 1), 2)
        + terms(coarse, 2)
        + terms(as_row(inv_std) + pltpu.roll(as_row(mean), 64, 1), 3)
    )
    coded = jnp.concatenate(coded + [jnp.zeros_like(coarse)], axis=0).astype(jnp.bfloat16)
    for s_r in range(nr):
        for s_f in range(nf):
            out_ref[s_r * nf + s_f, 0:sub, :] = sent[s_f * sub : (s_f + 1) * sub, s_r * 128 : (s_r + 1) * 128]
            out_ref[s_r * nf + s_f, sub : sub + 8, :] = coded


def spread_kernel(plan, got_ref, acts_ref, rows_ref, out_ref, sums_ref):
    sub, nr, nf = plan.sub, plan.nr, plan.nf
    low = lanes_at((sub, 128), 1) < 64
    low_row = lanes_at((1, 128), 1) < 64
    first_row = lanes_at((1, 128), 1) < sub
    source = []
    fine, coarse, moments = [[], []], [[], []], [[], []]
    for s_r in range(nr):
        ones, twos, c_ones, c_twos, invs, means = [], [], 0.0, 0.0, [], []
        for pair in range(nf // 2):
            at = s_r * nf + 2 * pair
            left, right = [got_ref[at + k, 0:sub, :].astype(jnp.float32) for k in range(2)]
            source.append(jnp.where(low, left, pltpu.roll(right, 64, 1)))
            source.append(jnp.where(low, pltpu.roll(left, 64, 1), right))
            coded = [got_ref[at + k, sub : sub + 8, :].astype(jnp.float32) for k in range(2)]
            sums = coded[0][0:1] + coded[0][1:2] + coded[1][0:1] + coded[1][1:2]
            ones.append(sums if pair == 0 else pltpu.roll(sums, 64, 1))
            twos.append(pltpu.roll(sums, 64, 1) if pair == 0 else sums)
            both = coded[0][4:5] + coded[0][5:6] + coded[0][6:7]
            invs.append(both if pair == 0 else pltpu.roll(both, 64, 1))
            means.append(pltpu.roll(both, 64, 1) if pair == 0 else both)
            for k in range(2):
                sums = coded[k][2:3] + coded[k][3:4]
                to = (2 * pair + k) * sub
                c_one = jnp.where(first_row, sums, 0.0)
                c_two = jnp.where(first_row, pltpu.roll(sums, 128 - sub, 1), 0.0)
                c_ones = c_ones + (pltpu.roll(c_one, to, 1) if to else c_one)
                c_twos = c_twos + (pltpu.roll(c_two, to, 1) if to else c_two)
        fine[0].append(jnp.where(low_row, ones[0], ones[1]))
        fine[1].append(jnp.where(low_row, twos[0], twos[1]))
        moments[0].append(jnp.where(low_row, invs[0], invs[1]))
        moments[1].append(jnp.where(low_row, means[0], means[1]))
        coarse[0].append(c_ones)
        coarse[1].append(c_twos)
    one, two, inv_std, mean, c_one, c_two = [jnp.concatenate(part, axis=1) for part in fine + moments + coarse]
    source = jnp.concatenate(source, axis=0).astype(jnp.bfloat16)
    result = one_hot_dot(pixel_order(plan, False), source, ((1,), (1,)))
    gain = rows_ref[2]
    entries = 4 * plan.places * plan.group_width
    group_one = in_lane_groups(gain * one, plan.group_width) / entries
    group_two = in_lane_groups(gain * two, plan.group_width) / entries
    normed = (acts_ref[...].astype(jnp.float32) - mean) * inv_std
    out_ref[...] = (result - inv_std * (group_one + normed * group_two)).astype(jnp.bfloat16)
    sums_ref[...] = jnp.concatenate([one, two, c_one, c_two] + [jnp.zeros_like(one)] * 4, axis=0)


def total_kernel(scales, both_ref, result_ref, result_hbm, out_hbms, rows_ref, sems):
    copies = fetched([(result_ref, result_hbm)], sems)
    rows = sum(both_ref[k] for k in range(both_ref.shape[0]))
    for k in range(4):
        rows_ref[k] = rows[k : k + 1] * scales[k]
    for k in range(4):
        copies.append(pltpu.make_async_copy(rows_ref.at[k], out_hbms[k], sems.at[k + 1]))
        copies[-1].start()
    for copy in copies:
        copy.wait()


def in_vmem(count):
    return [pl.BlockSpec(memory_space=pltpu.VMEM)] * count


def in_hbm(count):
    return [pl.BlockSpec(memory_space=pltpu.HBM)] * count


def kept(array):
    return pltpu.with_memory_space_constraint(array, pltpu.HBM)


def shape_of(shape, kind):
    return jax.ShapeDtypeStruct(shape, kind)


LIMIT = pltpu.CompilerParams(vmem_limit_bytes=40 * 1024 * 1024)


def fast_shards(
    plan,
    acts_fine,
    acts_coarse,
    grad_coarse,
    gain_fine,
    bias_fine,
    kernel_fine,
    gain_coarse,
    bias_coarse,
    kernel_coarse,
):
    nd = lax.axis_size("dp")
    count, sub, channels, places, local = plan.count, plan.sub, plan.channels, plan.places, plan.local
    f32, bf16 = jnp.float32, jnp.bfloat16
    rows = [part.reshape(1, channels) for part in (gain_coarse, bias_coarse, gain_fine, bias_fine)]
    packed, acts, weights_c, weights_f, columns, order, fine_order, by_column, rows = pl.pallas_call(
        functools.partial(pack_kernel, plan),
        out_shape=(
            shape_of((count, plan.block_rows, 128), bf16),
            shape_of((4 * local, channels), bf16),
            shape_of((27, 2 * sub, channels // 2), bf16),
            shape_of((27, 2 * sub, channels), bf16),
            shape_of((4, 2 * sub, 128), f32),
            shape_of((4 * plan.nr * local, 4 * plan.nr * local), bf16),
            shape_of((4 * plan.nr * local, 4 * plan.nr * local), bf16),
            shape_of((places, places + places // 2), bf16),
            shape_of((4, 1, channels), f32),
        ),
        in_specs=in_hbm(9),
        out_specs=tuple(in_vmem(9)),
        scratch_shapes=[
            pltpu.VMEM((local, channels), bf16),
            pltpu.VMEM((local, channels), bf16),
            pltpu.SemaphoreType.DMA((9,)),
        ],
        compiler_params=LIMIT,
    )(
        kept(grad_coarse.reshape(local, channels)),
        kept(acts_coarse.reshape(local, channels)),
        kept(acts_fine.reshape(4 * local, channels)),
        kept(kernel_coarse),
        kept(kernel_fine),
        *[kept(row) for row in rows],
    )
    got = lax.all_to_all(packed, BLOCK, 0, 0)
    mine, theirs, held, inv_std = pl.pallas_call(
        functools.partial(coarse_kernel, plan),
        out_shape=(
            shape_of((sub, places), f32),
            shape_of((sub, places), bf16),
            shape_of((3, sub, places), f32),
            shape_of((sub, 128), f32),
        ),
        in_specs=in_vmem(4),
        out_specs=tuple(in_vmem(4)),
        scratch_shapes=[
            pltpu.VMEM((places, channels // 2), bf16),
            pltpu.VMEM((54 * sub, places), f32),
            pltpu.VMEM((2 * sub, places), f32),
        ],
        compiler_params=LIMIT,
    )(got, weights_c, columns, order)
    both = lax.all_gather(theirs, "member")
    quartered, coarse_sums = pl.pallas_call(
        functools.partial(quarter_kernel, plan),
        out_shape=(shape_of((count, 2 * sub + sub // 2, 128), bf16), shape_of((2, 128), f32)),
        in_specs=in_vmem(6),
        out_specs=tuple(in_vmem(2)),
        compiler_params=LIMIT,
    )(mine, both, held, inv_std, columns, by_column)
    spread = lax.all_to_all(quartered, BLOCK, 0, 0)
    sent = pl.pallas_call(
        functools.partial(fine_kernel, plan),
        out_shape=shape_of((count, sub + 8, 128), bf16),
        in_specs=in_vmem(6),
        out_specs=in_vmem(1)[0],
        scratch_shapes=[
            pltpu.VMEM((channels, places // 2), bf16),
            pltpu.VMEM((channels, places // 2), bf16),
            pltpu.VMEM((54 * sub, places // 2), f32),
            pltpu.VMEM((18 * sub, places // 2), f32),
        ],
        compiler_params=LIMIT,
    )(spread, got, columns, fine_order, coarse_sums, weights_f)
    back = lax.all_to_all(sent, BLOCK, 0, 0)
    cells = nd * places
    fine_scale, coarse_scale = 1.0 / math.sqrt(4 * cells), 1.0 / math.sqrt(cells)
    out, sums = pl.pallas_call(
        functools.partial(spread_kernel, plan),
        out_shape=(pltpu.VMEM((4 * local, channels), bf16), shape_of((8, channels), f32)),
        in_specs=in_vmem(3),
        out_specs=tuple(in_vmem(2)),
        compiler_params=LIMIT,
    )(back, acts, rows)
    both = lax.all_gather(sums, "dp")
    out, sums = pl.pallas_call(
        functools.partial(total_kernel, (fine_scale, fine_scale, coarse_scale, coarse_scale)),
        out_shape=(pltpu.HBM((4 * local, channels), bf16), (pltpu.HBM((1, channels), f32),) * 4),
        in_specs=in_vmem(2),
        out_specs=(in_hbm(1)[0], tuple(in_hbm(4))),
        scratch_shapes=[pltpu.VMEM((4, 1, channels), f32), pltpu.SemaphoreType.DMA((5,))],
        compiler_params=LIMIT,
    )(both, out)
    bias_f, gain_f, bias_c, gain_c = [part.reshape(channels) for part in sums]
    return out.reshape(acts_fine.shape), gain_f, bias_f, gain_c, bias_c


def solution(mesh):
    def function(*arrays):
        local = [size // mesh.shape[axis] for size, axis in zip(arrays[1].shape, ("dp", "frames", "rows"))]
        sizes = (mesh.shape["frames"], mesh.shape["rows"])
        plan = Plan(sizes, (*local[1:], *arrays[1].shape[3:]), arrays[5].shape[1] // mesh.shape["rows"])
        if plan.fits:
            split = (mesh.shape["dp"], plan.nf // 2, 2, plan.nr)
            used = jax.sharding.Mesh(mesh.devices.reshape(split), ("dp", "pairs", "member", "rows"))
            shards, frames = functools.partial(fast_shards, plan), ("pairs", "member")
        else:
            used, shards, frames = mesh, plain_shards, "frames"
        blocks, kernel = P("dp", frames, "rows", None, None), P(None, "rows", None)
        in_specs = (blocks, blocks, blocks, P(), P(), kernel, P(), P(), kernel)
        out_specs = (blocks, P(), P(), P(), P())
        mapped = jax.shard_map(shards, mesh=used, in_specs=in_specs, out_specs=out_specs, check_vma=False)
        return mapped(*arrays)

    return function
```

```python
import functools
import math

import jax
import jax.numpy as jnp
from jax import lax
from jax.experimental import pallas as pl
from jax.experimental.pallas import tpu as pltpu
from jax.sharding import PartitionSpec as P

GROUPS = 32
EPSILON = 1e-06
BLOCK = ("rows", "pairs", "member")
PLAIN_BLOCK = ("frames", "rows")


def plain_everyone(block, count):
    copies = jnp.broadcast_to(block[None], (count,) + block.shape)
    return lax.all_to_all(copies, PLAIN_BLOCK, 0, 0)


def ahead(field, axis, distance):
    size = field.shape[axis]
    if distance == 0:
        return field
    widths = [(0, 0)] * field.ndim
    if distance > 0:
        widths[axis] = (0, distance)
        kept = lax.slice_in_dim(field, distance, size, axis=axis)
    else:
        widths[axis] = (-distance, 0)
        kept = lax.slice_in_dim(field, 0, size + distance, axis=axis)
    return jnp.pad(kept, widths)


def tap_products(source, kernel):
    sub = kernel.shape[1]
    frames, rows, cols, channels = source.shape
    products = lax.dot_general(
        kernel.reshape(27 * sub, channels),
        source.reshape(frames * rows * cols, channels),
        (((1,), (1,)), ((), ())),
        preferred_element_type=jnp.float32,
    ).reshape(3, 3, 3, sub, frames, rows, cols)
    return sum(ahead(products[depth], 3, 2 - depth) for depth in range(3))


def coarse_conv(source, kernel):
    spatial = tap_products(source, kernel)
    total = 0.0
    for row in range(3):
        part = sum(ahead(spatial[row, col], 3, 1 - col) for col in range(3))
        total = total + ahead(part, 2, 1 - row)
    return total


def fine_conv(source, kernel):
    spatial = tap_products(source, kernel)
    result = []
    for p in range(2):
        rows_of = []
        for q in range(2):
            total = 0.0
            for row in range(3):
                part = sum(ahead(spatial[row, col], 3, (q + 1 - col) // 2) for col in range(3))
                total = total + ahead(part, 2, (p + 1 - row) // 2)
            rows_of.append(total)
        result.append(jnp.stack(rows_of, 1))
    return jnp.stack(result, 1)


def group_total(sums, group_width):
    sub = sums.shape[-1]
    if sub % group_width == 0:
        grouped = jnp.sum(sums.reshape(-1, sub // group_width, group_width), axis=-1)
        return jnp.repeat(grouped, group_width, axis=-1)
    spread = jnp.moveaxis(lax.all_gather(sums, "frames"), 0, 1).reshape(sums.shape[0], -1, group_width)
    mine = lax.axis_index("frames") * sub // group_width
    grouped = lax.dynamic_index_in_dim(jnp.sum(spread, -1), mine, 1)
    return jnp.broadcast_to(grouped, sums.shape)


def level(acts, conv_grad, cotangent, gain, bias, group_width):
    sub = acts.shape[0]
    places = acts.size // sub
    values = acts.astype(jnp.float32).reshape(sub, places)
    conv_grad = conv_grad.reshape(sub, places)
    entries = places * group_width
    moments = group_total(
        jnp.stack([jnp.sum(values, 1), jnp.sum(values * values, 1)]), group_width
    ) / entries
    mean = moments[0]
    inv_std = lax.rsqrt(moments[1] - mean * mean + EPSILON)
    normed = (values - mean[:, None]) * inv_std[:, None]
    preact = gain[:, None] * normed + bias[:, None]
    squash = jax.nn.sigmoid(preact)
    pre_grad = conv_grad * squash * (1.0 + preact * (1.0 - squash))
    sums = jnp.stack([jnp.sum(pre_grad, 1), jnp.sum(pre_grad * normed, 1)])
    terms = group_total(sums * gain, group_width) / entries
    grad = cotangent.reshape(sub, places) + inv_std[:, None] * (
        gain[:, None] * pre_grad - terms[0][:, None] - normed * terms[1][:, None]
    )
    return grad, sums


def plain_shards(
    acts_fine,
    acts_coarse,
    grad_coarse,
    gain_fine,
    bias_fine,
    kernel_fine,
    gain_coarse,
    bias_coarse,
    kernel_coarse,
):
    nf, nr, nd = lax.axis_size("frames"), lax.axis_size("rows"), lax.axis_size("dp")
    count = nf * nr
    channels = acts_fine.shape[-1]
    slice_width = kernel_fine.shape[1]
    sub = slice_width // nf
    group_width = channels // GROUPS
    tl, hl, w = acts_coarse.shape[1:4]
    frames, rows = tl * nf, hl * nr
    f, r = lax.axis_index("frames"), lax.axis_index("rows")

    gathered = plain_everyone(grad_coarse[0], count)
    source = (
        gathered.reshape(nf, nr, tl, hl, w, channels)
        .transpose(0, 2, 1, 3, 4, 5)
        .reshape(frames, rows, w, channels)
    )
    coarse_in = acts_coarse[0].reshape(tl, hl, w, nr, nf, sub).transpose(4, 3, 5, 0, 1, 2)
    coarse_in = lax.all_to_all(coarse_in.reshape(count, sub, tl * hl * w), PLAIN_BLOCK, 0, 0)
    fine_in = acts_fine[0].reshape(tl, hl, 2, w, 2, nr, nf, sub).transpose(6, 5, 7, 2, 4, 0, 1, 3)
    fine_in = lax.all_to_all(fine_in.reshape(count, sub, 4 * tl * hl * w), PLAIN_BLOCK, 0, 0)

    def mine(vector):
        return lax.dynamic_slice_in_dim(vector, r * slice_width + f * sub, sub)

    def own(kernel):
        return lax.dynamic_slice_in_dim(kernel, f * sub, sub, axis=1)

    coarse_vals = (
        coarse_in.reshape(nf, nr, sub, tl, hl, w).transpose(2, 0, 3, 1, 4, 5).reshape(sub, frames, rows, w)
    )
    cot = lax.dynamic_slice_in_dim(source, r * slice_width + f * sub, sub, axis=3)
    cot = cot.astype(jnp.float32).transpose(3, 0, 1, 2)
    conv = coarse_conv(source, own(kernel_coarse))
    coarse_grad, coarse_sums = level(
        coarse_vals, conv, cot, mine(gain_coarse), mine(bias_coarse), group_width
    )
    quartered = (coarse_grad * 0.25).astype(jnp.bfloat16)
    spread = plain_everyone(quartered, count)
    source_fine = (
        spread.reshape(nf, nr, sub, frames, rows, w)
        .transpose(3, 4, 5, 1, 0, 2)
        .reshape(frames, rows, w, channels)
    )
    conv = fine_conv(source_fine, own(kernel_fine))
    fine_vals = (
        fine_in.reshape(nf, nr, sub, 2, 2, tl, hl, w)
        .transpose(2, 3, 4, 0, 5, 1, 6, 7)
        .reshape(sub, 2, 2, frames, rows, w)
    )
    cot = jnp.broadcast_to(
        quartered.astype(jnp.float32).reshape(sub, 1, 1, frames, rows, w), conv.shape
    )
    fine_grad, fine_sums = level(
        fine_vals, conv, cot, mine(gain_fine), mine(bias_fine), group_width
    )
    back = (
        fine_grad.astype(jnp.bfloat16)
        .reshape(sub, 2, 2, nf, tl, nr, hl, w)
        .transpose(3, 5, 0, 1, 2, 4, 6, 7)
        .reshape(count, sub, 4 * tl * hl * w)
    )
    sums = plain_everyone(jnp.concatenate([fine_sums, coarse_sums]), count)
    back = lax.all_to_all(back, PLAIN_BLOCK, 0, 0)
    out = (
        back.reshape(nf, nr, sub, 2, 2, tl, hl, w)
        .transpose(5, 6, 3, 7, 4, 1, 0, 2)
        .reshape(1, tl, 2 * hl, 2 * w, channels)
    )
    sums = sums.reshape(nf, nr, 4, sub).transpose(2, 1, 0, 3).reshape(4, channels)
    totals = lax.psum(sums, "dp")
    cells = nd * frames * rows * w
    scale_fine = 1.0 / jnp.sqrt(jnp.float32(4 * cells))
    scale_coarse = 1.0 / jnp.sqrt(jnp.float32(cells))
    return (
        out,
        totals[1] * scale_fine,
        totals[0] * scale_fine,
        totals[3] * scale_coarse,
        totals[2] * scale_coarse,
    )


def lanes_at(shape, axis):
    return lax.broadcasted_iota(jnp.int32, shape, axis)


def one_hot(found):
    return found.astype(jnp.float32).astype(jnp.bfloat16)


def pixel_order(plan, swapped):
    tl, hl, w = plan.tl, plan.hl, plan.w // 2
    size = 4 * plan.local
    lane = lanes_at((1, size), 1)
    j, i, t = lane % w, lane // w % hl, lane // (w * hl) % tl
    q, p = lane // (w * hl * tl) % 2, lane // (2 * w * hl * tl) % 2
    half = lane // (4 * w * hl * tl)
    if swapped:
        half = 1 - half
    pixel = (t * 2 * hl + 2 * i + p) * 4 * w + 2 * (half * w + j) + q
    return one_hot(lanes_at((size, size), 0) == pixel)


def merged_order(nr, outer, tl, cells):
    size = nr * outer * tl * cells
    lane = lanes_at((1, size), 1)
    cell, dev = lane % cells, lane // cells % nr
    t, o = lane // (cells * nr) % tl, lane // (cells * nr * tl)
    return one_hot(lanes_at((size, size), 0) == ((dev * outer + o) * tl + t) * cells + cell)


def column_order(plan):
    w = plan.w // 2
    lines = plan.places // plan.w
    lane = lanes_at((1, 4 * lines * w + 4 * lines), 1)
    inner = lane % (lines * w)
    place = inner // w * plan.w + lane // (lines * w) * w + inner % w
    past = lane - 2 * lines * w
    border = past % lines * plan.w + jnp.where(past < 2 * lines, w, w - 1)
    wanted = jnp.where(past >= 0, border, place)
    shape = (plan.places, 2 * lines * w + 4 * lines)
    return one_hot(lanes_at(shape, 0) == wanted[:, : shape[1]])


def one_hot_dot(a, b, dims):
    return lax.dot_general(a, b, (dims, ((), ())), preferred_element_type=jnp.float32)


def moved(field, distance, kept):
    size = field.shape[1]
    return jnp.where(kept, pltpu.roll(field, (-distance) % size, 1), 0.0)


def own_column(row, base, sub):
    shape = (sub, row.shape[1])
    mine = lanes_at(shape, 1) == lanes_at(shape, 0) + base
    return jnp.sum(jnp.where(mine, row, 0.0), axis=1, keepdims=True)


def as_row(column):
    shape = (column.shape[0], 128)
    here = lanes_at(shape, 1) == lanes_at(shape, 0)
    return jnp.sum(jnp.where(here, column, 0.0), axis=0, keepdims=True)


def terms(value, count):
    found = []
    for _ in range(count):
        found.append(value.astype(jnp.bfloat16).astype(jnp.float32))
        value = value - found[-1]
    return found


def in_groups(column, group_width):
    sub = column.shape[0]
    grouped = jnp.sum(column.reshape(sub // group_width, group_width, 1), axis=1, keepdims=True)
    return jnp.broadcast_to(grouped, (sub // group_width, group_width, 1)).reshape(sub, 1)


def in_lane_groups(row, group_width):
    lane = lanes_at(row.shape, 1)
    size = row.shape[1]
    step = 1
    while step < group_width:
        up, down = pltpu.roll(row, size - step, 1), pltpu.roll(row, step, 1)
        row = row + jnp.where(lane // step % 2 == 0, up, down)
        step *= 2
    return row


def total(parts):
    return sum(jnp.sum(part, axis=1, keepdims=True) for part in parts)


def statistics(one, two, entries, group_width):
    mean = in_groups(one, group_width) / entries
    square = in_groups(two, group_width) / entries
    return mean, lax.rsqrt(square - mean * mean + EPSILON)


def normalised(parts, gain, bias, mean, inv_std):
    normed, slope = [], []
    for part in parts:
        unit = (part - mean) * inv_std
        preact = gain * unit + bias
        squash = jax.nn.sigmoid(preact)
        normed.append(unit)
        slope.append(squash * (1.0 + preact * (1.0 - squash)))
    return normed, slope


class Plan:
    def __init__(self, mesh_sizes, acts_coarse, slice_width):
        self.nf, self.nr = mesh_sizes
        self.count = self.nf * self.nr
        self.tl, self.hl, self.w, self.channels = acts_coarse
        self.slice_width = slice_width
        self.sub = slice_width // self.nf
        self.cells = self.hl * self.w
        self.local = self.tl * self.cells
        self.image = self.cells * self.nr
        self.frames = self.tl * self.nf
        self.places = self.frames * self.image
        self.group_width = self.channels // GROUPS
        self.chunks = self.channels // 128
        self.acts_at = self.chunks // 2 * self.local
        self.packed_at = self.acts_at + self.sub
        self.cot_at = self.packed_at + 8
        self.stats_at = self.cot_at + 8
        self.block_rows = self.stats_at + 8
        self.fits = (
            self.sub == 32
            and self.slice_width == 128
            and self.group_width == 16
            and self.cells == 16
            and self.w == 8
            and self.tl == 2
            and self.nr == 4
            and self.nf == 4
            and self.slice_width * self.nr == self.channels
        )

    def holder(self, block):
        return block % 2 * 2 + block // 2

    def place_masks(self, w):
        lane = lanes_at((1, self.places // self.w * w), 1)
        col, row = lane % w, lane // w % (self.hl * self.nr)
        last_row = self.hl * self.nr - 1
        return (lane, col > 0, col < w - 1, row > 0, row < last_row)


def fetched(pairs, sems):
    copies = [pltpu.make_async_copy(src, dst, sems.at[k]) for k, (src, dst) in enumerate(pairs)]
    for copy in copies:
        copy.start()
    return copies


def own_place(plan):
    pair, member, r = lax.axis_index("pairs"), lax.axis_index("member"), lax.axis_index("rows")
    return pair, member, r, r * plan.slice_width + (2 * pair + member) * plan.sub


def pack_kernel(
    plan,
    g_hbm,
    coarse_hbm,
    fine_hbm,
    kernel_c,
    kernel_f,
    gain_c,
    bias_c,
    gain_f,
    bias_f,
    out_ref,
    fine_ref,
    weights_c,
    weights_f,
    columns,
    order,
    fine_order,
    by_column,
    rows,
    g_ref,
    coarse_ref,
    sems,
):
    sub, chunks, local = plan.sub, plan.chunks, plan.local
    pair, member, r, base = own_place(plan)
    depth = plan.channels // 2
    half = pl.ds(pl.multiple_of(member * depth, depth), depth)
    both = pl.ds(pl.multiple_of(2 * pair * sub, 2 * sub), 2 * sub)
    copies = fetched(
        [(fine_hbm, fine_ref), (coarse_hbm, coarse_ref), (g_hbm, g_ref)]
        + [(row, rows.at[k]) for k, row in enumerate((gain_c, bias_c, gain_f, bias_f))]
        + [
            pieces
            for k in range(9)
            for taps in (pl.ds(3 * k, 3),)
            for pieces in (
                (kernel_c.at[taps, both, half], weights_c.at[taps]),
                (kernel_f.at[taps, both, :], weights_f.at[taps]),
            )
        ],
        sems,
    )
    order[...] = merged_order(plan.nr, 4, plan.tl, plan.cells)
    fine_order[...] = merged_order(plan.nr, 8, plan.tl, plan.cells // 2)
    by_column[...] = column_order(plan)
    shape = (local, 4 * 128)
    lane = lanes_at(shape, 1)
    quarter = one_hot(lanes_at(shape, 0) + lane // 128 * local == lane % 128)
    orders = jnp.concatenate([pixel_order(plan, swapped) for swapped in (False, True)], axis=1)
    copies[0].wait()
    acts = fine_ref[...]
    halves = one_hot_dot(acts, orders, ((0,), (0,))).astype(jnp.bfloat16)
    halves = [halves[:, :128], halves[:, 128:]]
    values = acts.astype(jnp.float32)
    one = jnp.sum(values, axis=0, keepdims=True)
    two = jnp.sum(values * values, axis=0, keepdims=True)
    stats = terms(one, 3) + terms(two, 3)
    stats = jnp.concatenate(stats + [jnp.zeros_like(one)] * 2, axis=0).astype(jnp.bfloat16)
    copies[1].wait()
    packed_acts = one_hot_dot(coarse_ref[...], quarter, ((0,), (0,)))
    copies[2].wait()
    packed_cot = one_hot_dot(g_ref[...], quarter, ((0,), (0,)))
    low = lanes_at((sub, 128), 1) < 64
    for s_r in range(plan.nr):
        for s_f in range(plan.nf):
            dest, c = s_r * plan.nf + s_f, s_r * plan.slice_width + s_f * sub
            first, half = s_r * plan.slice_width + s_f // 2 * 2 * sub, s_f % 2
            for k in range(chunks // 2):
                at = (half * chunks // 2 + k) * 128
                out_ref[dest, k * local : (k + 1) * local, :] = g_ref[:, at : at + 128]
            upper, lower = halves[half][first : first + sub], halves[1 - half][first + sub : first + 2 * sub]
            out_ref[dest, plan.acts_at : plan.packed_at, :] = jnp.where(low, upper, lower)
            for at, found in ((plan.packed_at, packed_acts), (plan.cot_at, packed_cot)):
                rows_of = sum(found[c + 8 * k : c + 8 * k + 8, k * 128 : (k + 1) * 128] for k in range(4))
                out_ref[dest, at : at + 8, :] = rows_of.astype(jnp.bfloat16)
            out_ref[dest, plan.stats_at : plan.block_rows, :] = stats[:, s_r * 128 : (s_r + 1) * 128]
    for copy in copies[3:7]:
        copy.wait()
    first = r * plan.slice_width + 2 * pair * sub
    for k in range(2):
        columns[k, 0:sub, :] = jnp.broadcast_to(own_column(rows[k], base, sub), (sub, 128))
        columns[2 + k] = jnp.broadcast_to(own_column(rows[2 + k], first, 2 * sub), (2 * sub, 128))
    for copy in copies[7:]:
        copy.wait()


def by_frame_device(plan, got_ref, at, height):
    return jnp.concatenate(
        [
            jnp.concatenate(
                [got_ref[r * plan.nf + plan.holder(f), at : at + height, :] for r in range(plan.nr)], axis=1
            )
            for f in range(plan.nf)
        ],
        axis=0,
    )


def in_places(plan, merged, height):
    width = plan.tl * plan.image
    return [
        jnp.concatenate(
            [merged[f * height : (f + 1) * height, k * width : (k + 1) * width] for f in range(plan.nf)],
            axis=1,
        )
        for k in range(4)
    ]


def coarse_kernel(
    plan, got_ref, weights, columns, order, mine_ref, sent_ref, held_ref, inv_ref, source, products, conv_ref
):
    sub, nr, nf, cells, tl, local = plan.sub, plan.nr, plan.nf, plan.cells, plan.tl, plan.local
    wide, depth = 2 * sub, plan.channels // 2
    _, member, _, _ = own_place(plan)
    for s_f in range(nf):
        for s_r in range(nr):
            for t in range(tl):
                at = (plan.holder(s_f) * tl + t) * plan.image + s_r * cells
                for k in range(plan.chunks // 2):
                    source[at : at + cells, k * 128 : (k + 1) * 128] = got_ref[
                        s_r * nf + s_f, k * local + t * cells : k * local + (t + 1) * cells, :
                    ]
    source[plan.places :, :] = jnp.zeros((2 * plan.image, depth), jnp.bfloat16)
    products[...] = sum(
        one_hot_dot(
            weights[9 * k : 9 * k + 9].reshape(9 * wide, depth),
            source[(2 - k) * plan.image : (2 - k) * plan.image + plan.places, :],
            ((1,), (1,)),
        )
        for k in range(3)
    )
    found = []
    for at in (plan.packed_at, plan.cot_at):
        merged = one_hot_dot(by_frame_device(plan, got_ref, at, 8), order[...], ((1,), (0,)))
        found.append(jnp.concatenate(in_places(plan, merged, 8), axis=0))
    values, cot = found
    gain, bias = columns[0][0:sub, 0:1], columns[1][0:sub, 0:1]
    entries = plan.places * plan.group_width
    mean, inv_std = statistics(total([values]), total([values * values]), entries, plan.group_width)
    (normed,), (slope,) = normalised([values], gain, bias, mean, inv_std)
    held_ref[0], held_ref[1], held_ref[2] = normed, slope, cot
    inv_ref[...] = jnp.broadcast_to(inv_std, (sub, 128))
    lane, has_left, has_right, has_up, has_down = plan.place_masks(plan.w)
    by_col = []
    for col in range(3):
        parts = [products[pl.ds((3 * row + col) * wide, wide), :] for row in range(3)]
        by_col.append(parts[1] + moved(parts[0], plan.w, has_down) + moved(parts[2], -plan.w, has_up))
    conv_ref[...] = by_col[1] + moved(by_col[0], 1, has_right) + moved(by_col[2], -1, has_left)
    mine_ref[...] = conv_ref[pl.ds(pl.multiple_of(member * sub, sub), sub), :]
    sent_ref[...] = conv_ref[pl.ds(pl.multiple_of((1 - member) * sub, sub), sub), :].astype(jnp.bfloat16)


def quarter_kernel(plan, mine_ref, both_ref, held_ref, inv_ref, columns, by_column, out_ref, sums_ref):
    sub = plan.sub
    _, member, _, _ = own_place(plan)
    conv = mine_ref[...] + both_ref[1 - member].astype(jnp.float32)
    normed, slope, cot = held_ref[0], held_ref[1], held_ref[2]
    gain, inv_std = columns[0][0:sub, 0:1], inv_ref[:, 0:1]
    entries = plan.places * plan.group_width
    pre = conv * slope
    one, two = total([pre]), total([pre * normed])
    group_one = in_groups(gain * one, plan.group_width) / entries
    group_two = in_groups(gain * two, plan.group_width) / entries
    grad = cot + inv_std * (gain * pre - group_one - normed * group_two)
    quartered = (grad * 0.25).astype(jnp.bfloat16)
    sent = one_hot_dot(quartered, by_column[...], ((1,), (0,))).astype(jnp.bfloat16)
    low = lanes_at((sub // 2, 128), 1) < 64
    for half in range(2):
        at = half * 256
        border = sent[:, 512 + half * 128 : 640 + half * 128]
        border = jnp.where(low, border[: sub // 2], border[sub // 2 :])
        for dest in range(half, plan.count, 2):
            out_ref[dest, 0:sub, :] = sent[:, at : at + 128]
            out_ref[dest, sub : 2 * sub, :] = sent[:, at + 128 : at + 256]
            out_ref[dest, 2 * sub : 2 * sub + sub // 2, :] = border
    sums_ref[...] = jnp.concatenate([as_row(one), as_row(two)], axis=0)


def halves_at(plan, merged):
    sub = plan.sub
    turned = jnp.concatenate([pltpu.roll(merged[:, k * 128 : (k + 1) * 128], 64, 1) for k in range(4)], axis=1)
    low = lanes_at((sub, 128), 1) < 64
    parts = []
    for pq in range(4):
        groups = []
        for group in range(2):
            e = 4 * group + pq
            at = e // 2 * 128
            strips = []
            for m in range(plan.nf // 2):
                first, second = slice(2 * m * sub, (2 * m + 1) * sub), slice((2 * m + 1) * sub, (2 * m + 2) * sub)
                if e % 2 == 0:
                    strips.append(jnp.where(low, merged[first, at : at + 128], turned[second, at : at + 128]))
                else:
                    strips.append(jnp.where(low, turned[first, at : at + 128], merged[second, at : at + 128]))
            groups.append(jnp.concatenate(strips, axis=1))
        parts.append(jnp.concatenate(groups, axis=0))
    return parts


def halves_from(plan, parts):
    sub = plan.sub
    low = lanes_at((sub, 128), 1) < 64
    down = []
    for f in range(plan.nf):
        across = []
        for v in range(4):
            pair = []
            for e in (2 * v, 2 * v + 1):
                group, pq = e // 4, e % 4
                strip = parts[pq][group * sub : (group + 1) * sub, f // 2 * 128 : (f // 2 + 1) * 128]
                pair.append(strip if e % 2 == f % 2 else pltpu.roll(strip, 64, 1))
            across.append(jnp.where(low, pair[0], pair[1]))
        down.append(jnp.concatenate(across, axis=1))
    return jnp.concatenate(down, axis=0)


def fine_kernel(
    plan, got_ref, acts_ref, columns, order, sums_ref, weights, out_ref, source, border, products, beyond
):
    sub, nr, nf, wide = plan.sub, plan.nr, plan.nf, 2 * plan.sub
    pair, member, r, _ = own_place(plan)
    w = plan.w // 2
    lines = plan.places // plan.w
    places = lines * w
    for k in range(2):
        source[:, k * 128 : (k + 1) * 128] = got_ref[:, k * sub : (k + 1) * sub, :].reshape(plan.channels, 128)
    packed = got_ref[:, wide : wide + sub // 2, :].reshape(plan.count * sub // 2, 128)
    shape = (128, places)
    beside = lanes_at(shape, 1) == lanes_at(shape, 0) % lines * w + (1 - member) * (w - 1)
    for k in range(2):
        here = one_hot(beside & (lanes_at(shape, 0) // lines == k))
        found = one_hot_dot(packed, here, ((1,), (0,))).astype(jnp.bfloat16)
        for s in range(plan.count):
            border[s * sub + k * (sub // 2) : s * sub + (k + 1) * (sub // 2), :] = found[
                s * (sub // 2) : (s + 1) * (sub // 2)
            ]
    image, shape = plan.image // 2, (places, places)
    sums, extras = 0.0, 0.0
    for k in range(3):
        here, beside = source[...], border[...]
        if k < 2:
            later = one_hot(lanes_at(shape, 0) == lanes_at(shape, 1) + (2 - k) * image)
            here, beside = [one_hot_dot(part, later, ((1,), (0,))).astype(jnp.bfloat16) for part in (here, beside)]
        sums = sums + one_hot_dot(
            weights[9 * k : 9 * k + 9].reshape(9 * wide, plan.channels), here, ((1,), (0,))
        )
        facing = jnp.concatenate([weights[9 * k + 3 * row + 2 * member] for row in range(3)], axis=0)
        extras = extras + one_hot_dot(facing, beside, ((1,), (0,)))
    products[...], beyond[...] = sums, extras
    merged = one_hot_dot(by_frame_device(plan, acts_ref, plan.acts_at, sub), order[...], ((1,), (0,)))
    parts = halves_at(plan, merged)
    stats = sum(
        acts_ref[s, plan.stats_at : plan.block_rows, :].astype(jnp.float32) for s in range(plan.count)
    )
    entries = 4 * plan.places * plan.group_width
    one = own_column(stats[0:1] + stats[1:2] + stats[2:3], pair * wide, wide)
    two = own_column(stats[3:4] + stats[4:5] + stats[5:6], pair * wide, wide)
    mean, inv_std = statistics(one, two, entries, plan.group_width)
    gain, bias = columns[2][:, 0:1], columns[3][:, 0:1]
    normed, slope = normalised(parts, gain, bias, mean, inv_std)
    lane, has_left, has_right, has_up, has_down = plan.place_masks(w)
    right, left = (1 - member).astype(jnp.float32), member.astype(jnp.float32)
    by_row = []
    for row in range(3):
        a, b, c = [products[pl.ds((3 * row + col) * wide, wide), :] for col in range(3)]
        extra = beyond[pl.ds(row * wide, wide), :]
        by_row.append(
            (a + b + moved(c, -1, has_left) + left * extra, moved(a, 1, has_right) + b + c + right * extra)
        )
    convs = [by_row[0][q] + by_row[1][q] + moved(by_row[2][q], -w, has_up) for q in range(2)]
    convs += [moved(by_row[0][q], w, has_down) + by_row[1][q] + by_row[2][q] for q in range(2)]
    pre = [conv * part for conv, part in zip(convs, slope)]
    one = total(pre)
    two = total([a * b for a, b in zip(pre, normed)])
    cot = source[pl.ds(pl.multiple_of(r * plan.slice_width + pair * wide, wide), wide), :].astype(jnp.float32)
    scale = inv_std * gain
    stacked = halves_from(plan, [cot + scale * part for part in pre]).astype(jnp.bfloat16)
    sent = one_hot_dot(stacked, order[...], ((1,), (1,))).astype(jnp.bfloat16)
    coarse = sums_ref[0:1] + pltpu.roll(sums_ref[1:2], sub, 1)
    coded = (
        terms(as_row(one) + pltpu.roll(as_row(two), 64, 1), 2)
        + terms(coarse, 2)
        + terms(as_row(inv_std) + pltpu.roll(as_row(mean), 64, 1), 3)
    )
    coded = jnp.concatenate(coded + [jnp.zeros_like(coarse)], axis=0).astype(jnp.bfloat16)
    for s_r in range(nr):
        for s_f in range(nf):
            dest = s_r * nf + plan.holder(s_f)
            out_ref[dest, 0:sub, :] = sent[s_f * sub : (s_f + 1) * sub, s_r * 128 : (s_r + 1) * 128]
            out_ref[dest, sub : sub + 8, :] = coded


def spread_kernel(plan, got_ref, acts_ref, rows_ref, out_ref, sums_ref):
    sub, nr, nf = plan.sub, plan.nr, plan.nf
    low = lanes_at((sub, 128), 1) < 64
    low_row = lanes_at((1, 128), 1) < 64
    first_row = lanes_at((1, 128), 1) < sub
    source = []
    fine, coarse, moments = [[], []], [[], []], [[], []]
    for s_r in range(nr):
        ones, twos, c_ones, c_twos, invs, means = [], [], 0.0, 0.0, [], []
        for pair in range(nf // 2):
            at = s_r * nf + 2 * pair
            left, right = [got_ref[at + k, 0:sub, :].astype(jnp.float32) for k in range(2)]
            source.append(jnp.where(low, left, pltpu.roll(right, 64, 1)))
            source.append(jnp.where(low, pltpu.roll(left, 64, 1), right))
            coded = [got_ref[at + k, sub : sub + 8, :].astype(jnp.float32) for k in range(2)]
            sums = coded[0][0:1] + coded[0][1:2] + coded[1][0:1] + coded[1][1:2]
            ones.append(sums if pair == 0 else pltpu.roll(sums, 64, 1))
            twos.append(pltpu.roll(sums, 64, 1) if pair == 0 else sums)
            both = coded[0][4:5] + coded[0][5:6] + coded[0][6:7]
            invs.append(both if pair == 0 else pltpu.roll(both, 64, 1))
            means.append(pltpu.roll(both, 64, 1) if pair == 0 else both)
            for k in range(2):
                sums = coded[k][2:3] + coded[k][3:4]
                to = (2 * pair + k) * sub
                c_one = jnp.where(first_row, sums, 0.0)
                c_two = jnp.where(first_row, pltpu.roll(sums, 128 - sub, 1), 0.0)
                c_ones = c_ones + (pltpu.roll(c_one, to, 1) if to else c_one)
                c_twos = c_twos + (pltpu.roll(c_two, to, 1) if to else c_two)
        fine[0].append(jnp.where(low_row, ones[0], ones[1]))
        fine[1].append(jnp.where(low_row, twos[0], twos[1]))
        moments[0].append(jnp.where(low_row, invs[0], invs[1]))
        moments[1].append(jnp.where(low_row, means[0], means[1]))
        coarse[0].append(c_ones)
        coarse[1].append(c_twos)
    one, two, inv_std, mean, c_one, c_two = [jnp.concatenate(part, axis=1) for part in fine + moments + coarse]
    source = jnp.concatenate(source, axis=0).astype(jnp.bfloat16)
    result = one_hot_dot(pixel_order(plan, False), source, ((1,), (1,)))
    gain = rows_ref[2]
    entries = 4 * plan.places * plan.group_width
    group_one = in_lane_groups(gain * one, plan.group_width) / entries
    group_two = in_lane_groups(gain * two, plan.group_width) / entries
    normed = (acts_ref[...].astype(jnp.float32) - mean) * inv_std
    out_ref[...] = (result - inv_std * (group_one + normed * group_two)).astype(jnp.bfloat16)
    sums_ref[...] = jnp.concatenate([one, two, c_one, c_two] + [jnp.zeros_like(one)] * 4, axis=0)


def total_kernel(scales, both_ref, result_ref, result_hbm, out_hbms, rows_ref, sems):
    copies = fetched([(result_ref, result_hbm)], sems)
    rows = sum(both_ref[k] for k in range(both_ref.shape[0]))
    for k in range(4):
        rows_ref[k] = rows[k : k + 1] * scales[k]
    for k in range(4):
        copies.append(pltpu.make_async_copy(rows_ref.at[k], out_hbms[k], sems.at[k + 1]))
        copies[-1].start()
    for copy in copies:
        copy.wait()


def in_vmem(count):
    return [pl.BlockSpec(memory_space=pltpu.VMEM)] * count


def in_hbm(count):
    return [pl.BlockSpec(memory_space=pltpu.HBM)] * count


def kept(array):
    return pltpu.with_memory_space_constraint(array, pltpu.HBM)


def shape_of(shape, kind):
    return jax.ShapeDtypeStruct(shape, kind)


LIMIT = pltpu.CompilerParams(vmem_limit_bytes=40 * 1024 * 1024)


def fast_shards(
    plan,
    acts_fine,
    acts_coarse,
    grad_coarse,
    gain_fine,
    bias_fine,
    kernel_fine,
    gain_coarse,
    bias_coarse,
    kernel_coarse,
):
    nd = lax.axis_size("dp")
    count, sub, channels, places, local = plan.count, plan.sub, plan.channels, plan.places, plan.local
    f32, bf16 = jnp.float32, jnp.bfloat16
    rows = [part.reshape(1, channels) for part in (gain_coarse, bias_coarse, gain_fine, bias_fine)]
    packed, acts, weights_c, weights_f, columns, order, fine_order, by_column, rows = pl.pallas_call(
        functools.partial(pack_kernel, plan),
        out_shape=(
            shape_of((count, plan.block_rows, 128), bf16),
            shape_of((4 * local, channels), bf16),
            shape_of((27, 2 * sub, channels // 2), bf16),
            shape_of((27, 2 * sub, channels), bf16),
            shape_of((4, 2 * sub, 128), f32),
            shape_of((4 * plan.nr * local, 4 * plan.nr * local), bf16),
            shape_of((4 * plan.nr * local, 4 * plan.nr * local), bf16),
            shape_of((places, places + places // 2), bf16),
            shape_of((4, 1, channels), f32),
        ),
        in_specs=in_hbm(9),
        out_specs=tuple(in_vmem(9)),
        scratch_shapes=[
            pltpu.VMEM((local, channels), bf16),
            pltpu.VMEM((local, channels), bf16),
            pltpu.SemaphoreType.DMA((25,)),
        ],
        compiler_params=LIMIT,
    )(
        kept(grad_coarse.reshape(local, channels)),
        kept(acts_coarse.reshape(local, channels)),
        kept(acts_fine.reshape(4 * local, channels)),
        kept(kernel_coarse),
        kept(kernel_fine),
        *[kept(row) for row in rows],
    )
    got = lax.all_to_all(packed, BLOCK, 0, 0)
    mine, theirs, held, inv_std = pl.pallas_call(
        functools.partial(coarse_kernel, plan),
        out_shape=(
            shape_of((sub, places), f32),
            shape_of((sub, places), bf16),
            shape_of((3, sub, places), f32),
            shape_of((sub, 128), f32),
        ),
        in_specs=in_vmem(4),
        out_specs=tuple(in_vmem(4)),
        scratch_shapes=[
            pltpu.VMEM((places + 2 * plan.image, channels // 2), bf16),
            pltpu.VMEM((18 * sub, places), f32),
            pltpu.VMEM((2 * sub, places), f32),
        ],
        compiler_params=LIMIT,
    )(got, weights_c, columns, order)
    both = lax.all_gather(theirs, "member")
    quartered, coarse_sums = pl.pallas_call(
        functools.partial(quarter_kernel, plan),
        out_shape=(shape_of((count, 2 * sub + sub // 2, 128), bf16), shape_of((2, 128), f32)),
        in_specs=in_vmem(6),
        out_specs=tuple(in_vmem(2)),
        compiler_params=LIMIT,
    )(mine, both, held, inv_std, columns, by_column)
    spread = lax.all_to_all(quartered, BLOCK, 0, 0)
    sent = pl.pallas_call(
        functools.partial(fine_kernel, plan),
        out_shape=shape_of((count, sub + 8, 128), bf16),
        in_specs=in_vmem(6),
        out_specs=in_vmem(1)[0],
        scratch_shapes=[
            pltpu.VMEM((channels, places // 2), bf16),
            pltpu.VMEM((channels, places // 2), bf16),
            pltpu.VMEM((18 * sub, places // 2), f32),
            pltpu.VMEM((6 * sub, places // 2), f32),
        ],
        compiler_params=LIMIT,
    )(spread, got, columns, fine_order, coarse_sums, weights_f)
    back = lax.all_to_all(sent, BLOCK, 0, 0)
    cells = nd * places
    fine_scale, coarse_scale = 1.0 / math.sqrt(4 * cells), 1.0 / math.sqrt(cells)
    out, sums = pl.pallas_call(
        functools.partial(spread_kernel, plan),
        out_shape=(pltpu.VMEM((4 * local, channels), bf16), shape_of((8, channels), f32)),
        in_specs=in_vmem(3),
        out_specs=tuple(in_vmem(2)),
        compiler_params=LIMIT,
    )(back, acts, rows)
    both = lax.all_gather(sums, "dp")
    out, sums = pl.pallas_call(
        functools.partial(total_kernel, (fine_scale, fine_scale, coarse_scale, coarse_scale)),
        out_shape=(pltpu.HBM((4 * local, channels), bf16), (pltpu.HBM((1, channels), f32),) * 4),
        in_specs=in_vmem(2),
        out_specs=(in_hbm(1)[0], tuple(in_hbm(4))),
        scratch_shapes=[pltpu.VMEM((4, 1, channels), f32), pltpu.SemaphoreType.DMA((5,))],
        compiler_params=LIMIT,
    )(both, out)
    bias_f, gain_f, bias_c, gain_c = [part.reshape(channels) for part in sums]
    return out.reshape(acts_fine.shape), gain_f, bias_f, gain_c, bias_c


def solution(mesh):
    def function(*arrays):
        local = [size // mesh.shape[axis] for size, axis in zip(arrays[1].shape, ("dp", "frames", "rows"))]
        sizes = (mesh.shape["frames"], mesh.shape["rows"])
        plan = Plan(sizes, (*local[1:], *arrays[1].shape[3:]), arrays[5].shape[1] // mesh.shape["rows"])
        if plan.fits:
            split = (mesh.shape["dp"], 2, plan.nf // 2, plan.nr)
            used = jax.sharding.Mesh(mesh.devices.reshape(split), ("dp", "member", "pairs", "rows"))
            shards, frames = functools.partial(fast_shards, plan), ("member", "pairs")
        else:
            used, shards, frames = mesh, plain_shards, "frames"
        blocks, kernel = P("dp", frames, "rows", None, None), P(None, "rows", None)
        in_specs = (blocks, blocks, blocks, P(), P(), kernel, P(), P(), kernel)
        out_specs = (blocks, P(), P(), P(), P())
        mapped = jax.shard_map(shards, mesh=used, in_specs=in_specs, out_specs=out_specs, check_vma=False)
        return mapped(*arrays)

    return function
```

```python
import functools
import math

import jax
import jax.numpy as jnp
from jax import lax
from jax.experimental import pallas as pl
from jax.experimental.pallas import tpu as pltpu
from jax.sharding import PartitionSpec as P

GROUPS = 32
EPSILON = 1e-06
BLOCK = ("rows", "pairs", "member")
PLAIN_BLOCK = ("frames", "rows")


def plain_everyone(block, count):
    copies = jnp.broadcast_to(block[None], (count,) + block.shape)
    return lax.all_to_all(copies, PLAIN_BLOCK, 0, 0)


def ahead(field, axis, distance):
    size = field.shape[axis]
    if distance == 0:
        return field
    widths = [(0, 0)] * field.ndim
    if distance > 0:
        widths[axis] = (0, distance)
        kept = lax.slice_in_dim(field, distance, size, axis=axis)
    else:
        widths[axis] = (-distance, 0)
        kept = lax.slice_in_dim(field, 0, size + distance, axis=axis)
    return jnp.pad(kept, widths)


def tap_products(source, kernel):
    sub = kernel.shape[1]
    frames, rows, cols, channels = source.shape
    products = lax.dot_general(
        kernel.reshape(27 * sub, channels),
        source.reshape(frames * rows * cols, channels),
        (((1,), (1,)), ((), ())),
        preferred_element_type=jnp.float32,
    ).reshape(3, 3, 3, sub, frames, rows, cols)
    return sum(ahead(products[depth], 3, 2 - depth) for depth in range(3))


def coarse_conv(source, kernel):
    spatial = tap_products(source, kernel)
    total = 0.0
    for row in range(3):
        part = sum(ahead(spatial[row, col], 3, 1 - col) for col in range(3))
        total = total + ahead(part, 2, 1 - row)
    return total


def fine_conv(source, kernel):
    spatial = tap_products(source, kernel)
    result = []
    for p in range(2):
        rows_of = []
        for q in range(2):
            total = 0.0
            for row in range(3):
                part = sum(ahead(spatial[row, col], 3, (q + 1 - col) // 2) for col in range(3))
                total = total + ahead(part, 2, (p + 1 - row) // 2)
            rows_of.append(total)
        result.append(jnp.stack(rows_of, 1))
    return jnp.stack(result, 1)


def group_total(sums, group_width):
    sub = sums.shape[-1]
    if sub % group_width == 0:
        grouped = jnp.sum(sums.reshape(-1, sub // group_width, group_width), axis=-1)
        return jnp.repeat(grouped, group_width, axis=-1)
    spread = jnp.moveaxis(lax.all_gather(sums, "frames"), 0, 1).reshape(sums.shape[0], -1, group_width)
    mine = lax.axis_index("frames") * sub // group_width
    grouped = lax.dynamic_index_in_dim(jnp.sum(spread, -1), mine, 1)
    return jnp.broadcast_to(grouped, sums.shape)


def level(acts, conv_grad, cotangent, gain, bias, group_width):
    sub = acts.shape[0]
    places = acts.size // sub
    values = acts.astype(jnp.float32).reshape(sub, places)
    conv_grad = conv_grad.reshape(sub, places)
    entries = places * group_width
    moments = group_total(
        jnp.stack([jnp.sum(values, 1), jnp.sum(values * values, 1)]), group_width
    ) / entries
    mean = moments[0]
    inv_std = lax.rsqrt(moments[1] - mean * mean + EPSILON)
    normed = (values - mean[:, None]) * inv_std[:, None]
    preact = gain[:, None] * normed + bias[:, None]
    squash = jax.nn.sigmoid(preact)
    pre_grad = conv_grad * squash * (1.0 + preact * (1.0 - squash))
    sums = jnp.stack([jnp.sum(pre_grad, 1), jnp.sum(pre_grad * normed, 1)])
    terms = group_total(sums * gain, group_width) / entries
    grad = cotangent.reshape(sub, places) + inv_std[:, None] * (
        gain[:, None] * pre_grad - terms[0][:, None] - normed * terms[1][:, None]
    )
    return grad, sums


def plain_shards(
    acts_fine,
    acts_coarse,
    grad_coarse,
    gain_fine,
    bias_fine,
    kernel_fine,
    gain_coarse,
    bias_coarse,
    kernel_coarse,
):
    nf, nr, nd = lax.axis_size("frames"), lax.axis_size("rows"), lax.axis_size("dp")
    count = nf * nr
    channels = acts_fine.shape[-1]
    slice_width = kernel_fine.shape[1]
    sub = slice_width // nf
    group_width = channels // GROUPS
    tl, hl, w = acts_coarse.shape[1:4]
    frames, rows = tl * nf, hl * nr
    f, r = lax.axis_index("frames"), lax.axis_index("rows")

    gathered = plain_everyone(grad_coarse[0], count)
    source = (
        gathered.reshape(nf, nr, tl, hl, w, channels)
        .transpose(0, 2, 1, 3, 4, 5)
        .reshape(frames, rows, w, channels)
    )
    coarse_in = acts_coarse[0].reshape(tl, hl, w, nr, nf, sub).transpose(4, 3, 5, 0, 1, 2)
    coarse_in = lax.all_to_all(coarse_in.reshape(count, sub, tl * hl * w), PLAIN_BLOCK, 0, 0)
    fine_in = acts_fine[0].reshape(tl, hl, 2, w, 2, nr, nf, sub).transpose(6, 5, 7, 2, 4, 0, 1, 3)
    fine_in = lax.all_to_all(fine_in.reshape(count, sub, 4 * tl * hl * w), PLAIN_BLOCK, 0, 0)

    def mine(vector):
        return lax.dynamic_slice_in_dim(vector, r * slice_width + f * sub, sub)

    def own(kernel):
        return lax.dynamic_slice_in_dim(kernel, f * sub, sub, axis=1)

    coarse_vals = (
        coarse_in.reshape(nf, nr, sub, tl, hl, w).transpose(2, 0, 3, 1, 4, 5).reshape(sub, frames, rows, w)
    )
    cot = lax.dynamic_slice_in_dim(source, r * slice_width + f * sub, sub, axis=3)
    cot = cot.astype(jnp.float32).transpose(3, 0, 1, 2)
    conv = coarse_conv(source, own(kernel_coarse))
    coarse_grad, coarse_sums = level(
        coarse_vals, conv, cot, mine(gain_coarse), mine(bias_coarse), group_width
    )
    quartered = (coarse_grad * 0.25).astype(jnp.bfloat16)
    spread = plain_everyone(quartered, count)
    source_fine = (
        spread.reshape(nf, nr, sub, frames, rows, w)
        .transpose(3, 4, 5, 1, 0, 2)
        .reshape(frames, rows, w, channels)
    )
    conv = fine_conv(source_fine, own(kernel_fine))
    fine_vals = (
        fine_in.reshape(nf, nr, sub, 2, 2, tl, hl, w)
        .transpose(2, 3, 4, 0, 5, 1, 6, 7)
        .reshape(sub, 2, 2, frames, rows, w)
    )
    cot = jnp.broadcast_to(
        quartered.astype(jnp.float32).reshape(sub, 1, 1, frames, rows, w), conv.shape
    )
    fine_grad, fine_sums = level(
        fine_vals, conv, cot, mine(gain_fine), mine(bias_fine), group_width
    )
    back = (
        fine_grad.astype(jnp.bfloat16)
        .reshape(sub, 2, 2, nf, tl, nr, hl, w)
        .transpose(3, 5, 0, 1, 2, 4, 6, 7)
        .reshape(count, sub, 4 * tl * hl * w)
    )
    sums = plain_everyone(jnp.concatenate([fine_sums, coarse_sums]), count)
    back = lax.all_to_all(back, PLAIN_BLOCK, 0, 0)
    out = (
        back.reshape(nf, nr, sub, 2, 2, tl, hl, w)
        .transpose(5, 6, 3, 7, 4, 1, 0, 2)
        .reshape(1, tl, 2 * hl, 2 * w, channels)
    )
    sums = sums.reshape(nf, nr, 4, sub).transpose(2, 1, 0, 3).reshape(4, channels)
    totals = lax.psum(sums, "dp")
    cells = nd * frames * rows * w
    scale_fine = 1.0 / jnp.sqrt(jnp.float32(4 * cells))
    scale_coarse = 1.0 / jnp.sqrt(jnp.float32(cells))
    return (
        out,
        totals[1] * scale_fine,
        totals[0] * scale_fine,
        totals[3] * scale_coarse,
        totals[2] * scale_coarse,
    )


def lanes_at(shape, axis):
    return lax.broadcasted_iota(jnp.int32, shape, axis)


def one_hot(found):
    return found.astype(jnp.float32).astype(jnp.bfloat16)


def pixel_order(plan, swapped):
    tl, hl, w = plan.tl, plan.hl, plan.w // 2
    size = 4 * plan.local
    lane = lanes_at((1, size), 1)
    j, i, t = lane % w, lane // w % hl, lane // (w * hl) % tl
    q, p = lane // (w * hl * tl) % 2, lane // (2 * w * hl * tl) % 2
    half = lane // (4 * w * hl * tl)
    if swapped:
        half = 1 - half
    pixel = (t * 2 * hl + 2 * i + p) * 4 * w + 2 * (half * w + j) + q
    return one_hot(lanes_at((size, size), 0) == pixel)


def merged_order(nr, outer, tl, cells):
    size = nr * outer * tl * cells
    lane = lanes_at((1, size), 1)
    cell, dev = lane % cells, lane // cells % nr
    t, o = lane // (cells * nr) % tl, lane // (cells * nr * tl)
    return one_hot(lanes_at((size, size), 0) == ((dev * outer + o) * tl + t) * cells + cell)


def column_order(plan):
    w = plan.w // 2
    lines = plan.places // plan.w
    lane = lanes_at((1, 4 * lines * w + 4 * lines), 1)
    inner = lane % (lines * w)
    place = inner // w * plan.w + lane // (lines * w) * w + inner % w
    past = lane - 2 * lines * w
    border = past % lines * plan.w + jnp.where(past < 2 * lines, w, w - 1)
    wanted = jnp.where(past >= 0, border, place)
    shape = (plan.places, 2 * lines * w + 4 * lines)
    return one_hot(lanes_at(shape, 0) == wanted[:, : shape[1]])


def one_hot_dot(a, b, dims):
    return lax.dot_general(a, b, (dims, ((), ())), preferred_element_type=jnp.float32)


def moved(field, distance, kept):
    size = field.shape[1]
    return jnp.where(kept, pltpu.roll(field, (-distance) % size, 1), 0.0)


def own_column(row, base, sub):
    shape = (sub, row.shape[1])
    mine = lanes_at(shape, 1) == lanes_at(shape, 0) + base
    return jnp.sum(jnp.where(mine, row, 0.0), axis=1, keepdims=True)


def as_row(column):
    shape = (column.shape[0], 128)
    here = lanes_at(shape, 1) == lanes_at(shape, 0)
    return jnp.sum(jnp.where(here, column, 0.0), axis=0, keepdims=True)


def terms(value, count):
    found = []
    for _ in range(count):
        found.append(value.astype(jnp.bfloat16).astype(jnp.float32))
        value = value - found[-1]
    return found


def in_groups(column, group_width):
    sub = column.shape[0]
    grouped = jnp.sum(column.reshape(sub // group_width, group_width, 1), axis=1, keepdims=True)
    return jnp.broadcast_to(grouped, (sub // group_width, group_width, 1)).reshape(sub, 1)


def in_lane_groups(row, group_width):
    lane = lanes_at(row.shape, 1)
    size = row.shape[1]
    step = 1
    while step < group_width:
        up, down = pltpu.roll(row, size - step, 1), pltpu.roll(row, step, 1)
        row = row + jnp.where(lane // step % 2 == 0, up, down)
        step *= 2
    return row


def total(parts):
    return sum(jnp.sum(part, axis=1, keepdims=True) for part in parts)


def statistics(one, two, entries, group_width):
    mean = in_groups(one, group_width) / entries
    square = in_groups(two, group_width) / entries
    return mean, lax.rsqrt(square - mean * mean + EPSILON)


def normalised(parts, gain, bias, mean, inv_std):
    normed, slope = [], []
    for part in parts:
        unit = (part - mean) * inv_std
        preact = gain * unit + bias
        squash = jax.nn.sigmoid(preact)
        normed.append(unit)
        slope.append(squash * (1.0 + preact * (1.0 - squash)))
    return normed, slope


class Plan:
    def __init__(self, mesh_sizes, acts_coarse, slice_width):
        self.nf, self.nr = mesh_sizes
        self.count = self.nf * self.nr
        self.tl, self.hl, self.w, self.channels = acts_coarse
        self.slice_width = slice_width
        self.sub = slice_width // self.nf
        self.cells = self.hl * self.w
        self.local = self.tl * self.cells
        self.image = self.cells * self.nr
        self.frames = self.tl * self.nf
        self.places = self.frames * self.image
        self.group_width = self.channels // GROUPS
        self.chunks = self.channels // 128
        self.acts_at = self.chunks // 2 * self.local
        self.packed_at = self.acts_at + self.sub
        self.cot_at = self.packed_at + 8
        self.block_rows = self.cot_at + 8
        self.fits = (
            self.sub == 32
            and self.slice_width == 128
            and self.group_width == 16
            and self.cells == 16
            and self.w == 8
            and self.tl == 2
            and self.nr == 4
            and self.nf == 4
            and self.slice_width * self.nr == self.channels
        )

    def place_masks(self, w):
        lane = lanes_at((1, self.places // self.w * w), 1)
        col, row = lane % w, lane // w % (self.hl * self.nr)
        last_row = self.hl * self.nr - 1
        return (lane, col > 0, col < w - 1, row > 0, row < last_row)


def fetched(pairs, sems):
    copies = [pltpu.make_async_copy(src, dst, sems.at[k]) for k, (src, dst) in enumerate(pairs)]
    for copy in copies:
        copy.start()
    return copies


def own_place(plan):
    pair, member, r = lax.axis_index("pairs"), lax.axis_index("member"), lax.axis_index("rows")
    return pair, member, r, r * plan.slice_width + (2 * pair + member) * plan.sub


def pack_kernel(
    plan,
    g_hbm,
    coarse_hbm,
    fine_hbm,
    kernel_c,
    kernel_f,
    gain_c,
    bias_c,
    gain_f,
    bias_f,
    out_ref,
    fine_ref,
    weights_c,
    weights_f,
    columns,
    order,
    fine_order,
    by_column,
    rows,
    g_ref,
    coarse_ref,
    sems,
):
    sub, chunks, local = plan.sub, plan.chunks, plan.local
    pair, member, r, base = own_place(plan)
    depth = plan.channels // 2
    half = pl.ds(pl.multiple_of(member * depth, depth), depth)
    both = pl.ds(pl.multiple_of(2 * pair * sub, 2 * sub), 2 * sub)
    copies = fetched(
        [(fine_hbm, fine_ref), (coarse_hbm, coarse_ref), (g_hbm, g_ref)]
        + [(row, rows.at[k]) for k, row in enumerate((gain_c, bias_c, gain_f, bias_f))]
        + [(kernel_c.at[:, both, half], weights_c), (kernel_f.at[:, both, :], weights_f)],
        sems,
    )
    order[...] = merged_order(plan.nr, 4, plan.tl, plan.cells)
    fine_order[...] = merged_order(plan.nr, 8, plan.tl, plan.cells // 2)
    by_column[...] = column_order(plan)
    shape = (local, 4 * 128)
    lane = lanes_at(shape, 1)
    quarter = one_hot(lanes_at(shape, 0) + lane // 128 * local == lane % 128)
    orders = jnp.concatenate([pixel_order(plan, swapped) for swapped in (False, True)], axis=1)
    copies[0].wait()
    acts = fine_ref[...]
    halves = one_hot_dot(acts, orders, ((0,), (0,))).astype(jnp.bfloat16)
    halves = [halves[:, :128], halves[:, 128:]]
    copies[1].wait()
    packed_acts = one_hot_dot(coarse_ref[...], quarter, ((0,), (0,)))
    copies[2].wait()
    packed_cot = one_hot_dot(g_ref[...], quarter, ((0,), (0,)))
    low = lanes_at((sub, 128), 1) < 64
    for s_r in range(plan.nr):
        for s_f in range(plan.nf):
            dest, c = s_r * plan.nf + s_f, s_r * plan.slice_width + s_f * sub
            first, half = s_r * plan.slice_width + s_f // 2 * 2 * sub, s_f % 2
            for k in range(chunks // 2):
                at = (half * chunks // 2 + k) * 128
                out_ref[dest, k * local : (k + 1) * local, :] = g_ref[:, at : at + 128]
            upper, lower = halves[half][first : first + sub], halves[1 - half][first + sub : first + 2 * sub]
            out_ref[dest, plan.acts_at : plan.packed_at, :] = jnp.where(low, upper, lower)
            for at, found in ((plan.packed_at, packed_acts), (plan.cot_at, packed_cot)):
                rows_of = sum(found[c + 8 * k : c + 8 * k + 8, k * 128 : (k + 1) * 128] for k in range(4))
                out_ref[dest, at : at + 8, :] = rows_of.astype(jnp.bfloat16)
    for copy in copies[3:7]:
        copy.wait()
    first = r * plan.slice_width + 2 * pair * sub
    for k in range(2):
        columns[k, 0:sub, :] = jnp.broadcast_to(own_column(rows[k], base, sub), (sub, 128))
        columns[2 + k] = jnp.broadcast_to(own_column(rows[2 + k], first, 2 * sub), (2 * sub, 128))
    for copy in copies[7:]:
        copy.wait()


def by_frame_device(plan, got_ref, at, height):
    return jnp.concatenate(
        [
            jnp.concatenate(
                [got_ref[r * plan.nf + f, at : at + height, :] for r in range(plan.nr)], axis=1
            )
            for f in range(plan.nf)
        ],
        axis=0,
    )


def in_places(plan, merged, height):
    width = plan.tl * plan.image
    return [
        jnp.concatenate(
            [merged[f * height : (f + 1) * height, k * width : (k + 1) * width] for f in range(plan.nf)],
            axis=1,
        )
        for k in range(4)
    ]


def frame_sum(products_ref, taps, sub, lane, places, image):
    near, middle, far = [products_ref[pl.ds(tap * sub, sub), :] for tap in reversed(taps)]
    return near + moved(middle, image, lane < places - image) + moved(far, 2 * image, lane < places - 2 * image)


def coarse_kernel(
    plan,
    got_ref,
    weights,
    columns,
    order,
    fine_order,
    mine_ref,
    sent_ref,
    held_ref,
    inv_ref,
    fine_ref,
    source,
    products,
    conv_ref,
):
    sub, nr, nf, cells, tl, local = plan.sub, plan.nr, plan.nf, plan.cells, plan.tl, plan.local
    wide, depth = 2 * sub, plan.channels // 2
    _, member, _, _ = own_place(plan)
    for s_f in range(nf):
        for s_r in range(nr):
            for t in range(tl):
                at = (s_f * tl + t) * plan.image + s_r * cells
                for k in range(plan.chunks // 2):
                    source[at : at + cells, k * 128 : (k + 1) * 128] = got_ref[
                        s_r * nf + s_f, k * local + t * cells : k * local + (t + 1) * cells, :
                    ]
    source[plan.places :, :] = jnp.zeros((2 * plan.image, depth), jnp.bfloat16)
    products[...] = sum(
        one_hot_dot(
            weights[9 * k : 9 * k + 9].reshape(9 * wide, depth),
            source[(2 - k) * plan.image : (2 - k) * plan.image + plan.places, :],
            ((1,), (1,)),
        )
        for k in range(3)
    )
    merged = one_hot_dot(by_frame_device(plan, got_ref, plan.acts_at, sub), fine_order[...], ((1,), (0,)))
    parts = halves_at(plan, merged)
    for pq in range(4):
        fine_ref[pq] = parts[pq]
    one, two = total(parts), total([part * part for part in parts])
    stats = terms(as_row(one) + pltpu.roll(as_row(two), 64, 1), 3)
    stats = jnp.concatenate(stats + [jnp.zeros_like(stats[0])] * 5, axis=0).astype(jnp.bfloat16)
    found = []
    for at in (plan.packed_at, plan.cot_at):
        merged = one_hot_dot(by_frame_device(plan, got_ref, at, 8), order[...], ((1,), (0,)))
        found.append(jnp.concatenate(in_places(plan, merged, 8), axis=0))
    values, cot = found
    gain, bias = columns[0][0:sub, 0:1], columns[1][0:sub, 0:1]
    entries = plan.places * plan.group_width
    mean, inv_std = statistics(total([values]), total([values * values]), entries, plan.group_width)
    (normed,), (slope,) = normalised([values], gain, bias, mean, inv_std)
    held_ref[0], held_ref[1], held_ref[2] = normed, slope, cot
    inv_ref[...] = jnp.broadcast_to(inv_std, (sub, 128))
    lane, has_left, has_right, has_up, has_down = plan.place_masks(plan.w)
    by_col = []
    for col in range(3):
        parts = [products[pl.ds((3 * row + col) * wide, wide), :] for row in range(3)]
        by_col.append(parts[1] + moved(parts[0], plan.w, has_down) + moved(parts[2], -plan.w, has_up))
    conv_ref[...] = by_col[1] + moved(by_col[0], 1, has_right) + moved(by_col[2], -1, has_left)
    mine_ref[...] = conv_ref[pl.ds(pl.multiple_of(member * sub, sub), sub), :]
    theirs = conv_ref[pl.ds(pl.multiple_of((1 - member) * sub, sub), sub), :]
    sent_ref[0:sub, :] = theirs.astype(jnp.bfloat16)
    sent_ref[sub:, 0:128] = stats
    sent_ref[sub:, 128:] = jnp.zeros((8, plan.places - 128), jnp.bfloat16)


def quarter_kernel(plan, mine_ref, both_ref, held_ref, inv_ref, columns, by_column, out_ref, sums_ref):
    sub = plan.sub
    _, member, _, _ = own_place(plan)
    conv = mine_ref[...] + both_ref[1 - member, 0:sub, :].astype(jnp.float32)
    normed, slope, cot = held_ref[0], held_ref[1], held_ref[2]
    gain, inv_std = columns[0][0:sub, 0:1], inv_ref[:, 0:1]
    entries = plan.places * plan.group_width
    pre = conv * slope
    one, two = total([pre]), total([pre * normed])
    group_one = in_groups(gain * one, plan.group_width) / entries
    group_two = in_groups(gain * two, plan.group_width) / entries
    grad = cot + inv_std * (gain * pre - group_one - normed * group_two)
    quartered = (grad * 0.25).astype(jnp.bfloat16)
    sent = one_hot_dot(quartered, by_column[...], ((1,), (0,))).astype(jnp.bfloat16)
    low = lanes_at((sub // 2, 128), 1) < 64
    for half in range(2):
        at = half * 256
        border = sent[:, 512 + half * 128 : 640 + half * 128]
        border = jnp.where(low, border[: sub // 2], border[sub // 2 :])
        for dest in range(half, plan.count, 2):
            out_ref[dest, 0:sub, :] = sent[:, at : at + 128]
            out_ref[dest, sub : 2 * sub, :] = sent[:, at + 128 : at + 256]
            out_ref[dest, 2 * sub : 2 * sub + sub // 2, :] = border
    sums_ref[...] = jnp.concatenate([as_row(one), as_row(two)], axis=0)


def halves_at(plan, merged):
    sub = plan.sub
    turned = jnp.concatenate([pltpu.roll(merged[:, k * 128 : (k + 1) * 128], 64, 1) for k in range(4)], axis=1)
    low = lanes_at((sub, 128), 1) < 64
    parts = []
    for pq in range(4):
        groups = []
        for group in range(2):
            e = 4 * group + pq
            at = e // 2 * 128
            strips = []
            for m in range(plan.nf // 2):
                first, second = slice(2 * m * sub, (2 * m + 1) * sub), slice((2 * m + 1) * sub, (2 * m + 2) * sub)
                if e % 2 == 0:
                    strips.append(jnp.where(low, merged[first, at : at + 128], turned[second, at : at + 128]))
                else:
                    strips.append(jnp.where(low, turned[first, at : at + 128], merged[second, at : at + 128]))
            groups.append(jnp.concatenate(strips, axis=1))
        parts.append(jnp.concatenate(groups, axis=0))
    return parts


def halves_from(plan, parts):
    sub = plan.sub
    low = lanes_at((sub, 128), 1) < 64
    down = []
    for f in range(plan.nf):
        across = []
        for v in range(4):
            pair = []
            for e in (2 * v, 2 * v + 1):
                group, pq = e // 4, e % 4
                strip = parts[pq][group * sub : (group + 1) * sub, f // 2 * 128 : (f // 2 + 1) * 128]
                pair.append(strip if e % 2 == f % 2 else pltpu.roll(strip, 64, 1))
            across.append(jnp.where(low, pair[0], pair[1]))
        down.append(jnp.concatenate(across, axis=1))
    return jnp.concatenate(down, axis=0)


def fine_kernel(
    plan, got_ref, acts_ref, both_ref, columns, order, sums_ref, weights, out_ref, source, border, products, beyond
):
    sub, nr, nf, wide = plan.sub, plan.nr, plan.nf, 2 * plan.sub
    pair, member, r, _ = own_place(plan)
    w = plan.w // 2
    lines = plan.places // plan.w
    places = lines * w
    for k in range(2):
        source[:, k * 128 : (k + 1) * 128] = got_ref[:, k * sub : (k + 1) * sub, :].reshape(plan.channels, 128)
    products[...] = one_hot_dot(weights[...].reshape(27 * wide, plan.channels), source[...], ((1,), (0,)))
    packed = got_ref[:, wide : wide + sub // 2, :].reshape(plan.count * sub // 2, 128)
    shape = (128, places)
    beside = lanes_at(shape, 1) == lanes_at(shape, 0) % lines * w + (1 - member) * (w - 1)
    for k in range(2):
        here = one_hot(beside & (lanes_at(shape, 0) // lines == k))
        found = one_hot_dot(packed, here, ((1,), (0,))).astype(jnp.bfloat16)
        for s in range(plan.count):
            border[s * sub + k * (sub // 2) : s * sub + (k + 1) * (sub // 2), :] = found[
                s * (sub // 2) : (s + 1) * (sub // 2)
            ]
    facing = jnp.concatenate([weights[3 * k + 2 * member] for k in range(9)], axis=0)
    beyond[...] = one_hot_dot(facing, border[...], ((1,), (0,)))
    parts = [acts_ref[pq] for pq in range(4)]
    stats = sum(both_ref[k, sub : sub + 8, 0:128].astype(jnp.float32) for k in range(2))
    stats = stats[0:1] + stats[1:2] + stats[2:3]
    entries = 4 * plan.places * plan.group_width
    one, two = own_column(stats, 0, wide), own_column(stats, 64, wide)
    mean, inv_std = statistics(one, two, entries, plan.group_width)
    gain, bias = columns[2][:, 0:1], columns[3][:, 0:1]
    normed, slope = normalised(parts, gain, bias, mean, inv_std)
    lane, has_left, has_right, has_up, has_down = plan.place_masks(w)
    image = plan.image // 2
    right, left = (1 - member).astype(jnp.float32), member.astype(jnp.float32)
    by_row = []
    for row in range(3):
        a, b, c = [
            frame_sum(products, [9 * depth + 3 * row + col for depth in range(3)], wide, lane, places, image)
            for col in range(3)
        ]
        extra = frame_sum(beyond, [3 * depth + row for depth in range(3)], wide, lane, places, image)
        by_row.append(
            (a + b + moved(c, -1, has_left) + left * extra, moved(a, 1, has_right) + b + c + right * extra)
        )
    convs = [by_row[0][q] + by_row[1][q] + moved(by_row[2][q], -w, has_up) for q in range(2)]
    convs += [moved(by_row[0][q], w, has_down) + by_row[1][q] + by_row[2][q] for q in range(2)]
    pre = [conv * part for conv, part in zip(convs, slope)]
    one = total(pre)
    two = total([a * b for a, b in zip(pre, normed)])
    cot = source[pl.ds(pl.multiple_of(r * plan.slice_width + pair * wide, wide), wide), :].astype(jnp.float32)
    scale = inv_std * gain
    stacked = halves_from(plan, [cot + scale * part for part in pre]).astype(jnp.bfloat16)
    sent = one_hot_dot(stacked, order[...], ((1,), (1,))).astype(jnp.bfloat16)
    coarse = sums_ref[0:1] + pltpu.roll(sums_ref[1:2], sub, 1)
    coded = (
        terms(as_row(one) + pltpu.roll(as_row(two), 64, 1), 2)
        + terms(coarse, 2)
        + terms(as_row(inv_std) + pltpu.roll(as_row(mean), 64, 1), 3)
    )
    coded = jnp.concatenate(coded + [jnp.zeros_like(coarse)], axis=0).astype(jnp.bfloat16)
    for s_r in range(nr):
        for s_f in range(nf):
            out_ref[s_r * nf + s_f, 0:sub, :] = sent[s_f * sub : (s_f + 1) * sub, s_r * 128 : (s_r + 1) * 128]
            out_ref[s_r * nf + s_f, sub : sub + 8, :] = coded


def spread_kernel(plan, got_ref, acts_ref, rows_ref, out_ref, sums_ref):
    sub, nr, nf = plan.sub, plan.nr, plan.nf
    low = lanes_at((sub, 128), 1) < 64
    low_row = lanes_at((1, 128), 1) < 64
    first_row = lanes_at((1, 128), 1) < sub
    source = []
    fine, coarse, moments = [[], []], [[], []], [[], []]
    for s_r in range(nr):
        ones, twos, c_ones, c_twos, invs, means = [], [], 0.0, 0.0, [], []
        for pair in range(nf // 2):
            at = s_r * nf + 2 * pair
            left, right = [got_ref[at + k, 0:sub, :].astype(jnp.float32) for k in range(2)]
            source.append(jnp.where(low, left, pltpu.roll(right, 64, 1)))
            source.append(jnp.where(low, pltpu.roll(left, 64, 1), right))
            coded = [got_ref[at + k, sub : sub + 8, :].astype(jnp.float32) for k in range(2)]
            sums = coded[0][0:1] + coded[0][1:2] + coded[1][0:1] + coded[1][1:2]
            ones.append(sums if pair == 0 else pltpu.roll(sums, 64, 1))
            twos.append(pltpu.roll(sums, 64, 1) if pair == 0 else sums)
            both = coded[0][4:5] + coded[0][5:6] + coded[0][6:7]
            invs.append(both if pair == 0 else pltpu.roll(both, 64, 1))
            means.append(pltpu.roll(both, 64, 1) if pair == 0 else both)
            for k in range(2):
                sums = coded[k][2:3] + coded[k][3:4]
                to = (2 * pair + k) * sub
                c_one = jnp.where(first_row, sums, 0.0)
                c_two = jnp.where(first_row, pltpu.roll(sums, 128 - sub, 1), 0.0)
                c_ones = c_ones + (pltpu.roll(c_one, to, 1) if to else c_one)
                c_twos = c_twos + (pltpu.roll(c_two, to, 1) if to else c_two)
        fine[0].append(jnp.where(low_row, ones[0], ones[1]))
        fine[1].append(jnp.where(low_row, twos[0], twos[1]))
        moments[0].append(jnp.where(low_row, invs[0], invs[1]))
        moments[1].append(jnp.where(low_row, means[0], means[1]))
        coarse[0].append(c_ones)
        coarse[1].append(c_twos)
    one, two, inv_std, mean, c_one, c_two = [jnp.concatenate(part, axis=1) for part in fine + moments + coarse]
    source = jnp.concatenate(source, axis=0).astype(jnp.bfloat16)
    result = one_hot_dot(pixel_order(plan, False), source, ((1,), (1,)))
    gain = rows_ref[2]
    entries = 4 * plan.places * plan.group_width
    group_one = in_lane_groups(gain * one, plan.group_width) / entries
    group_two = in_lane_groups(gain * two, plan.group_width) / entries
    normed = (acts_ref[...].astype(jnp.float32) - mean) * inv_std
    out_ref[...] = (result - inv_std * (group_one + normed * group_two)).astype(jnp.bfloat16)
    sums_ref[...] = jnp.concatenate([one, two, c_one, c_two] + [jnp.zeros_like(one)] * 4, axis=0)


def total_kernel(scales, both_ref, result_ref, result_hbm, out_hbms, rows_ref, sems):
    copies = fetched([(result_ref, result_hbm)], sems)
    rows = sum(both_ref[k] for k in range(both_ref.shape[0]))
    for k in range(4):
        rows_ref[k] = rows[k : k + 1] * scales[k]
    for k in range(4):
        copies.append(pltpu.make_async_copy(rows_ref.at[k], out_hbms[k], sems.at[k + 1]))
        copies[-1].start()
    for copy in copies:
        copy.wait()


def in_vmem(count):
    return [pl.BlockSpec(memory_space=pltpu.VMEM)] * count


def in_hbm(count):
    return [pl.BlockSpec(memory_space=pltpu.HBM)] * count


def kept(array):
    return pltpu.with_memory_space_constraint(array, pltpu.HBM)


def shape_of(shape, kind):
    return jax.ShapeDtypeStruct(shape, kind)


LIMIT = pltpu.CompilerParams(vmem_limit_bytes=40 * 1024 * 1024)


def fast_shards(
    plan,
    acts_fine,
    acts_coarse,
    grad_coarse,
    gain_fine,
    bias_fine,
    kernel_fine,
    gain_coarse,
    bias_coarse,
    kernel_coarse,
):
    nd = lax.axis_size("dp")
    count, sub, channels, places, local = plan.count, plan.sub, plan.channels, plan.places, plan.local
    f32, bf16 = jnp.float32, jnp.bfloat16
    rows = [part.reshape(1, channels) for part in (gain_coarse, bias_coarse, gain_fine, bias_fine)]
    packed, acts, weights_c, weights_f, columns, order, fine_order, by_column, rows = pl.pallas_call(
        functools.partial(pack_kernel, plan),
        out_shape=(
            shape_of((count, plan.block_rows, 128), bf16),
            shape_of((4 * local, channels), bf16),
            shape_of((27, 2 * sub, channels // 2), bf16),
            shape_of((27, 2 * sub, channels), bf16),
            shape_of((4, 2 * sub, 128), f32),
            shape_of((4 * plan.nr * local, 4 * plan.nr * local), bf16),
            shape_of((4 * plan.nr * local, 4 * plan.nr * local), bf16),
            shape_of((places, places + places // 2), bf16),
            shape_of((4, 1, channels), f32),
        ),
        in_specs=in_hbm(9),
        out_specs=tuple(in_vmem(9)),
        scratch_shapes=[
            pltpu.VMEM((local, channels), bf16),
            pltpu.VMEM((local, channels), bf16),
            pltpu.SemaphoreType.DMA((9,)),
        ],
        compiler_params=LIMIT,
    )(
        kept(grad_coarse.reshape(local, channels)),
        kept(acts_coarse.reshape(local, channels)),
        kept(acts_fine.reshape(4 * local, channels)),
        kept(kernel_coarse),
        kept(kernel_fine),
        *[kept(row) for row in rows],
    )
    got = lax.all_to_all(packed, BLOCK, 0, 0)
    mine, theirs, held, inv_std, fine_acts = pl.pallas_call(
        functools.partial(coarse_kernel, plan),
        out_shape=(
            shape_of((sub, places), f32),
            shape_of((sub + 8, places), bf16),
            shape_of((3, sub, places), f32),
            shape_of((sub, 128), f32),
            shape_of((4, 2 * sub, places // 2), f32),
        ),
        in_specs=in_vmem(5),
        out_specs=tuple(in_vmem(5)),
        scratch_shapes=[
            pltpu.VMEM((places + 2 * plan.image, channels // 2), bf16),
            pltpu.VMEM((18 * sub, places), f32),
            pltpu.VMEM((2 * sub, places), f32),
        ],
        compiler_params=LIMIT,
    )(got, weights_c, columns, order, fine_order)
    both = lax.all_gather(theirs, "member")
    quartered, coarse_sums = pl.pallas_call(
        functools.partial(quarter_kernel, plan),
        out_shape=(shape_of((count, 2 * sub + sub // 2, 128), bf16), shape_of((2, 128), f32)),
        in_specs=in_vmem(6),
        out_specs=tuple(in_vmem(2)),
        compiler_params=LIMIT,
    )(mine, both, held, inv_std, columns, by_column)
    spread = lax.all_to_all(quartered, BLOCK, 0, 0)
    sent = pl.pallas_call(
        functools.partial(fine_kernel, plan),
        out_shape=shape_of((count, sub + 8, 128), bf16),
        in_specs=in_vmem(7),
        out_specs=in_vmem(1)[0],
        scratch_shapes=[
            pltpu.VMEM((channels, places // 2), bf16),
            pltpu.VMEM((channels, places // 2), bf16),
            pltpu.VMEM((54 * sub, places // 2), f32),
            pltpu.VMEM((18 * sub, places // 2), f32),
        ],
        compiler_params=LIMIT,
    )(spread, fine_acts, both, columns, fine_order, coarse_sums, weights_f)
    back = lax.all_to_all(sent, BLOCK, 0, 0)
    cells = nd * places
    fine_scale, coarse_scale = 1.0 / math.sqrt(4 * cells), 1.0 / math.sqrt(cells)
    out, sums = pl.pallas_call(
        functools.partial(spread_kernel, plan),
        out_shape=(pltpu.VMEM((4 * local, channels), bf16), shape_of((8, channels), f32)),
        in_specs=in_vmem(3),
        out_specs=tuple(in_vmem(2)),
        compiler_params=LIMIT,
    )(back, acts, rows)
    both = lax.all_gather(sums, "dp")
    out, sums = pl.pallas_call(
        functools.partial(total_kernel, (fine_scale, fine_scale, coarse_scale, coarse_scale)),
        out_shape=(pltpu.HBM((4 * local, channels), bf16), (pltpu.HBM((1, channels), f32),) * 4),
        in_specs=in_vmem(2),
        out_specs=(in_hbm(1)[0], tuple(in_hbm(4))),
        scratch_shapes=[pltpu.VMEM((4, 1, channels), f32), pltpu.SemaphoreType.DMA((5,))],
        compiler_params=LIMIT,
    )(both, out)
    bias_f, gain_f, bias_c, gain_c = [part.reshape(channels) for part in sums]
    return out.reshape(acts_fine.shape), gain_f, bias_f, gain_c, bias_c


def solution(mesh):
    def function(*arrays):
        local = [size // mesh.shape[axis] for size, axis in zip(arrays[1].shape, ("dp", "frames", "rows"))]
        sizes = (mesh.shape["frames"], mesh.shape["rows"])
        plan = Plan(sizes, (*local[1:], *arrays[1].shape[3:]), arrays[5].shape[1] // mesh.shape["rows"])
        if plan.fits:
            split = (mesh.shape["dp"], plan.nf // 2, 2, plan.nr)
            used = jax.sharding.Mesh(mesh.devices.reshape(split), ("dp", "pairs", "member", "rows"))
            shards, frames = functools.partial(fast_shards, plan), ("pairs", "member")
        else:
            used, shards, frames = mesh, plain_shards, "frames"
        blocks, kernel = P("dp", frames, "rows", None, None), P(None, "rows", None)
        in_specs = (blocks, blocks, blocks, P(), P(), kernel, P(), P(), kernel)
        out_specs = (blocks, P(), P(), P(), P())
        mapped = jax.shard_map(shards, mesh=used, in_specs=in_specs, out_specs=out_specs, check_vma=False)
        return mapped(*arrays)

    return function
```

```python
import functools
import math

import jax
import jax.numpy as jnp
from jax import lax
from jax.experimental import pallas as pl
from jax.experimental.pallas import tpu as pltpu
from jax.sharding import PartitionSpec as P

GROUPS = 32
EPSILON = 1e-06
BLOCK = ("rows", "pairs", "member")
PLAIN_BLOCK = ("frames", "rows")


def plain_everyone(block, count):
    copies = jnp.broadcast_to(block[None], (count,) + block.shape)
    return lax.all_to_all(copies, PLAIN_BLOCK, 0, 0)


def ahead(field, axis, distance):
    size = field.shape[axis]
    if distance == 0:
        return field
    widths = [(0, 0)] * field.ndim
    if distance > 0:
        widths[axis] = (0, distance)
        kept = lax.slice_in_dim(field, distance, size, axis=axis)
    else:
        widths[axis] = (-distance, 0)
        kept = lax.slice_in_dim(field, 0, size + distance, axis=axis)
    return jnp.pad(kept, widths)


def tap_products(source, kernel):
    sub = kernel.shape[1]
    frames, rows, cols, channels = source.shape
    products = lax.dot_general(
        kernel.reshape(27 * sub, channels),
        source.reshape(frames * rows * cols, channels),
        (((1,), (1,)), ((), ())),
        preferred_element_type=jnp.float32,
    ).reshape(3, 3, 3, sub, frames, rows, cols)
    return sum(ahead(products[depth], 3, 2 - depth) for depth in range(3))


def coarse_conv(source, kernel):
    spatial = tap_products(source, kernel)
    total = 0.0
    for row in range(3):
        part = sum(ahead(spatial[row, col], 3, 1 - col) for col in range(3))
        total = total + ahead(part, 2, 1 - row)
    return total


def fine_conv(source, kernel):
    spatial = tap_products(source, kernel)
    result = []
    for p in range(2):
        rows_of = []
        for q in range(2):
            total = 0.0
            for row in range(3):
                part = sum(ahead(spatial[row, col], 3, (q + 1 - col) // 2) for col in range(3))
                total = total + ahead(part, 2, (p + 1 - row) // 2)
            rows_of.append(total)
        result.append(jnp.stack(rows_of, 1))
    return jnp.stack(result, 1)


def group_total(sums, group_width):
    sub = sums.shape[-1]
    if sub % group_width == 0:
        grouped = jnp.sum(sums.reshape(-1, sub // group_width, group_width), axis=-1)
        return jnp.repeat(grouped, group_width, axis=-1)
    spread = jnp.moveaxis(lax.all_gather(sums, "frames"), 0, 1).reshape(sums.shape[0], -1, group_width)
    mine = lax.axis_index("frames") * sub // group_width
    grouped = lax.dynamic_index_in_dim(jnp.sum(spread, -1), mine, 1)
    return jnp.broadcast_to(grouped, sums.shape)


def level(acts, conv_grad, cotangent, gain, bias, group_width):
    sub = acts.shape[0]
    places = acts.size // sub
    values = acts.astype(jnp.float32).reshape(sub, places)
    conv_grad = conv_grad.reshape(sub, places)
    entries = places * group_width
    moments = group_total(
        jnp.stack([jnp.sum(values, 1), jnp.sum(values * values, 1)]), group_width
    ) / entries
    mean = moments[0]
    inv_std = lax.rsqrt(moments[1] - mean * mean + EPSILON)
    normed = (values - mean[:, None]) * inv_std[:, None]
    preact = gain[:, None] * normed + bias[:, None]
    squash = jax.nn.sigmoid(preact)
    pre_grad = conv_grad * squash * (1.0 + preact * (1.0 - squash))
    sums = jnp.stack([jnp.sum(pre_grad, 1), jnp.sum(pre_grad * normed, 1)])
    terms = group_total(sums * gain, group_width) / entries
    grad = cotangent.reshape(sub, places) + inv_std[:, None] * (
        gain[:, None] * pre_grad - terms[0][:, None] - normed * terms[1][:, None]
    )
    return grad, sums


def plain_shards(
    acts_fine,
    acts_coarse,
    grad_coarse,
    gain_fine,
    bias_fine,
    kernel_fine,
    gain_coarse,
    bias_coarse,
    kernel_coarse,
):
    nf, nr, nd = lax.axis_size("frames"), lax.axis_size("rows"), lax.axis_size("dp")
    count = nf * nr
    channels = acts_fine.shape[-1]
    slice_width = kernel_fine.shape[1]
    sub = slice_width // nf
    group_width = channels // GROUPS
    tl, hl, w = acts_coarse.shape[1:4]
    frames, rows = tl * nf, hl * nr
    f, r = lax.axis_index("frames"), lax.axis_index("rows")

    gathered = plain_everyone(grad_coarse[0], count)
    source = (
        gathered.reshape(nf, nr, tl, hl, w, channels)
        .transpose(0, 2, 1, 3, 4, 5)
        .reshape(frames, rows, w, channels)
    )
    coarse_in = acts_coarse[0].reshape(tl, hl, w, nr, nf, sub).transpose(4, 3, 5, 0, 1, 2)
    coarse_in = lax.all_to_all(coarse_in.reshape(count, sub, tl * hl * w), PLAIN_BLOCK, 0, 0)
    fine_in = acts_fine[0].reshape(tl, hl, 2, w, 2, nr, nf, sub).transpose(6, 5, 7, 2, 4, 0, 1, 3)
    fine_in = lax.all_to_all(fine_in.reshape(count, sub, 4 * tl * hl * w), PLAIN_BLOCK, 0, 0)

    def mine(vector):
        return lax.dynamic_slice_in_dim(vector, r * slice_width + f * sub, sub)

    def own(kernel):
        return lax.dynamic_slice_in_dim(kernel, f * sub, sub, axis=1)

    coarse_vals = (
        coarse_in.reshape(nf, nr, sub, tl, hl, w).transpose(2, 0, 3, 1, 4, 5).reshape(sub, frames, rows, w)
    )
    cot = lax.dynamic_slice_in_dim(source, r * slice_width + f * sub, sub, axis=3)
    cot = cot.astype(jnp.float32).transpose(3, 0, 1, 2)
    conv = coarse_conv(source, own(kernel_coarse))
    coarse_grad, coarse_sums = level(
        coarse_vals, conv, cot, mine(gain_coarse), mine(bias_coarse), group_width
    )
    quartered = (coarse_grad * 0.25).astype(jnp.bfloat16)
    spread = plain_everyone(quartered, count)
    source_fine = (
        spread.reshape(nf, nr, sub, frames, rows, w)
        .transpose(3, 4, 5, 1, 0, 2)
        .reshape(frames, rows, w, channels)
    )
    conv = fine_conv(source_fine, own(kernel_fine))
    fine_vals = (
        fine_in.reshape(nf, nr, sub, 2, 2, tl, hl, w)
        .transpose(2, 3, 4, 0, 5, 1, 6, 7)
        .reshape(sub, 2, 2, frames, rows, w)
    )
    cot = jnp.broadcast_to(
        quartered.astype(jnp.float32).reshape(sub, 1, 1, frames, rows, w), conv.shape
    )
    fine_grad, fine_sums = level(
        fine_vals, conv, cot, mine(gain_fine), mine(bias_fine), group_width
    )
    back = (
        fine_grad.astype(jnp.bfloat16)
        .reshape(sub, 2, 2, nf, tl, nr, hl, w)
        .transpose(3, 5, 0, 1, 2, 4, 6, 7)
        .reshape(count, sub, 4 * tl * hl * w)
    )
    sums = plain_everyone(jnp.concatenate([fine_sums, coarse_sums]), count)
    back = lax.all_to_all(back, PLAIN_BLOCK, 0, 0)
    out = (
        back.reshape(nf, nr, sub, 2, 2, tl, hl, w)
        .transpose(5, 6, 3, 7, 4, 1, 0, 2)
        .reshape(1, tl, 2 * hl, 2 * w, channels)
    )
    sums = sums.reshape(nf, nr, 4, sub).transpose(2, 1, 0, 3).reshape(4, channels)
    totals = lax.psum(sums, "dp")
    cells = nd * frames * rows * w
    scale_fine = 1.0 / jnp.sqrt(jnp.float32(4 * cells))
    scale_coarse = 1.0 / jnp.sqrt(jnp.float32(cells))
    return (
        out,
        totals[1] * scale_fine,
        totals[0] * scale_fine,
        totals[3] * scale_coarse,
        totals[2] * scale_coarse,
    )


def lanes_at(shape, axis):
    return lax.broadcasted_iota(jnp.int32, shape, axis)


def one_hot(found):
    return found.astype(jnp.float32).astype(jnp.bfloat16)


def pixel_order(plan, swapped):
    tl, hl, w = plan.tl, plan.hl, plan.w // 2
    size = 4 * plan.local
    lane = lanes_at((1, size), 1)
    j, i, t = lane % w, lane // w % hl, lane // (w * hl) % tl
    q, p = lane // (w * hl * tl) % 2, lane // (2 * w * hl * tl) % 2
    half = lane // (4 * w * hl * tl)
    if swapped:
        half = 1 - half
    pixel = (t * 2 * hl + 2 * i + p) * 4 * w + 2 * (half * w + j) + q
    return one_hot(lanes_at((size, size), 0) == pixel)


def merged_order(nr, outer, tl, cells):
    size = nr * outer * tl * cells
    lane = lanes_at((1, size), 1)
    cell, dev = lane % cells, lane // cells % nr
    t, o = lane // (cells * nr) % tl, lane // (cells * nr * tl)
    return one_hot(lanes_at((size, size), 0) == ((dev * outer + o) * tl + t) * cells + cell)


def column_order(plan):
    w = plan.w // 2
    lines = plan.places // plan.w
    lane = lanes_at((1, 4 * lines * w + 4 * lines), 1)
    inner = lane % (lines * w)
    place = inner // w * plan.w + lane // (lines * w) * w + inner % w
    past = lane - 2 * lines * w
    border = past % lines * plan.w + jnp.where(past < 2 * lines, w, w - 1)
    wanted = jnp.where(past >= 0, border, place)
    shape = (plan.places, 2 * lines * w + 4 * lines)
    return one_hot(lanes_at(shape, 0) == wanted[:, : shape[1]])


def one_hot_dot(a, b, dims):
    return lax.dot_general(a, b, (dims, ((), ())), preferred_element_type=jnp.float32)


def moved(field, distance, kept):
    size = field.shape[1]
    return jnp.where(kept, pltpu.roll(field, (-distance) % size, 1), 0.0)


def own_column(row, base, sub):
    shape = (sub, row.shape[1])
    mine = lanes_at(shape, 1) == lanes_at(shape, 0) + base
    return jnp.sum(jnp.where(mine, row, 0.0), axis=1, keepdims=True)


def as_row(column):
    shape = (column.shape[0], 128)
    here = lanes_at(shape, 1) == lanes_at(shape, 0)
    return jnp.sum(jnp.where(here, column, 0.0), axis=0, keepdims=True)


def terms(value, count):
    found = []
    for _ in range(count):
        found.append(value.astype(jnp.bfloat16).astype(jnp.float32))
        value = value - found[-1]
    return found


def in_groups(column, group_width):
    sub = column.shape[0]
    grouped = jnp.sum(column.reshape(sub // group_width, group_width, 1), axis=1, keepdims=True)
    return jnp.broadcast_to(grouped, (sub // group_width, group_width, 1)).reshape(sub, 1)


def in_lane_groups(row, group_width):
    lane = lanes_at(row.shape, 1)
    size = row.shape[1]
    step = 1
    while step < group_width:
        up, down = pltpu.roll(row, size - step, 1), pltpu.roll(row, step, 1)
        row = row + jnp.where(lane // step % 2 == 0, up, down)
        step *= 2
    return row


def total(parts):
    return sum(jnp.sum(part, axis=1, keepdims=True) for part in parts)


def statistics(one, two, entries, group_width):
    mean = in_groups(one, group_width) / entries
    square = in_groups(two, group_width) / entries
    return mean, lax.rsqrt(square - mean * mean + EPSILON)


def normalised(parts, gain, bias, mean, inv_std):
    normed, slope = [], []
    for part in parts:
        unit = (part - mean) * inv_std
        preact = gain * unit + bias
        squash = jax.nn.sigmoid(preact)
        normed.append(unit)
        slope.append(squash * (1.0 + preact * (1.0 - squash)))
    return normed, slope


class Plan:
    def __init__(self, mesh_sizes, acts_coarse, slice_width):
        self.nf, self.nr = mesh_sizes
        self.count = self.nf * self.nr
        self.tl, self.hl, self.w, self.channels = acts_coarse
        self.slice_width = slice_width
        self.sub = slice_width // self.nf
        self.cells = self.hl * self.w
        self.local = self.tl * self.cells
        self.image = self.cells * self.nr
        self.frames = self.tl * self.nf
        self.places = self.frames * self.image
        self.group_width = self.channels // GROUPS
        self.chunks = self.channels // 128
        self.acts_at = self.chunks // 2 * self.local
        self.packed_at = self.acts_at + self.sub
        self.cot_at = self.packed_at + 8
        self.block_rows = self.cot_at + 8
        self.fits = (
            self.sub == 32
            and self.slice_width == 128
            and self.group_width == 16
            and self.cells == 16
            and self.w == 8
            and self.tl == 2
            and self.nr == 4
            and self.nf == 4
            and self.slice_width * self.nr == self.channels
        )

    def place_masks(self, w):
        lane = lanes_at((1, self.places // self.w * w), 1)
        col, row = lane % w, lane // w % (self.hl * self.nr)
        last_row = self.hl * self.nr - 1
        return (lane, col > 0, col < w - 1, row > 0, row < last_row)


def fetched(pairs, sems):
    copies = [pltpu.make_async_copy(src, dst, sems.at[k]) for k, (src, dst) in enumerate(pairs)]
    for copy in copies:
        copy.start()
    return copies


def own_place(plan):
    pair, member, r = lax.axis_index("pairs"), lax.axis_index("member"), lax.axis_index("rows")
    return pair, member, r, r * plan.slice_width + (2 * pair + member) * plan.sub


def pack_kernel(
    plan,
    g_hbm,
    coarse_hbm,
    fine_hbm,
    kernel_c,
    kernel_f,
    gain_c,
    bias_c,
    gain_f,
    bias_f,
    out_ref,
    fine_ref,
    weights_c,
    weights_f,
    columns,
    order,
    fine_order,
    by_column,
    rows,
    g_ref,
    coarse_ref,
    sems,
):
    sub, chunks, local = plan.sub, plan.chunks, plan.local
    pair, member, r, base = own_place(plan)
    depth = plan.channels // 2
    half = pl.ds(pl.multiple_of(member * depth, depth), depth)
    both = pl.ds(pl.multiple_of(2 * pair * sub, 2 * sub), 2 * sub)
    copies = fetched(
        [(fine_hbm, fine_ref), (coarse_hbm, coarse_ref), (g_hbm, g_ref)]
        + [(row, rows.at[k]) for k, row in enumerate((gain_c, bias_c, gain_f, bias_f))]
        + [(kernel_c.at[:, both, half], weights_c), (kernel_f.at[:, both, :], weights_f)],
        sems,
    )
    order[...] = merged_order(plan.nr, 4, plan.tl, plan.cells)
    fine_order[...] = merged_order(plan.nr, 8, plan.tl, plan.cells // 2)
    by_column[...] = column_order(plan)
    shape = (2 * local, 2 * 128)
    lane = lanes_at((1, 2 * 128), 1)
    repeated = one_hot(lanes_at(shape, 0) == lane % local + lane // 128 * local)
    shape = (plan.channels, 128)
    quarter = lanes_at(shape, 0) // 8 % 4 == lanes_at(shape, 1) // local
    orders = jnp.concatenate([pixel_order(plan, swapped) for swapped in (False, True)], axis=1)
    copies[0].wait()
    acts = fine_ref[...]
    halves = one_hot_dot(acts, orders, ((0,), (0,))).astype(jnp.bfloat16)
    halves = [halves[:, :128], halves[:, 128:]]
    copies[1].wait()
    copies[2].wait()
    small = one_hot_dot(jnp.concatenate([coarse_ref[...], g_ref[...]], axis=0), repeated, ((0,), (0,)))
    for k, at in enumerate((plan.packed_at, plan.cot_at)):
        rows_of = jnp.where(quarter, small[:, k * 128 : (k + 1) * 128], 0.0).reshape(plan.count, 4, 8, 128)
        out_ref[:, at : at + 8, :] = jnp.sum(rows_of, axis=1).astype(jnp.bfloat16)
    low = lanes_at((sub, 128), 1) < 64
    for s_r in range(plan.nr):
        for s_f in range(plan.nf):
            dest = s_r * plan.nf + s_f
            first, half = s_r * plan.slice_width + s_f // 2 * 2 * sub, s_f % 2
            for k in range(chunks // 2):
                at = (half * chunks // 2 + k) * 128
                out_ref[dest, k * local : (k + 1) * local, :] = g_ref[:, at : at + 128]
            upper, lower = halves[half][first : first + sub], halves[1 - half][first + sub : first + 2 * sub]
            out_ref[dest, plan.acts_at : plan.packed_at, :] = jnp.where(low, upper, lower)
    for copy in copies[3:7]:
        copy.wait()
    first = r * plan.slice_width + 2 * pair * sub
    for k in range(2):
        columns[k, 0:sub, :] = jnp.broadcast_to(own_column(rows[k], base, sub), (sub, 128))
        columns[2 + k] = jnp.broadcast_to(own_column(rows[2 + k], first, 2 * sub), (2 * sub, 128))
    for copy in copies[7:]:
        copy.wait()


def by_frame_device(plan, got_ref, at, height):
    return jnp.concatenate(
        [
            jnp.concatenate(
                [got_ref[r * plan.nf + f, at : at + height, :] for r in range(plan.nr)], axis=1
            )
            for f in range(plan.nf)
        ],
        axis=0,
    )


def in_places(plan, merged, height):
    width = plan.tl * plan.image
    return [
        jnp.concatenate(
            [merged[f * height : (f + 1) * height, k * width : (k + 1) * width] for f in range(plan.nf)],
            axis=1,
        )
        for k in range(4)
    ]


def coarse_kernel(
    plan,
    got_ref,
    weights,
    columns,
    order,
    fine_order,
    mine_ref,
    sent_ref,
    held_ref,
    inv_ref,
    fine_ref,
    source,
    products,
    conv_ref,
):
    sub, nr, nf, cells, tl, local = plan.sub, plan.nr, plan.nf, plan.cells, plan.tl, plan.local
    wide, depth = 2 * sub, plan.channels // 2
    _, member, _, _ = own_place(plan)
    for s_f in range(nf):
        for s_r in range(nr):
            for t in range(tl):
                at = (s_f * tl + t) * plan.image + s_r * cells
                for k in range(plan.chunks // 2):
                    source[at : at + cells, k * 128 : (k + 1) * 128] = got_ref[
                        s_r * nf + s_f, k * local + t * cells : k * local + (t + 1) * cells, :
                    ]
    source[plan.places :, :] = jnp.zeros((2 * plan.image, depth), jnp.bfloat16)
    products[...] = sum(
        one_hot_dot(
            weights[9 * k : 9 * k + 9].reshape(9 * wide, depth),
            source[(2 - k) * plan.image : (2 - k) * plan.image + plan.places, :],
            ((1,), (1,)),
        )
        for k in range(3)
    )
    merged = one_hot_dot(by_frame_device(plan, got_ref, plan.acts_at, sub), fine_order[...], ((1,), (0,)))
    parts = halves_at(plan, merged)
    for pq in range(4):
        fine_ref[pq] = parts[pq]
    one, two = total(parts), total([part * part for part in parts])
    stats = terms(as_row(one) + pltpu.roll(as_row(two), 64, 1), 3)
    stats = jnp.concatenate(stats + [jnp.zeros_like(stats[0])] * 5, axis=0).astype(jnp.bfloat16)
    found = []
    for at in (plan.packed_at, plan.cot_at):
        merged = one_hot_dot(by_frame_device(plan, got_ref, at, 8), order[...], ((1,), (0,)))
        found.append(jnp.concatenate(in_places(plan, merged, 8), axis=0))
    values, cot = found
    gain, bias = columns[0][0:sub, 0:1], columns[1][0:sub, 0:1]
    entries = plan.places * plan.group_width
    mean, inv_std = statistics(total([values]), total([values * values]), entries, plan.group_width)
    (normed,), (slope,) = normalised([values], gain, bias, mean, inv_std)
    held_ref[0], held_ref[1], held_ref[2] = normed, slope, cot
    inv_ref[...] = jnp.broadcast_to(inv_std, (sub, 128))
    lane, has_left, has_right, has_up, has_down = plan.place_masks(plan.w)
    by_col = []
    for col in range(3):
        parts = [products[pl.ds((3 * row + col) * wide, wide), :] for row in range(3)]
        by_col.append(parts[1] + moved(parts[0], plan.w, has_down) + moved(parts[2], -plan.w, has_up))
    conv_ref[...] = by_col[1] + moved(by_col[0], 1, has_right) + moved(by_col[2], -1, has_left)
    mine_ref[...] = conv_ref[pl.ds(pl.multiple_of(member * sub, sub), sub), :]
    theirs = conv_ref[pl.ds(pl.multiple_of((1 - member) * sub, sub), sub), :]
    sent_ref[0:sub, :] = theirs.astype(jnp.bfloat16)
    sent_ref[sub:, 0:128] = stats
    sent_ref[sub:, 128:] = jnp.zeros((8, plan.places - 128), jnp.bfloat16)


def quarter_kernel(plan, mine_ref, both_ref, held_ref, inv_ref, columns, by_column, out_ref, sums_ref):
    sub = plan.sub
    _, member, _, _ = own_place(plan)
    conv = mine_ref[...] + both_ref[1 - member, 0:sub, :].astype(jnp.float32)
    normed, slope, cot = held_ref[0], held_ref[1], held_ref[2]
    gain, inv_std = columns[0][0:sub, 0:1], inv_ref[:, 0:1]
    entries = plan.places * plan.group_width
    pre = conv * slope
    one, two = total([pre]), total([pre * normed])
    group_one = in_groups(gain * one, plan.group_width) / entries
    group_two = in_groups(gain * two, plan.group_width) / entries
    grad = cot + inv_std * (gain * pre - group_one - normed * group_two)
    quartered = (grad * 0.25).astype(jnp.bfloat16)
    sent = one_hot_dot(quartered, by_column[...], ((1,), (0,))).astype(jnp.bfloat16)
    low = lanes_at((sub // 2, 128), 1) < 64
    for half in range(2):
        at = half * 256
        border = sent[:, 512 + half * 128 : 640 + half * 128]
        border = jnp.where(low, border[: sub // 2], border[sub // 2 :])
        for dest in range(half, plan.count, 2):
            out_ref[dest, 0:sub, :] = sent[:, at : at + 128]
            out_ref[dest, sub : 2 * sub, :] = sent[:, at + 128 : at + 256]
            out_ref[dest, 2 * sub : 2 * sub + sub // 2, :] = border
    sums_ref[...] = jnp.concatenate([as_row(one), as_row(two)], axis=0)


def halves_at(plan, merged):
    sub = plan.sub
    turned = jnp.concatenate([pltpu.roll(merged[:, k * 128 : (k + 1) * 128], 64, 1) for k in range(4)], axis=1)
    low = lanes_at((sub, 128), 1) < 64
    parts = []
    for pq in range(4):
        groups = []
        for group in range(2):
            e = 4 * group + pq
            at = e // 2 * 128
            strips = []
            for m in range(plan.nf // 2):
                first, second = slice(2 * m * sub, (2 * m + 1) * sub), slice((2 * m + 1) * sub, (2 * m + 2) * sub)
                if e % 2 == 0:
                    strips.append(jnp.where(low, merged[first, at : at + 128], turned[second, at : at + 128]))
                else:
                    strips.append(jnp.where(low, turned[first, at : at + 128], merged[second, at : at + 128]))
            groups.append(jnp.concatenate(strips, axis=1))
        parts.append(jnp.concatenate(groups, axis=0))
    return parts


def halves_from(plan, parts):
    sub = plan.sub
    low = lanes_at((sub, 128), 1) < 64
    down = []
    for f in range(plan.nf):
        across = []
        for v in range(4):
            pair = []
            for e in (2 * v, 2 * v + 1):
                group, pq = e // 4, e % 4
                strip = parts[pq][group * sub : (group + 1) * sub, f // 2 * 128 : (f // 2 + 1) * 128]
                pair.append(strip if e % 2 == f % 2 else pltpu.roll(strip, 64, 1))
            across.append(jnp.where(low, pair[0], pair[1]))
        down.append(jnp.concatenate(across, axis=1))
    return jnp.concatenate(down, axis=0)


def fine_kernel(
    plan, got_ref, acts_ref, both_ref, columns, order, sums_ref, weights, out_ref, source, border, products, beyond
):
    sub, nr, nf, wide = plan.sub, plan.nr, plan.nf, 2 * plan.sub
    pair, member, r, _ = own_place(plan)
    w = plan.w // 2
    lines = plan.places // plan.w
    places = lines * w
    for k in range(2):
        source[:, k * 128 : (k + 1) * 128] = got_ref[:, k * sub : (k + 1) * sub, :].reshape(plan.channels, 128)
    packed = got_ref[:, wide : wide + sub // 2, :].reshape(plan.count * sub // 2, 128)
    shape = (128, places)
    beside = lanes_at(shape, 1) == lanes_at(shape, 0) % lines * w + (1 - member) * (w - 1)
    for k in range(2):
        here = one_hot(beside & (lanes_at(shape, 0) // lines == k))
        found = one_hot_dot(packed, here, ((1,), (0,))).astype(jnp.bfloat16)
        for s in range(plan.count):
            border[s * sub + k * (sub // 2) : s * sub + (k + 1) * (sub // 2), :] = found[
                s * (sub // 2) : (s + 1) * (sub // 2)
            ]
    image = plan.image // 2
    sums, extras = 0.0, 0.0
    for k in (2, 1, 0):
        here, beside = source[...], border[...]
        if k < 2:
            shift = (2 - k) * image
            inside = lanes_at((1, places), 1) < places - shift
            here, beside = [
                jnp.where(inside, pltpu.roll(part, places - shift, 1), jnp.zeros_like(part)) for part in (here, beside)
            ]
        sums = sums + one_hot_dot(
            weights[9 * k : 9 * k + 9].reshape(9 * wide, plan.channels), here, ((1,), (0,))
        )
        facing = jnp.concatenate([weights[9 * k + 3 * row + 2 * member] for row in range(3)], axis=0)
        extras = extras + one_hot_dot(facing, beside, ((1,), (0,)))
    products[...], beyond[...] = sums, extras
    parts = [acts_ref[pq] for pq in range(4)]
    stats = sum(both_ref[k, sub : sub + 8, 0:128].astype(jnp.float32) for k in range(2))
    stats = stats[0:1] + stats[1:2] + stats[2:3]
    entries = 4 * plan.places * plan.group_width
    one, two = own_column(stats, 0, wide), own_column(stats, 64, wide)
    mean, inv_std = statistics(one, two, entries, plan.group_width)
    gain, bias = columns[2][:, 0:1], columns[3][:, 0:1]
    normed, slope = normalised(parts, gain, bias, mean, inv_std)
    lane, has_left, has_right, has_up, has_down = plan.place_masks(w)
    right, left = (1 - member).astype(jnp.float32), member.astype(jnp.float32)
    by_row = []
    for row in range(3):
        a, b, c = [products[pl.ds((3 * row + col) * wide, wide), :] for col in range(3)]
        extra = beyond[pl.ds(row * wide, wide), :]
        by_row.append(
            (a + b + moved(c, -1, has_left) + left * extra, moved(a, 1, has_right) + b + c + right * extra)
        )
    convs = [by_row[0][q] + by_row[1][q] + moved(by_row[2][q], -w, has_up) for q in range(2)]
    convs += [moved(by_row[0][q], w, has_down) + by_row[1][q] + by_row[2][q] for q in range(2)]
    pre = [conv * part for conv, part in zip(convs, slope)]
    one = total(pre)
    two = total([a * b for a, b in zip(pre, normed)])
    cot = source[pl.ds(pl.multiple_of(r * plan.slice_width + pair * wide, wide), wide), :].astype(jnp.float32)
    scale = inv_std * gain
    stacked = halves_from(plan, [cot + scale * part for part in pre]).astype(jnp.bfloat16)
    sent = one_hot_dot(stacked, order[...], ((1,), (1,))).astype(jnp.bfloat16)
    coarse = sums_ref[0:1] + pltpu.roll(sums_ref[1:2], sub, 1)
    coded = (
        terms(as_row(one) + pltpu.roll(as_row(two), 64, 1), 2)
        + terms(coarse, 2)
        + terms(as_row(inv_std) + pltpu.roll(as_row(mean), 64, 1), 3)
    )
    coded = jnp.concatenate(coded + [jnp.zeros_like(coarse)], axis=0).astype(jnp.bfloat16)
    for s_r in range(nr):
        for s_f in range(nf):
            out_ref[s_r * nf + s_f, 0:sub, :] = sent[s_f * sub : (s_f + 1) * sub, s_r * 128 : (s_r + 1) * 128]
            out_ref[s_r * nf + s_f, sub : sub + 8, :] = coded


def spread_kernel(plan, got_ref, acts_ref, rows_ref, out_ref, sums_ref):
    sub, nr, nf = plan.sub, plan.nr, plan.nf
    low = lanes_at((sub, 128), 1) < 64
    low_row = lanes_at((1, 128), 1) < 64
    first_row = lanes_at((1, 128), 1) < sub
    source = []
    fine, coarse, moments = [[], []], [[], []], [[], []]
    for s_r in range(nr):
        ones, twos, c_ones, c_twos, invs, means = [], [], 0.0, 0.0, [], []
        for pair in range(nf // 2):
            at = s_r * nf + 2 * pair
            left, right = [got_ref[at + k, 0:sub, :].astype(jnp.float32) for k in range(2)]
            source.append(jnp.where(low, left, pltpu.roll(right, 64, 1)))
            source.append(jnp.where(low, pltpu.roll(left, 64, 1), right))
            coded = [got_ref[at + k, sub : sub + 8, :].astype(jnp.float32) for k in range(2)]
            sums = coded[0][0:1] + coded[0][1:2] + coded[1][0:1] + coded[1][1:2]
            ones.append(sums if pair == 0 else pltpu.roll(sums, 64, 1))
            twos.append(pltpu.roll(sums, 64, 1) if pair == 0 else sums)
            both = coded[0][4:5] + coded[0][5:6] + coded[0][6:7]
            invs.append(both if pair == 0 else pltpu.roll(both, 64, 1))
            means.append(pltpu.roll(both, 64, 1) if pair == 0 else both)
            for k in range(2):
                sums = coded[k][2:3] + coded[k][3:4]
                to = (2 * pair + k) * sub
                c_one = jnp.where(first_row, sums, 0.0)
                c_two = jnp.where(first_row, pltpu.roll(sums, 128 - sub, 1), 0.0)
                c_ones = c_ones + (pltpu.roll(c_one, to, 1) if to else c_one)
                c_twos = c_twos + (pltpu.roll(c_two, to, 1) if to else c_two)
        fine[0].append(jnp.where(low_row, ones[0], ones[1]))
        fine[1].append(jnp.where(low_row, twos[0], twos[1]))
        moments[0].append(jnp.where(low_row, invs[0], invs[1]))
        moments[1].append(jnp.where(low_row, means[0], means[1]))
        coarse[0].append(c_ones)
        coarse[1].append(c_twos)
    one, two, inv_std, mean, c_one, c_two = [jnp.concatenate(part, axis=1) for part in fine + moments + coarse]
    source = jnp.concatenate(source, axis=0).astype(jnp.bfloat16)
    result = one_hot_dot(pixel_order(plan, False), source, ((1,), (1,)))
    gain = rows_ref[2]
    entries = 4 * plan.places * plan.group_width
    group_one = in_lane_groups(gain * one, plan.group_width) / entries
    group_two = in_lane_groups(gain * two, plan.group_width) / entries
    normed = (acts_ref[...].astype(jnp.float32) - mean) * inv_std
    out_ref[...] = (result - inv_std * (group_one + normed * group_two)).astype(jnp.bfloat16)
    sums_ref[...] = jnp.concatenate([one, two, c_one, c_two] + [jnp.zeros_like(one)] * 4, axis=0)


def total_kernel(scales, both_ref, result_ref, result_hbm, out_hbms, rows_ref, sems):
    copies = fetched([(result_ref, result_hbm)], sems)
    rows = sum(both_ref[k] for k in range(both_ref.shape[0]))
    for k in range(4):
        rows_ref[k] = rows[k : k + 1] * scales[k]
    for k in range(4):
        copies.append(pltpu.make_async_copy(rows_ref.at[k], out_hbms[k], sems.at[k + 1]))
        copies[-1].start()
    for copy in copies:
        copy.wait()


def in_vmem(count):
    return [pl.BlockSpec(memory_space=pltpu.VMEM)] * count


def in_hbm(count):
    return [pl.BlockSpec(memory_space=pltpu.HBM)] * count


def kept(array):
    return pltpu.with_memory_space_constraint(array, pltpu.HBM)


def shape_of(shape, kind):
    return jax.ShapeDtypeStruct(shape, kind)


LIMIT = pltpu.CompilerParams(vmem_limit_bytes=40 * 1024 * 1024)


def fast_shards(
    plan,
    acts_fine,
    acts_coarse,
    grad_coarse,
    gain_fine,
    bias_fine,
    kernel_fine,
    gain_coarse,
    bias_coarse,
    kernel_coarse,
):
    nd = lax.axis_size("dp")
    count, sub, channels, places, local = plan.count, plan.sub, plan.channels, plan.places, plan.local
    f32, bf16 = jnp.float32, jnp.bfloat16
    rows = [part.reshape(1, channels) for part in (gain_coarse, bias_coarse, gain_fine, bias_fine)]
    packed, acts, weights_c, weights_f, columns, order, fine_order, by_column, rows = pl.pallas_call(
        functools.partial(pack_kernel, plan),
        out_shape=(
            shape_of((count, plan.block_rows, 128), bf16),
            shape_of((4 * local, channels), bf16),
            shape_of((27, 2 * sub, channels // 2), bf16),
            shape_of((27, 2 * sub, channels), bf16),
            shape_of((4, 2 * sub, 128), f32),
            shape_of((4 * plan.nr * local, 4 * plan.nr * local), bf16),
            shape_of((4 * plan.nr * local, 4 * plan.nr * local), bf16),
            shape_of((places, places + places // 2), bf16),
            shape_of((4, 1, channels), f32),
        ),
        in_specs=in_hbm(9),
        out_specs=tuple(in_vmem(9)),
        scratch_shapes=[
            pltpu.VMEM((local, channels), bf16),
            pltpu.VMEM((local, channels), bf16),
            pltpu.SemaphoreType.DMA((9,)),
        ],
        compiler_params=LIMIT,
    )(
        kept(grad_coarse.reshape(local, channels)),
        kept(acts_coarse.reshape(local, channels)),
        kept(acts_fine.reshape(4 * local, channels)),
        kept(kernel_coarse),
        kept(kernel_fine),
        *[kept(row) for row in rows],
    )
    got = lax.all_to_all(packed, BLOCK, 0, 0)
    mine, theirs, held, inv_std, fine_acts = pl.pallas_call(
        functools.partial(coarse_kernel, plan),
        out_shape=(
            shape_of((sub, places), f32),
            shape_of((sub + 8, places), bf16),
            shape_of((3, sub, places), f32),
            shape_of((sub, 128), f32),
            shape_of((4, 2 * sub, places // 2), f32),
        ),
        in_specs=in_vmem(5),
        out_specs=tuple(in_vmem(5)),
        scratch_shapes=[
            pltpu.VMEM((places + 2 * plan.image, channels // 2), bf16),
            pltpu.VMEM((18 * sub, places), f32),
            pltpu.VMEM((2 * sub, places), f32),
        ],
        compiler_params=LIMIT,
    )(got, weights_c, columns, order, fine_order)
    both = lax.all_gather(theirs, "member")
    quartered, coarse_sums = pl.pallas_call(
        functools.partial(quarter_kernel, plan),
        out_shape=(shape_of((count, 2 * sub + sub // 2, 128), bf16), shape_of((2, 128), f32)),
        in_specs=in_vmem(6),
        out_specs=tuple(in_vmem(2)),
        compiler_params=LIMIT,
    )(mine, both, held, inv_std, columns, by_column)
    spread = lax.all_to_all(quartered, BLOCK, 0, 0)
    sent = pl.pallas_call(
        functools.partial(fine_kernel, plan),
        out_shape=shape_of((count, sub + 8, 128), bf16),
        in_specs=in_vmem(7),
        out_specs=in_vmem(1)[0],
        scratch_shapes=[
            pltpu.VMEM((channels, places // 2), bf16),
            pltpu.VMEM((channels, places // 2), bf16),
            pltpu.VMEM((18 * sub, places // 2), f32),
            pltpu.VMEM((6 * sub, places // 2), f32),
        ],
        compiler_params=LIMIT,
    )(spread, fine_acts, both, columns, fine_order, coarse_sums, weights_f)
    back = lax.all_to_all(sent, BLOCK, 0, 0)
    cells = nd * places
    fine_scale, coarse_scale = 1.0 / math.sqrt(4 * cells), 1.0 / math.sqrt(cells)
    out, sums = pl.pallas_call(
        functools.partial(spread_kernel, plan),
        out_shape=(pltpu.VMEM((4 * local, channels), bf16), shape_of((8, channels), f32)),
        in_specs=in_vmem(3),
        out_specs=tuple(in_vmem(2)),
        compiler_params=LIMIT,
    )(back, acts, rows)
    both = lax.all_gather(sums, "dp")
    out, sums = pl.pallas_call(
        functools.partial(total_kernel, (fine_scale, fine_scale, coarse_scale, coarse_scale)),
        out_shape=(pltpu.HBM((4 * local, channels), bf16), (pltpu.HBM((1, channels), f32),) * 4),
        in_specs=in_vmem(2),
        out_specs=(in_hbm(1)[0], tuple(in_hbm(4))),
        scratch_shapes=[pltpu.VMEM((4, 1, channels), f32), pltpu.SemaphoreType.DMA((5,))],
        compiler_params=LIMIT,
    )(both, out)
    bias_f, gain_f, bias_c, gain_c = [part.reshape(channels) for part in sums]
    return out.reshape(acts_fine.shape), gain_f, bias_f, gain_c, bias_c


def solution(mesh):
    def function(*arrays):
        local = [size // mesh.shape[axis] for size, axis in zip(arrays[1].shape, ("dp", "frames", "rows"))]
        sizes = (mesh.shape["frames"], mesh.shape["rows"])
        plan = Plan(sizes, (*local[1:], *arrays[1].shape[3:]), arrays[5].shape[1] // mesh.shape["rows"])
        if plan.fits:
            split = (mesh.shape["dp"], plan.nf // 2, 2, plan.nr)
            used = jax.sharding.Mesh(mesh.devices.reshape(split), ("dp", "pairs", "member", "rows"))
            shards, frames = functools.partial(fast_shards, plan), ("pairs", "member")
        else:
            used, shards, frames = mesh, plain_shards, "frames"
        blocks, kernel = P("dp", frames, "rows", None, None), P(None, "rows", None)
        in_specs = (blocks, blocks, blocks, P(), P(), kernel, P(), P(), kernel)
        out_specs = (blocks, P(), P(), P(), P())
        mapped = jax.shard_map(shards, mesh=used, in_specs=in_specs, out_specs=out_specs, check_vma=False)
        return mapped(*arrays)

    return function
```

```python
import functools
import math

import jax
import jax.numpy as jnp
from jax import lax
from jax.experimental import pallas as pl
from jax.experimental.pallas import tpu as pltpu
from jax.sharding import PartitionSpec as P

GROUPS = 32
EPSILON = 1e-06
BLOCK = ("rows", "pairs", "member")
PLAIN_BLOCK = ("frames", "rows")


def plain_everyone(block, count):
    copies = jnp.broadcast_to(block[None], (count,) + block.shape)
    return lax.all_to_all(copies, PLAIN_BLOCK, 0, 0)


def ahead(field, axis, distance):
    size = field.shape[axis]
    if distance == 0:
        return field
    widths = [(0, 0)] * field.ndim
    if distance > 0:
        widths[axis] = (0, distance)
        kept = lax.slice_in_dim(field, distance, size, axis=axis)
    else:
        widths[axis] = (-distance, 0)
        kept = lax.slice_in_dim(field, 0, size + distance, axis=axis)
    return jnp.pad(kept, widths)


def tap_products(source, kernel):
    sub = kernel.shape[1]
    frames, rows, cols, channels = source.shape
    products = lax.dot_general(
        kernel.reshape(27 * sub, channels),
        source.reshape(frames * rows * cols, channels),
        (((1,), (1,)), ((), ())),
        preferred_element_type=jnp.float32,
    ).reshape(3, 3, 3, sub, frames, rows, cols)
    return sum(ahead(products[depth], 3, 2 - depth) for depth in range(3))


def coarse_conv(source, kernel):
    spatial = tap_products(source, kernel)
    total = 0.0
    for row in range(3):
        part = sum(ahead(spatial[row, col], 3, 1 - col) for col in range(3))
        total = total + ahead(part, 2, 1 - row)
    return total


def fine_conv(source, kernel):
    spatial = tap_products(source, kernel)
    result = []
    for p in range(2):
        rows_of = []
        for q in range(2):
            total = 0.0
            for row in range(3):
                part = sum(ahead(spatial[row, col], 3, (q + 1 - col) // 2) for col in range(3))
                total = total + ahead(part, 2, (p + 1 - row) // 2)
            rows_of.append(total)
        result.append(jnp.stack(rows_of, 1))
    return jnp.stack(result, 1)


def group_total(sums, group_width):
    sub = sums.shape[-1]
    if sub % group_width == 0:
        grouped = jnp.sum(sums.reshape(-1, sub // group_width, group_width), axis=-1)
        return jnp.repeat(grouped, group_width, axis=-1)
    spread = jnp.moveaxis(lax.all_gather(sums, "frames"), 0, 1).reshape(sums.shape[0], -1, group_width)
    mine = lax.axis_index("frames") * sub // group_width
    grouped = lax.dynamic_index_in_dim(jnp.sum(spread, -1), mine, 1)
    return jnp.broadcast_to(grouped, sums.shape)


def level(acts, conv_grad, cotangent, gain, bias, group_width):
    sub = acts.shape[0]
    places = acts.size // sub
    values = acts.astype(jnp.float32).reshape(sub, places)
    conv_grad = conv_grad.reshape(sub, places)
    entries = places * group_width
    moments = group_total(
        jnp.stack([jnp.sum(values, 1), jnp.sum(values * values, 1)]), group_width
    ) / entries
    mean = moments[0]
    inv_std = lax.rsqrt(moments[1] - mean * mean + EPSILON)
    normed = (values - mean[:, None]) * inv_std[:, None]
    preact = gain[:, None] * normed + bias[:, None]
    squash = jax.nn.sigmoid(preact)
    pre_grad = conv_grad * squash * (1.0 + preact * (1.0 - squash))
    sums = jnp.stack([jnp.sum(pre_grad, 1), jnp.sum(pre_grad * normed, 1)])
    terms = group_total(sums * gain, group_width) / entries
    grad = cotangent.reshape(sub, places) + inv_std[:, None] * (
        gain[:, None] * pre_grad - terms[0][:, None] - normed * terms[1][:, None]
    )
    return grad, sums


def plain_shards(
    acts_fine,
    acts_coarse,
    grad_coarse,
    gain_fine,
    bias_fine,
    kernel_fine,
    gain_coarse,
    bias_coarse,
    kernel_coarse,
):
    nf, nr, nd = lax.axis_size("frames"), lax.axis_size("rows"), lax.axis_size("dp")
    count = nf * nr
    channels = acts_fine.shape[-1]
    slice_width = kernel_fine.shape[1]
    sub = slice_width // nf
    group_width = channels // GROUPS
    tl, hl, w = acts_coarse.shape[1:4]
    frames, rows = tl * nf, hl * nr
    f, r = lax.axis_index("frames"), lax.axis_index("rows")

    gathered = plain_everyone(grad_coarse[0], count)
    source = (
        gathered.reshape(nf, nr, tl, hl, w, channels)
        .transpose(0, 2, 1, 3, 4, 5)
        .reshape(frames, rows, w, channels)
    )
    coarse_in = acts_coarse[0].reshape(tl, hl, w, nr, nf, sub).transpose(4, 3, 5, 0, 1, 2)
    coarse_in = lax.all_to_all(coarse_in.reshape(count, sub, tl * hl * w), PLAIN_BLOCK, 0, 0)
    fine_in = acts_fine[0].reshape(tl, hl, 2, w, 2, nr, nf, sub).transpose(6, 5, 7, 2, 4, 0, 1, 3)
    fine_in = lax.all_to_all(fine_in.reshape(count, sub, 4 * tl * hl * w), PLAIN_BLOCK, 0, 0)

    def mine(vector):
        return lax.dynamic_slice_in_dim(vector, r * slice_width + f * sub, sub)

    def own(kernel):
        return lax.dynamic_slice_in_dim(kernel, f * sub, sub, axis=1)

    coarse_vals = (
        coarse_in.reshape(nf, nr, sub, tl, hl, w).transpose(2, 0, 3, 1, 4, 5).reshape(sub, frames, rows, w)
    )
    cot = lax.dynamic_slice_in_dim(source, r * slice_width + f * sub, sub, axis=3)
    cot = cot.astype(jnp.float32).transpose(3, 0, 1, 2)
    conv = coarse_conv(source, own(kernel_coarse))
    coarse_grad, coarse_sums = level(
        coarse_vals, conv, cot, mine(gain_coarse), mine(bias_coarse), group_width
    )
    quartered = (coarse_grad * 0.25).astype(jnp.bfloat16)
    spread = plain_everyone(quartered, count)
    source_fine = (
        spread.reshape(nf, nr, sub, frames, rows, w)
        .transpose(3, 4, 5, 1, 0, 2)
        .reshape(frames, rows, w, channels)
    )
    conv = fine_conv(source_fine, own(kernel_fine))
    fine_vals = (
        fine_in.reshape(nf, nr, sub, 2, 2, tl, hl, w)
        .transpose(2, 3, 4, 0, 5, 1, 6, 7)
        .reshape(sub, 2, 2, frames, rows, w)
    )
    cot = jnp.broadcast_to(
        quartered.astype(jnp.float32).reshape(sub, 1, 1, frames, rows, w), conv.shape
    )
    fine_grad, fine_sums = level(
        fine_vals, conv, cot, mine(gain_fine), mine(bias_fine), group_width
    )
    back = (
        fine_grad.astype(jnp.bfloat16)
        .reshape(sub, 2, 2, nf, tl, nr, hl, w)
        .transpose(3, 5, 0, 1, 2, 4, 6, 7)
        .reshape(count, sub, 4 * tl * hl * w)
    )
    sums = plain_everyone(jnp.concatenate([fine_sums, coarse_sums]), count)
    back = lax.all_to_all(back, PLAIN_BLOCK, 0, 0)
    out = (
        back.reshape(nf, nr, sub, 2, 2, tl, hl, w)
        .transpose(5, 6, 3, 7, 4, 1, 0, 2)
        .reshape(1, tl, 2 * hl, 2 * w, channels)
    )
    sums = sums.reshape(nf, nr, 4, sub).transpose(2, 1, 0, 3).reshape(4, channels)
    totals = lax.psum(sums, "dp")
    cells = nd * frames * rows * w
    scale_fine = 1.0 / jnp.sqrt(jnp.float32(4 * cells))
    scale_coarse = 1.0 / jnp.sqrt(jnp.float32(cells))
    return (
        out,
        totals[1] * scale_fine,
        totals[0] * scale_fine,
        totals[3] * scale_coarse,
        totals[2] * scale_coarse,
    )


def lanes_at(shape, axis):
    return lax.broadcasted_iota(jnp.int32, shape, axis)


def one_hot(found):
    return found.astype(jnp.float32).astype(jnp.bfloat16)


def pixel_order(plan, swapped):
    tl, hl, w = plan.tl, plan.hl, plan.w // 2
    size = 4 * plan.local
    lane = lanes_at((1, size), 1)
    j, i, t = lane % w, lane // w % hl, lane // (w * hl) % tl
    q, p = lane // (w * hl * tl) % 2, lane // (2 * w * hl * tl) % 2
    half = lane // (4 * w * hl * tl)
    if swapped:
        half = 1 - half
    pixel = (t * 2 * hl + 2 * i + p) * 4 * w + 2 * (half * w + j) + q
    return one_hot(lanes_at((size, size), 0) == pixel)


def merged_order(nr, outer, tl, cells):
    size = nr * outer * tl * cells
    lane = lanes_at((1, size), 1)
    cell, dev = lane % cells, lane // cells % nr
    t, o = lane // (cells * nr) % tl, lane // (cells * nr * tl)
    return one_hot(lanes_at((size, size), 0) == ((dev * outer + o) * tl + t) * cells + cell)


def column_order(plan):
    w = plan.w // 2
    lines = plan.places // plan.w
    lane = lanes_at((1, 4 * lines * w + 4 * lines), 1)
    inner = lane % (lines * w)
    place = inner // w * plan.w + lane // (lines * w) * w + inner % w
    past = lane - 2 * lines * w
    border = past % lines * plan.w + jnp.where(past < 2 * lines, w, w - 1)
    wanted = jnp.where(past >= 0, border, place)
    shape = (plan.places, 2 * lines * w + 4 * lines)
    return one_hot(lanes_at(shape, 0) == wanted[:, : shape[1]])


def one_hot_dot(a, b, dims):
    return lax.dot_general(a, b, (dims, ((), ())), preferred_element_type=jnp.float32)


def moved(field, distance, kept):
    size = field.shape[1]
    return jnp.where(kept, pltpu.roll(field, (-distance) % size, 1), 0.0)


def own_column(row, base, sub):
    shape = (sub, row.shape[1])
    mine = lanes_at(shape, 1) == lanes_at(shape, 0) + base
    return jnp.sum(jnp.where(mine, row, 0.0), axis=1, keepdims=True)


def as_row(column):
    shape = (column.shape[0], 128)
    here = lanes_at(shape, 1) == lanes_at(shape, 0)
    return jnp.sum(jnp.where(here, column, 0.0), axis=0, keepdims=True)


def terms(value, count):
    found = []
    for _ in range(count):
        found.append(value.astype(jnp.bfloat16).astype(jnp.float32))
        value = value - found[-1]
    return found


def in_groups(column, group_width):
    sub = column.shape[0]
    grouped = jnp.sum(column.reshape(sub // group_width, group_width, 1), axis=1, keepdims=True)
    return jnp.broadcast_to(grouped, (sub // group_width, group_width, 1)).reshape(sub, 1)


def in_lane_groups(row, group_width):
    lane = lanes_at(row.shape, 1)
    size = row.shape[1]
    step = 1
    while step < group_width:
        up, down = pltpu.roll(row, size - step, 1), pltpu.roll(row, step, 1)
        row = row + jnp.where(lane // step % 2 == 0, up, down)
        step *= 2
    return row


def total(parts):
    return sum(jnp.sum(part, axis=1, keepdims=True) for part in parts)


def statistics(one, two, entries, group_width):
    mean = in_groups(one, group_width) / entries
    square = in_groups(two, group_width) / entries
    return mean, lax.rsqrt(square - mean * mean + EPSILON)


def normalised(parts, gain, bias, mean, inv_std):
    normed, slope = [], []
    for part in parts:
        unit = (part - mean) * inv_std
        preact = gain * unit + bias
        squash = jax.nn.sigmoid(preact)
        normed.append(unit)
        slope.append(squash * (1.0 + preact * (1.0 - squash)))
    return normed, slope


class Plan:
    def __init__(self, mesh_sizes, acts_coarse, slice_width):
        self.nf, self.nr = mesh_sizes
        self.count = self.nf * self.nr
        self.tl, self.hl, self.w, self.channels = acts_coarse
        self.slice_width = slice_width
        self.sub = slice_width // self.nf
        self.cells = self.hl * self.w
        self.local = self.tl * self.cells
        self.image = self.cells * self.nr
        self.frames = self.tl * self.nf
        self.places = self.frames * self.image
        self.group_width = self.channels // GROUPS
        self.chunks = self.channels // 128
        self.acts_at = self.chunks // 2 * self.local
        self.packed_at = self.acts_at + self.sub
        self.cot_at = self.packed_at + 8
        self.block_rows = self.cot_at + 8
        self.fits = (
            self.sub == 32
            and self.slice_width == 128
            and self.group_width == 16
            and self.cells == 16
            and self.w == 8
            and self.tl == 2
            and self.nr == 4
            and self.nf == 4
            and self.slice_width * self.nr == self.channels
        )

    def place_masks(self, w):
        lane = lanes_at((1, self.places // self.w * w), 1)
        col, row = lane % w, lane // w % (self.hl * self.nr)
        last_row = self.hl * self.nr - 1
        return (lane, col > 0, col < w - 1, row > 0, row < last_row)


def fetched(pairs, sems):
    copies = [pltpu.make_async_copy(src, dst, sems.at[k]) for k, (src, dst) in enumerate(pairs)]

    @pl.when(lax.axis_index("rows") >= 0)
    def _():
        for copy in copies:
            copy.start()

    return copies


def own_place(plan):
    pair, member, r = lax.axis_index("pairs"), lax.axis_index("member"), lax.axis_index("rows")
    return pair, member, r, r * plan.slice_width + (2 * pair + member) * plan.sub


def pack_kernel(
    plan,
    g_hbm,
    coarse_hbm,
    fine_hbm,
    kernel_c,
    kernel_f,
    gain_c,
    bias_c,
    gain_f,
    bias_f,
    out_ref,
    fine_ref,
    weights_c,
    weights_f,
    columns,
    order,
    fine_order,
    by_column,
    rows,
    g_ref,
    coarse_ref,
    sems,
):
    sub, chunks, local = plan.sub, plan.chunks, plan.local
    pair, member, r, base = own_place(plan)
    depth = plan.channels // 2
    half = pl.ds(pl.multiple_of(member * depth, depth), depth)
    both = pl.ds(pl.multiple_of(2 * pair * sub, 2 * sub), 2 * sub)
    copies = fetched(
        [(fine_hbm, fine_ref), (coarse_hbm, coarse_ref), (g_hbm, g_ref)]
        + [(row, rows.at[k]) for k, row in enumerate((gain_c, bias_c, gain_f, bias_f))]
        + [(kernel_c.at[:, both, half], weights_c), (kernel_f.at[pl.ds(18, 9), both, :], weights_f)],
        sems,
    )
    order[...] = merged_order(plan.nr, 4, plan.tl, plan.cells)
    fine_order[...] = merged_order(plan.nr, 8, plan.tl, plan.cells // 2)
    by_column[...] = column_order(plan)
    shape = (2 * local, 2 * 128)
    lane = lanes_at((1, 2 * 128), 1)
    repeated = one_hot(lanes_at(shape, 0) == lane % local + lane // 128 * local)
    shape = (plan.channels, 128)
    quarter = lanes_at(shape, 0) // 8 % 4 == lanes_at(shape, 1) // local
    orders = jnp.concatenate([pixel_order(plan, swapped) for swapped in (False, True)], axis=1)
    copies[0].wait()
    acts = fine_ref[...]
    halves = one_hot_dot(acts, orders, ((0,), (0,))).astype(jnp.bfloat16)
    halves = [halves[:, :128], halves[:, 128:]]
    copies[1].wait()
    copies[2].wait()
    small = one_hot_dot(jnp.concatenate([coarse_ref[...], g_ref[...]], axis=0), repeated, ((0,), (0,)))
    for k, at in enumerate((plan.packed_at, plan.cot_at)):
        rows_of = jnp.where(quarter, small[:, k * 128 : (k + 1) * 128], 0.0).reshape(plan.count, 4, 8, 128)
        out_ref[:, at : at + 8, :] = jnp.sum(rows_of, axis=1).astype(jnp.bfloat16)
    low = lanes_at((sub, 128), 1) < 64
    for s_r in range(plan.nr):
        for s_f in range(plan.nf):
            dest = s_r * plan.nf + s_f
            first, half = s_r * plan.slice_width + s_f // 2 * 2 * sub, s_f % 2
            for k in range(chunks // 2):
                at = (half * chunks // 2 + k) * 128
                out_ref[dest, k * local : (k + 1) * local, :] = g_ref[:, at : at + 128]
            upper, lower = halves[half][first : first + sub], halves[1 - half][first + sub : first + 2 * sub]
            out_ref[dest, plan.acts_at : plan.packed_at, :] = jnp.where(low, upper, lower)
    for copy in copies[3:7]:
        copy.wait()
    first = r * plan.slice_width + 2 * pair * sub
    for k in range(2):
        columns[k, 0:sub, :] = jnp.broadcast_to(own_column(rows[k], base, sub), (sub, 128))
        columns[2 + k] = jnp.broadcast_to(own_column(rows[2 + k], first, 2 * sub), (2 * sub, 128))
    for copy in copies[7:]:
        copy.wait()


def by_frame_device(plan, got_ref, at, height):
    return jnp.concatenate(
        [
            jnp.concatenate(
                [got_ref[r * plan.nf + f, at : at + height, :] for r in range(plan.nr)], axis=1
            )
            for f in range(plan.nf)
        ],
        axis=0,
    )


def in_places(plan, merged, height):
    width = plan.tl * plan.image
    return [
        jnp.concatenate(
            [merged[f * height : (f + 1) * height, k * width : (k + 1) * width] for f in range(plan.nf)],
            axis=1,
        )
        for k in range(4)
    ]


def coarse_kernel(
    plan,
    got_ref,
    weights,
    columns,
    order,
    fine_order,
    kernel_f,
    mine_ref,
    sent_ref,
    held_ref,
    inv_ref,
    fine_ref,
    weights_f,
    source,
    products,
    conv_ref,
    sems,
):
    sub, nr, nf, cells, tl, local = plan.sub, plan.nr, plan.nf, plan.cells, plan.tl, plan.local
    wide, depth = 2 * sub, plan.channels // 2
    pair, member, _, _ = own_place(plan)
    both = pl.ds(pl.multiple_of(pair * wide, wide), wide)
    copies = fetched([(kernel_f.at[pl.ds(0, 18), both, :], weights_f)], sems)
    for s_f in range(nf):
        for s_r in range(nr):
            for t in range(tl):
                at = (s_f * tl + t) * plan.image + s_r * cells
                for k in range(plan.chunks // 2):
                    source[at : at + cells, k * 128 : (k + 1) * 128] = got_ref[
                        s_r * nf + s_f, k * local + t * cells : k * local + (t + 1) * cells, :
                    ]
    source[plan.places :, :] = jnp.zeros((2 * plan.image, depth), jnp.bfloat16)
    products[...] = sum(
        one_hot_dot(
            weights[9 * k : 9 * k + 9].reshape(9 * wide, depth),
            source[(2 - k) * plan.image : (2 - k) * plan.image + plan.places, :],
            ((1,), (1,)),
        )
        for k in range(3)
    )
    merged = one_hot_dot(by_frame_device(plan, got_ref, plan.acts_at, sub), fine_order[...], ((1,), (0,)))
    parts = halves_at(plan, merged)
    for pq in range(4):
        fine_ref[pq] = parts[pq]
    one, two = total(parts), total([part * part for part in parts])
    stats = terms(as_row(one) + pltpu.roll(as_row(two), 64, 1), 3)
    stats = jnp.concatenate(stats + [jnp.zeros_like(stats[0])] * 5, axis=0).astype(jnp.bfloat16)
    found = []
    for at in (plan.packed_at, plan.cot_at):
        merged = one_hot_dot(by_frame_device(plan, got_ref, at, 8), order[...], ((1,), (0,)))
        found.append(jnp.concatenate(in_places(plan, merged, 8), axis=0))
    values, cot = found
    gain, bias = columns[0][0:sub, 0:1], columns[1][0:sub, 0:1]
    entries = plan.places * plan.group_width
    mean, inv_std = statistics(total([values]), total([values * values]), entries, plan.group_width)
    (normed,), (slope,) = normalised([values], gain, bias, mean, inv_std)
    held_ref[0], held_ref[1], held_ref[2] = normed, slope, cot
    inv_ref[...] = jnp.broadcast_to(inv_std, (sub, 128))
    lane, has_left, has_right, has_up, has_down = plan.place_masks(plan.w)
    by_col = []
    for col in range(3):
        parts = [products[pl.ds((3 * row + col) * wide, wide), :] for row in range(3)]
        by_col.append(parts[1] + moved(parts[0], plan.w, has_down) + moved(parts[2], -plan.w, has_up))
    conv_ref[...] = by_col[1] + moved(by_col[0], 1, has_right) + moved(by_col[2], -1, has_left)
    mine_ref[...] = conv_ref[pl.ds(pl.multiple_of(member * sub, sub), sub), :]
    theirs = conv_ref[pl.ds(pl.multiple_of((1 - member) * sub, sub), sub), :]
    sent_ref[0:sub, :] = theirs.astype(jnp.bfloat16)
    sent_ref[sub:, 0:128] = stats
    sent_ref[sub:, 128:] = jnp.zeros((8, plan.places - 128), jnp.bfloat16)
    for copy in copies:
        copy.wait()


def quarter_kernel(plan, mine_ref, both_ref, held_ref, inv_ref, columns, by_column, out_ref, sums_ref):
    sub = plan.sub
    _, member, _, _ = own_place(plan)
    conv = mine_ref[...] + both_ref[1 - member, 0:sub, :].astype(jnp.float32)
    normed, slope, cot = held_ref[0], held_ref[1], held_ref[2]
    gain, inv_std = columns[0][0:sub, 0:1], inv_ref[:, 0:1]
    entries = plan.places * plan.group_width
    pre = conv * slope
    one, two = total([pre]), total([pre * normed])
    group_one = in_groups(gain * one, plan.group_width) / entries
    group_two = in_groups(gain * two, plan.group_width) / entries
    grad = cot + inv_std * (gain * pre - group_one - normed * group_two)
    quartered = (grad * 0.25).astype(jnp.bfloat16)
    sent = one_hot_dot(quartered, by_column[...], ((1,), (0,))).astype(jnp.bfloat16)
    low = lanes_at((sub // 2, 128), 1) < 64
    for half in range(2):
        at = half * 256
        border = sent[:, 512 + half * 128 : 640 + half * 128]
        border = jnp.where(low, border[: sub // 2], border[sub // 2 :])
        for dest in range(half, plan.count, 2):
            out_ref[dest, 0:sub, :] = sent[:, at : at + 128]
            out_ref[dest, sub : 2 * sub, :] = sent[:, at + 128 : at + 256]
            out_ref[dest, 2 * sub : 2 * sub + sub // 2, :] = border
    sums_ref[...] = jnp.concatenate([as_row(one), as_row(two)], axis=0)


def halves_at(plan, merged):
    sub = plan.sub
    turned = jnp.concatenate([pltpu.roll(merged[:, k * 128 : (k + 1) * 128], 64, 1) for k in range(4)], axis=1)
    low = lanes_at((sub, 128), 1) < 64
    parts = []
    for pq in range(4):
        groups = []
        for group in range(2):
            e = 4 * group + pq
            at = e // 2 * 128
            strips = []
            for m in range(plan.nf // 2):
                first, second = slice(2 * m * sub, (2 * m + 1) * sub), slice((2 * m + 1) * sub, (2 * m + 2) * sub)
                if e % 2 == 0:
                    strips.append(jnp.where(low, merged[first, at : at + 128], turned[second, at : at + 128]))
                else:
                    strips.append(jnp.where(low, turned[first, at : at + 128], merged[second, at : at + 128]))
            groups.append(jnp.concatenate(strips, axis=1))
        parts.append(jnp.concatenate(groups, axis=0))
    return parts


def halves_from(plan, parts):
    sub = plan.sub
    low = lanes_at((sub, 128), 1) < 64
    down = []
    for f in range(plan.nf):
        across = []
        for v in range(4):
            pair = []
            for e in (2 * v, 2 * v + 1):
                group, pq = e // 4, e % 4
                strip = parts[pq][group * sub : (group + 1) * sub, f // 2 * 128 : (f // 2 + 1) * 128]
                pair.append(strip if e % 2 == f % 2 else pltpu.roll(strip, 64, 1))
            across.append(jnp.where(low, pair[0], pair[1]))
        down.append(jnp.concatenate(across, axis=1))
    return jnp.concatenate(down, axis=0)


def fine_kernel(
    plan, got_ref, acts_ref, both_ref, columns, order, sums_ref, late, early, out_ref, source, border, products, beyond
):
    sub, nr, nf, wide = plan.sub, plan.nr, plan.nf, 2 * plan.sub
    pair, member, r, _ = own_place(plan)
    w = plan.w // 2
    lines = plan.places // plan.w
    places = lines * w
    for k in range(2):
        source[:, k * 128 : (k + 1) * 128] = got_ref[:, k * sub : (k + 1) * sub, :].reshape(plan.channels, 128)
    packed = got_ref[:, wide : wide + sub // 2, :].reshape(plan.count * sub // 2, 128)
    shape = (128, places)
    beside = lanes_at(shape, 1) == lanes_at(shape, 0) % lines * w + (1 - member) * (w - 1)
    for k in range(2):
        here = one_hot(beside & (lanes_at(shape, 0) // lines == k))
        found = one_hot_dot(packed, here, ((1,), (0,))).astype(jnp.bfloat16)
        for s in range(plan.count):
            border[s * sub + k * (sub // 2) : s * sub + (k + 1) * (sub // 2), :] = found[
                s * (sub // 2) : (s + 1) * (sub // 2)
            ]
    image = plan.image // 2
    sums, extras = 0.0, 0.0
    for k in (2, 1, 0):
        here, beside = source[...], border[...]
        if k < 2:
            shift = (2 - k) * image
            inside = lanes_at((1, places), 1) < places - shift
            here, beside = [
                jnp.where(inside, pltpu.roll(part, places - shift, 1), jnp.zeros_like(part)) for part in (here, beside)
            ]
        weights, first = (late, 0) if k == 2 else (early, 9 * k)
        sums = sums + one_hot_dot(
            weights[first : first + 9].reshape(9 * wide, plan.channels), here, ((1,), (0,))
        )
        facing = jnp.concatenate([weights[first + 3 * row + 2 * member] for row in range(3)], axis=0)
        extras = extras + one_hot_dot(facing, beside, ((1,), (0,)))
    products[...], beyond[...] = sums, extras
    parts = [acts_ref[pq] for pq in range(4)]
    stats = sum(both_ref[k, sub : sub + 8, 0:128].astype(jnp.float32) for k in range(2))
    stats = stats[0:1] + stats[1:2] + stats[2:3]
    entries = 4 * plan.places * plan.group_width
    one, two = own_column(stats, 0, wide), own_column(stats, 64, wide)
    mean, inv_std = statistics(one, two, entries, plan.group_width)
    gain, bias = columns[2][:, 0:1], columns[3][:, 0:1]
    normed, slope = normalised(parts, gain, bias, mean, inv_std)
    lane, has_left, has_right, has_up, has_down = plan.place_masks(w)
    right, left = (1 - member).astype(jnp.float32), member.astype(jnp.float32)
    by_row = []
    for row in range(3):
        a, b, c = [products[pl.ds((3 * row + col) * wide, wide), :] for col in range(3)]
        extra = beyond[pl.ds(row * wide, wide), :]
        by_row.append(
            (a + b + moved(c, -1, has_left) + left * extra, moved(a, 1, has_right) + b + c + right * extra)
        )
    convs = [by_row[0][q] + by_row[1][q] + moved(by_row[2][q], -w, has_up) for q in range(2)]
    convs += [moved(by_row[0][q], w, has_down) + by_row[1][q] + by_row[2][q] for q in range(2)]
    pre = [conv * part for conv, part in zip(convs, slope)]
    one = total(pre)
    two = total([a * b for a, b in zip(pre, normed)])
    cot = source[pl.ds(pl.multiple_of(r * plan.slice_width + pair * wide, wide), wide), :].astype(jnp.float32)
    scale = inv_std * gain
    stacked = halves_from(plan, [cot + scale * part for part in pre]).astype(jnp.bfloat16)
    sent = one_hot_dot(stacked, order[...], ((1,), (1,))).astype(jnp.bfloat16)
    coarse = sums_ref[0:1] + pltpu.roll(sums_ref[1:2], sub, 1)
    coded = (
        terms(as_row(one) + pltpu.roll(as_row(two), 64, 1), 2)
        + terms(coarse, 2)
        + terms(as_row(inv_std) + pltpu.roll(as_row(mean), 64, 1), 3)
    )
    coded = jnp.concatenate(coded + [jnp.zeros_like(coarse)], axis=0).astype(jnp.bfloat16)
    for s_r in range(nr):
        for s_f in range(nf):
            out_ref[s_r * nf + s_f, 0:sub, :] = sent[s_f * sub : (s_f + 1) * sub, s_r * 128 : (s_r + 1) * 128]
            out_ref[s_r * nf + s_f, sub : sub + 8, :] = coded


def spread_kernel(plan, got_ref, acts_ref, rows_ref, out_ref, sums_ref):
    sub, nr, nf = plan.sub, plan.nr, plan.nf
    low = lanes_at((sub, 128), 1) < 64
    low_row = lanes_at((1, 128), 1) < 64
    first_row = lanes_at((1, 128), 1) < sub
    source = []
    fine, coarse, moments = [[], []], [[], []], [[], []]
    for s_r in range(nr):
        ones, twos, c_ones, c_twos, invs, means = [], [], 0.0, 0.0, [], []
        for pair in range(nf // 2):
            at = s_r * nf + 2 * pair
            left, right = [got_ref[at + k, 0:sub, :].astype(jnp.float32) for k in range(2)]
            source.append(jnp.where(low, left, pltpu.roll(right, 64, 1)))
            source.append(jnp.where(low, pltpu.roll(left, 64, 1), right))
            coded = [got_ref[at + k, sub : sub + 8, :].astype(jnp.float32) for k in range(2)]
            sums = coded[0][0:1] + coded[0][1:2] + coded[1][0:1] + coded[1][1:2]
            ones.append(sums if pair == 0 else pltpu.roll(sums, 64, 1))
            twos.append(pltpu.roll(sums, 64, 1) if pair == 0 else sums)
            both = coded[0][4:5] + coded[0][5:6] + coded[0][6:7]
            invs.append(both if pair == 0 else pltpu.roll(both, 64, 1))
            means.append(pltpu.roll(both, 64, 1) if pair == 0 else both)
            for k in range(2):
                sums = coded[k][2:3] + coded[k][3:4]
                to = (2 * pair + k) * sub
                c_one = jnp.where(first_row, sums, 0.0)
                c_two = jnp.where(first_row, pltpu.roll(sums, 128 - sub, 1), 0.0)
                c_ones = c_ones + (pltpu.roll(c_one, to, 1) if to else c_one)
                c_twos = c_twos + (pltpu.roll(c_two, to, 1) if to else c_two)
        fine[0].append(jnp.where(low_row, ones[0], ones[1]))
        fine[1].append(jnp.where(low_row, twos[0], twos[1]))
        moments[0].append(jnp.where(low_row, invs[0], invs[1]))
        moments[1].append(jnp.where(low_row, means[0], means[1]))
        coarse[0].append(c_ones)
        coarse[1].append(c_twos)
    one, two, inv_std, mean, c_one, c_two = [jnp.concatenate(part, axis=1) for part in fine + moments + coarse]
    source = jnp.concatenate(source, axis=0).astype(jnp.bfloat16)
    result = one_hot_dot(pixel_order(plan, False), source, ((1,), (1,)))
    gain = rows_ref[2]
    entries = 4 * plan.places * plan.group_width
    group_one = in_lane_groups(gain * one, plan.group_width) / entries
    group_two = in_lane_groups(gain * two, plan.group_width) / entries
    normed = (acts_ref[...].astype(jnp.float32) - mean) * inv_std
    out_ref[...] = (result - inv_std * (group_one + normed * group_two)).astype(jnp.bfloat16)
    sums_ref[...] = jnp.concatenate([one, two, c_one, c_two] + [jnp.zeros_like(one)] * 4, axis=0)


def total_kernel(scales, both_ref, result_ref, result_hbm, out_hbms, rows_ref, sems):
    copies = fetched([(result_ref, result_hbm)], sems)
    rows = sum(both_ref[k] for k in range(both_ref.shape[0]))
    for k in range(4):
        rows_ref[k] = rows[k : k + 1] * scales[k]
    for k in range(4):
        copies.append(pltpu.make_async_copy(rows_ref.at[k], out_hbms[k], sems.at[k + 1]))
        copies[-1].start()
    for copy in copies:
        copy.wait()


def in_vmem(count):
    return [pl.BlockSpec(memory_space=pltpu.VMEM)] * count


def in_hbm(count):
    return [pl.BlockSpec(memory_space=pltpu.HBM)] * count


def kept(array):
    return pltpu.with_memory_space_constraint(array, pltpu.HBM)


def shape_of(shape, kind):
    return jax.ShapeDtypeStruct(shape, kind)


LIMIT = pltpu.CompilerParams(vmem_limit_bytes=40 * 1024 * 1024)


def fast_shards(
    plan,
    acts_fine,
    acts_coarse,
    grad_coarse,
    gain_fine,
    bias_fine,
    kernel_fine,
    gain_coarse,
    bias_coarse,
    kernel_coarse,
):
    nd = lax.axis_size("dp")
    count, sub, channels, places, local = plan.count, plan.sub, plan.channels, plan.places, plan.local
    f32, bf16 = jnp.float32, jnp.bfloat16
    rows = [part.reshape(1, channels) for part in (gain_coarse, bias_coarse, gain_fine, bias_fine)]
    packed, acts, weights_c, weights_f, columns, order, fine_order, by_column, rows = pl.pallas_call(
        functools.partial(pack_kernel, plan),
        out_shape=(
            shape_of((count, plan.block_rows, 128), bf16),
            shape_of((4 * local, channels), bf16),
            shape_of((27, 2 * sub, channels // 2), bf16),
            shape_of((9, 2 * sub, channels), bf16),
            shape_of((4, 2 * sub, 128), f32),
            shape_of((4 * plan.nr * local, 4 * plan.nr * local), bf16),
            shape_of((4 * plan.nr * local, 4 * plan.nr * local), bf16),
            shape_of((places, places + places // 2), bf16),
            shape_of((4, 1, channels), f32),
        ),
        in_specs=in_hbm(9),
        out_specs=tuple(in_vmem(9)),
        scratch_shapes=[
            pltpu.VMEM((local, channels), bf16),
            pltpu.VMEM((local, channels), bf16),
            pltpu.SemaphoreType.DMA((9,)),
        ],
        compiler_params=LIMIT,
    )(
        kept(grad_coarse.reshape(local, channels)),
        kept(acts_coarse.reshape(local, channels)),
        kept(acts_fine.reshape(4 * local, channels)),
        kept(kernel_coarse),
        kept(kernel_fine),
        *[kept(row) for row in rows],
    )
    got = lax.all_to_all(packed, BLOCK, 0, 0)
    mine, theirs, held, inv_std, fine_acts, early_f = pl.pallas_call(
        functools.partial(coarse_kernel, plan),
        out_shape=(
            shape_of((sub, places), f32),
            shape_of((sub + 8, places), bf16),
            shape_of((3, sub, places), f32),
            shape_of((sub, 128), f32),
            shape_of((4, 2 * sub, places // 2), f32),
            shape_of((18, 2 * sub, channels), bf16),
        ),
        in_specs=in_vmem(5) + in_hbm(1),
        out_specs=tuple(in_vmem(6)),
        scratch_shapes=[
            pltpu.VMEM((places + 2 * plan.image, channels // 2), bf16),
            pltpu.VMEM((18 * sub, places), f32),
            pltpu.VMEM((2 * sub, places), f32),
            pltpu.SemaphoreType.DMA((1,)),
        ],
        compiler_params=LIMIT,
    )(got, weights_c, columns, order, fine_order, kept(kernel_fine))
    both = lax.all_gather(theirs, "member")
    quartered, coarse_sums = pl.pallas_call(
        functools.partial(quarter_kernel, plan),
        out_shape=(shape_of((count, 2 * sub + sub // 2, 128), bf16), shape_of((2, 128), f32)),
        in_specs=in_vmem(6),
        out_specs=tuple(in_vmem(2)),
        compiler_params=LIMIT,
    )(mine, both, held, inv_std, columns, by_column)
    spread = lax.all_to_all(quartered, BLOCK, 0, 0)
    sent = pl.pallas_call(
        functools.partial(fine_kernel, plan),
        out_shape=shape_of((count, sub + 8, 128), bf16),
        in_specs=in_vmem(8),
        out_specs=in_vmem(1)[0],
        scratch_shapes=[
            pltpu.VMEM((channels, places // 2), bf16),
            pltpu.VMEM((channels, places // 2), bf16),
            pltpu.VMEM((18 * sub, places // 2), f32),
            pltpu.VMEM((6 * sub, places // 2), f32),
        ],
        compiler_params=LIMIT,
    )(spread, fine_acts, both, columns, fine_order, coarse_sums, weights_f, early_f)
    back = lax.all_to_all(sent, BLOCK, 0, 0)
    cells = nd * places
    fine_scale, coarse_scale = 1.0 / math.sqrt(4 * cells), 1.0 / math.sqrt(cells)
    out, sums = pl.pallas_call(
        functools.partial(spread_kernel, plan),
        out_shape=(pltpu.VMEM((4 * local, channels), bf16), shape_of((8, channels), f32)),
        in_specs=in_vmem(3),
        out_specs=tuple(in_vmem(2)),
        compiler_params=LIMIT,
    )(back, acts, rows)
    both = lax.all_gather(sums, "dp")
    out, sums = pl.pallas_call(
        functools.partial(total_kernel, (fine_scale, fine_scale, coarse_scale, coarse_scale)),
        out_shape=(pltpu.HBM((4 * local, channels), bf16), (pltpu.HBM((1, channels), f32),) * 4),
        in_specs=in_vmem(2),
        out_specs=(in_hbm(1)[0], tuple(in_hbm(4))),
        scratch_shapes=[pltpu.VMEM((4, 1, channels), f32), pltpu.SemaphoreType.DMA((5,))],
        compiler_params=LIMIT,
    )(both, out)
    bias_f, gain_f, bias_c, gain_c = [part.reshape(channels) for part in sums]
    return out.reshape(acts_fine.shape), gain_f, bias_f, gain_c, bias_c


def solution(mesh):
    def function(*arrays):
        local = [size // mesh.shape[axis] for size, axis in zip(arrays[1].shape, ("dp", "frames", "rows"))]
        sizes = (mesh.shape["frames"], mesh.shape["rows"])
        plan = Plan(sizes, (*local[1:], *arrays[1].shape[3:]), arrays[5].shape[1] // mesh.shape["rows"])
        if plan.fits:
            split = (mesh.shape["dp"], plan.nf // 2, 2, plan.nr)
            used = jax.sharding.Mesh(mesh.devices.reshape(split), ("dp", "pairs", "member", "rows"))
            shards, frames = functools.partial(fast_shards, plan), ("pairs", "member")
        else:
            used, shards, frames = mesh, plain_shards, "frames"
        blocks, kernel = P("dp", frames, "rows", None, None), P(None, "rows", None)
        in_specs = (blocks, blocks, blocks, P(), P(), kernel, P(), P(), kernel)
        out_specs = (blocks, P(), P(), P(), P())
        mapped = jax.shard_map(shards, mesh=used, in_specs=in_specs, out_specs=out_specs, check_vma=False)
        return mapped(*arrays)

    return function
```

```python
import functools
import math

import jax
import jax.numpy as jnp
from jax import lax
from jax.experimental import pallas as pl
from jax.experimental.pallas import tpu as pltpu
from jax.sharding import PartitionSpec as P

GROUPS = 32
EPSILON = 1e-06
BLOCK = ("rows", "pairs", "member")
PLAIN_BLOCK = ("frames", "rows")


def plain_everyone(block, count):
    copies = jnp.broadcast_to(block[None], (count,) + block.shape)
    return lax.all_to_all(copies, PLAIN_BLOCK, 0, 0)


def ahead(field, axis, distance):
    size = field.shape[axis]
    if distance == 0:
        return field
    widths = [(0, 0)] * field.ndim
    if distance > 0:
        widths[axis] = (0, distance)
        kept = lax.slice_in_dim(field, distance, size, axis=axis)
    else:
        widths[axis] = (-distance, 0)
        kept = lax.slice_in_dim(field, 0, size + distance, axis=axis)
    return jnp.pad(kept, widths)


def tap_products(source, kernel):
    sub = kernel.shape[1]
    frames, rows, cols, channels = source.shape
    products = lax.dot_general(
        kernel.reshape(27 * sub, channels),
        source.reshape(frames * rows * cols, channels),
        (((1,), (1,)), ((), ())),
        preferred_element_type=jnp.float32,
    ).reshape(3, 3, 3, sub, frames, rows, cols)
    return sum(ahead(products[depth], 3, 2 - depth) for depth in range(3))


def coarse_conv(source, kernel):
    spatial = tap_products(source, kernel)
    total = 0.0
    for row in range(3):
        part = sum(ahead(spatial[row, col], 3, 1 - col) for col in range(3))
        total = total + ahead(part, 2, 1 - row)
    return total


def fine_conv(source, kernel):
    spatial = tap_products(source, kernel)
    result = []
    for p in range(2):
        rows_of = []
        for q in range(2):
            total = 0.0
            for row in range(3):
                part = sum(ahead(spatial[row, col], 3, (q + 1 - col) // 2) for col in range(3))
                total = total + ahead(part, 2, (p + 1 - row) // 2)
            rows_of.append(total)
        result.append(jnp.stack(rows_of, 1))
    return jnp.stack(result, 1)


def group_total(sums, group_width):
    sub = sums.shape[-1]
    if sub % group_width == 0:
        grouped = jnp.sum(sums.reshape(-1, sub // group_width, group_width), axis=-1)
        return jnp.repeat(grouped, group_width, axis=-1)
    spread = jnp.moveaxis(lax.all_gather(sums, "frames"), 0, 1).reshape(sums.shape[0], -1, group_width)
    mine = lax.axis_index("frames") * sub // group_width
    grouped = lax.dynamic_index_in_dim(jnp.sum(spread, -1), mine, 1)
    return jnp.broadcast_to(grouped, sums.shape)


def level(acts, conv_grad, cotangent, gain, bias, group_width):
    sub = acts.shape[0]
    places = acts.size // sub
    values = acts.astype(jnp.float32).reshape(sub, places)
    conv_grad = conv_grad.reshape(sub, places)
    entries = places * group_width
    moments = group_total(
        jnp.stack([jnp.sum(values, 1), jnp.sum(values * values, 1)]), group_width
    ) / entries
    mean = moments[0]
    inv_std = lax.rsqrt(moments[1] - mean * mean + EPSILON)
    normed = (values - mean[:, None]) * inv_std[:, None]
    preact = gain[:, None] * normed + bias[:, None]
    squash = jax.nn.sigmoid(preact)
    pre_grad = conv_grad * squash * (1.0 + preact * (1.0 - squash))
    sums = jnp.stack([jnp.sum(pre_grad, 1), jnp.sum(pre_grad * normed, 1)])
    terms = group_total(sums * gain, group_width) / entries
    grad = cotangent.reshape(sub, places) + inv_std[:, None] * (
        gain[:, None] * pre_grad - terms[0][:, None] - normed * terms[1][:, None]
    )
    return grad, sums


def plain_shards(
    acts_fine,
    acts_coarse,
    grad_coarse,
    gain_fine,
    bias_fine,
    kernel_fine,
    gain_coarse,
    bias_coarse,
    kernel_coarse,
):
    nf, nr, nd = lax.axis_size("frames"), lax.axis_size("rows"), lax.axis_size("dp")
    count = nf * nr
    channels = acts_fine.shape[-1]
    slice_width = kernel_fine.shape[1]
    sub = slice_width // nf
    group_width = channels // GROUPS
    tl, hl, w = acts_coarse.shape[1:4]
    frames, rows = tl * nf, hl * nr
    f, r = lax.axis_index("frames"), lax.axis_index("rows")

    gathered = plain_everyone(grad_coarse[0], count)
    source = (
        gathered.reshape(nf, nr, tl, hl, w, channels)
        .transpose(0, 2, 1, 3, 4, 5)
        .reshape(frames, rows, w, channels)
    )
    coarse_in = acts_coarse[0].reshape(tl, hl, w, nr, nf, sub).transpose(4, 3, 5, 0, 1, 2)
    coarse_in = lax.all_to_all(coarse_in.reshape(count, sub, tl * hl * w), PLAIN_BLOCK, 0, 0)
    fine_in = acts_fine[0].reshape(tl, hl, 2, w, 2, nr, nf, sub).transpose(6, 5, 7, 2, 4, 0, 1, 3)
    fine_in = lax.all_to_all(fine_in.reshape(count, sub, 4 * tl * hl * w), PLAIN_BLOCK, 0, 0)

    def mine(vector):
        return lax.dynamic_slice_in_dim(vector, r * slice_width + f * sub, sub)

    def own(kernel):
        return lax.dynamic_slice_in_dim(kernel, f * sub, sub, axis=1)

    coarse_vals = (
        coarse_in.reshape(nf, nr, sub, tl, hl, w).transpose(2, 0, 3, 1, 4, 5).reshape(sub, frames, rows, w)
    )
    cot = lax.dynamic_slice_in_dim(source, r * slice_width + f * sub, sub, axis=3)
    cot = cot.astype(jnp.float32).transpose(3, 0, 1, 2)
    conv = coarse_conv(source, own(kernel_coarse))
    coarse_grad, coarse_sums = level(
        coarse_vals, conv, cot, mine(gain_coarse), mine(bias_coarse), group_width
    )
    quartered = (coarse_grad * 0.25).astype(jnp.bfloat16)
    spread = plain_everyone(quartered, count)
    source_fine = (
        spread.reshape(nf, nr, sub, frames, rows, w)
        .transpose(3, 4, 5, 1, 0, 2)
        .reshape(frames, rows, w, channels)
    )
    conv = fine_conv(source_fine, own(kernel_fine))
    fine_vals = (
        fine_in.reshape(nf, nr, sub, 2, 2, tl, hl, w)
        .transpose(2, 3, 4, 0, 5, 1, 6, 7)
        .reshape(sub, 2, 2, frames, rows, w)
    )
    cot = jnp.broadcast_to(
        quartered.astype(jnp.float32).reshape(sub, 1, 1, frames, rows, w), conv.shape
    )
    fine_grad, fine_sums = level(
        fine_vals, conv, cot, mine(gain_fine), mine(bias_fine), group_width
    )
    back = (
        fine_grad.astype(jnp.bfloat16)
        .reshape(sub, 2, 2, nf, tl, nr, hl, w)
        .transpose(3, 5, 0, 1, 2, 4, 6, 7)
        .reshape(count, sub, 4 * tl * hl * w)
    )
    sums = plain_everyone(jnp.concatenate([fine_sums, coarse_sums]), count)
    back = lax.all_to_all(back, PLAIN_BLOCK, 0, 0)
    out = (
        back.reshape(nf, nr, sub, 2, 2, tl, hl, w)
        .transpose(5, 6, 3, 7, 4, 1, 0, 2)
        .reshape(1, tl, 2 * hl, 2 * w, channels)
    )
    sums = sums.reshape(nf, nr, 4, sub).transpose(2, 1, 0, 3).reshape(4, channels)
    totals = lax.psum(sums, "dp")
    cells = nd * frames * rows * w
    scale_fine = 1.0 / jnp.sqrt(jnp.float32(4 * cells))
    scale_coarse = 1.0 / jnp.sqrt(jnp.float32(cells))
    return (
        out,
        totals[1] * scale_fine,
        totals[0] * scale_fine,
        totals[3] * scale_coarse,
        totals[2] * scale_coarse,
    )


def lanes_at(shape, axis):
    return lax.broadcasted_iota(jnp.int32, shape, axis)


def one_hot(found):
    return found.astype(jnp.float32).astype(jnp.bfloat16)


def pixel_order(plan, swapped):
    tl, hl, w = plan.tl, plan.hl, plan.w // 2
    size = 4 * plan.local
    lane = lanes_at((1, size), 1)
    j, i, t = lane % w, lane // w % hl, lane // (w * hl) % tl
    q, p = lane // (w * hl * tl) % 2, lane // (2 * w * hl * tl) % 2
    half = lane // (4 * w * hl * tl)
    if swapped:
        half = 1 - half
    pixel = (t * 2 * hl + 2 * i + p) * 4 * w + 2 * (half * w + j) + q
    return one_hot(lanes_at((size, size), 0) == pixel)


def merged_order(nr, outer, tl, cells):
    size = nr * outer * tl * cells
    lane = lanes_at((1, size), 1)
    cell, dev = lane % cells, lane // cells % nr
    t, o = lane // (cells * nr) % tl, lane // (cells * nr * tl)
    return one_hot(lanes_at((size, size), 0) == ((dev * outer + o) * tl + t) * cells + cell)


def column_order(plan):
    w = plan.w // 2
    lines = plan.places // plan.w
    lane = lanes_at((1, 4 * lines * w + 4 * lines), 1)
    inner = lane % (lines * w)
    place = inner // w * plan.w + lane // (lines * w) * w + inner % w
    past = lane - 2 * lines * w
    border = past % lines * plan.w + jnp.where(past < 2 * lines, w, w - 1)
    wanted = jnp.where(past >= 0, border, place)
    shape = (plan.places, 2 * lines * w + 4 * lines)
    return one_hot(lanes_at(shape, 0) == wanted[:, : shape[1]])


def one_hot_dot(a, b, dims):
    return lax.dot_general(a, b, (dims, ((), ())), preferred_element_type=jnp.float32)


def moved(field, distance, kept):
    size = field.shape[1]
    return jnp.where(kept, pltpu.roll(field, (-distance) % size, 1), 0.0)


def own_column(row, base, sub):
    shape = (sub, row.shape[1])
    mine = lanes_at(shape, 1) == lanes_at(shape, 0) + base
    return jnp.sum(jnp.where(mine, row, 0.0), axis=1, keepdims=True)


def as_row(column):
    shape = (column.shape[0], 128)
    here = lanes_at(shape, 1) == lanes_at(shape, 0)
    return jnp.sum(jnp.where(here, column, 0.0), axis=0, keepdims=True)


def terms(value, count):
    found = []
    for _ in range(count):
        found.append(value.astype(jnp.bfloat16).astype(jnp.float32))
        value = value - found[-1]
    return found


def in_groups(column, group_width):
    sub = column.shape[0]
    grouped = jnp.sum(column.reshape(sub // group_width, group_width, 1), axis=1, keepdims=True)
    return jnp.broadcast_to(grouped, (sub // group_width, group_width, 1)).reshape(sub, 1)


def in_lane_groups(row, group_width):
    lane = lanes_at(row.shape, 1)
    size = row.shape[1]
    step = 1
    while step < group_width:
        up, down = pltpu.roll(row, size - step, 1), pltpu.roll(row, step, 1)
        row = row + jnp.where(lane // step % 2 == 0, up, down)
        step *= 2
    return row


def total(parts):
    return sum(jnp.sum(part, axis=1, keepdims=True) for part in parts)


def statistics(one, two, entries, group_width):
    mean = in_groups(one, group_width) / entries
    square = in_groups(two, group_width) / entries
    return mean, lax.rsqrt(square - mean * mean + EPSILON)


def normalised(parts, gain, bias, mean, inv_std):
    normed, slope = [], []
    for part in parts:
        unit = (part - mean) * inv_std
        preact = gain * unit + bias
        squash = jax.nn.sigmoid(preact)
        normed.append(unit)
        slope.append(squash * (1.0 + preact * (1.0 - squash)))
    return normed, slope


class Plan:
    def __init__(self, mesh_sizes, acts_coarse, slice_width):
        self.nf, self.nr = mesh_sizes
        self.count = self.nf * self.nr
        self.tl, self.hl, self.w, self.channels = acts_coarse
        self.slice_width = slice_width
        self.sub = slice_width // self.nf
        self.cells = self.hl * self.w
        self.local = self.tl * self.cells
        self.image = self.cells * self.nr
        self.frames = self.tl * self.nf
        self.places = self.frames * self.image
        self.group_width = self.channels // GROUPS
        self.chunks = self.channels // 128
        self.acts_at = self.chunks // 2 * self.local
        self.packed_at = self.acts_at + self.sub
        self.cot_at = self.packed_at + 8
        self.block_rows = self.cot_at + 8
        self.fits = (
            self.sub == 32
            and self.slice_width == 128
            and self.group_width == 16
            and self.cells == 16
            and self.w == 8
            and self.tl == 2
            and self.nr == 4
            and self.nf == 4
            and self.slice_width * self.nr == self.channels
        )

    def place_masks(self, w):
        lane = lanes_at((1, self.places // self.w * w), 1)
        col, row = lane % w, lane // w % (self.hl * self.nr)
        last_row = self.hl * self.nr - 1
        return (lane, col > 0, col < w - 1, row > 0, row < last_row)


def fetched(pairs, sems):
    copies = [pltpu.make_async_copy(src, dst, sems.at[k]) for k, (src, dst) in enumerate(pairs)]
    for copy in copies:
        copy.start()
    return copies


def own_place(plan):
    pair, member, r = lax.axis_index("pairs"), lax.axis_index("member"), lax.axis_index("rows")
    return pair, member, r, r * plan.slice_width + (2 * pair + member) * plan.sub


def pack_kernel(
    plan,
    g_hbm,
    coarse_hbm,
    fine_hbm,
    gain_c,
    bias_c,
    gain_f,
    bias_f,
    out_ref,
    fine_ref,
    columns,
    order,
    fine_order,
    by_column,
    rows,
    g_ref,
    coarse_ref,
    sems,
):
    sub, chunks, local = plan.sub, plan.chunks, plan.local
    pair, member, r, base = own_place(plan)
    copies = fetched(
        [(fine_hbm, fine_ref), (coarse_hbm, coarse_ref), (g_hbm, g_ref)]
        + [(row, rows.at[k]) for k, row in enumerate((gain_c, bias_c, gain_f, bias_f))],
        sems,
    )
    order[...] = merged_order(plan.nr, 4, plan.tl, plan.cells)
    fine_order[...] = merged_order(plan.nr, 8, plan.tl, plan.cells // 2)
    by_column[...] = column_order(plan)
    shape = (2 * local, 2 * 128)
    lane = lanes_at((1, 2 * 128), 1)
    repeated = one_hot(lanes_at(shape, 0) == lane % local + lane // 128 * local)
    shape = (plan.channels, 128)
    quarter = lanes_at(shape, 0) // 8 % 4 == lanes_at(shape, 1) // local
    orders = jnp.concatenate([pixel_order(plan, swapped) for swapped in (False, True)], axis=1)
    copies[0].wait()
    acts = fine_ref[...]
    halves = one_hot_dot(acts, orders, ((0,), (0,))).astype(jnp.bfloat16)
    halves = [halves[:, :128], halves[:, 128:]]
    copies[1].wait()
    copies[2].wait()
    small = one_hot_dot(jnp.concatenate([coarse_ref[...], g_ref[...]], axis=0), repeated, ((0,), (0,)))
    for k, at in enumerate((plan.packed_at, plan.cot_at)):
        rows_of = jnp.where(quarter, small[:, k * 128 : (k + 1) * 128], 0.0).reshape(plan.count, 4, 8, 128)
        out_ref[:, at : at + 8, :] = jnp.sum(rows_of, axis=1).astype(jnp.bfloat16)
    low = lanes_at((sub, 128), 1) < 64
    for s_r in range(plan.nr):
        for s_f in range(plan.nf):
            dest = s_r * plan.nf + s_f
            first, half = s_r * plan.slice_width + s_f // 2 * 2 * sub, s_f % 2
            for k in range(chunks // 2):
                at = (half * chunks // 2 + k) * 128
                out_ref[dest, k * local : (k + 1) * local, :] = g_ref[:, at : at + 128]
            upper, lower = halves[half][first : first + sub], halves[1 - half][first + sub : first + 2 * sub]
            out_ref[dest, plan.acts_at : plan.packed_at, :] = jnp.where(low, upper, lower)
    for copy in copies[3:7]:
        copy.wait()
    first = r * plan.slice_width + 2 * pair * sub
    for k in range(2):
        columns[k, 0:sub, :] = jnp.broadcast_to(own_column(rows[k], base, sub), (sub, 128))
        columns[2 + k] = jnp.broadcast_to(own_column(rows[2 + k], first, 2 * sub), (2 * sub, 128))


def by_frame_device(plan, got_ref, at, height):
    return jnp.concatenate(
        [
            jnp.concatenate(
                [got_ref[r * plan.nf + f, at : at + height, :] for r in range(plan.nr)], axis=1
            )
            for f in range(plan.nf)
        ],
        axis=0,
    )


def in_places(plan, merged, height):
    width = plan.tl * plan.image
    return [
        jnp.concatenate(
            [merged[f * height : (f + 1) * height, k * width : (k + 1) * width] for f in range(plan.nf)],
            axis=1,
        )
        for k in range(4)
    ]


def coarse_kernel(
    plan,
    got_ref,
    weights,
    columns,
    order,
    fine_order,
    mine_ref,
    sent_ref,
    held_ref,
    inv_ref,
    fine_ref,
    source,
    products,
    conv_ref,
):
    sub, nr, nf, cells, tl, local = plan.sub, plan.nr, plan.nf, plan.cells, plan.tl, plan.local
    wide, depth = 2 * sub, plan.channels // 2
    pair, member, _, _ = own_place(plan)
    both = pl.ds(pl.multiple_of(pair * wide, wide), wide)
    half = pl.ds(pl.multiple_of(member * depth, depth), depth)
    for s_f in range(nf):
        for s_r in range(nr):
            for t in range(tl):
                at = (s_f * tl + t) * plan.image + s_r * cells
                for k in range(plan.chunks // 2):
                    source[at : at + cells, k * 128 : (k + 1) * 128] = got_ref[
                        s_r * nf + s_f, k * local + t * cells : k * local + (t + 1) * cells, :
                    ]
    source[plan.places :, :] = jnp.zeros((2 * plan.image, depth), jnp.bfloat16)
    products[...] = sum(
        one_hot_dot(
            weights[9 * k : 9 * k + 9, both, half].reshape(9 * wide, depth),
            source[(2 - k) * plan.image : (2 - k) * plan.image + plan.places, :],
            ((1,), (1,)),
        )
        for k in range(3)
    )
    merged = one_hot_dot(by_frame_device(plan, got_ref, plan.acts_at, sub), fine_order[...], ((1,), (0,)))
    parts = halves_at(plan, merged)
    for pq in range(4):
        fine_ref[pq] = parts[pq]
    one, two = total(parts), total([part * part for part in parts])
    stats = terms(as_row(one) + pltpu.roll(as_row(two), 64, 1), 3)
    stats = jnp.concatenate(stats + [jnp.zeros_like(stats[0])] * 5, axis=0).astype(jnp.bfloat16)
    found = []
    for at in (plan.packed_at, plan.cot_at):
        merged = one_hot_dot(by_frame_device(plan, got_ref, at, 8), order[...], ((1,), (0,)))
        found.append(jnp.concatenate(in_places(plan, merged, 8), axis=0))
    values, cot = found
    gain, bias = columns[0][0:sub, 0:1], columns[1][0:sub, 0:1]
    entries = plan.places * plan.group_width
    mean, inv_std = statistics(total([values]), total([values * values]), entries, plan.group_width)
    (normed,), (slope,) = normalised([values], gain, bias, mean, inv_std)
    held_ref[0], held_ref[1], held_ref[2] = normed, slope, cot
    inv_ref[...] = jnp.broadcast_to(inv_std, (sub, 128))
    lane, has_left, has_right, has_up, has_down = plan.place_masks(plan.w)
    by_col = []
    for col in range(3):
        parts = [products[pl.ds((3 * row + col) * wide, wide), :] for row in range(3)]
        by_col.append(parts[1] + moved(parts[0], plan.w, has_down) + moved(parts[2], -plan.w, has_up))
    conv_ref[...] = by_col[1] + moved(by_col[0], 1, has_right) + moved(by_col[2], -1, has_left)
    mine_ref[...] = conv_ref[pl.ds(pl.multiple_of(member * sub, sub), sub), :]
    theirs = conv_ref[pl.ds(pl.multiple_of((1 - member) * sub, sub), sub), :]
    sent_ref[0:sub, :] = theirs.astype(jnp.bfloat16)
    sent_ref[sub:, 0:128] = stats
    sent_ref[sub:, 128:] = jnp.zeros((8, plan.places - 128), jnp.bfloat16)


def quarter_kernel(plan, mine_ref, both_ref, held_ref, inv_ref, columns, by_column, out_ref, sums_ref):
    sub = plan.sub
    _, member, _, _ = own_place(plan)
    conv = mine_ref[...] + both_ref[1 - member, 0:sub, :].astype(jnp.float32)
    normed, slope, cot = held_ref[0], held_ref[1], held_ref[2]
    gain, inv_std = columns[0][0:sub, 0:1], inv_ref[:, 0:1]
    entries = plan.places * plan.group_width
    pre = conv * slope
    one, two = total([pre]), total([pre * normed])
    group_one = in_groups(gain * one, plan.group_width) / entries
    group_two = in_groups(gain * two, plan.group_width) / entries
    grad = cot + inv_std * (gain * pre - group_one - normed * group_two)
    quartered = (grad * 0.25).astype(jnp.bfloat16)
    sent = one_hot_dot(quartered, by_column[...], ((1,), (0,))).astype(jnp.bfloat16)
    low = lanes_at((sub // 2, 128), 1) < 64
    for half in range(2):
        at = half * 256
        border = sent[:, 512 + half * 128 : 640 + half * 128]
        border = jnp.where(low, border[: sub // 2], border[sub // 2 :])
        for dest in range(half, plan.count, 2):
            out_ref[dest, 0:sub, :] = sent[:, at : at + 128]
            out_ref[dest, sub : 2 * sub, :] = sent[:, at + 128 : at + 256]
            out_ref[dest, 2 * sub : 2 * sub + sub // 2, :] = border
    sums_ref[...] = jnp.concatenate([as_row(one), as_row(two)], axis=0)


def halves_at(plan, merged):
    sub = plan.sub
    turned = jnp.concatenate([pltpu.roll(merged[:, k * 128 : (k + 1) * 128], 64, 1) for k in range(4)], axis=1)
    low = lanes_at((sub, 128), 1) < 64
    parts = []
    for pq in range(4):
        groups = []
        for group in range(2):
            e = 4 * group + pq
            at = e // 2 * 128
            strips = []
            for m in range(plan.nf // 2):
                first, second = slice(2 * m * sub, (2 * m + 1) * sub), slice((2 * m + 1) * sub, (2 * m + 2) * sub)
                if e % 2 == 0:
                    strips.append(jnp.where(low, merged[first, at : at + 128], turned[second, at : at + 128]))
                else:
                    strips.append(jnp.where(low, turned[first, at : at + 128], merged[second, at : at + 128]))
            groups.append(jnp.concatenate(strips, axis=1))
        parts.append(jnp.concatenate(groups, axis=0))
    return parts


def halves_from(plan, parts):
    sub = plan.sub
    low = lanes_at((sub, 128), 1) < 64
    down = []
    for f in range(plan.nf):
        across = []
        for v in range(4):
            pair = []
            for e in (2 * v, 2 * v + 1):
                group, pq = e // 4, e % 4
                strip = parts[pq][group * sub : (group + 1) * sub, f // 2 * 128 : (f // 2 + 1) * 128]
                pair.append(strip if e % 2 == f % 2 else pltpu.roll(strip, 64, 1))
            across.append(jnp.where(low, pair[0], pair[1]))
        down.append(jnp.concatenate(across, axis=1))
    return jnp.concatenate(down, axis=0)


def fine_kernel(
    plan, got_ref, acts_ref, both_ref, columns, order, sums_ref, weights, out_ref, source, border, products, beyond
):
    sub, nr, nf, wide = plan.sub, plan.nr, plan.nf, 2 * plan.sub
    pair, member, r, _ = own_place(plan)
    both = pl.ds(pl.multiple_of(pair * wide, wide), wide)
    w = plan.w // 2
    lines = plan.places // plan.w
    places = lines * w
    for k in range(2):
        source[:, k * 128 : (k + 1) * 128] = got_ref[:, k * sub : (k + 1) * sub, :].reshape(plan.channels, 128)
    packed = got_ref[:, wide : wide + sub // 2, :].reshape(plan.count * sub // 2, 128)
    shape = (128, places)
    beside = lanes_at(shape, 1) == lanes_at(shape, 0) % lines * w + (1 - member) * (w - 1)
    for k in range(2):
        here = one_hot(beside & (lanes_at(shape, 0) // lines == k))
        found = one_hot_dot(packed, here, ((1,), (0,))).astype(jnp.bfloat16)
        for s in range(plan.count):
            border[s * sub + k * (sub // 2) : s * sub + (k + 1) * (sub // 2), :] = found[
                s * (sub // 2) : (s + 1) * (sub // 2)
            ]
    image = plan.image // 2
    sums, extras = 0.0, 0.0
    for k in (2, 1, 0):
        here, beside = source[...], border[...]
        if k < 2:
            shift = (2 - k) * image
            inside = lanes_at((1, places), 1) < places - shift
            here, beside = [
                jnp.where(inside, pltpu.roll(part, places - shift, 1), jnp.zeros_like(part)) for part in (here, beside)
            ]
        sums = sums + one_hot_dot(
            weights[9 * k : 9 * k + 9, both, :].reshape(9 * wide, plan.channels), here, ((1,), (0,))
        )
        facing = jnp.concatenate([weights[9 * k + 3 * row + 2 * member, both, :] for row in range(3)], axis=0)
        extras = extras + one_hot_dot(facing, beside, ((1,), (0,)))
    products[...], beyond[...] = sums, extras
    parts = [acts_ref[pq] for pq in range(4)]
    stats = sum(both_ref[k, sub : sub + 8, 0:128].astype(jnp.float32) for k in range(2))
    stats = stats[0:1] + stats[1:2] + stats[2:3]
    entries = 4 * plan.places * plan.group_width
    one, two = own_column(stats, 0, wide), own_column(stats, 64, wide)
    mean, inv_std = statistics(one, two, entries, plan.group_width)
    gain, bias = columns[2][:, 0:1], columns[3][:, 0:1]
    normed, slope = normalised(parts, gain, bias, mean, inv_std)
    lane, has_left, has_right, has_up, has_down = plan.place_masks(w)
    right, left = (1 - member).astype(jnp.float32), member.astype(jnp.float32)
    by_row = []
    for row in range(3):
        a, b, c = [products[pl.ds((3 * row + col) * wide, wide), :] for col in range(3)]
        extra = beyond[pl.ds(row * wide, wide), :]
        by_row.append(
            (a + b + moved(c, -1, has_left) + left * extra, moved(a, 1, has_right) + b + c + right * extra)
        )
    convs = [by_row[0][q] + by_row[1][q] + moved(by_row[2][q], -w, has_up) for q in range(2)]
    convs += [moved(by_row[0][q], w, has_down) + by_row[1][q] + by_row[2][q] for q in range(2)]
    pre = [conv * part for conv, part in zip(convs, slope)]
    one = total(pre)
    two = total([a * b for a, b in zip(pre, normed)])
    cot = source[pl.ds(pl.multiple_of(r * plan.slice_width + pair * wide, wide), wide), :].astype(jnp.float32)
    scale = inv_std * gain
    stacked = halves_from(plan, [cot + scale * part for part in pre]).astype(jnp.bfloat16)
    sent = one_hot_dot(stacked, order[...], ((1,), (1,))).astype(jnp.bfloat16)
    coarse = sums_ref[0:1] + pltpu.roll(sums_ref[1:2], sub, 1)
    coded = (
        terms(as_row(one) + pltpu.roll(as_row(two), 64, 1), 2)
        + terms(coarse, 2)
        + terms(as_row(inv_std) + pltpu.roll(as_row(mean), 64, 1), 3)
    )
    coded = jnp.concatenate(coded + [jnp.zeros_like(coarse)], axis=0).astype(jnp.bfloat16)
    for s_r in range(nr):
        for s_f in range(nf):
            out_ref[s_r * nf + s_f, 0:sub, :] = sent[s_f * sub : (s_f + 1) * sub, s_r * 128 : (s_r + 1) * 128]
            out_ref[s_r * nf + s_f, sub : sub + 8, :] = coded


def spread_kernel(plan, got_ref, acts_ref, rows_ref, out_ref, sums_ref):
    sub, nr, nf = plan.sub, plan.nr, plan.nf
    low = lanes_at((sub, 128), 1) < 64
    low_row = lanes_at((1, 128), 1) < 64
    first_row = lanes_at((1, 128), 1) < sub
    source = []
    fine, coarse, moments = [[], []], [[], []], [[], []]
    for s_r in range(nr):
        ones, twos, c_ones, c_twos, invs, means = [], [], 0.0, 0.0, [], []
        for pair in range(nf // 2):
            at = s_r * nf + 2 * pair
            left, right = [got_ref[at + k, 0:sub, :].astype(jnp.float32) for k in range(2)]
            source.append(jnp.where(low, left, pltpu.roll(right, 64, 1)))
            source.append(jnp.where(low, pltpu.roll(left, 64, 1), right))
            coded = [got_ref[at + k, sub : sub + 8, :].astype(jnp.float32) for k in range(2)]
            sums = coded[0][0:1] + coded[0][1:2] + coded[1][0:1] + coded[1][1:2]
            ones.append(sums if pair == 0 else pltpu.roll(sums, 64, 1))
            twos.append(pltpu.roll(sums, 64, 1) if pair == 0 else sums)
            both = coded[0][4:5] + coded[0][5:6] + coded[0][6:7]
            invs.append(both if pair == 0 else pltpu.roll(both, 64, 1))
            means.append(pltpu.roll(both, 64, 1) if pair == 0 else both)
            for k in range(2):
                sums = coded[k][2:3] + coded[k][3:4]
                to = (2 * pair + k) * sub
                c_one = jnp.where(first_row, sums, 0.0)
                c_two = jnp.where(first_row, pltpu.roll(sums, 128 - sub, 1), 0.0)
                c_ones = c_ones + (pltpu.roll(c_one, to, 1) if to else c_one)
                c_twos = c_twos + (pltpu.roll(c_two, to, 1) if to else c_two)
        fine[0].append(jnp.where(low_row, ones[0], ones[1]))
        fine[1].append(jnp.where(low_row, twos[0], twos[1]))
        moments[0].append(jnp.where(low_row, invs[0], invs[1]))
        moments[1].append(jnp.where(low_row, means[0], means[1]))
        coarse[0].append(c_ones)
        coarse[1].append(c_twos)
    one, two, inv_std, mean, c_one, c_two = [jnp.concatenate(part, axis=1) for part in fine + moments + coarse]
    source = jnp.concatenate(source, axis=0).astype(jnp.bfloat16)
    result = one_hot_dot(pixel_order(plan, False), source, ((1,), (1,)))
    gain = rows_ref[2]
    entries = 4 * plan.places * plan.group_width
    group_one = in_lane_groups(gain * one, plan.group_width) / entries
    group_two = in_lane_groups(gain * two, plan.group_width) / entries
    normed = (acts_ref[...].astype(jnp.float32) - mean) * inv_std
    out_ref[...] = (result - inv_std * (group_one + normed * group_two)).astype(jnp.bfloat16)
    sums_ref[...] = jnp.concatenate([one, two, c_one, c_two] + [jnp.zeros_like(one)] * 4, axis=0)


def total_kernel(scales, both_ref, result_ref, result_hbm, out_hbms, rows_ref, sems):
    copies = fetched([(result_ref, result_hbm)], sems)
    rows = sum(both_ref[k] for k in range(both_ref.shape[0]))
    for k in range(4):
        rows_ref[k] = rows[k : k + 1] * scales[k]
    for k in range(4):
        copies.append(pltpu.make_async_copy(rows_ref.at[k], out_hbms[k], sems.at[k + 1]))
        copies[-1].start()
    for copy in copies:
        copy.wait()


def in_vmem(count):
    return [pl.BlockSpec(memory_space=pltpu.VMEM)] * count


def in_hbm(count):
    return [pl.BlockSpec(memory_space=pltpu.HBM)] * count


def kept(array):
    return pltpu.with_memory_space_constraint(array, pltpu.HBM)


def shape_of(shape, kind):
    return jax.ShapeDtypeStruct(shape, kind)


LIMIT = pltpu.CompilerParams(vmem_limit_bytes=40 * 1024 * 1024)
COST = pl.CostEstimate(flops=2_000_000_000, bytes_accessed=4_000_000, transcendentals=0)


def fast_shards(
    plan,
    acts_fine,
    acts_coarse,
    grad_coarse,
    gain_fine,
    bias_fine,
    kernel_fine,
    gain_coarse,
    bias_coarse,
    kernel_coarse,
):
    nd = lax.axis_size("dp")
    count, sub, channels, places, local = plan.count, plan.sub, plan.channels, plan.places, plan.local
    f32, bf16 = jnp.float32, jnp.bfloat16
    rows = [part.reshape(1, channels) for part in (gain_coarse, bias_coarse, gain_fine, bias_fine)]
    packed, acts, columns, order, fine_order, by_column, rows = pl.pallas_call(
        functools.partial(pack_kernel, plan),
        out_shape=(
            shape_of((count, plan.block_rows, 128), bf16),
            shape_of((4 * local, channels), bf16),
            shape_of((4, 2 * sub, 128), f32),
            shape_of((4 * plan.nr * local, 4 * plan.nr * local), bf16),
            shape_of((4 * plan.nr * local, 4 * plan.nr * local), bf16),
            shape_of((places, places + places // 2), bf16),
            shape_of((4, 1, channels), f32),
        ),
        in_specs=in_hbm(7),
        out_specs=tuple(in_vmem(7)),
        scratch_shapes=[
            pltpu.VMEM((local, channels), bf16),
            pltpu.VMEM((local, channels), bf16),
            pltpu.SemaphoreType.DMA((7,)),
        ],
        compiler_params=LIMIT,
        cost_estimate=COST,
    )(
        kept(grad_coarse.reshape(local, channels)),
        kept(acts_coarse.reshape(local, channels)),
        kept(acts_fine.reshape(4 * local, channels)),
        *[kept(row) for row in rows],
    )
    got = lax.all_to_all(packed, BLOCK, 0, 0)
    mine, theirs, held, inv_std, fine_acts = pl.pallas_call(
        functools.partial(coarse_kernel, plan),
        out_shape=(
            shape_of((sub, places), f32),
            shape_of((sub + 8, places), bf16),
            shape_of((3, sub, places), f32),
            shape_of((sub, 128), f32),
            shape_of((4, 2 * sub, places // 2), f32),
        ),
        in_specs=in_vmem(5),
        out_specs=tuple(in_vmem(5)),
        scratch_shapes=[
            pltpu.VMEM((places + 2 * plan.image, channels // 2), bf16),
            pltpu.VMEM((18 * sub, places), f32),
            pltpu.VMEM((2 * sub, places), f32),
        ],
        compiler_params=LIMIT,
        cost_estimate=COST,
    )(got, kernel_coarse, columns, order, fine_order)
    both = lax.all_gather(theirs, "member")
    quartered, coarse_sums = pl.pallas_call(
        functools.partial(quarter_kernel, plan),
        out_shape=(shape_of((count, 2 * sub + sub // 2, 128), bf16), shape_of((2, 128), f32)),
        in_specs=in_vmem(6),
        out_specs=tuple(in_vmem(2)),
        compiler_params=LIMIT,
        cost_estimate=COST,
    )(mine, both, held, inv_std, columns, by_column)
    spread = lax.all_to_all(quartered, BLOCK, 0, 0)
    sent = pl.pallas_call(
        functools.partial(fine_kernel, plan),
        out_shape=shape_of((count, sub + 8, 128), bf16),
        in_specs=in_vmem(7),
        out_specs=in_vmem(1)[0],
        scratch_shapes=[
            pltpu.VMEM((channels, places // 2), bf16),
            pltpu.VMEM((channels, places // 2), bf16),
            pltpu.VMEM((18 * sub, places // 2), f32),
            pltpu.VMEM((6 * sub, places // 2), f32),
        ],
        compiler_params=LIMIT,
        cost_estimate=COST,
    )(spread, fine_acts, both, columns, fine_order, coarse_sums, kernel_fine)
    back = lax.all_to_all(sent, BLOCK, 0, 0)
    cells = nd * places
    fine_scale, coarse_scale = 1.0 / math.sqrt(4 * cells), 1.0 / math.sqrt(cells)
    out, sums = pl.pallas_call(
        functools.partial(spread_kernel, plan),
        out_shape=(pltpu.VMEM((4 * local, channels), bf16), shape_of((8, channels), f32)),
        in_specs=in_vmem(3),
        out_specs=tuple(in_vmem(2)),
        compiler_params=LIMIT,
        cost_estimate=COST,
    )(back, acts, rows)
    both = lax.all_gather(sums, "dp")
    out, sums = pl.pallas_call(
        functools.partial(total_kernel, (fine_scale, fine_scale, coarse_scale, coarse_scale)),
        out_shape=(pltpu.HBM((4 * local, channels), bf16), (pltpu.HBM((1, channels), f32),) * 4),
        in_specs=in_vmem(2),
        out_specs=(in_hbm(1)[0], tuple(in_hbm(4))),
        scratch_shapes=[pltpu.VMEM((4, 1, channels), f32), pltpu.SemaphoreType.DMA((5,))],
        compiler_params=LIMIT,
        cost_estimate=COST,
    )(both, out)
    bias_f, gain_f, bias_c, gain_c = [part.reshape(channels) for part in sums]
    return out.reshape(acts_fine.shape), gain_f, bias_f, gain_c, bias_c


def solution(mesh):
    def function(*arrays):
        local = [size // mesh.shape[axis] for size, axis in zip(arrays[1].shape, ("dp", "frames", "rows"))]
        sizes = (mesh.shape["frames"], mesh.shape["rows"])
        plan = Plan(sizes, (*local[1:], *arrays[1].shape[3:]), arrays[5].shape[1] // mesh.shape["rows"])
        if plan.fits:
            split = (mesh.shape["dp"], plan.nf // 2, 2, plan.nr)
            used = jax.sharding.Mesh(mesh.devices.reshape(split), ("dp", "pairs", "member", "rows"))
            shards, frames = functools.partial(fast_shards, plan), ("pairs", "member")
        else:
            used, shards, frames = mesh, plain_shards, "frames"
        blocks, kernel = P("dp", frames, "rows", None, None), P(None, "rows", None)
        in_specs = (blocks, blocks, blocks, P(), P(), kernel, P(), P(), kernel)
        out_specs = (blocks, P(), P(), P(), P())
        mapped = jax.shard_map(shards, mesh=used, in_specs=in_specs, out_specs=out_specs, check_vma=False)
        return mapped(*arrays)

    return function
```

```python
import functools
import math

import jax
import jax.numpy as jnp
from jax import lax
from jax.experimental import pallas as pl
from jax.experimental.pallas import tpu as pltpu
from jax.sharding import PartitionSpec as P

GROUPS = 32
EPSILON = 1e-06
BLOCK = ("rows", "pairs", "member")
PLAIN_BLOCK = ("frames", "rows")


def plain_everyone(block, count):
    copies = jnp.broadcast_to(block[None], (count,) + block.shape)
    return lax.all_to_all(copies, PLAIN_BLOCK, 0, 0)


def ahead(field, axis, distance):
    size = field.shape[axis]
    if distance == 0:
        return field
    widths = [(0, 0)] * field.ndim
    if distance > 0:
        widths[axis] = (0, distance)
        kept = lax.slice_in_dim(field, distance, size, axis=axis)
    else:
        widths[axis] = (-distance, 0)
        kept = lax.slice_in_dim(field, 0, size + distance, axis=axis)
    return jnp.pad(kept, widths)


def tap_products(source, kernel):
    sub = kernel.shape[1]
    frames, rows, cols, channels = source.shape
    products = lax.dot_general(
        kernel.reshape(27 * sub, channels),
        source.reshape(frames * rows * cols, channels),
        (((1,), (1,)), ((), ())),
        preferred_element_type=jnp.float32,
    ).reshape(3, 3, 3, sub, frames, rows, cols)
    return sum(ahead(products[depth], 3, 2 - depth) for depth in range(3))


def coarse_conv(source, kernel):
    spatial = tap_products(source, kernel)
    total = 0.0
    for row in range(3):
        part = sum(ahead(spatial[row, col], 3, 1 - col) for col in range(3))
        total = total + ahead(part, 2, 1 - row)
    return total


def fine_conv(source, kernel):
    spatial = tap_products(source, kernel)
    result = []
    for p in range(2):
        rows_of = []
        for q in range(2):
            total = 0.0
            for row in range(3):
                part = sum(ahead(spatial[row, col], 3, (q + 1 - col) // 2) for col in range(3))
                total = total + ahead(part, 2, (p + 1 - row) // 2)
            rows_of.append(total)
        result.append(jnp.stack(rows_of, 1))
    return jnp.stack(result, 1)


def group_total(sums, group_width):
    sub = sums.shape[-1]
    if sub % group_width == 0:
        grouped = jnp.sum(sums.reshape(-1, sub // group_width, group_width), axis=-1)
        return jnp.repeat(grouped, group_width, axis=-1)
    spread = jnp.moveaxis(lax.all_gather(sums, "frames"), 0, 1).reshape(sums.shape[0], -1, group_width)
    mine = lax.axis_index("frames") * sub // group_width
    grouped = lax.dynamic_index_in_dim(jnp.sum(spread, -1), mine, 1)
    return jnp.broadcast_to(grouped, sums.shape)


def level(acts, conv_grad, cotangent, gain, bias, group_width):
    sub = acts.shape[0]
    places = acts.size // sub
    values = acts.astype(jnp.float32).reshape(sub, places)
    conv_grad = conv_grad.reshape(sub, places)
    entries = places * group_width
    moments = group_total(
        jnp.stack([jnp.sum(values, 1), jnp.sum(values * values, 1)]), group_width
    ) / entries
    mean = moments[0]
    inv_std = lax.rsqrt(moments[1] - mean * mean + EPSILON)
    normed = (values - mean[:, None]) * inv_std[:, None]
    preact = gain[:, None] * normed + bias[:, None]
    squash = jax.nn.sigmoid(preact)
    pre_grad = conv_grad * squash * (1.0 + preact * (1.0 - squash))
    sums = jnp.stack([jnp.sum(pre_grad, 1), jnp.sum(pre_grad * normed, 1)])
    terms = group_total(sums * gain, group_width) / entries
    grad = cotangent.reshape(sub, places) + inv_std[:, None] * (
        gain[:, None] * pre_grad - terms[0][:, None] - normed * terms[1][:, None]
    )
    return grad, sums


def plain_shards(
    acts_fine,
    acts_coarse,
    grad_coarse,
    gain_fine,
    bias_fine,
    kernel_fine,
    gain_coarse,
    bias_coarse,
    kernel_coarse,
):
    nf, nr, nd = lax.axis_size("frames"), lax.axis_size("rows"), lax.axis_size("dp")
    count = nf * nr
    channels = acts_fine.shape[-1]
    slice_width = kernel_fine.shape[1]
    sub = slice_width // nf
    group_width = channels // GROUPS
    tl, hl, w = acts_coarse.shape[1:4]
    frames, rows = tl * nf, hl * nr
    f, r = lax.axis_index("frames"), lax.axis_index("rows")

    gathered = plain_everyone(grad_coarse[0], count)
    source = (
        gathered.reshape(nf, nr, tl, hl, w, channels)
        .transpose(0, 2, 1, 3, 4, 5)
        .reshape(frames, rows, w, channels)
    )
    coarse_in = acts_coarse[0].reshape(tl, hl, w, nr, nf, sub).transpose(4, 3, 5, 0, 1, 2)
    coarse_in = lax.all_to_all(coarse_in.reshape(count, sub, tl * hl * w), PLAIN_BLOCK, 0, 0)
    fine_in = acts_fine[0].reshape(tl, hl, 2, w, 2, nr, nf, sub).transpose(6, 5, 7, 2, 4, 0, 1, 3)
    fine_in = lax.all_to_all(fine_in.reshape(count, sub, 4 * tl * hl * w), PLAIN_BLOCK, 0, 0)

    def mine(vector):
        return lax.dynamic_slice_in_dim(vector, r * slice_width + f * sub, sub)

    def own(kernel):
        return lax.dynamic_slice_in_dim(kernel, f * sub, sub, axis=1)

    coarse_vals = (
        coarse_in.reshape(nf, nr, sub, tl, hl, w).transpose(2, 0, 3, 1, 4, 5).reshape(sub, frames, rows, w)
    )
    cot = lax.dynamic_slice_in_dim(source, r * slice_width + f * sub, sub, axis=3)
    cot = cot.astype(jnp.float32).transpose(3, 0, 1, 2)
    conv = coarse_conv(source, own(kernel_coarse))
    coarse_grad, coarse_sums = level(
        coarse_vals, conv, cot, mine(gain_coarse), mine(bias_coarse), group_width
    )
    quartered = (coarse_grad * 0.25).astype(jnp.bfloat16)
    spread = plain_everyone(quartered, count)
    source_fine = (
        spread.reshape(nf, nr, sub, frames, rows, w)
        .transpose(3, 4, 5, 1, 0, 2)
        .reshape(frames, rows, w, channels)
    )
    conv = fine_conv(source_fine, own(kernel_fine))
    fine_vals = (
        fine_in.reshape(nf, nr, sub, 2, 2, tl, hl, w)
        .transpose(2, 3, 4, 0, 5, 1, 6, 7)
        .reshape(sub, 2, 2, frames, rows, w)
    )
    cot = jnp.broadcast_to(
        quartered.astype(jnp.float32).reshape(sub, 1, 1, frames, rows, w), conv.shape
    )
    fine_grad, fine_sums = level(
        fine_vals, conv, cot, mine(gain_fine), mine(bias_fine), group_width
    )
    back = (
        fine_grad.astype(jnp.bfloat16)
        .reshape(sub, 2, 2, nf, tl, nr, hl, w)
        .transpose(3, 5, 0, 1, 2, 4, 6, 7)
        .reshape(count, sub, 4 * tl * hl * w)
    )
    sums = plain_everyone(jnp.concatenate([fine_sums, coarse_sums]), count)
    back = lax.all_to_all(back, PLAIN_BLOCK, 0, 0)
    out = (
        back.reshape(nf, nr, sub, 2, 2, tl, hl, w)
        .transpose(5, 6, 3, 7, 4, 1, 0, 2)
        .reshape(1, tl, 2 * hl, 2 * w, channels)
    )
    sums = sums.reshape(nf, nr, 4, sub).transpose(2, 1, 0, 3).reshape(4, channels)
    totals = lax.psum(sums, "dp")
    cells = nd * frames * rows * w
    scale_fine = 1.0 / jnp.sqrt(jnp.float32(4 * cells))
    scale_coarse = 1.0 / jnp.sqrt(jnp.float32(cells))
    return (
        out,
        totals[1] * scale_fine,
        totals[0] * scale_fine,
        totals[3] * scale_coarse,
        totals[2] * scale_coarse,
    )


def lanes_at(shape, axis):
    return lax.broadcasted_iota(jnp.int32, shape, axis)


def one_hot(found):
    return found.astype(jnp.float32).astype(jnp.bfloat16)


def pixel_order(plan, swapped):
    tl, hl, w = plan.tl, plan.hl, plan.w // 2
    size = 4 * plan.local
    lane = lanes_at((1, size), 1)
    j, i, t = lane % w, lane // w % hl, lane // (w * hl) % tl
    q, p = lane // (w * hl * tl) % 2, lane // (2 * w * hl * tl) % 2
    half = lane // (4 * w * hl * tl)
    if swapped:
        half = 1 - half
    pixel = (t * 2 * hl + 2 * i + p) * 4 * w + 2 * (half * w + j) + q
    return one_hot(lanes_at((size, size), 0) == pixel)


def merged_order(nr, outer, tl, cells):
    size = nr * outer * tl * cells
    lane = lanes_at((1, size), 1)
    cell, dev = lane % cells, lane // cells % nr
    t, o = lane // (cells * nr) % tl, lane // (cells * nr * tl)
    return one_hot(lanes_at((size, size), 0) == ((dev * outer + o) * tl + t) * cells + cell)


def column_order(plan):
    w = plan.w // 2
    lines = plan.places // plan.w
    lane = lanes_at((1, 4 * lines * w + 4 * lines), 1)
    inner = lane % (lines * w)
    place = inner // w * plan.w + lane // (lines * w) * w + inner % w
    past = lane - 2 * lines * w
    border = past % lines * plan.w + jnp.where(past < 2 * lines, w, w - 1)
    wanted = jnp.where(past >= 0, border, place)
    shape = (plan.places, 2 * lines * w + 4 * lines)
    return one_hot(lanes_at(shape, 0) == wanted[:, : shape[1]])


def one_hot_dot(a, b, dims):
    return lax.dot_general(a, b, (dims, ((), ())), preferred_element_type=jnp.float32)


def moved(field, distance, kept):
    size = field.shape[1]
    return jnp.where(kept, pltpu.roll(field, (-distance) % size, 1), 0.0)


def own_column(row, base, sub):
    shape = (sub, row.shape[1])
    mine = lanes_at(shape, 1) == lanes_at(shape, 0) + base
    return jnp.sum(jnp.where(mine, row, 0.0), axis=1, keepdims=True)


def as_row(column):
    shape = (column.shape[0], 128)
    here = lanes_at(shape, 1) == lanes_at(shape, 0)
    return jnp.sum(jnp.where(here, column, 0.0), axis=0, keepdims=True)


def terms(value, count):
    found = []
    for _ in range(count):
        found.append(value.astype(jnp.bfloat16).astype(jnp.float32))
        value = value - found[-1]
    return found


def in_groups(column, group_width):
    sub = column.shape[0]
    grouped = jnp.sum(column.reshape(sub // group_width, group_width, 1), axis=1, keepdims=True)
    return jnp.broadcast_to(grouped, (sub // group_width, group_width, 1)).reshape(sub, 1)


def in_lane_groups(row, group_width):
    lane = lanes_at(row.shape, 1)
    size = row.shape[1]
    step = 1
    while step < group_width:
        up, down = pltpu.roll(row, size - step, 1), pltpu.roll(row, step, 1)
        row = row + jnp.where(lane // step % 2 == 0, up, down)
        step *= 2
    return row


def total(parts):
    return sum(jnp.sum(part, axis=1, keepdims=True) for part in parts)


def statistics(one, two, entries, group_width):
    mean = in_groups(one, group_width) / entries
    square = in_groups(two, group_width) / entries
    return mean, lax.rsqrt(square - mean * mean + EPSILON)


def normalised(parts, gain, bias, mean, inv_std):
    normed, slope = [], []
    for part in parts:
        unit = (part - mean) * inv_std
        preact = gain * unit + bias
        squash = jax.nn.sigmoid(preact)
        normed.append(unit)
        slope.append(squash * (1.0 + preact * (1.0 - squash)))
    return normed, slope


class Plan:
    def __init__(self, mesh_sizes, acts_coarse, slice_width):
        self.nf, self.nr = mesh_sizes
        self.count = self.nf * self.nr
        self.tl, self.hl, self.w, self.channels = acts_coarse
        self.slice_width = slice_width
        self.sub = slice_width // self.nf
        self.cells = self.hl * self.w
        self.local = self.tl * self.cells
        self.image = self.cells * self.nr
        self.frames = self.tl * self.nf
        self.places = self.frames * self.image
        self.group_width = self.channels // GROUPS
        self.chunks = self.channels // 128
        self.acts_at = self.chunks // 2 * self.local
        self.packed_at = self.acts_at + self.sub
        self.cot_at = self.packed_at + 8
        self.block_rows = self.cot_at + 8
        self.fits = (
            self.sub == 32
            and self.slice_width == 128
            and self.group_width == 16
            and self.cells == 16
            and self.w == 8
            and self.tl == 2
            and self.nr == 4
            and self.nf == 4
            and self.slice_width * self.nr == self.channels
        )

    def place_masks(self, w):
        lane = lanes_at((1, self.places // self.w * w), 1)
        col, row = lane % w, lane // w % (self.hl * self.nr)
        last_row = self.hl * self.nr - 1
        return (lane, col > 0, col < w - 1, row > 0, row < last_row)


def fetched(pairs, sems):
    copies = [pltpu.make_async_copy(src, dst, sems.at[k]) for k, (src, dst) in enumerate(pairs)]
    for copy in copies:
        copy.start()
    return copies


def own_place(plan):
    pair, member, r = lax.axis_index("pairs"), lax.axis_index("member"), lax.axis_index("rows")
    return pair, member, r, r * plan.slice_width + (2 * pair + member) * plan.sub


def pack_kernel(plan, g_hbm, coarse_hbm, fine_hbm, out_ref, fine_ref, g_ref, coarse_ref, sems):
    sub, chunks, local = plan.sub, plan.chunks, plan.local
    copies = fetched([(fine_hbm, fine_ref), (coarse_hbm, coarse_ref), (g_hbm, g_ref)], sems)
    shape = (2 * local, 2 * 128)
    lane = lanes_at((1, 2 * 128), 1)
    repeated = one_hot(lanes_at(shape, 0) == lane % local + lane // 128 * local)
    shape = (plan.channels, 128)
    quarter = lanes_at(shape, 0) // 8 % 4 == lanes_at(shape, 1) // local
    orders = jnp.concatenate([pixel_order(plan, swapped) for swapped in (False, True)], axis=1)
    copies[0].wait()
    acts = fine_ref[...]
    halves = one_hot_dot(acts, orders, ((0,), (0,))).astype(jnp.bfloat16)
    halves = [halves[:, :128], halves[:, 128:]]
    copies[1].wait()
    copies[2].wait()
    small = one_hot_dot(jnp.concatenate([coarse_ref[...], g_ref[...]], axis=0), repeated, ((0,), (0,)))
    for k, at in enumerate((plan.packed_at, plan.cot_at)):
        rows_of = jnp.where(quarter, small[:, k * 128 : (k + 1) * 128], 0.0).reshape(plan.count, 4, 8, 128)
        out_ref[:, at : at + 8, :] = jnp.sum(rows_of, axis=1).astype(jnp.bfloat16)
    low = lanes_at((sub, 128), 1) < 64
    for s_r in range(plan.nr):
        for s_f in range(plan.nf):
            dest = s_r * plan.nf + s_f
            first, half = s_r * plan.slice_width + s_f // 2 * 2 * sub, s_f % 2
            for k in range(chunks // 2):
                at = (half * chunks // 2 + k) * 128
                out_ref[dest, k * local : (k + 1) * local, :] = g_ref[:, at : at + 128]
            upper, lower = halves[half][first : first + sub], halves[1 - half][first + sub : first + 2 * sub]
            out_ref[dest, plan.acts_at : plan.packed_at, :] = jnp.where(low, upper, lower)


def by_frame_device(plan, got_ref, at, height):
    return jnp.concatenate(
        [
            jnp.concatenate(
                [got_ref[r * plan.nf + f, at : at + height, :] for r in range(plan.nr)], axis=1
            )
            for f in range(plan.nf)
        ],
        axis=0,
    )


def in_places(plan, merged, height):
    width = plan.tl * plan.image
    return [
        jnp.concatenate(
            [merged[f * height : (f + 1) * height, k * width : (k + 1) * width] for f in range(plan.nf)],
            axis=1,
        )
        for k in range(4)
    ]


def coarse_kernel(
    plan,
    got_ref,
    weights,
    gain_c,
    bias_c,
    gain_f,
    bias_f,
    mine_ref,
    sent_ref,
    held_ref,
    inv_ref,
    fine_ref,
    columns,
    fine_order,
    by_column,
    order,
    source,
    products,
    conv_ref,
):
    sub, nr, nf, cells, tl, local = plan.sub, plan.nr, plan.nf, plan.cells, plan.tl, plan.local
    wide, depth = 2 * sub, plan.channels // 2
    pair, member, r, base = own_place(plan)
    first = r * plan.slice_width + pair * wide
    columns[0, 0:sub, :] = jnp.broadcast_to(own_column(gain_c[...], base, sub), (sub, 128))
    columns[1, 0:sub, :] = jnp.broadcast_to(own_column(bias_c[...], base, sub), (sub, 128))
    columns[2] = jnp.broadcast_to(own_column(gain_f[...], first, wide), (wide, 128))
    columns[3] = jnp.broadcast_to(own_column(bias_f[...], first, wide), (wide, 128))
    order[...] = merged_order(plan.nr, 4, plan.tl, plan.cells)
    fine_order[...] = merged_order(plan.nr, 8, plan.tl, plan.cells // 2)
    by_column[...] = column_order(plan)
    both = pl.ds(pl.multiple_of(pair * wide, wide), wide)
    half = pl.ds(pl.multiple_of(member * depth, depth), depth)
    for s_f in range(nf):
        for s_r in range(nr):
            for t in range(tl):
                at = (s_f * tl + t) * plan.image + s_r * cells
                for k in range(plan.chunks // 2):
                    source[at : at + cells, k * 128 : (k + 1) * 128] = got_ref[
                        s_r * nf + s_f, k * local + t * cells : k * local + (t + 1) * cells, :
                    ]
    source[plan.places :, :] = jnp.zeros((2 * plan.image, depth), jnp.bfloat16)
    products[...] = sum(
        one_hot_dot(
            weights[9 * k : 9 * k + 9, both, half].reshape(9 * wide, depth),
            source[(2 - k) * plan.image : (2 - k) * plan.image + plan.places, :],
            ((1,), (1,)),
        )
        for k in range(3)
    )
    merged = one_hot_dot(by_frame_device(plan, got_ref, plan.acts_at, sub), fine_order[...], ((1,), (0,)))
    parts = halves_at(plan, merged)
    for pq in range(4):
        fine_ref[pq] = parts[pq]
    one, two = total(parts), total([part * part for part in parts])
    stats = terms(as_row(one) + pltpu.roll(as_row(two), 64, 1), 3)
    stats = jnp.concatenate(stats + [jnp.zeros_like(stats[0])] * 5, axis=0).astype(jnp.bfloat16)
    found = []
    for at in (plan.packed_at, plan.cot_at):
        merged = one_hot_dot(by_frame_device(plan, got_ref, at, 8), order[...], ((1,), (0,)))
        found.append(jnp.concatenate(in_places(plan, merged, 8), axis=0))
    values, cot = found
    gain, bias = columns[0][0:sub, 0:1], columns[1][0:sub, 0:1]
    entries = plan.places * plan.group_width
    mean, inv_std = statistics(total([values]), total([values * values]), entries, plan.group_width)
    (normed,), (slope,) = normalised([values], gain, bias, mean, inv_std)
    held_ref[0], held_ref[1], held_ref[2] = normed, slope, cot
    inv_ref[...] = jnp.broadcast_to(inv_std, (sub, 128))
    lane, has_left, has_right, has_up, has_down = plan.place_masks(plan.w)
    by_col = []
    for col in range(3):
        parts = [products[pl.ds((3 * row + col) * wide, wide), :] for row in range(3)]
        by_col.append(parts[1] + moved(parts[0], plan.w, has_down) + moved(parts[2], -plan.w, has_up))
    conv_ref[...] = by_col[1] + moved(by_col[0], 1, has_right) + moved(by_col[2], -1, has_left)
    mine_ref[...] = conv_ref[pl.ds(pl.multiple_of(member * sub, sub), sub), :]
    theirs = conv_ref[pl.ds(pl.multiple_of((1 - member) * sub, sub), sub), :]
    sent_ref[0:sub, :] = theirs.astype(jnp.bfloat16)
    sent_ref[sub:, 0:128] = stats
    sent_ref[sub:, 128:] = jnp.zeros((8, plan.places - 128), jnp.bfloat16)


def quarter_kernel(plan, mine_ref, both_ref, held_ref, inv_ref, columns, by_column, out_ref, sums_ref):
    sub = plan.sub
    _, member, _, _ = own_place(plan)
    conv = mine_ref[...] + both_ref[1 - member, 0:sub, :].astype(jnp.float32)
    normed, slope, cot = held_ref[0], held_ref[1], held_ref[2]
    gain, inv_std = columns[0][0:sub, 0:1], inv_ref[:, 0:1]
    entries = plan.places * plan.group_width
    pre = conv * slope
    one, two = total([pre]), total([pre * normed])
    group_one = in_groups(gain * one, plan.group_width) / entries
    group_two = in_groups(gain * two, plan.group_width) / entries
    grad = cot + inv_std * (gain * pre - group_one - normed * group_two)
    quartered = (grad * 0.25).astype(jnp.bfloat16)
    sent = one_hot_dot(quartered, by_column[...], ((1,), (0,))).astype(jnp.bfloat16)
    low = lanes_at((sub // 2, 128), 1) < 64
    for half in range(2):
        at = half * 256
        border = sent[:, 512 + half * 128 : 640 + half * 128]
        border = jnp.where(low, border[: sub // 2], border[sub // 2 :])
        for dest in range(half, plan.count, 2):
            out_ref[dest, 0:sub, :] = sent[:, at : at + 128]
            out_ref[dest, sub : 2 * sub, :] = sent[:, at + 128 : at + 256]
            out_ref[dest, 2 * sub : 2 * sub + sub // 2, :] = border
    sums_ref[...] = jnp.concatenate([as_row(one), as_row(two)], axis=0)


def halves_at(plan, merged):
    sub = plan.sub
    turned = jnp.concatenate([pltpu.roll(merged[:, k * 128 : (k + 1) * 128], 64, 1) for k in range(4)], axis=1)
    low = lanes_at((sub, 128), 1) < 64
    parts = []
    for pq in range(4):
        groups = []
        for group in range(2):
            e = 4 * group + pq
            at = e // 2 * 128
            strips = []
            for m in range(plan.nf // 2):
                first, second = slice(2 * m * sub, (2 * m + 1) * sub), slice((2 * m + 1) * sub, (2 * m + 2) * sub)
                if e % 2 == 0:
                    strips.append(jnp.where(low, merged[first, at : at + 128], turned[second, at : at + 128]))
                else:
                    strips.append(jnp.where(low, turned[first, at : at + 128], merged[second, at : at + 128]))
            groups.append(jnp.concatenate(strips, axis=1))
        parts.append(jnp.concatenate(groups, axis=0))
    return parts


def halves_from(plan, parts):
    sub = plan.sub
    low = lanes_at((sub, 128), 1) < 64
    down = []
    for f in range(plan.nf):
        across = []
        for v in range(4):
            pair = []
            for e in (2 * v, 2 * v + 1):
                group, pq = e // 4, e % 4
                strip = parts[pq][group * sub : (group + 1) * sub, f // 2 * 128 : (f // 2 + 1) * 128]
                pair.append(strip if e % 2 == f % 2 else pltpu.roll(strip, 64, 1))
            across.append(jnp.where(low, pair[0], pair[1]))
        down.append(jnp.concatenate(across, axis=1))
    return jnp.concatenate(down, axis=0)


def fine_kernel(
    plan, got_ref, acts_ref, both_ref, columns, order, sums_ref, weights, out_ref, source, border, products, beyond
):
    sub, nr, nf, wide = plan.sub, plan.nr, plan.nf, 2 * plan.sub
    pair, member, r, _ = own_place(plan)
    both = pl.ds(pl.multiple_of(pair * wide, wide), wide)
    w = plan.w // 2
    lines = plan.places // plan.w
    places = lines * w
    for k in range(2):
        source[:, k * 128 : (k + 1) * 128] = got_ref[:, k * sub : (k + 1) * sub, :].reshape(plan.channels, 128)
    packed = got_ref[:, wide : wide + sub // 2, :].reshape(plan.count * sub // 2, 128)
    shape = (128, places)
    beside = lanes_at(shape, 1) == lanes_at(shape, 0) % lines * w + (1 - member) * (w - 1)
    for k in range(2):
        here = one_hot(beside & (lanes_at(shape, 0) // lines == k))
        found = one_hot_dot(packed, here, ((1,), (0,))).astype(jnp.bfloat16)
        for s in range(plan.count):
            border[s * sub + k * (sub // 2) : s * sub + (k + 1) * (sub // 2), :] = found[
                s * (sub // 2) : (s + 1) * (sub // 2)
            ]
    image = plan.image // 2
    sums, extras = 0.0, 0.0
    for k in (2, 1, 0):
        here, beside = source[...], border[...]
        if k < 2:
            shift = (2 - k) * image
            inside = lanes_at((1, places), 1) < places - shift
            here, beside = [
                jnp.where(inside, pltpu.roll(part, places - shift, 1), jnp.zeros_like(part)) for part in (here, beside)
            ]
        sums = sums + one_hot_dot(
            weights[9 * k : 9 * k + 9, both, :].reshape(9 * wide, plan.channels), here, ((1,), (0,))
        )
        facing = jnp.concatenate([weights[9 * k + 3 * row + 2 * member, both, :] for row in range(3)], axis=0)
        extras = extras + one_hot_dot(facing, beside, ((1,), (0,)))
    products[...], beyond[...] = sums, extras
    parts = [acts_ref[pq] for pq in range(4)]
    stats = sum(both_ref[k, sub : sub + 8, 0:128].astype(jnp.float32) for k in range(2))
    stats = stats[0:1] + stats[1:2] + stats[2:3]
    entries = 4 * plan.places * plan.group_width
    one, two = own_column(stats, 0, wide), own_column(stats, 64, wide)
    mean, inv_std = statistics(one, two, entries, plan.group_width)
    gain, bias = columns[2][:, 0:1], columns[3][:, 0:1]
    normed, slope = normalised(parts, gain, bias, mean, inv_std)
    lane, has_left, has_right, has_up, has_down = plan.place_masks(w)
    right, left = (1 - member).astype(jnp.float32), member.astype(jnp.float32)
    by_row = []
    for row in range(3):
        a, b, c = [products[pl.ds((3 * row + col) * wide, wide), :] for col in range(3)]
        extra = beyond[pl.ds(row * wide, wide), :]
        by_row.append(
            (a + b + moved(c, -1, has_left) + left * extra, moved(a, 1, has_right) + b + c + right * extra)
        )
    convs = [by_row[0][q] + by_row[1][q] + moved(by_row[2][q], -w, has_up) for q in range(2)]
    convs += [moved(by_row[0][q], w, has_down) + by_row[1][q] + by_row[2][q] for q in range(2)]
    pre = [conv * part for conv, part in zip(convs, slope)]
    one = total(pre)
    two = total([a * b for a, b in zip(pre, normed)])
    cot = source[pl.ds(pl.multiple_of(r * plan.slice_width + pair * wide, wide), wide), :].astype(jnp.float32)
    scale = inv_std * gain
    stacked = halves_from(plan, [cot + scale * part for part in pre]).astype(jnp.bfloat16)
    sent = one_hot_dot(stacked, order[...], ((1,), (1,))).astype(jnp.bfloat16)
    coarse = sums_ref[0:1] + pltpu.roll(sums_ref[1:2], sub, 1)
    coded = (
        terms(as_row(one) + pltpu.roll(as_row(two), 64, 1), 2)
        + terms(coarse, 2)
        + terms(as_row(inv_std) + pltpu.roll(as_row(mean), 64, 1), 3)
    )
    coded = jnp.concatenate(coded + [jnp.zeros_like(coarse)], axis=0).astype(jnp.bfloat16)
    for s_r in range(nr):
        for s_f in range(nf):
            out_ref[s_r * nf + s_f, 0:sub, :] = sent[s_f * sub : (s_f + 1) * sub, s_r * 128 : (s_r + 1) * 128]
            out_ref[s_r * nf + s_f, sub : sub + 8, :] = coded


def spread_kernel(plan, got_ref, acts_ref, gain_ref, out_ref, sums_ref):
    sub, nr, nf = plan.sub, plan.nr, plan.nf
    low = lanes_at((sub, 128), 1) < 64
    low_row = lanes_at((1, 128), 1) < 64
    first_row = lanes_at((1, 128), 1) < sub
    source = []
    fine, coarse, moments = [[], []], [[], []], [[], []]
    for s_r in range(nr):
        ones, twos, c_ones, c_twos, invs, means = [], [], 0.0, 0.0, [], []
        for pair in range(nf // 2):
            at = s_r * nf + 2 * pair
            left, right = [got_ref[at + k, 0:sub, :].astype(jnp.float32) for k in range(2)]
            source.append(jnp.where(low, left, pltpu.roll(right, 64, 1)))
            source.append(jnp.where(low, pltpu.roll(left, 64, 1), right))
            coded = [got_ref[at + k, sub : sub + 8, :].astype(jnp.float32) for k in range(2)]
            sums = coded[0][0:1] + coded[0][1:2] + coded[1][0:1] + coded[1][1:2]
            ones.append(sums if pair == 0 else pltpu.roll(sums, 64, 1))
            twos.append(pltpu.roll(sums, 64, 1) if pair == 0 else sums)
            both = coded[0][4:5] + coded[0][5:6] + coded[0][6:7]
            invs.append(both if pair == 0 else pltpu.roll(both, 64, 1))
            means.append(pltpu.roll(both, 64, 1) if pair == 0 else both)
            for k in range(2):
                sums = coded[k][2:3] + coded[k][3:4]
                to = (2 * pair + k) * sub
                c_one = jnp.where(first_row, sums, 0.0)
                c_two = jnp.where(first_row, pltpu.roll(sums, 128 - sub, 1), 0.0)
                c_ones = c_ones + (pltpu.roll(c_one, to, 1) if to else c_one)
                c_twos = c_twos + (pltpu.roll(c_two, to, 1) if to else c_two)
        fine[0].append(jnp.where(low_row, ones[0], ones[1]))
        fine[1].append(jnp.where(low_row, twos[0], twos[1]))
        moments[0].append(jnp.where(low_row, invs[0], invs[1]))
        moments[1].append(jnp.where(low_row, means[0], means[1]))
        coarse[0].append(c_ones)
        coarse[1].append(c_twos)
    one, two, inv_std, mean, c_one, c_two = [jnp.concatenate(part, axis=1) for part in fine + moments + coarse]
    source = jnp.concatenate(source, axis=0).astype(jnp.bfloat16)
    result = one_hot_dot(pixel_order(plan, False), source, ((1,), (1,)))
    gain = gain_ref[...]
    entries = 4 * plan.places * plan.group_width
    group_one = in_lane_groups(gain * one, plan.group_width) / entries
    group_two = in_lane_groups(gain * two, plan.group_width) / entries
    normed = (acts_ref[...].astype(jnp.float32) - mean) * inv_std
    out_ref[...] = (result - inv_std * (group_one + normed * group_two)).astype(jnp.bfloat16)
    sums_ref[...] = jnp.concatenate([one, two, c_one, c_two] + [jnp.zeros_like(one)] * 4, axis=0)


def total_kernel(scales, both_ref, result_ref, result_hbm, out_hbms, rows_ref, sems):
    copies = fetched([(result_ref, result_hbm)], sems)
    rows = sum(both_ref[k] for k in range(both_ref.shape[0]))
    for k in range(4):
        rows_ref[k] = rows[k : k + 1] * scales[k]
    for k in range(4):
        copies.append(pltpu.make_async_copy(rows_ref.at[k], out_hbms[k], sems.at[k + 1]))
        copies[-1].start()
    for copy in copies:
        copy.wait()


def in_vmem(count):
    return [pl.BlockSpec(memory_space=pltpu.VMEM)] * count


def in_hbm(count):
    return [pl.BlockSpec(memory_space=pltpu.HBM)] * count


def kept(array):
    return pltpu.with_memory_space_constraint(array, pltpu.HBM)


def shape_of(shape, kind):
    return jax.ShapeDtypeStruct(shape, kind)


LIMIT = pltpu.CompilerParams(vmem_limit_bytes=40 * 1024 * 1024)
COST = pl.CostEstimate(flops=2_000_000_000, bytes_accessed=4_000_000, transcendentals=0)


def fast_shards(
    plan,
    acts_fine,
    acts_coarse,
    grad_coarse,
    gain_fine,
    bias_fine,
    kernel_fine,
    gain_coarse,
    bias_coarse,
    kernel_coarse,
):
    nd = lax.axis_size("dp")
    count, sub, channels, places, local = plan.count, plan.sub, plan.channels, plan.places, plan.local
    f32, bf16 = jnp.float32, jnp.bfloat16
    rows = [part.reshape(1, channels) for part in (gain_coarse, bias_coarse, gain_fine, bias_fine)]
    packed, acts = pl.pallas_call(
        functools.partial(pack_kernel, plan),
        out_shape=(
            shape_of((count, plan.block_rows, 128), bf16),
            shape_of((4 * local, channels), bf16),
        ),
        in_specs=in_hbm(3),
        out_specs=tuple(in_vmem(2)),
        scratch_shapes=[
            pltpu.VMEM((local, channels), bf16),
            pltpu.VMEM((local, channels), bf16),
            pltpu.SemaphoreType.DMA((3,)),
        ],
        compiler_params=LIMIT,
        cost_estimate=COST,
    )(
        kept(grad_coarse.reshape(local, channels)),
        kept(acts_coarse.reshape(local, channels)),
        kept(acts_fine.reshape(4 * local, channels)),
    )
    packed, kernel_coarse = lax.optimization_barrier((packed, kernel_coarse))
    got = lax.all_to_all(packed, BLOCK, 0, 0)
    mine, theirs, held, inv_std, fine_acts, columns, fine_order, by_column = pl.pallas_call(
        functools.partial(coarse_kernel, plan),
        out_shape=(
            shape_of((sub, places), f32),
            shape_of((sub + 8, places), bf16),
            shape_of((3, sub, places), f32),
            shape_of((sub, 128), f32),
            shape_of((4, 2 * sub, places // 2), f32),
            shape_of((4, 2 * sub, 128), f32),
            shape_of((4 * plan.nr * local, 4 * plan.nr * local), bf16),
            shape_of((places, places + places // 2), bf16),
        ),
        in_specs=in_vmem(6),
        out_specs=tuple(in_vmem(8)),
        scratch_shapes=[
            pltpu.VMEM((4 * plan.nr * local, 4 * plan.nr * local), bf16),
            pltpu.VMEM((places + 2 * plan.image, channels // 2), bf16),
            pltpu.VMEM((18 * sub, places), f32),
            pltpu.VMEM((2 * sub, places), f32),
        ],
        compiler_params=LIMIT,
        cost_estimate=COST,
    )(got, kernel_coarse, *rows)
    both = lax.all_gather(theirs, "member")
    quartered, coarse_sums = pl.pallas_call(
        functools.partial(quarter_kernel, plan),
        out_shape=(shape_of((count, 2 * sub + sub // 2, 128), bf16), shape_of((2, 128), f32)),
        in_specs=in_vmem(6),
        out_specs=tuple(in_vmem(2)),
        compiler_params=LIMIT,
        cost_estimate=COST,
    )(mine, both, held, inv_std, columns, by_column)
    spread = lax.all_to_all(quartered, BLOCK, 0, 0)
    sent = pl.pallas_call(
        functools.partial(fine_kernel, plan),
        out_shape=shape_of((count, sub + 8, 128), bf16),
        in_specs=in_vmem(7),
        out_specs=in_vmem(1)[0],
        scratch_shapes=[
            pltpu.VMEM((channels, places // 2), bf16),
            pltpu.VMEM((channels, places // 2), bf16),
            pltpu.VMEM((18 * sub, places // 2), f32),
            pltpu.VMEM((6 * sub, places // 2), f32),
        ],
        compiler_params=LIMIT,
        cost_estimate=COST,
    )(spread, fine_acts, both, columns, fine_order, coarse_sums, kernel_fine)
    back = lax.all_to_all(sent, BLOCK, 0, 0)
    cells = nd * places
    fine_scale, coarse_scale = 1.0 / math.sqrt(4 * cells), 1.0 / math.sqrt(cells)
    out, sums = pl.pallas_call(
        functools.partial(spread_kernel, plan),
        out_shape=(pltpu.VMEM((4 * local, channels), bf16), shape_of((8, channels), f32)),
        in_specs=in_vmem(3),
        out_specs=tuple(in_vmem(2)),
        compiler_params=LIMIT,
        cost_estimate=COST,
    )(back, acts, rows[2])
    both = lax.all_gather(sums, "dp")
    out, sums = pl.pallas_call(
        functools.partial(total_kernel, (fine_scale, fine_scale, coarse_scale, coarse_scale)),
        out_shape=(pltpu.HBM((4 * local, channels), bf16), (pltpu.HBM((1, channels), f32),) * 4),
        in_specs=in_vmem(2),
        out_specs=(in_hbm(1)[0], tuple(in_hbm(4))),
        scratch_shapes=[pltpu.VMEM((4, 1, channels), f32), pltpu.SemaphoreType.DMA((5,))],
        compiler_params=LIMIT,
        cost_estimate=COST,
    )(both, out)
    bias_f, gain_f, bias_c, gain_c = [part.reshape(channels) for part in sums]
    return out.reshape(acts_fine.shape), gain_f, bias_f, gain_c, bias_c


def solution(mesh):
    def function(*arrays):
        local = [size // mesh.shape[axis] for size, axis in zip(arrays[1].shape, ("dp", "frames", "rows"))]
        sizes = (mesh.shape["frames"], mesh.shape["rows"])
        plan = Plan(sizes, (*local[1:], *arrays[1].shape[3:]), arrays[5].shape[1] // mesh.shape["rows"])
        if plan.fits:
            split = (mesh.shape["dp"], plan.nf // 2, 2, plan.nr)
            used = jax.sharding.Mesh(mesh.devices.reshape(split), ("dp", "pairs", "member", "rows"))
            shards, frames = functools.partial(fast_shards, plan), ("pairs", "member")
        else:
            used, shards, frames = mesh, plain_shards, "frames"
        blocks, kernel = P("dp", frames, "rows", None, None), P(None, "rows", None)
        in_specs = (blocks, blocks, blocks, P(), P(), kernel, P(), P(), kernel)
        out_specs = (blocks, P(), P(), P(), P())
        mapped = jax.shard_map(shards, mesh=used, in_specs=in_specs, out_specs=out_specs, check_vma=False)
        return mapped(*arrays)

    return function
```

```python
import functools
import math

import jax
import jax.numpy as jnp
from jax import lax
from jax.experimental import pallas as pl
from jax.experimental.pallas import tpu as pltpu
from jax.sharding import PartitionSpec as P

GROUPS = 32
EPSILON = 1e-06
BLOCK = ("rows", "pairs", "member")
PLAIN_BLOCK = ("frames", "rows")


def plain_everyone(block, count):
    copies = jnp.broadcast_to(block[None], (count,) + block.shape)
    return lax.all_to_all(copies, PLAIN_BLOCK, 0, 0)


def ahead(field, axis, distance):
    size = field.shape[axis]
    if distance == 0:
        return field
    widths = [(0, 0)] * field.ndim
    if distance > 0:
        widths[axis] = (0, distance)
        kept = lax.slice_in_dim(field, distance, size, axis=axis)
    else:
        widths[axis] = (-distance, 0)
        kept = lax.slice_in_dim(field, 0, size + distance, axis=axis)
    return jnp.pad(kept, widths)


def tap_products(source, kernel):
    sub = kernel.shape[1]
    frames, rows, cols, channels = source.shape
    products = lax.dot_general(
        kernel.reshape(27 * sub, channels),
        source.reshape(frames * rows * cols, channels),
        (((1,), (1,)), ((), ())),
        preferred_element_type=jnp.float32,
    ).reshape(3, 3, 3, sub, frames, rows, cols)
    return sum(ahead(products[depth], 3, 2 - depth) for depth in range(3))


def coarse_conv(source, kernel):
    spatial = tap_products(source, kernel)
    total = 0.0
    for row in range(3):
        part = sum(ahead(spatial[row, col], 3, 1 - col) for col in range(3))
        total = total + ahead(part, 2, 1 - row)
    return total


def fine_conv(source, kernel):
    spatial = tap_products(source, kernel)
    result = []
    for p in range(2):
        rows_of = []
        for q in range(2):
            total = 0.0
            for row in range(3):
                part = sum(ahead(spatial[row, col], 3, (q + 1 - col) // 2) for col in range(3))
                total = total + ahead(part, 2, (p + 1 - row) // 2)
            rows_of.append(total)
        result.append(jnp.stack(rows_of, 1))
    return jnp.stack(result, 1)


def group_total(sums, group_width):
    sub = sums.shape[-1]
    if sub % group_width == 0:
        grouped = jnp.sum(sums.reshape(-1, sub // group_width, group_width), axis=-1)
        return jnp.repeat(grouped, group_width, axis=-1)
    spread = jnp.moveaxis(lax.all_gather(sums, "frames"), 0, 1).reshape(sums.shape[0], -1, group_width)
    mine = lax.axis_index("frames") * sub // group_width
    grouped = lax.dynamic_index_in_dim(jnp.sum(spread, -1), mine, 1)
    return jnp.broadcast_to(grouped, sums.shape)


def level(acts, conv_grad, cotangent, gain, bias, group_width):
    sub = acts.shape[0]
    places = acts.size // sub
    values = acts.astype(jnp.float32).reshape(sub, places)
    conv_grad = conv_grad.reshape(sub, places)
    entries = places * group_width
    moments = group_total(
        jnp.stack([jnp.sum(values, 1), jnp.sum(values * values, 1)]), group_width
    ) / entries
    mean = moments[0]
    inv_std = lax.rsqrt(moments[1] - mean * mean + EPSILON)
    normed = (values - mean[:, None]) * inv_std[:, None]
    preact = gain[:, None] * normed + bias[:, None]
    squash = jax.nn.sigmoid(preact)
    pre_grad = conv_grad * squash * (1.0 + preact * (1.0 - squash))
    sums = jnp.stack([jnp.sum(pre_grad, 1), jnp.sum(pre_grad * normed, 1)])
    terms = group_total(sums * gain, group_width) / entries
    grad = cotangent.reshape(sub, places) + inv_std[:, None] * (
        gain[:, None] * pre_grad - terms[0][:, None] - normed * terms[1][:, None]
    )
    return grad, sums


def plain_shards(
    acts_fine,
    acts_coarse,
    grad_coarse,
    gain_fine,
    bias_fine,
    kernel_fine,
    gain_coarse,
    bias_coarse,
    kernel_coarse,
):
    nf, nr, nd = lax.axis_size("frames"), lax.axis_size("rows"), lax.axis_size("dp")
    count = nf * nr
    channels = acts_fine.shape[-1]
    slice_width = kernel_fine.shape[1]
    sub = slice_width // nf
    group_width = channels // GROUPS
    tl, hl, w = acts_coarse.shape[1:4]
    frames, rows = tl * nf, hl * nr
    f, r = lax.axis_index("frames"), lax.axis_index("rows")

    gathered = plain_everyone(grad_coarse[0], count)
    source = (
        gathered.reshape(nf, nr, tl, hl, w, channels)
        .transpose(0, 2, 1, 3, 4, 5)
        .reshape(frames, rows, w, channels)
    )
    coarse_in = acts_coarse[0].reshape(tl, hl, w, nr, nf, sub).transpose(4, 3, 5, 0, 1, 2)
    coarse_in = lax.all_to_all(coarse_in.reshape(count, sub, tl * hl * w), PLAIN_BLOCK, 0, 0)
    fine_in = acts_fine[0].reshape(tl, hl, 2, w, 2, nr, nf, sub).transpose(6, 5, 7, 2, 4, 0, 1, 3)
    fine_in = lax.all_to_all(fine_in.reshape(count, sub, 4 * tl * hl * w), PLAIN_BLOCK, 0, 0)

    def mine(vector):
        return lax.dynamic_slice_in_dim(vector, r * slice_width + f * sub, sub)

    def own(kernel):
        return lax.dynamic_slice_in_dim(kernel, f * sub, sub, axis=1)

    coarse_vals = (
        coarse_in.reshape(nf, nr, sub, tl, hl, w).transpose(2, 0, 3, 1, 4, 5).reshape(sub, frames, rows, w)
    )
    cot = lax.dynamic_slice_in_dim(source, r * slice_width + f * sub, sub, axis=3)
    cot = cot.astype(jnp.float32).transpose(3, 0, 1, 2)
    conv = coarse_conv(source, own(kernel_coarse))
    coarse_grad, coarse_sums = level(
        coarse_vals, conv, cot, mine(gain_coarse), mine(bias_coarse), group_width
    )
    quartered = (coarse_grad * 0.25).astype(jnp.bfloat16)
    spread = plain_everyone(quartered, count)
    source_fine = (
        spread.reshape(nf, nr, sub, frames, rows, w)
        .transpose(3, 4, 5, 1, 0, 2)
        .reshape(frames, rows, w, channels)
    )
    conv = fine_conv(source_fine, own(kernel_fine))
    fine_vals = (
        fine_in.reshape(nf, nr, sub, 2, 2, tl, hl, w)
        .transpose(2, 3, 4, 0, 5, 1, 6, 7)
        .reshape(sub, 2, 2, frames, rows, w)
    )
    cot = jnp.broadcast_to(
        quartered.astype(jnp.float32).reshape(sub, 1, 1, frames, rows, w), conv.shape
    )
    fine_grad, fine_sums = level(
        fine_vals, conv, cot, mine(gain_fine), mine(bias_fine), group_width
    )
    back = (
        fine_grad.astype(jnp.bfloat16)
        .reshape(sub, 2, 2, nf, tl, nr, hl, w)
        .transpose(3, 5, 0, 1, 2, 4, 6, 7)
        .reshape(count, sub, 4 * tl * hl * w)
    )
    sums = plain_everyone(jnp.concatenate([fine_sums, coarse_sums]), count)
    back = lax.all_to_all(back, PLAIN_BLOCK, 0, 0)
    out = (
        back.reshape(nf, nr, sub, 2, 2, tl, hl, w)
        .transpose(5, 6, 3, 7, 4, 1, 0, 2)
        .reshape(1, tl, 2 * hl, 2 * w, channels)
    )
    sums = sums.reshape(nf, nr, 4, sub).transpose(2, 1, 0, 3).reshape(4, channels)
    totals = lax.psum(sums, "dp")
    cells = nd * frames * rows * w
    scale_fine = 1.0 / jnp.sqrt(jnp.float32(4 * cells))
    scale_coarse = 1.0 / jnp.sqrt(jnp.float32(cells))
    return (
        out,
        totals[1] * scale_fine,
        totals[0] * scale_fine,
        totals[3] * scale_coarse,
        totals[2] * scale_coarse,
    )


def lanes_at(shape, axis):
    return lax.broadcasted_iota(jnp.int32, shape, axis)


def one_hot(found):
    return found.astype(jnp.float32).astype(jnp.bfloat16)


def pixel_order(plan, swapped):
    tl, hl, w = plan.tl, plan.hl, plan.w // 2
    size = 4 * plan.local
    lane = lanes_at((1, size), 1)
    j, i, t = lane % w, lane // w % hl, lane // (w * hl) % tl
    q, p = lane // (w * hl * tl) % 2, lane // (2 * w * hl * tl) % 2
    half = lane // (4 * w * hl * tl)
    if swapped:
        half = 1 - half
    pixel = (t * 2 * hl + 2 * i + p) * 4 * w + 2 * (half * w + j) + q
    return one_hot(lanes_at((size, size), 0) == pixel)


def merged_order(nr, outer, tl, cells):
    size = nr * outer * tl * cells
    lane = lanes_at((1, size), 1)
    cell, dev = lane % cells, lane // cells % nr
    t, o = lane // (cells * nr) % tl, lane // (cells * nr * tl)
    return one_hot(lanes_at((size, size), 0) == ((dev * outer + o) * tl + t) * cells + cell)


def column_order(plan):
    w = plan.w // 2
    lines = plan.places // plan.w
    lane = lanes_at((1, 4 * lines * w + 4 * lines), 1)
    inner = lane % (lines * w)
    place = inner // w * plan.w + lane // (lines * w) * w + inner % w
    past = lane - 2 * lines * w
    border = past % lines * plan.w + jnp.where(past < 2 * lines, w, w - 1)
    wanted = jnp.where(past >= 0, border, place)
    shape = (plan.places, 2 * lines * w + 4 * lines)
    return one_hot(lanes_at(shape, 0) == wanted[:, : shape[1]])


def one_hot_dot(a, b, dims):
    return lax.dot_general(a, b, (dims, ((), ())), preferred_element_type=jnp.float32)


def moved(field, distance, kept):
    size = field.shape[1]
    return jnp.where(kept, pltpu.roll(field, (-distance) % size, 1), 0.0)


def own_column(row, base, sub):
    shape = (sub, row.shape[1])
    mine = lanes_at(shape, 1) == lanes_at(shape, 0) + base
    return jnp.sum(jnp.where(mine, row, 0.0), axis=1, keepdims=True)


def as_row(column):
    shape = (column.shape[0], 128)
    here = lanes_at(shape, 1) == lanes_at(shape, 0)
    return jnp.sum(jnp.where(here, column, 0.0), axis=0, keepdims=True)


def terms(value, count):
    found = []
    for _ in range(count):
        found.append(value.astype(jnp.bfloat16).astype(jnp.float32))
        value = value - found[-1]
    return found


def in_groups(column, group_width):
    sub = column.shape[0]
    grouped = jnp.sum(column.reshape(sub // group_width, group_width, 1), axis=1, keepdims=True)
    return jnp.broadcast_to(grouped, (sub // group_width, group_width, 1)).reshape(sub, 1)


def in_lane_groups(row, group_width):
    lane = lanes_at(row.shape, 1)
    size = row.shape[1]
    step = 1
    while step < group_width:
        up, down = pltpu.roll(row, size - step, 1), pltpu.roll(row, step, 1)
        row = row + jnp.where(lane // step % 2 == 0, up, down)
        step *= 2
    return row


def total(parts):
    return sum(jnp.sum(part, axis=1, keepdims=True) for part in parts)


def statistics(one, two, entries, group_width):
    mean = in_groups(one, group_width) / entries
    square = in_groups(two, group_width) / entries
    return mean, lax.rsqrt(square - mean * mean + EPSILON)


def normalised(parts, gain, bias, mean, inv_std):
    normed, slope = [], []
    for part in parts:
        unit = (part - mean) * inv_std
        preact = gain * unit + bias
        squash = jax.nn.sigmoid(preact)
        normed.append(unit)
        slope.append(squash * (1.0 + preact * (1.0 - squash)))
    return normed, slope


class Plan:
    def __init__(self, mesh_sizes, acts_coarse, slice_width):
        self.nf, self.nr = mesh_sizes
        self.count = self.nf * self.nr
        self.tl, self.hl, self.w, self.channels = acts_coarse
        self.slice_width = slice_width
        self.sub = slice_width // self.nf
        self.cells = self.hl * self.w
        self.local = self.tl * self.cells
        self.image = self.cells * self.nr
        self.frames = self.tl * self.nf
        self.places = self.frames * self.image
        self.group_width = self.channels // GROUPS
        self.chunks = self.channels // 128
        self.acts_at = self.chunks // 2 * self.local
        self.packed_at = self.acts_at + self.sub
        self.cot_at = self.packed_at + 8
        self.block_rows = self.cot_at + 8
        self.fits = (
            self.sub == 32
            and self.slice_width == 128
            and self.group_width == 16
            and self.cells == 16
            and self.w == 8
            and self.tl == 2
            and self.nr == 4
            and self.nf == 4
            and self.slice_width * self.nr == self.channels
        )

    def place_masks(self, w):
        lane = lanes_at((1, self.places // self.w * w), 1)
        col, row = lane % w, lane // w % (self.hl * self.nr)
        last_row = self.hl * self.nr - 1
        return (lane, col > 0, col < w - 1, row > 0, row < last_row)


def fetched(pairs, sems):
    copies = [pltpu.make_async_copy(src, dst, sems.at[k]) for k, (src, dst) in enumerate(pairs)]
    for copy in copies:
        copy.start()
    return copies


def own_place(plan):
    pair, member, r = lax.axis_index("pairs"), lax.axis_index("member"), lax.axis_index("rows")
    return pair, member, r, r * plan.slice_width + (2 * pair + member) * plan.sub


def fetch_kernel(g_hbm, coarse_hbm, fine_hbm, g_ref, coarse_ref, fine_ref, sems):
    for copy in fetched([(fine_hbm, fine_ref), (coarse_hbm, coarse_ref), (g_hbm, g_ref)], sems):
        copy.wait()


def pack_kernel(plan, g_ref, coarse_ref, fine_ref, out_ref):
    sub, chunks, local = plan.sub, plan.chunks, plan.local
    shape = (2 * local, 2 * 128)
    lane = lanes_at((1, 2 * 128), 1)
    repeated = one_hot(lanes_at(shape, 0) == lane % local + lane // 128 * local)
    shape = (plan.channels, 128)
    quarter = lanes_at(shape, 0) // 8 % 4 == lanes_at(shape, 1) // local
    orders = jnp.concatenate([pixel_order(plan, swapped) for swapped in (False, True)], axis=1)
    acts = fine_ref[...]
    halves = one_hot_dot(acts, orders, ((0,), (0,))).astype(jnp.bfloat16)
    halves = [halves[:, :128], halves[:, 128:]]
    small = one_hot_dot(jnp.concatenate([coarse_ref[...], g_ref[...]], axis=0), repeated, ((0,), (0,)))
    for k, at in enumerate((plan.packed_at, plan.cot_at)):
        rows_of = jnp.where(quarter, small[:, k * 128 : (k + 1) * 128], 0.0).reshape(plan.count, 4, 8, 128)
        out_ref[:, at : at + 8, :] = jnp.sum(rows_of, axis=1).astype(jnp.bfloat16)
    low = lanes_at((sub, 128), 1) < 64
    for s_r in range(plan.nr):
        for s_f in range(plan.nf):
            dest = s_r * plan.nf + s_f
            first, half = s_r * plan.slice_width + s_f // 2 * 2 * sub, s_f % 2
            for k in range(chunks // 2):
                at = (half * chunks // 2 + k) * 128
                out_ref[dest, k * local : (k + 1) * local, :] = g_ref[:, at : at + 128]
            upper, lower = halves[half][first : first + sub], halves[1 - half][first + sub : first + 2 * sub]
            out_ref[dest, plan.acts_at : plan.packed_at, :] = jnp.where(low, upper, lower)


def by_frame_device(plan, got_ref, at, height):
    return jnp.concatenate(
        [
            jnp.concatenate(
                [got_ref[r * plan.nf + f, at : at + height, :] for r in range(plan.nr)], axis=1
            )
            for f in range(plan.nf)
        ],
        axis=0,
    )


def in_places(plan, merged, height):
    width = plan.tl * plan.image
    return [
        jnp.concatenate(
            [merged[f * height : (f + 1) * height, k * width : (k + 1) * width] for f in range(plan.nf)],
            axis=1,
        )
        for k in range(4)
    ]


def coarse_kernel(
    plan,
    got_ref,
    weights,
    gain_c,
    bias_c,
    gain_f,
    bias_f,
    mine_ref,
    sent_ref,
    held_ref,
    inv_ref,
    fine_ref,
    columns,
    fine_order,
    by_column,
    order,
    source,
    products,
    conv_ref,
):
    sub, nr, nf, cells, tl, local = plan.sub, plan.nr, plan.nf, plan.cells, plan.tl, plan.local
    wide, depth = 2 * sub, plan.channels // 2
    pair, member, r, base = own_place(plan)
    first = r * plan.slice_width + pair * wide
    columns[0, 0:sub, :] = jnp.broadcast_to(own_column(gain_c[...], base, sub), (sub, 128))
    columns[1, 0:sub, :] = jnp.broadcast_to(own_column(bias_c[...], base, sub), (sub, 128))
    columns[2] = jnp.broadcast_to(own_column(gain_f[...], first, wide), (wide, 128))
    columns[3] = jnp.broadcast_to(own_column(bias_f[...], first, wide), (wide, 128))
    order[...] = merged_order(plan.nr, 4, plan.tl, plan.cells)
    fine_order[...] = merged_order(plan.nr, 8, plan.tl, plan.cells // 2)
    by_column[...] = column_order(plan)
    both = pl.ds(pl.multiple_of(pair * wide, wide), wide)
    half = pl.ds(pl.multiple_of(member * depth, depth), depth)
    for s_f in range(nf):
        for s_r in range(nr):
            for t in range(tl):
                at = (s_f * tl + t) * plan.image + s_r * cells
                for k in range(plan.chunks // 2):
                    source[at : at + cells, k * 128 : (k + 1) * 128] = got_ref[
                        s_r * nf + s_f, k * local + t * cells : k * local + (t + 1) * cells, :
                    ]
    source[plan.places :, :] = jnp.zeros((2 * plan.image, depth), jnp.bfloat16)
    products[...] = sum(
        one_hot_dot(
            weights[9 * k : 9 * k + 9, both, half].reshape(9 * wide, depth),
            source[(2 - k) * plan.image : (2 - k) * plan.image + plan.places, :],
            ((1,), (1,)),
        )
        for k in range(3)
    )
    merged = one_hot_dot(by_frame_device(plan, got_ref, plan.acts_at, sub), fine_order[...], ((1,), (0,)))
    parts = halves_at(plan, merged)
    for pq in range(4):
        fine_ref[pq] = parts[pq]
    one, two = total(parts), total([part * part for part in parts])
    stats = terms(as_row(one) + pltpu.roll(as_row(two), 64, 1), 3)
    stats = jnp.concatenate(stats + [jnp.zeros_like(stats[0])] * 5, axis=0).astype(jnp.bfloat16)
    found = []
    for at in (plan.packed_at, plan.cot_at):
        merged = one_hot_dot(by_frame_device(plan, got_ref, at, 8), order[...], ((1,), (0,)))
        found.append(jnp.concatenate(in_places(plan, merged, 8), axis=0))
    values, cot = found
    gain, bias = columns[0][0:sub, 0:1], columns[1][0:sub, 0:1]
    entries = plan.places * plan.group_width
    mean, inv_std = statistics(total([values]), total([values * values]), entries, plan.group_width)
    (normed,), (slope,) = normalised([values], gain, bias, mean, inv_std)
    held_ref[0], held_ref[1], held_ref[2] = normed, slope, cot
    inv_ref[...] = jnp.broadcast_to(inv_std, (sub, 128))
    lane, has_left, has_right, has_up, has_down = plan.place_masks(plan.w)
    by_col = []
    for col in range(3):
        parts = [products[pl.ds((3 * row + col) * wide, wide), :] for row in range(3)]
        by_col.append(parts[1] + moved(parts[0], plan.w, has_down) + moved(parts[2], -plan.w, has_up))
    conv_ref[...] = by_col[1] + moved(by_col[0], 1, has_right) + moved(by_col[2], -1, has_left)
    mine_ref[...] = conv_ref[pl.ds(pl.multiple_of(member * sub, sub), sub), :]
    theirs = conv_ref[pl.ds(pl.multiple_of((1 - member) * sub, sub), sub), :]
    sent_ref[0:sub, :] = theirs.astype(jnp.bfloat16)
    sent_ref[sub:, 0:128] = stats
    sent_ref[sub:, 128:] = jnp.zeros((8, plan.places - 128), jnp.bfloat16)


def quarter_kernel(plan, mine_ref, both_ref, held_ref, inv_ref, columns, by_column, out_ref, sums_ref):
    sub = plan.sub
    _, member, _, _ = own_place(plan)
    conv = mine_ref[...] + both_ref[1 - member, 0:sub, :].astype(jnp.float32)
    normed, slope, cot = held_ref[0], held_ref[1], held_ref[2]
    gain, inv_std = columns[0][0:sub, 0:1], inv_ref[:, 0:1]
    entries = plan.places * plan.group_width
    pre = conv * slope
    one, two = total([pre]), total([pre * normed])
    group_one = in_groups(gain * one, plan.group_width) / entries
    group_two = in_groups(gain * two, plan.group_width) / entries
    grad = cot + inv_std * (gain * pre - group_one - normed * group_two)
    quartered = (grad * 0.25).astype(jnp.bfloat16)
    sent = one_hot_dot(quartered, by_column[...], ((1,), (0,))).astype(jnp.bfloat16)
    low = lanes_at((sub // 2, 128), 1) < 64
    for half in range(2):
        at = half * 256
        border = sent[:, 512 + half * 128 : 640 + half * 128]
        border = jnp.where(low, border[: sub // 2], border[sub // 2 :])
        for dest in range(half, plan.count, 2):
            out_ref[dest, 0:sub, :] = sent[:, at : at + 128]
            out_ref[dest, sub : 2 * sub, :] = sent[:, at + 128 : at + 256]
            out_ref[dest, 2 * sub : 2 * sub + sub // 2, :] = border
    sums_ref[...] = jnp.concatenate([as_row(one), as_row(two)], axis=0)


def halves_at(plan, merged):
    sub = plan.sub
    turned = jnp.concatenate([pltpu.roll(merged[:, k * 128 : (k + 1) * 128], 64, 1) for k in range(4)], axis=1)
    low = lanes_at((sub, 128), 1) < 64
    parts = []
    for pq in range(4):
        groups = []
        for group in range(2):
            e = 4 * group + pq
            at = e // 2 * 128
            strips = []
            for m in range(plan.nf // 2):
                first, second = slice(2 * m * sub, (2 * m + 1) * sub), slice((2 * m + 1) * sub, (2 * m + 2) * sub)
                if e % 2 == 0:
                    strips.append(jnp.where(low, merged[first, at : at + 128], turned[second, at : at + 128]))
                else:
                    strips.append(jnp.where(low, turned[first, at : at + 128], merged[second, at : at + 128]))
            groups.append(jnp.concatenate(strips, axis=1))
        parts.append(jnp.concatenate(groups, axis=0))
    return parts


def halves_from(plan, parts):
    sub = plan.sub
    low = lanes_at((sub, 128), 1) < 64
    down = []
    for f in range(plan.nf):
        across = []
        for v in range(4):
            pair = []
            for e in (2 * v, 2 * v + 1):
                group, pq = e // 4, e % 4
                strip = parts[pq][group * sub : (group + 1) * sub, f // 2 * 128 : (f // 2 + 1) * 128]
                pair.append(strip if e % 2 == f % 2 else pltpu.roll(strip, 64, 1))
            across.append(jnp.where(low, pair[0], pair[1]))
        down.append(jnp.concatenate(across, axis=1))
    return jnp.concatenate(down, axis=0)


def fine_kernel(
    plan, got_ref, acts_ref, both_ref, columns, order, sums_ref, weights, out_ref, source, border, products, beyond
):
    sub, nr, nf, wide = plan.sub, plan.nr, plan.nf, 2 * plan.sub
    pair, member, r, _ = own_place(plan)
    both = pl.ds(pl.multiple_of(pair * wide, wide), wide)
    w = plan.w // 2
    lines = plan.places // plan.w
    places = lines * w
    for k in range(2):
        source[:, k * 128 : (k + 1) * 128] = got_ref[:, k * sub : (k + 1) * sub, :].reshape(plan.channels, 128)
    packed = got_ref[:, wide : wide + sub // 2, :].reshape(plan.count * sub // 2, 128)
    shape = (128, places)
    beside = lanes_at(shape, 1) == lanes_at(shape, 0) % lines * w + (1 - member) * (w - 1)
    for k in range(2):
        here = one_hot(beside & (lanes_at(shape, 0) // lines == k))
        found = one_hot_dot(packed, here, ((1,), (0,))).astype(jnp.bfloat16)
        for s in range(plan.count):
            border[s * sub + k * (sub // 2) : s * sub + (k + 1) * (sub // 2), :] = found[
                s * (sub // 2) : (s + 1) * (sub // 2)
            ]
    image = plan.image // 2
    sums, extras = 0.0, 0.0
    for k in (2, 1, 0):
        here, beside = source[...], border[...]
        if k < 2:
            shift = (2 - k) * image
            inside = lanes_at((1, places), 1) < places - shift
            here, beside = [
                jnp.where(inside, pltpu.roll(part, places - shift, 1), jnp.zeros_like(part)) for part in (here, beside)
            ]
        sums = sums + one_hot_dot(
            weights[9 * k : 9 * k + 9, both, :].reshape(9 * wide, plan.channels), here, ((1,), (0,))
        )
        facing = jnp.concatenate([weights[9 * k + 3 * row + 2 * member, both, :] for row in range(3)], axis=0)
        extras = extras + one_hot_dot(facing, beside, ((1,), (0,)))
    products[...], beyond[...] = sums, extras
    parts = [acts_ref[pq] for pq in range(4)]
    stats = sum(both_ref[k, sub : sub + 8, 0:128].astype(jnp.float32) for k in range(2))
    stats = stats[0:1] + stats[1:2] + stats[2:3]
    entries = 4 * plan.places * plan.group_width
    one, two = own_column(stats, 0, wide), own_column(stats, 64, wide)
    mean, inv_std = statistics(one, two, entries, plan.group_width)
    gain, bias = columns[2][:, 0:1], columns[3][:, 0:1]
    normed, slope = normalised(parts, gain, bias, mean, inv_std)
    lane, has_left, has_right, has_up, has_down = plan.place_masks(w)
    right, left = (1 - member).astype(jnp.float32), member.astype(jnp.float32)
    by_row = []
    for row in range(3):
        a, b, c = [products[pl.ds((3 * row + col) * wide, wide), :] for col in range(3)]
        extra = beyond[pl.ds(row * wide, wide), :]
        by_row.append(
            (a + b + moved(c, -1, has_left) + left * extra, moved(a, 1, has_right) + b + c + right * extra)
        )
    convs = [by_row[0][q] + by_row[1][q] + moved(by_row[2][q], -w, has_up) for q in range(2)]
    convs += [moved(by_row[0][q], w, has_down) + by_row[1][q] + by_row[2][q] for q in range(2)]
    pre = [conv * part for conv, part in zip(convs, slope)]
    one = total(pre)
    two = total([a * b for a, b in zip(pre, normed)])
    cot = source[pl.ds(pl.multiple_of(r * plan.slice_width + pair * wide, wide), wide), :].astype(jnp.float32)
    scale = inv_std * gain
    stacked = halves_from(plan, [cot + scale * part for part in pre]).astype(jnp.bfloat16)
    sent = one_hot_dot(stacked, order[...], ((1,), (1,))).astype(jnp.bfloat16)
    coarse = sums_ref[0:1] + pltpu.roll(sums_ref[1:2], sub, 1)
    coded = (
        terms(as_row(one) + pltpu.roll(as_row(two), 64, 1), 2)
        + terms(coarse, 2)
        + terms(as_row(inv_std) + pltpu.roll(as_row(mean), 64, 1), 3)
    )
    coded = jnp.concatenate(coded + [jnp.zeros_like(coarse)], axis=0).astype(jnp.bfloat16)
    for s_r in range(nr):
        for s_f in range(nf):
            out_ref[s_r * nf + s_f, 0:sub, :] = sent[s_f * sub : (s_f + 1) * sub, s_r * 128 : (s_r + 1) * 128]
            out_ref[s_r * nf + s_f, sub : sub + 8, :] = coded


def spread_kernel(plan, got_ref, acts_ref, gain_ref, out_ref, sums_ref):
    sub, nr, nf = plan.sub, plan.nr, plan.nf
    low = lanes_at((sub, 128), 1) < 64
    low_row = lanes_at((1, 128), 1) < 64
    first_row = lanes_at((1, 128), 1) < sub
    source = []
    fine, coarse, moments = [[], []], [[], []], [[], []]
    for s_r in range(nr):
        ones, twos, c_ones, c_twos, invs, means = [], [], 0.0, 0.0, [], []
        for pair in range(nf // 2):
            at = s_r * nf + 2 * pair
            left, right = [got_ref[at + k, 0:sub, :].astype(jnp.float32) for k in range(2)]
            source.append(jnp.where(low, left, pltpu.roll(right, 64, 1)))
            source.append(jnp.where(low, pltpu.roll(left, 64, 1), right))
            coded = [got_ref[at + k, sub : sub + 8, :].astype(jnp.float32) for k in range(2)]
            sums = coded[0][0:1] + coded[0][1:2] + coded[1][0:1] + coded[1][1:2]
            ones.append(sums if pair == 0 else pltpu.roll(sums, 64, 1))
            twos.append(pltpu.roll(sums, 64, 1) if pair == 0 else sums)
            both = coded[0][4:5] + coded[0][5:6] + coded[0][6:7]
            invs.append(both if pair == 0 else pltpu.roll(both, 64, 1))
            means.append(pltpu.roll(both, 64, 1) if pair == 0 else both)
            for k in range(2):
                sums = coded[k][2:3] + coded[k][3:4]
                to = (2 * pair + k) * sub
                c_one = jnp.where(first_row, sums, 0.0)
                c_two = jnp.where(first_row, pltpu.roll(sums, 128 - sub, 1), 0.0)
                c_ones = c_ones + (pltpu.roll(c_one, to, 1) if to else c_one)
                c_twos = c_twos + (pltpu.roll(c_two, to, 1) if to else c_two)
        fine[0].append(jnp.where(low_row, ones[0], ones[1]))
        fine[1].append(jnp.where(low_row, twos[0], twos[1]))
        moments[0].append(jnp.where(low_row, invs[0], invs[1]))
        moments[1].append(jnp.where(low_row, means[0], means[1]))
        coarse[0].append(c_ones)
        coarse[1].append(c_twos)
    one, two, inv_std, mean, c_one, c_two = [jnp.concatenate(part, axis=1) for part in fine + moments + coarse]
    source = jnp.concatenate(source, axis=0).astype(jnp.bfloat16)
    result = one_hot_dot(pixel_order(plan, False), source, ((1,), (1,)))
    gain = gain_ref[...]
    entries = 4 * plan.places * plan.group_width
    group_one = in_lane_groups(gain * one, plan.group_width) / entries
    group_two = in_lane_groups(gain * two, plan.group_width) / entries
    normed = (acts_ref[...].astype(jnp.float32) - mean) * inv_std
    out_ref[...] = (result - inv_std * (group_one + normed * group_two)).astype(jnp.bfloat16)
    sums_ref[...] = jnp.concatenate([one, two, c_one, c_two] + [jnp.zeros_like(one)] * 4, axis=0)


def total_kernel(scales, both_ref, result_ref, result_hbm, out_hbms, rows_ref, sems):
    copies = fetched([(result_ref, result_hbm)], sems)
    rows = sum(both_ref[k] for k in range(both_ref.shape[0]))
    for k in range(4):
        rows_ref[k] = rows[k : k + 1] * scales[k]
    for k in range(4):
        copies.append(pltpu.make_async_copy(rows_ref.at[k], out_hbms[k], sems.at[k + 1]))
        copies[-1].start()
    for copy in copies:
        copy.wait()


def in_vmem(count):
    return [pl.BlockSpec(memory_space=pltpu.VMEM)] * count


def in_hbm(count):
    return [pl.BlockSpec(memory_space=pltpu.HBM)] * count


def kept(array):
    return pltpu.with_memory_space_constraint(array, pltpu.HBM)


def shape_of(shape, kind):
    return jax.ShapeDtypeStruct(shape, kind)


LIMIT = pltpu.CompilerParams(vmem_limit_bytes=40 * 1024 * 1024)
COST = pl.CostEstimate(flops=2_000_000_000, bytes_accessed=4_000_000, transcendentals=0)


def fast_shards(
    plan,
    acts_fine,
    acts_coarse,
    grad_coarse,
    gain_fine,
    bias_fine,
    kernel_fine,
    gain_coarse,
    bias_coarse,
    kernel_coarse,
):
    nd = lax.axis_size("dp")
    count, sub, channels, places, local = plan.count, plan.sub, plan.channels, plan.places, plan.local
    f32, bf16 = jnp.float32, jnp.bfloat16
    rows = [part.reshape(1, channels) for part in (gain_coarse, bias_coarse, gain_fine, bias_fine)]
    places_of = ((local, channels), (local, channels), (4 * local, channels))
    fetched_of = pl.pallas_call(
        fetch_kernel,
        out_shape=tuple(pltpu.VMEM(shape, bf16) for shape in places_of),
        in_specs=in_hbm(3),
        out_specs=tuple(in_vmem(3)),
        scratch_shapes=[pltpu.SemaphoreType.DMA((3,))],
        compiler_params=LIMIT,
    )(*[kept(part.reshape(shape)) for part, shape in zip((grad_coarse, acts_coarse, acts_fine), places_of)])
    acts = fetched_of[2]
    packed = pl.pallas_call(
        functools.partial(pack_kernel, plan),
        out_shape=shape_of((count, plan.block_rows, 128), bf16),
        in_specs=in_vmem(3),
        out_specs=in_vmem(1)[0],
        compiler_params=LIMIT,
        cost_estimate=COST,
    )(*fetched_of)
    got = lax.all_to_all(packed, BLOCK, 0, 0)
    mine, theirs, held, inv_std, fine_acts, columns, fine_order, by_column = pl.pallas_call(
        functools.partial(coarse_kernel, plan),
        out_shape=(
            shape_of((sub, places), f32),
            shape_of((sub + 8, places), bf16),
            shape_of((3, sub, places), f32),
            shape_of((sub, 128), f32),
            shape_of((4, 2 * sub, places // 2), f32),
            shape_of((4, 2 * sub, 128), f32),
            shape_of((4 * plan.nr * local, 4 * plan.nr * local), bf16),
            shape_of((places, places + places // 2), bf16),
        ),
        in_specs=in_vmem(6),
        out_specs=tuple(in_vmem(8)),
        scratch_shapes=[
            pltpu.VMEM((4 * plan.nr * local, 4 * plan.nr * local), bf16),
            pltpu.VMEM((places + 2 * plan.image, channels // 2), bf16),
            pltpu.VMEM((18 * sub, places), f32),
            pltpu.VMEM((2 * sub, places), f32),
        ],
        compiler_params=LIMIT,
        cost_estimate=COST,
    )(got, kernel_coarse, *rows)
    both = lax.all_gather(theirs, "member")
    quartered, coarse_sums = pl.pallas_call(
        functools.partial(quarter_kernel, plan),
        out_shape=(shape_of((count, 2 * sub + sub // 2, 128), bf16), shape_of((2, 128), f32)),
        in_specs=in_vmem(6),
        out_specs=tuple(in_vmem(2)),
        compiler_params=LIMIT,
        cost_estimate=COST,
    )(mine, both, held, inv_std, columns, by_column)
    spread = lax.all_to_all(quartered, BLOCK, 0, 0)
    sent = pl.pallas_call(
        functools.partial(fine_kernel, plan),
        out_shape=shape_of((count, sub + 8, 128), bf16),
        in_specs=in_vmem(7),
        out_specs=in_vmem(1)[0],
        scratch_shapes=[
            pltpu.VMEM((channels, places // 2), bf16),
            pltpu.VMEM((channels, places // 2), bf16),
            pltpu.VMEM((18 * sub, places // 2), f32),
            pltpu.VMEM((6 * sub, places // 2), f32),
        ],
        compiler_params=LIMIT,
        cost_estimate=COST,
    )(spread, fine_acts, both, columns, fine_order, coarse_sums, kernel_fine)
    back = lax.all_to_all(sent, BLOCK, 0, 0)
    cells = nd * places
    fine_scale, coarse_scale = 1.0 / math.sqrt(4 * cells), 1.0 / math.sqrt(cells)
    out, sums = pl.pallas_call(
        functools.partial(spread_kernel, plan),
        out_shape=(pltpu.VMEM((4 * local, channels), bf16), shape_of((8, channels), f32)),
        in_specs=in_vmem(3),
        out_specs=tuple(in_vmem(2)),
        compiler_params=LIMIT,
        cost_estimate=COST,
    )(back, acts, rows[2])
    both = lax.all_gather(sums, "dp")
    out, sums = pl.pallas_call(
        functools.partial(total_kernel, (fine_scale, fine_scale, coarse_scale, coarse_scale)),
        out_shape=(pltpu.HBM((4 * local, channels), bf16), (pltpu.HBM((1, channels), f32),) * 4),
        in_specs=in_vmem(2),
        out_specs=(in_hbm(1)[0], tuple(in_hbm(4))),
        scratch_shapes=[pltpu.VMEM((4, 1, channels), f32), pltpu.SemaphoreType.DMA((5,))],
        compiler_params=LIMIT,
        cost_estimate=COST,
    )(both, out)
    bias_f, gain_f, bias_c, gain_c = [part.reshape(channels) for part in sums]
    return out.reshape(acts_fine.shape), gain_f, bias_f, gain_c, bias_c


def solution(mesh):
    def function(*arrays):
        local = [size // mesh.shape[axis] for size, axis in zip(arrays[1].shape, ("dp", "frames", "rows"))]
        sizes = (mesh.shape["frames"], mesh.shape["rows"])
        plan = Plan(sizes, (*local[1:], *arrays[1].shape[3:]), arrays[5].shape[1] // mesh.shape["rows"])
        if plan.fits:
            split = (mesh.shape["dp"], plan.nf // 2, 2, plan.nr)
            used = jax.sharding.Mesh(mesh.devices.reshape(split), ("dp", "pairs", "member", "rows"))
            shards, frames = functools.partial(fast_shards, plan), ("pairs", "member")
        else:
            used, shards, frames = mesh, plain_shards, "frames"
        blocks, kernel = P("dp", frames, "rows", None, None), P(None, "rows", None)
        in_specs = (blocks, blocks, blocks, P(), P(), kernel, P(), P(), kernel)
        out_specs = (blocks, P(), P(), P(), P())
        mapped = jax.shard_map(shards, mesh=used, in_specs=in_specs, out_specs=out_specs, check_vma=False)
        return mapped(*arrays)

    return function
```

```python
import functools
import math

import jax
import jax.numpy as jnp
from jax import lax
from jax.experimental import pallas as pl
from jax.experimental.pallas import tpu as pltpu
from jax.sharding import PartitionSpec as P

GROUPS = 32
EPSILON = 1e-06
BLOCK = ("rows", "pairs", "member")
BACK_BLOCK = ("pairs", "member", "rows")
PLAIN_BLOCK = ("frames", "rows")


def plain_everyone(block, count):
    copies = jnp.broadcast_to(block[None], (count,) + block.shape)
    return lax.all_to_all(copies, PLAIN_BLOCK, 0, 0)


def ahead(field, axis, distance):
    size = field.shape[axis]
    if distance == 0:
        return field
    widths = [(0, 0)] * field.ndim
    if distance > 0:
        widths[axis] = (0, distance)
        kept = lax.slice_in_dim(field, distance, size, axis=axis)
    else:
        widths[axis] = (-distance, 0)
        kept = lax.slice_in_dim(field, 0, size + distance, axis=axis)
    return jnp.pad(kept, widths)


def tap_products(source, kernel):
    sub = kernel.shape[1]
    frames, rows, cols, channels = source.shape
    products = lax.dot_general(
        kernel.reshape(27 * sub, channels),
        source.reshape(frames * rows * cols, channels),
        (((1,), (1,)), ((), ())),
        preferred_element_type=jnp.float32,
    ).reshape(3, 3, 3, sub, frames, rows, cols)
    return sum(ahead(products[depth], 3, 2 - depth) for depth in range(3))


def coarse_conv(source, kernel):
    spatial = tap_products(source, kernel)
    total = 0.0
    for row in range(3):
        part = sum(ahead(spatial[row, col], 3, 1 - col) for col in range(3))
        total = total + ahead(part, 2, 1 - row)
    return total


def fine_conv(source, kernel):
    spatial = tap_products(source, kernel)
    result = []
    for p in range(2):
        rows_of = []
        for q in range(2):
            total = 0.0
            for row in range(3):
                part = sum(ahead(spatial[row, col], 3, (q + 1 - col) // 2) for col in range(3))
                total = total + ahead(part, 2, (p + 1 - row) // 2)
            rows_of.append(total)
        result.append(jnp.stack(rows_of, 1))
    return jnp.stack(result, 1)


def group_total(sums, group_width):
    sub = sums.shape[-1]
    if sub % group_width == 0:
        grouped = jnp.sum(sums.reshape(-1, sub // group_width, group_width), axis=-1)
        return jnp.repeat(grouped, group_width, axis=-1)
    spread = jnp.moveaxis(lax.all_gather(sums, "frames"), 0, 1).reshape(sums.shape[0], -1, group_width)
    mine = lax.axis_index("frames") * sub // group_width
    grouped = lax.dynamic_index_in_dim(jnp.sum(spread, -1), mine, 1)
    return jnp.broadcast_to(grouped, sums.shape)


def level(acts, conv_grad, cotangent, gain, bias, group_width):
    sub = acts.shape[0]
    places = acts.size // sub
    values = acts.astype(jnp.float32).reshape(sub, places)
    conv_grad = conv_grad.reshape(sub, places)
    entries = places * group_width
    moments = group_total(
        jnp.stack([jnp.sum(values, 1), jnp.sum(values * values, 1)]), group_width
    ) / entries
    mean = moments[0]
    inv_std = lax.rsqrt(moments[1] - mean * mean + EPSILON)
    normed = (values - mean[:, None]) * inv_std[:, None]
    preact = gain[:, None] * normed + bias[:, None]
    squash = jax.nn.sigmoid(preact)
    pre_grad = conv_grad * squash * (1.0 + preact * (1.0 - squash))
    sums = jnp.stack([jnp.sum(pre_grad, 1), jnp.sum(pre_grad * normed, 1)])
    terms = group_total(sums * gain, group_width) / entries
    grad = cotangent.reshape(sub, places) + inv_std[:, None] * (
        gain[:, None] * pre_grad - terms[0][:, None] - normed * terms[1][:, None]
    )
    return grad, sums


def plain_shards(
    acts_fine,
    acts_coarse,
    grad_coarse,
    gain_fine,
    bias_fine,
    kernel_fine,
    gain_coarse,
    bias_coarse,
    kernel_coarse,
):
    nf, nr, nd = lax.axis_size("frames"), lax.axis_size("rows"), lax.axis_size("dp")
    count = nf * nr
    channels = acts_fine.shape[-1]
    slice_width = kernel_fine.shape[1]
    sub = slice_width // nf
    group_width = channels // GROUPS
    tl, hl, w = acts_coarse.shape[1:4]
    frames, rows = tl * nf, hl * nr
    f, r = lax.axis_index("frames"), lax.axis_index("rows")

    gathered = plain_everyone(grad_coarse[0], count)
    source = (
        gathered.reshape(nf, nr, tl, hl, w, channels)
        .transpose(0, 2, 1, 3, 4, 5)
        .reshape(frames, rows, w, channels)
    )
    coarse_in = acts_coarse[0].reshape(tl, hl, w, nr, nf, sub).transpose(4, 3, 5, 0, 1, 2)
    coarse_in = lax.all_to_all(coarse_in.reshape(count, sub, tl * hl * w), PLAIN_BLOCK, 0, 0)
    fine_in = acts_fine[0].reshape(tl, hl, 2, w, 2, nr, nf, sub).transpose(6, 5, 7, 2, 4, 0, 1, 3)
    fine_in = lax.all_to_all(fine_in.reshape(count, sub, 4 * tl * hl * w), PLAIN_BLOCK, 0, 0)

    def mine(vector):
        return lax.dynamic_slice_in_dim(vector, r * slice_width + f * sub, sub)

    def own(kernel):
        return lax.dynamic_slice_in_dim(kernel, f * sub, sub, axis=1)

    coarse_vals = (
        coarse_in.reshape(nf, nr, sub, tl, hl, w).transpose(2, 0, 3, 1, 4, 5).reshape(sub, frames, rows, w)
    )
    cot = lax.dynamic_slice_in_dim(source, r * slice_width + f * sub, sub, axis=3)
    cot = cot.astype(jnp.float32).transpose(3, 0, 1, 2)
    conv = coarse_conv(source, own(kernel_coarse))
    coarse_grad, coarse_sums = level(
        coarse_vals, conv, cot, mine(gain_coarse), mine(bias_coarse), group_width
    )
    quartered = (coarse_grad * 0.25).astype(jnp.bfloat16)
    spread = plain_everyone(quartered, count)
    source_fine = (
        spread.reshape(nf, nr, sub, frames, rows, w)
        .transpose(3, 4, 5, 1, 0, 2)
        .reshape(frames, rows, w, channels)
    )
    conv = fine_conv(source_fine, own(kernel_fine))
    fine_vals = (
        fine_in.reshape(nf, nr, sub, 2, 2, tl, hl, w)
        .transpose(2, 3, 4, 0, 5, 1, 6, 7)
        .reshape(sub, 2, 2, frames, rows, w)
    )
    cot = jnp.broadcast_to(
        quartered.astype(jnp.float32).reshape(sub, 1, 1, frames, rows, w), conv.shape
    )
    fine_grad, fine_sums = level(
        fine_vals, conv, cot, mine(gain_fine), mine(bias_fine), group_width
    )
    back = (
        fine_grad.astype(jnp.bfloat16)
        .reshape(sub, 2, 2, nf, tl, nr, hl, w)
        .transpose(3, 5, 0, 1, 2, 4, 6, 7)
        .reshape(count, sub, 4 * tl * hl * w)
    )
    sums = plain_everyone(jnp.concatenate([fine_sums, coarse_sums]), count)
    back = lax.all_to_all(back, PLAIN_BLOCK, 0, 0)
    out = (
        back.reshape(nf, nr, sub, 2, 2, tl, hl, w)
        .transpose(5, 6, 3, 7, 4, 1, 0, 2)
        .reshape(1, tl, 2 * hl, 2 * w, channels)
    )
    sums = sums.reshape(nf, nr, 4, sub).transpose(2, 1, 0, 3).reshape(4, channels)
    totals = lax.psum(sums, "dp")
    cells = nd * frames * rows * w
    scale_fine = 1.0 / jnp.sqrt(jnp.float32(4 * cells))
    scale_coarse = 1.0 / jnp.sqrt(jnp.float32(cells))
    return (
        out,
        totals[1] * scale_fine,
        totals[0] * scale_fine,
        totals[3] * scale_coarse,
        totals[2] * scale_coarse,
    )


def lanes_at(shape, axis):
    return lax.broadcasted_iota(jnp.int32, shape, axis)


def one_hot(found):
    return found.astype(jnp.float32).astype(jnp.bfloat16)


def pixel_order(plan, swapped):
    tl, hl, w = plan.tl, plan.hl, plan.w // 2
    size = 4 * plan.local
    lane = lanes_at((1, size), 1)
    j, i, t = lane % w, lane // w % hl, lane // (w * hl) % tl
    q, p = lane // (w * hl * tl) % 2, lane // (2 * w * hl * tl) % 2
    half = lane // (4 * w * hl * tl)
    if swapped:
        half = 1 - half
    pixel = (t * 2 * hl + 2 * i + p) * 4 * w + 2 * (half * w + j) + q
    return one_hot(lanes_at((size, size), 0) == pixel)


def merged_order(nr, outer, tl, cells):
    size = nr * outer * tl * cells
    lane = lanes_at((1, size), 1)
    cell, dev = lane % cells, lane // cells % nr
    t, o = lane // (cells * nr) % tl, lane // (cells * nr * tl)
    return one_hot(lanes_at((size, size), 0) == ((dev * outer + o) * tl + t) * cells + cell)


def column_order(plan):
    w = plan.w // 2
    lines = plan.places // plan.w
    lane = lanes_at((1, 4 * lines * w + 4 * lines), 1)
    inner = lane % (lines * w)
    place = inner // w * plan.w + lane // (lines * w) * w + inner % w
    past = lane - 2 * lines * w
    border = past % lines * plan.w + jnp.where(past < 2 * lines, w, w - 1)
    wanted = jnp.where(past >= 0, border, place)
    shape = (plan.places, 2 * lines * w + 4 * lines)
    return one_hot(lanes_at(shape, 0) == wanted[:, : shape[1]])


def one_hot_dot(a, b, dims):
    return lax.dot_general(a, b, (dims, ((), ())), preferred_element_type=jnp.float32)


def moved(field, distance, kept):
    size = field.shape[1]
    return jnp.where(kept, pltpu.roll(field, (-distance) % size, 1), 0.0)


def own_column(row, base, sub):
    shape = (sub, row.shape[1])
    mine = lanes_at(shape, 1) == lanes_at(shape, 0) + base
    return jnp.sum(jnp.where(mine, row, 0.0), axis=1, keepdims=True)


def as_row(column):
    shape = (column.shape[0], 128)
    here = lanes_at(shape, 1) == lanes_at(shape, 0)
    return jnp.sum(jnp.where(here, column, 0.0), axis=0, keepdims=True)


def terms(value, count):
    found = []
    for _ in range(count):
        found.append(value.astype(jnp.bfloat16).astype(jnp.float32))
        value = value - found[-1]
    return found


def in_groups(column, group_width):
    sub = column.shape[0]
    grouped = jnp.sum(column.reshape(sub // group_width, group_width, 1), axis=1, keepdims=True)
    return jnp.broadcast_to(grouped, (sub // group_width, group_width, 1)).reshape(sub, 1)


def in_lane_groups(row, group_width):
    lane = lanes_at(row.shape, 1)
    size = row.shape[1]
    step = 1
    while step < group_width:
        up, down = pltpu.roll(row, size - step, 1), pltpu.roll(row, step, 1)
        row = row + jnp.where(lane // step % 2 == 0, up, down)
        step *= 2
    return row


def total(parts):
    return sum(jnp.sum(part, axis=1, keepdims=True) for part in parts)


def statistics(one, two, entries, group_width):
    mean = in_groups(one, group_width) / entries
    square = in_groups(two, group_width) / entries
    return mean, lax.rsqrt(square - mean * mean + EPSILON)


def normalised(parts, gain, bias, mean, inv_std):
    normed, slope = [], []
    for part in parts:
        unit = (part - mean) * inv_std
        preact = gain * unit + bias
        squash = jax.nn.sigmoid(preact)
        normed.append(unit)
        slope.append(squash * (1.0 + preact * (1.0 - squash)))
    return normed, slope


class Plan:
    def __init__(self, mesh_sizes, acts_coarse, slice_width):
        self.nf, self.nr = mesh_sizes
        self.count = self.nf * self.nr
        self.tl, self.hl, self.w, self.channels = acts_coarse
        self.slice_width = slice_width
        self.sub = slice_width // self.nf
        self.cells = self.hl * self.w
        self.local = self.tl * self.cells
        self.image = self.cells * self.nr
        self.frames = self.tl * self.nf
        self.places = self.frames * self.image
        self.group_width = self.channels // GROUPS
        self.chunks = self.channels // 128
        self.acts_at = self.chunks // 2 * self.local
        self.packed_at = self.acts_at + self.sub
        self.cot_at = self.packed_at + 8
        self.block_rows = self.cot_at + 8
        self.fits = (
            self.sub == 32
            and self.slice_width == 128
            and self.group_width == 16
            and self.cells == 16
            and self.w == 8
            and self.tl == 2
            and self.nr == 4
            and self.nf == 4
            and self.slice_width * self.nr == self.channels
        )

    def place_masks(self, w):
        lane = lanes_at((1, self.places // self.w * w), 1)
        col, row = lane % w, lane // w % (self.hl * self.nr)
        last_row = self.hl * self.nr - 1
        return (lane, col > 0, col < w - 1, row > 0, row < last_row)


def fetched(pairs, sems):
    copies = [pltpu.make_async_copy(src, dst, sems.at[k]) for k, (src, dst) in enumerate(pairs)]
    for copy in copies:
        copy.start()
    return copies


def own_place(plan):
    pair, member, r = lax.axis_index("pairs"), lax.axis_index("member"), lax.axis_index("rows")
    return pair, member, r, r * plan.slice_width + (2 * pair + member) * plan.sub


def fetch_kernel(g_hbm, coarse_hbm, fine_hbm, g_ref, coarse_ref, fine_ref, sems):
    for copy in fetched([(fine_hbm, fine_ref), (coarse_hbm, coarse_ref), (g_hbm, g_ref)], sems):
        copy.wait()


def pack_kernel(plan, g_ref, coarse_ref, fine_ref, out_ref):
    sub, chunks, local = plan.sub, plan.chunks, plan.local
    shape = (2 * local, 2 * 128)
    lane = lanes_at((1, 2 * 128), 1)
    repeated = one_hot(lanes_at(shape, 0) == lane % local + lane // 128 * local)
    shape = (plan.channels, 128)
    quarter = lanes_at(shape, 0) // 8 % 4 == lanes_at(shape, 1) // local
    orders = jnp.concatenate([pixel_order(plan, swapped) for swapped in (False, True)], axis=1)
    acts = fine_ref[...]
    halves = one_hot_dot(acts, orders, ((0,), (0,))).astype(jnp.bfloat16)
    halves = [halves[:, :128], halves[:, 128:]]
    small = one_hot_dot(jnp.concatenate([coarse_ref[...], g_ref[...]], axis=0), repeated, ((0,), (0,)))
    for k, at in enumerate((plan.packed_at, plan.cot_at)):
        rows_of = jnp.where(quarter, small[:, k * 128 : (k + 1) * 128], 0.0).reshape(plan.count, 4, 8, 128)
        out_ref[:, at : at + 8, :] = jnp.sum(rows_of, axis=1).astype(jnp.bfloat16)
    low = lanes_at((sub, 128), 1) < 64
    for s_r in range(plan.nr):
        for s_f in range(plan.nf):
            dest = s_r * plan.nf + s_f
            first, half = s_r * plan.slice_width + s_f // 2 * 2 * sub, s_f % 2
            for k in range(chunks // 2):
                at = (half * chunks // 2 + k) * 128
                out_ref[dest, k * local : (k + 1) * local, :] = g_ref[:, at : at + 128]
            upper, lower = halves[half][first : first + sub], halves[1 - half][first + sub : first + 2 * sub]
            out_ref[dest, plan.acts_at : plan.packed_at, :] = jnp.where(low, upper, lower)


def by_frame_device(plan, got_ref, at, height):
    return jnp.concatenate(
        [
            jnp.concatenate(
                [got_ref[r * plan.nf + f, at : at + height, :] for r in range(plan.nr)], axis=1
            )
            for f in range(plan.nf)
        ],
        axis=0,
    )


def in_places(plan, merged, height):
    width = plan.tl * plan.image
    return [
        jnp.concatenate(
            [merged[f * height : (f + 1) * height, k * width : (k + 1) * width] for f in range(plan.nf)],
            axis=1,
        )
        for k in range(4)
    ]


def coarse_kernel(
    plan,
    got_ref,
    weights,
    gain_c,
    bias_c,
    gain_f,
    bias_f,
    mine_ref,
    sent_ref,
    held_ref,
    inv_ref,
    fine_ref,
    columns,
    fine_order,
    by_column,
    order,
    source,
    products,
    conv_ref,
):
    sub, nr, nf, cells, tl, local = plan.sub, plan.nr, plan.nf, plan.cells, plan.tl, plan.local
    wide, depth = 2 * sub, plan.channels // 2
    pair, member, r, base = own_place(plan)
    first = r * plan.slice_width + pair * wide
    columns[0, 0:sub, :] = jnp.broadcast_to(own_column(gain_c[...], base, sub), (sub, 128))
    columns[1, 0:sub, :] = jnp.broadcast_to(own_column(bias_c[...], base, sub), (sub, 128))
    columns[2] = jnp.broadcast_to(own_column(gain_f[...], first, wide), (wide, 128))
    columns[3] = jnp.broadcast_to(own_column(bias_f[...], first, wide), (wide, 128))
    order[...] = merged_order(plan.nr, 4, plan.tl, plan.cells)
    fine_order[...] = merged_order(plan.nr, 8, plan.tl, plan.cells // 2)
    by_column[...] = column_order(plan)
    both = pl.ds(pl.multiple_of(pair * wide, wide), wide)
    half = pl.ds(pl.multiple_of(member * depth, depth), depth)
    for s_f in range(nf):
        for s_r in range(nr):
            for t in range(tl):
                at = (s_f * tl + t) * plan.image + s_r * cells
                for k in range(plan.chunks // 2):
                    source[at : at + cells, k * 128 : (k + 1) * 128] = got_ref[
                        s_r * nf + s_f, k * local + t * cells : k * local + (t + 1) * cells, :
                    ]
    source[plan.places :, :] = jnp.zeros((2 * plan.image, depth), jnp.bfloat16)
    products[...] = sum(
        one_hot_dot(
            weights[9 * k : 9 * k + 9, both, half].reshape(9 * wide, depth),
            source[(2 - k) * plan.image : (2 - k) * plan.image + plan.places, :],
            ((1,), (1,)),
        )
        for k in range(3)
    )
    merged = one_hot_dot(by_frame_device(plan, got_ref, plan.acts_at, sub), fine_order[...], ((1,), (0,)))
    parts = halves_at(plan, merged)
    for pq in range(4):
        fine_ref[pq] = parts[pq]
    one, two = total(parts), total([part * part for part in parts])
    stats = terms(as_row(one) + pltpu.roll(as_row(two), 64, 1), 3)
    stats = jnp.concatenate(stats + [jnp.zeros_like(stats[0])] * 5, axis=0).astype(jnp.bfloat16)
    found = []
    for at in (plan.packed_at, plan.cot_at):
        merged = one_hot_dot(by_frame_device(plan, got_ref, at, 8), order[...], ((1,), (0,)))
        found.append(jnp.concatenate(in_places(plan, merged, 8), axis=0))
    values, cot = found
    gain, bias = columns[0][0:sub, 0:1], columns[1][0:sub, 0:1]
    entries = plan.places * plan.group_width
    mean, inv_std = statistics(total([values]), total([values * values]), entries, plan.group_width)
    (normed,), (slope,) = normalised([values], gain, bias, mean, inv_std)
    held_ref[0], held_ref[1], held_ref[2] = normed, slope, cot
    inv_ref[...] = jnp.broadcast_to(inv_std, (sub, 128))
    lane, has_left, has_right, has_up, has_down = plan.place_masks(plan.w)
    by_col = []
    for col in range(3):
        parts = [products[pl.ds((3 * row + col) * wide, wide), :] for row in range(3)]
        by_col.append(parts[1] + moved(parts[0], plan.w, has_down) + moved(parts[2], -plan.w, has_up))
    conv_ref[...] = by_col[1] + moved(by_col[0], 1, has_right) + moved(by_col[2], -1, has_left)
    mine_ref[...] = conv_ref[pl.ds(pl.multiple_of(member * sub, sub), sub), :]
    theirs = conv_ref[pl.ds(pl.multiple_of((1 - member) * sub, sub), sub), :]
    sent_ref[0:sub, :] = theirs.astype(jnp.bfloat16)
    sent_ref[sub:, 0:128] = stats
    sent_ref[sub:, 128:] = jnp.zeros((8, plan.places - 128), jnp.bfloat16)


def quarter_kernel(plan, mine_ref, both_ref, held_ref, inv_ref, columns, by_column, out_ref, sums_ref):
    sub = plan.sub
    _, member, _, _ = own_place(plan)
    conv = mine_ref[...] + both_ref[1 - member, 0:sub, :].astype(jnp.float32)
    normed, slope, cot = held_ref[0], held_ref[1], held_ref[2]
    gain, inv_std = columns[0][0:sub, 0:1], inv_ref[:, 0:1]
    entries = plan.places * plan.group_width
    pre = conv * slope
    one, two = total([pre]), total([pre * normed])
    group_one = in_groups(gain * one, plan.group_width) / entries
    group_two = in_groups(gain * two, plan.group_width) / entries
    grad = cot + inv_std * (gain * pre - group_one - normed * group_two)
    quartered = (grad * 0.25).astype(jnp.bfloat16)
    sent = one_hot_dot(quartered, by_column[...], ((1,), (0,))).astype(jnp.bfloat16)
    low = lanes_at((sub // 2, 128), 1) < 64
    for half in range(2):
        at = half * 256
        border = sent[:, 512 + half * 128 : 640 + half * 128]
        border = jnp.where(low, border[: sub // 2], border[sub // 2 :])
        for dest in range(half, plan.count, 2):
            out_ref[dest, 0:sub, :] = sent[:, at : at + 128]
            out_ref[dest, sub : 2 * sub, :] = sent[:, at + 128 : at + 256]
            out_ref[dest, 2 * sub : 2 * sub + sub // 2, :] = border
    sums_ref[...] = jnp.concatenate([as_row(one), as_row(two)], axis=0)


def halves_at(plan, merged):
    sub = plan.sub
    turned = jnp.concatenate([pltpu.roll(merged[:, k * 128 : (k + 1) * 128], 64, 1) for k in range(4)], axis=1)
    low = lanes_at((sub, 128), 1) < 64
    parts = []
    for pq in range(4):
        groups = []
        for group in range(2):
            e = 4 * group + pq
            at = e // 2 * 128
            strips = []
            for m in range(plan.nf // 2):
                first, second = slice(2 * m * sub, (2 * m + 1) * sub), slice((2 * m + 1) * sub, (2 * m + 2) * sub)
                if e % 2 == 0:
                    strips.append(jnp.where(low, merged[first, at : at + 128], turned[second, at : at + 128]))
                else:
                    strips.append(jnp.where(low, turned[first, at : at + 128], merged[second, at : at + 128]))
            groups.append(jnp.concatenate(strips, axis=1))
        parts.append(jnp.concatenate(groups, axis=0))
    return parts


def halves_from(plan, parts):
    sub = plan.sub
    low = lanes_at((sub, 128), 1) < 64
    down = []
    for f in range(plan.nf):
        across = []
        for v in range(4):
            pair = []
            for e in (2 * v, 2 * v + 1):
                group, pq = e // 4, e % 4
                strip = parts[pq][group * sub : (group + 1) * sub, f // 2 * 128 : (f // 2 + 1) * 128]
                pair.append(strip if e % 2 == f % 2 else pltpu.roll(strip, 64, 1))
            across.append(jnp.where(low, pair[0], pair[1]))
        down.append(jnp.concatenate(across, axis=1))
    return jnp.concatenate(down, axis=0)


def fine_kernel(
    plan, got_ref, acts_ref, both_ref, columns, order, sums_ref, weights, out_ref, source, border, products, beyond
):
    sub, nr, nf, wide = plan.sub, plan.nr, plan.nf, 2 * plan.sub
    pair, member, r, _ = own_place(plan)
    both = pl.ds(pl.multiple_of(pair * wide, wide), wide)
    w = plan.w // 2
    lines = plan.places // plan.w
    places = lines * w
    for k in range(2):
        source[:, k * 128 : (k + 1) * 128] = got_ref[:, k * sub : (k + 1) * sub, :].reshape(plan.channels, 128)
    packed = got_ref[:, wide : wide + sub // 2, :].reshape(plan.count * sub // 2, 128)
    shape = (128, places)
    beside = lanes_at(shape, 1) == lanes_at(shape, 0) % lines * w + (1 - member) * (w - 1)
    for k in range(2):
        here = one_hot(beside & (lanes_at(shape, 0) // lines == k))
        found = one_hot_dot(packed, here, ((1,), (0,))).astype(jnp.bfloat16)
        for s in range(plan.count):
            border[s * sub + k * (sub // 2) : s * sub + (k + 1) * (sub // 2), :] = found[
                s * (sub // 2) : (s + 1) * (sub // 2)
            ]
    image = plan.image // 2
    sums, extras = 0.0, 0.0
    for k in (2, 1, 0):
        here, beside = source[...], border[...]
        if k < 2:
            shift = (2 - k) * image
            inside = lanes_at((1, places), 1) < places - shift
            here, beside = [
                jnp.where(inside, pltpu.roll(part, places - shift, 1), jnp.zeros_like(part)) for part in (here, beside)
            ]
        sums = sums + one_hot_dot(
            weights[9 * k : 9 * k + 9, both, :].reshape(9 * wide, plan.channels), here, ((1,), (0,))
        )
        facing = jnp.concatenate([weights[9 * k + 3 * row + 2 * member, both, :] for row in range(3)], axis=0)
        extras = extras + one_hot_dot(facing, beside, ((1,), (0,)))
    products[...], beyond[...] = sums, extras
    parts = [acts_ref[pq] for pq in range(4)]
    stats = sum(both_ref[k, sub : sub + 8, 0:128].astype(jnp.float32) for k in range(2))
    stats = stats[0:1] + stats[1:2] + stats[2:3]
    entries = 4 * plan.places * plan.group_width
    one, two = own_column(stats, 0, wide), own_column(stats, 64, wide)
    mean, inv_std = statistics(one, two, entries, plan.group_width)
    gain, bias = columns[2][:, 0:1], columns[3][:, 0:1]
    normed, slope = normalised(parts, gain, bias, mean, inv_std)
    lane, has_left, has_right, has_up, has_down = plan.place_masks(w)
    right, left = (1 - member).astype(jnp.float32), member.astype(jnp.float32)
    by_row = []
    for row in range(3):
        a, b, c = [products[pl.ds((3 * row + col) * wide, wide), :] for col in range(3)]
        extra = beyond[pl.ds(row * wide, wide), :]
        by_row.append(
            (a + b + moved(c, -1, has_left) + left * extra, moved(a, 1, has_right) + b + c + right * extra)
        )
    convs = [by_row[0][q] + by_row[1][q] + moved(by_row[2][q], -w, has_up) for q in range(2)]
    convs += [moved(by_row[0][q], w, has_down) + by_row[1][q] + by_row[2][q] for q in range(2)]
    pre = [conv * part for conv, part in zip(convs, slope)]
    one = total(pre)
    two = total([a * b for a, b in zip(pre, normed)])
    cot = source[pl.ds(pl.multiple_of(r * plan.slice_width + pair * wide, wide), wide), :].astype(jnp.float32)
    scale = inv_std * gain
    stacked = halves_from(plan, [cot + scale * part for part in pre]).astype(jnp.bfloat16)
    sent = one_hot_dot(stacked, order[...], ((1,), (1,))).astype(jnp.bfloat16)
    coarse = sums_ref[0:1] + pltpu.roll(sums_ref[1:2], sub, 1)
    coded = (
        terms(as_row(one) + pltpu.roll(as_row(two), 64, 1), 2)
        + terms(coarse, 2)
        + terms(as_row(inv_std) + pltpu.roll(as_row(mean), 64, 1), 3)
    )
    coded = jnp.concatenate(coded + [jnp.zeros_like(coarse)], axis=0).astype(jnp.bfloat16)
    for s_r in range(nr):
        for s_f in range(nf):
            out_ref[s_f * nr + s_r, 0:sub, :] = sent[s_f * sub : (s_f + 1) * sub, s_r * 128 : (s_r + 1) * 128]
            out_ref[s_f * nr + s_r, sub : sub + 8, :] = coded


def spread_kernel(plan, got_ref, acts_ref, gain_ref, out_ref, sums_ref):
    sub, nr, nf = plan.sub, plan.nr, plan.nf
    low = lanes_at((sub, 128), 1) < 64
    low_row = lanes_at((1, 128), 1) < 64
    first_row = lanes_at((1, 128), 1) < sub
    source = []
    fine, coarse, moments = [[], []], [[], []], [[], []]
    for s_r in range(nr):
        ones, twos, c_ones, c_twos, invs, means = [], [], 0.0, 0.0, [], []
        for pair in range(nf // 2):
            at = 2 * pair * nr + s_r
            left, right = [got_ref[at + k * nr, 0:sub, :].astype(jnp.float32) for k in range(2)]
            source.append(jnp.where(low, left, pltpu.roll(right, 64, 1)))
            source.append(jnp.where(low, pltpu.roll(left, 64, 1), right))
            coded = [got_ref[at + k * nr, sub : sub + 8, :].astype(jnp.float32) for k in range(2)]
            sums = coded[0][0:1] + coded[0][1:2] + coded[1][0:1] + coded[1][1:2]
            ones.append(sums if pair == 0 else pltpu.roll(sums, 64, 1))
            twos.append(pltpu.roll(sums, 64, 1) if pair == 0 else sums)
            both = coded[0][4:5] + coded[0][5:6] + coded[0][6:7]
            invs.append(both if pair == 0 else pltpu.roll(both, 64, 1))
            means.append(pltpu.roll(both, 64, 1) if pair == 0 else both)
            for k in range(2):
                sums = coded[k][2:3] + coded[k][3:4]
                to = (2 * pair + k) * sub
                c_one = jnp.where(first_row, sums, 0.0)
                c_two = jnp.where(first_row, pltpu.roll(sums, 128 - sub, 1), 0.0)
                c_ones = c_ones + (pltpu.roll(c_one, to, 1) if to else c_one)
                c_twos = c_twos + (pltpu.roll(c_two, to, 1) if to else c_two)
        fine[0].append(jnp.where(low_row, ones[0], ones[1]))
        fine[1].append(jnp.where(low_row, twos[0], twos[1]))
        moments[0].append(jnp.where(low_row, invs[0], invs[1]))
        moments[1].append(jnp.where(low_row, means[0], means[1]))
        coarse[0].append(c_ones)
        coarse[1].append(c_twos)
    one, two, inv_std, mean, c_one, c_two = [jnp.concatenate(part, axis=1) for part in fine + moments + coarse]
    source = jnp.concatenate(source, axis=0).astype(jnp.bfloat16)
    result = one_hot_dot(pixel_order(plan, False), source, ((1,), (1,)))
    gain = gain_ref[...]
    entries = 4 * plan.places * plan.group_width
    group_one = in_lane_groups(gain * one, plan.group_width) / entries
    group_two = in_lane_groups(gain * two, plan.group_width) / entries
    normed = (acts_ref[...].astype(jnp.float32) - mean) * inv_std
    out_ref[...] = (result - inv_std * (group_one + normed * group_two)).astype(jnp.bfloat16)
    sums_ref[...] = jnp.concatenate([one, two, c_one, c_two] + [jnp.zeros_like(one)] * 4, axis=0)


def total_kernel(scales, both_ref, result_ref, result_hbm, out_hbms, rows_ref, sems):
    copies = fetched([(result_ref, result_hbm)], sems)
    rows = sum(both_ref[k] for k in range(both_ref.shape[0]))
    for k in range(4):
        rows_ref[k] = rows[k : k + 1] * scales[k]
    for k in range(4):
        copies.append(pltpu.make_async_copy(rows_ref.at[k], out_hbms[k], sems.at[k + 1]))
        copies[-1].start()
    for copy in copies:
        copy.wait()


def in_vmem(count):
    return [pl.BlockSpec(memory_space=pltpu.VMEM)] * count


def in_hbm(count):
    return [pl.BlockSpec(memory_space=pltpu.HBM)] * count


def kept(array):
    return pltpu.with_memory_space_constraint(array, pltpu.HBM)


def shape_of(shape, kind):
    return jax.ShapeDtypeStruct(shape, kind)


LIMIT = pltpu.CompilerParams(vmem_limit_bytes=40 * 1024 * 1024)
COST = pl.CostEstimate(flops=2_000_000_000, bytes_accessed=4_000_000, transcendentals=0)


def fast_shards(
    plan,
    acts_fine,
    acts_coarse,
    grad_coarse,
    gain_fine,
    bias_fine,
    kernel_fine,
    gain_coarse,
    bias_coarse,
    kernel_coarse,
):
    nd = lax.axis_size("dp")
    count, sub, channels, places, local = plan.count, plan.sub, plan.channels, plan.places, plan.local
    f32, bf16 = jnp.float32, jnp.bfloat16
    rows = [part.reshape(1, channels) for part in (gain_coarse, bias_coarse, gain_fine, bias_fine)]
    places_of = ((local, channels), (local, channels), (4 * local, channels))
    fetched_of = pl.pallas_call(
        fetch_kernel,
        out_shape=tuple(pltpu.VMEM(shape, bf16) for shape in places_of),
        in_specs=in_hbm(3),
        out_specs=tuple(in_vmem(3)),
        scratch_shapes=[pltpu.SemaphoreType.DMA((3,))],
        compiler_params=LIMIT,
    )(*[kept(part.reshape(shape)) for part, shape in zip((grad_coarse, acts_coarse, acts_fine), places_of)])
    acts = fetched_of[2]
    packed = pl.pallas_call(
        functools.partial(pack_kernel, plan),
        out_shape=shape_of((count, plan.block_rows, 128), bf16),
        in_specs=in_vmem(3),
        out_specs=in_vmem(1)[0],
        compiler_params=LIMIT,
        cost_estimate=COST,
    )(*fetched_of)
    got = lax.all_to_all(packed, BLOCK, 0, 0)
    mine, theirs, held, inv_std, fine_acts, columns, fine_order, by_column = pl.pallas_call(
        functools.partial(coarse_kernel, plan),
        out_shape=(
            shape_of((sub, places), f32),
            shape_of((sub + 8, places), bf16),
            shape_of((3, sub, places), f32),
            shape_of((sub, 128), f32),
            shape_of((4, 2 * sub, places // 2), f32),
            shape_of((4, 2 * sub, 128), f32),
            shape_of((4 * plan.nr * local, 4 * plan.nr * local), bf16),
            shape_of((places, places + places // 2), bf16),
        ),
        in_specs=in_vmem(6),
        out_specs=tuple(in_vmem(8)),
        scratch_shapes=[
            pltpu.VMEM((4 * plan.nr * local, 4 * plan.nr * local), bf16),
            pltpu.VMEM((places + 2 * plan.image, channels // 2), bf16),
            pltpu.VMEM((18 * sub, places), f32),
            pltpu.VMEM((2 * sub, places), f32),
        ],
        compiler_params=LIMIT,
        cost_estimate=COST,
    )(got, kernel_coarse, *rows)
    both = lax.all_gather(theirs, "member")
    quartered, coarse_sums = pl.pallas_call(
        functools.partial(quarter_kernel, plan),
        out_shape=(shape_of((count, 2 * sub + sub // 2, 128), bf16), shape_of((2, 128), f32)),
        in_specs=in_vmem(6),
        out_specs=tuple(in_vmem(2)),
        compiler_params=LIMIT,
        cost_estimate=COST,
    )(mine, both, held, inv_std, columns, by_column)
    spread = lax.all_to_all(quartered, BLOCK, 0, 0)
    sent = pl.pallas_call(
        functools.partial(fine_kernel, plan),
        out_shape=shape_of((count, sub + 8, 128), bf16),
        in_specs=in_vmem(7),
        out_specs=in_vmem(1)[0],
        scratch_shapes=[
            pltpu.VMEM((channels, places // 2), bf16),
            pltpu.VMEM((channels, places // 2), bf16),
            pltpu.VMEM((18 * sub, places // 2), f32),
            pltpu.VMEM((6 * sub, places // 2), f32),
        ],
        compiler_params=LIMIT,
        cost_estimate=COST,
    )(spread, fine_acts, both, columns, fine_order, coarse_sums, kernel_fine)
    back = lax.all_to_all(sent, BACK_BLOCK, 0, 0)
    cells = nd * places
    fine_scale, coarse_scale = 1.0 / math.sqrt(4 * cells), 1.0 / math.sqrt(cells)
    out, sums = pl.pallas_call(
        functools.partial(spread_kernel, plan),
        out_shape=(pltpu.VMEM((4 * local, channels), bf16), shape_of((8, channels), f32)),
        in_specs=in_vmem(3),
        out_specs=tuple(in_vmem(2)),
        compiler_params=LIMIT,
        cost_estimate=COST,
    )(back, acts, rows[2])
    both = lax.all_gather(sums, "dp")
    out, sums = pl.pallas_call(
        functools.partial(total_kernel, (fine_scale, fine_scale, coarse_scale, coarse_scale)),
        out_shape=(pltpu.HBM((4 * local, channels), bf16), (pltpu.HBM((1, channels), f32),) * 4),
        in_specs=in_vmem(2),
        out_specs=(in_hbm(1)[0], tuple(in_hbm(4))),
        scratch_shapes=[pltpu.VMEM((4, 1, channels), f32), pltpu.SemaphoreType.DMA((5,))],
        compiler_params=LIMIT,
        cost_estimate=COST,
    )(both, out)
    bias_f, gain_f, bias_c, gain_c = [part.reshape(channels) for part in sums]
    return out.reshape(acts_fine.shape), gain_f, bias_f, gain_c, bias_c


def solution(mesh):
    def function(*arrays):
        local = [size // mesh.shape[axis] for size, axis in zip(arrays[1].shape, ("dp", "frames", "rows"))]
        sizes = (mesh.shape["frames"], mesh.shape["rows"])
        plan = Plan(sizes, (*local[1:], *arrays[1].shape[3:]), arrays[5].shape[1] // mesh.shape["rows"])
        if plan.fits:
            split = (mesh.shape["dp"], plan.nf // 2, 2, plan.nr)
            used = jax.sharding.Mesh(mesh.devices.reshape(split), ("dp", "pairs", "member", "rows"))
            shards, frames = functools.partial(fast_shards, plan), ("pairs", "member")
        else:
            used, shards, frames = mesh, plain_shards, "frames"
        blocks, kernel = P("dp", frames, "rows", None, None), P(None, "rows", None)
        in_specs = (blocks, blocks, blocks, P(), P(), kernel, P(), P(), kernel)
        out_specs = (blocks, P(), P(), P(), P())
        mapped = jax.shard_map(shards, mesh=used, in_specs=in_specs, out_specs=out_specs, check_vma=False)
        return mapped(*arrays)

    return function
```

```python
import functools
import math

import jax
import jax.numpy as jnp
from jax import lax
from jax.experimental import pallas as pl
from jax.experimental.pallas import tpu as pltpu
from jax.sharding import PartitionSpec as P

GROUPS = 32
EPSILON = 1e-06
BLOCK = ("rows", "pairs", "member")
BACK_BLOCK = ("pairs", "member", "rows")
PLAIN_BLOCK = ("frames", "rows")


def plain_everyone(block, count):
    copies = jnp.broadcast_to(block[None], (count,) + block.shape)
    return lax.all_to_all(copies, PLAIN_BLOCK, 0, 0)


def ahead(field, axis, distance):
    size = field.shape[axis]
    if distance == 0:
        return field
    widths = [(0, 0)] * field.ndim
    if distance > 0:
        widths[axis] = (0, distance)
        kept = lax.slice_in_dim(field, distance, size, axis=axis)
    else:
        widths[axis] = (-distance, 0)
        kept = lax.slice_in_dim(field, 0, size + distance, axis=axis)
    return jnp.pad(kept, widths)


def tap_products(source, kernel):
    sub = kernel.shape[1]
    frames, rows, cols, channels = source.shape
    products = lax.dot_general(
        kernel.reshape(27 * sub, channels),
        source.reshape(frames * rows * cols, channels),
        (((1,), (1,)), ((), ())),
        preferred_element_type=jnp.float32,
    ).reshape(3, 3, 3, sub, frames, rows, cols)
    return sum(ahead(products[depth], 3, 2 - depth) for depth in range(3))


def coarse_conv(source, kernel):
    spatial = tap_products(source, kernel)
    total = 0.0
    for row in range(3):
        part = sum(ahead(spatial[row, col], 3, 1 - col) for col in range(3))
        total = total + ahead(part, 2, 1 - row)
    return total


def fine_conv(source, kernel):
    spatial = tap_products(source, kernel)
    result = []
    for p in range(2):
        rows_of = []
        for q in range(2):
            total = 0.0
            for row in range(3):
                part = sum(ahead(spatial[row, col], 3, (q + 1 - col) // 2) for col in range(3))
                total = total + ahead(part, 2, (p + 1 - row) // 2)
            rows_of.append(total)
        result.append(jnp.stack(rows_of, 1))
    return jnp.stack(result, 1)


def group_total(sums, group_width):
    sub = sums.shape[-1]
    if sub % group_width == 0:
        grouped = jnp.sum(sums.reshape(-1, sub // group_width, group_width), axis=-1)
        return jnp.repeat(grouped, group_width, axis=-1)
    spread = jnp.moveaxis(lax.all_gather(sums, "frames"), 0, 1).reshape(sums.shape[0], -1, group_width)
    mine = lax.axis_index("frames") * sub // group_width
    grouped = lax.dynamic_index_in_dim(jnp.sum(spread, -1), mine, 1)
    return jnp.broadcast_to(grouped, sums.shape)


def level(acts, conv_grad, cotangent, gain, bias, group_width):
    sub = acts.shape[0]
    places = acts.size // sub
    values = acts.astype(jnp.float32).reshape(sub, places)
    conv_grad = conv_grad.reshape(sub, places)
    entries = places * group_width
    moments = group_total(
        jnp.stack([jnp.sum(values, 1), jnp.sum(values * values, 1)]), group_width
    ) / entries
    mean = moments[0]
    inv_std = lax.rsqrt(moments[1] - mean * mean + EPSILON)
    normed = (values - mean[:, None]) * inv_std[:, None]
    preact = gain[:, None] * normed + bias[:, None]
    squash = jax.nn.sigmoid(preact)
    pre_grad = conv_grad * squash * (1.0 + preact * (1.0 - squash))
    sums = jnp.stack([jnp.sum(pre_grad, 1), jnp.sum(pre_grad * normed, 1)])
    terms = group_total(sums * gain, group_width) / entries
    grad = cotangent.reshape(sub, places) + inv_std[:, None] * (
        gain[:, None] * pre_grad - terms[0][:, None] - normed * terms[1][:, None]
    )
    return grad, sums


def plain_shards(
    acts_fine,
    acts_coarse,
    grad_coarse,
    gain_fine,
    bias_fine,
    kernel_fine,
    gain_coarse,
    bias_coarse,
    kernel_coarse,
):
    nf, nr, nd = lax.axis_size("frames"), lax.axis_size("rows"), lax.axis_size("dp")
    count = nf * nr
    channels = acts_fine.shape[-1]
    slice_width = kernel_fine.shape[1]
    sub = slice_width // nf
    group_width = channels // GROUPS
    tl, hl, w = acts_coarse.shape[1:4]
    frames, rows = tl * nf, hl * nr
    f, r = lax.axis_index("frames"), lax.axis_index("rows")

    gathered = plain_everyone(grad_coarse[0], count)
    source = (
        gathered.reshape(nf, nr, tl, hl, w, channels)
        .transpose(0, 2, 1, 3, 4, 5)
        .reshape(frames, rows, w, channels)
    )
    coarse_in = acts_coarse[0].reshape(tl, hl, w, nr, nf, sub).transpose(4, 3, 5, 0, 1, 2)
    coarse_in = lax.all_to_all(coarse_in.reshape(count, sub, tl * hl * w), PLAIN_BLOCK, 0, 0)
    fine_in = acts_fine[0].reshape(tl, hl, 2, w, 2, nr, nf, sub).transpose(6, 5, 7, 2, 4, 0, 1, 3)
    fine_in = lax.all_to_all(fine_in.reshape(count, sub, 4 * tl * hl * w), PLAIN_BLOCK, 0, 0)

    def mine(vector):
        return lax.dynamic_slice_in_dim(vector, r * slice_width + f * sub, sub)

    def own(kernel):
        return lax.dynamic_slice_in_dim(kernel, f * sub, sub, axis=1)

    coarse_vals = (
        coarse_in.reshape(nf, nr, sub, tl, hl, w).transpose(2, 0, 3, 1, 4, 5).reshape(sub, frames, rows, w)
    )
    cot = lax.dynamic_slice_in_dim(source, r * slice_width + f * sub, sub, axis=3)
    cot = cot.astype(jnp.float32).transpose(3, 0, 1, 2)
    conv = coarse_conv(source, own(kernel_coarse))
    coarse_grad, coarse_sums = level(
        coarse_vals, conv, cot, mine(gain_coarse), mine(bias_coarse), group_width
    )
    quartered = (coarse_grad * 0.25).astype(jnp.bfloat16)
    spread = plain_everyone(quartered, count)
    source_fine = (
        spread.reshape(nf, nr, sub, frames, rows, w)
        .transpose(3, 4, 5, 1, 0, 2)
        .reshape(frames, rows, w, channels)
    )
    conv = fine_conv(source_fine, own(kernel_fine))
    fine_vals = (
        fine_in.reshape(nf, nr, sub, 2, 2, tl, hl, w)
        .transpose(2, 3, 4, 0, 5, 1, 6, 7)
        .reshape(sub, 2, 2, frames, rows, w)
    )
    cot = jnp.broadcast_to(
        quartered.astype(jnp.float32).reshape(sub, 1, 1, frames, rows, w), conv.shape
    )
    fine_grad, fine_sums = level(
        fine_vals, conv, cot, mine(gain_fine), mine(bias_fine), group_width
    )
    back = (
        fine_grad.astype(jnp.bfloat16)
        .reshape(sub, 2, 2, nf, tl, nr, hl, w)
        .transpose(3, 5, 0, 1, 2, 4, 6, 7)
        .reshape(count, sub, 4 * tl * hl * w)
    )
    sums = plain_everyone(jnp.concatenate([fine_sums, coarse_sums]), count)
    back = lax.all_to_all(back, PLAIN_BLOCK, 0, 0)
    out = (
        back.reshape(nf, nr, sub, 2, 2, tl, hl, w)
        .transpose(5, 6, 3, 7, 4, 1, 0, 2)
        .reshape(1, tl, 2 * hl, 2 * w, channels)
    )
    sums = sums.reshape(nf, nr, 4, sub).transpose(2, 1, 0, 3).reshape(4, channels)
    totals = lax.psum(sums, "dp")
    cells = nd * frames * rows * w
    scale_fine = 1.0 / jnp.sqrt(jnp.float32(4 * cells))
    scale_coarse = 1.0 / jnp.sqrt(jnp.float32(cells))
    return (
        out,
        totals[1] * scale_fine,
        totals[0] * scale_fine,
        totals[3] * scale_coarse,
        totals[2] * scale_coarse,
    )


def lanes_at(shape, axis):
    return lax.broadcasted_iota(jnp.int32, shape, axis)


def one_hot(found):
    return found.astype(jnp.float32).astype(jnp.bfloat16)


def pixel_order(plan, swapped):
    tl, hl, w = plan.tl, plan.hl, plan.w // 2
    size = 4 * plan.local
    lane = lanes_at((1, size), 1)
    j, i, t = lane % w, lane // w % hl, lane // (w * hl) % tl
    q, p = lane // (w * hl * tl) % 2, lane // (2 * w * hl * tl) % 2
    half = lane // (4 * w * hl * tl)
    if swapped:
        half = 1 - half
    pixel = (t * 2 * hl + 2 * i + p) * 4 * w + 2 * (half * w + j) + q
    return one_hot(lanes_at((size, size), 0) == pixel)


def merged_order(nr, outer, tl, cells):
    size = nr * outer * tl * cells
    lane = lanes_at((1, size), 1)
    cell, dev = lane % cells, lane // cells % nr
    t, o = lane // (cells * nr) % tl, lane // (cells * nr * tl)
    return one_hot(lanes_at((size, size), 0) == ((dev * outer + o) * tl + t) * cells + cell)


def column_order(plan):
    w = plan.w // 2
    lines = plan.places // plan.w
    lane = lanes_at((1, 4 * lines * w + 4 * lines), 1)
    inner = lane % (lines * w)
    place = inner // w * plan.w + lane // (lines * w) * w + inner % w
    past = lane - 2 * lines * w
    border = past % lines * plan.w + jnp.where(past < 2 * lines, w, w - 1)
    wanted = jnp.where(past >= 0, border, place)
    shape = (plan.places, 2 * lines * w + 4 * lines)
    return one_hot(lanes_at(shape, 0) == wanted[:, : shape[1]])


def one_hot_dot(a, b, dims):
    return lax.dot_general(a, b, (dims, ((), ())), preferred_element_type=jnp.float32)


def moved(field, distance, kept):
    size = field.shape[1]
    return jnp.where(kept, pltpu.roll(field, (-distance) % size, 1), 0.0)


def own_column(row, base, sub):
    shape = (sub, row.shape[1])
    mine = lanes_at(shape, 1) == lanes_at(shape, 0) + base
    return jnp.sum(jnp.where(mine, row, 0.0), axis=1, keepdims=True)


def as_row(column):
    shape = (column.shape[0], 128)
    here = lanes_at(shape, 1) == lanes_at(shape, 0)
    return jnp.sum(jnp.where(here, column, 0.0), axis=0, keepdims=True)


def terms(value, count):
    found = []
    for _ in range(count):
        found.append(value.astype(jnp.bfloat16).astype(jnp.float32))
        value = value - found[-1]
    return found


def in_groups(column, group_width):
    sub = column.shape[0]
    grouped = jnp.sum(column.reshape(sub // group_width, group_width, 1), axis=1, keepdims=True)
    return jnp.broadcast_to(grouped, (sub // group_width, group_width, 1)).reshape(sub, 1)


def in_lane_groups(row, group_width):
    lane = lanes_at(row.shape, 1)
    size = row.shape[1]
    step = 1
    while step < group_width:
        up, down = pltpu.roll(row, size - step, 1), pltpu.roll(row, step, 1)
        row = row + jnp.where(lane // step % 2 == 0, up, down)
        step *= 2
    return row


def total(parts):
    return sum(jnp.sum(part, axis=1, keepdims=True) for part in parts)


def statistics(one, two, entries, group_width):
    mean = in_groups(one, group_width) / entries
    square = in_groups(two, group_width) / entries
    return mean, lax.rsqrt(square - mean * mean + EPSILON)


def normalised(parts, gain, bias, mean, inv_std):
    normed, slope = [], []
    for part in parts:
        unit = (part - mean) * inv_std
        preact = gain * unit + bias
        squash = 0.5 + 0.5 * jnp.tanh(0.5 * preact)
        normed.append(unit)
        slope.append(squash * (1.0 + preact * (1.0 - squash)))
    return normed, slope


class Plan:
    def __init__(self, mesh_sizes, acts_coarse, slice_width):
        self.nf, self.nr = mesh_sizes
        self.count = self.nf * self.nr
        self.tl, self.hl, self.w, self.channels = acts_coarse
        self.slice_width = slice_width
        self.sub = slice_width // self.nf
        self.cells = self.hl * self.w
        self.local = self.tl * self.cells
        self.image = self.cells * self.nr
        self.frames = self.tl * self.nf
        self.places = self.frames * self.image
        self.group_width = self.channels // GROUPS
        self.chunks = self.channels // 128
        self.acts_at = self.chunks // 2 * self.local
        self.packed_at = self.acts_at + self.sub
        self.cot_at = self.packed_at + 8
        self.block_rows = self.cot_at + 8
        self.fits = (
            self.sub == 32
            and self.slice_width == 128
            and self.group_width == 16
            and self.cells == 16
            and self.w == 8
            and self.tl == 2
            and self.nr == 4
            and self.nf == 4
            and self.slice_width * self.nr == self.channels
        )

    def place_masks(self, w):
        lane = lanes_at((1, self.places // self.w * w), 1)
        col, row = lane % w, lane // w % (self.hl * self.nr)
        last_row = self.hl * self.nr - 1
        return (lane, col > 0, col < w - 1, row > 0, row < last_row)


def fetched(pairs, sems):
    copies = [pltpu.make_async_copy(src, dst, sems.at[k]) for k, (src, dst) in enumerate(pairs)]
    for copy in copies:
        copy.start()
    return copies


def own_place(plan):
    pair, member, r = lax.axis_index("pairs"), lax.axis_index("member"), lax.axis_index("rows")
    return pair, member, r, r * plan.slice_width + (2 * pair + member) * plan.sub


def fetch_kernel(g_hbm, coarse_hbm, fine_hbm, g_ref, coarse_ref, fine_ref, sems):
    for copy in fetched([(fine_hbm, fine_ref), (coarse_hbm, coarse_ref), (g_hbm, g_ref)], sems):
        copy.wait()


def pack_kernel(plan, g_ref, coarse_ref, fine_ref, out_ref):
    sub, chunks, local = plan.sub, plan.chunks, plan.local
    shape = (2 * local, 2 * 128)
    lane = lanes_at((1, 2 * 128), 1)
    repeated = one_hot(lanes_at(shape, 0) == lane % local + lane // 128 * local)
    shape = (plan.channels, 128)
    quarter = lanes_at(shape, 0) // 8 % 4 == lanes_at(shape, 1) // local
    orders = jnp.concatenate([pixel_order(plan, swapped) for swapped in (False, True)], axis=1)
    acts = fine_ref[...]
    halves = one_hot_dot(acts, orders, ((0,), (0,))).astype(jnp.bfloat16)
    halves = [halves[:, :128], halves[:, 128:]]
    small = one_hot_dot(jnp.concatenate([coarse_ref[...], g_ref[...]], axis=0), repeated, ((0,), (0,)))
    for k, at in enumerate((plan.packed_at, plan.cot_at)):
        rows_of = jnp.where(quarter, small[:, k * 128 : (k + 1) * 128], 0.0).reshape(plan.count, 4, 8, 128)
        out_ref[:, at : at + 8, :] = jnp.sum(rows_of, axis=1).astype(jnp.bfloat16)
    low = lanes_at((sub, 128), 1) < 64
    for s_r in range(plan.nr):
        for s_f in range(plan.nf):
            dest = s_r * plan.nf + s_f
            first, half = s_r * plan.slice_width + s_f // 2 * 2 * sub, s_f % 2
            for k in range(chunks // 2):
                at = (half * chunks // 2 + k) * 128
                out_ref[dest, k * local : (k + 1) * local, :] = g_ref[:, at : at + 128]
            upper, lower = halves[half][first : first + sub], halves[1 - half][first + sub : first + 2 * sub]
            out_ref[dest, plan.acts_at : plan.packed_at, :] = jnp.where(low, upper, lower)


def by_frame_device(plan, got_ref, at, height):
    return jnp.concatenate(
        [
            jnp.concatenate(
                [got_ref[r * plan.nf + f, at : at + height, :] for r in range(plan.nr)], axis=1
            )
            for f in range(plan.nf)
        ],
        axis=0,
    )


def in_places(plan, merged, height):
    width = plan.tl * plan.image
    return [
        jnp.concatenate(
            [merged[f * height : (f + 1) * height, k * width : (k + 1) * width] for f in range(plan.nf)],
            axis=1,
        )
        for k in range(4)
    ]


def coarse_kernel(
    plan,
    got_ref,
    weights,
    gain_c,
    bias_c,
    gain_f,
    bias_f,
    mine_ref,
    sent_ref,
    held_ref,
    inv_ref,
    fine_ref,
    columns,
    fine_order,
    by_column,
    order,
    source,
    conv_ref,
):
    sub, nr, nf, cells, tl, local = plan.sub, plan.nr, plan.nf, plan.cells, plan.tl, plan.local
    wide, depth = 2 * sub, plan.channels // 2
    pair, member, r, base = own_place(plan)
    first = r * plan.slice_width + pair * wide
    columns[0, 0:sub, :] = jnp.broadcast_to(own_column(gain_c[...], base, sub), (sub, 128))
    columns[1, 0:sub, :] = jnp.broadcast_to(own_column(bias_c[...], base, sub), (sub, 128))
    columns[2] = jnp.broadcast_to(own_column(gain_f[...], first, wide), (wide, 128))
    columns[3] = jnp.broadcast_to(own_column(bias_f[...], first, wide), (wide, 128))
    order[...] = merged_order(plan.nr, 4, plan.tl, plan.cells)
    fine_order[...] = merged_order(plan.nr, 8, plan.tl, plan.cells // 2)
    by_column[...] = column_order(plan)
    both = pl.ds(pl.multiple_of(pair * wide, wide), wide)
    half = pl.ds(pl.multiple_of(member * depth, depth), depth)
    for s_f in range(nf):
        for s_r in range(nr):
            for t in range(tl):
                at = (s_f * tl + t) * plan.image + s_r * cells
                for k in range(plan.chunks // 2):
                    source[at : at + cells, k * 128 : (k + 1) * 128] = got_ref[
                        s_r * nf + s_f, k * local + t * cells : k * local + (t + 1) * cells, :
                    ]
    source[plan.places :, :] = jnp.zeros((2 * plan.image, depth), jnp.bfloat16)
    products = sum(
        one_hot_dot(
            weights[9 * k : 9 * k + 9, both, half].reshape(9 * wide, depth),
            source[(2 - k) * plan.image : (2 - k) * plan.image + plan.places, :],
            ((1,), (1,)),
        )
        for k in range(3)
    )
    merged = one_hot_dot(by_frame_device(plan, got_ref, plan.acts_at, sub), fine_order[...], ((1,), (0,)))
    parts = halves_at(plan, merged)
    for pq in range(4):
        fine_ref[pq] = parts[pq]
    one, two = total(parts), total([part * part for part in parts])
    stats = terms(as_row(one) + pltpu.roll(as_row(two), 64, 1), 3)
    stats = jnp.concatenate(stats + [jnp.zeros_like(stats[0])] * 5, axis=0).astype(jnp.bfloat16)
    small = [by_frame_device(plan, got_ref, at, 8) for at in (plan.packed_at, plan.cot_at)]
    merged = one_hot_dot(jnp.concatenate(small, axis=0), order[...], ((1,), (0,)))
    rows_of = 8 * nf
    values, cot = [
        jnp.concatenate(in_places(plan, merged[k * rows_of : (k + 1) * rows_of], 8), axis=0) for k in range(2)
    ]
    gain, bias = columns[0][0:sub, 0:1], columns[1][0:sub, 0:1]
    entries = plan.places * plan.group_width
    mean, inv_std = statistics(total([values]), total([values * values]), entries, plan.group_width)
    (normed,), (slope,) = normalised([values], gain, bias, mean, inv_std)
    held_ref[0], held_ref[1], held_ref[2] = normed, slope, cot
    inv_ref[...] = jnp.broadcast_to(inv_std, (sub, 128))
    lane, has_left, has_right, has_up, has_down = plan.place_masks(plan.w)
    by_col = []
    for col in range(3):
        parts = [products[(3 * row + col) * wide : (3 * row + col + 1) * wide] for row in range(3)]
        by_col.append(parts[1] + moved(parts[0], plan.w, has_down) + moved(parts[2], -plan.w, has_up))
    conv_ref[...] = by_col[1] + moved(by_col[0], 1, has_right) + moved(by_col[2], -1, has_left)
    mine_ref[...] = conv_ref[pl.ds(pl.multiple_of(member * sub, sub), sub), :]
    theirs = conv_ref[pl.ds(pl.multiple_of((1 - member) * sub, sub), sub), :]
    sent_ref[0:sub, :] = theirs.astype(jnp.bfloat16)
    sent_ref[sub:, 0:128] = stats
    sent_ref[sub:, 128:] = jnp.zeros((8, plan.places - 128), jnp.bfloat16)


def quarter_kernel(plan, mine_ref, both_ref, held_ref, inv_ref, columns, by_column, out_ref, sums_ref):
    sub = plan.sub
    _, member, _, _ = own_place(plan)
    conv = mine_ref[...] + both_ref[1 - member, 0:sub, :].astype(jnp.float32)
    normed, slope, cot = held_ref[0], held_ref[1], held_ref[2]
    gain, inv_std = columns[0][0:sub, 0:1], inv_ref[:, 0:1]
    entries = plan.places * plan.group_width
    pre = conv * slope
    one, two = total([pre]), total([pre * normed])
    group_one = in_groups(gain * one, plan.group_width) / entries
    group_two = in_groups(gain * two, plan.group_width) / entries
    grad = cot + inv_std * (gain * pre - group_one - normed * group_two)
    quartered = (grad * 0.25).astype(jnp.bfloat16)
    sent = one_hot_dot(quartered, by_column[...], ((1,), (0,))).astype(jnp.bfloat16)
    low = lanes_at((sub // 2, 128), 1) < 64
    for half in range(2):
        at = half * 256
        border = sent[:, 512 + half * 128 : 640 + half * 128]
        border = jnp.where(low, border[: sub // 2], border[sub // 2 :])
        for dest in range(half, plan.count, 2):
            out_ref[dest, 0:sub, :] = sent[:, at : at + 128]
            out_ref[dest, sub : 2 * sub, :] = sent[:, at + 128 : at + 256]
            out_ref[dest, 2 * sub : 2 * sub + sub // 2, :] = border
    sums_ref[...] = jnp.concatenate([as_row(one), as_row(two)], axis=0)


def halves_at(plan, merged):
    sub = plan.sub
    turned = jnp.concatenate([pltpu.roll(merged[:, k * 128 : (k + 1) * 128], 64, 1) for k in range(4)], axis=1)
    low = lanes_at((sub, 128), 1) < 64
    parts = []
    for pq in range(4):
        groups = []
        for group in range(2):
            e = 4 * group + pq
            at = e // 2 * 128
            strips = []
            for m in range(plan.nf // 2):
                first, second = slice(2 * m * sub, (2 * m + 1) * sub), slice((2 * m + 1) * sub, (2 * m + 2) * sub)
                if e % 2 == 0:
                    strips.append(jnp.where(low, merged[first, at : at + 128], turned[second, at : at + 128]))
                else:
                    strips.append(jnp.where(low, turned[first, at : at + 128], merged[second, at : at + 128]))
            groups.append(jnp.concatenate(strips, axis=1))
        parts.append(jnp.concatenate(groups, axis=0))
    return parts


def halves_from(plan, parts):
    sub = plan.sub
    low = lanes_at((sub, 128), 1) < 64
    down = []
    for f in range(plan.nf):
        across = []
        for v in range(4):
            pair = []
            for e in (2 * v, 2 * v + 1):
                group, pq = e // 4, e % 4
                strip = parts[pq][group * sub : (group + 1) * sub, f // 2 * 128 : (f // 2 + 1) * 128]
                pair.append(strip if e % 2 == f % 2 else pltpu.roll(strip, 64, 1))
            across.append(jnp.where(low, pair[0], pair[1]))
        down.append(jnp.concatenate(across, axis=1))
    return jnp.concatenate(down, axis=0)


def fine_kernel(
    plan, got_ref, acts_ref, both_ref, columns, order, sums_ref, weights, out_ref, source, border
):
    sub, nr, nf, wide = plan.sub, plan.nr, plan.nf, 2 * plan.sub
    pair, member, r, _ = own_place(plan)
    both = pl.ds(pl.multiple_of(pair * wide, wide), wide)
    w = plan.w // 2
    lines = plan.places // plan.w
    places = lines * w
    for k in range(2):
        source[:, k * 128 : (k + 1) * 128] = got_ref[:, k * sub : (k + 1) * sub, :].reshape(plan.channels, 128)
    packed = got_ref[:, wide : wide + sub // 2, :].reshape(plan.count * sub // 2, 128)
    shape = (128, places)
    beside = lanes_at(shape, 1) == lanes_at(shape, 0) % lines * w + (1 - member) * (w - 1)
    for k in range(2):
        here = one_hot(beside & (lanes_at(shape, 0) // lines == k))
        found = one_hot_dot(packed, here, ((1,), (0,))).astype(jnp.bfloat16)
        for s in range(plan.count):
            border[s * sub + k * (sub // 2) : s * sub + (k + 1) * (sub // 2), :] = found[
                s * (sub // 2) : (s + 1) * (sub // 2)
            ]
    image = plan.image // 2
    sums, extras = 0.0, 0.0
    for k in (2, 1, 0):
        here, beside = source[...], border[...]
        if k < 2:
            shift = (2 - k) * image
            inside = lanes_at((1, places), 1) < places - shift
            here, beside = [
                jnp.where(inside, pltpu.roll(part, places - shift, 1), jnp.zeros_like(part)) for part in (here, beside)
            ]
        sums = sums + one_hot_dot(
            weights[9 * k : 9 * k + 9, both, :].reshape(9 * wide, plan.channels), here, ((1,), (0,))
        )
        facing = jnp.concatenate([weights[9 * k + 3 * row + 2 * member, both, :] for row in range(3)], axis=0)
        extras = extras + one_hot_dot(facing, beside, ((1,), (0,)))
    parts = [acts_ref[pq] for pq in range(4)]
    stats = sum(both_ref[k, sub : sub + 8, 0:128].astype(jnp.float32) for k in range(2))
    stats = stats[0:1] + stats[1:2] + stats[2:3]
    entries = 4 * plan.places * plan.group_width
    one, two = own_column(stats, 0, wide), own_column(stats, 64, wide)
    mean, inv_std = statistics(one, two, entries, plan.group_width)
    gain, bias = columns[2][:, 0:1], columns[3][:, 0:1]
    normed, slope = normalised(parts, gain, bias, mean, inv_std)
    lane, has_left, has_right, has_up, has_down = plan.place_masks(w)
    right, left = (1 - member).astype(jnp.float32), member.astype(jnp.float32)
    by_row = []
    for row in range(3):
        a, b, c = [sums[(3 * row + col) * wide : (3 * row + col + 1) * wide] for col in range(3)]
        extra = extras[row * wide : (row + 1) * wide]
        by_row.append(
            (a + b + moved(c, -1, has_left) + left * extra, moved(a, 1, has_right) + b + c + right * extra)
        )
    convs = [by_row[0][q] + by_row[1][q] + moved(by_row[2][q], -w, has_up) for q in range(2)]
    convs += [moved(by_row[0][q], w, has_down) + by_row[1][q] + by_row[2][q] for q in range(2)]
    pre = [conv * part for conv, part in zip(convs, slope)]
    one = total(pre)
    two = total([a * b for a, b in zip(pre, normed)])
    cot = source[pl.ds(pl.multiple_of(r * plan.slice_width + pair * wide, wide), wide), :].astype(jnp.float32)
    scale = inv_std * gain
    stacked = halves_from(plan, [cot + scale * part for part in pre]).astype(jnp.bfloat16)
    sent = one_hot_dot(stacked, order[...], ((1,), (1,))).astype(jnp.bfloat16)
    coarse = sums_ref[0:1] + pltpu.roll(sums_ref[1:2], sub, 1)
    coded = (
        terms(as_row(one) + pltpu.roll(as_row(two), 64, 1), 2)
        + terms(coarse, 2)
        + terms(as_row(inv_std) + pltpu.roll(as_row(mean), 64, 1), 3)
    )
    coded = jnp.concatenate(coded + [jnp.zeros_like(coarse)], axis=0).astype(jnp.bfloat16)
    for s_r in range(nr):
        for s_f in range(nf):
            out_ref[s_f * nr + s_r, 0:sub, :] = sent[s_f * sub : (s_f + 1) * sub, s_r * 128 : (s_r + 1) * 128]
            out_ref[s_f * nr + s_r, sub : sub + 8, :] = coded


def spread_kernel(plan, got_ref, acts_ref, gain_ref, out_ref, sums_ref):
    sub, nr, nf = plan.sub, plan.nr, plan.nf
    low = lanes_at((sub, 128), 1) < 64
    low_row = lanes_at((1, 128), 1) < 64
    first_row = lanes_at((1, 128), 1) < sub
    source = []
    fine, coarse, moments = [[], []], [[], []], [[], []]
    for s_r in range(nr):
        ones, twos, c_ones, c_twos, invs, means = [], [], 0.0, 0.0, [], []
        for pair in range(nf // 2):
            at = 2 * pair * nr + s_r
            left, right = [got_ref[at + k * nr, 0:sub, :].astype(jnp.float32) for k in range(2)]
            source.append(jnp.where(low, left, pltpu.roll(right, 64, 1)))
            source.append(jnp.where(low, pltpu.roll(left, 64, 1), right))
            coded = [got_ref[at + k * nr, sub : sub + 8, :].astype(jnp.float32) for k in range(2)]
            sums = coded[0][0:1] + coded[0][1:2] + coded[1][0:1] + coded[1][1:2]
            ones.append(sums if pair == 0 else pltpu.roll(sums, 64, 1))
            twos.append(pltpu.roll(sums, 64, 1) if pair == 0 else sums)
            both = coded[0][4:5] + coded[0][5:6] + coded[0][6:7]
            invs.append(both if pair == 0 else pltpu.roll(both, 64, 1))
            means.append(pltpu.roll(both, 64, 1) if pair == 0 else both)
            for k in range(2):
                sums = coded[k][2:3] + coded[k][3:4]
                to = (2 * pair + k) * sub
                c_one = jnp.where(first_row, sums, 0.0)
                c_two = jnp.where(first_row, pltpu.roll(sums, 128 - sub, 1), 0.0)
                c_ones = c_ones + (pltpu.roll(c_one, to, 1) if to else c_one)
                c_twos = c_twos + (pltpu.roll(c_two, to, 1) if to else c_two)
        fine[0].append(jnp.where(low_row, ones[0], ones[1]))
        fine[1].append(jnp.where(low_row, twos[0], twos[1]))
        moments[0].append(jnp.where(low_row, invs[0], invs[1]))
        moments[1].append(jnp.where(low_row, means[0], means[1]))
        coarse[0].append(c_ones)
        coarse[1].append(c_twos)
    one, two, inv_std, mean, c_one, c_two = [jnp.concatenate(part, axis=1) for part in fine + moments + coarse]
    source = jnp.concatenate(source, axis=0).astype(jnp.bfloat16)
    result = one_hot_dot(pixel_order(plan, False), source, ((1,), (1,)))
    gain = gain_ref[...]
    entries = 4 * plan.places * plan.group_width
    group_one = in_lane_groups(gain * one, plan.group_width) / entries
    group_two = in_lane_groups(gain * two, plan.group_width) / entries
    normed = (acts_ref[...].astype(jnp.float32) - mean) * inv_std
    out_ref[...] = (result - inv_std * (group_one + normed * group_two)).astype(jnp.bfloat16)
    sums_ref[...] = jnp.concatenate([one, two, c_one, c_two] + [jnp.zeros_like(one)] * 4, axis=0)


def total_kernel(scales, both_ref, result_ref, result_hbm, out_hbms, rows_ref, sems):
    copies = fetched([(result_ref, result_hbm)], sems)
    rows = sum(both_ref[k] for k in range(both_ref.shape[0]))
    for k in range(4):
        rows_ref[k] = rows[k : k + 1] * scales[k]
    for k in range(4):
        copies.append(pltpu.make_async_copy(rows_ref.at[k], out_hbms[k], sems.at[k + 1]))
        copies[-1].start()
    for copy in copies:
        copy.wait()


def in_vmem(count):
    return [pl.BlockSpec(memory_space=pltpu.VMEM)] * count


def in_hbm(count):
    return [pl.BlockSpec(memory_space=pltpu.HBM)] * count


def kept(array):
    return pltpu.with_memory_space_constraint(array, pltpu.HBM)


def shape_of(shape, kind):
    return jax.ShapeDtypeStruct(shape, kind)


LIMIT = pltpu.CompilerParams(vmem_limit_bytes=40 * 1024 * 1024)
COST = pl.CostEstimate(flops=2_000_000_000, bytes_accessed=4_000_000, transcendentals=0)


def fast_shards(
    plan,
    acts_fine,
    acts_coarse,
    grad_coarse,
    gain_fine,
    bias_fine,
    kernel_fine,
    gain_coarse,
    bias_coarse,
    kernel_coarse,
):
    nd = lax.axis_size("dp")
    count, sub, channels, places, local = plan.count, plan.sub, plan.channels, plan.places, plan.local
    f32, bf16 = jnp.float32, jnp.bfloat16
    rows = [part.reshape(1, channels) for part in (gain_coarse, bias_coarse, gain_fine, bias_fine)]
    places_of = ((local, channels), (local, channels), (4 * local, channels))
    fetched_of = pl.pallas_call(
        fetch_kernel,
        out_shape=tuple(pltpu.VMEM(shape, bf16) for shape in places_of),
        in_specs=in_hbm(3),
        out_specs=tuple(in_vmem(3)),
        scratch_shapes=[pltpu.SemaphoreType.DMA((3,))],
        compiler_params=LIMIT,
    )(*[kept(part.reshape(shape)) for part, shape in zip((grad_coarse, acts_coarse, acts_fine), places_of)])
    acts = fetched_of[2]
    packed = pl.pallas_call(
        functools.partial(pack_kernel, plan),
        out_shape=shape_of((count, plan.block_rows, 128), bf16),
        in_specs=in_vmem(3),
        out_specs=in_vmem(1)[0],
        compiler_params=LIMIT,
        cost_estimate=COST,
    )(*fetched_of)
    got = lax.all_to_all(packed, BLOCK, 0, 0)
    mine, theirs, held, inv_std, fine_acts, columns, fine_order, by_column = pl.pallas_call(
        functools.partial(coarse_kernel, plan),
        out_shape=(
            shape_of((sub, places), f32),
            shape_of((sub + 8, places), bf16),
            shape_of((3, sub, places), f32),
            shape_of((sub, 128), f32),
            shape_of((4, 2 * sub, places // 2), f32),
            shape_of((4, 2 * sub, 128), f32),
            shape_of((4 * plan.nr * local, 4 * plan.nr * local), bf16),
            shape_of((places, places + places // 2), bf16),
        ),
        in_specs=in_vmem(6),
        out_specs=tuple(in_vmem(8)),
        scratch_shapes=[
            pltpu.VMEM((4 * plan.nr * local, 4 * plan.nr * local), bf16),
            pltpu.VMEM((places + 2 * plan.image, channels // 2), bf16),
            pltpu.VMEM((2 * sub, places), f32),
        ],
        compiler_params=LIMIT,
        cost_estimate=COST,
    )(got, kernel_coarse, *rows)
    both = lax.all_gather(theirs, "member")
    quartered, coarse_sums = pl.pallas_call(
        functools.partial(quarter_kernel, plan),
        out_shape=(shape_of((count, 2 * sub + sub // 2, 128), bf16), shape_of((2, 128), f32)),
        in_specs=in_vmem(6),
        out_specs=tuple(in_vmem(2)),
        compiler_params=LIMIT,
        cost_estimate=COST,
    )(mine, both, held, inv_std, columns, by_column)
    spread = lax.all_to_all(quartered, BLOCK, 0, 0)
    sent = pl.pallas_call(
        functools.partial(fine_kernel, plan),
        out_shape=shape_of((count, sub + 8, 128), bf16),
        in_specs=in_vmem(7),
        out_specs=in_vmem(1)[0],
        scratch_shapes=[
            pltpu.VMEM((channels, places // 2), bf16),
            pltpu.VMEM((channels, places // 2), bf16),
        ],
        compiler_params=LIMIT,
        cost_estimate=COST,
    )(spread, fine_acts, both, columns, fine_order, coarse_sums, kernel_fine)
    back = lax.all_to_all(sent, BACK_BLOCK, 0, 0)
    cells = nd * places
    fine_scale, coarse_scale = 1.0 / math.sqrt(4 * cells), 1.0 / math.sqrt(cells)
    out, sums = pl.pallas_call(
        functools.partial(spread_kernel, plan),
        out_shape=(pltpu.VMEM((4 * local, channels), bf16), shape_of((8, channels), f32)),
        in_specs=in_vmem(3),
        out_specs=tuple(in_vmem(2)),
        compiler_params=LIMIT,
        cost_estimate=COST,
    )(back, acts, rows[2])
    both = lax.all_gather(sums, "dp")
    out, sums = pl.pallas_call(
        functools.partial(total_kernel, (fine_scale, fine_scale, coarse_scale, coarse_scale)),
        out_shape=(pltpu.HBM((4 * local, channels), bf16), (pltpu.HBM((1, channels), f32),) * 4),
        in_specs=in_vmem(2),
        out_specs=(in_hbm(1)[0], tuple(in_hbm(4))),
        scratch_shapes=[pltpu.VMEM((4, 1, channels), f32), pltpu.SemaphoreType.DMA((5,))],
        compiler_params=LIMIT,
        cost_estimate=COST,
    )(both, out)
    bias_f, gain_f, bias_c, gain_c = [part.reshape(channels) for part in sums]
    return out.reshape(acts_fine.shape), gain_f, bias_f, gain_c, bias_c


def solution(mesh):
    def function(*arrays):
        local = [size // mesh.shape[axis] for size, axis in zip(arrays[1].shape, ("dp", "frames", "rows"))]
        sizes = (mesh.shape["frames"], mesh.shape["rows"])
        plan = Plan(sizes, (*local[1:], *arrays[1].shape[3:]), arrays[5].shape[1] // mesh.shape["rows"])
        if plan.fits:
            split = (mesh.shape["dp"], plan.nf // 2, 2, plan.nr)
            used = jax.sharding.Mesh(mesh.devices.reshape(split), ("dp", "pairs", "member", "rows"))
            shards, frames = functools.partial(fast_shards, plan), ("pairs", "member")
        else:
            used, shards, frames = mesh, plain_shards, "frames"
        blocks, kernel = P("dp", frames, "rows", None, None), P(None, "rows", None)
        in_specs = (blocks, blocks, blocks, P(), P(), kernel, P(), P(), kernel)
        out_specs = (blocks, P(), P(), P(), P())
        mapped = jax.shard_map(shards, mesh=used, in_specs=in_specs, out_specs=out_specs, check_vma=False)
        return mapped(*arrays)

    return function
```

```python
import functools
import math

import jax
import jax.numpy as jnp
from jax import lax
from jax.experimental import pallas as pl
from jax.experimental.pallas import tpu as pltpu
from jax.sharding import PartitionSpec as P

GROUPS = 32
EPSILON = 1e-06
BLOCK = ("rows", "pairs", "member")
BACK_BLOCK = ("pairs", "member", "rows")
PLAIN_BLOCK = ("frames", "rows")


def plain_everyone(block, count):
    copies = jnp.broadcast_to(block[None], (count,) + block.shape)
    return lax.all_to_all(copies, PLAIN_BLOCK, 0, 0)


def ahead(field, axis, distance):
    size = field.shape[axis]
    if distance == 0:
        return field
    widths = [(0, 0)] * field.ndim
    if distance > 0:
        widths[axis] = (0, distance)
        kept = lax.slice_in_dim(field, distance, size, axis=axis)
    else:
        widths[axis] = (-distance, 0)
        kept = lax.slice_in_dim(field, 0, size + distance, axis=axis)
    return jnp.pad(kept, widths)


def tap_products(source, kernel):
    sub = kernel.shape[1]
    frames, rows, cols, channels = source.shape
    products = lax.dot_general(
        kernel.reshape(27 * sub, channels),
        source.reshape(frames * rows * cols, channels),
        (((1,), (1,)), ((), ())),
        preferred_element_type=jnp.float32,
    ).reshape(3, 3, 3, sub, frames, rows, cols)
    return sum(ahead(products[depth], 3, 2 - depth) for depth in range(3))


def coarse_conv(source, kernel):
    spatial = tap_products(source, kernel)
    total = 0.0
    for row in range(3):
        part = sum(ahead(spatial[row, col], 3, 1 - col) for col in range(3))
        total = total + ahead(part, 2, 1 - row)
    return total


def fine_conv(source, kernel):
    spatial = tap_products(source, kernel)
    result = []
    for p in range(2):
        rows_of = []
        for q in range(2):
            total = 0.0
            for row in range(3):
                part = sum(ahead(spatial[row, col], 3, (q + 1 - col) // 2) for col in range(3))
                total = total + ahead(part, 2, (p + 1 - row) // 2)
            rows_of.append(total)
        result.append(jnp.stack(rows_of, 1))
    return jnp.stack(result, 1)


def group_total(sums, group_width):
    sub = sums.shape[-1]
    if sub % group_width == 0:
        grouped = jnp.sum(sums.reshape(-1, sub // group_width, group_width), axis=-1)
        return jnp.repeat(grouped, group_width, axis=-1)
    spread = jnp.moveaxis(lax.all_gather(sums, "frames"), 0, 1).reshape(sums.shape[0], -1, group_width)
    mine = lax.axis_index("frames") * sub // group_width
    grouped = lax.dynamic_index_in_dim(jnp.sum(spread, -1), mine, 1)
    return jnp.broadcast_to(grouped, sums.shape)


def level(acts, conv_grad, cotangent, gain, bias, group_width):
    sub = acts.shape[0]
    places = acts.size // sub
    values = acts.astype(jnp.float32).reshape(sub, places)
    conv_grad = conv_grad.reshape(sub, places)
    entries = places * group_width
    moments = group_total(
        jnp.stack([jnp.sum(values, 1), jnp.sum(values * values, 1)]), group_width
    ) / entries
    mean = moments[0]
    inv_std = lax.rsqrt(moments[1] - mean * mean + EPSILON)
    normed = (values - mean[:, None]) * inv_std[:, None]
    preact = gain[:, None] * normed + bias[:, None]
    squash = jax.nn.sigmoid(preact)
    pre_grad = conv_grad * squash * (1.0 + preact * (1.0 - squash))
    sums = jnp.stack([jnp.sum(pre_grad, 1), jnp.sum(pre_grad * normed, 1)])
    terms = group_total(sums * gain, group_width) / entries
    grad = cotangent.reshape(sub, places) + inv_std[:, None] * (
        gain[:, None] * pre_grad - terms[0][:, None] - normed * terms[1][:, None]
    )
    return grad, sums


def plain_shards(
    acts_fine,
    acts_coarse,
    grad_coarse,
    gain_fine,
    bias_fine,
    kernel_fine,
    gain_coarse,
    bias_coarse,
    kernel_coarse,
):
    nf, nr, nd = lax.axis_size("frames"), lax.axis_size("rows"), lax.axis_size("dp")
    count = nf * nr
    channels = acts_fine.shape[-1]
    slice_width = kernel_fine.shape[1]
    sub = slice_width // nf
    group_width = channels // GROUPS
    tl, hl, w = acts_coarse.shape[1:4]
    frames, rows = tl * nf, hl * nr
    f, r = lax.axis_index("frames"), lax.axis_index("rows")

    gathered = plain_everyone(grad_coarse[0], count)
    source = (
        gathered.reshape(nf, nr, tl, hl, w, channels)
        .transpose(0, 2, 1, 3, 4, 5)
        .reshape(frames, rows, w, channels)
    )
    coarse_in = acts_coarse[0].reshape(tl, hl, w, nr, nf, sub).transpose(4, 3, 5, 0, 1, 2)
    coarse_in = lax.all_to_all(coarse_in.reshape(count, sub, tl * hl * w), PLAIN_BLOCK, 0, 0)
    fine_in = acts_fine[0].reshape(tl, hl, 2, w, 2, nr, nf, sub).transpose(6, 5, 7, 2, 4, 0, 1, 3)
    fine_in = lax.all_to_all(fine_in.reshape(count, sub, 4 * tl * hl * w), PLAIN_BLOCK, 0, 0)

    def mine(vector):
        return lax.dynamic_slice_in_dim(vector, r * slice_width + f * sub, sub)

    def own(kernel):
        return lax.dynamic_slice_in_dim(kernel, f * sub, sub, axis=1)

    coarse_vals = (
        coarse_in.reshape(nf, nr, sub, tl, hl, w).transpose(2, 0, 3, 1, 4, 5).reshape(sub, frames, rows, w)
    )
    cot = lax.dynamic_slice_in_dim(source, r * slice_width + f * sub, sub, axis=3)
    cot = cot.astype(jnp.float32).transpose(3, 0, 1, 2)
    conv = coarse_conv(source, own(kernel_coarse))
    coarse_grad, coarse_sums = level(
        coarse_vals, conv, cot, mine(gain_coarse), mine(bias_coarse), group_width
    )
    quartered = (coarse_grad * 0.25).astype(jnp.bfloat16)
    spread = plain_everyone(quartered, count)
    source_fine = (
        spread.reshape(nf, nr, sub, frames, rows, w)
        .transpose(3, 4, 5, 1, 0, 2)
        .reshape(frames, rows, w, channels)
    )
    conv = fine_conv(source_fine, own(kernel_fine))
    fine_vals = (
        fine_in.reshape(nf, nr, sub, 2, 2, tl, hl, w)
        .transpose(2, 3, 4, 0, 5, 1, 6, 7)
        .reshape(sub, 2, 2, frames, rows, w)
    )
    cot = jnp.broadcast_to(
        quartered.astype(jnp.float32).reshape(sub, 1, 1, frames, rows, w), conv.shape
    )
    fine_grad, fine_sums = level(
        fine_vals, conv, cot, mine(gain_fine), mine(bias_fine), group_width
    )
    back = (
        fine_grad.astype(jnp.bfloat16)
        .reshape(sub, 2, 2, nf, tl, nr, hl, w)
        .transpose(3, 5, 0, 1, 2, 4, 6, 7)
        .reshape(count, sub, 4 * tl * hl * w)
    )
    sums = plain_everyone(jnp.concatenate([fine_sums, coarse_sums]), count)
    back = lax.all_to_all(back, PLAIN_BLOCK, 0, 0)
    out = (
        back.reshape(nf, nr, sub, 2, 2, tl, hl, w)
        .transpose(5, 6, 3, 7, 4, 1, 0, 2)
        .reshape(1, tl, 2 * hl, 2 * w, channels)
    )
    sums = sums.reshape(nf, nr, 4, sub).transpose(2, 1, 0, 3).reshape(4, channels)
    totals = lax.psum(sums, "dp")
    cells = nd * frames * rows * w
    scale_fine = 1.0 / jnp.sqrt(jnp.float32(4 * cells))
    scale_coarse = 1.0 / jnp.sqrt(jnp.float32(cells))
    return (
        out,
        totals[1] * scale_fine,
        totals[0] * scale_fine,
        totals[3] * scale_coarse,
        totals[2] * scale_coarse,
    )


def lanes_at(shape, axis):
    return lax.broadcasted_iota(jnp.int32, shape, axis)


def one_hot(found):
    return found.astype(jnp.float32).astype(jnp.bfloat16)


def pixel_order(plan, swapped):
    tl, hl, w = plan.tl, plan.hl, plan.w // 2
    size = 4 * plan.local
    lane = lanes_at((1, size), 1)
    j, i, t = lane % w, lane // w % hl, lane // (w * hl) % tl
    q, p = lane // (w * hl * tl) % 2, lane // (2 * w * hl * tl) % 2
    half = lane // (4 * w * hl * tl)
    if swapped:
        half = 1 - half
    pixel = (t * 2 * hl + 2 * i + p) * 4 * w + 2 * (half * w + j) + q
    return one_hot(lanes_at((size, size), 0) == pixel)


def merged_order(nr, outer, tl, cells):
    size = nr * outer * tl * cells
    lane = lanes_at((1, size), 1)
    cell, dev = lane % cells, lane // cells % nr
    t, o = lane // (cells * nr) % tl, lane // (cells * nr * tl)
    return one_hot(lanes_at((size, size), 0) == ((dev * outer + o) * tl + t) * cells + cell)


def column_order(plan):
    w = plan.w // 2
    lines = plan.places // plan.w
    lane = lanes_at((1, 4 * lines * w + 4 * lines), 1)
    inner = lane % (lines * w)
    place = inner // w * plan.w + lane // (lines * w) * w + inner % w
    past = lane - 2 * lines * w
    border = past % lines * plan.w + jnp.where(past < 2 * lines, w, w - 1)
    wanted = jnp.where(past >= 0, border, place)
    shape = (plan.places, 2 * lines * w + 4 * lines)
    return one_hot(lanes_at(shape, 0) == wanted[:, : shape[1]])


def one_hot_dot(a, b, dims):
    return lax.dot_general(a, b, (dims, ((), ())), preferred_element_type=jnp.float32)


def moved(field, distance, kept):
    size = field.shape[1]
    return jnp.where(kept, pltpu.roll(field, (-distance) % size, 1), 0.0)


def own_column(row, base, sub):
    shape = (sub, row.shape[1])
    mine = lanes_at(shape, 1) == lanes_at(shape, 0) + base
    return jnp.sum(jnp.where(mine, row, 0.0), axis=1, keepdims=True)


def as_row(column):
    shape = (column.shape[0], 128)
    here = lanes_at(shape, 1) == lanes_at(shape, 0)
    return jnp.sum(jnp.where(here, column, 0.0), axis=0, keepdims=True)


def terms(value, count):
    found = []
    for _ in range(count):
        found.append(value.astype(jnp.bfloat16).astype(jnp.float32))
        value = value - found[-1]
    return found


def in_groups(column, group_width):
    sub = column.shape[0]
    grouped = jnp.sum(column.reshape(sub // group_width, group_width, 1), axis=1, keepdims=True)
    return jnp.broadcast_to(grouped, (sub // group_width, group_width, 1)).reshape(sub, 1)


def in_lane_groups(row, group_width):
    lane = lanes_at(row.shape, 1)
    size = row.shape[1]
    step = 1
    while step < group_width:
        up, down = pltpu.roll(row, size - step, 1), pltpu.roll(row, step, 1)
        row = row + jnp.where(lane // step % 2 == 0, up, down)
        step *= 2
    return row


def total(parts):
    return sum(jnp.sum(part, axis=1, keepdims=True) for part in parts)


def statistics(one, two, entries, group_width):
    mean = in_groups(one, group_width) / entries
    square = in_groups(two, group_width) / entries
    return mean, lax.rsqrt(square - mean * mean + EPSILON)


def normalised(parts, gain, bias, mean, inv_std):
    normed, slope = [], []
    for part in parts:
        unit = (part - mean) * inv_std
        preact = gain * unit + bias
        squash = 0.5 + 0.5 * jnp.tanh(0.5 * preact)
        normed.append(unit)
        slope.append(squash * (1.0 + preact * (1.0 - squash)))
    return normed, slope


class Plan:
    def __init__(self, mesh_sizes, acts_coarse, slice_width):
        self.nf, self.nr = mesh_sizes
        self.count = self.nf * self.nr
        self.tl, self.hl, self.w, self.channels = acts_coarse
        self.slice_width = slice_width
        self.sub = slice_width // self.nf
        self.cells = self.hl * self.w
        self.local = self.tl * self.cells
        self.image = self.cells * self.nr
        self.frames = self.tl * self.nf
        self.places = self.frames * self.image
        self.group_width = self.channels // GROUPS
        self.chunks = self.channels // 128
        self.acts_at = self.chunks // 2 * self.local
        self.packed_at = self.acts_at + self.sub
        self.cot_at = self.packed_at + 8
        self.block_rows = self.cot_at + 8
        self.fits = (
            self.sub == 32
            and self.slice_width == 128
            and self.group_width == 16
            and self.cells == 16
            and self.w == 8
            and self.tl == 2
            and self.nr == 4
            and self.nf == 4
            and self.slice_width * self.nr == self.channels
        )

    def place_masks(self, w):
        lane = lanes_at((1, self.places // self.w * w), 1)
        col, row = lane % w, lane // w % (self.hl * self.nr)
        last_row = self.hl * self.nr - 1
        return (lane, col > 0, col < w - 1, row > 0, row < last_row)


def fetched(pairs, sems):
    copies = [pltpu.make_async_copy(src, dst, sems.at[k]) for k, (src, dst) in enumerate(pairs)]
    for copy in copies:
        copy.start()
    return copies


def own_place(plan):
    pair, member, r = lax.axis_index("pairs"), lax.axis_index("member"), lax.axis_index("rows")
    return pair, member, r, r * plan.slice_width + (2 * pair + member) * plan.sub


def fetch_kernel(g_hbm, coarse_hbm, fine_hbm, g_ref, coarse_ref, fine_ref, sems):
    for copy in fetched([(fine_hbm, fine_ref), (coarse_hbm, coarse_ref), (g_hbm, g_ref)], sems):
        copy.wait()


def pack_kernel(plan, g_ref, coarse_ref, fine_ref, out_ref):
    sub, chunks, local = plan.sub, plan.chunks, plan.local
    shape = (2 * local, 2 * 128)
    lane = lanes_at((1, 2 * 128), 1)
    repeated = one_hot(lanes_at(shape, 0) == lane % local + lane // 128 * local)
    shape = (plan.channels, 128)
    quarter = lanes_at(shape, 0) // 8 % 4 == lanes_at(shape, 1) // local
    orders = jnp.concatenate([pixel_order(plan, swapped) for swapped in (False, True)], axis=1)
    acts = fine_ref[...]
    halves = one_hot_dot(acts, orders, ((0,), (0,))).astype(jnp.bfloat16)
    halves = [halves[:, :128], halves[:, 128:]]
    small = one_hot_dot(jnp.concatenate([coarse_ref[...], g_ref[...]], axis=0), repeated, ((0,), (0,)))
    for k, at in enumerate((plan.packed_at, plan.cot_at)):
        rows_of = jnp.where(quarter, small[:, k * 128 : (k + 1) * 128], 0.0).reshape(plan.count, 4, 8, 128)
        out_ref[:, at : at + 8, :] = jnp.sum(rows_of, axis=1).astype(jnp.bfloat16)
    low = lanes_at((sub, 128), 1) < 64
    for s_r in range(plan.nr):
        for s_f in range(plan.nf):
            dest = s_r * plan.nf + s_f
            first, half = s_r * plan.slice_width + s_f // 2 * 2 * sub, s_f % 2
            for k in range(chunks // 2):
                at = (half * chunks // 2 + k) * 128
                out_ref[dest, k * local : (k + 1) * local, :] = g_ref[:, at : at + 128]
            upper, lower = halves[half][first : first + sub], halves[1 - half][first + sub : first + 2 * sub]
            out_ref[dest, plan.acts_at : plan.packed_at, :] = jnp.where(low, upper, lower)


def by_frame_device(plan, got_ref, at, height):
    return jnp.concatenate(
        [
            jnp.concatenate(
                [got_ref[r * plan.nf + f, at : at + height, :] for r in range(plan.nr)], axis=1
            )
            for f in range(plan.nf)
        ],
        axis=0,
    )


def in_places(plan, merged, height):
    width = plan.tl * plan.image
    return [
        jnp.concatenate(
            [merged[f * height : (f + 1) * height, k * width : (k + 1) * width] for f in range(plan.nf)],
            axis=1,
        )
        for k in range(4)
    ]


def coarse_kernel(
    plan,
    got_ref,
    weights,
    gain_c,
    bias_c,
    gain_f,
    bias_f,
    mine_ref,
    sent_ref,
    held_ref,
    inv_ref,
    fine_ref,
    columns,
    fine_order,
    by_column,
    order,
    source,
    conv_ref,
):
    sub, nr, nf, cells, tl, local = plan.sub, plan.nr, plan.nf, plan.cells, plan.tl, plan.local
    wide, depth = 2 * sub, plan.channels // 2
    pair, member, r, base = own_place(plan)
    first = r * plan.slice_width + pair * wide
    columns[0, 0:sub, :] = jnp.broadcast_to(own_column(gain_c[...], base, sub), (sub, 128))
    columns[1, 0:sub, :] = jnp.broadcast_to(own_column(bias_c[...], base, sub), (sub, 128))
    columns[2] = jnp.broadcast_to(own_column(gain_f[...], first, wide), (wide, 128))
    columns[3] = jnp.broadcast_to(own_column(bias_f[...], first, wide), (wide, 128))
    order[...] = merged_order(plan.nr, 4, plan.tl, plan.cells)
    fine_order[...] = merged_order(plan.nr, 8, plan.tl, plan.cells // 2)
    by_column[...] = column_order(plan)
    both = pl.ds(pl.multiple_of(pair * wide, wide), wide)
    half = pl.ds(pl.multiple_of(member * depth, depth), depth)
    for s_f in range(nf):
        for s_r in range(nr):
            for t in range(tl):
                at = (s_f * tl + t) * plan.image + s_r * cells
                for k in range(plan.chunks // 2):
                    source[at : at + cells, k * 128 : (k + 1) * 128] = got_ref[
                        s_r * nf + s_f, k * local + t * cells : k * local + (t + 1) * cells, :
                    ]
    source[plan.places :, :] = jnp.zeros((2 * plan.image, depth), jnp.bfloat16)
    products = sum(
        one_hot_dot(
            weights[9 * k : 9 * k + 9, both, half].reshape(9 * wide, depth),
            source[(2 - k) * plan.image : (2 - k) * plan.image + plan.places, :],
            ((1,), (1,)),
        )
        for k in range(3)
    )
    merged = one_hot_dot(by_frame_device(plan, got_ref, plan.acts_at, sub), fine_order[...], ((1,), (0,)))
    parts = halves_at(plan, merged)
    for pq in range(4):
        fine_ref[pq] = parts[pq]
    one, two = total(parts), total([part * part for part in parts])
    stats = terms(as_row(one) + pltpu.roll(as_row(two), 64, 1), 3)
    stats = jnp.concatenate(stats + [jnp.zeros_like(stats[0])] * 5, axis=0).astype(jnp.bfloat16)
    small = [by_frame_device(plan, got_ref, at, 8) for at in (plan.packed_at, plan.cot_at)]
    merged = one_hot_dot(jnp.concatenate(small, axis=0), order[...], ((1,), (0,)))
    rows_of = 8 * nf
    values, cot = [
        jnp.concatenate(in_places(plan, merged[k * rows_of : (k + 1) * rows_of], 8), axis=0) for k in range(2)
    ]
    gain, bias = columns[0][0:sub, 0:1], columns[1][0:sub, 0:1]
    entries = plan.places * plan.group_width
    mean, inv_std = statistics(total([values]), total([values * values]), entries, plan.group_width)
    (normed,), (slope,) = normalised([values], gain, bias, mean, inv_std)
    held_ref[0], held_ref[1], held_ref[2] = normed, slope, cot
    inv_ref[...] = jnp.broadcast_to(inv_std, (sub, 128))
    lane, has_left, has_right, has_up, has_down = plan.place_masks(plan.w)
    by_col = []
    for col in range(3):
        parts = [products[(3 * row + col) * wide : (3 * row + col + 1) * wide] for row in range(3)]
        by_col.append(parts[1] + moved(parts[0], plan.w, has_down) + moved(parts[2], -plan.w, has_up))
    conv_ref[...] = by_col[1] + moved(by_col[0], 1, has_right) + moved(by_col[2], -1, has_left)
    mine_ref[...] = conv_ref[pl.ds(pl.multiple_of(member * sub, sub), sub), :]
    theirs = conv_ref[pl.ds(pl.multiple_of((1 - member) * sub, sub), sub), :]
    sent_ref[0:sub, :] = theirs.astype(jnp.bfloat16)
    sent_ref[sub:, 0:128] = stats
    sent_ref[sub:, 128:] = jnp.zeros((8, plan.places - 128), jnp.bfloat16)


def quarter_kernel(plan, mine_ref, both_ref, held_ref, inv_ref, columns, by_column, out_ref, sums_ref):
    sub = plan.sub
    _, member, _, _ = own_place(plan)
    conv = mine_ref[...] + both_ref[1 - member, 0:sub, :].astype(jnp.float32)
    normed, slope, cot = held_ref[0], held_ref[1], held_ref[2]
    gain, inv_std = columns[0][0:sub, 0:1], inv_ref[:, 0:1]
    entries = plan.places * plan.group_width
    pre = conv * slope
    one, two = total([pre]), total([pre * normed])
    group_one = in_groups(gain * one, plan.group_width) / entries
    group_two = in_groups(gain * two, plan.group_width) / entries
    grad = cot + inv_std * (gain * pre - group_one - normed * group_two)
    quartered = (grad * 0.25).astype(jnp.bfloat16)
    sent = one_hot_dot(quartered, by_column[...], ((1,), (0,))).astype(jnp.bfloat16)
    low = lanes_at((sub // 2, 128), 1) < 64
    for half in range(2):
        at = half * 256
        border = sent[:, 512 + half * 128 : 640 + half * 128]
        border = jnp.where(low, border[: sub // 2], border[sub // 2 :])
        for dest in [f * plan.nr + r for f in range(half, plan.nf, 2) for r in range(plan.nr)]:
            out_ref[dest, 0:sub, :] = sent[:, at : at + 128]
            out_ref[dest, sub : 2 * sub, :] = sent[:, at + 128 : at + 256]
            out_ref[dest, 2 * sub : 2 * sub + sub // 2, :] = border
    sums_ref[...] = jnp.concatenate([as_row(one), as_row(two)], axis=0)


def halves_at(plan, merged):
    sub = plan.sub
    turned = jnp.concatenate([pltpu.roll(merged[:, k * 128 : (k + 1) * 128], 64, 1) for k in range(4)], axis=1)
    low = lanes_at((sub, 128), 1) < 64
    parts = []
    for pq in range(4):
        groups = []
        for group in range(2):
            e = 4 * group + pq
            at = e // 2 * 128
            strips = []
            for m in range(plan.nf // 2):
                first, second = slice(2 * m * sub, (2 * m + 1) * sub), slice((2 * m + 1) * sub, (2 * m + 2) * sub)
                if e % 2 == 0:
                    strips.append(jnp.where(low, merged[first, at : at + 128], turned[second, at : at + 128]))
                else:
                    strips.append(jnp.where(low, turned[first, at : at + 128], merged[second, at : at + 128]))
            groups.append(jnp.concatenate(strips, axis=1))
        parts.append(jnp.concatenate(groups, axis=0))
    return parts


def halves_from(plan, parts):
    sub = plan.sub
    low = lanes_at((sub, 128), 1) < 64
    down = []
    for f in range(plan.nf):
        across = []
        for v in range(4):
            pair = []
            for e in (2 * v, 2 * v + 1):
                group, pq = e // 4, e % 4
                strip = parts[pq][group * sub : (group + 1) * sub, f // 2 * 128 : (f // 2 + 1) * 128]
                pair.append(strip if e % 2 == f % 2 else pltpu.roll(strip, 64, 1))
            across.append(jnp.where(low, pair[0], pair[1]))
        down.append(jnp.concatenate(across, axis=1))
    return jnp.concatenate(down, axis=0)


def fine_kernel(
    plan, got_ref, acts_ref, both_ref, columns, order, sums_ref, weights, out_ref, source, border
):
    sub, nr, nf, wide = plan.sub, plan.nr, plan.nf, 2 * plan.sub
    pair, member, r, _ = own_place(plan)
    both = pl.ds(pl.multiple_of(pair * wide, wide), wide)
    w = plan.w // 2
    lines = plan.places // plan.w
    places = lines * w
    starts = [s % nr * plan.slice_width + s // nr * sub for s in range(plan.count)]
    for s, at in enumerate(starts):
        for k in range(2):
            source[at : at + sub, k * 128 : (k + 1) * 128] = got_ref[s, k * sub : (k + 1) * sub, :]
    packed = got_ref[:, wide : wide + sub // 2, :].reshape(plan.count * sub // 2, 128)
    shape = (128, places)
    beside = lanes_at(shape, 1) == lanes_at(shape, 0) % lines * w + (1 - member) * (w - 1)
    for k in range(2):
        here = one_hot(beside & (lanes_at(shape, 0) // lines == k))
        found = one_hot_dot(packed, here, ((1,), (0,))).astype(jnp.bfloat16)
        for s, at in enumerate(starts):
            border[at + k * (sub // 2) : at + (k + 1) * (sub // 2), :] = found[
                s * (sub // 2) : (s + 1) * (sub // 2)
            ]
    image = plan.image // 2
    sums, extras = 0.0, 0.0
    for k in (2, 1, 0):
        here, beside = source[...], border[...]
        if k < 2:
            shift = (2 - k) * image
            inside = lanes_at((1, places), 1) < places - shift
            here, beside = [
                jnp.where(inside, pltpu.roll(part, places - shift, 1), jnp.zeros_like(part)) for part in (here, beside)
            ]
        sums = sums + one_hot_dot(
            weights[9 * k : 9 * k + 9, both, :].reshape(9 * wide, plan.channels), here, ((1,), (0,))
        )
        facing = jnp.concatenate([weights[9 * k + 3 * row + 2 * member, both, :] for row in range(3)], axis=0)
        extras = extras + one_hot_dot(facing, beside, ((1,), (0,)))
    parts = [acts_ref[pq] for pq in range(4)]
    stats = sum(both_ref[k, sub : sub + 8, 0:128].astype(jnp.float32) for k in range(2))
    stats = stats[0:1] + stats[1:2] + stats[2:3]
    entries = 4 * plan.places * plan.group_width
    one, two = own_column(stats, 0, wide), own_column(stats, 64, wide)
    mean, inv_std = statistics(one, two, entries, plan.group_width)
    gain, bias = columns[2][:, 0:1], columns[3][:, 0:1]
    normed, slope = normalised(parts, gain, bias, mean, inv_std)
    lane, has_left, has_right, has_up, has_down = plan.place_masks(w)
    right, left = (1 - member).astype(jnp.float32), member.astype(jnp.float32)
    by_row = []
    for row in range(3):
        a, b, c = [sums[(3 * row + col) * wide : (3 * row + col + 1) * wide] for col in range(3)]
        extra = extras[row * wide : (row + 1) * wide]
        by_row.append(
            (a + b + moved(c, -1, has_left) + left * extra, moved(a, 1, has_right) + b + c + right * extra)
        )
    convs = [by_row[0][q] + by_row[1][q] + moved(by_row[2][q], -w, has_up) for q in range(2)]
    convs += [moved(by_row[0][q], w, has_down) + by_row[1][q] + by_row[2][q] for q in range(2)]
    pre = [conv * part for conv, part in zip(convs, slope)]
    one = total(pre)
    two = total([a * b for a, b in zip(pre, normed)])
    cot = source[pl.ds(pl.multiple_of(r * plan.slice_width + pair * wide, wide), wide), :].astype(jnp.float32)
    scale = inv_std * gain
    stacked = halves_from(plan, [cot + scale * part for part in pre]).astype(jnp.bfloat16)
    sent = one_hot_dot(stacked, order[...], ((1,), (1,))).astype(jnp.bfloat16)
    coarse = sums_ref[0:1] + pltpu.roll(sums_ref[1:2], sub, 1)
    coded = (
        terms(as_row(one) + pltpu.roll(as_row(two), 64, 1), 2)
        + terms(coarse, 2)
        + terms(as_row(inv_std) + pltpu.roll(as_row(mean), 64, 1), 3)
    )
    coded = jnp.concatenate(coded + [jnp.zeros_like(coarse)], axis=0).astype(jnp.bfloat16)
    for s_r in range(nr):
        for s_f in range(nf):
            out_ref[s_f * nr + s_r, 0:sub, :] = sent[s_f * sub : (s_f + 1) * sub, s_r * 128 : (s_r + 1) * 128]
            out_ref[s_f * nr + s_r, sub : sub + 8, :] = coded


def spread_kernel(plan, got_ref, acts_ref, gain_ref, out_ref, sums_ref):
    sub, nr, nf = plan.sub, plan.nr, plan.nf
    low = lanes_at((sub, 128), 1) < 64
    low_row = lanes_at((1, 128), 1) < 64
    first_row = lanes_at((1, 128), 1) < sub
    source = []
    fine, coarse, moments = [[], []], [[], []], [[], []]
    for s_r in range(nr):
        ones, twos, c_ones, c_twos, invs, means = [], [], 0.0, 0.0, [], []
        for pair in range(nf // 2):
            at = 2 * pair * nr + s_r
            left, right = [got_ref[at + k * nr, 0:sub, :].astype(jnp.float32) for k in range(2)]
            source.append(jnp.where(low, left, pltpu.roll(right, 64, 1)))
            source.append(jnp.where(low, pltpu.roll(left, 64, 1), right))
            coded = [got_ref[at + k * nr, sub : sub + 8, :].astype(jnp.float32) for k in range(2)]
            sums = coded[0][0:1] + coded[0][1:2] + coded[1][0:1] + coded[1][1:2]
            ones.append(sums if pair == 0 else pltpu.roll(sums, 64, 1))
            twos.append(pltpu.roll(sums, 64, 1) if pair == 0 else sums)
            both = coded[0][4:5] + coded[0][5:6] + coded[0][6:7]
            invs.append(both if pair == 0 else pltpu.roll(both, 64, 1))
            means.append(pltpu.roll(both, 64, 1) if pair == 0 else both)
            for k in range(2):
                sums = coded[k][2:3] + coded[k][3:4]
                to = (2 * pair + k) * sub
                c_one = jnp.where(first_row, sums, 0.0)
                c_two = jnp.where(first_row, pltpu.roll(sums, 128 - sub, 1), 0.0)
                c_ones = c_ones + (pltpu.roll(c_one, to, 1) if to else c_one)
                c_twos = c_twos + (pltpu.roll(c_two, to, 1) if to else c_two)
        fine[0].append(jnp.where(low_row, ones[0], ones[1]))
        fine[1].append(jnp.where(low_row, twos[0], twos[1]))
        moments[0].append(jnp.where(low_row, invs[0], invs[1]))
        moments[1].append(jnp.where(low_row, means[0], means[1]))
        coarse[0].append(c_ones)
        coarse[1].append(c_twos)
    one, two, inv_std, mean, c_one, c_two = [jnp.concatenate(part, axis=1) for part in fine + moments + coarse]
    source = jnp.concatenate(source, axis=0).astype(jnp.bfloat16)
    result = one_hot_dot(pixel_order(plan, False), source, ((1,), (1,)))
    gain = gain_ref[...]
    entries = 4 * plan.places * plan.group_width
    group_one = in_lane_groups(gain * one, plan.group_width) / entries
    group_two = in_lane_groups(gain * two, plan.group_width) / entries
    normed = (acts_ref[...].astype(jnp.float32) - mean) * inv_std
    out_ref[...] = (result - inv_std * (group_one + normed * group_two)).astype(jnp.bfloat16)
    sums_ref[...] = jnp.concatenate([one, two, c_one, c_two] + [jnp.zeros_like(one)] * 4, axis=0)


def total_kernel(scales, both_ref, result_ref, result_hbm, out_hbms, rows_ref, sems):
    copies = fetched([(result_ref, result_hbm)], sems)
    rows = sum(both_ref[k] for k in range(both_ref.shape[0]))
    for k in range(4):
        rows_ref[k] = rows[k : k + 1] * scales[k]
    for k in range(4):
        copies.append(pltpu.make_async_copy(rows_ref.at[k], out_hbms[k], sems.at[k + 1]))
        copies[-1].start()
    for copy in copies:
        copy.wait()


def in_vmem(count):
    return [pl.BlockSpec(memory_space=pltpu.VMEM)] * count


def in_hbm(count):
    return [pl.BlockSpec(memory_space=pltpu.HBM)] * count


def kept(array):
    return pltpu.with_memory_space_constraint(array, pltpu.HBM)


def shape_of(shape, kind):
    return jax.ShapeDtypeStruct(shape, kind)


LIMIT = pltpu.CompilerParams(vmem_limit_bytes=40 * 1024 * 1024)
COST = pl.CostEstimate(flops=2_000_000_000, bytes_accessed=4_000_000, transcendentals=0)


def fast_shards(
    plan,
    acts_fine,
    acts_coarse,
    grad_coarse,
    gain_fine,
    bias_fine,
    kernel_fine,
    gain_coarse,
    bias_coarse,
    kernel_coarse,
):
    nd = lax.axis_size("dp")
    count, sub, channels, places, local = plan.count, plan.sub, plan.channels, plan.places, plan.local
    f32, bf16 = jnp.float32, jnp.bfloat16
    rows = [part.reshape(1, channels) for part in (gain_coarse, bias_coarse, gain_fine, bias_fine)]
    places_of = ((local, channels), (local, channels), (4 * local, channels))
    fetched_of = pl.pallas_call(
        fetch_kernel,
        out_shape=tuple(pltpu.VMEM(shape, bf16) for shape in places_of),
        in_specs=in_hbm(3),
        out_specs=tuple(in_vmem(3)),
        scratch_shapes=[pltpu.SemaphoreType.DMA((3,))],
        compiler_params=LIMIT,
    )(*[kept(part.reshape(shape)) for part, shape in zip((grad_coarse, acts_coarse, acts_fine), places_of)])
    acts = fetched_of[2]
    packed = pl.pallas_call(
        functools.partial(pack_kernel, plan),
        out_shape=shape_of((count, plan.block_rows, 128), bf16),
        in_specs=in_vmem(3),
        out_specs=in_vmem(1)[0],
        compiler_params=LIMIT,
        cost_estimate=COST,
    )(*fetched_of)
    got = lax.all_to_all(packed, BLOCK, 0, 0)
    mine, theirs, held, inv_std, fine_acts, columns, fine_order, by_column = pl.pallas_call(
        functools.partial(coarse_kernel, plan),
        out_shape=(
            shape_of((sub, places), f32),
            shape_of((sub + 8, places), bf16),
            shape_of((3, sub, places), f32),
            shape_of((sub, 128), f32),
            shape_of((4, 2 * sub, places // 2), f32),
            shape_of((4, 2 * sub, 128), f32),
            shape_of((4 * plan.nr * local, 4 * plan.nr * local), bf16),
            shape_of((places, places + places // 2), bf16),
        ),
        in_specs=in_vmem(6),
        out_specs=tuple(in_vmem(8)),
        scratch_shapes=[
            pltpu.VMEM((4 * plan.nr * local, 4 * plan.nr * local), bf16),
            pltpu.VMEM((places + 2 * plan.image, channels // 2), bf16),
            pltpu.VMEM((2 * sub, places), f32),
        ],
        compiler_params=LIMIT,
        cost_estimate=COST,
    )(got, kernel_coarse, *rows)
    both = lax.all_gather(theirs, "member")
    quartered, coarse_sums = pl.pallas_call(
        functools.partial(quarter_kernel, plan),
        out_shape=(shape_of((count, 2 * sub + sub // 2, 128), bf16), shape_of((2, 128), f32)),
        in_specs=in_vmem(6),
        out_specs=tuple(in_vmem(2)),
        compiler_params=LIMIT,
        cost_estimate=COST,
    )(mine, both, held, inv_std, columns, by_column)
    spread = lax.all_to_all(quartered, BACK_BLOCK, 0, 0)
    sent = pl.pallas_call(
        functools.partial(fine_kernel, plan),
        out_shape=shape_of((count, sub + 8, 128), bf16),
        in_specs=in_vmem(7),
        out_specs=in_vmem(1)[0],
        scratch_shapes=[
            pltpu.VMEM((channels, places // 2), bf16),
            pltpu.VMEM((channels, places // 2), bf16),
        ],
        compiler_params=LIMIT,
        cost_estimate=COST,
    )(spread, fine_acts, both, columns, fine_order, coarse_sums, kernel_fine)
    back = lax.all_to_all(sent, BACK_BLOCK, 0, 0)
    cells = nd * places
    fine_scale, coarse_scale = 1.0 / math.sqrt(4 * cells), 1.0 / math.sqrt(cells)
    out, sums = pl.pallas_call(
        functools.partial(spread_kernel, plan),
        out_shape=(pltpu.VMEM((4 * local, channels), bf16), shape_of((8, channels), f32)),
        in_specs=in_vmem(3),
        out_specs=tuple(in_vmem(2)),
        compiler_params=LIMIT,
        cost_estimate=COST,
    )(back, acts, rows[2])
    both = lax.all_gather(sums, "dp")
    out, sums = pl.pallas_call(
        functools.partial(total_kernel, (fine_scale, fine_scale, coarse_scale, coarse_scale)),
        out_shape=(pltpu.HBM((4 * local, channels), bf16), (pltpu.HBM((1, channels), f32),) * 4),
        in_specs=in_vmem(2),
        out_specs=(in_hbm(1)[0], tuple(in_hbm(4))),
        scratch_shapes=[pltpu.VMEM((4, 1, channels), f32), pltpu.SemaphoreType.DMA((5,))],
        compiler_params=LIMIT,
        cost_estimate=COST,
    )(both, out)
    bias_f, gain_f, bias_c, gain_c = [part.reshape(channels) for part in sums]
    return out.reshape(acts_fine.shape), gain_f, bias_f, gain_c, bias_c


def solution(mesh):
    def function(*arrays):
        local = [size // mesh.shape[axis] for size, axis in zip(arrays[1].shape, ("dp", "frames", "rows"))]
        sizes = (mesh.shape["frames"], mesh.shape["rows"])
        plan = Plan(sizes, (*local[1:], *arrays[1].shape[3:]), arrays[5].shape[1] // mesh.shape["rows"])
        if plan.fits:
            split = (mesh.shape["dp"], plan.nf // 2, 2, plan.nr)
            used = jax.sharding.Mesh(mesh.devices.reshape(split), ("dp", "pairs", "member", "rows"))
            shards, frames = functools.partial(fast_shards, plan), ("pairs", "member")
        else:
            used, shards, frames = mesh, plain_shards, "frames"
        blocks, kernel = P("dp", frames, "rows", None, None), P(None, "rows", None)
        in_specs = (blocks, blocks, blocks, P(), P(), kernel, P(), P(), kernel)
        out_specs = (blocks, P(), P(), P(), P())
        mapped = jax.shard_map(shards, mesh=used, in_specs=in_specs, out_specs=out_specs, check_vma=False)
        return mapped(*arrays)

    return function
```

```python
import functools
import math

import jax
import jax.numpy as jnp
from jax import lax
from jax.experimental import pallas as pl
from jax.experimental.pallas import tpu as pltpu
from jax.sharding import PartitionSpec as P

GROUPS = 32
EPSILON = 1e-06
BLOCK = ("rows", "pairs", "member")
BACK_BLOCK = ("pairs", "member", "rows")
PLAIN_BLOCK = ("frames", "rows")


def plain_everyone(block, count):
    copies = jnp.broadcast_to(block[None], (count,) + block.shape)
    return lax.all_to_all(copies, PLAIN_BLOCK, 0, 0)


def ahead(field, axis, distance):
    size = field.shape[axis]
    if distance == 0:
        return field
    widths = [(0, 0)] * field.ndim
    if distance > 0:
        widths[axis] = (0, distance)
        kept = lax.slice_in_dim(field, distance, size, axis=axis)
    else:
        widths[axis] = (-distance, 0)
        kept = lax.slice_in_dim(field, 0, size + distance, axis=axis)
    return jnp.pad(kept, widths)


def tap_products(source, kernel):
    sub = kernel.shape[1]
    frames, rows, cols, channels = source.shape
    products = lax.dot_general(
        kernel.reshape(27 * sub, channels),
        source.reshape(frames * rows * cols, channels),
        (((1,), (1,)), ((), ())),
        preferred_element_type=jnp.float32,
    ).reshape(3, 3, 3, sub, frames, rows, cols)
    return sum(ahead(products[depth], 3, 2 - depth) for depth in range(3))


def coarse_conv(source, kernel):
    spatial = tap_products(source, kernel)
    total = 0.0
    for row in range(3):
        part = sum(ahead(spatial[row, col], 3, 1 - col) for col in range(3))
        total = total + ahead(part, 2, 1 - row)
    return total


def fine_conv(source, kernel):
    spatial = tap_products(source, kernel)
    result = []
    for p in range(2):
        rows_of = []
        for q in range(2):
            total = 0.0
            for row in range(3):
                part = sum(ahead(spatial[row, col], 3, (q + 1 - col) // 2) for col in range(3))
                total = total + ahead(part, 2, (p + 1 - row) // 2)
            rows_of.append(total)
        result.append(jnp.stack(rows_of, 1))
    return jnp.stack(result, 1)


def group_total(sums, group_width):
    sub = sums.shape[-1]
    if sub % group_width == 0:
        grouped = jnp.sum(sums.reshape(-1, sub // group_width, group_width), axis=-1)
        return jnp.repeat(grouped, group_width, axis=-1)
    spread = jnp.moveaxis(lax.all_gather(sums, "frames"), 0, 1).reshape(sums.shape[0], -1, group_width)
    mine = lax.axis_index("frames") * sub // group_width
    grouped = lax.dynamic_index_in_dim(jnp.sum(spread, -1), mine, 1)
    return jnp.broadcast_to(grouped, sums.shape)


def level(acts, conv_grad, cotangent, gain, bias, group_width):
    sub = acts.shape[0]
    places = acts.size // sub
    values = acts.astype(jnp.float32).reshape(sub, places)
    conv_grad = conv_grad.reshape(sub, places)
    entries = places * group_width
    moments = group_total(
        jnp.stack([jnp.sum(values, 1), jnp.sum(values * values, 1)]), group_width
    ) / entries
    mean = moments[0]
    inv_std = lax.rsqrt(moments[1] - mean * mean + EPSILON)
    normed = (values - mean[:, None]) * inv_std[:, None]
    preact = gain[:, None] * normed + bias[:, None]
    squash = jax.nn.sigmoid(preact)
    pre_grad = conv_grad * squash * (1.0 + preact * (1.0 - squash))
    sums = jnp.stack([jnp.sum(pre_grad, 1), jnp.sum(pre_grad * normed, 1)])
    terms = group_total(sums * gain, group_width) / entries
    grad = cotangent.reshape(sub, places) + inv_std[:, None] * (
        gain[:, None] * pre_grad - terms[0][:, None] - normed * terms[1][:, None]
    )
    return grad, sums


def plain_shards(
    acts_fine,
    acts_coarse,
    grad_coarse,
    gain_fine,
    bias_fine,
    kernel_fine,
    gain_coarse,
    bias_coarse,
    kernel_coarse,
):
    nf, nr, nd = lax.axis_size("frames"), lax.axis_size("rows"), lax.axis_size("dp")
    count = nf * nr
    channels = acts_fine.shape[-1]
    slice_width = kernel_fine.shape[1]
    sub = slice_width // nf
    group_width = channels // GROUPS
    tl, hl, w = acts_coarse.shape[1:4]
    frames, rows = tl * nf, hl * nr
    f, r = lax.axis_index("frames"), lax.axis_index("rows")

    gathered = plain_everyone(grad_coarse[0], count)
    source = (
        gathered.reshape(nf, nr, tl, hl, w, channels)
        .transpose(0, 2, 1, 3, 4, 5)
        .reshape(frames, rows, w, channels)
    )
    coarse_in = acts_coarse[0].reshape(tl, hl, w, nr, nf, sub).transpose(4, 3, 5, 0, 1, 2)
    coarse_in = lax.all_to_all(coarse_in.reshape(count, sub, tl * hl * w), PLAIN_BLOCK, 0, 0)
    fine_in = acts_fine[0].reshape(tl, hl, 2, w, 2, nr, nf, sub).transpose(6, 5, 7, 2, 4, 0, 1, 3)
    fine_in = lax.all_to_all(fine_in.reshape(count, sub, 4 * tl * hl * w), PLAIN_BLOCK, 0, 0)

    def mine(vector):
        return lax.dynamic_slice_in_dim(vector, r * slice_width + f * sub, sub)

    def own(kernel):
        return lax.dynamic_slice_in_dim(kernel, f * sub, sub, axis=1)

    coarse_vals = (
        coarse_in.reshape(nf, nr, sub, tl, hl, w).transpose(2, 0, 3, 1, 4, 5).reshape(sub, frames, rows, w)
    )
    cot = lax.dynamic_slice_in_dim(source, r * slice_width + f * sub, sub, axis=3)
    cot = cot.astype(jnp.float32).transpose(3, 0, 1, 2)
    conv = coarse_conv(source, own(kernel_coarse))
    coarse_grad, coarse_sums = level(
        coarse_vals, conv, cot, mine(gain_coarse), mine(bias_coarse), group_width
    )
    quartered = (coarse_grad * 0.25).astype(jnp.bfloat16)
    spread = plain_everyone(quartered, count)
    source_fine = (
        spread.reshape(nf, nr, sub, frames, rows, w)
        .transpose(3, 4, 5, 1, 0, 2)
        .reshape(frames, rows, w, channels)
    )
    conv = fine_conv(source_fine, own(kernel_fine))
    fine_vals = (
        fine_in.reshape(nf, nr, sub, 2, 2, tl, hl, w)
        .transpose(2, 3, 4, 0, 5, 1, 6, 7)
        .reshape(sub, 2, 2, frames, rows, w)
    )
    cot = jnp.broadcast_to(
        quartered.astype(jnp.float32).reshape(sub, 1, 1, frames, rows, w), conv.shape
    )
    fine_grad, fine_sums = level(
        fine_vals, conv, cot, mine(gain_fine), mine(bias_fine), group_width
    )
    back = (
        fine_grad.astype(jnp.bfloat16)
        .reshape(sub, 2, 2, nf, tl, nr, hl, w)
        .transpose(3, 5, 0, 1, 2, 4, 6, 7)
        .reshape(count, sub, 4 * tl * hl * w)
    )
    sums = plain_everyone(jnp.concatenate([fine_sums, coarse_sums]), count)
    back = lax.all_to_all(back, PLAIN_BLOCK, 0, 0)
    out = (
        back.reshape(nf, nr, sub, 2, 2, tl, hl, w)
        .transpose(5, 6, 3, 7, 4, 1, 0, 2)
        .reshape(1, tl, 2 * hl, 2 * w, channels)
    )
    sums = sums.reshape(nf, nr, 4, sub).transpose(2, 1, 0, 3).reshape(4, channels)
    totals = lax.psum(sums, "dp")
    cells = nd * frames * rows * w
    scale_fine = 1.0 / jnp.sqrt(jnp.float32(4 * cells))
    scale_coarse = 1.0 / jnp.sqrt(jnp.float32(cells))
    return (
        out,
        totals[1] * scale_fine,
        totals[0] * scale_fine,
        totals[3] * scale_coarse,
        totals[2] * scale_coarse,
    )


def lanes_at(shape, axis):
    return lax.broadcasted_iota(jnp.int32, shape, axis)


def one_hot(found):
    return found.astype(jnp.float32).astype(jnp.bfloat16)


def pixel_order(plan, swapped):
    tl, hl, w = plan.tl, plan.hl, plan.w // 2
    size = 4 * plan.local
    lane = lanes_at((1, size), 1)
    j, i, t = lane % w, lane // w % hl, lane // (w * hl) % tl
    q, p = lane // (w * hl * tl) % 2, lane // (2 * w * hl * tl) % 2
    half = lane // (4 * w * hl * tl)
    if swapped:
        half = 1 - half
    pixel = (t * 2 * hl + 2 * i + p) * 4 * w + 2 * (half * w + j) + q
    return one_hot(lanes_at((size, size), 0) == pixel)


def merged_order(nr, outer, tl, cells):
    size = nr * outer * tl * cells
    lane = lanes_at((1, size), 1)
    cell, dev = lane % cells, lane // cells % nr
    t, o = lane // (cells * nr) % tl, lane // (cells * nr * tl)
    return one_hot(lanes_at((size, size), 0) == ((dev * outer + o) * tl + t) * cells + cell)


def column_order(plan):
    w = plan.w // 2
    lines = plan.places // plan.w
    lane = lanes_at((1, 4 * lines * w + 4 * lines), 1)
    inner = lane % (lines * w)
    place = inner // w * plan.w + lane // (lines * w) * w + inner % w
    past = lane - 2 * lines * w
    border = past % lines * plan.w + jnp.where(past < 2 * lines, w, w - 1)
    wanted = jnp.where(past >= 0, border, place)
    shape = (plan.places, 2 * lines * w + 4 * lines)
    return one_hot(lanes_at(shape, 0) == wanted[:, : shape[1]])


def one_hot_dot(a, b, dims):
    return lax.dot_general(a, b, (dims, ((), ())), preferred_element_type=jnp.float32)


def moved(field, distance, kept):
    size = field.shape[1]
    return jnp.where(kept, pltpu.roll(field, (-distance) % size, 1), 0.0)


def own_column(row, base, sub):
    shape = (sub, row.shape[1])
    mine = lanes_at(shape, 1) == lanes_at(shape, 0) + base
    return jnp.sum(jnp.where(mine, row, 0.0), axis=1, keepdims=True)


def as_row(column):
    shape = (column.shape[0], 128)
    here = lanes_at(shape, 1) == lanes_at(shape, 0)
    return jnp.sum(jnp.where(here, column, 0.0), axis=0, keepdims=True)


def terms(value, count):
    found = []
    for _ in range(count):
        found.append(value.astype(jnp.bfloat16).astype(jnp.float32))
        value = value - found[-1]
    return found


def in_groups(column, group_width):
    sub = column.shape[0]
    grouped = jnp.sum(column.reshape(sub // group_width, group_width, 1), axis=1, keepdims=True)
    return jnp.broadcast_to(grouped, (sub // group_width, group_width, 1)).reshape(sub, 1)


def in_lane_groups(row, group_width):
    lane = lanes_at(row.shape, 1)
    size = row.shape[1]
    step = 1
    while step < group_width:
        up, down = pltpu.roll(row, size - step, 1), pltpu.roll(row, step, 1)
        row = row + jnp.where(lane // step % 2 == 0, up, down)
        step *= 2
    return row


def total(parts):
    return sum(jnp.sum(part, axis=1, keepdims=True) for part in parts)


def statistics(one, two, entries, group_width):
    mean = in_groups(one, group_width) / entries
    square = in_groups(two, group_width) / entries
    return mean, lax.rsqrt(square - mean * mean + EPSILON)


def normalised(parts, gain, bias, mean, inv_std):
    normed, slope = [], []
    for part in parts:
        unit = (part - mean) * inv_std
        preact = gain * unit + bias
        squash = 0.5 + 0.5 * jnp.tanh(0.5 * preact)
        normed.append(unit)
        slope.append(squash * (1.0 + preact * (1.0 - squash)))
    return normed, slope


class Plan:
    def __init__(self, mesh_sizes, acts_coarse, slice_width):
        self.nf, self.nr = mesh_sizes
        self.count = self.nf * self.nr
        self.tl, self.hl, self.w, self.channels = acts_coarse
        self.slice_width = slice_width
        self.sub = slice_width // self.nf
        self.cells = self.hl * self.w
        self.local = self.tl * self.cells
        self.image = self.cells * self.nr
        self.frames = self.tl * self.nf
        self.places = self.frames * self.image
        self.group_width = self.channels // GROUPS
        self.chunks = self.channels // 128
        self.acts_at = self.chunks // 2 * self.local
        self.packed_at = self.acts_at + self.sub
        self.block_rows = self.packed_at + 16
        self.fits = (
            self.sub == 32
            and self.slice_width == 128
            and self.group_width == 16
            and self.cells == 16
            and self.w == 8
            and self.tl == 2
            and self.nr == 4
            and self.nf == 4
            and self.slice_width * self.nr == self.channels
        )

    def place_masks(self, w):
        lane = lanes_at((1, self.places // self.w * w), 1)
        col, row = lane % w, lane // w % (self.hl * self.nr)
        last_row = self.hl * self.nr - 1
        return (lane, col > 0, col < w - 1, row > 0, row < last_row)


def fetched(pairs, sems):
    copies = [pltpu.make_async_copy(src, dst, sems.at[k]) for k, (src, dst) in enumerate(pairs)]
    for copy in copies:
        copy.start()
    return copies


def own_place(plan):
    pair, member, r = lax.axis_index("pairs"), lax.axis_index("member"), lax.axis_index("rows")
    return pair, member, r, r * plan.slice_width + (2 * pair + member) * plan.sub


def fetch_kernel(g_hbm, coarse_hbm, fine_hbm, g_ref, coarse_ref, fine_ref, sems):
    for copy in fetched([(fine_hbm, fine_ref), (coarse_hbm, coarse_ref), (g_hbm, g_ref)], sems):
        copy.wait()


def pack_kernel(plan, g_ref, coarse_ref, fine_ref, out_ref):
    sub, chunks, local = plan.sub, plan.chunks, plan.local
    shape = (2 * local, 2 * 128)
    lane = lanes_at((1, 2 * 128), 1)
    repeated = one_hot(lanes_at(shape, 0) == lane % local + lane // 128 * local)
    shape = (plan.channels, 128)
    quarter = lanes_at(shape, 0) // 8 % 4 == lanes_at(shape, 1) // local
    orders = jnp.concatenate([pixel_order(plan, swapped) for swapped in (False, True)], axis=1)
    acts = fine_ref[...]
    halves = one_hot_dot(acts, orders, ((0,), (0,))).astype(jnp.bfloat16)
    halves = [halves[:, :128], halves[:, 128:]]
    small = one_hot_dot(jnp.concatenate([coarse_ref[...], g_ref[...]], axis=0), repeated, ((0,), (0,)))
    rows_of = [
        jnp.sum(jnp.where(quarter, small[:, k : k + 128], 0.0).reshape(plan.count, 4, 8, 128), axis=1) for k in (0, 128)
    ]
    out_ref[:, plan.packed_at : plan.block_rows, :] = jnp.concatenate(rows_of, axis=1).astype(jnp.bfloat16)
    low = lanes_at((sub, 128), 1) < 64
    for s_r in range(plan.nr):
        for s_f in range(plan.nf):
            dest = s_r * plan.nf + s_f
            first, half = s_r * plan.slice_width + s_f // 2 * 2 * sub, s_f % 2
            for k in range(chunks // 2):
                at = (half * chunks // 2 + k) * 128
                out_ref[dest, k * local : (k + 1) * local, :] = g_ref[:, at : at + 128]
            upper, lower = halves[half][first : first + sub], halves[1 - half][first + sub : first + 2 * sub]
            out_ref[dest, plan.acts_at : plan.packed_at, :] = jnp.where(low, upper, lower)


def by_frame_device(plan, got_ref, at, height):
    return jnp.concatenate(
        [
            jnp.concatenate(
                [got_ref[r * plan.nf + f, at : at + height, :] for r in range(plan.nr)], axis=1
            )
            for f in range(plan.nf)
        ],
        axis=0,
    )


def in_places(plan, merged, height):
    width = plan.tl * plan.image
    return [
        jnp.concatenate(
            [merged[f * height : (f + 1) * height, k * width : (k + 1) * width] for f in range(plan.nf)],
            axis=1,
        )
        for k in range(4)
    ]


def coarse_kernel(
    plan,
    got_ref,
    weights,
    gain_c,
    bias_c,
    gain_f,
    bias_f,
    mine_ref,
    sent_ref,
    held_ref,
    inv_ref,
    fine_ref,
    columns,
    fine_order,
    by_column,
    order,
    source,
    conv_ref,
):
    sub, nr, nf, cells, tl, local = plan.sub, plan.nr, plan.nf, plan.cells, plan.tl, plan.local
    wide, depth = 2 * sub, plan.channels // 2
    pair, member, r, base = own_place(plan)
    first = r * plan.slice_width + pair * wide
    columns[0, 0:sub, :] = jnp.broadcast_to(own_column(gain_c[...], base, sub), (sub, 128))
    columns[1, 0:sub, :] = jnp.broadcast_to(own_column(bias_c[...], base, sub), (sub, 128))
    columns[2] = jnp.broadcast_to(own_column(gain_f[...], first, wide), (wide, 128))
    columns[3] = jnp.broadcast_to(own_column(bias_f[...], first, wide), (wide, 128))
    order[...] = merged_order(plan.nr, 4, plan.tl, plan.cells)
    fine_order[...] = merged_order(plan.nr, 8, plan.tl, plan.cells // 2)
    by_column[...] = column_order(plan)
    both = pl.ds(pl.multiple_of(pair * wide, wide), wide)
    half = pl.ds(pl.multiple_of(member * depth, depth), depth)
    for s_f in range(nf):
        for s_r in range(nr):
            for t in range(tl):
                at = (s_f * tl + t) * plan.image + s_r * cells
                for k in range(plan.chunks // 2):
                    source[at : at + cells, k * 128 : (k + 1) * 128] = got_ref[
                        s_r * nf + s_f, k * local + t * cells : k * local + (t + 1) * cells, :
                    ]
    source[plan.places :, :] = jnp.zeros((2 * plan.image, depth), jnp.bfloat16)
    products = sum(
        one_hot_dot(
            weights[9 * k : 9 * k + 9, both, half].reshape(9 * wide, depth),
            source[(2 - k) * plan.image : (2 - k) * plan.image + plan.places, :],
            ((1,), (1,)),
        )
        for k in range(3)
    )
    merged = one_hot_dot(by_frame_device(plan, got_ref, plan.acts_at, sub), fine_order[...], ((1,), (0,)))
    parts = halves_at(plan, merged)
    for pq in range(4):
        fine_ref[pq] = parts[pq]
    one, two = total(parts), total([part * part for part in parts])
    stats = terms(as_row(one) + pltpu.roll(as_row(two), 64, 1), 3)
    stats = jnp.concatenate(stats + [jnp.zeros_like(stats[0])] * 5, axis=0).astype(jnp.bfloat16)
    merged = one_hot_dot(by_frame_device(plan, got_ref, plan.packed_at, 16), order[...], ((1,), (0,)))
    unpacked = in_places(plan, merged, 16)
    values, cot = [jnp.concatenate([part[k : k + 8] for part in unpacked], axis=0) for k in (0, 8)]
    gain, bias = columns[0][0:sub, 0:1], columns[1][0:sub, 0:1]
    entries = plan.places * plan.group_width
    mean, inv_std = statistics(total([values]), total([values * values]), entries, plan.group_width)
    (normed,), (slope,) = normalised([values], gain, bias, mean, inv_std)
    held_ref[0], held_ref[1], held_ref[2] = normed, slope, cot
    inv_ref[...] = jnp.broadcast_to(inv_std, (sub, 128))
    lane, has_left, has_right, has_up, has_down = plan.place_masks(plan.w)
    by_col = []
    for col in range(3):
        parts = [products[(3 * row + col) * wide : (3 * row + col + 1) * wide] for row in range(3)]
        by_col.append(parts[1] + moved(parts[0], plan.w, has_down) + moved(parts[2], -plan.w, has_up))
    conv_ref[...] = by_col[1] + moved(by_col[0], 1, has_right) + moved(by_col[2], -1, has_left)
    mine_ref[...] = conv_ref[pl.ds(pl.multiple_of(member * sub, sub), sub), :]
    theirs = conv_ref[pl.ds(pl.multiple_of((1 - member) * sub, sub), sub), :]
    sent_ref[0:sub, :] = theirs.astype(jnp.bfloat16)
    sent_ref[sub:, 0:128] = stats
    sent_ref[sub:, 128:] = jnp.zeros((8, plan.places - 128), jnp.bfloat16)


def quarter_kernel(plan, mine_ref, both_ref, held_ref, inv_ref, columns, by_column, out_ref, sums_ref):
    sub = plan.sub
    _, member, _, _ = own_place(plan)
    conv = mine_ref[...] + both_ref[1 - member, 0:sub, :].astype(jnp.float32)
    normed, slope, cot = held_ref[0], held_ref[1], held_ref[2]
    gain, inv_std = columns[0][0:sub, 0:1], inv_ref[:, 0:1]
    entries = plan.places * plan.group_width
    pre = conv * slope
    one, two = total([pre]), total([pre * normed])
    group_one = in_groups(gain * one, plan.group_width) / entries
    group_two = in_groups(gain * two, plan.group_width) / entries
    grad = cot + inv_std * (gain * pre - group_one - normed * group_two)
    quartered = (grad * 0.25).astype(jnp.bfloat16)
    sent = one_hot_dot(quartered, by_column[...], ((1,), (0,))).astype(jnp.bfloat16)
    low = lanes_at((sub // 2, 128), 1) < 64
    for half in range(2):
        at = half * 256
        border = sent[:, 512 + half * 128 : 640 + half * 128]
        border = jnp.where(low, border[: sub // 2], border[sub // 2 :])
        for dest in range(half, plan.count, 2):
            out_ref[dest, 0:sub, :] = sent[:, at : at + 128]
            out_ref[dest, sub : 2 * sub, :] = sent[:, at + 128 : at + 256]
            out_ref[dest, 2 * sub : 2 * sub + sub // 2, :] = border
    sums_ref[...] = jnp.concatenate([as_row(one), as_row(two)], axis=0)


def halves_at(plan, merged):
    sub = plan.sub
    turned = jnp.concatenate([pltpu.roll(merged[:, k * 128 : (k + 1) * 128], 64, 1) for k in range(4)], axis=1)
    low = lanes_at((sub, 128), 1) < 64
    parts = []
    for pq in range(4):
        groups = []
        for group in range(2):
            e = 4 * group + pq
            at = e // 2 * 128
            strips = []
            for m in range(plan.nf // 2):
                first, second = slice(2 * m * sub, (2 * m + 1) * sub), slice((2 * m + 1) * sub, (2 * m + 2) * sub)
                if e % 2 == 0:
                    strips.append(jnp.where(low, merged[first, at : at + 128], turned[second, at : at + 128]))
                else:
                    strips.append(jnp.where(low, turned[first, at : at + 128], merged[second, at : at + 128]))
            groups.append(jnp.concatenate(strips, axis=1))
        parts.append(jnp.concatenate(groups, axis=0))
    return parts


def halves_from(plan, parts):
    sub = plan.sub
    low = lanes_at((sub, 128), 1) < 64
    down = []
    for f in range(plan.nf):
        across = []
        for v in range(4):
            pair = []
            for e in (2 * v, 2 * v + 1):
                group, pq = e // 4, e % 4
                strip = parts[pq][group * sub : (group + 1) * sub, f // 2 * 128 : (f // 2 + 1) * 128]
                pair.append(strip if e % 2 == f % 2 else pltpu.roll(strip, 64, 1))
            across.append(jnp.where(low, pair[0], pair[1]))
        down.append(jnp.concatenate(across, axis=1))
    return jnp.concatenate(down, axis=0)


def fine_kernel(
    plan, got_ref, acts_ref, both_ref, columns, order, sums_ref, weights, out_ref, source, border
):
    sub, nr, nf, wide = plan.sub, plan.nr, plan.nf, 2 * plan.sub
    pair, member, r, _ = own_place(plan)
    both = pl.ds(pl.multiple_of(pair * wide, wide), wide)
    w = plan.w // 2
    lines = plan.places // plan.w
    places = lines * w
    for k in range(2):
        source[:, k * 128 : (k + 1) * 128] = got_ref[:, k * sub : (k + 1) * sub, :].reshape(plan.channels, 128)
    packed = got_ref[:, wide : wide + sub // 2, :].reshape(plan.count * sub // 2, 128)
    shape = (128, places)
    beside = lanes_at(shape, 1) == lanes_at(shape, 0) % lines * w + (1 - member) * (w - 1)
    for k in range(2):
        here = one_hot(beside & (lanes_at(shape, 0) // lines == k))
        found = one_hot_dot(packed, here, ((1,), (0,))).astype(jnp.bfloat16)
        for s in range(plan.count):
            border[s * sub + k * (sub // 2) : s * sub + (k + 1) * (sub // 2), :] = found[
                s * (sub // 2) : (s + 1) * (sub // 2)
            ]
    image = plan.image // 2
    sums, extras = 0.0, 0.0
    for k in (2, 1, 0):
        here, beside = source[...], border[...]
        if k < 2:
            shift = (2 - k) * image
            inside = lanes_at((1, places), 1) < places - shift
            here, beside = [
                jnp.where(inside, pltpu.roll(part, places - shift, 1), jnp.zeros_like(part)) for part in (here, beside)
            ]
        sums = sums + one_hot_dot(
            weights[9 * k : 9 * k + 9, both, :].reshape(9 * wide, plan.channels), here, ((1,), (0,))
        )
        facing = jnp.concatenate([weights[9 * k + 3 * row + 2 * member, both, :] for row in range(3)], axis=0)
        extras = extras + one_hot_dot(facing, beside, ((1,), (0,)))
    parts = [acts_ref[pq] for pq in range(4)]
    stats = sum(both_ref[k, sub : sub + 8, 0:128].astype(jnp.float32) for k in range(2))
    stats = stats[0:1] + stats[1:2] + stats[2:3]
    entries = 4 * plan.places * plan.group_width
    one, two = own_column(stats, 0, wide), own_column(stats, 64, wide)
    mean, inv_std = statistics(one, two, entries, plan.group_width)
    gain, bias = columns[2][:, 0:1], columns[3][:, 0:1]
    normed, slope = normalised(parts, gain, bias, mean, inv_std)
    lane, has_left, has_right, has_up, has_down = plan.place_masks(w)
    right, left = (1 - member).astype(jnp.float32), member.astype(jnp.float32)
    by_row = []
    for row in range(3):
        a, b, c = [sums[(3 * row + col) * wide : (3 * row + col + 1) * wide] for col in range(3)]
        extra = extras[row * wide : (row + 1) * wide]
        by_row.append(
            (a + b + moved(c, -1, has_left) + left * extra, moved(a, 1, has_right) + b + c + right * extra)
        )
    convs = [by_row[0][q] + by_row[1][q] + moved(by_row[2][q], -w, has_up) for q in range(2)]
    convs += [moved(by_row[0][q], w, has_down) + by_row[1][q] + by_row[2][q] for q in range(2)]
    pre = [conv * part for conv, part in zip(convs, slope)]
    one = total(pre)
    two = total([a * b for a, b in zip(pre, normed)])
    cot = source[pl.ds(pl.multiple_of(r * plan.slice_width + pair * wide, wide), wide), :].astype(jnp.float32)
    group_one = in_groups(gain * one, plan.group_width) * (2.0 / entries)
    group_two = in_groups(gain * two, plan.group_width) * (2.0 / entries)
    grads = [cot + inv_std * (gain * part - group_one - unit * group_two) for part, unit in zip(pre, normed)]
    stacked = halves_from(plan, grads).astype(jnp.bfloat16)
    sent = one_hot_dot(stacked, order[...], ((1,), (1,))).astype(jnp.bfloat16)
    coarse = sums_ref[0:1] + pltpu.roll(sums_ref[1:2], sub, 1)
    coded = (
        terms(as_row(one) + pltpu.roll(as_row(two), 64, 1), 2)
        + terms(coarse, 2)
        + terms(as_row(inv_std) + pltpu.roll(as_row(mean), 64, 1), 3)
    )
    coded = jnp.concatenate(coded + [jnp.zeros_like(coarse)], axis=0).astype(jnp.bfloat16)
    for s_r in range(nr):
        for s_f in range(nf):
            out_ref[s_f * nr + s_r, 0:sub, :] = sent[s_f * sub : (s_f + 1) * sub, s_r * 128 : (s_r + 1) * 128]
            out_ref[s_f * nr + s_r, sub : sub + 8, :] = coded


def spread_kernel(plan, got_ref, acts_ref, gain_ref, out_ref, sums_ref):
    sub, nr, nf = plan.sub, plan.nr, plan.nf
    low = lanes_at((sub, 128), 1) < 64
    low_row = lanes_at((1, 128), 1) < 64
    first_row = lanes_at((1, 128), 1) < sub
    source = []
    fine, apart, coarse, moments = [[], []], [[], []], [[], []], [[], []]
    for s_r in range(nr):
        ones, twos, c_ones, c_twos, invs, means = [], [], 0.0, 0.0, [], []
        apart_ones, apart_twos = [], []
        for pair in range(nf // 2):
            at = 2 * pair * nr + s_r
            left, right = [got_ref[at + k * nr, 0:sub, :].astype(jnp.float32) for k in range(2)]
            source.append(jnp.where(low, left, pltpu.roll(right, 64, 1)))
            source.append(jnp.where(low, pltpu.roll(left, 64, 1), right))
            coded = [got_ref[at + k * nr, sub : sub + 8, :].astype(jnp.float32) for k in range(2)]
            halves = [part[0:1] + part[1:2] for part in coded]
            sums, differences = halves[0] + halves[1], halves[1] - halves[0]
            ones.append(sums if pair == 0 else pltpu.roll(sums, 64, 1))
            twos.append(pltpu.roll(sums, 64, 1) if pair == 0 else sums)
            apart_ones.append(differences if pair == 0 else pltpu.roll(differences, 64, 1))
            apart_twos.append(pltpu.roll(differences, 64, 1) if pair == 0 else differences)
            both = coded[0][4:5] + coded[0][5:6] + coded[0][6:7]
            invs.append(both if pair == 0 else pltpu.roll(both, 64, 1))
            means.append(pltpu.roll(both, 64, 1) if pair == 0 else both)
            for k in range(2):
                sums = coded[k][2:3] + coded[k][3:4]
                to = (2 * pair + k) * sub
                c_one = jnp.where(first_row, sums, 0.0)
                c_two = jnp.where(first_row, pltpu.roll(sums, 128 - sub, 1), 0.0)
                c_ones = c_ones + (pltpu.roll(c_one, to, 1) if to else c_one)
                c_twos = c_twos + (pltpu.roll(c_two, to, 1) if to else c_two)
        fine[0].append(jnp.where(low_row, ones[0], ones[1]))
        fine[1].append(jnp.where(low_row, twos[0], twos[1]))
        apart[0].append(jnp.where(low_row, apart_ones[0], apart_ones[1]))
        apart[1].append(jnp.where(low_row, apart_twos[0], apart_twos[1]))
        moments[0].append(jnp.where(low_row, invs[0], invs[1]))
        moments[1].append(jnp.where(low_row, means[0], means[1]))
        coarse[0].append(c_ones)
        coarse[1].append(c_twos)
    one, two, inv_std, mean, c_one, c_two, apart_one, apart_two = [
        jnp.concatenate(part, axis=1) for part in fine + moments + coarse + apart
    ]
    source = jnp.concatenate(source, axis=0).astype(jnp.bfloat16)
    result = one_hot_dot(pixel_order(plan, False), source, ((1,), (1,)))
    gain = gain_ref[...]
    entries = 4 * plan.places * plan.group_width
    group_one = in_lane_groups(gain * apart_one, plan.group_width) / entries
    group_two = in_lane_groups(gain * apart_two, plan.group_width) / entries
    normed = (acts_ref[...].astype(jnp.float32) - mean) * inv_std
    half = lanes_at((4 * plan.local, 1), 0) // plan.w % 2
    signed = jnp.where(half == 0, inv_std, -inv_std)
    out_ref[...] = (result - signed * (group_one + normed * group_two)).astype(jnp.bfloat16)
    sums_ref[...] = jnp.concatenate([one, two, c_one, c_two] + [jnp.zeros_like(one)] * 4, axis=0)


def total_kernel(scales, both_ref, result_ref, result_hbm, out_hbms, rows_ref, sems):
    copies = fetched([(result_ref, result_hbm)], sems)
    rows = sum(both_ref[k] for k in range(both_ref.shape[0]))
    for k in range(4):
        rows_ref[k] = rows[k : k + 1] * scales[k]
    for k in range(4):
        copies.append(pltpu.make_async_copy(rows_ref.at[k], out_hbms[k], sems.at[k + 1]))
        copies[-1].start()
    for copy in copies:
        copy.wait()


def in_vmem(count):
    return [pl.BlockSpec(memory_space=pltpu.VMEM)] * count


def in_hbm(count):
    return [pl.BlockSpec(memory_space=pltpu.HBM)] * count


def kept(array):
    return pltpu.with_memory_space_constraint(array, pltpu.HBM)


def shape_of(shape, kind):
    return jax.ShapeDtypeStruct(shape, kind)


LIMIT = pltpu.CompilerParams(vmem_limit_bytes=40 * 1024 * 1024)
COST = pl.CostEstimate(flops=2_000_000_000, bytes_accessed=4_000_000, transcendentals=0)


def fast_shards(
    plan,
    acts_fine,
    acts_coarse,
    grad_coarse,
    gain_fine,
    bias_fine,
    kernel_fine,
    gain_coarse,
    bias_coarse,
    kernel_coarse,
):
    nd = lax.axis_size("dp")
    count, sub, channels, places, local = plan.count, plan.sub, plan.channels, plan.places, plan.local
    f32, bf16 = jnp.float32, jnp.bfloat16
    rows = [part.reshape(1, channels) for part in (gain_coarse, bias_coarse, gain_fine, bias_fine)]
    places_of = ((local, channels), (local, channels), (4 * local, channels))
    fetched_of = pl.pallas_call(
        fetch_kernel,
        out_shape=tuple(pltpu.VMEM(shape, bf16) for shape in places_of),
        in_specs=in_hbm(3),
        out_specs=tuple(in_vmem(3)),
        scratch_shapes=[pltpu.SemaphoreType.DMA((3,))],
        compiler_params=LIMIT,
    )(*[kept(part.reshape(shape)) for part, shape in zip((grad_coarse, acts_coarse, acts_fine), places_of)])
    acts = fetched_of[2]
    packed = pl.pallas_call(
        functools.partial(pack_kernel, plan),
        out_shape=shape_of((count, plan.block_rows, 128), bf16),
        in_specs=in_vmem(3),
        out_specs=in_vmem(1)[0],
        compiler_params=LIMIT,
        cost_estimate=COST,
    )(*fetched_of)
    got = lax.all_to_all(packed, BLOCK, 0, 0)
    mine, theirs, held, inv_std, fine_acts, columns, fine_order, by_column = pl.pallas_call(
        functools.partial(coarse_kernel, plan),
        out_shape=(
            shape_of((sub, places), f32),
            shape_of((sub + 8, places), bf16),
            shape_of((3, sub, places), f32),
            shape_of((sub, 128), f32),
            shape_of((4, 2 * sub, places // 2), f32),
            shape_of((4, 2 * sub, 128), f32),
            shape_of((4 * plan.nr * local, 4 * plan.nr * local), bf16),
            shape_of((places, places + places // 2), bf16),
        ),
        in_specs=in_vmem(6),
        out_specs=tuple(in_vmem(8)),
        scratch_shapes=[
            pltpu.VMEM((4 * plan.nr * local, 4 * plan.nr * local), bf16),
            pltpu.VMEM((places + 2 * plan.image, channels // 2), bf16),
            pltpu.VMEM((2 * sub, places), f32),
        ],
        compiler_params=LIMIT,
        cost_estimate=COST,
    )(got, kernel_coarse, *rows)
    both = lax.all_gather(theirs, "member")
    quartered, coarse_sums = pl.pallas_call(
        functools.partial(quarter_kernel, plan),
        out_shape=(shape_of((count, 2 * sub + sub // 2, 128), bf16), shape_of((2, 128), f32)),
        in_specs=in_vmem(6),
        out_specs=tuple(in_vmem(2)),
        compiler_params=LIMIT,
        cost_estimate=COST,
    )(mine, both, held, inv_std, columns, by_column)
    spread = lax.all_to_all(quartered, BLOCK, 0, 0)
    sent = pl.pallas_call(
        functools.partial(fine_kernel, plan),
        out_shape=shape_of((count, sub + 8, 128), bf16),
        in_specs=in_vmem(7),
        out_specs=in_vmem(1)[0],
        scratch_shapes=[
            pltpu.VMEM((channels, places // 2), bf16),
            pltpu.VMEM((channels, places // 2), bf16),
        ],
        compiler_params=LIMIT,
        cost_estimate=COST,
    )(spread, fine_acts, both, columns, fine_order, coarse_sums, kernel_fine)
    back = lax.all_to_all(sent, BACK_BLOCK, 0, 0)
    cells = nd * places
    fine_scale, coarse_scale = 1.0 / math.sqrt(4 * cells), 1.0 / math.sqrt(cells)
    out, sums = pl.pallas_call(
        functools.partial(spread_kernel, plan),
        out_shape=(pltpu.VMEM((4 * local, channels), bf16), shape_of((8, channels), f32)),
        in_specs=in_vmem(3),
        out_specs=tuple(in_vmem(2)),
        compiler_params=LIMIT,
        cost_estimate=COST,
    )(back, acts, rows[2])
    both = lax.all_gather(sums, "dp")
    out, sums = pl.pallas_call(
        functools.partial(total_kernel, (fine_scale, fine_scale, coarse_scale, coarse_scale)),
        out_shape=(pltpu.HBM((4 * local, channels), bf16), (pltpu.HBM((1, channels), f32),) * 4),
        in_specs=in_vmem(2),
        out_specs=(in_hbm(1)[0], tuple(in_hbm(4))),
        scratch_shapes=[pltpu.VMEM((4, 1, channels), f32), pltpu.SemaphoreType.DMA((5,))],
        compiler_params=LIMIT,
        cost_estimate=COST,
    )(both, out)
    bias_f, gain_f, bias_c, gain_c = [part.reshape(channels) for part in sums]
    return out.reshape(acts_fine.shape), gain_f, bias_f, gain_c, bias_c


def solution(mesh):
    def function(*arrays):
        local = [size // mesh.shape[axis] for size, axis in zip(arrays[1].shape, ("dp", "frames", "rows"))]
        sizes = (mesh.shape["frames"], mesh.shape["rows"])
        plan = Plan(sizes, (*local[1:], *arrays[1].shape[3:]), arrays[5].shape[1] // mesh.shape["rows"])
        if plan.fits:
            split = (mesh.shape["dp"], plan.nf // 2, 2, plan.nr)
            used = jax.sharding.Mesh(mesh.devices.reshape(split), ("dp", "pairs", "member", "rows"))
            shards, frames = functools.partial(fast_shards, plan), ("pairs", "member")
        else:
            used, shards, frames = mesh, plain_shards, "frames"
        blocks, kernel = P("dp", frames, "rows", None, None), P(None, "rows", None)
        in_specs = (blocks, blocks, blocks, P(), P(), kernel, P(), P(), kernel)
        out_specs = (blocks, P(), P(), P(), P())
        mapped = jax.shard_map(shards, mesh=used, in_specs=in_specs, out_specs=out_specs, check_vma=False)
        return mapped(*arrays)

    return function
```

```python
import functools
import math

import jax
import jax.numpy as jnp
from jax import lax
from jax.experimental import pallas as pl
from jax.experimental.pallas import tpu as pltpu
from jax.sharding import PartitionSpec as P

GROUPS = 32
EPSILON = 1e-06
BLOCK = ("rows", "pairs", "member")
BACK_BLOCK = ("pairs", "member", "rows")
PLAIN_BLOCK = ("frames", "rows")


def plain_everyone(block, count):
    copies = jnp.broadcast_to(block[None], (count,) + block.shape)
    return lax.all_to_all(copies, PLAIN_BLOCK, 0, 0)


def ahead(field, axis, distance):
    size = field.shape[axis]
    if distance == 0:
        return field
    widths = [(0, 0)] * field.ndim
    if distance > 0:
        widths[axis] = (0, distance)
        kept = lax.slice_in_dim(field, distance, size, axis=axis)
    else:
        widths[axis] = (-distance, 0)
        kept = lax.slice_in_dim(field, 0, size + distance, axis=axis)
    return jnp.pad(kept, widths)


def tap_products(source, kernel):
    sub = kernel.shape[1]
    frames, rows, cols, channels = source.shape
    products = lax.dot_general(
        kernel.reshape(27 * sub, channels),
        source.reshape(frames * rows * cols, channels),
        (((1,), (1,)), ((), ())),
        preferred_element_type=jnp.float32,
    ).reshape(3, 3, 3, sub, frames, rows, cols)
    return sum(ahead(products[depth], 3, 2 - depth) for depth in range(3))


def coarse_conv(source, kernel):
    spatial = tap_products(source, kernel)
    total = 0.0
    for row in range(3):
        part = sum(ahead(spatial[row, col], 3, 1 - col) for col in range(3))
        total = total + ahead(part, 2, 1 - row)
    return total


def fine_conv(source, kernel):
    spatial = tap_products(source, kernel)
    result = []
    for p in range(2):
        rows_of = []
        for q in range(2):
            total = 0.0
            for row in range(3):
                part = sum(ahead(spatial[row, col], 3, (q + 1 - col) // 2) for col in range(3))
                total = total + ahead(part, 2, (p + 1 - row) // 2)
            rows_of.append(total)
        result.append(jnp.stack(rows_of, 1))
    return jnp.stack(result, 1)


def group_total(sums, group_width):
    sub = sums.shape[-1]
    if sub % group_width == 0:
        grouped = jnp.sum(sums.reshape(-1, sub // group_width, group_width), axis=-1)
        return jnp.repeat(grouped, group_width, axis=-1)
    spread = jnp.moveaxis(lax.all_gather(sums, "frames"), 0, 1).reshape(sums.shape[0], -1, group_width)
    mine = lax.axis_index("frames") * sub // group_width
    grouped = lax.dynamic_index_in_dim(jnp.sum(spread, -1), mine, 1)
    return jnp.broadcast_to(grouped, sums.shape)


def level(acts, conv_grad, cotangent, gain, bias, group_width):
    sub = acts.shape[0]
    places = acts.size // sub
    values = acts.astype(jnp.float32).reshape(sub, places)
    conv_grad = conv_grad.reshape(sub, places)
    entries = places * group_width
    moments = group_total(
        jnp.stack([jnp.sum(values, 1), jnp.sum(values * values, 1)]), group_width
    ) / entries
    mean = moments[0]
    inv_std = lax.rsqrt(moments[1] - mean * mean + EPSILON)
    normed = (values - mean[:, None]) * inv_std[:, None]
    preact = gain[:, None] * normed + bias[:, None]
    squash = jax.nn.sigmoid(preact)
    pre_grad = conv_grad * squash * (1.0 + preact * (1.0 - squash))
    sums = jnp.stack([jnp.sum(pre_grad, 1), jnp.sum(pre_grad * normed, 1)])
    terms = group_total(sums * gain, group_width) / entries
    grad = cotangent.reshape(sub, places) + inv_std[:, None] * (
        gain[:, None] * pre_grad - terms[0][:, None] - normed * terms[1][:, None]
    )
    return grad, sums


def plain_shards(
    acts_fine,
    acts_coarse,
    grad_coarse,
    gain_fine,
    bias_fine,
    kernel_fine,
    gain_coarse,
    bias_coarse,
    kernel_coarse,
):
    nf, nr, nd = lax.axis_size("frames"), lax.axis_size("rows"), lax.axis_size("dp")
    count = nf * nr
    channels = acts_fine.shape[-1]
    slice_width = kernel_fine.shape[1]
    sub = slice_width // nf
    group_width = channels // GROUPS
    tl, hl, w = acts_coarse.shape[1:4]
    frames, rows = tl * nf, hl * nr
    f, r = lax.axis_index("frames"), lax.axis_index("rows")

    gathered = plain_everyone(grad_coarse[0], count)
    source = (
        gathered.reshape(nf, nr, tl, hl, w, channels)
        .transpose(0, 2, 1, 3, 4, 5)
        .reshape(frames, rows, w, channels)
    )
    coarse_in = acts_coarse[0].reshape(tl, hl, w, nr, nf, sub).transpose(4, 3, 5, 0, 1, 2)
    coarse_in = lax.all_to_all(coarse_in.reshape(count, sub, tl * hl * w), PLAIN_BLOCK, 0, 0)
    fine_in = acts_fine[0].reshape(tl, hl, 2, w, 2, nr, nf, sub).transpose(6, 5, 7, 2, 4, 0, 1, 3)
    fine_in = lax.all_to_all(fine_in.reshape(count, sub, 4 * tl * hl * w), PLAIN_BLOCK, 0, 0)

    def mine(vector):
        return lax.dynamic_slice_in_dim(vector, r * slice_width + f * sub, sub)

    def own(kernel):
        return lax.dynamic_slice_in_dim(kernel, f * sub, sub, axis=1)

    coarse_vals = (
        coarse_in.reshape(nf, nr, sub, tl, hl, w).transpose(2, 0, 3, 1, 4, 5).reshape(sub, frames, rows, w)
    )
    cot = lax.dynamic_slice_in_dim(source, r * slice_width + f * sub, sub, axis=3)
    cot = cot.astype(jnp.float32).transpose(3, 0, 1, 2)
    conv = coarse_conv(source, own(kernel_coarse))
    coarse_grad, coarse_sums = level(
        coarse_vals, conv, cot, mine(gain_coarse), mine(bias_coarse), group_width
    )
    quartered = (coarse_grad * 0.25).astype(jnp.bfloat16)
    spread = plain_everyone(quartered, count)
    source_fine = (
        spread.reshape(nf, nr, sub, frames, rows, w)
        .transpose(3, 4, 5, 1, 0, 2)
        .reshape(frames, rows, w, channels)
    )
    conv = fine_conv(source_fine, own(kernel_fine))
    fine_vals = (
        fine_in.reshape(nf, nr, sub, 2, 2, tl, hl, w)
        .transpose(2, 3, 4, 0, 5, 1, 6, 7)
        .reshape(sub, 2, 2, frames, rows, w)
    )
    cot = jnp.broadcast_to(
        quartered.astype(jnp.float32).reshape(sub, 1, 1, frames, rows, w), conv.shape
    )
    fine_grad, fine_sums = level(
        fine_vals, conv, cot, mine(gain_fine), mine(bias_fine), group_width
    )
    back = (
        fine_grad.astype(jnp.bfloat16)
        .reshape(sub, 2, 2, nf, tl, nr, hl, w)
        .transpose(3, 5, 0, 1, 2, 4, 6, 7)
        .reshape(count, sub, 4 * tl * hl * w)
    )
    sums = plain_everyone(jnp.concatenate([fine_sums, coarse_sums]), count)
    back = lax.all_to_all(back, PLAIN_BLOCK, 0, 0)
    out = (
        back.reshape(nf, nr, sub, 2, 2, tl, hl, w)
        .transpose(5, 6, 3, 7, 4, 1, 0, 2)
        .reshape(1, tl, 2 * hl, 2 * w, channels)
    )
    sums = sums.reshape(nf, nr, 4, sub).transpose(2, 1, 0, 3).reshape(4, channels)
    totals = lax.psum(sums, "dp")
    cells = nd * frames * rows * w
    scale_fine = 1.0 / jnp.sqrt(jnp.float32(4 * cells))
    scale_coarse = 1.0 / jnp.sqrt(jnp.float32(cells))
    return (
        out,
        totals[1] * scale_fine,
        totals[0] * scale_fine,
        totals[3] * scale_coarse,
        totals[2] * scale_coarse,
    )


def lanes_at(shape, axis):
    return lax.broadcasted_iota(jnp.int32, shape, axis)


def one_hot(found):
    return found.astype(jnp.float32).astype(jnp.bfloat16)


def pixel_order(plan, swapped):
    tl, hl, w = plan.tl, plan.hl, plan.w // 2
    size = 4 * plan.local
    lane = lanes_at((1, size), 1)
    j, i, t = lane % w, lane // w % hl, lane // (w * hl) % tl
    q, p = lane // (w * hl * tl) % 2, lane // (2 * w * hl * tl) % 2
    half = lane // (4 * w * hl * tl)
    if swapped:
        half = 1 - half
    pixel = (t * 2 * hl + 2 * i + p) * 4 * w + 2 * (half * w + j) + q
    return one_hot(lanes_at((size, size), 0) == pixel)


def merged_order(nr, outer, tl, cells):
    size = nr * outer * tl * cells
    lane = lanes_at((1, size), 1)
    cell, dev = lane % cells, lane // cells % nr
    t, o = lane // (cells * nr) % tl, lane // (cells * nr * tl)
    return one_hot(lanes_at((size, size), 0) == ((dev * outer + o) * tl + t) * cells + cell)


def column_order(plan):
    w = plan.w // 2
    lines = plan.places // plan.w
    lane = lanes_at((1, 4 * lines * w + 4 * lines), 1)
    inner = lane % (lines * w)
    place = inner // w * plan.w + lane // (lines * w) * w + inner % w
    past = lane - 2 * lines * w
    border = past % lines * plan.w + jnp.where(past < 2 * lines, w, w - 1)
    wanted = jnp.where(past >= 0, border, place)
    shape = (plan.places, 2 * lines * w + 4 * lines)
    return one_hot(lanes_at(shape, 0) == wanted[:, : shape[1]])


def one_hot_dot(a, b, dims):
    return lax.dot_general(a, b, (dims, ((), ())), preferred_element_type=jnp.float32)


def moved(field, distance, kept):
    size = field.shape[1]
    return jnp.where(kept, pltpu.roll(field, (-distance) % size, 1), 0.0)


def own_column(row, base, sub):
    shape = (sub, row.shape[1])
    mine = lanes_at(shape, 1) == lanes_at(shape, 0) + base
    return jnp.sum(jnp.where(mine, row, 0.0), axis=1, keepdims=True)


def as_row(column):
    shape = (column.shape[0], 128)
    here = lanes_at(shape, 1) == lanes_at(shape, 0)
    return jnp.sum(jnp.where(here, column, 0.0), axis=0, keepdims=True)


def terms(value, count):
    found = []
    for _ in range(count):
        found.append(value.astype(jnp.bfloat16).astype(jnp.float32))
        value = value - found[-1]
    return found


def in_groups(column, group_width):
    sub = column.shape[0]
    grouped = jnp.sum(column.reshape(sub // group_width, group_width, 1), axis=1, keepdims=True)
    return jnp.broadcast_to(grouped, (sub // group_width, group_width, 1)).reshape(sub, 1)


def in_lane_groups(row, group_width):
    lane = lanes_at(row.shape, 1)
    size = row.shape[1]
    step = 1
    while step < group_width:
        up, down = pltpu.roll(row, size - step, 1), pltpu.roll(row, step, 1)
        row = row + jnp.where(lane // step % 2 == 0, up, down)
        step *= 2
    return row


def total(parts):
    return sum(jnp.sum(part, axis=1, keepdims=True) for part in parts)


def statistics(one, two, entries, group_width):
    mean = in_groups(one, group_width) / entries
    square = in_groups(two, group_width) / entries
    return mean, lax.rsqrt(square - mean * mean + EPSILON)


def normalised(parts, gain, bias, mean, inv_std):
    normed, slope = [], []
    for part in parts:
        unit = (part - mean) * inv_std
        preact = gain * unit + bias
        squash = 0.5 + 0.5 * jnp.tanh(0.5 * preact)
        normed.append(unit)
        slope.append(squash * (1.0 + preact * (1.0 - squash)))
    return normed, slope


class Plan:
    def __init__(self, mesh_sizes, acts_coarse, slice_width):
        self.nf, self.nr = mesh_sizes
        self.count = self.nf * self.nr
        self.tl, self.hl, self.w, self.channels = acts_coarse
        self.slice_width = slice_width
        self.sub = slice_width // self.nf
        self.cells = self.hl * self.w
        self.local = self.tl * self.cells
        self.image = self.cells * self.nr
        self.frames = self.tl * self.nf
        self.places = self.frames * self.image
        self.group_width = self.channels // GROUPS
        self.chunks = self.channels // 128
        self.acts_at = self.chunks // 2 * self.local
        self.packed_at = self.acts_at + self.sub
        self.cot_at = self.packed_at + 8
        self.block_rows = self.cot_at + 8
        self.fits = (
            self.sub == 32
            and self.slice_width == 128
            and self.group_width == 16
            and self.cells == 16
            and self.w == 8
            and self.tl == 2
            and self.nr == 4
            and self.nf == 4
            and self.slice_width * self.nr == self.channels
        )

    def place_masks(self, w):
        lane = lanes_at((1, self.places // self.w * w), 1)
        col, row = lane % w, lane // w % (self.hl * self.nr)
        last_row = self.hl * self.nr - 1
        return (lane, col > 0, col < w - 1, row > 0, row < last_row)


def fetched(pairs, sems):
    copies = [pltpu.make_async_copy(src, dst, sems.at[k]) for k, (src, dst) in enumerate(pairs)]
    for copy in copies:
        copy.start()
    return copies


def own_place(plan):
    pair, member, r = lax.axis_index("pairs"), lax.axis_index("member"), lax.axis_index("rows")
    return pair, member, r, r * plan.slice_width + (2 * pair + member) * plan.sub


def fetch_kernel(g_hbm, coarse_hbm, fine_hbm, g_ref, coarse_ref, fine_ref, sems):
    for copy in fetched([(fine_hbm, fine_ref), (coarse_hbm, coarse_ref), (g_hbm, g_ref)], sems):
        copy.wait()


def pack_kernel(plan, g_ref, coarse_ref, fine_ref, out_ref):
    sub, chunks, local = plan.sub, plan.chunks, plan.local
    shape = (2 * local, 2 * 128)
    lane = lanes_at((1, 2 * 128), 1)
    repeated = one_hot(lanes_at(shape, 0) == lane % local + lane // 128 * local)
    shape = (plan.channels, 128)
    quarter = lanes_at(shape, 0) // 8 % 4 == lanes_at(shape, 1) // local
    orders = jnp.concatenate([pixel_order(plan, swapped) for swapped in (False, True)], axis=1)
    acts = fine_ref[...]
    halves = one_hot_dot(acts, orders, ((0,), (0,))).astype(jnp.bfloat16)
    halves = [halves[:, :128], halves[:, 128:]]
    small = one_hot_dot(jnp.concatenate([coarse_ref[...], g_ref[...]], axis=0), repeated, ((0,), (0,)))
    for k, at in enumerate((plan.packed_at, plan.cot_at)):
        rows_of = jnp.where(quarter, small[:, k * 128 : (k + 1) * 128], 0.0).reshape(plan.count, 4, 8, 128)
        out_ref[:, at : at + 8, :] = jnp.sum(rows_of, axis=1).astype(jnp.bfloat16)
    low = lanes_at((sub, 128), 1) < 64
    for s_r in range(plan.nr):
        for s_f in range(plan.nf):
            dest = s_r * plan.nf + s_f
            first, half = s_r * plan.slice_width + s_f // 2 * 2 * sub, s_f % 2
            for k in range(chunks // 2):
                at = (half * chunks // 2 + k) * 128
                out_ref[dest, k * local : (k + 1) * local, :] = g_ref[:, at : at + 128]
            upper, lower = halves[half][first : first + sub], halves[1 - half][first + sub : first + 2 * sub]
            out_ref[dest, plan.acts_at : plan.packed_at, :] = jnp.where(low, upper, lower)


def by_frame_device(plan, got_ref, at, height):
    return jnp.concatenate(
        [
            jnp.concatenate(
                [got_ref[r * plan.nf + f, at : at + height, :] for r in range(plan.nr)], axis=1
            )
            for f in range(plan.nf)
        ],
        axis=0,
    )


def in_places(plan, merged, height):
    width = plan.tl * plan.image
    return [
        jnp.concatenate(
            [merged[f * height : (f + 1) * height, k * width : (k + 1) * width] for f in range(plan.nf)],
            axis=1,
        )
        for k in range(4)
    ]


def coarse_kernel(
    plan,
    got_ref,
    weights,
    gain_c,
    bias_c,
    gain_f,
    bias_f,
    mine_ref,
    sent_ref,
    held_ref,
    inv_ref,
    fine_ref,
    columns,
    fine_order,
    by_column,
    order,
    source,
    conv_ref,
):
    sub, nr, nf, cells, tl, local = plan.sub, plan.nr, plan.nf, plan.cells, plan.tl, plan.local
    wide, depth = 2 * sub, plan.channels // 2
    pair, member, r, base = own_place(plan)
    first = r * plan.slice_width + pair * wide
    columns[0, 0:sub, :] = jnp.broadcast_to(own_column(gain_c[...], base, sub), (sub, 128))
    columns[1, 0:sub, :] = jnp.broadcast_to(own_column(bias_c[...], base, sub), (sub, 128))
    columns[2] = jnp.broadcast_to(own_column(gain_f[...], first, wide), (wide, 128))
    columns[3] = jnp.broadcast_to(own_column(bias_f[...], first, wide), (wide, 128))
    order[...] = merged_order(plan.nr, 4, plan.tl, plan.cells)
    fine_order[...] = merged_order(plan.nr, 8, plan.tl, plan.cells // 2)
    by_column[...] = column_order(plan)
    both = pl.ds(pl.multiple_of(pair * wide, wide), wide)
    half = pl.ds(pl.multiple_of(member * depth, depth), depth)
    for s_f in range(nf):
        for s_r in range(nr):
            for t in range(tl):
                at = (s_f * tl + t) * plan.image + s_r * cells
                for k in range(plan.chunks // 2):
                    source[at : at + cells, k * 128 : (k + 1) * 128] = got_ref[
                        s_r * nf + s_f, k * local + t * cells : k * local + (t + 1) * cells, :
                    ]
    source[plan.places :, :] = jnp.zeros((2 * plan.image, depth), jnp.bfloat16)
    products = sum(
        one_hot_dot(
            weights[9 * k : 9 * k + 9, both, half].reshape(9 * wide, depth),
            source[(2 - k) * plan.image : (2 - k) * plan.image + plan.places, :],
            ((1,), (1,)),
        )
        for k in range(3)
    )
    merged = one_hot_dot(by_frame_device(plan, got_ref, plan.acts_at, sub), fine_order[...], ((1,), (0,)))
    parts = halves_at(plan, merged)
    for pq in range(4):
        fine_ref[pq] = parts[pq]
    one, two = total(parts), total([part * part for part in parts])
    stats = terms(as_row(one) + pltpu.roll(as_row(two), 64, 1), 3)
    stats = jnp.concatenate(stats + [jnp.zeros_like(stats[0])] * 5, axis=0).astype(jnp.bfloat16)
    small = [by_frame_device(plan, got_ref, at, 8) for at in (plan.packed_at, plan.cot_at)]
    merged = one_hot_dot(jnp.concatenate(small, axis=0), order[...], ((1,), (0,)))
    rows_of = 8 * nf
    values, cot = [
        jnp.concatenate(in_places(plan, merged[k * rows_of : (k + 1) * rows_of], 8), axis=0) for k in range(2)
    ]
    gain, bias = columns[0][0:sub, 0:1], columns[1][0:sub, 0:1]
    entries = plan.places * plan.group_width
    mean, inv_std = statistics(total([values]), total([values * values]), entries, plan.group_width)
    (normed,), (slope,) = normalised([values], gain, bias, mean, inv_std)
    held_ref[0], held_ref[1], held_ref[2] = normed, slope, cot
    inv_ref[...] = jnp.broadcast_to(inv_std, (sub, 128))
    lane, has_left, has_right, has_up, has_down = plan.place_masks(plan.w)
    by_col = []
    for col in range(3):
        parts = [products[(3 * row + col) * wide : (3 * row + col + 1) * wide] for row in range(3)]
        by_col.append(parts[1] + moved(parts[0], plan.w, has_down) + moved(parts[2], -plan.w, has_up))
    conv_ref[...] = by_col[1] + moved(by_col[0], 1, has_right) + moved(by_col[2], -1, has_left)
    mine_ref[...] = conv_ref[pl.ds(pl.multiple_of(member * sub, sub), sub), :]
    theirs = conv_ref[pl.ds(pl.multiple_of((1 - member) * sub, sub), sub), :]
    sent_ref[0, 0:sub, :] = theirs.astype(jnp.bfloat16)
    sent_ref[0, sub:, 0:128] = stats
    sent_ref[0, sub:, 128:] = jnp.zeros((8, plan.places - 128), jnp.bfloat16)


def quarter_kernel(plan, mine_ref, both_ref, held_ref, inv_ref, columns, by_column, out_ref, sums_ref):
    sub = plan.sub
    _, member, _, _ = own_place(plan)
    conv = mine_ref[...] + both_ref[1 - member, 0:sub, :].astype(jnp.float32)
    normed, slope, cot = held_ref[0], held_ref[1], held_ref[2]
    gain, inv_std = columns[0][0:sub, 0:1], inv_ref[:, 0:1]
    entries = plan.places * plan.group_width
    pre = conv * slope
    one, two = total([pre]), total([pre * normed])
    group_one = in_groups(gain * one, plan.group_width) / entries
    group_two = in_groups(gain * two, plan.group_width) / entries
    grad = cot + inv_std * (gain * pre - group_one - normed * group_two)
    quartered = (grad * 0.25).astype(jnp.bfloat16)
    sent = one_hot_dot(quartered, by_column[...], ((1,), (0,))).astype(jnp.bfloat16)
    low = lanes_at((sub // 2, 128), 1) < 64
    for half in range(2):
        at = half * 256
        border = sent[:, 512 + half * 128 : 640 + half * 128]
        border = jnp.where(low, border[: sub // 2], border[sub // 2 :])
        for dest in range(half, plan.count, 2):
            out_ref[dest, 0:sub, :] = sent[:, at : at + 128]
            out_ref[dest, sub : 2 * sub, :] = sent[:, at + 128 : at + 256]
            out_ref[dest, 2 * sub : 2 * sub + sub // 2, :] = border
    sums_ref[...] = jnp.concatenate([as_row(one), as_row(two)], axis=0)


def halves_at(plan, merged):
    sub = plan.sub
    turned = jnp.concatenate([pltpu.roll(merged[:, k * 128 : (k + 1) * 128], 64, 1) for k in range(4)], axis=1)
    low = lanes_at((sub, 128), 1) < 64
    parts = []
    for pq in range(4):
        groups = []
        for group in range(2):
            e = 4 * group + pq
            at = e // 2 * 128
            strips = []
            for m in range(plan.nf // 2):
                first, second = slice(2 * m * sub, (2 * m + 1) * sub), slice((2 * m + 1) * sub, (2 * m + 2) * sub)
                if e % 2 == 0:
                    strips.append(jnp.where(low, merged[first, at : at + 128], turned[second, at : at + 128]))
                else:
                    strips.append(jnp.where(low, turned[first, at : at + 128], merged[second, at : at + 128]))
            groups.append(jnp.concatenate(strips, axis=1))
        parts.append(jnp.concatenate(groups, axis=0))
    return parts


def halves_from(plan, parts):
    sub = plan.sub
    low = lanes_at((sub, 128), 1) < 64
    down = []
    for f in range(plan.nf):
        across = []
        for v in range(4):
            pair = []
            for e in (2 * v, 2 * v + 1):
                group, pq = e // 4, e % 4
                strip = parts[pq][group * sub : (group + 1) * sub, f // 2 * 128 : (f // 2 + 1) * 128]
                pair.append(strip if e % 2 == f % 2 else pltpu.roll(strip, 64, 1))
            across.append(jnp.where(low, pair[0], pair[1]))
        down.append(jnp.concatenate(across, axis=1))
    return jnp.concatenate(down, axis=0)


def fine_kernel(
    plan, got_ref, acts_ref, both_ref, columns, order, sums_ref, weights, out_ref, source, border
):
    sub, nr, nf, wide = plan.sub, plan.nr, plan.nf, 2 * plan.sub
    pair, member, r, _ = own_place(plan)
    both = pl.ds(pl.multiple_of(pair * wide, wide), wide)
    w = plan.w // 2
    lines = plan.places // plan.w
    places = lines * w
    for k in range(2):
        source[:, k * 128 : (k + 1) * 128] = got_ref[:, k * sub : (k + 1) * sub, :].reshape(plan.channels, 128)
    packed = got_ref[:, wide : wide + sub // 2, :].reshape(plan.count * sub // 2, 128)
    shape = (128, places)
    beside = lanes_at(shape, 1) == lanes_at(shape, 0) % lines * w + (1 - member) * (w - 1)
    for k in range(2):
        here = one_hot(beside & (lanes_at(shape, 0) // lines == k))
        found = one_hot_dot(packed, here, ((1,), (0,))).astype(jnp.bfloat16)
        for s in range(plan.count):
            border[s * sub + k * (sub // 2) : s * sub + (k + 1) * (sub // 2), :] = found[
                s * (sub // 2) : (s + 1) * (sub // 2)
            ]
    image = plan.image // 2
    sums, extras = 0.0, 0.0
    for k in (2, 1, 0):
        here, beside = source[...], border[...]
        if k < 2:
            shift = (2 - k) * image
            inside = lanes_at((1, places), 1) < places - shift
            here, beside = [
                jnp.where(inside, pltpu.roll(part, places - shift, 1), jnp.zeros_like(part)) for part in (here, beside)
            ]
        sums = sums + one_hot_dot(
            weights[9 * k : 9 * k + 9, both, :].reshape(9 * wide, plan.channels), here, ((1,), (0,))
        )
        facing = jnp.concatenate([weights[9 * k + 3 * row + 2 * member, both, :] for row in range(3)], axis=0)
        extras = extras + one_hot_dot(facing, beside, ((1,), (0,)))
    parts = [acts_ref[pq] for pq in range(4)]
    stats = sum(both_ref[k, sub : sub + 8, 0:128].astype(jnp.float32) for k in range(2))
    stats = stats[0:1] + stats[1:2] + stats[2:3]
    entries = 4 * plan.places * plan.group_width
    one, two = own_column(stats, 0, wide), own_column(stats, 64, wide)
    mean, inv_std = statistics(one, two, entries, plan.group_width)
    gain, bias = columns[2][:, 0:1], columns[3][:, 0:1]
    normed, slope = normalised(parts, gain, bias, mean, inv_std)
    lane, has_left, has_right, has_up, has_down = plan.place_masks(w)
    right, left = (1 - member).astype(jnp.float32), member.astype(jnp.float32)
    by_row = []
    for row in range(3):
        a, b, c = [sums[(3 * row + col) * wide : (3 * row + col + 1) * wide] for col in range(3)]
        extra = extras[row * wide : (row + 1) * wide]
        by_row.append(
            (a + b + moved(c, -1, has_left) + left * extra, moved(a, 1, has_right) + b + c + right * extra)
        )
    convs = [by_row[0][q] + by_row[1][q] + moved(by_row[2][q], -w, has_up) for q in range(2)]
    convs += [moved(by_row[0][q], w, has_down) + by_row[1][q] + by_row[2][q] for q in range(2)]
    pre = [conv * part for conv, part in zip(convs, slope)]
    one = total(pre)
    two = total([a * b for a, b in zip(pre, normed)])
    cot = source[pl.ds(pl.multiple_of(r * plan.slice_width + pair * wide, wide), wide), :].astype(jnp.float32)
    scale = inv_std * gain
    stacked = halves_from(plan, [cot + scale * part for part in pre]).astype(jnp.bfloat16)
    sent = one_hot_dot(stacked, order[...], ((1,), (1,))).astype(jnp.bfloat16)
    coarse = sums_ref[0:1] + pltpu.roll(sums_ref[1:2], sub, 1)
    coded = (
        terms(as_row(one) + pltpu.roll(as_row(two), 64, 1), 2)
        + terms(coarse, 2)
        + terms(as_row(inv_std) + pltpu.roll(as_row(mean), 64, 1), 3)
    )
    coded = jnp.concatenate(coded + [jnp.zeros_like(coarse)], axis=0).astype(jnp.bfloat16)
    for s_r in range(nr):
        for s_f in range(nf):
            out_ref[s_f * nr + s_r, 0:sub, :] = sent[s_f * sub : (s_f + 1) * sub, s_r * 128 : (s_r + 1) * 128]
            out_ref[s_f * nr + s_r, sub : sub + 8, :] = coded


def spread_kernel(plan, got_ref, acts_ref, gain_ref, out_ref, sums_ref):
    sub, nr, nf = plan.sub, plan.nr, plan.nf
    low = lanes_at((sub, 128), 1) < 64
    low_row = lanes_at((1, 128), 1) < 64
    first_row = lanes_at((1, 128), 1) < sub
    source = []
    fine, coarse, moments = [[], []], [[], []], [[], []]
    for s_r in range(nr):
        ones, twos, c_ones, c_twos, invs, means = [], [], 0.0, 0.0, [], []
        for pair in range(nf // 2):
            at = 2 * pair * nr + s_r
            left, right = [got_ref[at + k * nr, 0:sub, :].astype(jnp.float32) for k in range(2)]
            source.append(jnp.where(low, left, pltpu.roll(right, 64, 1)))
            source.append(jnp.where(low, pltpu.roll(left, 64, 1), right))
            coded = [got_ref[at + k * nr, sub : sub + 8, :].astype(jnp.float32) for k in range(2)]
            sums = coded[0][0:1] + coded[0][1:2] + coded[1][0:1] + coded[1][1:2]
            ones.append(sums if pair == 0 else pltpu.roll(sums, 64, 1))
            twos.append(pltpu.roll(sums, 64, 1) if pair == 0 else sums)
            both = coded[0][4:5] + coded[0][5:6] + coded[0][6:7]
            invs.append(both if pair == 0 else pltpu.roll(both, 64, 1))
            means.append(pltpu.roll(both, 64, 1) if pair == 0 else both)
            for k in range(2):
                sums = coded[k][2:3] + coded[k][3:4]
                to = (2 * pair + k) * sub
                c_one = jnp.where(first_row, sums, 0.0)
                c_two = jnp.where(first_row, pltpu.roll(sums, 128 - sub, 1), 0.0)
                c_ones = c_ones + (pltpu.roll(c_one, to, 1) if to else c_one)
                c_twos = c_twos + (pltpu.roll(c_two, to, 1) if to else c_two)
        fine[0].append(jnp.where(low_row, ones[0], ones[1]))
        fine[1].append(jnp.where(low_row, twos[0], twos[1]))
        moments[0].append(jnp.where(low_row, invs[0], invs[1]))
        moments[1].append(jnp.where(low_row, means[0], means[1]))
        coarse[0].append(c_ones)
        coarse[1].append(c_twos)
    one, two, inv_std, mean, c_one, c_two = [jnp.concatenate(part, axis=1) for part in fine + moments + coarse]
    source = jnp.concatenate(source, axis=0).astype(jnp.bfloat16)
    result = one_hot_dot(pixel_order(plan, False), source, ((1,), (1,)))
    gain = gain_ref[...]
    entries = 4 * plan.places * plan.group_width
    group_one = in_lane_groups(gain * one, plan.group_width) / entries
    group_two = in_lane_groups(gain * two, plan.group_width) / entries
    normed = (acts_ref[...].astype(jnp.float32) - mean) * inv_std
    out_ref[...] = (result - inv_std * (group_one + normed * group_two)).astype(jnp.bfloat16)
    sums_ref[0] = jnp.concatenate([one, two, c_one, c_two] + [jnp.zeros_like(one)] * 4, axis=0)


def total_kernel(scales, both_ref, result_ref, result_hbm, out_hbms, rows_ref, sems):
    copies = fetched([(result_ref, result_hbm)], sems)
    rows = sum(both_ref[k] for k in range(both_ref.shape[0]))
    for k in range(4):
        rows_ref[k] = rows[k : k + 1] * scales[k]
    for k in range(4):
        copies.append(pltpu.make_async_copy(rows_ref.at[k], out_hbms[k], sems.at[k + 1]))
        copies[-1].start()
    for copy in copies:
        copy.wait()


def in_vmem(count):
    return [pl.BlockSpec(memory_space=pltpu.VMEM)] * count


def in_hbm(count):
    return [pl.BlockSpec(memory_space=pltpu.HBM)] * count


def kept(array):
    return pltpu.with_memory_space_constraint(array, pltpu.HBM)


def shape_of(shape, kind):
    return jax.ShapeDtypeStruct(shape, kind)


LIMIT = pltpu.CompilerParams(vmem_limit_bytes=40 * 1024 * 1024)
COST = pl.CostEstimate(flops=2_000_000_000, bytes_accessed=4_000_000, transcendentals=0)


def fast_shards(
    plan,
    acts_fine,
    acts_coarse,
    grad_coarse,
    gain_fine,
    bias_fine,
    kernel_fine,
    gain_coarse,
    bias_coarse,
    kernel_coarse,
):
    nd = lax.axis_size("dp")
    count, sub, channels, places, local = plan.count, plan.sub, plan.channels, plan.places, plan.local
    f32, bf16 = jnp.float32, jnp.bfloat16
    rows = [part.reshape(1, channels) for part in (gain_coarse, bias_coarse, gain_fine, bias_fine)]
    places_of = ((local, channels), (local, channels), (4 * local, channels))
    fetched_of = pl.pallas_call(
        fetch_kernel,
        out_shape=tuple(pltpu.VMEM(shape, bf16) for shape in places_of),
        in_specs=in_hbm(3),
        out_specs=tuple(in_vmem(3)),
        scratch_shapes=[pltpu.SemaphoreType.DMA((3,))],
        compiler_params=LIMIT,
    )(*[kept(part.reshape(shape)) for part, shape in zip((grad_coarse, acts_coarse, acts_fine), places_of)])
    acts = fetched_of[2]
    packed = pl.pallas_call(
        functools.partial(pack_kernel, plan),
        out_shape=shape_of((count, plan.block_rows, 128), bf16),
        in_specs=in_vmem(3),
        out_specs=in_vmem(1)[0],
        compiler_params=LIMIT,
        cost_estimate=COST,
    )(*fetched_of)
    got = lax.all_to_all(packed, BLOCK, 0, 0)
    mine, theirs, held, inv_std, fine_acts, columns, fine_order, by_column = pl.pallas_call(
        functools.partial(coarse_kernel, plan),
        out_shape=(
            shape_of((sub, places), f32),
            shape_of((1, sub + 8, places), bf16),
            shape_of((3, sub, places), f32),
            shape_of((sub, 128), f32),
            shape_of((4, 2 * sub, places // 2), f32),
            shape_of((4, 2 * sub, 128), f32),
            shape_of((4 * plan.nr * local, 4 * plan.nr * local), bf16),
            shape_of((places, places + places // 2), bf16),
        ),
        in_specs=in_vmem(6),
        out_specs=tuple(in_vmem(8)),
        scratch_shapes=[
            pltpu.VMEM((4 * plan.nr * local, 4 * plan.nr * local), bf16),
            pltpu.VMEM((places + 2 * plan.image, channels // 2), bf16),
            pltpu.VMEM((2 * sub, places), f32),
        ],
        compiler_params=LIMIT,
        cost_estimate=COST,
    )(got, kernel_coarse, *rows)
    both = lax.all_gather(theirs, "member", axis=0, tiled=True)
    quartered, coarse_sums = pl.pallas_call(
        functools.partial(quarter_kernel, plan),
        out_shape=(shape_of((count, 2 * sub + sub // 2, 128), bf16), shape_of((2, 128), f32)),
        in_specs=in_vmem(6),
        out_specs=tuple(in_vmem(2)),
        compiler_params=LIMIT,
        cost_estimate=COST,
    )(mine, both, held, inv_std, columns, by_column)
    spread = lax.all_to_all(quartered, BLOCK, 0, 0)
    sent = pl.pallas_call(
        functools.partial(fine_kernel, plan),
        out_shape=shape_of((count, sub + 8, 128), bf16),
        in_specs=in_vmem(7),
        out_specs=in_vmem(1)[0],
        scratch_shapes=[
            pltpu.VMEM((channels, places // 2), bf16),
            pltpu.VMEM((channels, places // 2), bf16),
        ],
        compiler_params=LIMIT,
        cost_estimate=COST,
    )(spread, fine_acts, both, columns, fine_order, coarse_sums, kernel_fine)
    back = lax.all_to_all(sent, BACK_BLOCK, 0, 0)
    cells = nd * places
    fine_scale, coarse_scale = 1.0 / math.sqrt(4 * cells), 1.0 / math.sqrt(cells)
    out, sums = pl.pallas_call(
        functools.partial(spread_kernel, plan),
        out_shape=(pltpu.VMEM((4 * local, channels), bf16), shape_of((1, 8, channels), f32)),
        in_specs=in_vmem(3),
        out_specs=tuple(in_vmem(2)),
        compiler_params=LIMIT,
        cost_estimate=COST,
    )(back, acts, rows[2])
    both = lax.all_gather(sums, "dp", axis=0, tiled=True)
    out, sums = pl.pallas_call(
        functools.partial(total_kernel, (fine_scale, fine_scale, coarse_scale, coarse_scale)),
        out_shape=(pltpu.HBM((4 * local, channels), bf16), (pltpu.HBM((1, channels), f32),) * 4),
        in_specs=in_vmem(2),
        out_specs=(in_hbm(1)[0], tuple(in_hbm(4))),
        scratch_shapes=[pltpu.VMEM((4, 1, channels), f32), pltpu.SemaphoreType.DMA((5,))],
        compiler_params=LIMIT,
        cost_estimate=COST,
    )(both, out)
    bias_f, gain_f, bias_c, gain_c = [part.reshape(channels) for part in sums]
    return out.reshape(acts_fine.shape), gain_f, bias_f, gain_c, bias_c


def solution(mesh):
    def function(*arrays):
        local = [size // mesh.shape[axis] for size, axis in zip(arrays[1].shape, ("dp", "frames", "rows"))]
        sizes = (mesh.shape["frames"], mesh.shape["rows"])
        plan = Plan(sizes, (*local[1:], *arrays[1].shape[3:]), arrays[5].shape[1] // mesh.shape["rows"])
        if plan.fits:
            split = (mesh.shape["dp"], plan.nf // 2, 2, plan.nr)
            used = jax.sharding.Mesh(mesh.devices.reshape(split), ("dp", "pairs", "member", "rows"))
            shards, frames = functools.partial(fast_shards, plan), ("pairs", "member")
        else:
            used, shards, frames = mesh, plain_shards, "frames"
        blocks, kernel = P("dp", frames, "rows", None, None), P(None, "rows", None)
        in_specs = (blocks, blocks, blocks, P(), P(), kernel, P(), P(), kernel)
        out_specs = (blocks, P(), P(), P(), P())
        mapped = jax.shard_map(shards, mesh=used, in_specs=in_specs, out_specs=out_specs, check_vma=False)
        return mapped(*arrays)

    return function
```

```python
import functools
import math

import jax
import jax.numpy as jnp
from jax import lax
from jax.experimental import pallas as pl
from jax.experimental.pallas import tpu as pltpu
from jax.sharding import PartitionSpec as P

GROUPS = 32
EPSILON = 1e-06
BLOCK = ("rows", "pairs", "member")
BACK_BLOCK = ("pairs", "member", "rows")
PLAIN_BLOCK = ("frames", "rows")


def plain_everyone(block, count):
    copies = jnp.broadcast_to(block[None], (count,) + block.shape)
    return lax.all_to_all(copies, PLAIN_BLOCK, 0, 0)


def ahead(field, axis, distance):
    size = field.shape[axis]
    if distance == 0:
        return field
    widths = [(0, 0)] * field.ndim
    if distance > 0:
        widths[axis] = (0, distance)
        kept = lax.slice_in_dim(field, distance, size, axis=axis)
    else:
        widths[axis] = (-distance, 0)
        kept = lax.slice_in_dim(field, 0, size + distance, axis=axis)
    return jnp.pad(kept, widths)


def tap_products(source, kernel):
    sub = kernel.shape[1]
    frames, rows, cols, channels = source.shape
    products = lax.dot_general(
        kernel.reshape(27 * sub, channels),
        source.reshape(frames * rows * cols, channels),
        (((1,), (1,)), ((), ())),
        preferred_element_type=jnp.float32,
    ).reshape(3, 3, 3, sub, frames, rows, cols)
    return sum(ahead(products[depth], 3, 2 - depth) for depth in range(3))


def coarse_conv(source, kernel):
    spatial = tap_products(source, kernel)
    total = 0.0
    for row in range(3):
        part = sum(ahead(spatial[row, col], 3, 1 - col) for col in range(3))
        total = total + ahead(part, 2, 1 - row)
    return total


def fine_conv(source, kernel):
    spatial = tap_products(source, kernel)
    result = []
    for p in range(2):
        rows_of = []
        for q in range(2):
            total = 0.0
            for row in range(3):
                part = sum(ahead(spatial[row, col], 3, (q + 1 - col) // 2) for col in range(3))
                total = total + ahead(part, 2, (p + 1 - row) // 2)
            rows_of.append(total)
        result.append(jnp.stack(rows_of, 1))
    return jnp.stack(result, 1)


def group_total(sums, group_width):
    sub = sums.shape[-1]
    if sub % group_width == 0:
        grouped = jnp.sum(sums.reshape(-1, sub // group_width, group_width), axis=-1)
        return jnp.repeat(grouped, group_width, axis=-1)
    spread = jnp.moveaxis(lax.all_gather(sums, "frames"), 0, 1).reshape(sums.shape[0], -1, group_width)
    mine = lax.axis_index("frames") * sub // group_width
    grouped = lax.dynamic_index_in_dim(jnp.sum(spread, -1), mine, 1)
    return jnp.broadcast_to(grouped, sums.shape)


def level(acts, conv_grad, cotangent, gain, bias, group_width):
    sub = acts.shape[0]
    places = acts.size // sub
    values = acts.astype(jnp.float32).reshape(sub, places)
    conv_grad = conv_grad.reshape(sub, places)
    entries = places * group_width
    moments = group_total(
        jnp.stack([jnp.sum(values, 1), jnp.sum(values * values, 1)]), group_width
    ) / entries
    mean = moments[0]
    inv_std = lax.rsqrt(moments[1] - mean * mean + EPSILON)
    normed = (values - mean[:, None]) * inv_std[:, None]
    preact = gain[:, None] * normed + bias[:, None]
    squash = jax.nn.sigmoid(preact)
    pre_grad = conv_grad * squash * (1.0 + preact * (1.0 - squash))
    sums = jnp.stack([jnp.sum(pre_grad, 1), jnp.sum(pre_grad * normed, 1)])
    terms = group_total(sums * gain, group_width) / entries
    grad = cotangent.reshape(sub, places) + inv_std[:, None] * (
        gain[:, None] * pre_grad - terms[0][:, None] - normed * terms[1][:, None]
    )
    return grad, sums


def plain_shards(
    acts_fine,
    acts_coarse,
    grad_coarse,
    gain_fine,
    bias_fine,
    kernel_fine,
    gain_coarse,
    bias_coarse,
    kernel_coarse,
):
    nf, nr, nd = lax.axis_size("frames"), lax.axis_size("rows"), lax.axis_size("dp")
    count = nf * nr
    channels = acts_fine.shape[-1]
    slice_width = kernel_fine.shape[1]
    sub = slice_width // nf
    group_width = channels // GROUPS
    tl, hl, w = acts_coarse.shape[1:4]
    frames, rows = tl * nf, hl * nr
    f, r = lax.axis_index("frames"), lax.axis_index("rows")

    gathered = plain_everyone(grad_coarse[0], count)
    source = (
        gathered.reshape(nf, nr, tl, hl, w, channels)
        .transpose(0, 2, 1, 3, 4, 5)
        .reshape(frames, rows, w, channels)
    )
    coarse_in = acts_coarse[0].reshape(tl, hl, w, nr, nf, sub).transpose(4, 3, 5, 0, 1, 2)
    coarse_in = lax.all_to_all(coarse_in.reshape(count, sub, tl * hl * w), PLAIN_BLOCK, 0, 0)
    fine_in = acts_fine[0].reshape(tl, hl, 2, w, 2, nr, nf, sub).transpose(6, 5, 7, 2, 4, 0, 1, 3)
    fine_in = lax.all_to_all(fine_in.reshape(count, sub, 4 * tl * hl * w), PLAIN_BLOCK, 0, 0)

    def mine(vector):
        return lax.dynamic_slice_in_dim(vector, r * slice_width + f * sub, sub)

    def own(kernel):
        return lax.dynamic_slice_in_dim(kernel, f * sub, sub, axis=1)

    coarse_vals = (
        coarse_in.reshape(nf, nr, sub, tl, hl, w).transpose(2, 0, 3, 1, 4, 5).reshape(sub, frames, rows, w)
    )
    cot = lax.dynamic_slice_in_dim(source, r * slice_width + f * sub, sub, axis=3)
    cot = cot.astype(jnp.float32).transpose(3, 0, 1, 2)
    conv = coarse_conv(source, own(kernel_coarse))
    coarse_grad, coarse_sums = level(
        coarse_vals, conv, cot, mine(gain_coarse), mine(bias_coarse), group_width
    )
    quartered = (coarse_grad * 0.25).astype(jnp.bfloat16)
    spread = plain_everyone(quartered, count)
    source_fine = (
        spread.reshape(nf, nr, sub, frames, rows, w)
        .transpose(3, 4, 5, 1, 0, 2)
        .reshape(frames, rows, w, channels)
    )
    conv = fine_conv(source_fine, own(kernel_fine))
    fine_vals = (
        fine_in.reshape(nf, nr, sub, 2, 2, tl, hl, w)
        .transpose(2, 3, 4, 0, 5, 1, 6, 7)
        .reshape(sub, 2, 2, frames, rows, w)
    )
    cot = jnp.broadcast_to(
        quartered.astype(jnp.float32).reshape(sub, 1, 1, frames, rows, w), conv.shape
    )
    fine_grad, fine_sums = level(
        fine_vals, conv, cot, mine(gain_fine), mine(bias_fine), group_width
    )
    back = (
        fine_grad.astype(jnp.bfloat16)
        .reshape(sub, 2, 2, nf, tl, nr, hl, w)
        .transpose(3, 5, 0, 1, 2, 4, 6, 7)
        .reshape(count, sub, 4 * tl * hl * w)
    )
    sums = plain_everyone(jnp.concatenate([fine_sums, coarse_sums]), count)
    back = lax.all_to_all(back, PLAIN_BLOCK, 0, 0)
    out = (
        back.reshape(nf, nr, sub, 2, 2, tl, hl, w)
        .transpose(5, 6, 3, 7, 4, 1, 0, 2)
        .reshape(1, tl, 2 * hl, 2 * w, channels)
    )
    sums = sums.reshape(nf, nr, 4, sub).transpose(2, 1, 0, 3).reshape(4, channels)
    totals = lax.psum(sums, "dp")
    cells = nd * frames * rows * w
    scale_fine = 1.0 / jnp.sqrt(jnp.float32(4 * cells))
    scale_coarse = 1.0 / jnp.sqrt(jnp.float32(cells))
    return (
        out,
        totals[1] * scale_fine,
        totals[0] * scale_fine,
        totals[3] * scale_coarse,
        totals[2] * scale_coarse,
    )


def lanes_at(shape, axis):
    return lax.broadcasted_iota(jnp.int32, shape, axis)


def one_hot(found):
    return found.astype(jnp.float32).astype(jnp.bfloat16)


def pixel_order(plan, swapped):
    tl, hl, w = plan.tl, plan.hl, plan.w // 2
    size = 4 * plan.local
    lane = lanes_at((1, size), 1)
    j, i, t = lane % w, lane // w % hl, lane // (w * hl) % tl
    q, p = lane // (w * hl * tl) % 2, lane // (2 * w * hl * tl) % 2
    half = lane // (4 * w * hl * tl)
    if swapped:
        half = 1 - half
    pixel = (t * 2 * hl + 2 * i + p) * 4 * w + 2 * (half * w + j) + q
    return one_hot(lanes_at((size, size), 0) == pixel)


def merged_order(nr, outer, tl, cells):
    size = nr * outer * tl * cells
    lane = lanes_at((1, size), 1)
    cell, dev = lane % cells, lane // cells % nr
    t, o = lane // (cells * nr) % tl, lane // (cells * nr * tl)
    return one_hot(lanes_at((size, size), 0) == ((dev * outer + o) * tl + t) * cells + cell)


def column_order(plan):
    w = plan.w // 2
    lines = plan.places // plan.w
    lane = lanes_at((1, 4 * lines * w + 4 * lines), 1)
    inner = lane % (lines * w)
    place = inner // w * plan.w + lane // (lines * w) * w + inner % w
    past = lane - 2 * lines * w
    border = past % lines * plan.w + jnp.where(past < 2 * lines, w, w - 1)
    wanted = jnp.where(past >= 0, border, place)
    shape = (plan.places, 2 * lines * w + 4 * lines)
    return one_hot(lanes_at(shape, 0) == wanted[:, : shape[1]])


def one_hot_dot(a, b, dims):
    return lax.dot_general(a, b, (dims, ((), ())), preferred_element_type=jnp.float32)


def moved(field, distance, kept):
    size = field.shape[1]
    return jnp.where(kept, pltpu.roll(field, (-distance) % size, 1), 0.0)


def own_column(row, base, sub):
    shape = (sub, row.shape[1])
    mine = lanes_at(shape, 1) == lanes_at(shape, 0) + base
    return jnp.sum(jnp.where(mine, row, 0.0), axis=1, keepdims=True)


def as_row(column):
    shape = (column.shape[0], 128)
    here = lanes_at(shape, 1) == lanes_at(shape, 0)
    return jnp.sum(jnp.where(here, column, 0.0), axis=0, keepdims=True)


def terms(value, count):
    found = []
    for _ in range(count):
        found.append(value.astype(jnp.bfloat16).astype(jnp.float32))
        value = value - found[-1]
    return found


def in_groups(column, group_width):
    sub = column.shape[0]
    grouped = jnp.sum(column.reshape(sub // group_width, group_width, 1), axis=1, keepdims=True)
    return jnp.broadcast_to(grouped, (sub // group_width, group_width, 1)).reshape(sub, 1)


def in_lane_groups(row, group_width):
    lane = lanes_at(row.shape, 1)
    size = row.shape[1]
    step = 1
    while step < group_width:
        up, down = pltpu.roll(row, size - step, 1), pltpu.roll(row, step, 1)
        row = row + jnp.where(lane // step % 2 == 0, up, down)
        step *= 2
    return row


def total(parts):
    return sum(jnp.sum(part, axis=1, keepdims=True) for part in parts)


def statistics(one, two, entries, group_width):
    mean = in_groups(one, group_width) / entries
    square = in_groups(two, group_width) / entries
    return mean, lax.rsqrt(square - mean * mean + EPSILON)


def normalised(parts, gain, bias, mean, inv_std):
    normed, slope = [], []
    for part in parts:
        unit = (part - mean) * inv_std
        preact = gain * unit + bias
        squash = 0.5 + 0.5 * jnp.tanh(0.5 * preact)
        normed.append(unit)
        slope.append(squash * (1.0 + preact * (1.0 - squash)))
    return normed, slope


class Plan:
    def __init__(self, mesh_sizes, acts_coarse, slice_width):
        self.nf, self.nr = mesh_sizes
        self.count = self.nf * self.nr
        self.tl, self.hl, self.w, self.channels = acts_coarse
        self.slice_width = slice_width
        self.sub = slice_width // self.nf
        self.cells = self.hl * self.w
        self.local = self.tl * self.cells
        self.image = self.cells * self.nr
        self.frames = self.tl * self.nf
        self.places = self.frames * self.image
        self.group_width = self.channels // GROUPS
        self.chunks = self.channels // 128
        self.acts_at = self.chunks // 2 * self.local
        self.packed_at = self.acts_at + self.sub
        self.cot_at = self.packed_at + 8
        self.block_rows = self.cot_at + 8
        self.fits = (
            self.sub == 32
            and self.slice_width == 128
            and self.group_width == 16
            and self.cells == 16
            and self.w == 8
            and self.tl == 2
            and self.nr == 4
            and self.nf == 4
            and self.slice_width * self.nr == self.channels
        )

    def place_masks(self, w):
        lane = lanes_at((1, self.places // self.w * w), 1)
        col, row = lane % w, lane // w % (self.hl * self.nr)
        last_row = self.hl * self.nr - 1
        return (lane, col > 0, col < w - 1, row > 0, row < last_row)


def fetched(pairs, sems):
    copies = [pltpu.make_async_copy(src, dst, sems.at[k]) for k, (src, dst) in enumerate(pairs)]
    for copy in copies:
        copy.start()
    return copies


def own_place(plan):
    pair, member, r = lax.axis_index("pairs"), lax.axis_index("member"), lax.axis_index("rows")
    return pair, member, r, r * plan.slice_width + (2 * pair + member) * plan.sub


def fetch_kernel(g_hbm, coarse_hbm, fine_hbm, g_ref, coarse_ref, fine_ref, sems):
    for copy in fetched([(fine_hbm, fine_ref), (coarse_hbm, coarse_ref), (g_hbm, g_ref)], sems):
        copy.wait()


def pack_kernel(plan, g_ref, coarse_ref, fine_ref, out_ref):
    sub, chunks, local = plan.sub, plan.chunks, plan.local
    shape = (2 * local, 2 * 128)
    lane = lanes_at((1, 2 * 128), 1)
    repeated = one_hot(lanes_at(shape, 0) == lane % local + lane // 128 * local)
    shape = (plan.channels, 128)
    quarter = lanes_at(shape, 0) // 8 % 4 == lanes_at(shape, 1) // local
    orders = jnp.concatenate([pixel_order(plan, swapped) for swapped in (False, True)], axis=1)
    acts = fine_ref[...]
    halves = one_hot_dot(acts, orders, ((0,), (0,))).astype(jnp.bfloat16)
    halves = [halves[:, :128], halves[:, 128:]]
    small = one_hot_dot(jnp.concatenate([coarse_ref[...], g_ref[...]], axis=0), repeated, ((0,), (0,)))
    for k, at in enumerate((plan.packed_at, plan.cot_at)):
        rows_of = jnp.where(quarter, small[:, k * 128 : (k + 1) * 128], 0.0).reshape(plan.count, 4, 8, 128)
        out_ref[:, at : at + 8, :] = jnp.sum(rows_of, axis=1).astype(jnp.bfloat16)
    low = lanes_at((sub, 128), 1) < 64
    for s_r in range(plan.nr):
        for s_f in range(plan.nf):
            dest = s_r * plan.nf + s_f
            first, half = s_r * plan.slice_width + s_f // 2 * 2 * sub, s_f % 2
            for k in range(chunks // 2):
                at = (half * chunks // 2 + k) * 128
                out_ref[dest, k * local : (k + 1) * local, :] = g_ref[:, at : at + 128]
            upper, lower = halves[half][first : first + sub], halves[1 - half][first + sub : first + 2 * sub]
            out_ref[dest, plan.acts_at : plan.packed_at, :] = jnp.where(low, upper, lower)


def by_frame_device(plan, got_ref, at, height):
    return jnp.concatenate(
        [
            jnp.concatenate(
                [got_ref[r * plan.nf + f, at : at + height, :] for r in range(plan.nr)], axis=1
            )
            for f in range(plan.nf)
        ],
        axis=0,
    )


def in_places(plan, merged, height):
    width = plan.tl * plan.image
    return [
        jnp.concatenate(
            [merged[f * height : (f + 1) * height, k * width : (k + 1) * width] for f in range(plan.nf)],
            axis=1,
        )
        for k in range(4)
    ]


def coarse_kernel(
    plan,
    got_ref,
    weights,
    gain_c,
    bias_c,
    gain_f,
    bias_f,
    mine_ref,
    sent_ref,
    held_ref,
    inv_ref,
    fine_ref,
    columns,
    fine_order,
    by_column,
    order,
    source,
    conv_ref,
):
    sub, nr, nf, cells, tl, local = plan.sub, plan.nr, plan.nf, plan.cells, plan.tl, plan.local
    wide, depth = 2 * sub, plan.channels // 2
    pair, member, r, base = own_place(plan)
    first = r * plan.slice_width + pair * wide
    columns[0, 0:sub, :] = jnp.broadcast_to(own_column(gain_c[...], base, sub), (sub, 128))
    columns[1, 0:sub, :] = jnp.broadcast_to(own_column(bias_c[...], base, sub), (sub, 128))
    columns[2] = jnp.broadcast_to(own_column(gain_f[...], first, wide), (wide, 128))
    columns[3] = jnp.broadcast_to(own_column(bias_f[...], first, wide), (wide, 128))
    order[...] = merged_order(plan.nr, 4, plan.tl, plan.cells)
    fine_order[...] = merged_order(plan.nr, 8, plan.tl, plan.cells // 2)
    by_column[...] = column_order(plan)
    both = pl.ds(pl.multiple_of(pair * wide, wide), wide)
    half = pl.ds(pl.multiple_of(member * depth, depth), depth)
    for s_f in range(nf):
        for s_r in range(nr):
            for t in range(tl):
                at = (s_f * tl + t) * plan.image + s_r * cells
                for k in range(plan.chunks // 2):
                    source[at : at + cells, k * 128 : (k + 1) * 128] = got_ref[
                        s_r * nf + s_f, k * local + t * cells : k * local + (t + 1) * cells, :
                    ]
    source[plan.places :, :] = jnp.zeros((2 * plan.image, depth), jnp.bfloat16)
    products = sum(
        one_hot_dot(
            weights[9 * k : 9 * k + 9, both, half].reshape(9 * wide, depth),
            source[(2 - k) * plan.image : (2 - k) * plan.image + plan.places, :],
            ((1,), (1,)),
        )
        for k in range(3)
    )
    merged = one_hot_dot(by_frame_device(plan, got_ref, plan.acts_at, sub), fine_order[...], ((1,), (0,)))
    parts = halves_at(plan, merged)
    for pq in range(4):
        fine_ref[pq] = parts[pq]
    one, two = total(parts), total([part * part for part in parts])
    stats = terms(as_row(one) + pltpu.roll(as_row(two), 64, 1), 3)
    stats = jnp.concatenate(stats + [jnp.zeros_like(stats[0])] * 5, axis=0).astype(jnp.bfloat16)
    small = [by_frame_device(plan, got_ref, at, 8) for at in (plan.packed_at, plan.cot_at)]
    merged = one_hot_dot(jnp.concatenate(small, axis=0), order[...], ((1,), (0,)))
    rows_of = 8 * nf
    values, cot = [
        jnp.concatenate(in_places(plan, merged[k * rows_of : (k + 1) * rows_of], 8), axis=0) for k in range(2)
    ]
    gain, bias = columns[0][0:sub, 0:1], columns[1][0:sub, 0:1]
    entries = plan.places * plan.group_width
    mean, inv_std = statistics(total([values]), total([values * values]), entries, plan.group_width)
    (normed,), (slope,) = normalised([values], gain, bias, mean, inv_std)
    held_ref[0], held_ref[1], held_ref[2] = normed, slope, cot
    inv_ref[...] = jnp.broadcast_to(inv_std, (sub, 128))
    lane, has_left, has_right, has_up, has_down = plan.place_masks(plan.w)
    by_col = []
    for col in range(3):
        parts = [products[(3 * row + col) * wide : (3 * row + col + 1) * wide] for row in range(3)]
        by_col.append(parts[1] + moved(parts[0], plan.w, has_down) + moved(parts[2], -plan.w, has_up))
    conv_ref[...] = by_col[1] + moved(by_col[0], 1, has_right) + moved(by_col[2], -1, has_left)
    mine_ref[...] = conv_ref[pl.ds(pl.multiple_of(member * sub, sub), sub), :]
    for k in range(2):
        sent_ref[k, 0:sub, :] = conv_ref[k * sub : (k + 1) * sub, :].astype(jnp.bfloat16)
        sent_ref[k, sub:, 0:128] = stats
        sent_ref[k, sub:, 128:] = jnp.zeros((8, plan.places - 128), jnp.bfloat16)


def quarter_kernel(plan, mine_ref, both_ref, held_ref, inv_ref, columns, by_column, out_ref, sums_ref):
    sub = plan.sub
    _, member, _, _ = own_place(plan)
    conv = mine_ref[...] + both_ref[1 - member, 0:sub, :].astype(jnp.float32)
    normed, slope, cot = held_ref[0], held_ref[1], held_ref[2]
    gain, inv_std = columns[0][0:sub, 0:1], inv_ref[:, 0:1]
    entries = plan.places * plan.group_width
    pre = conv * slope
    one, two = total([pre]), total([pre * normed])
    group_one = in_groups(gain * one, plan.group_width) / entries
    group_two = in_groups(gain * two, plan.group_width) / entries
    grad = cot + inv_std * (gain * pre - group_one - normed * group_two)
    quartered = (grad * 0.25).astype(jnp.bfloat16)
    sent = one_hot_dot(quartered, by_column[...], ((1,), (0,))).astype(jnp.bfloat16)
    low = lanes_at((sub // 2, 128), 1) < 64
    for half in range(2):
        at = half * 256
        border = sent[:, 512 + half * 128 : 640 + half * 128]
        border = jnp.where(low, border[: sub // 2], border[sub // 2 :])
        for dest in range(half, plan.count, 2):
            out_ref[dest, 0:sub, :] = sent[:, at : at + 128]
            out_ref[dest, sub : 2 * sub, :] = sent[:, at + 128 : at + 256]
            out_ref[dest, 2 * sub : 2 * sub + sub // 2, :] = border
    sums_ref[...] = jnp.concatenate([as_row(one), as_row(two)], axis=0)


def halves_at(plan, merged):
    sub = plan.sub
    turned = jnp.concatenate([pltpu.roll(merged[:, k * 128 : (k + 1) * 128], 64, 1) for k in range(4)], axis=1)
    low = lanes_at((sub, 128), 1) < 64
    parts = []
    for pq in range(4):
        groups = []
        for group in range(2):
            e = 4 * group + pq
            at = e // 2 * 128
            strips = []
            for m in range(plan.nf // 2):
                first, second = slice(2 * m * sub, (2 * m + 1) * sub), slice((2 * m + 1) * sub, (2 * m + 2) * sub)
                if e % 2 == 0:
                    strips.append(jnp.where(low, merged[first, at : at + 128], turned[second, at : at + 128]))
                else:
                    strips.append(jnp.where(low, turned[first, at : at + 128], merged[second, at : at + 128]))
            groups.append(jnp.concatenate(strips, axis=1))
        parts.append(jnp.concatenate(groups, axis=0))
    return parts


def halves_from(plan, parts):
    sub = plan.sub
    low = lanes_at((sub, 128), 1) < 64
    down = []
    for f in range(plan.nf):
        across = []
        for v in range(4):
            pair = []
            for e in (2 * v, 2 * v + 1):
                group, pq = e // 4, e % 4
                strip = parts[pq][group * sub : (group + 1) * sub, f // 2 * 128 : (f // 2 + 1) * 128]
                pair.append(strip if e % 2 == f % 2 else pltpu.roll(strip, 64, 1))
            across.append(jnp.where(low, pair[0], pair[1]))
        down.append(jnp.concatenate(across, axis=1))
    return jnp.concatenate(down, axis=0)


def fine_kernel(
    plan, got_ref, acts_ref, both_ref, columns, order, sums_ref, weights, out_ref, source, border
):
    sub, nr, nf, wide = plan.sub, plan.nr, plan.nf, 2 * plan.sub
    pair, member, r, _ = own_place(plan)
    both = pl.ds(pl.multiple_of(pair * wide, wide), wide)
    w = plan.w // 2
    lines = plan.places // plan.w
    places = lines * w
    for k in range(2):
        source[:, k * 128 : (k + 1) * 128] = got_ref[:, k * sub : (k + 1) * sub, :].reshape(plan.channels, 128)
    packed = got_ref[:, wide : wide + sub // 2, :].reshape(plan.count * sub // 2, 128)
    shape = (128, places)
    beside = lanes_at(shape, 1) == lanes_at(shape, 0) % lines * w + (1 - member) * (w - 1)
    for k in range(2):
        here = one_hot(beside & (lanes_at(shape, 0) // lines == k))
        found = one_hot_dot(packed, here, ((1,), (0,))).astype(jnp.bfloat16)
        for s in range(plan.count):
            border[s * sub + k * (sub // 2) : s * sub + (k + 1) * (sub // 2), :] = found[
                s * (sub // 2) : (s + 1) * (sub // 2)
            ]
    image = plan.image // 2
    sums, extras = 0.0, 0.0
    for k in (2, 1, 0):
        here, beside = source[...], border[...]
        if k < 2:
            shift = (2 - k) * image
            inside = lanes_at((1, places), 1) < places - shift
            here, beside = [
                jnp.where(inside, pltpu.roll(part, places - shift, 1), jnp.zeros_like(part)) for part in (here, beside)
            ]
        sums = sums + one_hot_dot(
            weights[9 * k : 9 * k + 9, both, :].reshape(9 * wide, plan.channels), here, ((1,), (0,))
        )
        facing = jnp.concatenate([weights[9 * k + 3 * row + 2 * member, both, :] for row in range(3)], axis=0)
        extras = extras + one_hot_dot(facing, beside, ((1,), (0,)))
    parts = [acts_ref[pq] for pq in range(4)]
    stats = sum(both_ref[k, sub : sub + 8, 0:128].astype(jnp.float32) for k in range(2))
    stats = stats[0:1] + stats[1:2] + stats[2:3]
    entries = 4 * plan.places * plan.group_width
    one, two = own_column(stats, 0, wide), own_column(stats, 64, wide)
    mean, inv_std = statistics(one, two, entries, plan.group_width)
    gain, bias = columns[2][:, 0:1], columns[3][:, 0:1]
    normed, slope = normalised(parts, gain, bias, mean, inv_std)
    lane, has_left, has_right, has_up, has_down = plan.place_masks(w)
    right, left = (1 - member).astype(jnp.float32), member.astype(jnp.float32)
    by_row = []
    for row in range(3):
        a, b, c = [sums[(3 * row + col) * wide : (3 * row + col + 1) * wide] for col in range(3)]
        extra = extras[row * wide : (row + 1) * wide]
        by_row.append(
            (a + b + moved(c, -1, has_left) + left * extra, moved(a, 1, has_right) + b + c + right * extra)
        )
    convs = [by_row[0][q] + by_row[1][q] + moved(by_row[2][q], -w, has_up) for q in range(2)]
    convs += [moved(by_row[0][q], w, has_down) + by_row[1][q] + by_row[2][q] for q in range(2)]
    pre = [conv * part for conv, part in zip(convs, slope)]
    one = total(pre)
    two = total([a * b for a, b in zip(pre, normed)])
    cot = source[pl.ds(pl.multiple_of(r * plan.slice_width + pair * wide, wide), wide), :].astype(jnp.float32)
    scale = inv_std * gain
    stacked = halves_from(plan, [cot + scale * part for part in pre]).astype(jnp.bfloat16)
    sent = one_hot_dot(stacked, order[...], ((1,), (1,))).astype(jnp.bfloat16)
    coarse = sums_ref[0:1] + pltpu.roll(sums_ref[1:2], sub, 1)
    coded = (
        terms(as_row(one) + pltpu.roll(as_row(two), 64, 1), 2)
        + terms(coarse, 2)
        + terms(as_row(inv_std) + pltpu.roll(as_row(mean), 64, 1), 3)
    )
    coded = jnp.concatenate(coded + [jnp.zeros_like(coarse)], axis=0).astype(jnp.bfloat16)
    for s_r in range(nr):
        for s_f in range(nf):
            out_ref[s_f * nr + s_r, 0:sub, :] = sent[s_f * sub : (s_f + 1) * sub, s_r * 128 : (s_r + 1) * 128]
            out_ref[s_f * nr + s_r, sub : sub + 8, :] = coded


def spread_kernel(plan, got_ref, acts_ref, gain_ref, out_ref, sums_ref):
    sub, nr, nf = plan.sub, plan.nr, plan.nf
    low = lanes_at((sub, 128), 1) < 64
    low_row = lanes_at((1, 128), 1) < 64
    first_row = lanes_at((1, 128), 1) < sub
    source = []
    fine, coarse, moments = [[], []], [[], []], [[], []]
    for s_r in range(nr):
        ones, twos, c_ones, c_twos, invs, means = [], [], 0.0, 0.0, [], []
        for pair in range(nf // 2):
            at = 2 * pair * nr + s_r
            left, right = [got_ref[at + k * nr, 0:sub, :].astype(jnp.float32) for k in range(2)]
            source.append(jnp.where(low, left, pltpu.roll(right, 64, 1)))
            source.append(jnp.where(low, pltpu.roll(left, 64, 1), right))
            coded = [got_ref[at + k * nr, sub : sub + 8, :].astype(jnp.float32) for k in range(2)]
            sums = coded[0][0:1] + coded[0][1:2] + coded[1][0:1] + coded[1][1:2]
            ones.append(sums if pair == 0 else pltpu.roll(sums, 64, 1))
            twos.append(pltpu.roll(sums, 64, 1) if pair == 0 else sums)
            both = coded[0][4:5] + coded[0][5:6] + coded[0][6:7]
            invs.append(both if pair == 0 else pltpu.roll(both, 64, 1))
            means.append(pltpu.roll(both, 64, 1) if pair == 0 else both)
            for k in range(2):
                sums = coded[k][2:3] + coded[k][3:4]
                to = (2 * pair + k) * sub
                c_one = jnp.where(first_row, sums, 0.0)
                c_two = jnp.where(first_row, pltpu.roll(sums, 128 - sub, 1), 0.0)
                c_ones = c_ones + (pltpu.roll(c_one, to, 1) if to else c_one)
                c_twos = c_twos + (pltpu.roll(c_two, to, 1) if to else c_two)
        fine[0].append(jnp.where(low_row, ones[0], ones[1]))
        fine[1].append(jnp.where(low_row, twos[0], twos[1]))
        moments[0].append(jnp.where(low_row, invs[0], invs[1]))
        moments[1].append(jnp.where(low_row, means[0], means[1]))
        coarse[0].append(c_ones)
        coarse[1].append(c_twos)
    one, two, inv_std, mean, c_one, c_two = [jnp.concatenate(part, axis=1) for part in fine + moments + coarse]
    source = jnp.concatenate(source, axis=0).astype(jnp.bfloat16)
    result = one_hot_dot(pixel_order(plan, False), source, ((1,), (1,)))
    gain = gain_ref[...]
    entries = 4 * plan.places * plan.group_width
    group_one = in_lane_groups(gain * one, plan.group_width) / entries
    group_two = in_lane_groups(gain * two, plan.group_width) / entries
    normed = (acts_ref[...].astype(jnp.float32) - mean) * inv_std
    out_ref[...] = (result - inv_std * (group_one + normed * group_two)).astype(jnp.bfloat16)
    sums_ref[...] = jnp.concatenate([one, two, c_one, c_two] + [jnp.zeros_like(one)] * 4, axis=0)


def total_kernel(scales, both_ref, result_ref, result_hbm, out_hbms, rows_ref, sems):
    copies = fetched([(result_ref, result_hbm)], sems)
    rows = sum(both_ref[k] for k in range(both_ref.shape[0]))
    for k in range(4):
        rows_ref[k] = rows[k : k + 1] * scales[k]
    for k in range(4):
        copies.append(pltpu.make_async_copy(rows_ref.at[k], out_hbms[k], sems.at[k + 1]))
        copies[-1].start()
    for copy in copies:
        copy.wait()


def in_vmem(count):
    return [pl.BlockSpec(memory_space=pltpu.VMEM)] * count


def in_hbm(count):
    return [pl.BlockSpec(memory_space=pltpu.HBM)] * count


def kept(array):
    return pltpu.with_memory_space_constraint(array, pltpu.HBM)


def shape_of(shape, kind):
    return jax.ShapeDtypeStruct(shape, kind)


LIMIT = pltpu.CompilerParams(vmem_limit_bytes=40 * 1024 * 1024)
COST = pl.CostEstimate(flops=2_000_000_000, bytes_accessed=4_000_000, transcendentals=0)


def fast_shards(
    plan,
    acts_fine,
    acts_coarse,
    grad_coarse,
    gain_fine,
    bias_fine,
    kernel_fine,
    gain_coarse,
    bias_coarse,
    kernel_coarse,
):
    nd = lax.axis_size("dp")
    count, sub, channels, places, local = plan.count, plan.sub, plan.channels, plan.places, plan.local
    f32, bf16 = jnp.float32, jnp.bfloat16
    rows = [part.reshape(1, channels) for part in (gain_coarse, bias_coarse, gain_fine, bias_fine)]
    places_of = ((local, channels), (local, channels), (4 * local, channels))
    fetched_of = pl.pallas_call(
        fetch_kernel,
        out_shape=tuple(pltpu.VMEM(shape, bf16) for shape in places_of),
        in_specs=in_hbm(3),
        out_specs=tuple(in_vmem(3)),
        scratch_shapes=[pltpu.SemaphoreType.DMA((3,))],
        compiler_params=LIMIT,
    )(*[kept(part.reshape(shape)) for part, shape in zip((grad_coarse, acts_coarse, acts_fine), places_of)])
    acts = fetched_of[2]
    packed = pl.pallas_call(
        functools.partial(pack_kernel, plan),
        out_shape=shape_of((count, plan.block_rows, 128), bf16),
        in_specs=in_vmem(3),
        out_specs=in_vmem(1)[0],
        compiler_params=LIMIT,
        cost_estimate=COST,
    )(*fetched_of)
    got = lax.all_to_all(packed, BLOCK, 0, 0)
    mine, theirs, held, inv_std, fine_acts, columns, fine_order, by_column = pl.pallas_call(
        functools.partial(coarse_kernel, plan),
        out_shape=(
            shape_of((sub, places), f32),
            shape_of((2, sub + 8, places), bf16),
            shape_of((3, sub, places), f32),
            shape_of((sub, 128), f32),
            shape_of((4, 2 * sub, places // 2), f32),
            shape_of((4, 2 * sub, 128), f32),
            shape_of((4 * plan.nr * local, 4 * plan.nr * local), bf16),
            shape_of((places, places + places // 2), bf16),
        ),
        in_specs=in_vmem(6),
        out_specs=tuple(in_vmem(8)),
        scratch_shapes=[
            pltpu.VMEM((4 * plan.nr * local, 4 * plan.nr * local), bf16),
            pltpu.VMEM((places + 2 * plan.image, channels // 2), bf16),
            pltpu.VMEM((2 * sub, places), f32),
        ],
        compiler_params=LIMIT,
        cost_estimate=COST,
    )(got, kernel_coarse, *rows)
    both = lax.all_to_all(theirs, "member", 0, 0)
    quartered, coarse_sums = pl.pallas_call(
        functools.partial(quarter_kernel, plan),
        out_shape=(shape_of((count, 2 * sub + sub // 2, 128), bf16), shape_of((2, 128), f32)),
        in_specs=in_vmem(6),
        out_specs=tuple(in_vmem(2)),
        compiler_params=LIMIT,
        cost_estimate=COST,
    )(mine, both, held, inv_std, columns, by_column)
    spread = lax.all_to_all(quartered, BLOCK, 0, 0)
    sent = pl.pallas_call(
        functools.partial(fine_kernel, plan),
        out_shape=shape_of((count, sub + 8, 128), bf16),
        in_specs=in_vmem(7),
        out_specs=in_vmem(1)[0],
        scratch_shapes=[
            pltpu.VMEM((channels, places // 2), bf16),
            pltpu.VMEM((channels, places // 2), bf16),
        ],
        compiler_params=LIMIT,
        cost_estimate=COST,
    )(spread, fine_acts, both, columns, fine_order, coarse_sums, kernel_fine)
    back = lax.all_to_all(sent, BACK_BLOCK, 0, 0)
    cells = nd * places
    fine_scale, coarse_scale = 1.0 / math.sqrt(4 * cells), 1.0 / math.sqrt(cells)
    out, sums = pl.pallas_call(
        functools.partial(spread_kernel, plan),
        out_shape=(pltpu.VMEM((4 * local, channels), bf16), shape_of((8, channels), f32)),
        in_specs=in_vmem(3),
        out_specs=tuple(in_vmem(2)),
        compiler_params=LIMIT,
        cost_estimate=COST,
    )(back, acts, rows[2])
    both = lax.all_gather(sums, "dp")
    out, sums = pl.pallas_call(
        functools.partial(total_kernel, (fine_scale, fine_scale, coarse_scale, coarse_scale)),
        out_shape=(pltpu.HBM((4 * local, channels), bf16), (pltpu.HBM((1, channels), f32),) * 4),
        in_specs=in_vmem(2),
        out_specs=(in_hbm(1)[0], tuple(in_hbm(4))),
        scratch_shapes=[pltpu.VMEM((4, 1, channels), f32), pltpu.SemaphoreType.DMA((5,))],
        compiler_params=LIMIT,
        cost_estimate=COST,
    )(both, out)
    bias_f, gain_f, bias_c, gain_c = [part.reshape(channels) for part in sums]
    return out.reshape(acts_fine.shape), gain_f, bias_f, gain_c, bias_c


def solution(mesh):
    def function(*arrays):
        local = [size // mesh.shape[axis] for size, axis in zip(arrays[1].shape, ("dp", "frames", "rows"))]
        sizes = (mesh.shape["frames"], mesh.shape["rows"])
        plan = Plan(sizes, (*local[1:], *arrays[1].shape[3:]), arrays[5].shape[1] // mesh.shape["rows"])
        if plan.fits:
            split = (mesh.shape["dp"], plan.nf // 2, 2, plan.nr)
            used = jax.sharding.Mesh(mesh.devices.reshape(split), ("dp", "pairs", "member", "rows"))
            shards, frames = functools.partial(fast_shards, plan), ("pairs", "member")
        else:
            used, shards, frames = mesh, plain_shards, "frames"
        blocks, kernel = P("dp", frames, "rows", None, None), P(None, "rows", None)
        in_specs = (blocks, blocks, blocks, P(), P(), kernel, P(), P(), kernel)
        out_specs = (blocks, P(), P(), P(), P())
        mapped = jax.shard_map(shards, mesh=used, in_specs=in_specs, out_specs=out_specs, check_vma=False)
        return mapped(*arrays)

    return function
```

```python
import functools
import math

import jax
import jax.numpy as jnp
from jax import lax
from jax.experimental import pallas as pl
from jax.experimental.pallas import tpu as pltpu
from jax.sharding import PartitionSpec as P

GROUPS = 32
EPSILON = 1e-06
BLOCK = ("rows", "pairs", "member")
BACK_BLOCK = ("pairs", "member", "rows")
PLAIN_BLOCK = ("frames", "rows")


def plain_everyone(block, count):
    copies = jnp.broadcast_to(block[None], (count,) + block.shape)
    return lax.all_to_all(copies, PLAIN_BLOCK, 0, 0)


def ahead(field, axis, distance):
    size = field.shape[axis]
    if distance == 0:
        return field
    widths = [(0, 0)] * field.ndim
    if distance > 0:
        widths[axis] = (0, distance)
        kept = lax.slice_in_dim(field, distance, size, axis=axis)
    else:
        widths[axis] = (-distance, 0)
        kept = lax.slice_in_dim(field, 0, size + distance, axis=axis)
    return jnp.pad(kept, widths)


def tap_products(source, kernel):
    sub = kernel.shape[1]
    frames, rows, cols, channels = source.shape
    products = lax.dot_general(
        kernel.reshape(27 * sub, channels),
        source.reshape(frames * rows * cols, channels),
        (((1,), (1,)), ((), ())),
        preferred_element_type=jnp.float32,
    ).reshape(3, 3, 3, sub, frames, rows, cols)
    return sum(ahead(products[depth], 3, 2 - depth) for depth in range(3))


def coarse_conv(source, kernel):
    spatial = tap_products(source, kernel)
    total = 0.0
    for row in range(3):
        part = sum(ahead(spatial[row, col], 3, 1 - col) for col in range(3))
        total = total + ahead(part, 2, 1 - row)
    return total


def fine_conv(source, kernel):
    spatial = tap_products(source, kernel)
    result = []
    for p in range(2):
        rows_of = []
        for q in range(2):
            total = 0.0
            for row in range(3):
                part = sum(ahead(spatial[row, col], 3, (q + 1 - col) // 2) for col in range(3))
                total = total + ahead(part, 2, (p + 1 - row) // 2)
            rows_of.append(total)
        result.append(jnp.stack(rows_of, 1))
    return jnp.stack(result, 1)


def group_total(sums, group_width):
    sub = sums.shape[-1]
    if sub % group_width == 0:
        grouped = jnp.sum(sums.reshape(-1, sub // group_width, group_width), axis=-1)
        return jnp.repeat(grouped, group_width, axis=-1)
    spread = jnp.moveaxis(lax.all_gather(sums, "frames"), 0, 1).reshape(sums.shape[0], -1, group_width)
    mine = lax.axis_index("frames") * sub // group_width
    grouped = lax.dynamic_index_in_dim(jnp.sum(spread, -1), mine, 1)
    return jnp.broadcast_to(grouped, sums.shape)


def level(acts, conv_grad, cotangent, gain, bias, group_width):
    sub = acts.shape[0]
    places = acts.size // sub
    values = acts.astype(jnp.float32).reshape(sub, places)
    conv_grad = conv_grad.reshape(sub, places)
    entries = places * group_width
    moments = group_total(
        jnp.stack([jnp.sum(values, 1), jnp.sum(values * values, 1)]), group_width
    ) / entries
    mean = moments[0]
    inv_std = lax.rsqrt(moments[1] - mean * mean + EPSILON)
    normed = (values - mean[:, None]) * inv_std[:, None]
    preact = gain[:, None] * normed + bias[:, None]
    squash = jax.nn.sigmoid(preact)
    pre_grad = conv_grad * squash * (1.0 + preact * (1.0 - squash))
    sums = jnp.stack([jnp.sum(pre_grad, 1), jnp.sum(pre_grad * normed, 1)])
    terms = group_total(sums * gain, group_width) / entries
    grad = cotangent.reshape(sub, places) + inv_std[:, None] * (
        gain[:, None] * pre_grad - terms[0][:, None] - normed * terms[1][:, None]
    )
    return grad, sums


def plain_shards(
    acts_fine,
    acts_coarse,
    grad_coarse,
    gain_fine,
    bias_fine,
    kernel_fine,
    gain_coarse,
    bias_coarse,
    kernel_coarse,
):
    nf, nr, nd = lax.axis_size("frames"), lax.axis_size("rows"), lax.axis_size("dp")
    count = nf * nr
    channels = acts_fine.shape[-1]
    slice_width = kernel_fine.shape[1]
    sub = slice_width // nf
    group_width = channels // GROUPS
    tl, hl, w = acts_coarse.shape[1:4]
    frames, rows = tl * nf, hl * nr
    f, r = lax.axis_index("frames"), lax.axis_index("rows")

    gathered = plain_everyone(grad_coarse[0], count)
    source = (
        gathered.reshape(nf, nr, tl, hl, w, channels)
        .transpose(0, 2, 1, 3, 4, 5)
        .reshape(frames, rows, w, channels)
    )
    coarse_in = acts_coarse[0].reshape(tl, hl, w, nr, nf, sub).transpose(4, 3, 5, 0, 1, 2)
    coarse_in = lax.all_to_all(coarse_in.reshape(count, sub, tl * hl * w), PLAIN_BLOCK, 0, 0)
    fine_in = acts_fine[0].reshape(tl, hl, 2, w, 2, nr, nf, sub).transpose(6, 5, 7, 2, 4, 0, 1, 3)
    fine_in = lax.all_to_all(fine_in.reshape(count, sub, 4 * tl * hl * w), PLAIN_BLOCK, 0, 0)

    def mine(vector):
        return lax.dynamic_slice_in_dim(vector, r * slice_width + f * sub, sub)

    def own(kernel):
        return lax.dynamic_slice_in_dim(kernel, f * sub, sub, axis=1)

    coarse_vals = (
        coarse_in.reshape(nf, nr, sub, tl, hl, w).transpose(2, 0, 3, 1, 4, 5).reshape(sub, frames, rows, w)
    )
    cot = lax.dynamic_slice_in_dim(source, r * slice_width + f * sub, sub, axis=3)
    cot = cot.astype(jnp.float32).transpose(3, 0, 1, 2)
    conv = coarse_conv(source, own(kernel_coarse))
    coarse_grad, coarse_sums = level(
        coarse_vals, conv, cot, mine(gain_coarse), mine(bias_coarse), group_width
    )
    quartered = (coarse_grad * 0.25).astype(jnp.bfloat16)
    spread = plain_everyone(quartered, count)
    source_fine = (
        spread.reshape(nf, nr, sub, frames, rows, w)
        .transpose(3, 4, 5, 1, 0, 2)
        .reshape(frames, rows, w, channels)
    )
    conv = fine_conv(source_fine, own(kernel_fine))
    fine_vals = (
        fine_in.reshape(nf, nr, sub, 2, 2, tl, hl, w)
        .transpose(2, 3, 4, 0, 5, 1, 6, 7)
        .reshape(sub, 2, 2, frames, rows, w)
    )
    cot = jnp.broadcast_to(
        quartered.astype(jnp.float32).reshape(sub, 1, 1, frames, rows, w), conv.shape
    )
    fine_grad, fine_sums = level(
        fine_vals, conv, cot, mine(gain_fine), mine(bias_fine), group_width
    )
    back = (
        fine_grad.astype(jnp.bfloat16)
        .reshape(sub, 2, 2, nf, tl, nr, hl, w)
        .transpose(3, 5, 0, 1, 2, 4, 6, 7)
        .reshape(count, sub, 4 * tl * hl * w)
    )
    sums = plain_everyone(jnp.concatenate([fine_sums, coarse_sums]), count)
    back = lax.all_to_all(back, PLAIN_BLOCK, 0, 0)
    out = (
        back.reshape(nf, nr, sub, 2, 2, tl, hl, w)
        .transpose(5, 6, 3, 7, 4, 1, 0, 2)
        .reshape(1, tl, 2 * hl, 2 * w, channels)
    )
    sums = sums.reshape(nf, nr, 4, sub).transpose(2, 1, 0, 3).reshape(4, channels)
    totals = lax.psum(sums, "dp")
    cells = nd * frames * rows * w
    scale_fine = 1.0 / jnp.sqrt(jnp.float32(4 * cells))
    scale_coarse = 1.0 / jnp.sqrt(jnp.float32(cells))
    return (
        out,
        totals[1] * scale_fine,
        totals[0] * scale_fine,
        totals[3] * scale_coarse,
        totals[2] * scale_coarse,
    )


def lanes_at(shape, axis):
    return lax.broadcasted_iota(jnp.int32, shape, axis)


def one_hot(found):
    return found.astype(jnp.float32).astype(jnp.bfloat16)


def pixel_order(plan, swapped):
    tl, hl, w = plan.tl, plan.hl, plan.w // 2
    size = 4 * plan.local
    lane = lanes_at((1, size), 1)
    j, i, t = lane % w, lane // w % hl, lane // (w * hl) % tl
    q, p = lane // (w * hl * tl) % 2, lane // (2 * w * hl * tl) % 2
    half = lane // (4 * w * hl * tl)
    if swapped:
        half = 1 - half
    pixel = (t * 2 * hl + 2 * i + p) * 4 * w + 2 * (half * w + j) + q
    return one_hot(lanes_at((size, size), 0) == pixel)


def merged_order(nr, outer, tl, cells):
    size = nr * outer * tl * cells
    lane = lanes_at((1, size), 1)
    cell, dev = lane % cells, lane // cells % nr
    t, o = lane // (cells * nr) % tl, lane // (cells * nr * tl)
    return one_hot(lanes_at((size, size), 0) == ((dev * outer + o) * tl + t) * cells + cell)


def column_order(plan):
    w = plan.w // 2
    lines = plan.places // plan.w
    lane = lanes_at((1, 4 * lines * w + 4 * lines), 1)
    inner = lane % (lines * w)
    place = inner // w * plan.w + lane // (lines * w) * w + inner % w
    past = lane - 2 * lines * w
    border = past % lines * plan.w + jnp.where(past < 2 * lines, w, w - 1)
    wanted = jnp.where(past >= 0, border, place)
    shape = (plan.places, 2 * lines * w + 4 * lines)
    return one_hot(lanes_at(shape, 0) == wanted[:, : shape[1]])


def one_hot_dot(a, b, dims):
    return lax.dot_general(a, b, (dims, ((), ())), preferred_element_type=jnp.float32)


def moved(field, distance, kept):
    size = field.shape[1]
    return jnp.where(kept, pltpu.roll(field, (-distance) % size, 1), 0.0)


def own_column(row, base, sub):
    shape = (sub, row.shape[1])
    mine = lanes_at(shape, 1) == lanes_at(shape, 0) + base
    return jnp.sum(jnp.where(mine, row, 0.0), axis=1, keepdims=True)


def as_row(column):
    shape = (column.shape[0], 128)
    here = lanes_at(shape, 1) == lanes_at(shape, 0)
    return jnp.sum(jnp.where(here, column, 0.0), axis=0, keepdims=True)


def terms(value, count):
    found = []
    for _ in range(count):
        found.append(value.astype(jnp.bfloat16).astype(jnp.float32))
        value = value - found[-1]
    return found


def in_groups(column, group_width):
    sub = column.shape[0]
    grouped = jnp.sum(column.reshape(sub // group_width, group_width, 1), axis=1, keepdims=True)
    return jnp.broadcast_to(grouped, (sub // group_width, group_width, 1)).reshape(sub, 1)


def in_lane_groups(row, group_width):
    lane = lanes_at(row.shape, 1)
    size = row.shape[1]
    step = 1
    while step < group_width:
        up, down = pltpu.roll(row, size - step, 1), pltpu.roll(row, step, 1)
        row = row + jnp.where(lane // step % 2 == 0, up, down)
        step *= 2
    return row


def total(parts):
    return sum(jnp.sum(part, axis=1, keepdims=True) for part in parts)


def statistics(one, two, entries, group_width):
    mean = in_groups(one, group_width) / entries
    square = in_groups(two, group_width) / entries
    return mean, lax.rsqrt(square - mean * mean + EPSILON)


def normalised(parts, gain, bias, mean, inv_std):
    normed, slope = [], []
    for part in parts:
        unit = (part - mean) * inv_std
        preact = gain * unit + bias
        squash = 0.5 + 0.5 * jnp.tanh(0.5 * preact)
        normed.append(unit)
        slope.append(squash * (1.0 + preact * (1.0 - squash)))
    return normed, slope


class Plan:
    def __init__(self, mesh_sizes, acts_coarse, slice_width):
        self.nf, self.nr = mesh_sizes
        self.count = self.nf * self.nr
        self.tl, self.hl, self.w, self.channels = acts_coarse
        self.slice_width = slice_width
        self.sub = slice_width // self.nf
        self.cells = self.hl * self.w
        self.local = self.tl * self.cells
        self.image = self.cells * self.nr
        self.frames = self.tl * self.nf
        self.places = self.frames * self.image
        self.group_width = self.channels // GROUPS
        self.chunks = self.channels // 128
        self.acts_at = self.chunks // 2 * self.local
        self.packed_at = self.acts_at + self.sub
        self.cot_at = self.packed_at + 8
        self.block_rows = self.cot_at + 8
        self.fits = (
            self.sub == 32
            and self.slice_width == 128
            and self.group_width == 16
            and self.cells == 16
            and self.w == 8
            and self.tl == 2
            and self.nr == 4
            and self.nf == 4
            and self.slice_width * self.nr == self.channels
        )

    def place_masks(self, w):
        lane = lanes_at((1, self.places // self.w * w), 1)
        col, row = lane % w, lane // w % (self.hl * self.nr)
        last_row = self.hl * self.nr - 1
        return (lane, col > 0, col < w - 1, row > 0, row < last_row)


def fetched(pairs, sems):
    copies = [pltpu.make_async_copy(src, dst, sems.at[k]) for k, (src, dst) in enumerate(pairs)]
    for copy in copies:
        copy.start()
    return copies


def own_place(plan):
    pair, member, r = lax.axis_index("pairs"), lax.axis_index("member"), lax.axis_index("rows")
    return pair, member, r, r * plan.slice_width + (2 * pair + member) * plan.sub


def fetch_kernel(g_hbm, coarse_hbm, fine_hbm, g_ref, coarse_ref, fine_ref, sems):
    for copy in fetched([(fine_hbm, fine_ref), (coarse_hbm, coarse_ref), (g_hbm, g_ref)], sems):
        copy.wait()


def pack_kernel(plan, g_ref, coarse_ref, fine_ref, out_ref):
    sub, chunks, local = plan.sub, plan.chunks, plan.local
    shape = (2 * local, 2 * 128)
    lane = lanes_at((1, 2 * 128), 1)
    repeated = one_hot(lanes_at(shape, 0) == lane % local + lane // 128 * local)
    shape = (plan.channels, 128)
    quarter = lanes_at(shape, 0) // 8 % 4 == lanes_at(shape, 1) // local
    orders = jnp.concatenate([pixel_order(plan, swapped) for swapped in (False, True)], axis=1)
    acts = fine_ref[...]
    halves = one_hot_dot(acts, orders, ((0,), (0,))).astype(jnp.bfloat16)
    halves = [halves[:, :128], halves[:, 128:]]
    small = one_hot_dot(jnp.concatenate([coarse_ref[...], g_ref[...]], axis=0), repeated, ((0,), (0,)))
    for k, at in enumerate((plan.packed_at, plan.cot_at)):
        rows_of = jnp.where(quarter, small[:, k * 128 : (k + 1) * 128], 0.0).reshape(plan.count, 4, 8, 128)
        rows_of = jnp.sum(rows_of, axis=1).astype(jnp.bfloat16)
        for c in range(plan.count):
            out_ref[c % plan.nf * plan.nr + c // plan.nf, at : at + 8, :] = rows_of[c]
    low = lanes_at((sub, 128), 1) < 64
    for s_r in range(plan.nr):
        for s_f in range(plan.nf):
            dest = s_f * plan.nr + s_r
            first, half = s_r * plan.slice_width + s_f // 2 * 2 * sub, s_f % 2
            for k in range(chunks // 2):
                at = (half * chunks // 2 + k) * 128
                out_ref[dest, k * local : (k + 1) * local, :] = g_ref[:, at : at + 128]
            upper, lower = halves[half][first : first + sub], halves[1 - half][first + sub : first + 2 * sub]
            out_ref[dest, plan.acts_at : plan.packed_at, :] = jnp.where(low, upper, lower)


def by_frame_device(plan, got_ref, at, height):
    return jnp.concatenate(
        [
            jnp.concatenate(
                [got_ref[f * plan.nr + r, at : at + height, :] for r in range(plan.nr)], axis=1
            )
            for f in range(plan.nf)
        ],
        axis=0,
    )


def in_places(plan, merged, height):
    width = plan.tl * plan.image
    return [
        jnp.concatenate(
            [merged[f * height : (f + 1) * height, k * width : (k + 1) * width] for f in range(plan.nf)],
            axis=1,
        )
        for k in range(4)
    ]


def coarse_kernel(
    plan,
    got_ref,
    weights,
    gain_c,
    bias_c,
    gain_f,
    bias_f,
    mine_ref,
    sent_ref,
    held_ref,
    inv_ref,
    fine_ref,
    columns,
    fine_order,
    by_column,
    order,
    source,
    conv_ref,
):
    sub, nr, nf, cells, tl, local = plan.sub, plan.nr, plan.nf, plan.cells, plan.tl, plan.local
    wide, depth = 2 * sub, plan.channels // 2
    pair, member, r, base = own_place(plan)
    first = r * plan.slice_width + pair * wide
    columns[0, 0:sub, :] = jnp.broadcast_to(own_column(gain_c[...], base, sub), (sub, 128))
    columns[1, 0:sub, :] = jnp.broadcast_to(own_column(bias_c[...], base, sub), (sub, 128))
    columns[2] = jnp.broadcast_to(own_column(gain_f[...], first, wide), (wide, 128))
    columns[3] = jnp.broadcast_to(own_column(bias_f[...], first, wide), (wide, 128))
    order[...] = merged_order(plan.nr, 4, plan.tl, plan.cells)
    fine_order[...] = merged_order(plan.nr, 8, plan.tl, plan.cells // 2)
    by_column[...] = column_order(plan)
    both = pl.ds(pl.multiple_of(pair * wide, wide), wide)
    half = pl.ds(pl.multiple_of(member * depth, depth), depth)
    for s_f in range(nf):
        for s_r in range(nr):
            for t in range(tl):
                at = (s_f * tl + t) * plan.image + s_r * cells
                for k in range(plan.chunks // 2):
                    source[at : at + cells, k * 128 : (k + 1) * 128] = got_ref[
                        s_f * nr + s_r, k * local + t * cells : k * local + (t + 1) * cells, :
                    ]
    source[plan.places :, :] = jnp.zeros((2 * plan.image, depth), jnp.bfloat16)
    products = sum(
        one_hot_dot(
            weights[9 * k : 9 * k + 9, both, half].reshape(9 * wide, depth),
            source[(2 - k) * plan.image : (2 - k) * plan.image + plan.places, :],
            ((1,), (1,)),
        )
        for k in range(3)
    )
    merged = one_hot_dot(by_frame_device(plan, got_ref, plan.acts_at, sub), fine_order[...], ((1,), (0,)))
    parts = halves_at(plan, merged)
    for pq in range(4):
        fine_ref[pq] = parts[pq]
    one, two = total(parts), total([part * part for part in parts])
    stats = terms(as_row(one) + pltpu.roll(as_row(two), 64, 1), 3)
    stats = jnp.concatenate(stats + [jnp.zeros_like(stats[0])] * 5, axis=0).astype(jnp.bfloat16)
    small = [by_frame_device(plan, got_ref, at, 8) for at in (plan.packed_at, plan.cot_at)]
    merged = one_hot_dot(jnp.concatenate(small, axis=0), order[...], ((1,), (0,)))
    rows_of = 8 * nf
    values, cot = [
        jnp.concatenate(in_places(plan, merged[k * rows_of : (k + 1) * rows_of], 8), axis=0) for k in range(2)
    ]
    gain, bias = columns[0][0:sub, 0:1], columns[1][0:sub, 0:1]
    entries = plan.places * plan.group_width
    mean, inv_std = statistics(total([values]), total([values * values]), entries, plan.group_width)
    (normed,), (slope,) = normalised([values], gain, bias, mean, inv_std)
    held_ref[0], held_ref[1], held_ref[2] = normed, slope, cot
    inv_ref[...] = jnp.broadcast_to(inv_std, (sub, 128))
    lane, has_left, has_right, has_up, has_down = plan.place_masks(plan.w)
    by_col = []
    for col in range(3):
        parts = [products[(3 * row + col) * wide : (3 * row + col + 1) * wide] for row in range(3)]
        by_col.append(parts[1] + moved(parts[0], plan.w, has_down) + moved(parts[2], -plan.w, has_up))
    conv_ref[...] = by_col[1] + moved(by_col[0], 1, has_right) + moved(by_col[2], -1, has_left)
    mine_ref[...] = conv_ref[pl.ds(pl.multiple_of(member * sub, sub), sub), :]
    theirs = conv_ref[pl.ds(pl.multiple_of((1 - member) * sub, sub), sub), :]
    sent_ref[0:sub, :] = theirs.astype(jnp.bfloat16)
    sent_ref[sub:, 0:128] = stats
    sent_ref[sub:, 128:] = jnp.zeros((8, plan.places - 128), jnp.bfloat16)


def quarter_kernel(plan, mine_ref, both_ref, held_ref, inv_ref, columns, by_column, out_ref, sums_ref):
    sub = plan.sub
    _, member, _, _ = own_place(plan)
    conv = mine_ref[...] + both_ref[1 - member, 0:sub, :].astype(jnp.float32)
    normed, slope, cot = held_ref[0], held_ref[1], held_ref[2]
    gain, inv_std = columns[0][0:sub, 0:1], inv_ref[:, 0:1]
    entries = plan.places * plan.group_width
    pre = conv * slope
    one, two = total([pre]), total([pre * normed])
    group_one = in_groups(gain * one, plan.group_width) / entries
    group_two = in_groups(gain * two, plan.group_width) / entries
    grad = cot + inv_std * (gain * pre - group_one - normed * group_two)
    quartered = (grad * 0.25).astype(jnp.bfloat16)
    sent = one_hot_dot(quartered, by_column[...], ((1,), (0,))).astype(jnp.bfloat16)
    low = lanes_at((sub // 2, 128), 1) < 64
    for half in range(2):
        at = half * 256
        border = sent[:, 512 + half * 128 : 640 + half * 128]
        border = jnp.where(low, border[: sub // 2], border[sub // 2 :])
        for dest in range(half, plan.count, 2):
            out_ref[dest, 0:sub, :] = sent[:, at : at + 128]
            out_ref[dest, sub : 2 * sub, :] = sent[:, at + 128 : at + 256]
            out_ref[dest, 2 * sub : 2 * sub + sub // 2, :] = border
    sums_ref[...] = jnp.concatenate([as_row(one), as_row(two)], axis=0)


def halves_at(plan, merged):
    sub = plan.sub
    turned = jnp.concatenate([pltpu.roll(merged[:, k * 128 : (k + 1) * 128], 64, 1) for k in range(4)], axis=1)
    low = lanes_at((sub, 128), 1) < 64
    parts = []
    for pq in range(4):
        groups = []
        for group in range(2):
            e = 4 * group + pq
            at = e // 2 * 128
            strips = []
            for m in range(plan.nf // 2):
                first, second = slice(2 * m * sub, (2 * m + 1) * sub), slice((2 * m + 1) * sub, (2 * m + 2) * sub)
                if e % 2 == 0:
                    strips.append(jnp.where(low, merged[first, at : at + 128], turned[second, at : at + 128]))
                else:
                    strips.append(jnp.where(low, turned[first, at : at + 128], merged[second, at : at + 128]))
            groups.append(jnp.concatenate(strips, axis=1))
        parts.append(jnp.concatenate(groups, axis=0))
    return parts


def halves_from(plan, parts):
    sub = plan.sub
    low = lanes_at((sub, 128), 1) < 64
    down = []
    for f in range(plan.nf):
        across = []
        for v in range(4):
            pair = []
            for e in (2 * v, 2 * v + 1):
                group, pq = e // 4, e % 4
                strip = parts[pq][group * sub : (group + 1) * sub, f // 2 * 128 : (f // 2 + 1) * 128]
                pair.append(strip if e % 2 == f % 2 else pltpu.roll(strip, 64, 1))
            across.append(jnp.where(low, pair[0], pair[1]))
        down.append(jnp.concatenate(across, axis=1))
    return jnp.concatenate(down, axis=0)


def fine_kernel(
    plan, got_ref, acts_ref, both_ref, columns, order, sums_ref, weights, out_ref, source, border
):
    sub, nr, nf, wide = plan.sub, plan.nr, plan.nf, 2 * plan.sub
    pair, member, r, _ = own_place(plan)
    both = pl.ds(pl.multiple_of(pair * wide, wide), wide)
    w = plan.w // 2
    lines = plan.places // plan.w
    places = lines * w
    for k in range(2):
        source[:, k * 128 : (k + 1) * 128] = got_ref[:, k * sub : (k + 1) * sub, :].reshape(plan.channels, 128)
    packed = got_ref[:, wide : wide + sub // 2, :].reshape(plan.count * sub // 2, 128)
    shape = (128, places)
    beside = lanes_at(shape, 1) == lanes_at(shape, 0) % lines * w + (1 - member) * (w - 1)
    for k in range(2):
        here = one_hot(beside & (lanes_at(shape, 0) // lines == k))
        found = one_hot_dot(packed, here, ((1,), (0,))).astype(jnp.bfloat16)
        for s in range(plan.count):
            border[s * sub + k * (sub // 2) : s * sub + (k + 1) * (sub // 2), :] = found[
                s * (sub // 2) : (s + 1) * (sub // 2)
            ]
    image = plan.image // 2
    sums, extras = 0.0, 0.0
    for k in (2, 1, 0):
        here, beside = source[...], border[...]
        if k < 2:
            shift = (2 - k) * image
            inside = lanes_at((1, places), 1) < places - shift
            here, beside = [
                jnp.where(inside, pltpu.roll(part, places - shift, 1), jnp.zeros_like(part)) for part in (here, beside)
            ]
        sums = sums + one_hot_dot(
            weights[9 * k : 9 * k + 9, both, :].reshape(9 * wide, plan.channels), here, ((1,), (0,))
        )
        facing = jnp.concatenate([weights[9 * k + 3 * row + 2 * member, both, :] for row in range(3)], axis=0)
        extras = extras + one_hot_dot(facing, beside, ((1,), (0,)))
    parts = [acts_ref[pq] for pq in range(4)]
    stats = sum(both_ref[k, sub : sub + 8, 0:128].astype(jnp.float32) for k in range(2))
    stats = stats[0:1] + stats[1:2] + stats[2:3]
    entries = 4 * plan.places * plan.group_width
    one, two = own_column(stats, 0, wide), own_column(stats, 64, wide)
    mean, inv_std = statistics(one, two, entries, plan.group_width)
    gain, bias = columns[2][:, 0:1], columns[3][:, 0:1]
    normed, slope = normalised(parts, gain, bias, mean, inv_std)
    lane, has_left, has_right, has_up, has_down = plan.place_masks(w)
    right, left = (1 - member).astype(jnp.float32), member.astype(jnp.float32)
    by_row = []
    for row in range(3):
        a, b, c = [sums[(3 * row + col) * wide : (3 * row + col + 1) * wide] for col in range(3)]
        extra = extras[row * wide : (row + 1) * wide]
        by_row.append(
            (a + b + moved(c, -1, has_left) + left * extra, moved(a, 1, has_right) + b + c + right * extra)
        )
    convs = [by_row[0][q] + by_row[1][q] + moved(by_row[2][q], -w, has_up) for q in range(2)]
    convs += [moved(by_row[0][q], w, has_down) + by_row[1][q] + by_row[2][q] for q in range(2)]
    pre = [conv * part for conv, part in zip(convs, slope)]
    one = total(pre)
    two = total([a * b for a, b in zip(pre, normed)])
    cot = source[pl.ds(pl.multiple_of(r * plan.slice_width + pair * wide, wide), wide), :].astype(jnp.float32)
    scale = inv_std * gain
    stacked = halves_from(plan, [cot + scale * part for part in pre]).astype(jnp.bfloat16)
    sent = one_hot_dot(stacked, order[...], ((1,), (1,))).astype(jnp.bfloat16)
    coarse = sums_ref[0:1] + pltpu.roll(sums_ref[1:2], sub, 1)
    coded = (
        terms(as_row(one) + pltpu.roll(as_row(two), 64, 1), 2)
        + terms(coarse, 2)
        + terms(as_row(inv_std) + pltpu.roll(as_row(mean), 64, 1), 3)
    )
    coded = jnp.concatenate(coded + [jnp.zeros_like(coarse)], axis=0).astype(jnp.bfloat16)
    for s_r in range(nr):
        for s_f in range(nf):
            out_ref[s_f * nr + s_r, 0:sub, :] = sent[s_f * sub : (s_f + 1) * sub, s_r * 128 : (s_r + 1) * 128]
            out_ref[s_f * nr + s_r, sub : sub + 8, :] = coded


def spread_kernel(plan, got_ref, acts_ref, gain_ref, out_ref, sums_ref):
    sub, nr, nf = plan.sub, plan.nr, plan.nf
    low = lanes_at((sub, 128), 1) < 64
    low_row = lanes_at((1, 128), 1) < 64
    first_row = lanes_at((1, 128), 1) < sub
    source = []
    fine, coarse, moments = [[], []], [[], []], [[], []]
    for s_r in range(nr):
        ones, twos, c_ones, c_twos, invs, means = [], [], 0.0, 0.0, [], []
        for pair in range(nf // 2):
            at = 2 * pair * nr + s_r
            left, right = [got_ref[at + k * nr, 0:sub, :].astype(jnp.float32) for k in range(2)]
            source.append(jnp.where(low, left, pltpu.roll(right, 64, 1)))
            source.append(jnp.where(low, pltpu.roll(left, 64, 1), right))
            coded = [got_ref[at + k * nr, sub : sub + 8, :].astype(jnp.float32) for k in range(2)]
            sums = coded[0][0:1] + coded[0][1:2] + coded[1][0:1] + coded[1][1:2]
            ones.append(sums if pair == 0 else pltpu.roll(sums, 64, 1))
            twos.append(pltpu.roll(sums, 64, 1) if pair == 0 else sums)
            both = coded[0][4:5] + coded[0][5:6] + coded[0][6:7]
            invs.append(both if pair == 0 else pltpu.roll(both, 64, 1))
            means.append(pltpu.roll(both, 64, 1) if pair == 0 else both)
            for k in range(2):
                sums = coded[k][2:3] + coded[k][3:4]
                to = (2 * pair + k) * sub
                c_one = jnp.where(first_row, sums, 0.0)
                c_two = jnp.where(first_row, pltpu.roll(sums, 128 - sub, 1), 0.0)
                c_ones = c_ones + (pltpu.roll(c_one, to, 1) if to else c_one)
                c_twos = c_twos + (pltpu.roll(c_two, to, 1) if to else c_two)
        fine[0].append(jnp.where(low_row, ones[0], ones[1]))
        fine[1].append(jnp.where(low_row, twos[0], twos[1]))
        moments[0].append(jnp.where(low_row, invs[0], invs[1]))
        moments[1].append(jnp.where(low_row, means[0], means[1]))
        coarse[0].append(c_ones)
        coarse[1].append(c_twos)
    one, two, inv_std, mean, c_one, c_two = [jnp.concatenate(part, axis=1) for part in fine + moments + coarse]
    source = jnp.concatenate(source, axis=0).astype(jnp.bfloat16)
    result = one_hot_dot(pixel_order(plan, False), source, ((1,), (1,)))
    gain = gain_ref[...]
    entries = 4 * plan.places * plan.group_width
    group_one = in_lane_groups(gain * one, plan.group_width) / entries
    group_two = in_lane_groups(gain * two, plan.group_width) / entries
    normed = (acts_ref[...].astype(jnp.float32) - mean) * inv_std
    out_ref[...] = (result - inv_std * (group_one + normed * group_two)).astype(jnp.bfloat16)
    sums_ref[...] = jnp.concatenate([one, two, c_one, c_two] + [jnp.zeros_like(one)] * 4, axis=0)


def total_kernel(scales, both_ref, result_ref, result_hbm, out_hbms, rows_ref, sems):
    copies = fetched([(result_ref, result_hbm)], sems)
    rows = sum(both_ref[k] for k in range(both_ref.shape[0]))
    for k in range(4):
        rows_ref[k] = rows[k : k + 1] * scales[k]
    for k in range(4):
        copies.append(pltpu.make_async_copy(rows_ref.at[k], out_hbms[k], sems.at[k + 1]))
        copies[-1].start()
    for copy in copies:
        copy.wait()


def in_vmem(count):
    return [pl.BlockSpec(memory_space=pltpu.VMEM)] * count


def in_hbm(count):
    return [pl.BlockSpec(memory_space=pltpu.HBM)] * count


def kept(array):
    return pltpu.with_memory_space_constraint(array, pltpu.HBM)


def shape_of(shape, kind):
    return jax.ShapeDtypeStruct(shape, kind)


LIMIT = pltpu.CompilerParams(vmem_limit_bytes=40 * 1024 * 1024)
COST = pl.CostEstimate(flops=2_000_000_000, bytes_accessed=4_000_000, transcendentals=0)


def fast_shards(
    plan,
    acts_fine,
    acts_coarse,
    grad_coarse,
    gain_fine,
    bias_fine,
    kernel_fine,
    gain_coarse,
    bias_coarse,
    kernel_coarse,
):
    nd = lax.axis_size("dp")
    count, sub, channels, places, local = plan.count, plan.sub, plan.channels, plan.places, plan.local
    f32, bf16 = jnp.float32, jnp.bfloat16
    rows = [part.reshape(1, channels) for part in (gain_coarse, bias_coarse, gain_fine, bias_fine)]
    places_of = ((local, channels), (local, channels), (4 * local, channels))
    fetched_of = pl.pallas_call(
        fetch_kernel,
        out_shape=tuple(pltpu.VMEM(shape, bf16) for shape in places_of),
        in_specs=in_hbm(3),
        out_specs=tuple(in_vmem(3)),
        scratch_shapes=[pltpu.SemaphoreType.DMA((3,))],
        compiler_params=LIMIT,
    )(*[kept(part.reshape(shape)) for part, shape in zip((grad_coarse, acts_coarse, acts_fine), places_of)])
    acts = fetched_of[2]
    packed = pl.pallas_call(
        functools.partial(pack_kernel, plan),
        out_shape=shape_of((count, plan.block_rows, 128), bf16),
        in_specs=in_vmem(3),
        out_specs=in_vmem(1)[0],
        compiler_params=LIMIT,
        cost_estimate=COST,
    )(*fetched_of)
    got = lax.all_to_all(packed, BACK_BLOCK, 0, 0)
    mine, theirs, held, inv_std, fine_acts, columns, fine_order, by_column = pl.pallas_call(
        functools.partial(coarse_kernel, plan),
        out_shape=(
            shape_of((sub, places), f32),
            shape_of((sub + 8, places), bf16),
            shape_of((3, sub, places), f32),
            shape_of((sub, 128), f32),
            shape_of((4, 2 * sub, places // 2), f32),
            shape_of((4, 2 * sub, 128), f32),
            shape_of((4 * plan.nr * local, 4 * plan.nr * local), bf16),
            shape_of((places, places + places // 2), bf16),
        ),
        in_specs=in_vmem(6),
        out_specs=tuple(in_vmem(8)),
        scratch_shapes=[
            pltpu.VMEM((4 * plan.nr * local, 4 * plan.nr * local), bf16),
            pltpu.VMEM((places + 2 * plan.image, channels // 2), bf16),
            pltpu.VMEM((2 * sub, places), f32),
        ],
        compiler_params=LIMIT,
        cost_estimate=COST,
    )(got, kernel_coarse, *rows)
    both = lax.all_gather(theirs, "member")
    quartered, coarse_sums = pl.pallas_call(
        functools.partial(quarter_kernel, plan),
        out_shape=(shape_of((count, 2 * sub + sub // 2, 128), bf16), shape_of((2, 128), f32)),
        in_specs=in_vmem(6),
        out_specs=tuple(in_vmem(2)),
        compiler_params=LIMIT,
        cost_estimate=COST,
    )(mine, both, held, inv_std, columns, by_column)
    spread = lax.all_to_all(quartered, BLOCK, 0, 0)
    sent = pl.pallas_call(
        functools.partial(fine_kernel, plan),
        out_shape=shape_of((count, sub + 8, 128), bf16),
        in_specs=in_vmem(7),
        out_specs=in_vmem(1)[0],
        scratch_shapes=[
            pltpu.VMEM((channels, places // 2), bf16),
            pltpu.VMEM((channels, places // 2), bf16),
        ],
        compiler_params=LIMIT,
        cost_estimate=COST,
    )(spread, fine_acts, both, columns, fine_order, coarse_sums, kernel_fine)
    back = lax.all_to_all(sent, BACK_BLOCK, 0, 0)
    cells = nd * places
    fine_scale, coarse_scale = 1.0 / math.sqrt(4 * cells), 1.0 / math.sqrt(cells)
    out, sums = pl.pallas_call(
        functools.partial(spread_kernel, plan),
        out_shape=(pltpu.VMEM((4 * local, channels), bf16), shape_of((8, channels), f32)),
        in_specs=in_vmem(3),
        out_specs=tuple(in_vmem(2)),
        compiler_params=LIMIT,
        cost_estimate=COST,
    )(back, acts, rows[2])
    both = lax.all_gather(sums, "dp")
    out, sums = pl.pallas_call(
        functools.partial(total_kernel, (fine_scale, fine_scale, coarse_scale, coarse_scale)),
        out_shape=(pltpu.HBM((4 * local, channels), bf16), (pltpu.HBM((1, channels), f32),) * 4),
        in_specs=in_vmem(2),
        out_specs=(in_hbm(1)[0], tuple(in_hbm(4))),
        scratch_shapes=[pltpu.VMEM((4, 1, channels), f32), pltpu.SemaphoreType.DMA((5,))],
        compiler_params=LIMIT,
        cost_estimate=COST,
    )(both, out)
    bias_f, gain_f, bias_c, gain_c = [part.reshape(channels) for part in sums]
    return out.reshape(acts_fine.shape), gain_f, bias_f, gain_c, bias_c


def solution(mesh):
    def function(*arrays):
        local = [size // mesh.shape[axis] for size, axis in zip(arrays[1].shape, ("dp", "frames", "rows"))]
        sizes = (mesh.shape["frames"], mesh.shape["rows"])
        plan = Plan(sizes, (*local[1:], *arrays[1].shape[3:]), arrays[5].shape[1] // mesh.shape["rows"])
        if plan.fits:
            split = (mesh.shape["dp"], plan.nf // 2, 2, plan.nr)
            used = jax.sharding.Mesh(mesh.devices.reshape(split), ("dp", "pairs", "member", "rows"))
            shards, frames = functools.partial(fast_shards, plan), ("pairs", "member")
        else:
            used, shards, frames = mesh, plain_shards, "frames"
        blocks, kernel = P("dp", frames, "rows", None, None), P(None, "rows", None)
        in_specs = (blocks, blocks, blocks, P(), P(), kernel, P(), P(), kernel)
        out_specs = (blocks, P(), P(), P(), P())
        mapped = jax.shard_map(shards, mesh=used, in_specs=in_specs, out_specs=out_specs, check_vma=False)
        return mapped(*arrays)

    return function
```

```python
import functools
import math

import jax
import jax.numpy as jnp
from jax import lax
from jax.experimental import pallas as pl
from jax.experimental.pallas import tpu as pltpu
from jax.sharding import PartitionSpec as P

GROUPS = 32
EPSILON = 1e-06
BLOCK = ("rows", "pairs", "member")
BACK_BLOCK = ("pairs", "member", "rows")
PLAIN_BLOCK = ("frames", "rows")


def plain_everyone(block, count):
    copies = jnp.broadcast_to(block[None], (count,) + block.shape)
    return lax.all_to_all(copies, PLAIN_BLOCK, 0, 0)


def ahead(field, axis, distance):
    size = field.shape[axis]
    if distance == 0:
        return field
    widths = [(0, 0)] * field.ndim
    if distance > 0:
        widths[axis] = (0, distance)
        kept = lax.slice_in_dim(field, distance, size, axis=axis)
    else:
        widths[axis] = (-distance, 0)
        kept = lax.slice_in_dim(field, 0, size + distance, axis=axis)
    return jnp.pad(kept, widths)


def tap_products(source, kernel):
    sub = kernel.shape[1]
    frames, rows, cols, channels = source.shape
    products = lax.dot_general(
        kernel.reshape(27 * sub, channels),
        source.reshape(frames * rows * cols, channels),
        (((1,), (1,)), ((), ())),
        preferred_element_type=jnp.float32,
    ).reshape(3, 3, 3, sub, frames, rows, cols)
    return sum(ahead(products[depth], 3, 2 - depth) for depth in range(3))


def coarse_conv(source, kernel):
    spatial = tap_products(source, kernel)
    total = 0.0
    for row in range(3):
        part = sum(ahead(spatial[row, col], 3, 1 - col) for col in range(3))
        total = total + ahead(part, 2, 1 - row)
    return total


def fine_conv(source, kernel):
    spatial = tap_products(source, kernel)
    result = []
    for p in range(2):
        rows_of = []
        for q in range(2):
            total = 0.0
            for row in range(3):
                part = sum(ahead(spatial[row, col], 3, (q + 1 - col) // 2) for col in range(3))
                total = total + ahead(part, 2, (p + 1 - row) // 2)
            rows_of.append(total)
        result.append(jnp.stack(rows_of, 1))
    return jnp.stack(result, 1)


def group_total(sums, group_width):
    sub = sums.shape[-1]
    if sub % group_width == 0:
        grouped = jnp.sum(sums.reshape(-1, sub // group_width, group_width), axis=-1)
        return jnp.repeat(grouped, group_width, axis=-1)
    spread = jnp.moveaxis(lax.all_gather(sums, "frames"), 0, 1).reshape(sums.shape[0], -1, group_width)
    mine = lax.axis_index("frames") * sub // group_width
    grouped = lax.dynamic_index_in_dim(jnp.sum(spread, -1), mine, 1)
    return jnp.broadcast_to(grouped, sums.shape)


def level(acts, conv_grad, cotangent, gain, bias, group_width):
    sub = acts.shape[0]
    places = acts.size // sub
    values = acts.astype(jnp.float32).reshape(sub, places)
    conv_grad = conv_grad.reshape(sub, places)
    entries = places * group_width
    moments = group_total(
        jnp.stack([jnp.sum(values, 1), jnp.sum(values * values, 1)]), group_width
    ) / entries
    mean = moments[0]
    inv_std = lax.rsqrt(moments[1] - mean * mean + EPSILON)
    normed = (values - mean[:, None]) * inv_std[:, None]
    preact = gain[:, None] * normed + bias[:, None]
    squash = jax.nn.sigmoid(preact)
    pre_grad = conv_grad * squash * (1.0 + preact * (1.0 - squash))
    sums = jnp.stack([jnp.sum(pre_grad, 1), jnp.sum(pre_grad * normed, 1)])
    terms = group_total(sums * gain, group_width) / entries
    grad = cotangent.reshape(sub, places) + inv_std[:, None] * (
        gain[:, None] * pre_grad - terms[0][:, None] - normed * terms[1][:, None]
    )
    return grad, sums


def plain_shards(
    acts_fine,
    acts_coarse,
    grad_coarse,
    gain_fine,
    bias_fine,
    kernel_fine,
    gain_coarse,
    bias_coarse,
    kernel_coarse,
):
    nf, nr, nd = lax.axis_size("frames"), lax.axis_size("rows"), lax.axis_size("dp")
    count = nf * nr
    channels = acts_fine.shape[-1]
    slice_width = kernel_fine.shape[1]
    sub = slice_width // nf
    group_width = channels // GROUPS
    tl, hl, w = acts_coarse.shape[1:4]
    frames, rows = tl * nf, hl * nr
    f, r = lax.axis_index("frames"), lax.axis_index("rows")

    gathered = plain_everyone(grad_coarse[0], count)
    source = (
        gathered.reshape(nf, nr, tl, hl, w, channels)
        .transpose(0, 2, 1, 3, 4, 5)
        .reshape(frames, rows, w, channels)
    )
    coarse_in = acts_coarse[0].reshape(tl, hl, w, nr, nf, sub).transpose(4, 3, 5, 0, 1, 2)
    coarse_in = lax.all_to_all(coarse_in.reshape(count, sub, tl * hl * w), PLAIN_BLOCK, 0, 0)
    fine_in = acts_fine[0].reshape(tl, hl, 2, w, 2, nr, nf, sub).transpose(6, 5, 7, 2, 4, 0, 1, 3)
    fine_in = lax.all_to_all(fine_in.reshape(count, sub, 4 * tl * hl * w), PLAIN_BLOCK, 0, 0)

    def mine(vector):
        return lax.dynamic_slice_in_dim(vector, r * slice_width + f * sub, sub)

    def own(kernel):
        return lax.dynamic_slice_in_dim(kernel, f * sub, sub, axis=1)

    coarse_vals = (
        coarse_in.reshape(nf, nr, sub, tl, hl, w).transpose(2, 0, 3, 1, 4, 5).reshape(sub, frames, rows, w)
    )
    cot = lax.dynamic_slice_in_dim(source, r * slice_width + f * sub, sub, axis=3)
    cot = cot.astype(jnp.float32).transpose(3, 0, 1, 2)
    conv = coarse_conv(source, own(kernel_coarse))
    coarse_grad, coarse_sums = level(
        coarse_vals, conv, cot, mine(gain_coarse), mine(bias_coarse), group_width
    )
    quartered = (coarse_grad * 0.25).astype(jnp.bfloat16)
    spread = plain_everyone(quartered, count)
    source_fine = (
        spread.reshape(nf, nr, sub, frames, rows, w)
        .transpose(3, 4, 5, 1, 0, 2)
        .reshape(frames, rows, w, channels)
    )
    conv = fine_conv(source_fine, own(kernel_fine))
    fine_vals = (
        fine_in.reshape(nf, nr, sub, 2, 2, tl, hl, w)
        .transpose(2, 3, 4, 0, 5, 1, 6, 7)
        .reshape(sub, 2, 2, frames, rows, w)
    )
    cot = jnp.broadcast_to(
        quartered.astype(jnp.float32).reshape(sub, 1, 1, frames, rows, w), conv.shape
    )
    fine_grad, fine_sums = level(
        fine_vals, conv, cot, mine(gain_fine), mine(bias_fine), group_width
    )
    back = (
        fine_grad.astype(jnp.bfloat16)
        .reshape(sub, 2, 2, nf, tl, nr, hl, w)
        .transpose(3, 5, 0, 1, 2, 4, 6, 7)
        .reshape(count, sub, 4 * tl * hl * w)
    )
    sums = plain_everyone(jnp.concatenate([fine_sums, coarse_sums]), count)
    back = lax.all_to_all(back, PLAIN_BLOCK, 0, 0)
    out = (
        back.reshape(nf, nr, sub, 2, 2, tl, hl, w)
        .transpose(5, 6, 3, 7, 4, 1, 0, 2)
        .reshape(1, tl, 2 * hl, 2 * w, channels)
    )
    sums = sums.reshape(nf, nr, 4, sub).transpose(2, 1, 0, 3).reshape(4, channels)
    totals = lax.psum(sums, "dp")
    cells = nd * frames * rows * w
    scale_fine = 1.0 / jnp.sqrt(jnp.float32(4 * cells))
    scale_coarse = 1.0 / jnp.sqrt(jnp.float32(cells))
    return (
        out,
        totals[1] * scale_fine,
        totals[0] * scale_fine,
        totals[3] * scale_coarse,
        totals[2] * scale_coarse,
    )


def lanes_at(shape, axis):
    return lax.broadcasted_iota(jnp.int32, shape, axis)


def one_hot(found):
    return found.astype(jnp.float32).astype(jnp.bfloat16)


def pixel_order(plan, swapped):
    tl, hl, w = plan.tl, plan.hl, plan.w // 2
    size = 4 * plan.local
    lane = lanes_at((1, size), 1)
    j, i, t = lane % w, lane // w % hl, lane // (w * hl) % tl
    q, p = lane // (w * hl * tl) % 2, lane // (2 * w * hl * tl) % 2
    half = lane // (4 * w * hl * tl)
    if swapped:
        half = 1 - half
    pixel = (t * 2 * hl + 2 * i + p) * 4 * w + 2 * (half * w + j) + q
    return one_hot(lanes_at((size, size), 0) == pixel)


def merged_order(nr, outer, tl, cells):
    size = nr * outer * tl * cells
    lane = lanes_at((1, size), 1)
    cell, dev = lane % cells, lane // cells % nr
    t, o = lane // (cells * nr) % tl, lane // (cells * nr * tl)
    return one_hot(lanes_at((size, size), 0) == ((dev * outer + o) * tl + t) * cells + cell)


def column_order(plan):
    w = plan.w // 2
    lines = plan.places // plan.w
    lane = lanes_at((1, 4 * lines * w + 4 * lines), 1)
    inner = lane % (lines * w)
    place = inner // w * plan.w + lane // (lines * w) * w + inner % w
    past = lane - 2 * lines * w
    border = past % lines * plan.w + jnp.where(past < 2 * lines, w, w - 1)
    wanted = jnp.where(past >= 0, border, place)
    shape = (plan.places, 2 * lines * w + 4 * lines)
    return one_hot(lanes_at(shape, 0) == wanted[:, : shape[1]])


def one_hot_dot(a, b, dims):
    return lax.dot_general(a, b, (dims, ((), ())), preferred_element_type=jnp.float32)


def moved(field, distance, kept):
    size = field.shape[1]
    return jnp.where(kept, pltpu.roll(field, (-distance) % size, 1), 0.0)


def own_column(row, base, sub):
    shape = (sub, row.shape[1])
    mine = lanes_at(shape, 1) == lanes_at(shape, 0) + base
    return jnp.sum(jnp.where(mine, row, 0.0), axis=1, keepdims=True)


def as_row(column):
    shape = (column.shape[0], 128)
    here = lanes_at(shape, 1) == lanes_at(shape, 0)
    return jnp.sum(jnp.where(here, column, 0.0), axis=0, keepdims=True)


def terms(value, count):
    found = []
    for _ in range(count):
        found.append(value.astype(jnp.bfloat16).astype(jnp.float32))
        value = value - found[-1]
    return found


def in_groups(column, group_width):
    sub = column.shape[0]
    grouped = jnp.sum(column.reshape(sub // group_width, group_width, 1), axis=1, keepdims=True)
    return jnp.broadcast_to(grouped, (sub // group_width, group_width, 1)).reshape(sub, 1)


def in_lane_groups(row, group_width):
    lane = lanes_at(row.shape, 1)
    size = row.shape[1]
    step = 1
    while step < group_width:
        up, down = pltpu.roll(row, size - step, 1), pltpu.roll(row, step, 1)
        row = row + jnp.where(lane // step % 2 == 0, up, down)
        step *= 2
    return row


def total(parts):
    return sum(jnp.sum(part, axis=1, keepdims=True) for part in parts)


def statistics(one, two, entries, group_width):
    mean = in_groups(one, group_width) / entries
    square = in_groups(two, group_width) / entries
    return mean, lax.rsqrt(square - mean * mean + EPSILON)


def normalised(parts, gain, bias, mean, inv_std):
    normed, slope = [], []
    for part in parts:
        unit = (part - mean) * inv_std
        preact = gain * unit + bias
        squash = 0.5 + 0.5 * jnp.tanh(0.5 * preact)
        normed.append(unit)
        slope.append(squash * (1.0 + preact * (1.0 - squash)))
    return normed, slope


class Plan:
    def __init__(self, mesh_sizes, acts_coarse, slice_width):
        self.nf, self.nr = mesh_sizes
        self.count = self.nf * self.nr
        self.tl, self.hl, self.w, self.channels = acts_coarse
        self.slice_width = slice_width
        self.sub = slice_width // self.nf
        self.cells = self.hl * self.w
        self.local = self.tl * self.cells
        self.image = self.cells * self.nr
        self.frames = self.tl * self.nf
        self.places = self.frames * self.image
        self.group_width = self.channels // GROUPS
        self.chunks = self.channels // 128
        self.acts_at = self.chunks // 2 * self.local
        self.packed_at = self.acts_at + self.sub
        self.cot_at = self.packed_at + 8
        self.block_rows = self.cot_at + 8
        self.fits = (
            self.sub == 32
            and self.slice_width == 128
            and self.group_width == 16
            and self.cells == 16
            and self.w == 8
            and self.tl == 2
            and self.nr == 4
            and self.nf == 4
            and self.slice_width * self.nr == self.channels
        )

    def place_masks(self, w):
        lane = lanes_at((1, self.places // self.w * w), 1)
        col, row = lane % w, lane // w % (self.hl * self.nr)
        last_row = self.hl * self.nr - 1
        return (lane, col > 0, col < w - 1, row > 0, row < last_row)


def fetched(pairs, sems):
    copies = [pltpu.make_async_copy(src, dst, sems.at[k]) for k, (src, dst) in enumerate(pairs)]
    for copy in copies:
        copy.start()
    return copies


def own_place(plan):
    pair, member, r = lax.axis_index("pairs"), lax.axis_index("member"), lax.axis_index("rows")
    return pair, member, r, r * plan.slice_width + (2 * pair + member) * plan.sub


def fetch_kernel(g_hbm, coarse_hbm, fine_hbm, g_ref, coarse_ref, fine_ref, sems):
    for copy in fetched([(fine_hbm, fine_ref), (coarse_hbm, coarse_ref), (g_hbm, g_ref)], sems):
        copy.wait()


def pack_kernel(plan, g_ref, coarse_ref, fine_ref, out_ref):
    sub, chunks, local = plan.sub, plan.chunks, plan.local
    shape = (2 * local, 2 * 128)
    lane = lanes_at((1, 2 * 128), 1)
    repeated = one_hot(lanes_at(shape, 0) == lane % local + lane // 128 * local)
    shape = (plan.channels, 128)
    quarter = lanes_at(shape, 0) // 8 % 4 == lanes_at(shape, 1) // local
    orders = jnp.concatenate([pixel_order(plan, swapped) for swapped in (False, True)], axis=1)
    acts = fine_ref[...]
    halves = one_hot_dot(acts, orders, ((0,), (0,))).astype(jnp.bfloat16)
    halves = [halves[:, :128], halves[:, 128:]]
    small = one_hot_dot(jnp.concatenate([coarse_ref[...], g_ref[...]], axis=0), repeated, ((0,), (0,)))
    for k, at in enumerate((plan.packed_at, plan.cot_at)):
        rows_of = jnp.where(quarter, small[:, k * 128 : (k + 1) * 128], 0.0).reshape(plan.count, 4, 8, 128)
        out_ref[:, at : at + 8, :] = jnp.sum(rows_of, axis=1).astype(jnp.bfloat16)
    low = lanes_at((sub, 128), 1) < 64
    for s_r in range(plan.nr):
        for s_f in range(plan.nf):
            dest = s_r * plan.nf + s_f
            first, half = s_r * plan.slice_width + s_f // 2 * 2 * sub, s_f % 2
            for k in range(chunks // 2):
                at = (half * chunks // 2 + k) * 128
                out_ref[dest, k * local : (k + 1) * local, :] = g_ref[:, at : at + 128]
            upper, lower = halves[half][first : first + sub], halves[1 - half][first + sub : first + 2 * sub]
            out_ref[dest, plan.acts_at : plan.packed_at, :] = jnp.where(low, upper, lower)


def by_frame_device(plan, got_ref, at, height):
    return jnp.concatenate(
        [
            jnp.concatenate(
                [got_ref[r * plan.nf + f, at : at + height, :] for r in range(plan.nr)], axis=1
            )
            for f in range(plan.nf)
        ],
        axis=0,
    )


def in_places(plan, merged, height):
    width = plan.tl * plan.image
    return [
        jnp.concatenate(
            [merged[f * height : (f + 1) * height, k * width : (k + 1) * width] for f in range(plan.nf)],
            axis=1,
        )
        for k in range(4)
    ]


def coarse_kernel(
    plan,
    got_ref,
    weights,
    gain_c,
    bias_c,
    gain_f,
    bias_f,
    mine_ref,
    sent_ref,
    held_ref,
    inv_ref,
    fine_ref,
    columns,
    fine_order,
    by_column,
    order,
    source,
    conv_ref,
):
    sub, nr, nf, cells, tl, local = plan.sub, plan.nr, plan.nf, plan.cells, plan.tl, plan.local
    wide, depth = 2 * sub, plan.channels // 2
    pair, member, r, base = own_place(plan)
    first = r * plan.slice_width + pair * wide
    columns[0, 0:sub, :] = jnp.broadcast_to(own_column(gain_c[...], base, sub), (sub, 128))
    columns[1, 0:sub, :] = jnp.broadcast_to(own_column(bias_c[...], base, sub), (sub, 128))
    columns[2] = jnp.broadcast_to(own_column(gain_f[...], first, wide), (wide, 128))
    columns[3] = jnp.broadcast_to(own_column(bias_f[...], first, wide), (wide, 128))
    order[...] = merged_order(plan.nr, 4, plan.tl, plan.cells)
    fine_order[...] = merged_order(plan.nr, 8, plan.tl, plan.cells // 2)
    by_column[...] = column_order(plan)
    both = pl.ds(pl.multiple_of(pair * wide, wide), wide)
    half = pl.ds(pl.multiple_of(member * depth, depth), depth)
    for s_f in range(nf):
        for s_r in range(nr):
            for t in range(tl):
                at = (s_f * tl + t) * plan.image + s_r * cells
                for k in range(plan.chunks // 2):
                    source[at : at + cells, k * 128 : (k + 1) * 128] = got_ref[
                        s_r * nf + s_f, k * local + t * cells : k * local + (t + 1) * cells, :
                    ]
    source[plan.places :, :] = jnp.zeros((2 * plan.image, depth), jnp.bfloat16)
    products = sum(
        one_hot_dot(
            weights[9 * k : 9 * k + 9, both, half].reshape(9 * wide, depth),
            source[(2 - k) * plan.image : (2 - k) * plan.image + plan.places, :],
            ((1,), (1,)),
        )
        for k in range(3)
    )
    merged = one_hot_dot(by_frame_device(plan, got_ref, plan.acts_at, sub), fine_order[...], ((1,), (0,)))
    parts = halves_at(plan, merged)
    for pq in range(4):
        fine_ref[pq] = parts[pq]
    one, two = total(parts), total([part * part for part in parts])
    stats = terms(as_row(one) + pltpu.roll(as_row(two), 64, 1), 3)
    stats = jnp.concatenate(stats + [jnp.zeros_like(stats[0])] * 5, axis=0).astype(jnp.bfloat16)
    small = [by_frame_device(plan, got_ref, at, 8) for at in (plan.packed_at, plan.cot_at)]
    merged = one_hot_dot(jnp.concatenate(small, axis=0), order[...], ((1,), (0,)))
    rows_of = 8 * nf
    values, cot = [
        jnp.concatenate(in_places(plan, merged[k * rows_of : (k + 1) * rows_of], 8), axis=0) for k in range(2)
    ]
    gain, bias = columns[0][0:sub, 0:1], columns[1][0:sub, 0:1]
    entries = plan.places * plan.group_width
    mean, inv_std = statistics(total([values]), total([values * values]), entries, plan.group_width)
    (normed,), (slope,) = normalised([values], gain, bias, mean, inv_std)
    held_ref[0], held_ref[1], held_ref[2] = normed, slope, cot
    inv_ref[...] = jnp.broadcast_to(inv_std, (sub, 128))
    lane, has_left, has_right, has_up, has_down = plan.place_masks(plan.w)
    by_col = []
    for col in range(3):
        parts = [products[(3 * row + col) * wide : (3 * row + col + 1) * wide] for row in range(3)]
        by_col.append(parts[1] + moved(parts[0], plan.w, has_down) + moved(parts[2], -plan.w, has_up))
    conv_ref[...] = by_col[1] + moved(by_col[0], 1, has_right) + moved(by_col[2], -1, has_left)
    mine_ref[...] = conv_ref[pl.ds(pl.multiple_of(member * sub, sub), sub), :]
    theirs = conv_ref[pl.ds(pl.multiple_of((1 - member) * sub, sub), sub), :]
    for k in range(plan.places // 128):
        sent_ref[k * sub : (k + 1) * sub, :] = theirs[:, k * 128 : (k + 1) * 128].astype(jnp.bfloat16)
    sent_ref[plan.places // 128 * sub :, :] = stats


def quarter_kernel(plan, mine_ref, both_ref, held_ref, inv_ref, columns, by_column, out_ref, sums_ref):
    sub = plan.sub
    _, member, _, _ = own_place(plan)
    theirs = [both_ref[1 - member, k * sub : (k + 1) * sub, :] for k in range(plan.places // 128)]
    conv = mine_ref[...] + jnp.concatenate(theirs, axis=1).astype(jnp.float32)
    normed, slope, cot = held_ref[0], held_ref[1], held_ref[2]
    gain, inv_std = columns[0][0:sub, 0:1], inv_ref[:, 0:1]
    entries = plan.places * plan.group_width
    pre = conv * slope
    one, two = total([pre]), total([pre * normed])
    group_one = in_groups(gain * one, plan.group_width) / entries
    group_two = in_groups(gain * two, plan.group_width) / entries
    grad = cot + inv_std * (gain * pre - group_one - normed * group_two)
    quartered = (grad * 0.25).astype(jnp.bfloat16)
    sent = one_hot_dot(quartered, by_column[...], ((1,), (0,))).astype(jnp.bfloat16)
    low = lanes_at((sub // 2, 128), 1) < 64
    for half in range(2):
        at = half * 256
        border = sent[:, 512 + half * 128 : 640 + half * 128]
        border = jnp.where(low, border[: sub // 2], border[sub // 2 :])
        for dest in range(half, plan.count, 2):
            out_ref[dest, 0:sub, :] = sent[:, at : at + 128]
            out_ref[dest, sub : 2 * sub, :] = sent[:, at + 128 : at + 256]
            out_ref[dest, 2 * sub : 2 * sub + sub // 2, :] = border
    sums_ref[...] = jnp.concatenate([as_row(one), as_row(two)], axis=0)


def halves_at(plan, merged):
    sub = plan.sub
    turned = jnp.concatenate([pltpu.roll(merged[:, k * 128 : (k + 1) * 128], 64, 1) for k in range(4)], axis=1)
    low = lanes_at((sub, 128), 1) < 64
    parts = []
    for pq in range(4):
        groups = []
        for group in range(2):
            e = 4 * group + pq
            at = e // 2 * 128
            strips = []
            for m in range(plan.nf // 2):
                first, second = slice(2 * m * sub, (2 * m + 1) * sub), slice((2 * m + 1) * sub, (2 * m + 2) * sub)
                if e % 2 == 0:
                    strips.append(jnp.where(low, merged[first, at : at + 128], turned[second, at : at + 128]))
                else:
                    strips.append(jnp.where(low, turned[first, at : at + 128], merged[second, at : at + 128]))
            groups.append(jnp.concatenate(strips, axis=1))
        parts.append(jnp.concatenate(groups, axis=0))
    return parts


def halves_from(plan, parts):
    sub = plan.sub
    low = lanes_at((sub, 128), 1) < 64
    down = []
    for f in range(plan.nf):
        across = []
        for v in range(4):
            pair = []
            for e in (2 * v, 2 * v + 1):
                group, pq = e // 4, e % 4
                strip = parts[pq][group * sub : (group + 1) * sub, f // 2 * 128 : (f // 2 + 1) * 128]
                pair.append(strip if e % 2 == f % 2 else pltpu.roll(strip, 64, 1))
            across.append(jnp.where(low, pair[0], pair[1]))
        down.append(jnp.concatenate(across, axis=1))
    return jnp.concatenate(down, axis=0)


def fine_kernel(
    plan, got_ref, acts_ref, both_ref, columns, order, sums_ref, weights, out_ref
):
    sub, nr, nf, wide = plan.sub, plan.nr, plan.nf, 2 * plan.sub
    pair, member, r, _ = own_place(plan)
    both = pl.ds(pl.multiple_of(pair * wide, wide), wide)
    w = plan.w // 2
    lines = plan.places // plan.w
    places = lines * w
    source = jnp.concatenate(
        [got_ref[:, k * sub : (k + 1) * sub, :].reshape(plan.channels, 128) for k in range(2)], axis=1
    )
    packed = got_ref[:, wide : wide + sub // 2, :].reshape(plan.count * sub // 2, 128)
    shape = (128, places)
    beside = lanes_at(shape, 1) == lanes_at(shape, 0) % lines * w + (1 - member) * (w - 1)
    border = []
    for k in range(2):
        here = one_hot(beside & (lanes_at(shape, 0) // lines == k))
        found = one_hot_dot(packed, here, ((1,), (0,))).astype(jnp.bfloat16)
        border.append(found.reshape(plan.count, sub // 2, places))
    border = jnp.concatenate(border, axis=1).reshape(plan.channels, places)
    image = plan.image // 2
    sums, extras = 0.0, 0.0
    for k in (2, 1, 0):
        here, beside = source, border
        if k < 2:
            shift = (2 - k) * image
            inside = lanes_at((1, places), 1) < places - shift
            here, beside = [
                jnp.where(inside, pltpu.roll(part, places - shift, 1), jnp.zeros_like(part)) for part in (here, beside)
            ]
        sums = sums + one_hot_dot(
            weights[9 * k : 9 * k + 9, both, :].reshape(9 * wide, plan.channels), here, ((1,), (0,))
        )
        facing = jnp.concatenate([weights[9 * k + 3 * row + 2 * member, both, :] for row in range(3)], axis=0)
        extras = extras + one_hot_dot(facing, beside, ((1,), (0,)))
    parts = [acts_ref[pq] for pq in range(4)]
    at = plan.places // 128 * sub
    stats = sum(both_ref[k, at : at + 8, :].astype(jnp.float32) for k in range(2))
    stats = stats[0:1] + stats[1:2] + stats[2:3]
    entries = 4 * plan.places * plan.group_width
    one, two = own_column(stats, 0, wide), own_column(stats, 64, wide)
    mean, inv_std = statistics(one, two, entries, plan.group_width)
    gain, bias = columns[2][:, 0:1], columns[3][:, 0:1]
    normed, slope = normalised(parts, gain, bias, mean, inv_std)
    lane, has_left, has_right, has_up, has_down = plan.place_masks(w)
    right, left = (1 - member).astype(jnp.float32), member.astype(jnp.float32)
    by_row = []
    for row in range(3):
        a, b, c = [sums[(3 * row + col) * wide : (3 * row + col + 1) * wide] for col in range(3)]
        extra = extras[row * wide : (row + 1) * wide]
        by_row.append(
            (a + b + moved(c, -1, has_left) + left * extra, moved(a, 1, has_right) + b + c + right * extra)
        )
    convs = [by_row[0][q] + by_row[1][q] + moved(by_row[2][q], -w, has_up) for q in range(2)]
    convs += [moved(by_row[0][q], w, has_down) + by_row[1][q] + by_row[2][q] for q in range(2)]
    pre = [conv * part for conv, part in zip(convs, slope)]
    one = total(pre)
    two = total([a * b for a, b in zip(pre, normed)])
    cot = jnp.concatenate(
        [
            jnp.concatenate(
                [got_ref[r * nf + 2 * pair + m, k * sub : (k + 1) * sub, :] for k in range(2)], axis=1
            )
            for m in range(2)
        ],
        axis=0,
    ).astype(jnp.float32)
    scale = inv_std * gain
    stacked = halves_from(plan, [cot + scale * part for part in pre]).astype(jnp.bfloat16)
    sent = one_hot_dot(stacked, order[...], ((1,), (1,))).astype(jnp.bfloat16)
    coarse = sums_ref[0:1] + pltpu.roll(sums_ref[1:2], sub, 1)
    coded = (
        terms(as_row(one) + pltpu.roll(as_row(two), 64, 1), 2)
        + terms(coarse, 2)
        + terms(as_row(inv_std) + pltpu.roll(as_row(mean), 64, 1), 3)
    )
    coded = jnp.concatenate(coded + [jnp.zeros_like(coarse)], axis=0).astype(jnp.bfloat16)
    for s_r in range(nr):
        for s_f in range(nf):
            out_ref[s_f * nr + s_r, 0:sub, :] = sent[s_f * sub : (s_f + 1) * sub, s_r * 128 : (s_r + 1) * 128]
            out_ref[s_f * nr + s_r, sub : sub + 8, :] = coded


def spread_kernel(plan, got_ref, acts_ref, gain_ref, out_ref, sums_ref):
    sub, nr, nf = plan.sub, plan.nr, plan.nf
    low = lanes_at((sub, 128), 1) < 64
    low_row = lanes_at((1, 128), 1) < 64
    first_row = lanes_at((1, 128), 1) < sub
    source = []
    fine, coarse, moments = [[], []], [[], []], [[], []]
    for s_r in range(nr):
        ones, twos, c_ones, c_twos, invs, means = [], [], 0.0, 0.0, [], []
        for pair in range(nf // 2):
            at = 2 * pair * nr + s_r
            left, right = [got_ref[at + k * nr, 0:sub, :].astype(jnp.float32) for k in range(2)]
            source.append(jnp.where(low, left, pltpu.roll(right, 64, 1)))
            source.append(jnp.where(low, pltpu.roll(left, 64, 1), right))
            coded = [got_ref[at + k * nr, sub : sub + 8, :].astype(jnp.float32) for k in range(2)]
            sums = coded[0][0:1] + coded[0][1:2] + coded[1][0:1] + coded[1][1:2]
            ones.append(sums if pair == 0 else pltpu.roll(sums, 64, 1))
            twos.append(pltpu.roll(sums, 64, 1) if pair == 0 else sums)
            both = coded[0][4:5] + coded[0][5:6] + coded[0][6:7]
            invs.append(both if pair == 0 else pltpu.roll(both, 64, 1))
            means.append(pltpu.roll(both, 64, 1) if pair == 0 else both)
            for k in range(2):
                sums = coded[k][2:3] + coded[k][3:4]
                to = (2 * pair + k) * sub
                c_one = jnp.where(first_row, sums, 0.0)
                c_two = jnp.where(first_row, pltpu.roll(sums, 128 - sub, 1), 0.0)
                c_ones = c_ones + (pltpu.roll(c_one, to, 1) if to else c_one)
                c_twos = c_twos + (pltpu.roll(c_two, to, 1) if to else c_two)
        fine[0].append(jnp.where(low_row, ones[0], ones[1]))
        fine[1].append(jnp.where(low_row, twos[0], twos[1]))
        moments[0].append(jnp.where(low_row, invs[0], invs[1]))
        moments[1].append(jnp.where(low_row, means[0], means[1]))
        coarse[0].append(c_ones)
        coarse[1].append(c_twos)
    one, two, inv_std, mean, c_one, c_two = [jnp.concatenate(part, axis=1) for part in fine + moments + coarse]
    source = jnp.concatenate(source, axis=0).astype(jnp.bfloat16)
    result = one_hot_dot(pixel_order(plan, False), source, ((1,), (1,)))
    gain = gain_ref[...]
    entries = 4 * plan.places * plan.group_width
    group_one = in_lane_groups(gain * one, plan.group_width) / entries
    group_two = in_lane_groups(gain * two, plan.group_width) / entries
    normed = (acts_ref[...].astype(jnp.float32) - mean) * inv_std
    out_ref[...] = (result - inv_std * (group_one + normed * group_two)).astype(jnp.bfloat16)
    sums_ref[...] = jnp.concatenate([one, two, c_one, c_two] + [jnp.zeros_like(one)] * 4, axis=0)


def total_kernel(scales, both_ref, result_ref, result_hbm, out_hbms, rows_ref, sems):
    copies = fetched([(result_ref, result_hbm)], sems)
    rows = sum(both_ref[k] for k in range(both_ref.shape[0]))
    for k in range(4):
        rows_ref[k] = rows[k : k + 1] * scales[k]
    for k in range(4):
        copies.append(pltpu.make_async_copy(rows_ref.at[k], out_hbms[k], sems.at[k + 1]))
        copies[-1].start()
    for copy in copies:
        copy.wait()


def in_vmem(count):
    return [pl.BlockSpec(memory_space=pltpu.VMEM)] * count


def in_hbm(count):
    return [pl.BlockSpec(memory_space=pltpu.HBM)] * count


def kept(array):
    return pltpu.with_memory_space_constraint(array, pltpu.HBM)


def shape_of(shape, kind):
    return jax.ShapeDtypeStruct(shape, kind)


LIMIT = pltpu.CompilerParams(vmem_limit_bytes=40 * 1024 * 1024)
COST = pl.CostEstimate(flops=2_000_000_000, bytes_accessed=4_000_000, transcendentals=0)


def fast_shards(
    plan,
    acts_fine,
    acts_coarse,
    grad_coarse,
    gain_fine,
    bias_fine,
    kernel_fine,
    gain_coarse,
    bias_coarse,
    kernel_coarse,
):
    nd = lax.axis_size("dp")
    count, sub, channels, places, local = plan.count, plan.sub, plan.channels, plan.places, plan.local
    f32, bf16 = jnp.float32, jnp.bfloat16
    rows = [part.reshape(1, channels) for part in (gain_coarse, bias_coarse, gain_fine, bias_fine)]
    places_of = ((local, channels), (local, channels), (4 * local, channels))
    fetched_of = pl.pallas_call(
        fetch_kernel,
        out_shape=tuple(pltpu.VMEM(shape, bf16) for shape in places_of),
        in_specs=in_hbm(3),
        out_specs=tuple(in_vmem(3)),
        scratch_shapes=[pltpu.SemaphoreType.DMA((3,))],
        compiler_params=LIMIT,
    )(*[kept(part.reshape(shape)) for part, shape in zip((grad_coarse, acts_coarse, acts_fine), places_of)])
    acts = fetched_of[2]
    packed = pl.pallas_call(
        functools.partial(pack_kernel, plan),
        out_shape=shape_of((count, plan.block_rows, 128), bf16),
        in_specs=in_vmem(3),
        out_specs=in_vmem(1)[0],
        compiler_params=LIMIT,
        cost_estimate=COST,
    )(*fetched_of)
    got = lax.all_to_all(packed, BLOCK, 0, 0)
    mine, theirs, held, inv_std, fine_acts, columns, fine_order, by_column = pl.pallas_call(
        functools.partial(coarse_kernel, plan),
        out_shape=(
            shape_of((sub, places), f32),
            shape_of((places // 128 * sub + 8, 128), bf16),
            shape_of((3, sub, places), f32),
            shape_of((sub, 128), f32),
            shape_of((4, 2 * sub, places // 2), f32),
            shape_of((4, 2 * sub, 128), f32),
            shape_of((4 * plan.nr * local, 4 * plan.nr * local), bf16),
            shape_of((places, places + places // 2), bf16),
        ),
        in_specs=in_vmem(6),
        out_specs=tuple(in_vmem(8)),
        scratch_shapes=[
            pltpu.VMEM((4 * plan.nr * local, 4 * plan.nr * local), bf16),
            pltpu.VMEM((places + 2 * plan.image, channels // 2), bf16),
            pltpu.VMEM((2 * sub, places), f32),
        ],
        compiler_params=LIMIT,
        cost_estimate=COST,
    )(got, kernel_coarse, *rows)
    both = lax.all_gather(theirs, "member")
    quartered, coarse_sums = pl.pallas_call(
        functools.partial(quarter_kernel, plan),
        out_shape=(shape_of((count, 2 * sub + sub // 2, 128), bf16), shape_of((2, 128), f32)),
        in_specs=in_vmem(6),
        out_specs=tuple(in_vmem(2)),
        compiler_params=LIMIT,
        cost_estimate=COST,
    )(mine, both, held, inv_std, columns, by_column)
    spread = lax.all_to_all(quartered, BLOCK, 0, 0)
    sent = pl.pallas_call(
        functools.partial(fine_kernel, plan),
        out_shape=shape_of((count, sub + 8, 128), bf16),
        in_specs=in_vmem(7),
        out_specs=in_vmem(1)[0],
        compiler_params=LIMIT,
        cost_estimate=COST,
    )(spread, fine_acts, both, columns, fine_order, coarse_sums, kernel_fine)
    back = lax.all_to_all(sent, BACK_BLOCK, 0, 0)
    cells = nd * places
    fine_scale, coarse_scale = 1.0 / math.sqrt(4 * cells), 1.0 / math.sqrt(cells)
    out, sums = pl.pallas_call(
        functools.partial(spread_kernel, plan),
        out_shape=(pltpu.VMEM((4 * local, channels), bf16), shape_of((8, channels), f32)),
        in_specs=in_vmem(3),
        out_specs=tuple(in_vmem(2)),
        compiler_params=LIMIT,
        cost_estimate=COST,
    )(back, acts, rows[2])
    both = lax.all_gather(sums, "dp")
    out, sums = pl.pallas_call(
        functools.partial(total_kernel, (fine_scale, fine_scale, coarse_scale, coarse_scale)),
        out_shape=(pltpu.HBM((4 * local, channels), bf16), (pltpu.HBM((1, channels), f32),) * 4),
        in_specs=in_vmem(2),
        out_specs=(in_hbm(1)[0], tuple(in_hbm(4))),
        scratch_shapes=[pltpu.VMEM((4, 1, channels), f32), pltpu.SemaphoreType.DMA((5,))],
        compiler_params=LIMIT,
        cost_estimate=COST,
    )(both, out)
    bias_f, gain_f, bias_c, gain_c = [part.reshape(channels) for part in sums]
    return out.reshape(acts_fine.shape), gain_f, bias_f, gain_c, bias_c


def solution(mesh):
    def function(*arrays):
        local = [size // mesh.shape[axis] for size, axis in zip(arrays[1].shape, ("dp", "frames", "rows"))]
        sizes = (mesh.shape["frames"], mesh.shape["rows"])
        plan = Plan(sizes, (*local[1:], *arrays[1].shape[3:]), arrays[5].shape[1] // mesh.shape["rows"])
        if plan.fits:
            split = (mesh.shape["dp"], plan.nf // 2, 2, plan.nr)
            used = jax.sharding.Mesh(mesh.devices.reshape(split), ("dp", "pairs", "member", "rows"))
            shards, frames = functools.partial(fast_shards, plan), ("pairs", "member")
        else:
            used, shards, frames = mesh, plain_shards, "frames"
        blocks, kernel = P("dp", frames, "rows", None, None), P(None, "rows", None)
        in_specs = (blocks, blocks, blocks, P(), P(), kernel, P(), P(), kernel)
        out_specs = (blocks, P(), P(), P(), P())
        mapped = jax.shard_map(shards, mesh=used, in_specs=in_specs, out_specs=out_specs, check_vma=False)
        return mapped(*arrays)

    return function
```

```python
import functools
import math

import jax
import jax.numpy as jnp
from jax import lax
from jax.experimental import pallas as pl
from jax.experimental.pallas import tpu as pltpu
from jax.sharding import PartitionSpec as P

GROUPS = 32
EPSILON = 1e-06
BLOCK = ("rows", "pairs", "member")
BACK_BLOCK = ("pairs", "member", "rows")
PLAIN_BLOCK = ("frames", "rows")


def plain_everyone(block, count):
    copies = jnp.broadcast_to(block[None], (count,) + block.shape)
    return lax.all_to_all(copies, PLAIN_BLOCK, 0, 0)


def ahead(field, axis, distance):
    size = field.shape[axis]
    if distance == 0:
        return field
    widths = [(0, 0)] * field.ndim
    if distance > 0:
        widths[axis] = (0, distance)
        kept = lax.slice_in_dim(field, distance, size, axis=axis)
    else:
        widths[axis] = (-distance, 0)
        kept = lax.slice_in_dim(field, 0, size + distance, axis=axis)
    return jnp.pad(kept, widths)


def tap_products(source, kernel):
    sub = kernel.shape[1]
    frames, rows, cols, channels = source.shape
    products = lax.dot_general(
        kernel.reshape(27 * sub, channels),
        source.reshape(frames * rows * cols, channels),
        (((1,), (1,)), ((), ())),
        preferred_element_type=jnp.float32,
    ).reshape(3, 3, 3, sub, frames, rows, cols)
    return sum(ahead(products[depth], 3, 2 - depth) for depth in range(3))


def coarse_conv(source, kernel):
    spatial = tap_products(source, kernel)
    total = 0.0
    for row in range(3):
        part = sum(ahead(spatial[row, col], 3, 1 - col) for col in range(3))
        total = total + ahead(part, 2, 1 - row)
    return total


def fine_conv(source, kernel):
    spatial = tap_products(source, kernel)
    result = []
    for p in range(2):
        rows_of = []
        for q in range(2):
            total = 0.0
            for row in range(3):
                part = sum(ahead(spatial[row, col], 3, (q + 1 - col) // 2) for col in range(3))
                total = total + ahead(part, 2, (p + 1 - row) // 2)
            rows_of.append(total)
        result.append(jnp.stack(rows_of, 1))
    return jnp.stack(result, 1)


def group_total(sums, group_width):
    sub = sums.shape[-1]
    if sub % group_width == 0:
        grouped = jnp.sum(sums.reshape(-1, sub // group_width, group_width), axis=-1)
        return jnp.repeat(grouped, group_width, axis=-1)
    spread = jnp.moveaxis(lax.all_gather(sums, "frames"), 0, 1).reshape(sums.shape[0], -1, group_width)
    mine = lax.axis_index("frames") * sub // group_width
    grouped = lax.dynamic_index_in_dim(jnp.sum(spread, -1), mine, 1)
    return jnp.broadcast_to(grouped, sums.shape)


def level(acts, conv_grad, cotangent, gain, bias, group_width):
    sub = acts.shape[0]
    places = acts.size // sub
    values = acts.astype(jnp.float32).reshape(sub, places)
    conv_grad = conv_grad.reshape(sub, places)
    entries = places * group_width
    moments = group_total(
        jnp.stack([jnp.sum(values, 1), jnp.sum(values * values, 1)]), group_width
    ) / entries
    mean = moments[0]
    inv_std = lax.rsqrt(moments[1] - mean * mean + EPSILON)
    normed = (values - mean[:, None]) * inv_std[:, None]
    preact = gain[:, None] * normed + bias[:, None]
    squash = jax.nn.sigmoid(preact)
    pre_grad = conv_grad * squash * (1.0 + preact * (1.0 - squash))
    sums = jnp.stack([jnp.sum(pre_grad, 1), jnp.sum(pre_grad * normed, 1)])
    terms = group_total(sums * gain, group_width) / entries
    grad = cotangent.reshape(sub, places) + inv_std[:, None] * (
        gain[:, None] * pre_grad - terms[0][:, None] - normed * terms[1][:, None]
    )
    return grad, sums


def plain_shards(
    acts_fine,
    acts_coarse,
    grad_coarse,
    gain_fine,
    bias_fine,
    kernel_fine,
    gain_coarse,
    bias_coarse,
    kernel_coarse,
):
    nf, nr, nd = lax.axis_size("frames"), lax.axis_size("rows"), lax.axis_size("dp")
    count = nf * nr
    channels = acts_fine.shape[-1]
    slice_width = kernel_fine.shape[1]
    sub = slice_width // nf
    group_width = channels // GROUPS
    tl, hl, w = acts_coarse.shape[1:4]
    frames, rows = tl * nf, hl * nr
    f, r = lax.axis_index("frames"), lax.axis_index("rows")

    gathered = plain_everyone(grad_coarse[0], count)
    source = (
        gathered.reshape(nf, nr, tl, hl, w, channels)
        .transpose(0, 2, 1, 3, 4, 5)
        .reshape(frames, rows, w, channels)
    )
    coarse_in = acts_coarse[0].reshape(tl, hl, w, nr, nf, sub).transpose(4, 3, 5, 0, 1, 2)
    coarse_in = lax.all_to_all(coarse_in.reshape(count, sub, tl * hl * w), PLAIN_BLOCK, 0, 0)
    fine_in = acts_fine[0].reshape(tl, hl, 2, w, 2, nr, nf, sub).transpose(6, 5, 7, 2, 4, 0, 1, 3)
    fine_in = lax.all_to_all(fine_in.reshape(count, sub, 4 * tl * hl * w), PLAIN_BLOCK, 0, 0)

    def mine(vector):
        return lax.dynamic_slice_in_dim(vector, r * slice_width + f * sub, sub)

    def own(kernel):
        return lax.dynamic_slice_in_dim(kernel, f * sub, sub, axis=1)

    coarse_vals = (
        coarse_in.reshape(nf, nr, sub, tl, hl, w).transpose(2, 0, 3, 1, 4, 5).reshape(sub, frames, rows, w)
    )
    cot = lax.dynamic_slice_in_dim(source, r * slice_width + f * sub, sub, axis=3)
    cot = cot.astype(jnp.float32).transpose(3, 0, 1, 2)
    conv = coarse_conv(source, own(kernel_coarse))
    coarse_grad, coarse_sums = level(
        coarse_vals, conv, cot, mine(gain_coarse), mine(bias_coarse), group_width
    )
    quartered = (coarse_grad * 0.25).astype(jnp.bfloat16)
    spread = plain_everyone(quartered, count)
    source_fine = (
        spread.reshape(nf, nr, sub, frames, rows, w)
        .transpose(3, 4, 5, 1, 0, 2)
        .reshape(frames, rows, w, channels)
    )
    conv = fine_conv(source_fine, own(kernel_fine))
    fine_vals = (
        fine_in.reshape(nf, nr, sub, 2, 2, tl, hl, w)
        .transpose(2, 3, 4, 0, 5, 1, 6, 7)
        .reshape(sub, 2, 2, frames, rows, w)
    )
    cot = jnp.broadcast_to(
        quartered.astype(jnp.float32).reshape(sub, 1, 1, frames, rows, w), conv.shape
    )
    fine_grad, fine_sums = level(
        fine_vals, conv, cot, mine(gain_fine), mine(bias_fine), group_width
    )
    back = (
        fine_grad.astype(jnp.bfloat16)
        .reshape(sub, 2, 2, nf, tl, nr, hl, w)
        .transpose(3, 5, 0, 1, 2, 4, 6, 7)
        .reshape(count, sub, 4 * tl * hl * w)
    )
    sums = plain_everyone(jnp.concatenate([fine_sums, coarse_sums]), count)
    back = lax.all_to_all(back, PLAIN_BLOCK, 0, 0)
    out = (
        back.reshape(nf, nr, sub, 2, 2, tl, hl, w)
        .transpose(5, 6, 3, 7, 4, 1, 0, 2)
        .reshape(1, tl, 2 * hl, 2 * w, channels)
    )
    sums = sums.reshape(nf, nr, 4, sub).transpose(2, 1, 0, 3).reshape(4, channels)
    totals = lax.psum(sums, "dp")
    cells = nd * frames * rows * w
    scale_fine = 1.0 / jnp.sqrt(jnp.float32(4 * cells))
    scale_coarse = 1.0 / jnp.sqrt(jnp.float32(cells))
    return (
        out,
        totals[1] * scale_fine,
        totals[0] * scale_fine,
        totals[3] * scale_coarse,
        totals[2] * scale_coarse,
    )


def lanes_at(shape, axis):
    return lax.broadcasted_iota(jnp.int32, shape, axis)


def one_hot(found):
    return found.astype(jnp.float32).astype(jnp.bfloat16)


def pixel_order(plan, swapped):
    tl, hl, w = plan.tl, plan.hl, plan.w // 2
    size = 4 * plan.local
    lane = lanes_at((1, size), 1)
    j, i, t = lane % w, lane // w % hl, lane // (w * hl) % tl
    q, p = lane // (w * hl * tl) % 2, lane // (2 * w * hl * tl) % 2
    half = lane // (4 * w * hl * tl)
    if swapped:
        half = 1 - half
    pixel = (t * 2 * hl + 2 * i + p) * 4 * w + 2 * (half * w + j) + q
    return one_hot(lanes_at((size, size), 0) == pixel)


def merged_order(nr, outer, tl, cells):
    size = nr * outer * tl * cells
    lane = lanes_at((1, size), 1)
    cell, dev = lane % cells, lane // cells % nr
    t, o = lane // (cells * nr) % tl, lane // (cells * nr * tl)
    return one_hot(lanes_at((size, size), 0) == ((dev * outer + o) * tl + t) * cells + cell)


def column_order(plan):
    w = plan.w // 2
    lines = plan.places // plan.w
    lane = lanes_at((1, 4 * lines * w + 4 * lines), 1)
    inner = lane % (lines * w)
    place = inner // w * plan.w + lane // (lines * w) * w + inner % w
    past = lane - 2 * lines * w
    border = past % lines * plan.w + jnp.where(past < 2 * lines, w, w - 1)
    wanted = jnp.where(past >= 0, border, place)
    shape = (plan.places, 2 * lines * w + 4 * lines)
    return one_hot(lanes_at(shape, 0) == wanted[:, : shape[1]])


def one_hot_dot(a, b, dims):
    return lax.dot_general(a, b, (dims, ((), ())), preferred_element_type=jnp.float32)


def moved(field, distance, kept):
    size = field.shape[1]
    return jnp.where(kept, pltpu.roll(field, (-distance) % size, 1), 0.0)


def own_column(row, base, sub):
    shape = (sub, row.shape[1])
    mine = lanes_at(shape, 1) == lanes_at(shape, 0) + base
    return jnp.sum(jnp.where(mine, row, 0.0), axis=1, keepdims=True)


def as_row(column):
    shape = (column.shape[0], 128)
    here = lanes_at(shape, 1) == lanes_at(shape, 0)
    return jnp.sum(jnp.where(here, column, 0.0), axis=0, keepdims=True)


def terms(value, count):
    found = []
    for _ in range(count):
        found.append(value.astype(jnp.bfloat16).astype(jnp.float32))
        value = value - found[-1]
    return found


def in_groups(column, group_width):
    sub = column.shape[0]
    grouped = jnp.sum(column.reshape(sub // group_width, group_width, 1), axis=1, keepdims=True)
    return jnp.broadcast_to(grouped, (sub // group_width, group_width, 1)).reshape(sub, 1)


def in_lane_groups(row, group_width):
    lane = lanes_at(row.shape, 1)
    size = row.shape[1]
    step = 1
    while step < group_width:
        up, down = pltpu.roll(row, size - step, 1), pltpu.roll(row, step, 1)
        row = row + jnp.where(lane // step % 2 == 0, up, down)
        step *= 2
    return row


def total(parts):
    return sum(jnp.sum(part, axis=1, keepdims=True) for part in parts)


def statistics(one, two, entries, group_width):
    mean = in_groups(one, group_width) / entries
    square = in_groups(two, group_width) / entries
    return mean, lax.rsqrt(square - mean * mean + EPSILON)


def normalised(parts, gain, bias, mean, inv_std):
    normed, slope = [], []
    for part in parts:
        unit = (part - mean) * inv_std
        preact = gain * unit + bias
        squash = 0.5 + 0.5 * jnp.tanh(0.5 * preact)
        normed.append(unit)
        slope.append(squash * (1.0 + preact * (1.0 - squash)))
    return normed, slope


class Plan:
    def __init__(self, mesh_sizes, acts_coarse, slice_width):
        self.nf, self.nr = mesh_sizes
        self.count = self.nf * self.nr
        self.tl, self.hl, self.w, self.channels = acts_coarse
        self.slice_width = slice_width
        self.sub = slice_width // self.nf
        self.cells = self.hl * self.w
        self.local = self.tl * self.cells
        self.image = self.cells * self.nr
        self.frames = self.tl * self.nf
        self.places = self.frames * self.image
        self.group_width = self.channels // GROUPS
        self.chunks = self.channels // 128
        self.packed_at = self.chunks // 2 * self.local
        self.acts_at = 2 * self.sub + self.sub // 2
        self.stats_at = self.acts_at + self.sub
        self.cot_at = self.packed_at + 8
        self.block_rows = self.cot_at + 8
        self.fits = (
            self.sub == 32
            and self.slice_width == 128
            and self.group_width == 16
            and self.cells == 16
            and self.w == 8
            and self.tl == 2
            and self.nr == 4
            and self.nf == 4
            and self.slice_width * self.nr == self.channels
        )

    def place_masks(self, w):
        lane = lanes_at((1, self.places // self.w * w), 1)
        col, row = lane % w, lane // w % (self.hl * self.nr)
        last_row = self.hl * self.nr - 1
        return (lane, col > 0, col < w - 1, row > 0, row < last_row)


def fetched(pairs, sems):
    copies = [pltpu.make_async_copy(src, dst, sems.at[k]) for k, (src, dst) in enumerate(pairs)]
    for copy in copies:
        copy.start()
    return copies


def own_place(plan):
    pair, member, r = lax.axis_index("pairs"), lax.axis_index("member"), lax.axis_index("rows")
    return pair, member, r, r * plan.slice_width + (2 * pair + member) * plan.sub


def fetch_kernel(g_hbm, coarse_hbm, fine_hbm, g_ref, coarse_ref, fine_ref, sems):
    for copy in fetched([(fine_hbm, fine_ref), (coarse_hbm, coarse_ref), (g_hbm, g_ref)], sems):
        copy.wait()


def pack_kernel(plan, g_ref, coarse_ref, fine_ref, out_ref, later_ref):
    sub, chunks, local = plan.sub, plan.chunks, plan.local
    shape = (2 * local, 2 * 128)
    lane = lanes_at((1, 2 * 128), 1)
    repeated = one_hot(lanes_at(shape, 0) == lane % local + lane // 128 * local)
    shape = (plan.channels, 128)
    quarter = lanes_at(shape, 0) // 8 % 4 == lanes_at(shape, 1) // local
    orders = jnp.concatenate([pixel_order(plan, swapped) for swapped in (False, True)], axis=1)
    acts = fine_ref[...]
    halves = one_hot_dot(acts, orders, ((0,), (0,))).astype(jnp.bfloat16)
    halves = [halves[:, :128], halves[:, 128:]]
    values = acts.astype(jnp.float32)
    one = jnp.sum(values, axis=0, keepdims=True)
    two = jnp.sum(values * values, axis=0, keepdims=True)
    stats = terms(one, 3) + terms(two, 3) + [jnp.zeros_like(one)] * 2
    stats = jnp.concatenate(stats, axis=0).astype(jnp.bfloat16)
    small = one_hot_dot(jnp.concatenate([coarse_ref[...], g_ref[...]], axis=0), repeated, ((0,), (0,)))
    for k, at in enumerate((plan.packed_at, plan.cot_at)):
        rows_of = jnp.where(quarter, small[:, k * 128 : (k + 1) * 128], 0.0).reshape(plan.count, 4, 8, 128)
        out_ref[:, at : at + 8, :] = jnp.sum(rows_of, axis=1).astype(jnp.bfloat16)
    low = lanes_at((sub, 128), 1) < 64
    for s_r in range(plan.nr):
        for s_f in range(plan.nf):
            dest = s_r * plan.nf + s_f
            first, half = s_r * plan.slice_width + s_f // 2 * 2 * sub, s_f % 2
            for k in range(chunks // 2):
                at = (half * chunks // 2 + k) * 128
                out_ref[dest, k * local : (k + 1) * local, :] = g_ref[:, at : at + 128]
            upper, lower = halves[half][first : first + sub], halves[1 - half][first + sub : first + 2 * sub]
            later_ref[dest, 0:sub, :] = jnp.where(low, upper, lower)
            later_ref[dest, sub:, :] = stats[:, s_r * 128 : (s_r + 1) * 128]


def by_frame_device(plan, got_ref, at, height):
    return jnp.concatenate(
        [
            jnp.concatenate(
                [got_ref[r * plan.nf + f, at : at + height, :] for r in range(plan.nr)], axis=1
            )
            for f in range(plan.nf)
        ],
        axis=0,
    )


def in_places(plan, merged, height):
    width = plan.tl * plan.image
    return [
        jnp.concatenate(
            [merged[f * height : (f + 1) * height, k * width : (k + 1) * width] for f in range(plan.nf)],
            axis=1,
        )
        for k in range(4)
    ]


def coarse_kernel(
    plan,
    got_ref,
    weights,
    gain_c,
    bias_c,
    gain_f,
    bias_f,
    mine_ref,
    sent_ref,
    held_ref,
    inv_ref,
    columns,
    fine_order,
    by_column,
    order,
    source,
    conv_ref,
):
    sub, nr, nf, cells, tl, local = plan.sub, plan.nr, plan.nf, plan.cells, plan.tl, plan.local
    wide, depth = 2 * sub, plan.channels // 2
    pair, member, r, base = own_place(plan)
    first = r * plan.slice_width + pair * wide
    columns[0, 0:sub, :] = jnp.broadcast_to(own_column(gain_c[...], base, sub), (sub, 128))
    columns[1, 0:sub, :] = jnp.broadcast_to(own_column(bias_c[...], base, sub), (sub, 128))
    columns[2] = jnp.broadcast_to(own_column(gain_f[...], first, wide), (wide, 128))
    columns[3] = jnp.broadcast_to(own_column(bias_f[...], first, wide), (wide, 128))
    order[...] = merged_order(plan.nr, 4, plan.tl, plan.cells)
    fine_order[...] = merged_order(plan.nr, 8, plan.tl, plan.cells // 2)
    by_column[...] = column_order(plan)
    both = pl.ds(pl.multiple_of(pair * wide, wide), wide)
    half = pl.ds(pl.multiple_of(member * depth, depth), depth)
    for s_f in range(nf):
        for s_r in range(nr):
            for t in range(tl):
                at = (s_f * tl + t) * plan.image + s_r * cells
                for k in range(plan.chunks // 2):
                    source[at : at + cells, k * 128 : (k + 1) * 128] = got_ref[
                        s_r * nf + s_f, k * local + t * cells : k * local + (t + 1) * cells, :
                    ]
    source[plan.places :, :] = jnp.zeros((2 * plan.image, depth), jnp.bfloat16)
    products = sum(
        one_hot_dot(
            weights[9 * k : 9 * k + 9, both, half].reshape(9 * wide, depth),
            source[(2 - k) * plan.image : (2 - k) * plan.image + plan.places, :],
            ((1,), (1,)),
        )
        for k in range(3)
    )
    small = [by_frame_device(plan, got_ref, at, 8) for at in (plan.packed_at, plan.cot_at)]
    merged = one_hot_dot(jnp.concatenate(small, axis=0), order[...], ((1,), (0,)))
    rows_of = 8 * nf
    values, cot = [
        jnp.concatenate(in_places(plan, merged[k * rows_of : (k + 1) * rows_of], 8), axis=0) for k in range(2)
    ]
    gain, bias = columns[0][0:sub, 0:1], columns[1][0:sub, 0:1]
    entries = plan.places * plan.group_width
    mean, inv_std = statistics(total([values]), total([values * values]), entries, plan.group_width)
    (normed,), (slope,) = normalised([values], gain, bias, mean, inv_std)
    held_ref[0], held_ref[1], held_ref[2] = normed, slope, cot
    inv_ref[...] = jnp.broadcast_to(inv_std, (sub, 128))
    lane, has_left, has_right, has_up, has_down = plan.place_masks(plan.w)
    by_col = []
    for col in range(3):
        parts = [products[(3 * row + col) * wide : (3 * row + col + 1) * wide] for row in range(3)]
        by_col.append(parts[1] + moved(parts[0], plan.w, has_down) + moved(parts[2], -plan.w, has_up))
    conv_ref[...] = by_col[1] + moved(by_col[0], 1, has_right) + moved(by_col[2], -1, has_left)
    mine_ref[...] = conv_ref[pl.ds(pl.multiple_of(member * sub, sub), sub), :]
    theirs = conv_ref[pl.ds(pl.multiple_of((1 - member) * sub, sub), sub), :]
    sent_ref[...] = theirs.astype(jnp.bfloat16)


def quarter_kernel(plan, mine_ref, both_ref, held_ref, inv_ref, columns, by_column, later_ref, out_ref, sums_ref):
    sub = plan.sub
    _, member, _, _ = own_place(plan)
    conv = mine_ref[...] + both_ref[1 - member].astype(jnp.float32)
    normed, slope, cot = held_ref[0], held_ref[1], held_ref[2]
    gain, inv_std = columns[0][0:sub, 0:1], inv_ref[:, 0:1]
    entries = plan.places * plan.group_width
    pre = conv * slope
    one, two = total([pre]), total([pre * normed])
    group_one = in_groups(gain * one, plan.group_width) / entries
    group_two = in_groups(gain * two, plan.group_width) / entries
    grad = cot + inv_std * (gain * pre - group_one - normed * group_two)
    quartered = (grad * 0.25).astype(jnp.bfloat16)
    sent = one_hot_dot(quartered, by_column[...], ((1,), (0,))).astype(jnp.bfloat16)
    low = lanes_at((sub // 2, 128), 1) < 64
    for half in range(2):
        at = half * 256
        border = sent[:, 512 + half * 128 : 640 + half * 128]
        border = jnp.where(low, border[: sub // 2], border[sub // 2 :])
        for dest in range(half, plan.count, 2):
            out_ref[dest, 0:sub, :] = sent[:, at : at + 128]
            out_ref[dest, sub : 2 * sub, :] = sent[:, at + 128 : at + 256]
            out_ref[dest, 2 * sub : plan.acts_at, :] = border
            out_ref[dest, plan.acts_at :, :] = later_ref[dest]
    sums_ref[...] = jnp.concatenate([as_row(one), as_row(two)], axis=0)


def halves_at(plan, merged):
    sub = plan.sub
    turned = jnp.concatenate([pltpu.roll(merged[:, k * 128 : (k + 1) * 128], 64, 1) for k in range(4)], axis=1)
    low = lanes_at((sub, 128), 1) < 64
    parts = []
    for pq in range(4):
        groups = []
        for group in range(2):
            e = 4 * group + pq
            at = e // 2 * 128
            strips = []
            for m in range(plan.nf // 2):
                first, second = slice(2 * m * sub, (2 * m + 1) * sub), slice((2 * m + 1) * sub, (2 * m + 2) * sub)
                if e % 2 == 0:
                    strips.append(jnp.where(low, merged[first, at : at + 128], turned[second, at : at + 128]))
                else:
                    strips.append(jnp.where(low, turned[first, at : at + 128], merged[second, at : at + 128]))
            groups.append(jnp.concatenate(strips, axis=1))
        parts.append(jnp.concatenate(groups, axis=0))
    return parts


def halves_from(plan, parts):
    sub = plan.sub
    low = lanes_at((sub, 128), 1) < 64
    down = []
    for f in range(plan.nf):
        across = []
        for v in range(4):
            pair = []
            for e in (2 * v, 2 * v + 1):
                group, pq = e // 4, e % 4
                strip = parts[pq][group * sub : (group + 1) * sub, f // 2 * 128 : (f // 2 + 1) * 128]
                pair.append(strip if e % 2 == f % 2 else pltpu.roll(strip, 64, 1))
            across.append(jnp.where(low, pair[0], pair[1]))
        down.append(jnp.concatenate(across, axis=1))
    return jnp.concatenate(down, axis=0)


def fine_kernel(
    plan, got_ref, columns, order, sums_ref, weights, out_ref, source, border
):
    sub, nr, nf, wide = plan.sub, plan.nr, plan.nf, 2 * plan.sub
    pair, member, r, _ = own_place(plan)
    both = pl.ds(pl.multiple_of(pair * wide, wide), wide)
    w = plan.w // 2
    lines = plan.places // plan.w
    places = lines * w
    for k in range(2):
        source[:, k * 128 : (k + 1) * 128] = got_ref[:, k * sub : (k + 1) * sub, :].reshape(plan.channels, 128)
    packed = got_ref[:, wide : wide + sub // 2, :].reshape(plan.count * sub // 2, 128)
    shape = (128, places)
    beside = lanes_at(shape, 1) == lanes_at(shape, 0) % lines * w + (1 - member) * (w - 1)
    for k in range(2):
        here = one_hot(beside & (lanes_at(shape, 0) // lines == k))
        found = one_hot_dot(packed, here, ((1,), (0,))).astype(jnp.bfloat16)
        for s in range(plan.count):
            border[s * sub + k * (sub // 2) : s * sub + (k + 1) * (sub // 2), :] = found[
                s * (sub // 2) : (s + 1) * (sub // 2)
            ]
    image = plan.image // 2
    sums, extras = 0.0, 0.0
    for k in (2, 1, 0):
        here, beside = source[...], border[...]
        if k < 2:
            shift = (2 - k) * image
            inside = lanes_at((1, places), 1) < places - shift
            here, beside = [
                jnp.where(inside, pltpu.roll(part, places - shift, 1), jnp.zeros_like(part)) for part in (here, beside)
            ]
        sums = sums + one_hot_dot(
            weights[9 * k : 9 * k + 9, both, :].reshape(9 * wide, plan.channels), here, ((1,), (0,))
        )
        facing = jnp.concatenate([weights[9 * k + 3 * row + 2 * member, both, :] for row in range(3)], axis=0)
        extras = extras + one_hot_dot(facing, beside, ((1,), (0,)))
    merged = one_hot_dot(by_frame_device(plan, got_ref, plan.acts_at, sub), order[...], ((1,), (0,)))
    parts = halves_at(plan, merged)
    stats = sum(got_ref[s, plan.stats_at : plan.stats_at + 8, :].astype(jnp.float32) for s in range(plan.count))
    entries = 4 * plan.places * plan.group_width
    one = own_column(stats[0:1] + stats[1:2] + stats[2:3], pair * wide, wide)
    two = own_column(stats[3:4] + stats[4:5] + stats[5:6], pair * wide, wide)
    mean, inv_std = statistics(one, two, entries, plan.group_width)
    gain, bias = columns[2][:, 0:1], columns[3][:, 0:1]
    normed, slope = normalised(parts, gain, bias, mean, inv_std)
    lane, has_left, has_right, has_up, has_down = plan.place_masks(w)
    right, left = (1 - member).astype(jnp.float32), member.astype(jnp.float32)
    by_row = []
    for row in range(3):
        a, b, c = [sums[(3 * row + col) * wide : (3 * row + col + 1) * wide] for col in range(3)]
        extra = extras[row * wide : (row + 1) * wide]
        by_row.append(
            (a + b + moved(c, -1, has_left) + left * extra, moved(a, 1, has_right) + b + c + right * extra)
        )
    convs = [by_row[0][q] + by_row[1][q] + moved(by_row[2][q], -w, has_up) for q in range(2)]
    convs += [moved(by_row[0][q], w, has_down) + by_row[1][q] + by_row[2][q] for q in range(2)]
    pre = [conv * part for conv, part in zip(convs, slope)]
    one = total(pre)
    two = total([a * b for a, b in zip(pre, normed)])
    cot = source[pl.ds(pl.multiple_of(r * plan.slice_width + pair * wide, wide), wide), :].astype(jnp.float32)
    scale = inv_std * gain
    stacked = halves_from(plan, [cot + scale * part for part in pre]).astype(jnp.bfloat16)
    sent = one_hot_dot(stacked, order[...], ((1,), (1,))).astype(jnp.bfloat16)
    coarse = sums_ref[0:1] + pltpu.roll(sums_ref[1:2], sub, 1)
    coded = (
        terms(as_row(one) + pltpu.roll(as_row(two), 64, 1), 2)
        + terms(coarse, 2)
        + terms(as_row(inv_std) + pltpu.roll(as_row(mean), 64, 1), 3)
    )
    coded = jnp.concatenate(coded + [jnp.zeros_like(coarse)], axis=0).astype(jnp.bfloat16)
    for s_r in range(nr):
        for s_f in range(nf):
            out_ref[s_f * nr + s_r, 0:sub, :] = sent[s_f * sub : (s_f + 1) * sub, s_r * 128 : (s_r + 1) * 128]
            out_ref[s_f * nr + s_r, sub : sub + 8, :] = coded


def spread_kernel(plan, got_ref, acts_ref, gain_ref, out_ref, sums_ref):
    sub, nr, nf = plan.sub, plan.nr, plan.nf
    low = lanes_at((sub, 128), 1) < 64
    low_row = lanes_at((1, 128), 1) < 64
    first_row = lanes_at((1, 128), 1) < sub
    source = []
    fine, coarse, moments = [[], []], [[], []], [[], []]
    for s_r in range(nr):
        ones, twos, c_ones, c_twos, invs, means = [], [], 0.0, 0.0, [], []
        for pair in range(nf // 2):
            at = 2 * pair * nr + s_r
            left, right = [got_ref[at + k * nr, 0:sub, :].astype(jnp.float32) for k in range(2)]
            source.append(jnp.where(low, left, pltpu.roll(right, 64, 1)))
            source.append(jnp.where(low, pltpu.roll(left, 64, 1), right))
            coded = [got_ref[at + k * nr, sub : sub + 8, :].astype(jnp.float32) for k in range(2)]
            sums = coded[0][0:1] + coded[0][1:2] + coded[1][0:1] + coded[1][1:2]
            ones.append(sums if pair == 0 else pltpu.roll(sums, 64, 1))
            twos.append(pltpu.roll(sums, 64, 1) if pair == 0 else sums)
            both = coded[0][4:5] + coded[0][5:6] + coded[0][6:7]
            invs.append(both if pair == 0 else pltpu.roll(both, 64, 1))
            means.append(pltpu.roll(both, 64, 1) if pair == 0 else both)
            for k in range(2):
                sums = coded[k][2:3] + coded[k][3:4]
                to = (2 * pair + k) * sub
                c_one = jnp.where(first_row, sums, 0.0)
                c_two = jnp.where(first_row, pltpu.roll(sums, 128 - sub, 1), 0.0)
                c_ones = c_ones + (pltpu.roll(c_one, to, 1) if to else c_one)
                c_twos = c_twos + (pltpu.roll(c_two, to, 1) if to else c_two)
        fine[0].append(jnp.where(low_row, ones[0], ones[1]))
        fine[1].append(jnp.where(low_row, twos[0], twos[1]))
        moments[0].append(jnp.where(low_row, invs[0], invs[1]))
        moments[1].append(jnp.where(low_row, means[0], means[1]))
        coarse[0].append(c_ones)
        coarse[1].append(c_twos)
    one, two, inv_std, mean, c_one, c_two = [jnp.concatenate(part, axis=1) for part in fine + moments + coarse]
    source = jnp.concatenate(source, axis=0).astype(jnp.bfloat16)
    result = one_hot_dot(pixel_order(plan, False), source, ((1,), (1,)))
    gain = gain_ref[...]
    entries = 4 * plan.places * plan.group_width
    group_one = in_lane_groups(gain * one, plan.group_width) / entries
    group_two = in_lane_groups(gain * two, plan.group_width) / entries
    normed = (acts_ref[...].astype(jnp.float32) - mean) * inv_std
    out_ref[...] = (result - inv_std * (group_one + normed * group_two)).astype(jnp.bfloat16)
    sums_ref[...] = jnp.concatenate([one, two, c_one, c_two] + [jnp.zeros_like(one)] * 4, axis=0)


def total_kernel(scales, both_ref, result_ref, result_hbm, out_hbms, rows_ref, sems):
    copies = fetched([(result_ref, result_hbm)], sems)
    rows = sum(both_ref[k] for k in range(both_ref.shape[0]))
    for k in range(4):
        rows_ref[k] = rows[k : k + 1] * scales[k]
    for k in range(4):
        copies.append(pltpu.make_async_copy(rows_ref.at[k], out_hbms[k], sems.at[k + 1]))
        copies[-1].start()
    for copy in copies:
        copy.wait()


def in_vmem(count):
    return [pl.BlockSpec(memory_space=pltpu.VMEM)] * count


def in_hbm(count):
    return [pl.BlockSpec(memory_space=pltpu.HBM)] * count


def kept(array):
    return pltpu.with_memory_space_constraint(array, pltpu.HBM)


def shape_of(shape, kind):
    return jax.ShapeDtypeStruct(shape, kind)


LIMIT = pltpu.CompilerParams(vmem_limit_bytes=40 * 1024 * 1024)
COST = pl.CostEstimate(flops=2_000_000_000, bytes_accessed=4_000_000, transcendentals=0)


def fast_shards(
    plan,
    acts_fine,
    acts_coarse,
    grad_coarse,
    gain_fine,
    bias_fine,
    kernel_fine,
    gain_coarse,
    bias_coarse,
    kernel_coarse,
):
    nd = lax.axis_size("dp")
    count, sub, channels, places, local = plan.count, plan.sub, plan.channels, plan.places, plan.local
    f32, bf16 = jnp.float32, jnp.bfloat16
    rows = [part.reshape(1, channels) for part in (gain_coarse, bias_coarse, gain_fine, bias_fine)]
    places_of = ((local, channels), (local, channels), (4 * local, channels))
    fetched_of = pl.pallas_call(
        fetch_kernel,
        out_shape=tuple(pltpu.VMEM(shape, bf16) for shape in places_of),
        in_specs=in_hbm(3),
        out_specs=tuple(in_vmem(3)),
        scratch_shapes=[pltpu.SemaphoreType.DMA((3,))],
        compiler_params=LIMIT,
    )(*[kept(part.reshape(shape)) for part, shape in zip((grad_coarse, acts_coarse, acts_fine), places_of)])
    acts = fetched_of[2]
    packed, later = pl.pallas_call(
        functools.partial(pack_kernel, plan),
        out_shape=(shape_of((count, plan.block_rows, 128), bf16), shape_of((count, sub + 8, 128), bf16)),
        in_specs=in_vmem(3),
        out_specs=tuple(in_vmem(2)),
        compiler_params=LIMIT,
        cost_estimate=COST,
    )(*fetched_of)
    got = lax.all_to_all(packed, BLOCK, 0, 0)
    mine, theirs, held, inv_std, columns, fine_order, by_column = pl.pallas_call(
        functools.partial(coarse_kernel, plan),
        out_shape=(
            shape_of((sub, places), f32),
            shape_of((sub, places), bf16),
            shape_of((3, sub, places), f32),
            shape_of((sub, 128), f32),
            shape_of((4, 2 * sub, 128), f32),
            shape_of((4 * plan.nr * local, 4 * plan.nr * local), bf16),
            shape_of((places, places + places // 2), bf16),
        ),
        in_specs=in_vmem(6),
        out_specs=tuple(in_vmem(7)),
        scratch_shapes=[
            pltpu.VMEM((4 * plan.nr * local, 4 * plan.nr * local), bf16),
            pltpu.VMEM((places + 2 * plan.image, channels // 2), bf16),
            pltpu.VMEM((2 * sub, places), f32),
        ],
        compiler_params=LIMIT,
        cost_estimate=COST,
    )(got, kernel_coarse, *rows)
    both = lax.all_gather(theirs, "member")
    quartered, coarse_sums = pl.pallas_call(
        functools.partial(quarter_kernel, plan),
        out_shape=(shape_of((count, plan.stats_at + 8, 128), bf16), shape_of((2, 128), f32)),
        in_specs=in_vmem(7),
        out_specs=tuple(in_vmem(2)),
        compiler_params=LIMIT,
        cost_estimate=COST,
    )(mine, both, held, inv_std, columns, by_column, later)
    spread = lax.all_to_all(quartered, BLOCK, 0, 0)
    sent = pl.pallas_call(
        functools.partial(fine_kernel, plan),
        out_shape=shape_of((count, sub + 8, 128), bf16),
        in_specs=in_vmem(5),
        out_specs=in_vmem(1)[0],
        scratch_shapes=[
            pltpu.VMEM((channels, places // 2), bf16),
            pltpu.VMEM((channels, places // 2), bf16),
        ],
        compiler_params=LIMIT,
        cost_estimate=COST,
    )(spread, columns, fine_order, coarse_sums, kernel_fine)
    back = lax.all_to_all(sent, BACK_BLOCK, 0, 0)
    cells = nd * places
    fine_scale, coarse_scale = 1.0 / math.sqrt(4 * cells), 1.0 / math.sqrt(cells)
    out, sums = pl.pallas_call(
        functools.partial(spread_kernel, plan),
        out_shape=(pltpu.VMEM((4 * local, channels), bf16), shape_of((8, channels), f32)),
        in_specs=in_vmem(3),
        out_specs=tuple(in_vmem(2)),
        compiler_params=LIMIT,
        cost_estimate=COST,
    )(back, acts, rows[2])
    both = lax.all_gather(sums, "dp")
    out, sums = pl.pallas_call(
        functools.partial(total_kernel, (fine_scale, fine_scale, coarse_scale, coarse_scale)),
        out_shape=(pltpu.HBM((4 * local, channels), bf16), (pltpu.HBM((1, channels), f32),) * 4),
        in_specs=in_vmem(2),
        out_specs=(in_hbm(1)[0], tuple(in_hbm(4))),
        scratch_shapes=[pltpu.VMEM((4, 1, channels), f32), pltpu.SemaphoreType.DMA((5,))],
        compiler_params=LIMIT,
        cost_estimate=COST,
    )(both, out)
    bias_f, gain_f, bias_c, gain_c = [part.reshape(channels) for part in sums]
    return out.reshape(acts_fine.shape), gain_f, bias_f, gain_c, bias_c


def solution(mesh):
    def function(*arrays):
        local = [size // mesh.shape[axis] for size, axis in zip(arrays[1].shape, ("dp", "frames", "rows"))]
        sizes = (mesh.shape["frames"], mesh.shape["rows"])
        plan = Plan(sizes, (*local[1:], *arrays[1].shape[3:]), arrays[5].shape[1] // mesh.shape["rows"])
        if plan.fits:
            split = (mesh.shape["dp"], plan.nf // 2, 2, plan.nr)
            used = jax.sharding.Mesh(mesh.devices.reshape(split), ("dp", "pairs", "member", "rows"))
            shards, frames = functools.partial(fast_shards, plan), ("pairs", "member")
        else:
            used, shards, frames = mesh, plain_shards, "frames"
        blocks, kernel = P("dp", frames, "rows", None, None), P(None, "rows", None)
        in_specs = (blocks, blocks, blocks, P(), P(), kernel, P(), P(), kernel)
        out_specs = (blocks, P(), P(), P(), P())
        mapped = jax.shard_map(shards, mesh=used, in_specs=in_specs, out_specs=out_specs, check_vma=False)
        return mapped(*arrays)

    return function
```

```python
import functools
import math

import jax
import jax.numpy as jnp
from jax import lax
from jax.experimental import pallas as pl
from jax.experimental.pallas import tpu as pltpu
from jax.sharding import PartitionSpec as P

GROUPS = 32
EPSILON = 1e-06
BLOCK = ("rows", "pairs", "member")
BACK_BLOCK = ("pairs", "member", "rows")
PLAIN_BLOCK = ("frames", "rows")


def plain_everyone(block, count):
    copies = jnp.broadcast_to(block[None], (count,) + block.shape)
    return lax.all_to_all(copies, PLAIN_BLOCK, 0, 0)


def ahead(field, axis, distance):
    size = field.shape[axis]
    if distance == 0:
        return field
    widths = [(0, 0)] * field.ndim
    if distance > 0:
        widths[axis] = (0, distance)
        kept = lax.slice_in_dim(field, distance, size, axis=axis)
    else:
        widths[axis] = (-distance, 0)
        kept = lax.slice_in_dim(field, 0, size + distance, axis=axis)
    return jnp.pad(kept, widths)


def tap_products(source, kernel):
    sub = kernel.shape[1]
    frames, rows, cols, channels = source.shape
    products = lax.dot_general(
        kernel.reshape(27 * sub, channels),
        source.reshape(frames * rows * cols, channels),
        (((1,), (1,)), ((), ())),
        preferred_element_type=jnp.float32,
    ).reshape(3, 3, 3, sub, frames, rows, cols)
    return sum(ahead(products[depth], 3, 2 - depth) for depth in range(3))


def coarse_conv(source, kernel):
    spatial = tap_products(source, kernel)
    total = 0.0
    for row in range(3):
        part = sum(ahead(spatial[row, col], 3, 1 - col) for col in range(3))
        total = total + ahead(part, 2, 1 - row)
    return total


def fine_conv(source, kernel):
    spatial = tap_products(source, kernel)
    result = []
    for p in range(2):
        rows_of = []
        for q in range(2):
            total = 0.0
            for row in range(3):
                part = sum(ahead(spatial[row, col], 3, (q + 1 - col) // 2) for col in range(3))
                total = total + ahead(part, 2, (p + 1 - row) // 2)
            rows_of.append(total)
        result.append(jnp.stack(rows_of, 1))
    return jnp.stack(result, 1)


def group_total(sums, group_width):
    sub = sums.shape[-1]
    if sub % group_width == 0:
        grouped = jnp.sum(sums.reshape(-1, sub // group_width, group_width), axis=-1)
        return jnp.repeat(grouped, group_width, axis=-1)
    spread = jnp.moveaxis(lax.all_gather(sums, "frames"), 0, 1).reshape(sums.shape[0], -1, group_width)
    mine = lax.axis_index("frames") * sub // group_width
    grouped = lax.dynamic_index_in_dim(jnp.sum(spread, -1), mine, 1)
    return jnp.broadcast_to(grouped, sums.shape)


def level(acts, conv_grad, cotangent, gain, bias, group_width):
    sub = acts.shape[0]
    places = acts.size // sub
    values = acts.astype(jnp.float32).reshape(sub, places)
    conv_grad = conv_grad.reshape(sub, places)
    entries = places * group_width
    moments = group_total(
        jnp.stack([jnp.sum(values, 1), jnp.sum(values * values, 1)]), group_width
    ) / entries
    mean = moments[0]
    inv_std = lax.rsqrt(moments[1] - mean * mean + EPSILON)
    normed = (values - mean[:, None]) * inv_std[:, None]
    preact = gain[:, None] * normed + bias[:, None]
    squash = jax.nn.sigmoid(preact)
    pre_grad = conv_grad * squash * (1.0 + preact * (1.0 - squash))
    sums = jnp.stack([jnp.sum(pre_grad, 1), jnp.sum(pre_grad * normed, 1)])
    terms = group_total(sums * gain, group_width) / entries
    grad = cotangent.reshape(sub, places) + inv_std[:, None] * (
        gain[:, None] * pre_grad - terms[0][:, None] - normed * terms[1][:, None]
    )
    return grad, sums


def plain_shards(
    acts_fine,
    acts_coarse,
    grad_coarse,
    gain_fine,
    bias_fine,
    kernel_fine,
    gain_coarse,
    bias_coarse,
    kernel_coarse,
):
    nf, nr, nd = lax.axis_size("frames"), lax.axis_size("rows"), lax.axis_size("dp")
    count = nf * nr
    channels = acts_fine.shape[-1]
    slice_width = kernel_fine.shape[1]
    sub = slice_width // nf
    group_width = channels // GROUPS
    tl, hl, w = acts_coarse.shape[1:4]
    frames, rows = tl * nf, hl * nr
    f, r = lax.axis_index("frames"), lax.axis_index("rows")

    gathered = plain_everyone(grad_coarse[0], count)
    source = (
        gathered.reshape(nf, nr, tl, hl, w, channels)
        .transpose(0, 2, 1, 3, 4, 5)
        .reshape(frames, rows, w, channels)
    )
    coarse_in = acts_coarse[0].reshape(tl, hl, w, nr, nf, sub).transpose(4, 3, 5, 0, 1, 2)
    coarse_in = lax.all_to_all(coarse_in.reshape(count, sub, tl * hl * w), PLAIN_BLOCK, 0, 0)
    fine_in = acts_fine[0].reshape(tl, hl, 2, w, 2, nr, nf, sub).transpose(6, 5, 7, 2, 4, 0, 1, 3)
    fine_in = lax.all_to_all(fine_in.reshape(count, sub, 4 * tl * hl * w), PLAIN_BLOCK, 0, 0)

    def mine(vector):
        return lax.dynamic_slice_in_dim(vector, r * slice_width + f * sub, sub)

    def own(kernel):
        return lax.dynamic_slice_in_dim(kernel, f * sub, sub, axis=1)

    coarse_vals = (
        coarse_in.reshape(nf, nr, sub, tl, hl, w).transpose(2, 0, 3, 1, 4, 5).reshape(sub, frames, rows, w)
    )
    cot = lax.dynamic_slice_in_dim(source, r * slice_width + f * sub, sub, axis=3)
    cot = cot.astype(jnp.float32).transpose(3, 0, 1, 2)
    conv = coarse_conv(source, own(kernel_coarse))
    coarse_grad, coarse_sums = level(
        coarse_vals, conv, cot, mine(gain_coarse), mine(bias_coarse), group_width
    )
    quartered = (coarse_grad * 0.25).astype(jnp.bfloat16)
    spread = plain_everyone(quartered, count)
    source_fine = (
        spread.reshape(nf, nr, sub, frames, rows, w)
        .transpose(3, 4, 5, 1, 0, 2)
        .reshape(frames, rows, w, channels)
    )
    conv = fine_conv(source_fine, own(kernel_fine))
    fine_vals = (
        fine_in.reshape(nf, nr, sub, 2, 2, tl, hl, w)
        .transpose(2, 3, 4, 0, 5, 1, 6, 7)
        .reshape(sub, 2, 2, frames, rows, w)
    )
    cot = jnp.broadcast_to(
        quartered.astype(jnp.float32).reshape(sub, 1, 1, frames, rows, w), conv.shape
    )
    fine_grad, fine_sums = level(
        fine_vals, conv, cot, mine(gain_fine), mine(bias_fine), group_width
    )
    back = (
        fine_grad.astype(jnp.bfloat16)
        .reshape(sub, 2, 2, nf, tl, nr, hl, w)
        .transpose(3, 5, 0, 1, 2, 4, 6, 7)
        .reshape(count, sub, 4 * tl * hl * w)
    )
    sums = plain_everyone(jnp.concatenate([fine_sums, coarse_sums]), count)
    back = lax.all_to_all(back, PLAIN_BLOCK, 0, 0)
    out = (
        back.reshape(nf, nr, sub, 2, 2, tl, hl, w)
        .transpose(5, 6, 3, 7, 4, 1, 0, 2)
        .reshape(1, tl, 2 * hl, 2 * w, channels)
    )
    sums = sums.reshape(nf, nr, 4, sub).transpose(2, 1, 0, 3).reshape(4, channels)
    totals = lax.psum(sums, "dp")
    cells = nd * frames * rows * w
    scale_fine = 1.0 / jnp.sqrt(jnp.float32(4 * cells))
    scale_coarse = 1.0 / jnp.sqrt(jnp.float32(cells))
    return (
        out,
        totals[1] * scale_fine,
        totals[0] * scale_fine,
        totals[3] * scale_coarse,
        totals[2] * scale_coarse,
    )


def lanes_at(shape, axis):
    return lax.broadcasted_iota(jnp.int32, shape, axis)


def one_hot(found):
    return found.astype(jnp.float32).astype(jnp.bfloat16)


def pixel_order(plan, swapped):
    tl, hl, w = plan.tl, plan.hl, plan.w // 2
    size = 4 * plan.local
    lane = lanes_at((1, size), 1)
    j, i, t = lane % w, lane // w % hl, lane // (w * hl) % tl
    q, p = lane // (w * hl * tl) % 2, lane // (2 * w * hl * tl) % 2
    half = lane // (4 * w * hl * tl)
    if swapped:
        half = 1 - half
    pixel = (t * 2 * hl + 2 * i + p) * 4 * w + 2 * (half * w + j) + q
    return one_hot(lanes_at((size, size), 0) == pixel)


def merged_order(nr, outer, tl, cells):
    size = nr * outer * tl * cells
    lane = lanes_at((1, size), 1)
    cell, dev = lane % cells, lane // cells % nr
    t, o = lane // (cells * nr) % tl, lane // (cells * nr * tl)
    return one_hot(lanes_at((size, size), 0) == ((dev * outer + o) * tl + t) * cells + cell)


def column_order(plan):
    w = plan.w // 2
    lines = plan.places // plan.w
    lane = lanes_at((1, 4 * lines * w + 4 * lines), 1)
    inner = lane % (lines * w)
    place = inner // w * plan.w + lane // (lines * w) * w + inner % w
    past = lane - 2 * lines * w
    border = past % lines * plan.w + jnp.where(past < 2 * lines, w, w - 1)
    wanted = jnp.where(past >= 0, border, place)
    shape = (plan.places, 2 * lines * w + 4 * lines)
    return one_hot(lanes_at(shape, 0) == wanted[:, : shape[1]])


def one_hot_dot(a, b, dims):
    return lax.dot_general(a, b, (dims, ((), ())), preferred_element_type=jnp.float32)


def moved(field, distance, kept):
    size = field.shape[1]
    return jnp.where(kept, pltpu.roll(field, (-distance) % size, 1), 0.0)


def own_column(row, base, sub):
    shape = (sub, row.shape[1])
    mine = lanes_at(shape, 1) == lanes_at(shape, 0) + base
    return jnp.sum(jnp.where(mine, row, 0.0), axis=1, keepdims=True)


def as_row(column):
    shape = (column.shape[0], 128)
    here = lanes_at(shape, 1) == lanes_at(shape, 0)
    return jnp.sum(jnp.where(here, column, 0.0), axis=0, keepdims=True)


def terms(value, count):
    found = []
    for _ in range(count):
        found.append(value.astype(jnp.bfloat16).astype(jnp.float32))
        value = value - found[-1]
    return found


def in_groups(column, group_width):
    sub = column.shape[0]
    grouped = jnp.sum(column.reshape(sub // group_width, group_width, 1), axis=1, keepdims=True)
    return jnp.broadcast_to(grouped, (sub // group_width, group_width, 1)).reshape(sub, 1)


def in_lane_groups(row, group_width):
    lane = lanes_at(row.shape, 1)
    size = row.shape[1]
    step = 1
    while step < group_width:
        up, down = pltpu.roll(row, size - step, 1), pltpu.roll(row, step, 1)
        row = row + jnp.where(lane // step % 2 == 0, up, down)
        step *= 2
    return row


def total(parts):
    return sum(jnp.sum(part, axis=1, keepdims=True) for part in parts)


def statistics(one, two, entries, group_width):
    mean = in_groups(one, group_width) / entries
    square = in_groups(two, group_width) / entries
    return mean, lax.rsqrt(square - mean * mean + EPSILON)


def normalised(parts, gain, bias, mean, inv_std):
    normed, slope = [], []
    for part in parts:
        unit = (part - mean) * inv_std
        preact = gain * unit + bias
        squash = 0.5 + 0.5 * jnp.tanh(0.5 * preact)
        normed.append(unit)
        slope.append(squash * (1.0 + preact * (1.0 - squash)))
    return normed, slope


class Plan:
    def __init__(self, mesh_sizes, acts_coarse, slice_width):
        self.nf, self.nr = mesh_sizes
        self.count = self.nf * self.nr
        self.tl, self.hl, self.w, self.channels = acts_coarse
        self.slice_width = slice_width
        self.sub = slice_width // self.nf
        self.cells = self.hl * self.w
        self.local = self.tl * self.cells
        self.image = self.cells * self.nr
        self.frames = self.tl * self.nf
        self.places = self.frames * self.image
        self.group_width = self.channels // GROUPS
        self.chunks = self.channels // 128
        self.acts_at = self.chunks // 2 * self.local
        self.packed_at = self.acts_at + self.sub
        self.cot_at = self.packed_at + 8
        self.block_rows = self.cot_at + 8
        self.fits = (
            self.sub == 32
            and self.slice_width == 128
            and self.group_width == 16
            and self.cells == 16
            and self.w == 8
            and self.tl == 2
            and self.nr == 4
            and self.nf == 4
            and self.slice_width * self.nr == self.channels
        )

    def place_masks(self, w):
        lane = lanes_at((1, self.places // self.w * w), 1)
        col, row = lane % w, lane // w % (self.hl * self.nr)
        last_row = self.hl * self.nr - 1
        return (lane, col > 0, col < w - 1, row > 0, row < last_row)


def fetched(pairs, sems):
    copies = [pltpu.make_async_copy(src, dst, sems.at[k]) for k, (src, dst) in enumerate(pairs)]
    for copy in copies:
        copy.start()
    return copies


def own_place(plan):
    pair, member, r = lax.axis_index("pairs"), lax.axis_index("member"), lax.axis_index("rows")
    return pair, member, r, r * plan.slice_width + (2 * pair + member) * plan.sub


def fetch_kernel(g_hbm, coarse_hbm, fine_hbm, g_ref, coarse_ref, fine_ref, sems):
    for copy in fetched([(fine_hbm, fine_ref), (coarse_hbm, coarse_ref), (g_hbm, g_ref)], sems):
        copy.wait()


def pack_kernel(plan, g_ref, coarse_ref, fine_ref, out_ref):
    sub, chunks, local = plan.sub, plan.chunks, plan.local
    shape = (2 * local, 2 * 128)
    lane = lanes_at((1, 2 * 128), 1)
    repeated = one_hot(lanes_at(shape, 0) == lane % local + lane // 128 * local)
    shape = (plan.channels, 128)
    quarter = lanes_at(shape, 0) // 8 % 4 == lanes_at(shape, 1) // local
    orders = jnp.concatenate([pixel_order(plan, swapped) for swapped in (False, True)], axis=1)
    acts = fine_ref[...]
    halves = one_hot_dot(acts, orders, ((0,), (0,))).astype(jnp.bfloat16)
    halves = [halves[:, :128], halves[:, 128:]]
    small = one_hot_dot(jnp.concatenate([coarse_ref[...], g_ref[...]], axis=0), repeated, ((0,), (0,)))
    for k, at in enumerate((plan.packed_at, plan.cot_at)):
        rows_of = jnp.where(quarter, small[:, k * 128 : (k + 1) * 128], 0.0).reshape(plan.count, 4, 8, 128)
        out_ref[:, at : at + 8, :] = jnp.sum(rows_of, axis=1).astype(jnp.bfloat16)
    low = lanes_at((sub, 128), 1) < 64
    for s_r in range(plan.nr):
        for s_f in range(plan.nf):
            dest = s_r * plan.nf + s_f
            first, half = s_r * plan.slice_width + s_f // 2 * 2 * sub, s_f % 2
            for k in range(chunks // 2):
                at = (half * chunks // 2 + k) * 128
                out_ref[dest, k * local : (k + 1) * local, :] = g_ref[:, at : at + 128]
            upper, lower = halves[half][first : first + sub], halves[1 - half][first + sub : first + 2 * sub]
            out_ref[dest, plan.acts_at : plan.packed_at, :] = jnp.where(low, upper, lower)


def by_frame_device(plan, got_ref, at, height):
    return jnp.concatenate(
        [
            jnp.concatenate(
                [got_ref[r * plan.nf + f, at : at + height, :] for r in range(plan.nr)], axis=1
            )
            for f in range(plan.nf)
        ],
        axis=0,
    )


def in_places(plan, merged, height):
    width = plan.tl * plan.image
    return [
        jnp.concatenate(
            [merged[f * height : (f + 1) * height, k * width : (k + 1) * width] for f in range(plan.nf)],
            axis=1,
        )
        for k in range(4)
    ]


def coarse_kernel(
    plan,
    got_ref,
    weights,
    gain_c,
    bias_c,
    gain_f,
    bias_f,
    mine_ref,
    sent_ref,
    held_ref,
    inv_ref,
    fine_ref,
    columns,
    fine_order,
    by_column,
    order,
    source,
    conv_ref,
):
    sub, nr, nf, cells, tl, local = plan.sub, plan.nr, plan.nf, plan.cells, plan.tl, plan.local
    wide, depth = 2 * sub, plan.channels // 2
    pair, member, r, base = own_place(plan)
    first = r * plan.slice_width + pair * wide
    columns[0, 0:sub, :] = jnp.broadcast_to(own_column(gain_c[...], base, sub), (sub, 128))
    columns[1, 0:sub, :] = jnp.broadcast_to(own_column(bias_c[...], base, sub), (sub, 128))
    columns[2] = jnp.broadcast_to(own_column(gain_f[...], first, wide), (wide, 128))
    columns[3] = jnp.broadcast_to(own_column(bias_f[...], first, wide), (wide, 128))
    order[...] = merged_order(plan.nr, 4, plan.tl, plan.cells)
    fine_order[...] = merged_order(plan.nr, 8, plan.tl, plan.cells // 2)
    by_column[...] = column_order(plan)
    both = pl.ds(pl.multiple_of(pair * wide, wide), wide)
    half = pl.ds(pl.multiple_of(member * depth, depth), depth)
    for s_f in range(nf):
        for s_r in range(nr):
            for t in range(tl):
                at = (s_f * tl + t) * plan.image + s_r * cells
                for k in range(plan.chunks // 2):
                    source[at : at + cells, k * 128 : (k + 1) * 128] = got_ref[
                        s_r * nf + s_f, k * local + t * cells : k * local + (t + 1) * cells, :
                    ]
    source[plan.places :, :] = jnp.zeros((2 * plan.image, depth), jnp.bfloat16)
    products = sum(
        one_hot_dot(
            weights[9 * k : 9 * k + 9, both, half].reshape(9 * wide, depth),
            source[(2 - k) * plan.image : (2 - k) * plan.image + plan.places, :],
            ((1,), (1,)),
        )
        for k in range(3)
    )
    merged = one_hot_dot(by_frame_device(plan, got_ref, plan.acts_at, sub), fine_order[...], ((1,), (0,)))
    parts = halves_at(plan, merged)
    for pq in range(4):
        fine_ref[pq] = parts[pq]
    one, two = total(parts), total([part * part for part in parts])
    stats = terms(as_row(one) + pltpu.roll(as_row(two), 64, 1), 3)
    stats = jnp.concatenate(stats + [jnp.zeros_like(stats[0])] * 5, axis=0).astype(jnp.bfloat16)
    small = [by_frame_device(plan, got_ref, at, 8) for at in (plan.packed_at, plan.cot_at)]
    merged = one_hot_dot(jnp.concatenate(small, axis=0), order[...], ((1,), (0,)))
    rows_of = 8 * nf
    values, cot = [
        jnp.concatenate(in_places(plan, merged[k * rows_of : (k + 1) * rows_of], 8), axis=0) for k in range(2)
    ]
    gain, bias = columns[0][0:sub, 0:1], columns[1][0:sub, 0:1]
    entries = plan.places * plan.group_width
    mean, inv_std = statistics(total([values]), total([values * values]), entries, plan.group_width)
    (normed,), (slope,) = normalised([values], gain, bias, mean, inv_std)
    held_ref[0], held_ref[1], held_ref[2] = normed, slope, cot
    inv_ref[...] = jnp.broadcast_to(inv_std, (sub, 128))
    lane, has_left, has_right, has_up, has_down = plan.place_masks(plan.w)
    by_col = []
    for col in range(3):
        parts = [products[(3 * row + col) * wide : (3 * row + col + 1) * wide] for row in range(3)]
        by_col.append(parts[1] + moved(parts[0], plan.w, has_down) + moved(parts[2], -plan.w, has_up))
    conv_ref[...] = by_col[1] + moved(by_col[0], 1, has_right) + moved(by_col[2], -1, has_left)
    mine_ref[...] = conv_ref[pl.ds(pl.multiple_of(member * sub, sub), sub), :]
    theirs = conv_ref[pl.ds(pl.multiple_of((1 - member) * sub, sub), sub), :]
    for k in range(plan.places // 128):
        sent_ref[k * sub : (k + 1) * sub, :] = theirs[:, k * 128 : (k + 1) * 128].astype(jnp.bfloat16)
    sent_ref[plan.places // 128 * sub :, :] = stats


def quarter_kernel(plan, mine_ref, both_ref, held_ref, inv_ref, columns, by_column, out_ref, sums_ref):
    sub = plan.sub
    _, member, _, _ = own_place(plan)
    theirs = [both_ref[1 - member, k * sub : (k + 1) * sub, :] for k in range(plan.places // 128)]
    conv = mine_ref[...] + jnp.concatenate(theirs, axis=1).astype(jnp.float32)
    normed, slope, cot = held_ref[0], held_ref[1], held_ref[2]
    gain, inv_std = columns[0][0:sub, 0:1], inv_ref[:, 0:1]
    entries = plan.places * plan.group_width
    pre = conv * slope
    one, two = total([pre]), total([pre * normed])
    group_one = in_groups(gain * one, plan.group_width) / entries
    group_two = in_groups(gain * two, plan.group_width) / entries
    grad = cot + inv_std * (gain * pre - group_one - normed * group_two)
    quartered = (grad * 0.25).astype(jnp.bfloat16)
    sent = one_hot_dot(quartered, by_column[...], ((1,), (0,))).astype(jnp.bfloat16)
    low = lanes_at((sub // 2, 128), 1) < 64
    for half in range(2):
        at = half * 256
        border = sent[:, 512 + half * 128 : 640 + half * 128]
        border = jnp.where(low, border[: sub // 2], border[sub // 2 :])
        for dest in range(half, plan.count, 2):
            out_ref[dest, 0:sub, :] = sent[:, at : at + 128]
            out_ref[dest, sub : 2 * sub, :] = sent[:, at + 128 : at + 256]
            out_ref[dest, 2 * sub : 2 * sub + sub // 2, :] = border
    sums_ref[...] = jnp.concatenate([as_row(one), as_row(two)], axis=0)


def halves_at(plan, merged):
    sub = plan.sub
    turned = jnp.concatenate([pltpu.roll(merged[:, k * 128 : (k + 1) * 128], 64, 1) for k in range(4)], axis=1)
    low = lanes_at((sub, 128), 1) < 64
    parts = []
    for pq in range(4):
        groups = []
        for group in range(2):
            e = 4 * group + pq
            at = e // 2 * 128
            strips = []
            for m in range(plan.nf // 2):
                first, second = slice(2 * m * sub, (2 * m + 1) * sub), slice((2 * m + 1) * sub, (2 * m + 2) * sub)
                if e % 2 == 0:
                    strips.append(jnp.where(low, merged[first, at : at + 128], turned[second, at : at + 128]))
                else:
                    strips.append(jnp.where(low, turned[first, at : at + 128], merged[second, at : at + 128]))
            groups.append(jnp.concatenate(strips, axis=1))
        parts.append(jnp.concatenate(groups, axis=0))
    return parts


def halves_from(plan, parts):
    sub = plan.sub
    low = lanes_at((sub, 128), 1) < 64
    down = []
    for f in range(plan.nf):
        across = []
        for v in range(4):
            pair = []
            for e in (2 * v, 2 * v + 1):
                group, pq = e // 4, e % 4
                strip = parts[pq][group * sub : (group + 1) * sub, f // 2 * 128 : (f // 2 + 1) * 128]
                pair.append(strip if e % 2 == f % 2 else pltpu.roll(strip, 64, 1))
            across.append(jnp.where(low, pair[0], pair[1]))
        down.append(jnp.concatenate(across, axis=1))
    return jnp.concatenate(down, axis=0)


def fine_kernel(
    plan, got_ref, acts_ref, both_ref, columns, order, sums_ref, weights, out_ref
):
    sub, nr, nf, wide = plan.sub, plan.nr, plan.nf, 2 * plan.sub
    pair, member, r, _ = own_place(plan)
    both = pl.ds(pl.multiple_of(pair * wide, wide), wide)
    w = plan.w // 2
    lines = plan.places // plan.w
    places = lines * w
    source = jnp.concatenate(
        [got_ref[:, k * sub : (k + 1) * sub, :].reshape(plan.channels, 128) for k in range(2)], axis=1
    )
    packed = got_ref[:, wide : wide + sub // 2, :].reshape(plan.count * sub // 2, 128)
    shape = (128, places)
    beside = lanes_at(shape, 1) == lanes_at(shape, 0) % lines * w + (1 - member) * (w - 1)
    border = []
    for k in range(2):
        here = one_hot(beside & (lanes_at(shape, 0) // lines == k))
        found = one_hot_dot(packed, here, ((1,), (0,))).astype(jnp.bfloat16)
        border.append(found.reshape(plan.count, sub // 2, places))
    border = jnp.concatenate(border, axis=1).reshape(plan.channels, places)
    image = plan.image // 2
    sums, extras = 0.0, 0.0
    for k in (2, 1, 0):
        here, beside = source, border
        if k < 2:
            shift = (2 - k) * image
            inside = lanes_at((1, places), 1) < places - shift
            here, beside = [
                jnp.where(inside, pltpu.roll(part, places - shift, 1), jnp.zeros_like(part)) for part in (here, beside)
            ]
        sums = sums + one_hot_dot(
            weights[9 * k : 9 * k + 9, both, :].reshape(9 * wide, plan.channels), here, ((1,), (0,))
        )
        facing = jnp.concatenate([weights[9 * k + 3 * row + 2 * member, both, :] for row in range(3)], axis=0)
        extras = extras + one_hot_dot(facing, beside, ((1,), (0,)))
    parts = [acts_ref[pq] for pq in range(4)]
    at = plan.places // 128 * sub
    stats = sum(both_ref[k, at : at + 8, :].astype(jnp.float32) for k in range(2))
    stats = stats[0:1] + stats[1:2] + stats[2:3]
    entries = 4 * plan.places * plan.group_width
    one, two = own_column(stats, 0, wide), own_column(stats, 64, wide)
    mean, inv_std = statistics(one, two, entries, plan.group_width)
    gain, bias = columns[2][:, 0:1], columns[3][:, 0:1]
    normed, slope = normalised(parts, gain, bias, mean, inv_std)
    lane, has_left, has_right, has_up, has_down = plan.place_masks(w)
    right, left = (1 - member).astype(jnp.float32), member.astype(jnp.float32)
    by_row = []
    for row in range(3):
        a, b, c = [sums[(3 * row + col) * wide : (3 * row + col + 1) * wide] for col in range(3)]
        extra = extras[row * wide : (row + 1) * wide]
        by_row.append(
            (a + b + moved(c, -1, has_left) + left * extra, moved(a, 1, has_right) + b + c + right * extra)
        )
    convs = [by_row[0][q] + by_row[1][q] + moved(by_row[2][q], -w, has_up) for q in range(2)]
    convs += [moved(by_row[0][q], w, has_down) + by_row[1][q] + by_row[2][q] for q in range(2)]
    pre = [conv * part for conv, part in zip(convs, slope)]
    one = total(pre)
    two = total([a * b for a, b in zip(pre, normed)])
    cot = jnp.concatenate(
        [
            jnp.concatenate(
                [got_ref[r * nf + 2 * pair + m, k * sub : (k + 1) * sub, :] for k in range(2)], axis=1
            )
            for m in range(2)
        ],
        axis=0,
    ).astype(jnp.float32)
    scale = inv_std * gain
    stacked = halves_from(plan, [cot + scale * part for part in pre]).astype(jnp.bfloat16)
    sent = one_hot_dot(stacked, order[...], ((1,), (1,))).astype(jnp.bfloat16)
    coarse = sums_ref[0:1] + pltpu.roll(sums_ref[1:2], sub, 1)
    coded = (
        terms(as_row(one) + pltpu.roll(as_row(two), 64, 1), 2)
        + terms(coarse, 2)
        + terms(as_row(inv_std) + pltpu.roll(as_row(mean), 64, 1), 3)
    )
    coded = jnp.concatenate(coded + [jnp.zeros_like(coarse)], axis=0).astype(jnp.bfloat16)
    for s_r in range(nr):
        for s_f in range(nf):
            out_ref[s_f * nr + s_r, 0:sub, :] = sent[s_f * sub : (s_f + 1) * sub, s_r * 128 : (s_r + 1) * 128]
            out_ref[s_f * nr + s_r, sub : sub + 8, :] = coded


def spread_kernel(plan, got_ref, gain_ref, sums_ref, rows_ref):
    sub, nr, nf = plan.sub, plan.nr, plan.nf
    low_row = lanes_at((1, 128), 1) < 64
    first_row = lanes_at((1, 128), 1) < sub
    fine, coarse, moments = [[], []], [[], []], [[], []]
    for s_r in range(nr):
        ones, twos, c_ones, c_twos, invs, means = [], [], 0.0, 0.0, [], []
        for pair in range(nf // 2):
            at = 2 * pair * nr + s_r
            coded = [got_ref[at + k * nr, sub : sub + 8, :].astype(jnp.float32) for k in range(2)]
            sums = coded[0][0:1] + coded[0][1:2] + coded[1][0:1] + coded[1][1:2]
            ones.append(sums if pair == 0 else pltpu.roll(sums, 64, 1))
            twos.append(pltpu.roll(sums, 64, 1) if pair == 0 else sums)
            both = coded[0][4:5] + coded[0][5:6] + coded[0][6:7]
            invs.append(both if pair == 0 else pltpu.roll(both, 64, 1))
            means.append(pltpu.roll(both, 64, 1) if pair == 0 else both)
            for k in range(2):
                sums = coded[k][2:3] + coded[k][3:4]
                to = (2 * pair + k) * sub
                c_one = jnp.where(first_row, sums, 0.0)
                c_two = jnp.where(first_row, pltpu.roll(sums, 128 - sub, 1), 0.0)
                c_ones = c_ones + (pltpu.roll(c_one, to, 1) if to else c_one)
                c_twos = c_twos + (pltpu.roll(c_two, to, 1) if to else c_two)
        fine[0].append(jnp.where(low_row, ones[0], ones[1]))
        fine[1].append(jnp.where(low_row, twos[0], twos[1]))
        moments[0].append(jnp.where(low_row, invs[0], invs[1]))
        moments[1].append(jnp.where(low_row, means[0], means[1]))
        coarse[0].append(c_ones)
        coarse[1].append(c_twos)
    one, two, inv_std, mean, c_one, c_two = [jnp.concatenate(part, axis=1) for part in fine + moments + coarse]
    gain = gain_ref[...]
    entries = 4 * plan.places * plan.group_width
    group_one = in_lane_groups(gain * one, plan.group_width) / entries
    group_two = in_lane_groups(gain * two, plan.group_width) / entries
    rows_ref[...] = jnp.concatenate([inv_std, mean, group_one, group_two] + [jnp.zeros_like(one)] * 4, axis=0)
    sums_ref[...] = jnp.concatenate([one, two, c_one, c_two] + [jnp.zeros_like(one)] * 4, axis=0)


def total_kernel(plan, scales, both_ref, got_ref, acts_ref, rows_ref, result_hbm, out_hbms, total_ref, out_ref, sems):
    sub, nr, nf = plan.sub, plan.nr, plan.nf
    totals = sum(both_ref[k] for k in range(both_ref.shape[0]))
    copies = []
    for k in range(4):
        total_ref[k] = totals[k : k + 1] * scales[k]
        copies.append(pltpu.make_async_copy(total_ref.at[k], out_hbms[k], sems.at[k]))
        copies[-1].start()
    low = lanes_at((sub, 128), 1) < 64
    source = []
    for s_r in range(nr):
        for pair in range(nf // 2):
            at = 2 * pair * nr + s_r
            left, right = [got_ref[at + k * nr, 0:sub, :].astype(jnp.float32) for k in range(2)]
            source.append(jnp.where(low, left, pltpu.roll(right, 64, 1)))
            source.append(jnp.where(low, pltpu.roll(left, 64, 1), right))
    source = jnp.concatenate(source, axis=0).astype(jnp.bfloat16)
    inv_std, mean, group_one, group_two = [rows_ref[k : k + 1] for k in range(4)]
    pixels = pixel_order(plan, False)
    height = 2 * plan.local
    for k in range(2):
        chunk = pl.ds(k * height, height)
        result = one_hot_dot(pixels[k * height : (k + 1) * height], source, ((1,), (1,)))
        normed = (acts_ref[chunk, :].astype(jnp.float32) - mean) * inv_std
        out_ref[chunk, :] = (result - inv_std * (group_one + normed * group_two)).astype(jnp.bfloat16)
        copies.append(pltpu.make_async_copy(out_ref.at[chunk], result_hbm.at[chunk], sems.at[4 + k]))
        copies[-1].start()
    for copy in copies:
        copy.wait()


def in_vmem(count):
    return [pl.BlockSpec(memory_space=pltpu.VMEM)] * count


def in_hbm(count):
    return [pl.BlockSpec(memory_space=pltpu.HBM)] * count


def kept(array):
    return pltpu.with_memory_space_constraint(array, pltpu.HBM)


def shape_of(shape, kind):
    return jax.ShapeDtypeStruct(shape, kind)


LIMIT = pltpu.CompilerParams(vmem_limit_bytes=40 * 1024 * 1024)
COST = pl.CostEstimate(flops=2_000_000_000, bytes_accessed=4_000_000, transcendentals=0)


def fast_shards(
    plan,
    acts_fine,
    acts_coarse,
    grad_coarse,
    gain_fine,
    bias_fine,
    kernel_fine,
    gain_coarse,
    bias_coarse,
    kernel_coarse,
):
    nd = lax.axis_size("dp")
    count, sub, channels, places, local = plan.count, plan.sub, plan.channels, plan.places, plan.local
    f32, bf16 = jnp.float32, jnp.bfloat16
    rows = [part.reshape(1, channels) for part in (gain_coarse, bias_coarse, gain_fine, bias_fine)]
    places_of = ((local, channels), (local, channels), (4 * local, channels))
    fetched_of = pl.pallas_call(
        fetch_kernel,
        out_shape=tuple(pltpu.VMEM(shape, bf16) for shape in places_of),
        in_specs=in_hbm(3),
        out_specs=tuple(in_vmem(3)),
        scratch_shapes=[pltpu.SemaphoreType.DMA((3,))],
        compiler_params=LIMIT,
    )(*[kept(part.reshape(shape)) for part, shape in zip((grad_coarse, acts_coarse, acts_fine), places_of)])
    acts = fetched_of[2]
    packed = pl.pallas_call(
        functools.partial(pack_kernel, plan),
        out_shape=shape_of((count, plan.block_rows, 128), bf16),
        in_specs=in_vmem(3),
        out_specs=in_vmem(1)[0],
        compiler_params=LIMIT,
        cost_estimate=COST,
    )(*fetched_of)
    got = lax.all_to_all(packed, BLOCK, 0, 0)
    mine, theirs, held, inv_std, fine_acts, columns, fine_order, by_column = pl.pallas_call(
        functools.partial(coarse_kernel, plan),
        out_shape=(
            shape_of((sub, places), f32),
            shape_of((places // 128 * sub + 8, 128), bf16),
            shape_of((3, sub, places), f32),
            shape_of((sub, 128), f32),
            shape_of((4, 2 * sub, places // 2), f32),
            shape_of((4, 2 * sub, 128), f32),
            shape_of((4 * plan.nr * local, 4 * plan.nr * local), bf16),
            shape_of((places, places + places // 2), bf16),
        ),
        in_specs=in_vmem(6),
        out_specs=tuple(in_vmem(8)),
        scratch_shapes=[
            pltpu.VMEM((4 * plan.nr * local, 4 * plan.nr * local), bf16),
            pltpu.VMEM((places + 2 * plan.image, channels // 2), bf16),
            pltpu.VMEM((2 * sub, places), f32),
        ],
        compiler_params=LIMIT,
        cost_estimate=COST,
    )(got, kernel_coarse, *rows)
    both = lax.all_gather(theirs, "member")
    quartered, coarse_sums = pl.pallas_call(
        functools.partial(quarter_kernel, plan),
        out_shape=(shape_of((count, 2 * sub + sub // 2, 128), bf16), shape_of((2, 128), f32)),
        in_specs=in_vmem(6),
        out_specs=tuple(in_vmem(2)),
        compiler_params=LIMIT,
        cost_estimate=COST,
    )(mine, both, held, inv_std, columns, by_column)
    spread = lax.all_to_all(quartered, BLOCK, 0, 0)
    sent = pl.pallas_call(
        functools.partial(fine_kernel, plan),
        out_shape=shape_of((count, sub + 8, 128), bf16),
        in_specs=in_vmem(7),
        out_specs=in_vmem(1)[0],
        compiler_params=LIMIT,
        cost_estimate=COST,
    )(spread, fine_acts, both, columns, fine_order, coarse_sums, kernel_fine)
    back = lax.all_to_all(sent, BACK_BLOCK, 0, 0)
    cells = nd * places
    fine_scale, coarse_scale = 1.0 / math.sqrt(4 * cells), 1.0 / math.sqrt(cells)
    sums, moments = pl.pallas_call(
        functools.partial(spread_kernel, plan),
        out_shape=(shape_of((8, channels), f32), shape_of((8, channels), f32)),
        in_specs=in_vmem(2),
        out_specs=tuple(in_vmem(2)),
        compiler_params=LIMIT,
        cost_estimate=COST,
    )(back, rows[2])
    both = lax.all_gather(sums, "dp")
    out, sums = pl.pallas_call(
        functools.partial(total_kernel, plan, (fine_scale, fine_scale, coarse_scale, coarse_scale)),
        out_shape=(pltpu.HBM((4 * local, channels), bf16), (pltpu.HBM((1, channels), f32),) * 4),
        in_specs=in_vmem(4),
        out_specs=(in_hbm(1)[0], tuple(in_hbm(4))),
        scratch_shapes=[
            pltpu.VMEM((4, 1, channels), f32),
            pltpu.VMEM((4 * local, channels), bf16),
            pltpu.SemaphoreType.DMA((6,)),
        ],
        compiler_params=LIMIT,
        cost_estimate=COST,
    )(both, back, acts, moments)
    bias_f, gain_f, bias_c, gain_c = [part.reshape(channels) for part in sums]
    return out.reshape(acts_fine.shape), gain_f, bias_f, gain_c, bias_c


def solution(mesh):
    def function(*arrays):
        local = [size // mesh.shape[axis] for size, axis in zip(arrays[1].shape, ("dp", "frames", "rows"))]
        sizes = (mesh.shape["frames"], mesh.shape["rows"])
        plan = Plan(sizes, (*local[1:], *arrays[1].shape[3:]), arrays[5].shape[1] // mesh.shape["rows"])
        if plan.fits:
            split = (mesh.shape["dp"], plan.nf // 2, 2, plan.nr)
            used = jax.sharding.Mesh(mesh.devices.reshape(split), ("dp", "pairs", "member", "rows"))
            shards, frames = functools.partial(fast_shards, plan), ("pairs", "member")
        else:
            used, shards, frames = mesh, plain_shards, "frames"
        blocks, kernel = P("dp", frames, "rows", None, None), P(None, "rows", None)
        in_specs = (blocks, blocks, blocks, P(), P(), kernel, P(), P(), kernel)
        out_specs = (blocks, P(), P(), P(), P())
        mapped = jax.shard_map(shards, mesh=used, in_specs=in_specs, out_specs=out_specs, check_vma=False)
        return mapped(*arrays)

    return function
```

```python
import functools
import math

import jax
import jax.numpy as jnp
from jax import lax
from jax.experimental import pallas as pl
from jax.experimental.pallas import tpu as pltpu
from jax.sharding import PartitionSpec as P

GROUPS = 32
EPSILON = 1e-06
BLOCK = ("rows", "pairs", "member")
BACK_BLOCK = ("pairs", "member", "rows")
PLAIN_BLOCK = ("frames", "rows")


def plain_everyone(block, count):
    copies = jnp.broadcast_to(block[None], (count,) + block.shape)
    return lax.all_to_all(copies, PLAIN_BLOCK, 0, 0)


def ahead(field, axis, distance):
    size = field.shape[axis]
    if distance == 0:
        return field
    widths = [(0, 0)] * field.ndim
    if distance > 0:
        widths[axis] = (0, distance)
        kept = lax.slice_in_dim(field, distance, size, axis=axis)
    else:
        widths[axis] = (-distance, 0)
        kept = lax.slice_in_dim(field, 0, size + distance, axis=axis)
    return jnp.pad(kept, widths)


def tap_products(source, kernel):
    sub = kernel.shape[1]
    frames, rows, cols, channels = source.shape
    products = lax.dot_general(
        kernel.reshape(27 * sub, channels),
        source.reshape(frames * rows * cols, channels),
        (((1,), (1,)), ((), ())),
        preferred_element_type=jnp.float32,
    ).reshape(3, 3, 3, sub, frames, rows, cols)
    return sum(ahead(products[depth], 3, 2 - depth) for depth in range(3))


def coarse_conv(source, kernel):
    spatial = tap_products(source, kernel)
    total = 0.0
    for row in range(3):
        part = sum(ahead(spatial[row, col], 3, 1 - col) for col in range(3))
        total = total + ahead(part, 2, 1 - row)
    return total


def fine_conv(source, kernel):
    spatial = tap_products(source, kernel)
    result = []
    for p in range(2):
        rows_of = []
        for q in range(2):
            total = 0.0
            for row in range(3):
                part = sum(ahead(spatial[row, col], 3, (q + 1 - col) // 2) for col in range(3))
                total = total + ahead(part, 2, (p + 1 - row) // 2)
            rows_of.append(total)
        result.append(jnp.stack(rows_of, 1))
    return jnp.stack(result, 1)


def group_total(sums, group_width):
    sub = sums.shape[-1]
    if sub % group_width == 0:
        grouped = jnp.sum(sums.reshape(-1, sub // group_width, group_width), axis=-1)
        return jnp.repeat(grouped, group_width, axis=-1)
    spread = jnp.moveaxis(lax.all_gather(sums, "frames"), 0, 1).reshape(sums.shape[0], -1, group_width)
    mine = lax.axis_index("frames") * sub // group_width
    grouped = lax.dynamic_index_in_dim(jnp.sum(spread, -1), mine, 1)
    return jnp.broadcast_to(grouped, sums.shape)


def level(acts, conv_grad, cotangent, gain, bias, group_width):
    sub = acts.shape[0]
    places = acts.size // sub
    values = acts.astype(jnp.float32).reshape(sub, places)
    conv_grad = conv_grad.reshape(sub, places)
    entries = places * group_width
    moments = group_total(
        jnp.stack([jnp.sum(values, 1), jnp.sum(values * values, 1)]), group_width
    ) / entries
    mean = moments[0]
    inv_std = lax.rsqrt(moments[1] - mean * mean + EPSILON)
    normed = (values - mean[:, None]) * inv_std[:, None]
    preact = gain[:, None] * normed + bias[:, None]
    squash = jax.nn.sigmoid(preact)
    pre_grad = conv_grad * squash * (1.0 + preact * (1.0 - squash))
    sums = jnp.stack([jnp.sum(pre_grad, 1), jnp.sum(pre_grad * normed, 1)])
    terms = group_total(sums * gain, group_width) / entries
    grad = cotangent.reshape(sub, places) + inv_std[:, None] * (
        gain[:, None] * pre_grad - terms[0][:, None] - normed * terms[1][:, None]
    )
    return grad, sums


def plain_shards(
    acts_fine,
    acts_coarse,
    grad_coarse,
    gain_fine,
    bias_fine,
    kernel_fine,
    gain_coarse,
    bias_coarse,
    kernel_coarse,
):
    nf, nr, nd = lax.axis_size("frames"), lax.axis_size("rows"), lax.axis_size("dp")
    count = nf * nr
    channels = acts_fine.shape[-1]
    slice_width = kernel_fine.shape[1]
    sub = slice_width // nf
    group_width = channels // GROUPS
    tl, hl, w = acts_coarse.shape[1:4]
    frames, rows = tl * nf, hl * nr
    f, r = lax.axis_index("frames"), lax.axis_index("rows")

    gathered = plain_everyone(grad_coarse[0], count)
    source = (
        gathered.reshape(nf, nr, tl, hl, w, channels)
        .transpose(0, 2, 1, 3, 4, 5)
        .reshape(frames, rows, w, channels)
    )
    coarse_in = acts_coarse[0].reshape(tl, hl, w, nr, nf, sub).transpose(4, 3, 5, 0, 1, 2)
    coarse_in = lax.all_to_all(coarse_in.reshape(count, sub, tl * hl * w), PLAIN_BLOCK, 0, 0)
    fine_in = acts_fine[0].reshape(tl, hl, 2, w, 2, nr, nf, sub).transpose(6, 5, 7, 2, 4, 0, 1, 3)
    fine_in = lax.all_to_all(fine_in.reshape(count, sub, 4 * tl * hl * w), PLAIN_BLOCK, 0, 0)

    def mine(vector):
        return lax.dynamic_slice_in_dim(vector, r * slice_width + f * sub, sub)

    def own(kernel):
        return lax.dynamic_slice_in_dim(kernel, f * sub, sub, axis=1)

    coarse_vals = (
        coarse_in.reshape(nf, nr, sub, tl, hl, w).transpose(2, 0, 3, 1, 4, 5).reshape(sub, frames, rows, w)
    )
    cot = lax.dynamic_slice_in_dim(source, r * slice_width + f * sub, sub, axis=3)
    cot = cot.astype(jnp.float32).transpose(3, 0, 1, 2)
    conv = coarse_conv(source, own(kernel_coarse))
    coarse_grad, coarse_sums = level(
        coarse_vals, conv, cot, mine(gain_coarse), mine(bias_coarse), group_width
    )
    quartered = (coarse_grad * 0.25).astype(jnp.bfloat16)
    spread = plain_everyone(quartered, count)
    source_fine = (
        spread.reshape(nf, nr, sub, frames, rows, w)
        .transpose(3, 4, 5, 1, 0, 2)
        .reshape(frames, rows, w, channels)
    )
    conv = fine_conv(source_fine, own(kernel_fine))
    fine_vals = (
        fine_in.reshape(nf, nr, sub, 2, 2, tl, hl, w)
        .transpose(2, 3, 4, 0, 5, 1, 6, 7)
        .reshape(sub, 2, 2, frames, rows, w)
    )
    cot = jnp.broadcast_to(
        quartered.astype(jnp.float32).reshape(sub, 1, 1, frames, rows, w), conv.shape
    )
    fine_grad, fine_sums = level(
        fine_vals, conv, cot, mine(gain_fine), mine(bias_fine), group_width
    )
    back = (
        fine_grad.astype(jnp.bfloat16)
        .reshape(sub, 2, 2, nf, tl, nr, hl, w)
        .transpose(3, 5, 0, 1, 2, 4, 6, 7)
        .reshape(count, sub, 4 * tl * hl * w)
    )
    sums = plain_everyone(jnp.concatenate([fine_sums, coarse_sums]), count)
    back = lax.all_to_all(back, PLAIN_BLOCK, 0, 0)
    out = (
        back.reshape(nf, nr, sub, 2, 2, tl, hl, w)
        .transpose(5, 6, 3, 7, 4, 1, 0, 2)
        .reshape(1, tl, 2 * hl, 2 * w, channels)
    )
    sums = sums.reshape(nf, nr, 4, sub).transpose(2, 1, 0, 3).reshape(4, channels)
    totals = lax.psum(sums, "dp")
    cells = nd * frames * rows * w
    scale_fine = 1.0 / jnp.sqrt(jnp.float32(4 * cells))
    scale_coarse = 1.0 / jnp.sqrt(jnp.float32(cells))
    return (
        out,
        totals[1] * scale_fine,
        totals[0] * scale_fine,
        totals[3] * scale_coarse,
        totals[2] * scale_coarse,
    )


def lanes_at(shape, axis):
    return lax.broadcasted_iota(jnp.int32, shape, axis)


def one_hot(found):
    return found.astype(jnp.float32).astype(jnp.bfloat16)


def pixel_order(plan, swapped):
    tl, hl, w = plan.tl, plan.hl, plan.w // 2
    size = 4 * plan.local
    lane = lanes_at((1, size), 1)
    j, i, t = lane % w, lane // w % hl, lane // (w * hl) % tl
    q, p = lane // (w * hl * tl) % 2, lane // (2 * w * hl * tl) % 2
    half = lane // (4 * w * hl * tl)
    if swapped:
        half = 1 - half
    pixel = (t * 2 * hl + 2 * i + p) * 4 * w + 2 * (half * w + j) + q
    return one_hot(lanes_at((size, size), 0) == pixel)


def merged_order(nr, outer, tl, cells):
    size = nr * outer * tl * cells
    lane = lanes_at((1, size), 1)
    cell, dev = lane % cells, lane // cells % nr
    t, o = lane // (cells * nr) % tl, lane // (cells * nr * tl)
    return one_hot(lanes_at((size, size), 0) == ((dev * outer + o) * tl + t) * cells + cell)


def column_order(plan):
    w = plan.w // 2
    lines = plan.places // plan.w
    lane = lanes_at((1, 4 * lines * w + 4 * lines), 1)
    inner = lane % (lines * w)
    place = inner // w * plan.w + lane // (lines * w) * w + inner % w
    past = lane - 2 * lines * w
    border = past % lines * plan.w + jnp.where(past < 2 * lines, w, w - 1)
    wanted = jnp.where(past >= 0, border, place)
    shape = (plan.places, 2 * lines * w + 4 * lines)
    return one_hot(lanes_at(shape, 0) == wanted[:, : shape[1]])


def one_hot_dot(a, b, dims):
    return lax.dot_general(a, b, (dims, ((), ())), preferred_element_type=jnp.float32)


def moved(field, distance, kept):
    size = field.shape[1]
    return jnp.where(kept, pltpu.roll(field, (-distance) % size, 1), 0.0)


def own_column(row, base, sub):
    shape = (sub, row.shape[1])
    mine = lanes_at(shape, 1) == lanes_at(shape, 0) + base
    return jnp.sum(jnp.where(mine, row, 0.0), axis=1, keepdims=True)


def as_row(column):
    shape = (column.shape[0], 128)
    here = lanes_at(shape, 1) == lanes_at(shape, 0)
    return jnp.sum(jnp.where(here, column, 0.0), axis=0, keepdims=True)


def terms(value, count):
    found = []
    for _ in range(count):
        found.append(value.astype(jnp.bfloat16).astype(jnp.float32))
        value = value - found[-1]
    return found


def in_groups(column, group_width):
    sub = column.shape[0]
    grouped = jnp.sum(column.reshape(sub // group_width, group_width, 1), axis=1, keepdims=True)
    return jnp.broadcast_to(grouped, (sub // group_width, group_width, 1)).reshape(sub, 1)


def in_lane_groups(row, group_width):
    lane = lanes_at(row.shape, 1)
    size = row.shape[1]
    step = 1
    while step < group_width:
        up, down = pltpu.roll(row, size - step, 1), pltpu.roll(row, step, 1)
        row = row + jnp.where(lane // step % 2 == 0, up, down)
        step *= 2
    return row


def total(parts):
    return sum(jnp.sum(part, axis=1, keepdims=True) for part in parts)


def statistics(one, two, entries, group_width):
    mean = in_groups(one, group_width) / entries
    square = in_groups(two, group_width) / entries
    return mean, lax.rsqrt(square - mean * mean + EPSILON)


def normalised(parts, gain, bias, mean, inv_std):
    normed, slope = [], []
    for part in parts:
        unit = (part - mean) * inv_std
        preact = gain * unit + bias
        squash = 0.5 + 0.5 * jnp.tanh(0.5 * preact)
        normed.append(unit)
        slope.append(squash * (1.0 + preact * (1.0 - squash)))
    return normed, slope


class Plan:
    def __init__(self, mesh_sizes, acts_coarse, slice_width):
        self.nf, self.nr = mesh_sizes
        self.count = self.nf * self.nr
        self.tl, self.hl, self.w, self.channels = acts_coarse
        self.slice_width = slice_width
        self.sub = slice_width // self.nf
        self.cells = self.hl * self.w
        self.local = self.tl * self.cells
        self.image = self.cells * self.nr
        self.frames = self.tl * self.nf
        self.places = self.frames * self.image
        self.group_width = self.channels // GROUPS
        self.chunks = self.channels // 128
        self.acts_at = self.chunks // 2 * self.local
        self.packed_at = self.acts_at + self.sub
        self.cot_at = self.packed_at + 8
        self.block_rows = self.cot_at + 8
        self.fits = (
            self.sub == 32
            and self.slice_width == 128
            and self.group_width == 16
            and self.cells == 16
            and self.w == 8
            and self.tl == 2
            and self.nr == 4
            and self.nf == 4
            and self.slice_width * self.nr == self.channels
        )

    def place_masks(self, w):
        lane = lanes_at((1, self.places // self.w * w), 1)
        col, row = lane % w, lane // w % (self.hl * self.nr)
        last_row = self.hl * self.nr - 1
        return (lane, col > 0, col < w - 1, row > 0, row < last_row)


def fetched(pairs, sems):
    copies = [pltpu.make_async_copy(src, dst, sems.at[k]) for k, (src, dst) in enumerate(pairs)]
    for copy in copies:
        copy.start()
    return copies


def own_place(plan):
    pair, member, r = lax.axis_index("pairs"), lax.axis_index("member"), lax.axis_index("rows")
    return pair, member, r, r * plan.slice_width + (2 * pair + member) * plan.sub


def fetch_kernel(g_hbm, coarse_hbm, fine_hbm, g_ref, coarse_ref, fine_ref, sems):
    for copy in fetched([(fine_hbm, fine_ref), (coarse_hbm, coarse_ref), (g_hbm, g_ref)], sems):
        copy.wait()


def pack_kernel(plan, g_ref, coarse_ref, fine_ref, out_ref):
    sub, chunks, local = plan.sub, plan.chunks, plan.local
    shape = (2 * local, 2 * 128)
    lane = lanes_at((1, 2 * 128), 1)
    repeated = one_hot(lanes_at(shape, 0) == lane % local + lane // 128 * local)
    shape = (plan.channels, 128)
    quarter = lanes_at(shape, 0) // 8 % 4 == lanes_at(shape, 1) // local
    orders = jnp.concatenate([pixel_order(plan, swapped) for swapped in (False, True)], axis=1)
    acts = fine_ref[...]
    halves = one_hot_dot(acts, orders, ((0,), (0,))).astype(jnp.bfloat16)
    halves = [halves[:, :128], halves[:, 128:]]
    small = one_hot_dot(jnp.concatenate([coarse_ref[...], g_ref[...]], axis=0), repeated, ((0,), (0,)))
    for k, at in enumerate((plan.packed_at, plan.cot_at)):
        rows_of = jnp.where(quarter, small[:, k * 128 : (k + 1) * 128], 0.0).reshape(plan.count, 4, 8, 128)
        out_ref[:, at : at + 8, :] = jnp.sum(rows_of, axis=1).astype(jnp.bfloat16)
    low = lanes_at((sub, 128), 1) < 64
    for s_r in range(plan.nr):
        for s_f in range(plan.nf):
            dest = s_r * plan.nf + s_f
            first, half = s_r * plan.slice_width + s_f // 2 * 2 * sub, s_f % 2
            for k in range(chunks // 2):
                at = (half * chunks // 2 + k) * 128
                out_ref[dest, k * local : (k + 1) * local, :] = g_ref[:, at : at + 128]
            upper, lower = halves[half][first : first + sub], halves[1 - half][first + sub : first + 2 * sub]
            out_ref[dest, plan.acts_at : plan.packed_at, :] = jnp.where(low, upper, lower)


def by_frame_device(plan, got_ref, at, height):
    return jnp.concatenate(
        [
            jnp.concatenate(
                [got_ref[r * plan.nf + f, at : at + height, :] for r in range(plan.nr)], axis=1
            )
            for f in range(plan.nf)
        ],
        axis=0,
    )


def in_places(plan, merged, height):
    width = plan.tl * plan.image
    return [
        jnp.concatenate(
            [merged[f * height : (f + 1) * height, k * width : (k + 1) * width] for f in range(plan.nf)],
            axis=1,
        )
        for k in range(4)
    ]


def coarse_kernel(
    plan,
    got_ref,
    weights,
    gain_c,
    bias_c,
    gain_f,
    bias_f,
    mine_ref,
    sent_ref,
    held_ref,
    inv_ref,
    fine_ref,
    columns,
    fine_order,
    by_column,
    order,
    source,
    conv_ref,
):
    sub, nr, nf, cells, tl, local = plan.sub, plan.nr, plan.nf, plan.cells, plan.tl, plan.local
    wide, depth = 2 * sub, plan.channels // 2
    pair, member, r, base = own_place(plan)
    first = r * plan.slice_width + pair * wide
    columns[0, 0:sub, :] = jnp.broadcast_to(own_column(gain_c[...], base, sub), (sub, 128))
    columns[1, 0:sub, :] = jnp.broadcast_to(own_column(bias_c[...], base, sub), (sub, 128))
    columns[2] = jnp.broadcast_to(own_column(gain_f[...], first, wide), (wide, 128))
    columns[3] = jnp.broadcast_to(own_column(bias_f[...], first, wide), (wide, 128))
    order[...] = merged_order(plan.nr, 4, plan.tl, plan.cells)
    fine_order[...] = merged_order(plan.nr, 8, plan.tl, plan.cells // 2)
    by_column[...] = column_order(plan)
    both = pl.ds(pl.multiple_of(pair * wide, wide), wide)
    half = pl.ds(pl.multiple_of(member * depth, depth), depth)
    for s_f in range(nf):
        for s_r in range(nr):
            for t in range(tl):
                at = (s_f * tl + t) * plan.image + s_r * cells
                for k in range(plan.chunks // 2):
                    source[at : at + cells, k * 128 : (k + 1) * 128] = got_ref[
                        s_r * nf + s_f, k * local + t * cells : k * local + (t + 1) * cells, :
                    ]
    source[plan.places :, :] = jnp.zeros((2 * plan.image, depth), jnp.bfloat16)
    products = sum(
        one_hot_dot(
            weights[9 * k : 9 * k + 9, both, half].reshape(9 * wide, depth),
            source[(2 - k) * plan.image : (2 - k) * plan.image + plan.places, :],
            ((1,), (1,)),
        )
        for k in range(3)
    )
    merged = one_hot_dot(by_frame_device(plan, got_ref, plan.acts_at, sub), fine_order[...], ((1,), (0,)))
    parts = halves_at(plan, merged)
    for pq in range(4):
        fine_ref[pq] = parts[pq]
    one, two = total(parts), total([part * part for part in parts])
    stats = terms(as_row(one) + pltpu.roll(as_row(two), 64, 1), 3)
    stats = jnp.concatenate(stats + [jnp.zeros_like(stats[0])] * 5, axis=0).astype(jnp.bfloat16)
    small = [by_frame_device(plan, got_ref, at, 8) for at in (plan.packed_at, plan.cot_at)]
    merged = one_hot_dot(jnp.concatenate(small, axis=0), order[...], ((1,), (0,)))
    rows_of = 8 * nf
    values, cot = [
        jnp.concatenate(in_places(plan, merged[k * rows_of : (k + 1) * rows_of], 8), axis=0) for k in range(2)
    ]
    gain, bias = columns[0][0:sub, 0:1], columns[1][0:sub, 0:1]
    entries = plan.places * plan.group_width
    mean, inv_std = statistics(total([values]), total([values * values]), entries, plan.group_width)
    (normed,), (slope,) = normalised([values], gain, bias, mean, inv_std)
    held_ref[0], held_ref[1], held_ref[2] = normed, slope, cot
    inv_ref[...] = jnp.broadcast_to(inv_std, (sub, 128))
    lane, has_left, has_right, has_up, has_down = plan.place_masks(plan.w)
    by_col = []
    for col in range(3):
        parts = [products[(3 * row + col) * wide : (3 * row + col + 1) * wide] for row in range(3)]
        by_col.append(parts[1] + moved(parts[0], plan.w, has_down) + moved(parts[2], -plan.w, has_up))
    conv_ref[...] = by_col[1] + moved(by_col[0], 1, has_right) + moved(by_col[2], -1, has_left)
    mine_ref[...] = conv_ref[pl.ds(pl.multiple_of(member * sub, sub), sub), :]
    theirs = conv_ref[pl.ds(pl.multiple_of((1 - member) * sub, sub), sub), :]
    for k in range(plan.places // 128):
        sent_ref[k * sub : (k + 1) * sub, :] = theirs[:, k * 128 : (k + 1) * 128].astype(jnp.bfloat16)
    sent_ref[plan.places // 128 * sub :, :] = stats


def quarter_kernel(plan, mine_ref, both_ref, held_ref, inv_ref, columns, by_column, out_ref, sums_ref):
    sub = plan.sub
    _, member, _, _ = own_place(plan)
    theirs = [both_ref[1 - member, k * sub : (k + 1) * sub, :] for k in range(plan.places // 128)]
    conv = mine_ref[...] + jnp.concatenate(theirs, axis=1).astype(jnp.float32)
    normed, slope, cot = held_ref[0], held_ref[1], held_ref[2]
    gain, inv_std = columns[0][0:sub, 0:1], inv_ref[:, 0:1]
    entries = plan.places * plan.group_width
    pre = conv * slope
    one, two = total([pre]), total([pre * normed])
    group_one = in_groups(gain * one, plan.group_width) / entries
    group_two = in_groups(gain * two, plan.group_width) / entries
    grad = cot + inv_std * (gain * pre - group_one - normed * group_two)
    quartered = (grad * 0.25).astype(jnp.bfloat16)
    sent = one_hot_dot(quartered, by_column[...], ((1,), (0,))).astype(jnp.bfloat16)
    low = lanes_at((sub // 2, 128), 1) < 64
    for half in range(2):
        at = half * 256
        border = sent[:, 512 + half * 128 : 640 + half * 128]
        border = jnp.where(low, border[: sub // 2], border[sub // 2 :])
        for dest in range(half, plan.count, 2):
            out_ref[dest, 0:sub, :] = sent[:, at : at + 128]
            out_ref[dest, sub : 2 * sub, :] = sent[:, at + 128 : at + 256]
            out_ref[dest, 2 * sub : 2 * sub + sub // 2, :] = border
    sums_ref[...] = jnp.concatenate([as_row(one), as_row(two)], axis=0)


def halves_at(plan, merged):
    sub = plan.sub
    turned = jnp.concatenate([pltpu.roll(merged[:, k * 128 : (k + 1) * 128], 64, 1) for k in range(4)], axis=1)
    low = lanes_at((sub, 128), 1) < 64
    parts = []
    for pq in range(4):
        groups = []
        for group in range(2):
            e = 4 * group + pq
            at = e // 2 * 128
            strips = []
            for m in range(plan.nf // 2):
                first, second = slice(2 * m * sub, (2 * m + 1) * sub), slice((2 * m + 1) * sub, (2 * m + 2) * sub)
                if e % 2 == 0:
                    strips.append(jnp.where(low, merged[first, at : at + 128], turned[second, at : at + 128]))
                else:
                    strips.append(jnp.where(low, turned[first, at : at + 128], merged[second, at : at + 128]))
            groups.append(jnp.concatenate(strips, axis=1))
        parts.append(jnp.concatenate(groups, axis=0))
    return parts


def halves_from(plan, parts):
    sub = plan.sub
    low = lanes_at((sub, 128), 1) < 64
    down = []
    for f in range(plan.nf):
        across = []
        for v in range(4):
            pair = []
            for e in (2 * v, 2 * v + 1):
                group, pq = e // 4, e % 4
                strip = parts[pq][group * sub : (group + 1) * sub, f // 2 * 128 : (f // 2 + 1) * 128]
                pair.append(strip if e % 2 == f % 2 else pltpu.roll(strip, 64, 1))
            across.append(jnp.where(low, pair[0], pair[1]))
        down.append(jnp.concatenate(across, axis=1))
    return jnp.concatenate(down, axis=0)


def fine_kernel(
    plan, got_ref, acts_ref, both_ref, columns, order, sums_ref, weights, out_ref
):
    sub, nr, nf, wide = plan.sub, plan.nr, plan.nf, 2 * plan.sub
    pair, member, r, _ = own_place(plan)
    both = pl.ds(pl.multiple_of(pair * wide, wide), wide)
    w = plan.w // 2
    lines = plan.places // plan.w
    places = lines * w
    source = jnp.concatenate(
        [got_ref[:, k * sub : (k + 1) * sub, :].reshape(plan.channels, 128) for k in range(2)], axis=1
    )
    packed = got_ref[:, wide : wide + sub // 2, :].reshape(plan.count * sub // 2, 128)
    shape = (128, places)
    beside = lanes_at(shape, 1) == lanes_at(shape, 0) % lines * w + (1 - member) * (w - 1)
    border = []
    for k in range(2):
        here = one_hot(beside & (lanes_at(shape, 0) // lines == k))
        found = one_hot_dot(packed, here, ((1,), (0,))).astype(jnp.bfloat16)
        border.append(found.reshape(plan.count, sub // 2, places))
    border = jnp.concatenate(border, axis=1).reshape(plan.channels, places)
    image = plan.image // 2
    sums, extras = 0.0, 0.0
    for k in (2, 1, 0):
        here, beside = source, border
        if k < 2:
            shift = (2 - k) * image
            inside = lanes_at((1, places), 1) < places - shift
            here, beside = [
                jnp.where(inside, pltpu.roll(part, places - shift, 1), jnp.zeros_like(part)) for part in (here, beside)
            ]
        sums = sums + one_hot_dot(
            weights[9 * k : 9 * k + 9, both, :].reshape(9 * wide, plan.channels), here, ((1,), (0,))
        )
        facing = jnp.concatenate([weights[9 * k + 3 * row + 2 * member, both, :] for row in range(3)], axis=0)
        extras = extras + one_hot_dot(facing, beside, ((1,), (0,)))
    parts = [acts_ref[pq] for pq in range(4)]
    at = plan.places // 128 * sub
    stats = sum(both_ref[k, at : at + 8, :].astype(jnp.float32) for k in range(2))
    stats = stats[0:1] + stats[1:2] + stats[2:3]
    entries = 4 * plan.places * plan.group_width
    one, two = own_column(stats, 0, wide), own_column(stats, 64, wide)
    mean, inv_std = statistics(one, two, entries, plan.group_width)
    gain, bias = columns[2][:, 0:1], columns[3][:, 0:1]
    normed, slope = normalised(parts, gain, bias, mean, inv_std)
    lane, has_left, has_right, has_up, has_down = plan.place_masks(w)
    right, left = (1 - member).astype(jnp.float32), member.astype(jnp.float32)
    by_row = []
    for row in range(3):
        a, b, c = [sums[(3 * row + col) * wide : (3 * row + col + 1) * wide] for col in range(3)]
        extra = extras[row * wide : (row + 1) * wide]
        by_row.append(
            (a + b + moved(c, -1, has_left) + left * extra, moved(a, 1, has_right) + b + c + right * extra)
        )
    convs = [by_row[0][q] + by_row[1][q] + moved(by_row[2][q], -w, has_up) for q in range(2)]
    convs += [moved(by_row[0][q], w, has_down) + by_row[1][q] + by_row[2][q] for q in range(2)]
    pre = [conv * part for conv, part in zip(convs, slope)]
    one = total(pre)
    two = total([a * b for a, b in zip(pre, normed)])
    cot = jnp.concatenate(
        [
            jnp.concatenate(
                [got_ref[r * nf + 2 * pair + m, k * sub : (k + 1) * sub, :] for k in range(2)], axis=1
            )
            for m in range(2)
        ],
        axis=0,
    ).astype(jnp.float32)
    scale = inv_std * gain
    stacked = halves_from(plan, [cot + scale * part for part in pre]).astype(jnp.bfloat16)
    sent = one_hot_dot(stacked, order[...], ((1,), (1,))).astype(jnp.bfloat16)
    coarse = sums_ref[0:1] + pltpu.roll(sums_ref[1:2], sub, 1)
    coded = (
        terms(as_row(one) + pltpu.roll(as_row(two), 64, 1), 2)
        + terms(coarse, 2)
        + terms(as_row(inv_std) + pltpu.roll(as_row(mean), 64, 1), 3)
    )
    coded = jnp.concatenate(coded + [jnp.zeros_like(coarse)], axis=0).astype(jnp.bfloat16)
    for s_r in range(nr):
        for s_f in range(nf):
            out_ref[s_f * nr + s_r, 0:sub, :] = sent[s_f * sub : (s_f + 1) * sub, s_r * 128 : (s_r + 1) * 128]
            out_ref[s_f * nr + s_r, sub : sub + 8, :] = coded


def spread_kernel(plan, got_ref, sums_ref, rows_ref):
    sub, nr, nf = plan.sub, plan.nr, plan.nf
    low_row = lanes_at((1, 128), 1) < 64
    first_row = lanes_at((1, 128), 1) < sub
    fine, coarse, moments = [[], []], [[], []], [[], []]
    for s_r in range(nr):
        ones, twos, c_ones, c_twos, invs, means = [], [], 0.0, 0.0, [], []
        for pair in range(nf // 2):
            at = 2 * pair * nr + s_r
            coded = [got_ref[at + k * nr, sub : sub + 8, :].astype(jnp.float32) for k in range(2)]
            sums = coded[0][0:1] + coded[0][1:2] + coded[1][0:1] + coded[1][1:2]
            ones.append(sums if pair == 0 else pltpu.roll(sums, 64, 1))
            twos.append(pltpu.roll(sums, 64, 1) if pair == 0 else sums)
            both = coded[0][4:5] + coded[0][5:6] + coded[0][6:7]
            invs.append(both if pair == 0 else pltpu.roll(both, 64, 1))
            means.append(pltpu.roll(both, 64, 1) if pair == 0 else both)
            for k in range(2):
                sums = coded[k][2:3] + coded[k][3:4]
                to = (2 * pair + k) * sub
                c_one = jnp.where(first_row, sums, 0.0)
                c_two = jnp.where(first_row, pltpu.roll(sums, 128 - sub, 1), 0.0)
                c_ones = c_ones + (pltpu.roll(c_one, to, 1) if to else c_one)
                c_twos = c_twos + (pltpu.roll(c_two, to, 1) if to else c_two)
        fine[0].append(jnp.where(low_row, ones[0], ones[1]))
        fine[1].append(jnp.where(low_row, twos[0], twos[1]))
        moments[0].append(jnp.where(low_row, invs[0], invs[1]))
        moments[1].append(jnp.where(low_row, means[0], means[1]))
        coarse[0].append(c_ones)
        coarse[1].append(c_twos)
    one, two, inv_std, mean, c_one, c_two = [jnp.concatenate(part, axis=1) for part in fine + moments + coarse]
    rows_ref[...] = jnp.concatenate([inv_std, mean, one, two] + [jnp.zeros_like(one)] * 4, axis=0)
    sums_ref[...] = jnp.concatenate([one, two, c_one, c_two] + [jnp.zeros_like(one)] * 4, axis=0)


def total_kernel(plan, scales, both_ref, got_ref, acts_ref, gain_ref, rows_ref, result_hbm, out_hbms, total_ref, out_ref, sems):
    sub, nr, nf = plan.sub, plan.nr, plan.nf
    totals = sum(both_ref[k] for k in range(both_ref.shape[0]))
    copies = []
    for k in range(4):
        total_ref[k] = totals[k : k + 1] * scales[k]
        copies.append(pltpu.make_async_copy(total_ref.at[k], out_hbms[k], sems.at[k]))
        copies[-1].start()
    low = lanes_at((sub, 128), 1) < 64
    source = []
    for s_r in range(nr):
        for pair in range(nf // 2):
            at = 2 * pair * nr + s_r
            left, right = [got_ref[at + k * nr, 0:sub, :].astype(jnp.float32) for k in range(2)]
            source.append(jnp.where(low, left, pltpu.roll(right, 64, 1)))
            source.append(jnp.where(low, pltpu.roll(left, 64, 1), right))
    source = jnp.concatenate(source, axis=0).astype(jnp.bfloat16)
    inv_std, mean = rows_ref[0:1], rows_ref[1:2]
    entries = 4 * plan.places * plan.group_width
    grouped = in_lane_groups(gain_ref[...] * rows_ref[2:4], plan.group_width) / entries
    group_one, group_two = grouped[0:1], grouped[1:2]
    pixels = pixel_order(plan, False)
    height = 2 * plan.local
    for k in range(2):
        chunk = pl.ds(k * height, height)
        result = one_hot_dot(pixels[k * height : (k + 1) * height], source, ((1,), (1,)))
        normed = (acts_ref[chunk, :].astype(jnp.float32) - mean) * inv_std
        out_ref[chunk, :] = (result - inv_std * (group_one + normed * group_two)).astype(jnp.bfloat16)
        copies.append(pltpu.make_async_copy(out_ref.at[chunk], result_hbm.at[chunk], sems.at[4 + k]))
        copies[-1].start()
    for copy in copies:
        copy.wait()


def in_vmem(count):
    return [pl.BlockSpec(memory_space=pltpu.VMEM)] * count


def in_hbm(count):
    return [pl.BlockSpec(memory_space=pltpu.HBM)] * count


def kept(array):
    return pltpu.with_memory_space_constraint(array, pltpu.HBM)


def shape_of(shape, kind):
    return jax.ShapeDtypeStruct(shape, kind)


LIMIT = pltpu.CompilerParams(vmem_limit_bytes=40 * 1024 * 1024)
COST = pl.CostEstimate(flops=2_000_000_000, bytes_accessed=4_000_000, transcendentals=0)


def fast_shards(
    plan,
    acts_fine,
    acts_coarse,
    grad_coarse,
    gain_fine,
    bias_fine,
    kernel_fine,
    gain_coarse,
    bias_coarse,
    kernel_coarse,
):
    nd = lax.axis_size("dp")
    count, sub, channels, places, local = plan.count, plan.sub, plan.channels, plan.places, plan.local
    f32, bf16 = jnp.float32, jnp.bfloat16
    rows = [part.reshape(1, channels) for part in (gain_coarse, bias_coarse, gain_fine, bias_fine)]
    places_of = ((local, channels), (local, channels), (4 * local, channels))
    fetched_of = pl.pallas_call(
        fetch_kernel,
        out_shape=tuple(pltpu.VMEM(shape, bf16) for shape in places_of),
        in_specs=in_hbm(3),
        out_specs=tuple(in_vmem(3)),
        scratch_shapes=[pltpu.SemaphoreType.DMA((3,))],
        compiler_params=LIMIT,
    )(*[kept(part.reshape(shape)) for part, shape in zip((grad_coarse, acts_coarse, acts_fine), places_of)])
    acts = fetched_of[2]
    packed = pl.pallas_call(
        functools.partial(pack_kernel, plan),
        out_shape=shape_of((count, plan.block_rows, 128), bf16),
        in_specs=in_vmem(3),
        out_specs=in_vmem(1)[0],
        compiler_params=LIMIT,
        cost_estimate=COST,
    )(*fetched_of)
    got = lax.all_to_all(packed, BLOCK, 0, 0)
    mine, theirs, held, inv_std, fine_acts, columns, fine_order, by_column = pl.pallas_call(
        functools.partial(coarse_kernel, plan),
        out_shape=(
            shape_of((sub, places), f32),
            shape_of((places // 128 * sub + 8, 128), bf16),
            shape_of((3, sub, places), f32),
            shape_of((sub, 128), f32),
            shape_of((4, 2 * sub, places // 2), f32),
            shape_of((4, 2 * sub, 128), f32),
            shape_of((4 * plan.nr * local, 4 * plan.nr * local), bf16),
            shape_of((places, places + places // 2), bf16),
        ),
        in_specs=in_vmem(6),
        out_specs=tuple(in_vmem(8)),
        scratch_shapes=[
            pltpu.VMEM((4 * plan.nr * local, 4 * plan.nr * local), bf16),
            pltpu.VMEM((places + 2 * plan.image, channels // 2), bf16),
            pltpu.VMEM((2 * sub, places), f32),
        ],
        compiler_params=LIMIT,
        cost_estimate=COST,
    )(got, kernel_coarse, *rows)
    both = lax.all_gather(theirs, "member")
    quartered, coarse_sums = pl.pallas_call(
        functools.partial(quarter_kernel, plan),
        out_shape=(shape_of((count, 2 * sub + sub // 2, 128), bf16), shape_of((2, 128), f32)),
        in_specs=in_vmem(6),
        out_specs=tuple(in_vmem(2)),
        compiler_params=LIMIT,
        cost_estimate=COST,
    )(mine, both, held, inv_std, columns, by_column)
    spread = lax.all_to_all(quartered, BLOCK, 0, 0)
    sent = pl.pallas_call(
        functools.partial(fine_kernel, plan),
        out_shape=shape_of((count, sub + 8, 128), bf16),
        in_specs=in_vmem(7),
        out_specs=in_vmem(1)[0],
        compiler_params=LIMIT,
        cost_estimate=COST,
    )(spread, fine_acts, both, columns, fine_order, coarse_sums, kernel_fine)
    back = lax.all_to_all(sent, BACK_BLOCK, 0, 0)
    cells = nd * places
    fine_scale, coarse_scale = 1.0 / math.sqrt(4 * cells), 1.0 / math.sqrt(cells)
    sums, moments = pl.pallas_call(
        functools.partial(spread_kernel, plan),
        out_shape=(shape_of((8, channels), f32), shape_of((8, channels), f32)),
        in_specs=in_vmem(1),
        out_specs=tuple(in_vmem(2)),
        compiler_params=LIMIT,
        cost_estimate=COST,
    )(back)
    both = lax.all_gather(sums, "dp")
    out, sums = pl.pallas_call(
        functools.partial(total_kernel, plan, (fine_scale, fine_scale, coarse_scale, coarse_scale)),
        out_shape=(pltpu.HBM((4 * local, channels), bf16), (pltpu.HBM((1, channels), f32),) * 4),
        in_specs=in_vmem(5),
        out_specs=(in_hbm(1)[0], tuple(in_hbm(4))),
        scratch_shapes=[
            pltpu.VMEM((4, 1, channels), f32),
            pltpu.VMEM((4 * local, channels), bf16),
            pltpu.SemaphoreType.DMA((6,)),
        ],
        compiler_params=LIMIT,
        cost_estimate=COST,
    )(both, back, acts, rows[2], moments)
    bias_f, gain_f, bias_c, gain_c = [part.reshape(channels) for part in sums]
    return out.reshape(acts_fine.shape), gain_f, bias_f, gain_c, bias_c


def solution(mesh):
    def function(*arrays):
        local = [size // mesh.shape[axis] for size, axis in zip(arrays[1].shape, ("dp", "frames", "rows"))]
        sizes = (mesh.shape["frames"], mesh.shape["rows"])
        plan = Plan(sizes, (*local[1:], *arrays[1].shape[3:]), arrays[5].shape[1] // mesh.shape["rows"])
        if plan.fits:
            split = (mesh.shape["dp"], plan.nf // 2, 2, plan.nr)
            used = jax.sharding.Mesh(mesh.devices.reshape(split), ("dp", "pairs", "member", "rows"))
            shards, frames = functools.partial(fast_shards, plan), ("pairs", "member")
        else:
            used, shards, frames = mesh, plain_shards, "frames"
        blocks, kernel = P("dp", frames, "rows", None, None), P(None, "rows", None)
        in_specs = (blocks, blocks, blocks, P(), P(), kernel, P(), P(), kernel)
        out_specs = (blocks, P(), P(), P(), P())
        mapped = jax.shard_map(shards, mesh=used, in_specs=in_specs, out_specs=out_specs, check_vma=False)
        return mapped(*arrays)

    return function
```

```python
import functools
import math

import jax
import jax.numpy as jnp
from jax import lax
from jax.experimental import pallas as pl
from jax.experimental.pallas import tpu as pltpu
from jax.sharding import PartitionSpec as P

GROUPS = 32
EPSILON = 1e-06
BLOCK = ("rows", "pairs", "member")
BACK_BLOCK = ("pairs", "member", "rows")
PLAIN_BLOCK = ("frames", "rows")


def plain_everyone(block, count):
    copies = jnp.broadcast_to(block[None], (count,) + block.shape)
    return lax.all_to_all(copies, PLAIN_BLOCK, 0, 0)


def ahead(field, axis, distance):
    size = field.shape[axis]
    if distance == 0:
        return field
    widths = [(0, 0)] * field.ndim
    if distance > 0:
        widths[axis] = (0, distance)
        kept = lax.slice_in_dim(field, distance, size, axis=axis)
    else:
        widths[axis] = (-distance, 0)
        kept = lax.slice_in_dim(field, 0, size + distance, axis=axis)
    return jnp.pad(kept, widths)


def tap_products(source, kernel):
    sub = kernel.shape[1]
    frames, rows, cols, channels = source.shape
    products = lax.dot_general(
        kernel.reshape(27 * sub, channels),
        source.reshape(frames * rows * cols, channels),
        (((1,), (1,)), ((), ())),
        preferred_element_type=jnp.float32,
    ).reshape(3, 3, 3, sub, frames, rows, cols)
    return sum(ahead(products[depth], 3, 2 - depth) for depth in range(3))


def coarse_conv(source, kernel):
    spatial = tap_products(source, kernel)
    total = 0.0
    for row in range(3):
        part = sum(ahead(spatial[row, col], 3, 1 - col) for col in range(3))
        total = total + ahead(part, 2, 1 - row)
    return total


def fine_conv(source, kernel):
    spatial = tap_products(source, kernel)
    result = []
    for p in range(2):
        rows_of = []
        for q in range(2):
            total = 0.0
            for row in range(3):
                part = sum(ahead(spatial[row, col], 3, (q + 1 - col) // 2) for col in range(3))
                total = total + ahead(part, 2, (p + 1 - row) // 2)
            rows_of.append(total)
        result.append(jnp.stack(rows_of, 1))
    return jnp.stack(result, 1)


def group_total(sums, group_width):
    sub = sums.shape[-1]
    if sub % group_width == 0:
        grouped = jnp.sum(sums.reshape(-1, sub // group_width, group_width), axis=-1)
        return jnp.repeat(grouped, group_width, axis=-1)
    spread = jnp.moveaxis(lax.all_gather(sums, "frames"), 0, 1).reshape(sums.shape[0], -1, group_width)
    mine = lax.axis_index("frames") * sub // group_width
    grouped = lax.dynamic_index_in_dim(jnp.sum(spread, -1), mine, 1)
    return jnp.broadcast_to(grouped, sums.shape)


def level(acts, conv_grad, cotangent, gain, bias, group_width):
    sub = acts.shape[0]
    places = acts.size // sub
    values = acts.astype(jnp.float32).reshape(sub, places)
    conv_grad = conv_grad.reshape(sub, places)
    entries = places * group_width
    moments = group_total(
        jnp.stack([jnp.sum(values, 1), jnp.sum(values * values, 1)]), group_width
    ) / entries
    mean = moments[0]
    inv_std = lax.rsqrt(moments[1] - mean * mean + EPSILON)
    normed = (values - mean[:, None]) * inv_std[:, None]
    preact = gain[:, None] * normed + bias[:, None]
    squash = jax.nn.sigmoid(preact)
    pre_grad = conv_grad * squash * (1.0 + preact * (1.0 - squash))
    sums = jnp.stack([jnp.sum(pre_grad, 1), jnp.sum(pre_grad * normed, 1)])
    terms = group_total(sums * gain, group_width) / entries
    grad = cotangent.reshape(sub, places) + inv_std[:, None] * (
        gain[:, None] * pre_grad - terms[0][:, None] - normed * terms[1][:, None]
    )
    return grad, sums


def plain_shards(
    acts_fine,
    acts_coarse,
    grad_coarse,
    gain_fine,
    bias_fine,
    kernel_fine,
    gain_coarse,
    bias_coarse,
    kernel_coarse,
):
    nf, nr, nd = lax.axis_size("frames"), lax.axis_size("rows"), lax.axis_size("dp")
    count = nf * nr
    channels = acts_fine.shape[-1]
    slice_width = kernel_fine.shape[1]
    sub = slice_width // nf
    group_width = channels // GROUPS
    tl, hl, w = acts_coarse.shape[1:4]
    frames, rows = tl * nf, hl * nr
    f, r = lax.axis_index("frames"), lax.axis_index("rows")

    gathered = plain_everyone(grad_coarse[0], count)
    source = (
        gathered.reshape(nf, nr, tl, hl, w, channels)
        .transpose(0, 2, 1, 3, 4, 5)
        .reshape(frames, rows, w, channels)
    )
    coarse_in = acts_coarse[0].reshape(tl, hl, w, nr, nf, sub).transpose(4, 3, 5, 0, 1, 2)
    coarse_in = lax.all_to_all(coarse_in.reshape(count, sub, tl * hl * w), PLAIN_BLOCK, 0, 0)
    fine_in = acts_fine[0].reshape(tl, hl, 2, w, 2, nr, nf, sub).transpose(6, 5, 7, 2, 4, 0, 1, 3)
    fine_in = lax.all_to_all(fine_in.reshape(count, sub, 4 * tl * hl * w), PLAIN_BLOCK, 0, 0)

    def mine(vector):
        return lax.dynamic_slice_in_dim(vector, r * slice_width + f * sub, sub)

    def own(kernel):
        return lax.dynamic_slice_in_dim(kernel, f * sub, sub, axis=1)

    coarse_vals = (
        coarse_in.reshape(nf, nr, sub, tl, hl, w).transpose(2, 0, 3, 1, 4, 5).reshape(sub, frames, rows, w)
    )
    cot = lax.dynamic_slice_in_dim(source, r * slice_width + f * sub, sub, axis=3)
    cot = cot.astype(jnp.float32).transpose(3, 0, 1, 2)
    conv = coarse_conv(source, own(kernel_coarse))
    coarse_grad, coarse_sums = level(
        coarse_vals, conv, cot, mine(gain_coarse), mine(bias_coarse), group_width
    )
    quartered = (coarse_grad * 0.25).astype(jnp.bfloat16)
    spread = plain_everyone(quartered, count)
    source_fine = (
        spread.reshape(nf, nr, sub, frames, rows, w)
        .transpose(3, 4, 5, 1, 0, 2)
        .reshape(frames, rows, w, channels)
    )
    conv = fine_conv(source_fine, own(kernel_fine))
    fine_vals = (
        fine_in.reshape(nf, nr, sub, 2, 2, tl, hl, w)
        .transpose(2, 3, 4, 0, 5, 1, 6, 7)
        .reshape(sub, 2, 2, frames, rows, w)
    )
    cot = jnp.broadcast_to(
        quartered.astype(jnp.float32).reshape(sub, 1, 1, frames, rows, w), conv.shape
    )
    fine_grad, fine_sums = level(
        fine_vals, conv, cot, mine(gain_fine), mine(bias_fine), group_width
    )
    back = (
        fine_grad.astype(jnp.bfloat16)
        .reshape(sub, 2, 2, nf, tl, nr, hl, w)
        .transpose(3, 5, 0, 1, 2, 4, 6, 7)
        .reshape(count, sub, 4 * tl * hl * w)
    )
    sums = plain_everyone(jnp.concatenate([fine_sums, coarse_sums]), count)
    back = lax.all_to_all(back, PLAIN_BLOCK, 0, 0)
    out = (
        back.reshape(nf, nr, sub, 2, 2, tl, hl, w)
        .transpose(5, 6, 3, 7, 4, 1, 0, 2)
        .reshape(1, tl, 2 * hl, 2 * w, channels)
    )
    sums = sums.reshape(nf, nr, 4, sub).transpose(2, 1, 0, 3).reshape(4, channels)
    totals = lax.psum(sums, "dp")
    cells = nd * frames * rows * w
    scale_fine = 1.0 / jnp.sqrt(jnp.float32(4 * cells))
    scale_coarse = 1.0 / jnp.sqrt(jnp.float32(cells))
    return (
        out,
        totals[1] * scale_fine,
        totals[0] * scale_fine,
        totals[3] * scale_coarse,
        totals[2] * scale_coarse,
    )


def lanes_at(shape, axis):
    return lax.broadcasted_iota(jnp.int32, shape, axis)


def one_hot(found):
    return found.astype(jnp.float32).astype(jnp.bfloat16)


def pixel_order(plan, swapped):
    tl, hl, w = plan.tl, plan.hl, plan.w // 2
    size = 4 * plan.local
    lane = lanes_at((1, size), 1)
    j, i, t = lane % w, lane // w % hl, lane // (w * hl) % tl
    q, p = lane // (w * hl * tl) % 2, lane // (2 * w * hl * tl) % 2
    half = lane // (4 * w * hl * tl)
    if swapped:
        half = 1 - half
    pixel = (t * 2 * hl + 2 * i + p) * 4 * w + 2 * (half * w + j) + q
    return one_hot(lanes_at((size, size), 0) == pixel)


def merged_order(nr, outer, tl, cells):
    size = nr * outer * tl * cells
    lane = lanes_at((1, size), 1)
    cell, dev = lane % cells, lane // cells % nr
    t, o = lane // (cells * nr) % tl, lane // (cells * nr * tl)
    return one_hot(lanes_at((size, size), 0) == ((dev * outer + o) * tl + t) * cells + cell)


def column_order(plan):
    w = plan.w // 2
    lines = plan.places // plan.w
    lane = lanes_at((1, 4 * lines * w + 4 * lines), 1)
    inner = lane % (lines * w)
    place = inner // w * plan.w + lane // (lines * w) * w + inner % w
    past = lane - 2 * lines * w
    border = past % lines * plan.w + jnp.where(past < 2 * lines, w, w - 1)
    wanted = jnp.where(past >= 0, border, place)
    shape = (plan.places, 2 * lines * w + 4 * lines)
    return one_hot(lanes_at(shape, 0) == wanted[:, : shape[1]])


def one_hot_dot(a, b, dims):
    return lax.dot_general(a, b, (dims, ((), ())), preferred_element_type=jnp.float32)


def moved(field, distance, kept):
    size = field.shape[1]
    return jnp.where(kept, pltpu.roll(field, (-distance) % size, 1), 0.0)


def own_column(row, base, sub):
    shape = (sub, row.shape[1])
    mine = lanes_at(shape, 1) == lanes_at(shape, 0) + base
    return jnp.sum(jnp.where(mine, row, 0.0), axis=1, keepdims=True)


def as_row(column):
    shape = (column.shape[0], 128)
    here = lanes_at(shape, 1) == lanes_at(shape, 0)
    return jnp.sum(jnp.where(here, column, 0.0), axis=0, keepdims=True)


def terms(value, count):
    found = []
    for _ in range(count):
        found.append(value.astype(jnp.bfloat16).astype(jnp.float32))
        value = value - found[-1]
    return found


def in_groups(column, group_width):
    sub = column.shape[0]
    grouped = jnp.sum(column.reshape(sub // group_width, group_width, 1), axis=1, keepdims=True)
    return jnp.broadcast_to(grouped, (sub // group_width, group_width, 1)).reshape(sub, 1)


def total(parts):
    return sum(jnp.sum(part, axis=1, keepdims=True) for part in parts)


def statistics(one, two, entries, group_width):
    mean = in_groups(one, group_width) / entries
    square = in_groups(two, group_width) / entries
    return mean, lax.rsqrt(square - mean * mean + EPSILON)


def normalised(parts, gain, bias, mean, inv_std):
    normed, slope = [], []
    for part in parts:
        unit = (part - mean) * inv_std
        preact = gain * unit + bias
        squash = 0.5 + 0.5 * jnp.tanh(0.5 * preact)
        normed.append(unit)
        slope.append(squash * (1.0 + preact * (1.0 - squash)))
    return normed, slope


class Plan:
    def __init__(self, mesh_sizes, acts_coarse, slice_width):
        self.nf, self.nr = mesh_sizes
        self.count = self.nf * self.nr
        self.tl, self.hl, self.w, self.channels = acts_coarse
        self.slice_width = slice_width
        self.sub = slice_width // self.nf
        self.cells = self.hl * self.w
        self.local = self.tl * self.cells
        self.image = self.cells * self.nr
        self.frames = self.tl * self.nf
        self.places = self.frames * self.image
        self.group_width = self.channels // GROUPS
        self.chunks = self.channels // 128
        self.acts_at = self.chunks // 2 * self.local
        self.packed_at = self.acts_at + self.sub
        self.cot_at = self.packed_at + 8
        self.block_rows = self.cot_at + 8
        self.fits = (
            self.sub == 32
            and self.slice_width == 128
            and self.group_width == 16
            and self.cells == 16
            and self.w == 8
            and self.tl == 2
            and self.nr == 4
            and self.nf == 4
            and self.slice_width * self.nr == self.channels
        )

    def place_masks(self, w):
        lane = lanes_at((1, self.places // self.w * w), 1)
        col, row = lane % w, lane // w % (self.hl * self.nr)
        last_row = self.hl * self.nr - 1
        return (lane, col > 0, col < w - 1, row > 0, row < last_row)


def fetched(pairs, sems):
    copies = [pltpu.make_async_copy(src, dst, sems.at[k]) for k, (src, dst) in enumerate(pairs)]
    for copy in copies:
        copy.start()
    return copies


def own_place(plan):
    pair, member, r = lax.axis_index("pairs"), lax.axis_index("member"), lax.axis_index("rows")
    return pair, member, r, r * plan.slice_width + (2 * pair + member) * plan.sub


def fetch_kernel(g_hbm, coarse_hbm, fine_hbm, g_ref, coarse_ref, fine_ref, sems):
    for copy in fetched([(fine_hbm, fine_ref), (coarse_hbm, coarse_ref), (g_hbm, g_ref)], sems):
        copy.wait()


def pack_kernel(plan, g_ref, coarse_ref, fine_ref, out_ref):
    sub, chunks, local = plan.sub, plan.chunks, plan.local
    shape = (2 * local, 2 * 128)
    lane = lanes_at((1, 2 * 128), 1)
    repeated = one_hot(lanes_at(shape, 0) == lane % local + lane // 128 * local)
    shape = (plan.channels, 128)
    quarter = lanes_at(shape, 0) // 8 % 4 == lanes_at(shape, 1) // local
    orders = jnp.concatenate([pixel_order(plan, swapped) for swapped in (False, True)], axis=1)
    acts = fine_ref[...]
    halves = one_hot_dot(acts, orders, ((0,), (0,))).astype(jnp.bfloat16)
    halves = [halves[:, :128], halves[:, 128:]]
    small = one_hot_dot(jnp.concatenate([coarse_ref[...], g_ref[...]], axis=0), repeated, ((0,), (0,)))
    for k, at in enumerate((plan.packed_at, plan.cot_at)):
        rows_of = jnp.where(quarter, small[:, k * 128 : (k + 1) * 128], 0.0).reshape(plan.count, 4, 8, 128)
        out_ref[:, at : at + 8, :] = jnp.sum(rows_of, axis=1).astype(jnp.bfloat16)
    low = lanes_at((sub, 128), 1) < 64
    for s_r in range(plan.nr):
        for s_f in range(plan.nf):
            dest = s_r * plan.nf + s_f
            first, half = s_r * plan.slice_width + s_f // 2 * 2 * sub, s_f % 2
            for k in range(chunks // 2):
                at = (half * chunks // 2 + k) * 128
                out_ref[dest, k * local : (k + 1) * local, :] = g_ref[:, at : at + 128]
            upper, lower = halves[half][first : first + sub], halves[1 - half][first + sub : first + 2 * sub]
            out_ref[dest, plan.acts_at : plan.packed_at, :] = jnp.where(low, upper, lower)


def by_frame_device(plan, got_ref, at, height):
    return jnp.concatenate(
        [
            jnp.concatenate(
                [got_ref[r * plan.nf + f, at : at + height, :] for r in range(plan.nr)], axis=1
            )
            for f in range(plan.nf)
        ],
        axis=0,
    )


def in_places(plan, merged, height):
    width = plan.tl * plan.image
    return [
        jnp.concatenate(
            [merged[f * height : (f + 1) * height, k * width : (k + 1) * width] for f in range(plan.nf)],
            axis=1,
        )
        for k in range(4)
    ]


def coarse_kernel(
    plan,
    got_ref,
    weights,
    gain_c,
    bias_c,
    gain_f,
    bias_f,
    mine_ref,
    sent_ref,
    held_ref,
    inv_ref,
    fine_ref,
    columns,
    fine_order,
    by_column,
    order,
    source,
    conv_ref,
):
    sub, nr, nf, cells, tl, local = plan.sub, plan.nr, plan.nf, plan.cells, plan.tl, plan.local
    wide, depth = 2 * sub, plan.channels // 2
    pair, member, r, base = own_place(plan)
    first = r * plan.slice_width + pair * wide
    columns[0, 0:sub, :] = jnp.broadcast_to(own_column(gain_c[...], base, sub), (sub, 128))
    columns[1, 0:sub, :] = jnp.broadcast_to(own_column(bias_c[...], base, sub), (sub, 128))
    columns[2] = jnp.broadcast_to(own_column(gain_f[...], first, wide), (wide, 128))
    columns[3] = jnp.broadcast_to(own_column(bias_f[...], first, wide), (wide, 128))
    order[...] = merged_order(plan.nr, 4, plan.tl, plan.cells)
    fine_order[...] = merged_order(plan.nr, 8, plan.tl, plan.cells // 2)
    by_column[...] = column_order(plan)
    both = pl.ds(pl.multiple_of(pair * wide, wide), wide)
    half = pl.ds(pl.multiple_of(member * depth, depth), depth)
    for s_f in range(nf):
        for s_r in range(nr):
            for t in range(tl):
                at = (s_f * tl + t) * plan.image + s_r * cells
                for k in range(plan.chunks // 2):
                    source[at : at + cells, k * 128 : (k + 1) * 128] = got_ref[
                        s_r * nf + s_f, k * local + t * cells : k * local + (t + 1) * cells, :
                    ]
    source[plan.places :, :] = jnp.zeros((2 * plan.image, depth), jnp.bfloat16)
    products = sum(
        one_hot_dot(
            weights[9 * k : 9 * k + 9, both, half].reshape(9 * wide, depth),
            source[(2 - k) * plan.image : (2 - k) * plan.image + plan.places, :],
            ((1,), (1,)),
        )
        for k in range(3)
    )
    merged = one_hot_dot(by_frame_device(plan, got_ref, plan.acts_at, sub), fine_order[...], ((1,), (0,)))
    parts = halves_at(plan, merged)
    for pq in range(4):
        fine_ref[pq] = parts[pq]
    one, two = total(parts), total([part * part for part in parts])
    stats = terms(as_row(one) + pltpu.roll(as_row(two), 64, 1), 3)
    stats = jnp.concatenate(stats + [jnp.zeros_like(stats[0])] * 5, axis=0).astype(jnp.bfloat16)
    small = [by_frame_device(plan, got_ref, at, 8) for at in (plan.packed_at, plan.cot_at)]
    merged = one_hot_dot(jnp.concatenate(small, axis=0), order[...], ((1,), (0,)))
    rows_of = 8 * nf
    values, cot = [
        jnp.concatenate(in_places(plan, merged[k * rows_of : (k + 1) * rows_of], 8), axis=0) for k in range(2)
    ]
    gain, bias = columns[0][0:sub, 0:1], columns[1][0:sub, 0:1]
    entries = plan.places * plan.group_width
    mean, inv_std = statistics(total([values]), total([values * values]), entries, plan.group_width)
    (normed,), (slope,) = normalised([values], gain, bias, mean, inv_std)
    held_ref[0], held_ref[1], held_ref[2] = normed, slope, cot
    inv_ref[...] = jnp.broadcast_to(inv_std, (sub, 128))
    lane, has_left, has_right, has_up, has_down = plan.place_masks(plan.w)
    by_col = []
    for col in range(3):
        parts = [products[(3 * row + col) * wide : (3 * row + col + 1) * wide] for row in range(3)]
        by_col.append(parts[1] + moved(parts[0], plan.w, has_down) + moved(parts[2], -plan.w, has_up))
    conv_ref[...] = by_col[1] + moved(by_col[0], 1, has_right) + moved(by_col[2], -1, has_left)
    mine_ref[...] = conv_ref[pl.ds(pl.multiple_of(member * sub, sub), sub), :]
    theirs = conv_ref[pl.ds(pl.multiple_of((1 - member) * sub, sub), sub), :]
    for k in range(plan.places // 128):
        sent_ref[k * sub : (k + 1) * sub, :] = theirs[:, k * 128 : (k + 1) * 128].astype(jnp.bfloat16)
    sent_ref[plan.places // 128 * sub :, :] = stats


def quarter_kernel(plan, mine_ref, both_ref, held_ref, inv_ref, columns, by_column, out_ref, sums_ref):
    sub = plan.sub
    _, member, _, _ = own_place(plan)
    theirs = [both_ref[1 - member, k * sub : (k + 1) * sub, :] for k in range(plan.places // 128)]
    conv = mine_ref[...] + jnp.concatenate(theirs, axis=1).astype(jnp.float32)
    normed, slope, cot = held_ref[0], held_ref[1], held_ref[2]
    gain, inv_std = columns[0][0:sub, 0:1], inv_ref[:, 0:1]
    entries = plan.places * plan.group_width
    pre = conv * slope
    one, two = total([pre]), total([pre * normed])
    group_one = in_groups(gain * one, plan.group_width) / entries
    group_two = in_groups(gain * two, plan.group_width) / entries
    grad = cot + inv_std * (gain * pre - group_one - normed * group_two)
    quartered = (grad * 0.25).astype(jnp.bfloat16)
    sent = one_hot_dot(quartered, by_column[...], ((1,), (0,))).astype(jnp.bfloat16)
    low = lanes_at((sub // 2, 128), 1) < 64
    for half in range(2):
        at = half * 256
        border = sent[:, 512 + half * 128 : 640 + half * 128]
        border = jnp.where(low, border[: sub // 2], border[sub // 2 :])
        for dest in range(half, plan.count, 2):
            out_ref[dest, 0:sub, :] = sent[:, at : at + 128]
            out_ref[dest, sub : 2 * sub, :] = sent[:, at + 128 : at + 256]
            out_ref[dest, 2 * sub : 2 * sub + sub // 2, :] = border
    sums_ref[...] = jnp.concatenate([as_row(one), as_row(two)], axis=0)


def halves_at(plan, merged):
    sub = plan.sub
    turned = jnp.concatenate([pltpu.roll(merged[:, k * 128 : (k + 1) * 128], 64, 1) for k in range(4)], axis=1)
    low = lanes_at((sub, 128), 1) < 64
    parts = []
    for pq in range(4):
        groups = []
        for group in range(2):
            e = 4 * group + pq
            at = e // 2 * 128
            strips = []
            for m in range(plan.nf // 2):
                first, second = slice(2 * m * sub, (2 * m + 1) * sub), slice((2 * m + 1) * sub, (2 * m + 2) * sub)
                if e % 2 == 0:
                    strips.append(jnp.where(low, merged[first, at : at + 128], turned[second, at : at + 128]))
                else:
                    strips.append(jnp.where(low, turned[first, at : at + 128], merged[second, at : at + 128]))
            groups.append(jnp.concatenate(strips, axis=1))
        parts.append(jnp.concatenate(groups, axis=0))
    return parts


def halves_from(plan, parts):
    sub = plan.sub
    low = lanes_at((sub, 128), 1) < 64
    down = []
    for f in range(plan.nf):
        across = []
        for v in range(4):
            pair = []
            for e in (2 * v, 2 * v + 1):
                group, pq = e // 4, e % 4
                strip = parts[pq][group * sub : (group + 1) * sub, f // 2 * 128 : (f // 2 + 1) * 128]
                pair.append(strip if e % 2 == f % 2 else pltpu.roll(strip, 64, 1))
            across.append(jnp.where(low, pair[0], pair[1]))
        down.append(jnp.concatenate(across, axis=1))
    return jnp.concatenate(down, axis=0)


def fine_kernel(
    plan, got_ref, acts_ref, both_ref, columns, order, sums_ref, weights, out_ref
):
    sub, nr, nf, wide = plan.sub, plan.nr, plan.nf, 2 * plan.sub
    pair, member, r, _ = own_place(plan)
    both = pl.ds(pl.multiple_of(pair * wide, wide), wide)
    w = plan.w // 2
    lines = plan.places // plan.w
    places = lines * w
    source = jnp.concatenate(
        [got_ref[:, k * sub : (k + 1) * sub, :].reshape(plan.channels, 128) for k in range(2)], axis=1
    )
    packed = got_ref[:, wide : wide + sub // 2, :].reshape(plan.count * sub // 2, 128)
    shape = (128, places)
    beside = lanes_at(shape, 1) == lanes_at(shape, 0) % lines * w + (1 - member) * (w - 1)
    border = []
    for k in range(2):
        here = one_hot(beside & (lanes_at(shape, 0) // lines == k))
        found = one_hot_dot(packed, here, ((1,), (0,))).astype(jnp.bfloat16)
        border.append(found.reshape(plan.count, sub // 2, places))
    border = jnp.concatenate(border, axis=1).reshape(plan.channels, places)
    image = plan.image // 2
    sums, extras = 0.0, 0.0
    for k in (2, 1, 0):
        here, beside = source, border
        if k < 2:
            shift = (2 - k) * image
            inside = lanes_at((1, places), 1) < places - shift
            here, beside = [
                jnp.where(inside, pltpu.roll(part, places - shift, 1), jnp.zeros_like(part)) for part in (here, beside)
            ]
        sums = sums + one_hot_dot(
            weights[9 * k : 9 * k + 9, both, :].reshape(9 * wide, plan.channels), here, ((1,), (0,))
        )
        facing = jnp.concatenate([weights[9 * k + 3 * row + 2 * member, both, :] for row in range(3)], axis=0)
        extras = extras + one_hot_dot(facing, beside, ((1,), (0,)))
    parts = [acts_ref[pq] for pq in range(4)]
    at = plan.places // 128 * sub
    stats = sum(both_ref[k, at : at + 8, :].astype(jnp.float32) for k in range(2))
    stats = stats[0:1] + stats[1:2] + stats[2:3]
    entries = 4 * plan.places * plan.group_width
    one, two = own_column(stats, 0, wide), own_column(stats, 64, wide)
    mean, inv_std = statistics(one, two, entries, plan.group_width)
    gain, bias = columns[2][:, 0:1], columns[3][:, 0:1]
    normed, slope = normalised(parts, gain, bias, mean, inv_std)
    lane, has_left, has_right, has_up, has_down = plan.place_masks(w)
    right, left = (1 - member).astype(jnp.float32), member.astype(jnp.float32)
    by_row = []
    for row in range(3):
        a, b, c = [sums[(3 * row + col) * wide : (3 * row + col + 1) * wide] for col in range(3)]
        extra = extras[row * wide : (row + 1) * wide]
        by_row.append(
            (a + b + moved(c, -1, has_left) + left * extra, moved(a, 1, has_right) + b + c + right * extra)
        )
    convs = [by_row[0][q] + by_row[1][q] + moved(by_row[2][q], -w, has_up) for q in range(2)]
    convs += [moved(by_row[0][q], w, has_down) + by_row[1][q] + by_row[2][q] for q in range(2)]
    pre = [conv * part for conv, part in zip(convs, slope)]
    one = total(pre)
    two = total([a * b for a, b in zip(pre, normed)])
    cot = jnp.concatenate(
        [
            jnp.concatenate(
                [got_ref[r * nf + 2 * pair + m, k * sub : (k + 1) * sub, :] for k in range(2)], axis=1
            )
            for m in range(2)
        ],
        axis=0,
    ).astype(jnp.float32)
    scale = inv_std * gain
    stacked = halves_from(plan, [cot + scale * part for part in pre]).astype(jnp.bfloat16)
    sent = one_hot_dot(stacked, order[...], ((1,), (1,))).astype(jnp.bfloat16)
    coarse = sums_ref[0:1] + pltpu.roll(sums_ref[1:2], sub, 1)
    group_one = in_groups(gain * one, plan.group_width) / entries
    group_two = in_groups(gain * two, plan.group_width) / entries
    coded = (
        terms(as_row(one) + pltpu.roll(as_row(two), 64, 1), 2)
        + terms(coarse, 2)
        + terms(as_row(inv_std) + pltpu.roll(as_row(mean), 64, 1), 2)
        + terms(as_row(group_one) + pltpu.roll(as_row(group_two), 64, 1), 2)
    )
    coded = jnp.concatenate(coded, axis=0).astype(jnp.bfloat16)
    for s_r in range(nr):
        for s_f in range(nf):
            out_ref[s_f * nr + s_r, 0:sub, :] = sent[s_f * sub : (s_f + 1) * sub, s_r * 128 : (s_r + 1) * 128]
            out_ref[s_f * nr + s_r, sub : sub + 8, :] = coded


def spread_kernel(plan, got_ref, acts_ref, out_ref, sums_ref):
    sub, nr, nf = plan.sub, plan.nr, plan.nf
    low = lanes_at((sub, 128), 1) < 64
    low_row = lanes_at((1, 128), 1) < 64
    first_row = lanes_at((1, 128), 1) < sub
    source = []
    fine, coarse, moments, groups = [[], []], [[], []], [[], []], [[], []]
    for s_r in range(nr):
        ones, twos, c_ones, c_twos, invs, means = [], [], 0.0, 0.0, [], []
        g_ones, g_twos = [], []
        for pair in range(nf // 2):
            at = 2 * pair * nr + s_r
            left, right = [got_ref[at + k * nr, 0:sub, :].astype(jnp.float32) for k in range(2)]
            source.append(jnp.where(low, left, pltpu.roll(right, 64, 1)))
            source.append(jnp.where(low, pltpu.roll(left, 64, 1), right))
            coded = [got_ref[at + k * nr, sub : sub + 8, :].astype(jnp.float32) for k in range(2)]
            sums = coded[0][0:1] + coded[0][1:2] + coded[1][0:1] + coded[1][1:2]
            ones.append(sums if pair == 0 else pltpu.roll(sums, 64, 1))
            twos.append(pltpu.roll(sums, 64, 1) if pair == 0 else sums)
            grouped = coded[0][6:7] + coded[0][7:8] + coded[1][6:7] + coded[1][7:8]
            g_ones.append(grouped if pair == 0 else pltpu.roll(grouped, 64, 1))
            g_twos.append(pltpu.roll(grouped, 64, 1) if pair == 0 else grouped)
            both = coded[0][4:5] + coded[0][5:6]
            invs.append(both if pair == 0 else pltpu.roll(both, 64, 1))
            means.append(pltpu.roll(both, 64, 1) if pair == 0 else both)
            for k in range(2):
                sums = coded[k][2:3] + coded[k][3:4]
                to = (2 * pair + k) * sub
                c_one = jnp.where(first_row, sums, 0.0)
                c_two = jnp.where(first_row, pltpu.roll(sums, 128 - sub, 1), 0.0)
                c_ones = c_ones + (pltpu.roll(c_one, to, 1) if to else c_one)
                c_twos = c_twos + (pltpu.roll(c_two, to, 1) if to else c_two)
        fine[0].append(jnp.where(low_row, ones[0], ones[1]))
        fine[1].append(jnp.where(low_row, twos[0], twos[1]))
        groups[0].append(jnp.where(low_row, g_ones[0], g_ones[1]))
        groups[1].append(jnp.where(low_row, g_twos[0], g_twos[1]))
        moments[0].append(jnp.where(low_row, invs[0], invs[1]))
        moments[1].append(jnp.where(low_row, means[0], means[1]))
        coarse[0].append(c_ones)
        coarse[1].append(c_twos)
    one, two, inv_std, mean, c_one, c_two, group_one, group_two = [
        jnp.concatenate(part, axis=1) for part in fine + moments + coarse + groups
    ]
    source = jnp.concatenate(source, axis=0).astype(jnp.bfloat16)
    result = one_hot_dot(pixel_order(plan, False), source, ((1,), (1,)))
    normed = (acts_ref[...].astype(jnp.float32) - mean) * inv_std
    out_ref[...] = (result - inv_std * (group_one + normed * group_two)).astype(jnp.bfloat16)
    sums_ref[...] = jnp.concatenate([one, two, c_one, c_two] + [jnp.zeros_like(one)] * 4, axis=0)


def total_kernel(scales, both_ref, result_ref, result_hbm, out_hbms, rows_ref, sems):
    copies = fetched([(result_ref, result_hbm)], sems)
    rows = sum(both_ref[k] for k in range(both_ref.shape[0]))
    for k in range(4):
        rows_ref[k] = rows[k : k + 1] * scales[k]
    for k in range(4):
        copies.append(pltpu.make_async_copy(rows_ref.at[k], out_hbms[k], sems.at[k + 1]))
        copies[-1].start()
    for copy in copies:
        copy.wait()


def in_vmem(count):
    return [pl.BlockSpec(memory_space=pltpu.VMEM)] * count


def in_hbm(count):
    return [pl.BlockSpec(memory_space=pltpu.HBM)] * count


def kept(array):
    return pltpu.with_memory_space_constraint(array, pltpu.HBM)


def shape_of(shape, kind):
    return jax.ShapeDtypeStruct(shape, kind)


LIMIT = pltpu.CompilerParams(vmem_limit_bytes=40 * 1024 * 1024)
COST = pl.CostEstimate(flops=2_000_000_000, bytes_accessed=4_000_000, transcendentals=0)


def fast_shards(
    plan,
    acts_fine,
    acts_coarse,
    grad_coarse,
    gain_fine,
    bias_fine,
    kernel_fine,
    gain_coarse,
    bias_coarse,
    kernel_coarse,
):
    nd = lax.axis_size("dp")
    count, sub, channels, places, local = plan.count, plan.sub, plan.channels, plan.places, plan.local
    f32, bf16 = jnp.float32, jnp.bfloat16
    rows = [part.reshape(1, channels) for part in (gain_coarse, bias_coarse, gain_fine, bias_fine)]
    places_of = ((local, channels), (local, channels), (4 * local, channels))
    fetched_of = pl.pallas_call(
        fetch_kernel,
        out_shape=tuple(pltpu.VMEM(shape, bf16) for shape in places_of),
        in_specs=in_hbm(3),
        out_specs=tuple(in_vmem(3)),
        scratch_shapes=[pltpu.SemaphoreType.DMA((3,))],
        compiler_params=LIMIT,
    )(*[kept(part.reshape(shape)) for part, shape in zip((grad_coarse, acts_coarse, acts_fine), places_of)])
    acts = fetched_of[2]
    packed = pl.pallas_call(
        functools.partial(pack_kernel, plan),
        out_shape=shape_of((count, plan.block_rows, 128), bf16),
        in_specs=in_vmem(3),
        out_specs=in_vmem(1)[0],
        compiler_params=LIMIT,
        cost_estimate=COST,
    )(*fetched_of)
    got = lax.all_to_all(packed, BLOCK, 0, 0)
    mine, theirs, held, inv_std, fine_acts, columns, fine_order, by_column = pl.pallas_call(
        functools.partial(coarse_kernel, plan),
        out_shape=(
            shape_of((sub, places), f32),
            shape_of((places // 128 * sub + 8, 128), bf16),
            shape_of((3, sub, places), f32),
            shape_of((sub, 128), f32),
            shape_of((4, 2 * sub, places // 2), f32),
            shape_of((4, 2 * sub, 128), f32),
            shape_of((4 * plan.nr * local, 4 * plan.nr * local), bf16),
            shape_of((places, places + places // 2), bf16),
        ),
        in_specs=in_vmem(6),
        out_specs=tuple(in_vmem(8)),
        scratch_shapes=[
            pltpu.VMEM((4 * plan.nr * local, 4 * plan.nr * local), bf16),
            pltpu.VMEM((places + 2 * plan.image, channels // 2), bf16),
            pltpu.VMEM((2 * sub, places), f32),
        ],
        compiler_params=LIMIT,
        cost_estimate=COST,
    )(got, kernel_coarse, *rows)
    both = lax.all_gather(theirs, "member")
    quartered, coarse_sums = pl.pallas_call(
        functools.partial(quarter_kernel, plan),
        out_shape=(shape_of((count, 2 * sub + sub // 2, 128), bf16), shape_of((2, 128), f32)),
        in_specs=in_vmem(6),
        out_specs=tuple(in_vmem(2)),
        compiler_params=LIMIT,
        cost_estimate=COST,
    )(mine, both, held, inv_std, columns, by_column)
    spread = lax.all_to_all(quartered, BLOCK, 0, 0)
    sent = pl.pallas_call(
        functools.partial(fine_kernel, plan),
        out_shape=shape_of((count, sub + 8, 128), bf16),
        in_specs=in_vmem(7),
        out_specs=in_vmem(1)[0],
        compiler_params=LIMIT,
        cost_estimate=COST,
    )(spread, fine_acts, both, columns, fine_order, coarse_sums, kernel_fine)
    back = lax.all_to_all(sent, BACK_BLOCK, 0, 0)
    cells = nd * places
    fine_scale, coarse_scale = 1.0 / math.sqrt(4 * cells), 1.0 / math.sqrt(cells)
    out, sums = pl.pallas_call(
        functools.partial(spread_kernel, plan),
        out_shape=(pltpu.VMEM((4 * local, channels), bf16), shape_of((8, channels), f32)),
        in_specs=in_vmem(2),
        out_specs=tuple(in_vmem(2)),
        compiler_params=LIMIT,
        cost_estimate=COST,
    )(back, acts)
    both = lax.all_gather(sums, "dp")
    out, sums = pl.pallas_call(
        functools.partial(total_kernel, (fine_scale, fine_scale, coarse_scale, coarse_scale)),
        out_shape=(pltpu.HBM((4 * local, channels), bf16), (pltpu.HBM((1, channels), f32),) * 4),
        in_specs=in_vmem(2),
        out_specs=(in_hbm(1)[0], tuple(in_hbm(4))),
        scratch_shapes=[pltpu.VMEM((4, 1, channels), f32), pltpu.SemaphoreType.DMA((5,))],
        compiler_params=LIMIT,
        cost_estimate=COST,
    )(both, out)
    bias_f, gain_f, bias_c, gain_c = [part.reshape(channels) for part in sums]
    return out.reshape(acts_fine.shape), gain_f, bias_f, gain_c, bias_c


def solution(mesh):
    def function(*arrays):
        local = [size // mesh.shape[axis] for size, axis in zip(arrays[1].shape, ("dp", "frames", "rows"))]
        sizes = (mesh.shape["frames"], mesh.shape["rows"])
        plan = Plan(sizes, (*local[1:], *arrays[1].shape[3:]), arrays[5].shape[1] // mesh.shape["rows"])
        if plan.fits:
            split = (mesh.shape["dp"], plan.nf // 2, 2, plan.nr)
            used = jax.sharding.Mesh(mesh.devices.reshape(split), ("dp", "pairs", "member", "rows"))
            shards, frames = functools.partial(fast_shards, plan), ("pairs", "member")
        else:
            used, shards, frames = mesh, plain_shards, "frames"
        blocks, kernel = P("dp", frames, "rows", None, None), P(None, "rows", None)
        in_specs = (blocks, blocks, blocks, P(), P(), kernel, P(), P(), kernel)
        out_specs = (blocks, P(), P(), P(), P())
        mapped = jax.shard_map(shards, mesh=used, in_specs=in_specs, out_specs=out_specs, check_vma=False)
        return mapped(*arrays)

    return function
```

```python
import functools
import math

import jax
import jax.numpy as jnp
from jax import lax
from jax.experimental import pallas as pl
from jax.experimental.pallas import tpu as pltpu
from jax.sharding import PartitionSpec as P

GROUPS = 32
EPSILON = 1e-06
BLOCK = ("rows", "pairs", "member")
BACK_BLOCK = ("pairs", "member", "rows")
PLAIN_BLOCK = ("frames", "rows")


def plain_everyone(block, count):
    copies = jnp.broadcast_to(block[None], (count,) + block.shape)
    return lax.all_to_all(copies, PLAIN_BLOCK, 0, 0)


def ahead(field, axis, distance):
    size = field.shape[axis]
    if distance == 0:
        return field
    widths = [(0, 0)] * field.ndim
    if distance > 0:
        widths[axis] = (0, distance)
        kept = lax.slice_in_dim(field, distance, size, axis=axis)
    else:
        widths[axis] = (-distance, 0)
        kept = lax.slice_in_dim(field, 0, size + distance, axis=axis)
    return jnp.pad(kept, widths)


def tap_products(source, kernel):
    sub = kernel.shape[1]
    frames, rows, cols, channels = source.shape
    products = lax.dot_general(
        kernel.reshape(27 * sub, channels),
        source.reshape(frames * rows * cols, channels),
        (((1,), (1,)), ((), ())),
        preferred_element_type=jnp.float32,
    ).reshape(3, 3, 3, sub, frames, rows, cols)
    return sum(ahead(products[depth], 3, 2 - depth) for depth in range(3))


def coarse_conv(source, kernel):
    spatial = tap_products(source, kernel)
    total = 0.0
    for row in range(3):
        part = sum(ahead(spatial[row, col], 3, 1 - col) for col in range(3))
        total = total + ahead(part, 2, 1 - row)
    return total


def fine_conv(source, kernel):
    spatial = tap_products(source, kernel)
    result = []
    for p in range(2):
        rows_of = []
        for q in range(2):
            total = 0.0
            for row in range(3):
                part = sum(ahead(spatial[row, col], 3, (q + 1 - col) // 2) for col in range(3))
                total = total + ahead(part, 2, (p + 1 - row) // 2)
            rows_of.append(total)
        result.append(jnp.stack(rows_of, 1))
    return jnp.stack(result, 1)


def group_total(sums, group_width):
    sub = sums.shape[-1]
    if sub % group_width == 0:
        grouped = jnp.sum(sums.reshape(-1, sub // group_width, group_width), axis=-1)
        return jnp.repeat(grouped, group_width, axis=-1)
    spread = jnp.moveaxis(lax.all_gather(sums, "frames"), 0, 1).reshape(sums.shape[0], -1, group_width)
    mine = lax.axis_index("frames") * sub // group_width
    grouped = lax.dynamic_index_in_dim(jnp.sum(spread, -1), mine, 1)
    return jnp.broadcast_to(grouped, sums.shape)


def level(acts, conv_grad, cotangent, gain, bias, group_width):
    sub = acts.shape[0]
    places = acts.size // sub
    values = acts.astype(jnp.float32).reshape(sub, places)
    conv_grad = conv_grad.reshape(sub, places)
    entries = places * group_width
    moments = group_total(
        jnp.stack([jnp.sum(values, 1), jnp.sum(values * values, 1)]), group_width
    ) / entries
    mean = moments[0]
    inv_std = lax.rsqrt(moments[1] - mean * mean + EPSILON)
    normed = (values - mean[:, None]) * inv_std[:, None]
    preact = gain[:, None] * normed + bias[:, None]
    squash = jax.nn.sigmoid(preact)
    pre_grad = conv_grad * squash * (1.0 + preact * (1.0 - squash))
    sums = jnp.stack([jnp.sum(pre_grad, 1), jnp.sum(pre_grad * normed, 1)])
    terms = group_total(sums * gain, group_width) / entries
    grad = cotangent.reshape(sub, places) + inv_std[:, None] * (
        gain[:, None] * pre_grad - terms[0][:, None] - normed * terms[1][:, None]
    )
    return grad, sums


def plain_shards(
    acts_fine,
    acts_coarse,
    grad_coarse,
    gain_fine,
    bias_fine,
    kernel_fine,
    gain_coarse,
    bias_coarse,
    kernel_coarse,
):
    nf, nr, nd = lax.axis_size("frames"), lax.axis_size("rows"), lax.axis_size("dp")
    count = nf * nr
    channels = acts_fine.shape[-1]
    slice_width = kernel_fine.shape[1]
    sub = slice_width // nf
    group_width = channels // GROUPS
    tl, hl, w = acts_coarse.shape[1:4]
    frames, rows = tl * nf, hl * nr
    f, r = lax.axis_index("frames"), lax.axis_index("rows")

    gathered = plain_everyone(grad_coarse[0], count)
    source = (
        gathered.reshape(nf, nr, tl, hl, w, channels)
        .transpose(0, 2, 1, 3, 4, 5)
        .reshape(frames, rows, w, channels)
    )
    coarse_in = acts_coarse[0].reshape(tl, hl, w, nr, nf, sub).transpose(4, 3, 5, 0, 1, 2)
    coarse_in = lax.all_to_all(coarse_in.reshape(count, sub, tl * hl * w), PLAIN_BLOCK, 0, 0)
    fine_in = acts_fine[0].reshape(tl, hl, 2, w, 2, nr, nf, sub).transpose(6, 5, 7, 2, 4, 0, 1, 3)
    fine_in = lax.all_to_all(fine_in.reshape(count, sub, 4 * tl * hl * w), PLAIN_BLOCK, 0, 0)

    def mine(vector):
        return lax.dynamic_slice_in_dim(vector, r * slice_width + f * sub, sub)

    def own(kernel):
        return lax.dynamic_slice_in_dim(kernel, f * sub, sub, axis=1)

    coarse_vals = (
        coarse_in.reshape(nf, nr, sub, tl, hl, w).transpose(2, 0, 3, 1, 4, 5).reshape(sub, frames, rows, w)
    )
    cot = lax.dynamic_slice_in_dim(source, r * slice_width + f * sub, sub, axis=3)
    cot = cot.astype(jnp.float32).transpose(3, 0, 1, 2)
    conv = coarse_conv(source, own(kernel_coarse))
    coarse_grad, coarse_sums = level(
        coarse_vals, conv, cot, mine(gain_coarse), mine(bias_coarse), group_width
    )
    quartered = (coarse_grad * 0.25).astype(jnp.bfloat16)
    spread = plain_everyone(quartered, count)
    source_fine = (
        spread.reshape(nf, nr, sub, frames, rows, w)
        .transpose(3, 4, 5, 1, 0, 2)
        .reshape(frames, rows, w, channels)
    )
    conv = fine_conv(source_fine, own(kernel_fine))
    fine_vals = (
        fine_in.reshape(nf, nr, sub, 2, 2, tl, hl, w)
        .transpose(2, 3, 4, 0, 5, 1, 6, 7)
        .reshape(sub, 2, 2, frames, rows, w)
    )
    cot = jnp.broadcast_to(
        quartered.astype(jnp.float32).reshape(sub, 1, 1, frames, rows, w), conv.shape
    )
    fine_grad, fine_sums = level(
        fine_vals, conv, cot, mine(gain_fine), mine(bias_fine), group_width
    )
    back = (
        fine_grad.astype(jnp.bfloat16)
        .reshape(sub, 2, 2, nf, tl, nr, hl, w)
        .transpose(3, 5, 0, 1, 2, 4, 6, 7)
        .reshape(count, sub, 4 * tl * hl * w)
    )
    sums = plain_everyone(jnp.concatenate([fine_sums, coarse_sums]), count)
    back = lax.all_to_all(back, PLAIN_BLOCK, 0, 0)
    out = (
        back.reshape(nf, nr, sub, 2, 2, tl, hl, w)
        .transpose(5, 6, 3, 7, 4, 1, 0, 2)
        .reshape(1, tl, 2 * hl, 2 * w, channels)
    )
    sums = sums.reshape(nf, nr, 4, sub).transpose(2, 1, 0, 3).reshape(4, channels)
    totals = lax.psum(sums, "dp")
    cells = nd * frames * rows * w
    scale_fine = 1.0 / jnp.sqrt(jnp.float32(4 * cells))
    scale_coarse = 1.0 / jnp.sqrt(jnp.float32(cells))
    return (
        out,
        totals[1] * scale_fine,
        totals[0] * scale_fine,
        totals[3] * scale_coarse,
        totals[2] * scale_coarse,
    )


def lanes_at(shape, axis):
    return lax.broadcasted_iota(jnp.int32, shape, axis)


def one_hot(found):
    return found.astype(jnp.float32).astype(jnp.bfloat16)


def pixel_order(plan, swapped):
    tl, hl, w = plan.tl, plan.hl, plan.w // 2
    size = 4 * plan.local
    lane = lanes_at((1, size), 1)
    j, i, t = lane % w, lane // w % hl, lane // (w * hl) % tl
    q, p = lane // (w * hl * tl) % 2, lane // (2 * w * hl * tl) % 2
    half = lane // (4 * w * hl * tl)
    if swapped:
        half = 1 - half
    pixel = (t * 2 * hl + 2 * i + p) * 4 * w + 2 * (half * w + j) + q
    return one_hot(lanes_at((size, size), 0) == pixel)


def merged_order(nr, outer, tl, cells):
    size = nr * outer * tl * cells
    lane = lanes_at((1, size), 1)
    cell, dev = lane % cells, lane // cells % nr
    t, o = lane // (cells * nr) % tl, lane // (cells * nr * tl)
    return one_hot(lanes_at((size, size), 0) == ((dev * outer + o) * tl + t) * cells + cell)


def column_order(plan):
    w = plan.w // 2
    lines = plan.places // plan.w
    lane = lanes_at((1, 4 * lines * w + 4 * lines), 1)
    inner = lane % (lines * w)
    place = inner // w * plan.w + lane // (lines * w) * w + inner % w
    past = lane - 2 * lines * w
    border = past % lines * plan.w + jnp.where(past < 2 * lines, w, w - 1)
    wanted = jnp.where(past >= 0, border, place)
    shape = (plan.places, 2 * lines * w + 4 * lines)
    return one_hot(lanes_at(shape, 0) == wanted[:, : shape[1]])


def one_hot_dot(a, b, dims):
    return lax.dot_general(a, b, (dims, ((), ())), preferred_element_type=jnp.float32)


def moved(field, distance, kept):
    size = field.shape[1]
    return jnp.where(kept, pltpu.roll(field, (-distance) % size, 1), 0.0)


def own_column(row, base, sub):
    shape = (sub, row.shape[1])
    mine = lanes_at(shape, 1) == lanes_at(shape, 0) + base
    return jnp.sum(jnp.where(mine, row, 0.0), axis=1, keepdims=True)


def as_row(column):
    shape = (column.shape[0], 128)
    here = lanes_at(shape, 1) == lanes_at(shape, 0)
    return jnp.sum(jnp.where(here, column, 0.0), axis=0, keepdims=True)


def terms(value, count):
    found = []
    for _ in range(count):
        found.append(value.astype(jnp.bfloat16).astype(jnp.float32))
        value = value - found[-1]
    return found


def in_groups(column, group_width):
    sub = column.shape[0]
    grouped = jnp.sum(column.reshape(sub // group_width, group_width, 1), axis=1, keepdims=True)
    return jnp.broadcast_to(grouped, (sub // group_width, group_width, 1)).reshape(sub, 1)


def total(parts):
    return sum(jnp.sum(part, axis=1, keepdims=True) for part in parts)


def statistics(one, two, entries, group_width):
    mean = in_groups(one, group_width) / entries
    square = in_groups(two, group_width) / entries
    return mean, lax.rsqrt(square - mean * mean + EPSILON)


def normalised(parts, gain, bias, mean, inv_std):
    normed, slope = [], []
    for part in parts:
        unit = (part - mean) * inv_std
        preact = gain * unit + bias
        squash = 0.5 + 0.5 * jnp.tanh(0.5 * preact)
        normed.append(unit)
        slope.append(squash * (1.0 + preact * (1.0 - squash)))
    return normed, slope


class Plan:
    def __init__(self, mesh_sizes, acts_coarse, slice_width):
        self.nf, self.nr = mesh_sizes
        self.count = self.nf * self.nr
        self.tl, self.hl, self.w, self.channels = acts_coarse
        self.slice_width = slice_width
        self.sub = slice_width // self.nf
        self.cells = self.hl * self.w
        self.local = self.tl * self.cells
        self.image = self.cells * self.nr
        self.frames = self.tl * self.nf
        self.places = self.frames * self.image
        self.group_width = self.channels // GROUPS
        self.chunks = self.channels // 128
        self.acts_at = self.chunks // 2 * self.local
        self.packed_at = self.acts_at + self.sub
        self.cot_at = self.packed_at + 8
        self.block_rows = self.cot_at + 8
        self.fits = (
            self.sub == 32
            and self.slice_width == 128
            and self.group_width == 16
            and self.cells == 16
            and self.w == 8
            and self.tl == 2
            and self.nr == 4
            and self.nf == 4
            and self.slice_width * self.nr == self.channels
        )

    def place_masks(self, w):
        lane = lanes_at((1, self.places // self.w * w), 1)
        col, row = lane % w, lane // w % (self.hl * self.nr)
        last_row = self.hl * self.nr - 1
        return (lane, col > 0, col < w - 1, row > 0, row < last_row)


def fetched(pairs, sems):
    copies = [pltpu.make_async_copy(src, dst, sems.at[k]) for k, (src, dst) in enumerate(pairs)]
    for copy in copies:
        copy.start()
    return copies


def own_place(plan):
    pair, member, r = lax.axis_index("pairs"), lax.axis_index("member"), lax.axis_index("rows")
    return pair, member, r, r * plan.slice_width + (2 * pair + member) * plan.sub


def fetch_kernel(g_hbm, coarse_hbm, fine_hbm, g_ref, coarse_ref, fine_ref, sems):
    for copy in fetched([(fine_hbm, fine_ref), (coarse_hbm, coarse_ref), (g_hbm, g_ref)], sems):
        copy.wait()


def pack_kernel(plan, g_ref, coarse_ref, fine_ref, out_ref):
    sub, chunks, local = plan.sub, plan.chunks, plan.local
    shape = (2 * local, 2 * 128)
    lane = lanes_at((1, 2 * 128), 1)
    repeated = one_hot(lanes_at(shape, 0) == lane % local + lane // 128 * local)
    shape = (plan.channels, 128)
    quarter = lanes_at(shape, 0) // 8 % 4 == lanes_at(shape, 1) // local
    orders = jnp.concatenate([pixel_order(plan, swapped) for swapped in (False, True)], axis=1)
    acts = fine_ref[...]
    halves = one_hot_dot(acts, orders, ((0,), (0,))).astype(jnp.bfloat16)
    halves = [halves[:, :128], halves[:, 128:]]
    small = one_hot_dot(jnp.concatenate([coarse_ref[...], g_ref[...]], axis=0), repeated, ((0,), (0,)))
    for k, at in enumerate((plan.packed_at, plan.cot_at)):
        rows_of = jnp.where(quarter, small[:, k * 128 : (k + 1) * 128], 0.0).reshape(plan.count, 4, 8, 128)
        out_ref[:, at : at + 8, :] = jnp.sum(rows_of, axis=1).astype(jnp.bfloat16)
    low = lanes_at((sub, 128), 1) < 64
    for s_r in range(plan.nr):
        for s_f in range(plan.nf):
            dest = s_r * plan.nf + s_f
            first, half = s_r * plan.slice_width + s_f // 2 * 2 * sub, s_f % 2
            for k in range(chunks // 2):
                at = (half * chunks // 2 + k) * 128
                out_ref[dest, k * local : (k + 1) * local, :] = g_ref[:, at : at + 128]
            upper, lower = halves[half][first : first + sub], halves[1 - half][first + sub : first + 2 * sub]
            out_ref[dest, plan.acts_at : plan.packed_at, :] = jnp.where(low, upper, lower)


def by_frame_device(plan, got_ref, at, height):
    return jnp.concatenate(
        [
            jnp.concatenate(
                [got_ref[r * plan.nf + f, at : at + height, :] for r in range(plan.nr)], axis=1
            )
            for f in range(plan.nf)
        ],
        axis=0,
    )


def in_places(plan, merged, height):
    width = plan.tl * plan.image
    return [
        jnp.concatenate(
            [merged[f * height : (f + 1) * height, k * width : (k + 1) * width] for f in range(plan.nf)],
            axis=1,
        )
        for k in range(4)
    ]


def coarse_kernel(
    plan,
    got_ref,
    weights,
    gain_c,
    bias_c,
    gain_f,
    bias_f,
    mine_ref,
    sent_ref,
    held_ref,
    inv_ref,
    fine_ref,
    columns,
    fine_order,
    by_column,
    order,
    source,
    conv_ref,
):
    sub, nr, nf, cells, tl, local = plan.sub, plan.nr, plan.nf, plan.cells, plan.tl, plan.local
    wide, depth = 2 * sub, plan.channels // 2
    pair, member, r, base = own_place(plan)
    first = r * plan.slice_width + pair * wide
    columns[0, 0:sub, :] = jnp.broadcast_to(own_column(gain_c[...], base, sub), (sub, 128))
    columns[1, 0:sub, :] = jnp.broadcast_to(own_column(bias_c[...], base, sub), (sub, 128))
    columns[2] = jnp.broadcast_to(own_column(gain_f[...], first, wide), (wide, 128))
    columns[3] = jnp.broadcast_to(own_column(bias_f[...], first, wide), (wide, 128))
    order[...] = merged_order(plan.nr, 4, plan.tl, plan.cells)
    fine_order[...] = merged_order(plan.nr, 8, plan.tl, plan.cells // 2)
    by_column[...] = column_order(plan)
    both = pl.ds(pl.multiple_of(pair * wide, wide), wide)
    half = pl.ds(pl.multiple_of(member * depth, depth), depth)
    for s_f in range(nf):
        for s_r in range(nr):
            for t in range(tl):
                at = (s_f * tl + t) * plan.image + s_r * cells
                for k in range(plan.chunks // 2):
                    source[at : at + cells, k * 128 : (k + 1) * 128] = got_ref[
                        s_r * nf + s_f, k * local + t * cells : k * local + (t + 1) * cells, :
                    ]
    source[plan.places :, :] = jnp.zeros((2 * plan.image, depth), jnp.bfloat16)
    products = sum(
        one_hot_dot(
            weights[9 * k : 9 * k + 9, both, half].reshape(9 * wide, depth),
            source[(2 - k) * plan.image : (2 - k) * plan.image + plan.places, :],
            ((1,), (1,)),
        )
        for k in range(3)
    )
    merged = one_hot_dot(by_frame_device(plan, got_ref, plan.acts_at, sub), fine_order[...], ((1,), (0,)))
    parts = halves_at(plan, merged)
    for pq in range(4):
        fine_ref[pq] = parts[pq]
    one, two = total(parts), total([part * part for part in parts])
    stats = terms(as_row(one) + pltpu.roll(as_row(two), 64, 1), 3)
    stats = jnp.concatenate(stats + [jnp.zeros_like(stats[0])] * 5, axis=0).astype(jnp.bfloat16)
    small = [by_frame_device(plan, got_ref, at, 8) for at in (plan.packed_at, plan.cot_at)]
    merged = one_hot_dot(jnp.concatenate(small, axis=0), order[...], ((1,), (0,)))
    rows_of = 8 * nf
    values, cot = [
        jnp.concatenate(in_places(plan, merged[k * rows_of : (k + 1) * rows_of], 8), axis=0) for k in range(2)
    ]
    gain, bias = columns[0][0:sub, 0:1], columns[1][0:sub, 0:1]
    entries = plan.places * plan.group_width
    mean, inv_std = statistics(total([values]), total([values * values]), entries, plan.group_width)
    (normed,), (slope,) = normalised([values], gain, bias, mean, inv_std)
    held_ref[0], held_ref[1], held_ref[2] = normed, slope, cot
    inv_ref[...] = jnp.broadcast_to(inv_std, (sub, 128))
    lane, has_left, has_right, has_up, has_down = plan.place_masks(plan.w)
    by_col = []
    for col in range(3):
        parts = [products[(3 * row + col) * wide : (3 * row + col + 1) * wide] for row in range(3)]
        by_col.append(parts[1] + moved(parts[0], plan.w, has_down) + moved(parts[2], -plan.w, has_up))
    conv_ref[...] = by_col[1] + moved(by_col[0], 1, has_right) + moved(by_col[2], -1, has_left)
    mine_ref[...] = conv_ref[pl.ds(pl.multiple_of(member * sub, sub), sub), :]
    theirs = conv_ref[pl.ds(pl.multiple_of((1 - member) * sub, sub), sub), :]
    for k in range(plan.places // 128):
        sent_ref[k * sub : (k + 1) * sub, :] = theirs[:, k * 128 : (k + 1) * 128].astype(jnp.bfloat16)
    sent_ref[plan.places // 128 * sub :, :] = stats


def quarter_kernel(plan, mine_ref, both_ref, held_ref, inv_ref, columns, by_column, out_ref, sums_ref):
    sub = plan.sub
    _, member, _, _ = own_place(plan)
    theirs = [both_ref[1 - member, k * sub : (k + 1) * sub, :] for k in range(plan.places // 128)]
    conv = mine_ref[...] + jnp.concatenate(theirs, axis=1).astype(jnp.float32)
    normed, slope, cot = held_ref[0], held_ref[1], held_ref[2]
    gain, inv_std = columns[0][0:sub, 0:1], inv_ref[:, 0:1]
    entries = plan.places * plan.group_width
    pre = conv * slope
    one, two = total([pre]), total([pre * normed])
    group_one = in_groups(gain * one, plan.group_width) / entries
    group_two = in_groups(gain * two, plan.group_width) / entries
    grad = cot + inv_std * (gain * pre - group_one - normed * group_two)
    quartered = (grad * 0.25).astype(jnp.bfloat16)
    sent = one_hot_dot(quartered, by_column[...], ((1,), (0,))).astype(jnp.bfloat16)
    low = lanes_at((sub // 2, 128), 1) < 64
    for half in range(2):
        at = half * 256
        border = sent[:, 512 + half * 128 : 640 + half * 128]
        border = jnp.where(low, border[: sub // 2], border[sub // 2 :])
        for dest in range(half, plan.count, 2):
            out_ref[dest, 0:sub, :] = sent[:, at : at + 128]
            out_ref[dest, sub : 2 * sub, :] = sent[:, at + 128 : at + 256]
            out_ref[dest, 2 * sub : 2 * sub + sub // 2, :] = border
    sums_ref[...] = jnp.concatenate([as_row(one), as_row(two)], axis=0)


def halves_at(plan, merged):
    sub = plan.sub
    turned = jnp.concatenate([pltpu.roll(merged[:, k * 128 : (k + 1) * 128], 64, 1) for k in range(4)], axis=1)
    low = lanes_at((sub, 128), 1) < 64
    parts = []
    for pq in range(4):
        groups = []
        for group in range(2):
            e = 4 * group + pq
            at = e // 2 * 128
            strips = []
            for m in range(plan.nf // 2):
                first, second = slice(2 * m * sub, (2 * m + 1) * sub), slice((2 * m + 1) * sub, (2 * m + 2) * sub)
                if e % 2 == 0:
                    strips.append(jnp.where(low, merged[first, at : at + 128], turned[second, at : at + 128]))
                else:
                    strips.append(jnp.where(low, turned[first, at : at + 128], merged[second, at : at + 128]))
            groups.append(jnp.concatenate(strips, axis=1))
        parts.append(jnp.concatenate(groups, axis=0))
    return parts


def halves_from(plan, parts):
    sub = plan.sub
    low = lanes_at((sub, 128), 1) < 64
    down = []
    for f in range(plan.nf):
        across = []
        for v in range(4):
            pair = []
            for e in (2 * v, 2 * v + 1):
                group, pq = e // 4, e % 4
                strip = parts[pq][group * sub : (group + 1) * sub, f // 2 * 128 : (f // 2 + 1) * 128]
                pair.append(strip if e % 2 == f % 2 else pltpu.roll(strip, 64, 1))
            across.append(jnp.where(low, pair[0], pair[1]))
        down.append(jnp.concatenate(across, axis=1))
    return jnp.concatenate(down, axis=0)


def fine_kernel(
    plan, got_ref, acts_ref, both_ref, columns, order, sums_ref, weights, out_ref
):
    sub, nr, nf, wide = plan.sub, plan.nr, plan.nf, 2 * plan.sub
    pair, member, r, _ = own_place(plan)
    both = pl.ds(pl.multiple_of(pair * wide, wide), wide)
    w = plan.w // 2
    lines = plan.places // plan.w
    places = lines * w
    source = jnp.concatenate(
        [got_ref[:, k * sub : (k + 1) * sub, :].reshape(plan.channels, 128) for k in range(2)], axis=1
    )
    packed = got_ref[:, wide : wide + sub // 2, :].reshape(plan.count * sub // 2, 128)
    shape = (128, places)
    beside = lanes_at(shape, 1) == lanes_at(shape, 0) % lines * w + (1 - member) * (w - 1)
    border = []
    for k in range(2):
        here = one_hot(beside & (lanes_at(shape, 0) // lines == k))
        found = one_hot_dot(packed, here, ((1,), (0,))).astype(jnp.bfloat16)
        border.append(found.reshape(plan.count, sub // 2, places))
    border = jnp.concatenate(border, axis=1).reshape(plan.channels, places)
    image = plan.image // 2
    sums, extras = 0.0, 0.0
    for k in (2, 1, 0):
        here, beside = source, border
        if k < 2:
            shift = (2 - k) * image
            inside = lanes_at((1, places), 1) < places - shift
            here, beside = [
                jnp.where(inside, pltpu.roll(part, places - shift, 1), jnp.zeros_like(part)) for part in (here, beside)
            ]
        sums = sums + one_hot_dot(
            weights[9 * k : 9 * k + 9, both, :].reshape(9 * wide, plan.channels), here, ((1,), (0,))
        )
        facing = jnp.concatenate([weights[9 * k + 3 * row + 2 * member, both, :] for row in range(3)], axis=0)
        extras = extras + one_hot_dot(facing, beside, ((1,), (0,)))
    parts = [acts_ref[pq] for pq in range(4)]
    at = plan.places // 128 * sub
    stats = sum(both_ref[k, at : at + 8, :].astype(jnp.float32) for k in range(2))
    stats = stats[0:1] + stats[1:2] + stats[2:3]
    entries = 4 * plan.places * plan.group_width
    one, two = own_column(stats, 0, wide), own_column(stats, 64, wide)
    mean, inv_std = statistics(one, two, entries, plan.group_width)
    gain, bias = columns[2][:, 0:1], columns[3][:, 0:1]
    normed, slope = normalised(parts, gain, bias, mean, inv_std)
    lane, has_left, has_right, has_up, has_down = plan.place_masks(w)
    right, left = (1 - member).astype(jnp.float32), member.astype(jnp.float32)
    by_row = []
    for row in range(3):
        a, b, c = [sums[(3 * row + col) * wide : (3 * row + col + 1) * wide] for col in range(3)]
        extra = extras[row * wide : (row + 1) * wide]
        by_row.append(
            (a + b + moved(c, -1, has_left) + left * extra, moved(a, 1, has_right) + b + c + right * extra)
        )
    convs = [by_row[0][q] + by_row[1][q] + moved(by_row[2][q], -w, has_up) for q in range(2)]
    convs += [moved(by_row[0][q], w, has_down) + by_row[1][q] + by_row[2][q] for q in range(2)]
    pre = [conv * part for conv, part in zip(convs, slope)]
    one = total(pre)
    two = total([a * b for a, b in zip(pre, normed)])
    cot = jnp.concatenate(
        [
            jnp.concatenate(
                [got_ref[r * nf + 2 * pair + m, k * sub : (k + 1) * sub, :] for k in range(2)], axis=1
            )
            for m in range(2)
        ],
        axis=0,
    ).astype(jnp.float32)
    scale = inv_std * gain
    stacked = halves_from(plan, [cot + scale * part for part in pre]).astype(jnp.bfloat16)
    sent = one_hot_dot(stacked, order[...], ((1,), (1,))).astype(jnp.bfloat16)
    coarse = sums_ref[0:1] + pltpu.roll(sums_ref[1:2], sub, 1)
    group_one = in_groups(gain * one, plan.group_width) / entries
    group_two = in_groups(gain * two, plan.group_width) / entries
    coded = (
        terms(as_row(one) + pltpu.roll(as_row(two), 64, 1), 2)
        + terms(coarse, 2)
        + terms(as_row(inv_std) + pltpu.roll(as_row(mean), 64, 1), 2)
        + terms(as_row(group_one) + pltpu.roll(as_row(group_two), 64, 1), 2)
    )
    coded = jnp.concatenate(coded, axis=0).astype(jnp.bfloat16)
    for s_r in range(nr):
        for s_f in range(nf):
            out_ref[s_f * nr + s_r, 0:sub, :] = sent[s_f * sub : (s_f + 1) * sub, s_r * 128 : (s_r + 1) * 128]
            out_ref[s_f * nr + s_r, sub : sub + 8, :] = coded


def spread_kernel(plan, got_ref, acts_ref, out_ref, sums_ref):
    sub, nr, nf = plan.sub, plan.nr, plan.nf
    low = lanes_at((sub, 128), 1) < 64
    low_row = lanes_at((1, 128), 1) < 64
    first_row = lanes_at((1, 128), 1) < sub
    source = []
    fine, coarse, moments, groups = [[], []], [[], []], [[], []], [[], []]
    for s_r in range(nr):
        ones, twos, c_ones, c_twos, invs, means = [], [], 0.0, 0.0, [], []
        g_ones, g_twos = [], []
        for pair in range(nf // 2):
            at = 2 * pair * nr + s_r
            left, right = [got_ref[at + k * nr, 0:sub, :].astype(jnp.float32) for k in range(2)]
            source.append(jnp.where(low, left, pltpu.roll(right, 64, 1)))
            source.append(jnp.where(low, pltpu.roll(left, 64, 1), right))
            coded = [got_ref[at + k * nr, sub : sub + 8, :].astype(jnp.float32) for k in range(2)]
            sums = coded[0][0:1] + coded[0][1:2] + coded[1][0:1] + coded[1][1:2]
            ones.append(sums if pair == 0 else pltpu.roll(sums, 64, 1))
            twos.append(pltpu.roll(sums, 64, 1) if pair == 0 else sums)
            grouped = coded[0][6:7] + coded[0][7:8] + coded[1][6:7] + coded[1][7:8]
            g_ones.append(grouped if pair == 0 else pltpu.roll(grouped, 64, 1))
            g_twos.append(pltpu.roll(grouped, 64, 1) if pair == 0 else grouped)
            both = coded[0][4:5] + coded[0][5:6]
            invs.append(both if pair == 0 else pltpu.roll(both, 64, 1))
            means.append(pltpu.roll(both, 64, 1) if pair == 0 else both)
            for k in range(2):
                sums = coded[k][2:3] + coded[k][3:4]
                to = (2 * pair + k) * sub
                c_one = jnp.where(first_row, sums, 0.0)
                c_two = jnp.where(first_row, pltpu.roll(sums, 128 - sub, 1), 0.0)
                c_ones = c_ones + (pltpu.roll(c_one, to, 1) if to else c_one)
                c_twos = c_twos + (pltpu.roll(c_two, to, 1) if to else c_two)
        fine[0].append(jnp.where(low_row, ones[0], ones[1]))
        fine[1].append(jnp.where(low_row, twos[0], twos[1]))
        groups[0].append(jnp.where(low_row, g_ones[0], g_ones[1]))
        groups[1].append(jnp.where(low_row, g_twos[0], g_twos[1]))
        moments[0].append(jnp.where(low_row, invs[0], invs[1]))
        moments[1].append(jnp.where(low_row, means[0], means[1]))
        coarse[0].append(c_ones)
        coarse[1].append(c_twos)
    one, two, inv_std, mean, c_one, c_two, group_one, group_two = [
        jnp.concatenate(part, axis=1) for part in fine + moments + coarse + groups
    ]
    source = jnp.concatenate(source, axis=0).astype(jnp.bfloat16)
    result = one_hot_dot(pixel_order(plan, False), source, ((1,), (1,)))
    normed = (acts_ref[...].astype(jnp.float32) - mean) * inv_std
    out_ref[...] = (result - inv_std * (group_one + normed * group_two)).astype(jnp.bfloat16)
    sums_ref[...] = jnp.concatenate([one, two, c_one, c_two], axis=0)


def total_kernel(scales, both_ref, result_ref, result_hbm, out_hbms, rows_ref, sems):
    copies = fetched([(result_ref, result_hbm)], sems)
    rows = sum(both_ref[k] for k in range(both_ref.shape[0]))
    for k in range(4):
        rows_ref[k] = rows[k : k + 1] * scales[k]
    for k in range(4):
        copies.append(pltpu.make_async_copy(rows_ref.at[k], out_hbms[k], sems.at[k + 1]))
        copies[-1].start()
    for copy in copies:
        copy.wait()


def in_vmem(count):
    return [pl.BlockSpec(memory_space=pltpu.VMEM)] * count


def in_hbm(count):
    return [pl.BlockSpec(memory_space=pltpu.HBM)] * count


def kept(array):
    return pltpu.with_memory_space_constraint(array, pltpu.HBM)


def shape_of(shape, kind):
    return jax.ShapeDtypeStruct(shape, kind)


LIMIT = pltpu.CompilerParams(vmem_limit_bytes=40 * 1024 * 1024)
COST = pl.CostEstimate(flops=2_000_000_000, bytes_accessed=4_000_000, transcendentals=0)


def fast_shards(
    plan,
    acts_fine,
    acts_coarse,
    grad_coarse,
    gain_fine,
    bias_fine,
    kernel_fine,
    gain_coarse,
    bias_coarse,
    kernel_coarse,
):
    nd = lax.axis_size("dp")
    count, sub, channels, places, local = plan.count, plan.sub, plan.channels, plan.places, plan.local
    f32, bf16 = jnp.float32, jnp.bfloat16
    rows = [part.reshape(1, channels) for part in (gain_coarse, bias_coarse, gain_fine, bias_fine)]
    places_of = ((local, channels), (local, channels), (4 * local, channels))
    fetched_of = pl.pallas_call(
        fetch_kernel,
        out_shape=tuple(pltpu.VMEM(shape, bf16) for shape in places_of),
        in_specs=in_hbm(3),
        out_specs=tuple(in_vmem(3)),
        scratch_shapes=[pltpu.SemaphoreType.DMA((3,))],
        compiler_params=LIMIT,
    )(*[kept(part.reshape(shape)) for part, shape in zip((grad_coarse, acts_coarse, acts_fine), places_of)])
    acts = fetched_of[2]
    packed = pl.pallas_call(
        functools.partial(pack_kernel, plan),
        out_shape=shape_of((count, plan.block_rows, 128), bf16),
        in_specs=in_vmem(3),
        out_specs=in_vmem(1)[0],
        compiler_params=LIMIT,
        cost_estimate=COST,
    )(*fetched_of)
    got = lax.all_to_all(packed, BLOCK, 0, 0)
    mine, theirs, held, inv_std, fine_acts, columns, fine_order, by_column = pl.pallas_call(
        functools.partial(coarse_kernel, plan),
        out_shape=(
            shape_of((sub, places), f32),
            shape_of((places // 128 * sub + 8, 128), bf16),
            shape_of((3, sub, places), f32),
            shape_of((sub, 128), f32),
            shape_of((4, 2 * sub, places // 2), f32),
            shape_of((4, 2 * sub, 128), f32),
            shape_of((4 * plan.nr * local, 4 * plan.nr * local), bf16),
            shape_of((places, places + places // 2), bf16),
        ),
        in_specs=in_vmem(6),
        out_specs=tuple(in_vmem(8)),
        scratch_shapes=[
            pltpu.VMEM((4 * plan.nr * local, 4 * plan.nr * local), bf16),
            pltpu.VMEM((places + 2 * plan.image, channels // 2), bf16),
            pltpu.VMEM((2 * sub, places), f32),
        ],
        compiler_params=LIMIT,
        cost_estimate=COST,
    )(got, kernel_coarse, *rows)
    both = lax.all_gather(theirs, "member")
    quartered, coarse_sums = pl.pallas_call(
        functools.partial(quarter_kernel, plan),
        out_shape=(shape_of((count, 2 * sub + sub // 2, 128), bf16), shape_of((2, 128), f32)),
        in_specs=in_vmem(6),
        out_specs=tuple(in_vmem(2)),
        compiler_params=LIMIT,
        cost_estimate=COST,
    )(mine, both, held, inv_std, columns, by_column)
    spread = lax.all_to_all(quartered, BLOCK, 0, 0)
    sent = pl.pallas_call(
        functools.partial(fine_kernel, plan),
        out_shape=shape_of((count, sub + 8, 128), bf16),
        in_specs=in_vmem(7),
        out_specs=in_vmem(1)[0],
        compiler_params=LIMIT,
        cost_estimate=COST,
    )(spread, fine_acts, both, columns, fine_order, coarse_sums, kernel_fine)
    back = lax.all_to_all(sent, BACK_BLOCK, 0, 0)
    cells = nd * places
    fine_scale, coarse_scale = 1.0 / math.sqrt(4 * cells), 1.0 / math.sqrt(cells)
    out, sums = pl.pallas_call(
        functools.partial(spread_kernel, plan),
        out_shape=(pltpu.VMEM((4 * local, channels), bf16), shape_of((4, channels), f32)),
        in_specs=in_vmem(2),
        out_specs=tuple(in_vmem(2)),
        compiler_params=LIMIT,
        cost_estimate=COST,
    )(back, acts)
    both = lax.all_gather(sums, "dp")
    out, sums = pl.pallas_call(
        functools.partial(total_kernel, (fine_scale, fine_scale, coarse_scale, coarse_scale)),
        out_shape=(pltpu.HBM((4 * local, channels), bf16), (pltpu.HBM((1, channels), f32),) * 4),
        in_specs=in_vmem(2),
        out_specs=(in_hbm(1)[0], tuple(in_hbm(4))),
        scratch_shapes=[pltpu.VMEM((4, 1, channels), f32), pltpu.SemaphoreType.DMA((5,))],
        compiler_params=LIMIT,
        cost_estimate=COST,
    )(both, out)
    bias_f, gain_f, bias_c, gain_c = [part.reshape(channels) for part in sums]
    return out.reshape(acts_fine.shape), gain_f, bias_f, gain_c, bias_c


def solution(mesh):
    def function(*arrays):
        local = [size // mesh.shape[axis] for size, axis in zip(arrays[1].shape, ("dp", "frames", "rows"))]
        sizes = (mesh.shape["frames"], mesh.shape["rows"])
        plan = Plan(sizes, (*local[1:], *arrays[1].shape[3:]), arrays[5].shape[1] // mesh.shape["rows"])
        if plan.fits:
            split = (mesh.shape["dp"], plan.nf // 2, 2, plan.nr)
            used = jax.sharding.Mesh(mesh.devices.reshape(split), ("dp", "pairs", "member", "rows"))
            shards, frames = functools.partial(fast_shards, plan), ("pairs", "member")
        else:
            used, shards, frames = mesh, plain_shards, "frames"
        blocks, kernel = P("dp", frames, "rows", None, None), P(None, "rows", None)
        in_specs = (blocks, blocks, blocks, P(), P(), kernel, P(), P(), kernel)
        out_specs = (blocks, P(), P(), P(), P())
        mapped = jax.shard_map(shards, mesh=used, in_specs=in_specs, out_specs=out_specs, check_vma=False)
        return mapped(*arrays)

    return function
```
